32 devices in a mesh: fsdp: 4 (over y, core), ctx: 8 (over z, x).
Axes of the slice: x: 2, y: 2, z: 4, core: 2. Of those that a mesh axis runs over, the one named last changes fastest.
Arguments:
- tokens: bfloat16 [1024, 8, 1152], P('ctx', 'fsdp'), may hold values from -6 to 6
- w_query: bfloat16 [1152, 1152], P('fsdp'), may hold values from -0.1875 to 0.1875
- w_key: bfloat16 [1152, 384], P('fsdp'), may hold values from -0.1875 to 0.1875
- w_value: bfloat16 [1152, 384], P('fsdp'), may hold values from -0.1875 to 0.1875
- w_out: bfloat16 [1152, 1152], P('fsdp'), may hold values from -1.5 to 1.5
- w_gate: bfloat16 [1152, 3072], P('fsdp'), may hold values from -0.1875 to 0.1875
- w_up: bfloat16 [1152, 3072], P('fsdp'), may hold values from -0.1875 to 0.1875
- w_down: bfloat16 [3072, 1152], P('fsdp'), may hold values from -0.109375 to 0.109375
- gain_attn: bfloat16 [1152], P('fsdp'), may hold values from 0.5 to 1.5
- gain_ffn: bfloat16 [1152], P('fsdp'), may hold values from 0.5 to 1.5
- cotangent: bfloat16 [1024, 8, 1152], P('ctx', 'fsdp'), may hold values from -6 to 6
Outputs:
- layer_out: bfloat16 [1024, 8, 1152], P('ctx', 'fsdp')
- grad_tokens: float32 [1024, 8, 1152], P('ctx', 'fsdp')
- grad_query: float32 [1152, 1152], P('fsdp')
- grad_key: float32 [1152, 384], P('fsdp')
- grad_value: float32 [1152, 384], P('fsdp')
- grad_out: float32 [1152, 1152], P('fsdp')
- grad_gate: float32 [1152, 3072], P('fsdp')
- grad_up: float32 [1152, 3072], P('fsdp')
- grad_down: float32 [3072, 1152], P('fsdp')
- grad_gain_attn: float32 [1152], P('fsdp')
- grad_gain_ffn: float32 [1152], P('fsdp')
The draws below stay inside these ranges and needn't reach their ends.
All inputs are finite; a program needn't handle non-finite values.
Results may differ from the reference program's by a relative error of at most 0.023.
Values may be sent and summed in bfloat16 or wider, within the bound.
A program may use at most 320 MiB of HBM per device.

```python
import jax
import jax.numpy as jnp
from jax import lax

D = 1152
H = 18
KVH = 6
HD = 64
FF = 3072
LEN = 1024
SEQS = 8


def level_of(key, extent, split, least, high):
    level = 1.0
    for axis_at, blocks in split:
        heights = jax.random.uniform(jax.random.fold_in(jax.random.fold_in(key, 6), axis_at), (blocks,), jnp.float32, least / len(split), high / len(split))
        level = level * jnp.repeat(jnp.exp(heights), extent[axis_at] // blocks).reshape((-1,) + (1,) * (len(extent) - 1 - axis_at))
    return level


def gaussian(key, extent, deviation, bound, cuts=(), kind=jnp.bfloat16):
    loudness = level_of(key, extent, cuts, -0.22, 0.18) if cuts else 1.0
    entries = jax.random.normal(key, extent, jnp.float32) * deviation * loudness
    return jnp.minimum(jnp.maximum(entries, -bound), bound).astype(kind)


def setup_inputs(seed: int = 0) -> dict:
    streams_of = jax.random.split(jax.random.key(seed), 12)
    return {
        "tokens": gaussian(streams_of[0], (LEN, SEQS, D), 1.0, 6.0, ((0, 8), (1, 4))),
        "w_query": gaussian(streams_of[1], (D, D), D ** -0.5, 0.1875, ((0, 4),)),
        "w_key": gaussian(streams_of[2], (D, KVH * HD), D ** -0.5, 0.1875, ((0, 4),)),
        "w_value": gaussian(streams_of[3], (D, KVH * HD), D ** -0.5, 0.1875, ((0, 4),)),
        "w_out": gaussian(streams_of[4], (D, D), (D // 64) ** -0.5, 1.5, ((0, 4),)),
        "w_gate": gaussian(streams_of[5], (D, FF), D ** -0.5, 0.1875, ((0, 4),)),
        "w_up": gaussian(streams_of[6], (D, FF), D ** -0.5, 0.1875, ((0, 4),)),
        "w_down": gaussian(streams_of[7], (FF, D), FF ** -0.5, 0.109375, ((0, 4),)),
        "gain_attn": jnp.clip(1.0 + 0.1 * jax.random.normal(streams_of[8], (D,), jnp.float32), 0.5, 1.5).astype(jnp.bfloat16),
        "gain_ffn": jnp.clip(1.0 + 0.1 * jax.random.normal(streams_of[9], (D,), jnp.float32), 0.5, 1.5).astype(jnp.bfloat16),
        "cotangent": gaussian(streams_of[10], (LEN, SEQS, D), 1.0, 6.0, ((0, 8), (1, 4))),
    }


@jax.custom_vjp
def low(v):
    return lax.optimization_barrier(v.astype(jnp.bfloat16)).astype(jnp.float32)

@jax.custom_vjp
def low_back(v):
    return v

def low_keep(v):
    return (low(v), None)

def low_pass(kept, grad):
    return (grad,)

def back_keep(v):
    return (v, None)

def back_low(kept, grad):
    return (low(grad),)
low.defvjp(low_keep, low_pass)
low_back.defvjp(back_keep, back_low)
EPSILON = 1e-05
ROTARY_BASE = 10000.0
MASKED_SCORE = -1e+30
HIGHEST = lax.Precision.HIGHEST

def product(left, right):
    return jnp.dot(left, right, precision=HIGHEST)

def rms_norm(rows, gain):
    scale = lax.rsqrt(lax.optimization_barrier(jnp.mean(rows * rows, axis=-1, keepdims=True)) + EPSILON)
    return rows * scale * gain

def rotary(values, positions):
    half = HD // 2
    freqs = ROTARY_BASE ** (-2.0 * jnp.arange(half, dtype=jnp.float32) / HD)
    angles = positions.astype(jnp.float32)[:, None] * freqs[None, :]
    cosine = jnp.cos(angles)[:, None, :]
    sine = jnp.sin(angles)[:, None, :]
    first = values[..., :half]
    second = values[..., half:]
    return jnp.concatenate([first * cosine - second * sine, second * cosine + first * sine], axis=-1)

def attention(queries, keys, values):
    width = min(512, LEN)
    groups = H // KVH
    blocks = queries.reshape(LEN // width, width, KVH, groups, HD)
    starts = width * jnp.arange(LEN // width, dtype=jnp.int32)
    columns = jnp.arange(LEN, dtype=jnp.int32)

    def one_block(item):
        block, start = item
        scores = jnp.einsum('qkgd,pkd->kgqp', block, keys, precision=HIGHEST) * HD ** (-0.5)
        scores = low_back(scores)
        rows = start + jnp.arange(width, dtype=jnp.int32)
        scores = jnp.where(columns[None, :] <= rows[:, None], scores, MASKED_SCORE)
        weights = low(jax.nn.softmax(scores, axis=-1))
        return jnp.einsum('kgqp,pkd->qkgd', weights, values, precision=HIGHEST)
    mixed = lax.map(jax.checkpoint(one_block), (blocks, starts))
    return mixed.reshape(LEN, D)

def layer(inputs, w_query, w_key, w_value, w_out, w_gate, w_up, w_down, gain_attn, gain_ffn):
    positions = jnp.arange(LEN, dtype=jnp.int32)
    normed_attn = low(rms_norm(inputs, gain_attn))
    queries = low(rotary(low_back(product(normed_attn, w_query)).reshape(LEN, H, HD), positions))
    keys = low(rotary(low_back(product(normed_attn, w_key)).reshape(LEN, KVH, HD), positions))
    values = low(low_back(product(normed_attn, w_value))).reshape(LEN, KVH, HD)
    mixed = low(low_back(attention(queries, keys, values)))
    resid = inputs + low_back(product(mixed, w_out))
    normed_ffn = low(rms_norm(resid, gain_ffn))
    gate = low_back(product(normed_ffn, w_gate))
    upward = low_back(product(normed_ffn, w_up))
    act = low(jax.nn.silu(gate) * upward)
    return resid + low_back(product(act, w_down))

def reference(tokens, w_query, w_key, w_value, w_out, w_gate, w_up, w_down, gain_attn, gain_ffn, cotangent):
    weights = tuple((w.astype(jnp.float32) for w in (w_query, w_key, w_value, w_out, w_gate, w_up, w_down, gain_attn, gain_ffn)))
    inputs = jnp.swapaxes(tokens.astype(jnp.float32), 0, 1)
    cotangents = jnp.swapaxes(cotangent.astype(jnp.float32), 0, 1)

    def one_sequence(carry, item):
        sequence, upstream = item
        result, pullback = jax.vjp(layer, sequence, *weights)
        grads = pullback(upstream)
        carry = tuple((total + grad for total, grad in zip(carry, grads[1:])))
        return (carry, (result, grads[0]))
    start = tuple((jnp.zeros_like(w) for w in weights))
    totals, (results, grad_inputs) = lax.scan(one_sequence, start, (inputs, cotangents))
    layer_out = jnp.swapaxes(results, 0, 1).astype(jnp.bfloat16)
    grad_tokens = jnp.swapaxes(grad_inputs, 0, 1)
    return (layer_out, grad_tokens, totals[0], totals[1], totals[2], totals[3], totals[4], totals[5], totals[6], totals[7], totals[8])
```

```python
import jax
import jax.numpy as jnp
from jax import lax
from jax.experimental import pallas as pl
from jax.experimental.pallas import tpu as pltpu
from jax.sharding import PartitionSpec as P

H = 18
KVH = 6
HD = 64
FF = 3072


EPSILON = 1e-05
ROTARY_BASE = 10000.0
MASKED_SCORE = -1e30


def rotary(values, positions, direction):
    half = values.shape[-1] // 2
    freqs = ROTARY_BASE ** (-2.0 * jnp.arange(half, dtype=jnp.float32) / values.shape[-1])
    angles = positions.astype(jnp.float32)[:, None] * freqs[None, :]
    cosine = jnp.cos(angles)[:, None, None, :]
    sine = direction * jnp.sin(angles)[:, None, None, :]
    first = values[..., :half]
    second = values[..., half:]
    return jnp.concatenate(
        [first * cosine - second * sine, second * cosine + first * sine], axis=-1
    )


def norm_scale(rows):
    return lax.rsqrt(jnp.mean(rows * rows, axis=-1, keepdims=True) + EPSILON)


def norm_back(rows, scale, gain, upstream):
    scaled = upstream * gain
    inward = scale * scaled - rows * scale**3 * jnp.mean(scaled * rows, axis=-1, keepdims=True)
    return (inward, jnp.sum(upstream * rows * scale, axis=0))


def forward_dot(left, right):
    return jnp.dot(left, right, preferred_element_type=jnp.float32)


def backward_dot(grad, weight):
    return jnp.einsum("rn,cn->rc", grad, weight, preferred_element_type=jnp.float32)


def attend_kernel(q_ref, kv_ref, mix_ref, log_ref):
    me = lax.axis_index("ctx")
    units, deep, wide = q_ref.shape
    keys = kv_ref.shape[2]

    def unit_step(unit, unused):
        q = q_ref[unit]

        def attend(block, top, total, mixed, diagonal):
            kv = kv_ref[block, unit]
            scores = jnp.dot(kv, q, preferred_element_type=jnp.float32)
            if diagonal:
                key_at = lax.broadcasted_iota(jnp.int32, scores.shape, 0)
                query_at = lax.rem(lax.broadcasted_iota(jnp.int32, scores.shape, 1), keys)
                scores = jnp.where(key_at <= query_at, scores, MASKED_SCORE)
            new_top = jnp.maximum(top, jnp.max(scores, axis=0, keepdims=True))
            fade = jnp.exp(top - new_top)
            weights = jnp.exp(scores - new_top)
            total = total * fade + jnp.sum(weights, axis=0, keepdims=True)
            added = jnp.dot(
                kv.T, weights.astype(jnp.bfloat16), preferred_element_type=jnp.float32
            )
            return new_top, total, mixed * fade + added[HD:]

        state = (
            jnp.full((1, wide), MASKED_SCORE, jnp.float32),
            jnp.zeros((1, wide), jnp.float32),
            jnp.zeros((HD, wide), jnp.float32),
        )
        state = attend(me, *state, True)
        top, total, mixed = lax.fori_loop(
            0, me, lambda block, state: attend(block, *state, False), state
        )
        mix_ref[unit] = mixed / total
        log_ref[unit] = top + jnp.log(total)
        return unused

    lax.fori_loop(0, units, unit_step, 0)


def attend_back_kernel(q_ref, g_ref, qg_ref, kv_ref, mix_ref, log_ref, grad_q_ref, grad_kv_ref):
    me = lax.axis_index("ctx")
    units, deep, wide = q_ref.shape
    blocks, _, keys, _ = kv_ref.shape

    def clear(block, unused):
        grad_kv_ref[block] = jnp.zeros(grad_kv_ref.shape[1:], grad_kv_ref.dtype)
        return unused

    lax.fori_loop(me + 1, blocks, clear, 0)

    def unit_step(unit, unused):
        q, g, qg, log_total = q_ref[unit], g_ref[unit], qg_ref[unit], log_ref[unit]
        delta = jnp.sum(g[HD:].astype(jnp.float32) * mix_ref[unit], axis=0, keepdims=True)

        def back(block, grad_q, diagonal):
            kv = kv_ref[block, unit]
            scores = jnp.dot(kv, q, preferred_element_type=jnp.float32)
            probs = jnp.exp(scores - log_total)
            if diagonal:
                key_at = lax.broadcasted_iota(jnp.int32, scores.shape, 0)
                query_at = lax.rem(lax.broadcasted_iota(jnp.int32, scores.shape, 1), keys)
                probs = jnp.where(key_at <= query_at, probs, 0.0)
            grad_probs = jnp.dot(kv, g, preferred_element_type=jnp.float32)
            grad_scores = (probs * (grad_probs - delta)).astype(jnp.bfloat16)
            both = jnp.concatenate([grad_scores, probs.astype(jnp.bfloat16)], axis=1)
            grad_kv_ref[block, unit] = jnp.dot(
                both, qg, preferred_element_type=jnp.float32
            ).astype(grad_kv_ref.dtype)
            added = jnp.dot(kv.T, grad_scores, preferred_element_type=jnp.float32)
            return grad_q + added[:HD]

        grad_q = back(me, jnp.zeros((HD, wide), jnp.float32), True)
        grad_q = lax.fori_loop(0, me, lambda block, held: back(block, held, False), grad_q)
        grad_q_ref[unit] = grad_q * HD ** (-0.5)
        return unused

    lax.fori_loop(0, units, unit_step, 0)


def call(kernel, outs, *args):
    return pl.pallas_call(
        kernel,
        out_shape=outs,
        in_specs=[pl.BlockSpec(memory_space=pltpu.VMEM)] * len(args),
        out_specs=[pl.BlockSpec(memory_space=pltpu.VMEM)] * len(outs),
        compiler_params=pltpu.CompilerParams(vmem_limit_bytes=56 << 20),
    )(*args)


def unit_columns(rows, seq_count, block_len):
    groups = H // KVH
    split = rows.reshape(block_len, seq_count, KVH, groups, HD)
    return jnp.transpose(split, (1, 2, 4, 3, 0)).reshape(
        seq_count * KVH, HD, groups * block_len
    )


def unit_rows(columns, seq_count, block_len):
    groups = H // KVH
    split = columns.reshape(seq_count, KVH, HD, groups, block_len)
    return jnp.transpose(split, (4, 0, 1, 3, 2)).reshape(block_len * seq_count, H * HD)


def on_device(
    tokens, w_query, w_key, w_value, w_out, w_gate, w_up, w_down, gain_attn, gain_ffn, cotangent
):
    block_len, seq_count, width = tokens.shape
    rows_count = block_len * seq_count
    groups = H // KVH
    kv_width = KVH * HD
    own_weights = (w_query, w_key, w_value, w_out, w_gate, w_up, w_down, gain_attn, gain_ffn)
    (
        full_query,
        full_key,
        full_value,
        full_out,
        full_gate,
        full_up,
        full_down,
        full_gain_attn,
        full_gain_ffn,
    ) = (
        lax.all_gather(own_weights[0], "fsdp", axis=0, tiled=True),
        lax.all_gather(own_weights[1], "fsdp", axis=0, tiled=True),
        lax.all_gather(own_weights[2], "fsdp", axis=0, tiled=True),
        lax.all_gather(own_weights[3], "fsdp", axis=0, tiled=True),
        lax.all_gather(own_weights[4], "fsdp", axis=0, tiled=True),
        lax.all_gather(own_weights[5], "fsdp", axis=0, tiled=True),
        lax.all_gather(own_weights[6], "fsdp", axis=0, tiled=True),
        lax.all_gather(own_weights[7], "fsdp", axis=0, tiled=True),
        lax.all_gather(own_weights[8], "fsdp", axis=0, tiled=True),
    )
    my_start = lax.axis_index("ctx") * block_len
    positions = my_start + jnp.arange(block_len, dtype=jnp.int32)
    inputs = tokens.astype(jnp.float32).reshape(rows_count, width)
    scale_attn = norm_scale(inputs)
    normed_attn = (inputs * scale_attn * full_gain_attn.astype(jnp.float32)).astype(jnp.bfloat16)
    query_raw = forward_dot(normed_attn, full_query)
    key_raw = forward_dot(normed_attn, full_key)
    value_raw = forward_dot(normed_attn, full_value)
    units = seq_count * KVH
    wide = groups * block_len
    queries = (
        rotary(query_raw.reshape(block_len, seq_count, H, HD), positions, 1.0)
        .astype(jnp.bfloat16)
        .reshape(rows_count, width)
    )
    keys_local = rotary(
        key_raw.reshape(block_len, seq_count, KVH, HD), positions, 1.0
    ).astype(jnp.bfloat16)
    values_local = value_raw.astype(jnp.bfloat16).reshape(block_len, seq_count, KVH, HD)
    pairs = jnp.transpose(
        jnp.concatenate([keys_local, values_local], axis=-1), (1, 2, 0, 3)
    ).reshape(units, block_len, 2 * HD)
    all_pairs = lax.all_gather(pairs, "ctx", axis=0)
    q_unit = unit_columns(queries * jnp.bfloat16(HD ** (-0.5)), seq_count, block_len)
    q_wide = jnp.concatenate([q_unit, jnp.zeros_like(q_unit)], axis=1)
    mix_unit, log_total = call(
        attend_kernel,
        [
            jax.ShapeDtypeStruct((units, HD, wide), jnp.float32),
            jax.ShapeDtypeStruct((units, 1, wide), jnp.float32),
        ],
        q_wide,
        all_pairs,
    )
    attn_low = unit_rows(mix_unit.astype(jnp.bfloat16), seq_count, block_len)
    resid = inputs + forward_dot(attn_low, full_out)
    scale_ffn = norm_scale(resid)
    normed_ffn = (resid * scale_ffn * full_gain_ffn.astype(jnp.float32)).astype(jnp.bfloat16)
    gate = forward_dot(normed_ffn, full_gate)
    upward = forward_dot(normed_ffn, full_up)
    sigmoid_gate = jax.nn.sigmoid(gate)
    act_low = (gate * sigmoid_gate * upward).astype(jnp.bfloat16)
    layer_out = (
        (resid + forward_dot(act_low, full_down))
        .astype(jnp.bfloat16)
        .reshape(block_len, seq_count, width)
    )
    upstream_low = cotangent.reshape(rows_count, width)
    upstream = upstream_low.astype(jnp.float32)
    grad_act = backward_dot(upstream_low, full_down)
    grad_gate_low = (grad_act * upward * sigmoid_gate * (1.0 + gate * (1.0 - sigmoid_gate))).astype(
        jnp.bfloat16
    )
    grad_up_low = (grad_act * gate * sigmoid_gate).astype(jnp.bfloat16)
    grad_normed_ffn = backward_dot(grad_gate_low, full_gate) + backward_dot(grad_up_low, full_up)
    inward_ffn, gain_term_ffn = norm_back(
        resid, scale_ffn, full_gain_ffn.astype(jnp.float32), grad_normed_ffn
    )
    grad_resid = upstream + inward_ffn
    grad_branch = grad_resid.astype(jnp.bfloat16)
    grad_mix = backward_dot(grad_branch, full_out).astype(jnp.bfloat16)
    g_unit = unit_columns(grad_mix, seq_count, block_len)
    g_wide = jnp.concatenate([jnp.zeros_like(g_unit), g_unit], axis=1)
    q_rows, g_rows = jnp.swapaxes(q_unit, 1, 2), jnp.swapaxes(g_unit, 1, 2)
    blank = jnp.zeros_like(q_rows)
    qg = jnp.concatenate(
        [jnp.concatenate([q_rows, blank], axis=2), jnp.concatenate([blank, g_rows], axis=2)],
        axis=1,
    )
    grad_q_unit, grad_pairs = call(
        attend_back_kernel,
        [
            jax.ShapeDtypeStruct((units, HD, wide), jnp.float32),
            jax.ShapeDtypeStruct(all_pairs.shape, jnp.bfloat16),
        ],
        q_wide,
        g_wide,
        qg,
        all_pairs,
        mix_unit,
        log_total,
    )
    summed_pairs = lax.psum_scatter(grad_pairs, "ctx", scatter_dimension=0, tiled=True)
    summed_pairs = jnp.transpose(
        summed_pairs.reshape(seq_count, KVH, block_len, 2 * HD), (2, 0, 1, 3)
    )
    grad_query_low = (
        rotary(
            unit_rows(grad_q_unit, seq_count, block_len).reshape(block_len, seq_count, H, HD),
            positions,
            -1.0,
        )
        .astype(jnp.bfloat16)
        .reshape(rows_count, width)
    )
    grad_key_low = (
        rotary(summed_pairs[..., :HD].astype(jnp.float32), positions, -1.0)
        .astype(jnp.bfloat16)
        .reshape(rows_count, kv_width)
    )
    grad_value_low = summed_pairs[..., HD:].reshape(rows_count, kv_width)
    grad_normed_attn = (
        backward_dot(grad_query_low, full_query)
        + backward_dot(grad_key_low, full_key)
        + backward_dot(grad_value_low, full_value)
    )
    inward_attn, gain_term_attn = norm_back(
        inputs, scale_attn, full_gain_attn.astype(jnp.float32), grad_normed_attn
    )
    grad_tokens = (grad_resid + inward_attn).reshape(block_len, seq_count, width)

    def part(acts, grads):
        return jnp.einsum("rc,rn->cn", acts, grads, preferred_element_type=jnp.float32)

    row_shares = lax.psum_scatter(
        jnp.concatenate(
            [
                part(normed_attn, grad_query_low),
                part(normed_attn, grad_key_low),
                part(normed_attn, grad_value_low),
                part(attn_low, grad_branch),
                part(normed_ffn, grad_gate_low),
                part(normed_ffn, grad_up_low),
            ],
            axis=1,
        ).astype(jnp.bfloat16),
        "fsdp",
        scatter_dimension=0,
        tiled=True,
    )
    down_term = jnp.einsum("rc,rn->cn", act_low, upstream_low, preferred_element_type=jnp.float32)
    gain_term = jnp.stack([gain_term_attn, gain_term_ffn], axis=1)
    down_share, gain_share = (
        lax.psum_scatter(
            down_term.astype(jnp.bfloat16), "fsdp", scatter_dimension=0, tiled=True
        ).astype(jnp.float32),
        lax.psum_scatter(
            gain_term.astype(jnp.bfloat16), "fsdp", scatter_dimension=0, tiled=True
        ).astype(jnp.float32),
    )
    row_total, down_total, gain_total = (
        lax.psum(row_shares, "ctx").astype(jnp.float32),
        lax.psum(down_share.astype(jnp.bfloat16), "ctx").astype(jnp.float32),
        lax.psum(gain_share.astype(jnp.bfloat16), "ctx").astype(jnp.float32),
    )
    edges = [
        0,
        width,
        width + kv_width,
        width + 2 * kv_width,
        2 * width + 2 * kv_width,
        2 * width + 2 * kv_width + FF,
        2 * width + 2 * kv_width + 2 * FF,
    ]
    grad_query = row_total[:, edges[0] : edges[1]]
    grad_key = row_total[:, edges[1] : edges[2]]
    grad_value = row_total[:, edges[2] : edges[3]]
    grad_out = row_total[:, edges[3] : edges[4]]
    grad_gate = row_total[:, edges[4] : edges[5]]
    grad_up = row_total[:, edges[5] : edges[6]]
    return (
        layer_out,
        grad_tokens,
        grad_query,
        grad_key,
        grad_value,
        grad_out,
        grad_gate,
        grad_up,
        down_total,
        gain_total[:, 0],
        gain_total[:, 1],
    )


def solution(mesh):
    return jax.shard_map(
        on_device,
        mesh=mesh,
        in_specs=(
            P("ctx", "fsdp", None),
            P("fsdp", None),
            P("fsdp", None),
            P("fsdp", None),
            P("fsdp", None),
            P("fsdp", None),
            P("fsdp", None),
            P("fsdp", None),
            P("fsdp"),
            P("fsdp"),
            P("ctx", "fsdp", None),
        ),
        out_specs=(
            P("ctx", "fsdp", None),
            P("ctx", "fsdp", None),
            P("fsdp", None),
            P("fsdp", None),
            P("fsdp", None),
            P("fsdp", None),
            P("fsdp", None),
            P("fsdp", None),
            P("fsdp", None),
            P("fsdp"),
            P("fsdp"),
        ),
        check_vma=False,
    )
```

```python
import jax
import jax.numpy as jnp
from jax import lax
from jax.experimental import pallas as pl
from jax.experimental.pallas import tpu as pltpu
from jax.sharding import PartitionSpec as P

H = 18
KVH = 6
HD = 64
FF = 3072


EPSILON = 1e-05
ROTARY_BASE = 10000.0
MASKED_SCORE = -1e30


def rotary(values, positions, direction):
    half = values.shape[-1] // 2
    freqs = ROTARY_BASE ** (-2.0 * jnp.arange(half, dtype=jnp.float32) / values.shape[-1])
    angles = positions.astype(jnp.float32)[:, None] * freqs[None, :]
    cosine = jnp.cos(angles)[:, None, None, :]
    sine = direction * jnp.sin(angles)[:, None, None, :]
    first = values[..., :half]
    second = values[..., half:]
    return jnp.concatenate(
        [first * cosine - second * sine, second * cosine + first * sine], axis=-1
    )


def norm_scale(rows):
    return lax.rsqrt(jnp.mean(rows * rows, axis=-1, keepdims=True) + EPSILON)


def norm_back(rows, scale, gain, upstream):
    scaled = upstream * gain
    inward = scale * scaled - rows * scale**3 * jnp.mean(scaled * rows, axis=-1, keepdims=True)
    return (inward, jnp.sum(upstream * rows * scale, axis=0))


def forward_dot(left, right):
    return jnp.dot(left, right, preferred_element_type=jnp.float32)


def backward_dot(grad, weight):
    return jnp.einsum("rn,cn->rc", grad, weight, preferred_element_type=jnp.float32)


def attend_kernel(q_ref, kv_ref, mix_ref, log_ref):
    me = lax.axis_index("ctx")
    units, deep, wide = q_ref.shape
    keys = kv_ref.shape[2]

    def unit_step(unit, unused):
        q = q_ref[unit]

        def attend(block, top, total, mixed, diagonal):
            kv = kv_ref[block, unit]
            scores = jnp.dot(kv, q, preferred_element_type=jnp.float32)
            if diagonal:
                key_at = lax.broadcasted_iota(jnp.int32, scores.shape, 0)
                query_at = lax.rem(lax.broadcasted_iota(jnp.int32, scores.shape, 1), keys)
                scores = jnp.where(key_at <= query_at, scores, MASKED_SCORE)
            new_top = jnp.maximum(top, jnp.max(scores, axis=0, keepdims=True))
            fade = jnp.exp(top - new_top)
            weights = jnp.exp(scores - new_top)
            total = total * fade + jnp.sum(weights, axis=0, keepdims=True)
            added = jnp.dot(
                kv.T, weights.astype(jnp.bfloat16), preferred_element_type=jnp.float32
            )
            return new_top, total, mixed * fade + added[HD:]

        state = (
            jnp.full((1, wide), MASKED_SCORE, jnp.float32),
            jnp.zeros((1, wide), jnp.float32),
            jnp.zeros((HD, wide), jnp.float32),
        )
        state = attend(me, *state, True)
        top, total, mixed = lax.fori_loop(
            0, me, lambda block, state: attend(block, *state, False), state
        )
        mix_ref[unit] = mixed / total
        log_ref[unit] = top + jnp.log(total)
        return unused

    lax.fori_loop(0, units, unit_step, 0)


def attend_back_kernel(q_ref, g_ref, qg_ref, kv_ref, mix_ref, log_ref, grad_q_ref, grad_kv_ref):
    me = lax.axis_index("ctx")
    units, deep, wide = q_ref.shape
    blocks, _, keys, _ = kv_ref.shape

    def clear(block, unused):
        grad_kv_ref[block] = jnp.zeros(grad_kv_ref.shape[1:], grad_kv_ref.dtype)
        return unused

    lax.fori_loop(me + 1, blocks, clear, 0)

    def unit_step(unit, unused):
        q, g, qg, log_total = q_ref[unit], g_ref[unit], qg_ref[unit], log_ref[unit]
        delta = jnp.sum(g[HD:].astype(jnp.float32) * mix_ref[unit], axis=0, keepdims=True)

        def back(block, grad_q, diagonal):
            kv = kv_ref[block, unit]
            scores = jnp.dot(kv, q, preferred_element_type=jnp.float32)
            probs = jnp.exp(scores - log_total)
            if diagonal:
                key_at = lax.broadcasted_iota(jnp.int32, scores.shape, 0)
                query_at = lax.rem(lax.broadcasted_iota(jnp.int32, scores.shape, 1), keys)
                probs = jnp.where(key_at <= query_at, probs, 0.0)
            grad_probs = jnp.dot(kv, g, preferred_element_type=jnp.float32)
            grad_scores = (probs * (grad_probs - delta)).astype(jnp.bfloat16)
            both = jnp.concatenate([grad_scores, probs.astype(jnp.bfloat16)], axis=1)
            grad_kv_ref[block, unit] = jnp.dot(
                both, qg, preferred_element_type=jnp.float32
            ).astype(grad_kv_ref.dtype)
            added = jnp.dot(kv.T, grad_scores, preferred_element_type=jnp.float32)
            return grad_q + added[:HD]

        grad_q = back(me, jnp.zeros((HD, wide), jnp.float32), True)
        grad_q = lax.fori_loop(0, me, lambda block, held: back(block, held, False), grad_q)
        grad_q_ref[unit] = grad_q * HD ** (-0.5)
        return unused

    lax.fori_loop(0, units, unit_step, 0)


MESH = pl.DeviceIdType.MESH
LANES = 128


def ring_place(ctx, fsdp, count):
    column, side = lax.div(ctx, 2), lax.rem(ctx, 2)
    place = column + side * (count - 1 - 2 * column)
    odd = lax.rem(fsdp, 2)
    return place + odd * (count - 1 - 2 * place)


def ring_ctx(place, fsdp, count):
    odd = lax.rem(fsdp, 2)
    place = place + odd * (count - 1 - 2 * place)
    late = lax.div(place, count // 2)
    return (1 - late) * 2 * place + late * (2 * (count - 1 - place) + 1)


def ring_neighbours(count):
    ctx, fsdp = lax.axis_index("ctx"), lax.axis_index("fsdp")
    place = ring_place(ctx, fsdp, count)
    after = ring_ctx(lax.rem(place + 1, count), fsdp, count)
    before = ring_ctx(lax.rem(place + count - 1, count), fsdp, count)
    return place, (fsdp, after), (fsdp, before)


class Ring:
    def __init__(self, count, works, landings, totals, sends, arrivals):
        self.count, self.works, self.landings, self.totals = count, works, landings, totals
        self.sends, self.arrivals = sends, arrivals
        self.place, self.after, self.before = ring_neighbours(count)
        self.ticks = 2 * count - 2

    def chunk(self, held, index):
        per = held.shape[0] // self.count
        return held.at[pl.ds(index * per, per)]

    def copy(self, stream, step, index, summing):
        source = self.chunk((self.works if summing else self.totals)[stream], index)
        target = self.landings[stream].at[step] if summing else source
        return pltpu.make_async_remote_copy(
            src_ref=source,
            dst_ref=target,
            send_sem=self.sends.at[stream, step],
            recv_sem=self.arrivals.at[stream, step],
            device_id=self.after,
            device_id_type=MESH,
        )

    def start(self, stream):
        self.copy(stream, 0, self.place, True).start()

    def tick(self, step):
        index = lax.rem(self.place + 3 * self.count - 1 - step, self.count)
        last = self.count - 2
        for stream in range(len(self.works)):
            self.copy(stream, step, index, False).wait_recv()

            def add(target, stream=stream):
                part = self.chunk(self.works[stream], index)
                landed = self.landings[stream].at[jnp.minimum(step, last)]
                for row in range(part.shape[0]):
                    target[row] = (
                        part[row].astype(jnp.float32) + landed[row].astype(jnp.float32)
                    ).astype(part.dtype)

            @pl.when(step < last)
            def _():
                add(self.chunk(self.works[stream], index))
                self.copy(stream, jnp.minimum(step + 1, last), index, True).start()

            @pl.when(step == last)
            def _():
                add(self.chunk(self.totals[stream], index))

            @pl.when(jnp.logical_and(step >= last, step < self.ticks - 1))
            def _():
                self.copy(stream, jnp.minimum(step + 1, self.ticks - 1), index, False).start()

    def finish(self):
        def wait(step, unused):
            for stream in range(len(self.works)):
                self.copy(stream, step, self.place, False).wait_send()
            return unused

        lax.fori_loop(0, self.ticks, wait, 0)


def reduce_kernel(
    gate_ref, up_ref, down_ref, rest_ref, gate_total, up_total, down_total, rest_total,
    gate_work, up_work, down_work, rest_work, gate_land, up_land, down_land, rest_land,
    sends, arrivals, part_sends, part_arrivals, local_sems,
):
    fsdp, ctx = lax.axis_index("fsdp"), lax.axis_index("ctx")
    group, count = lax.axis_size("fsdp"), lax.axis_size("ctx")
    works = [gate_work, up_work, down_work, rest_work]
    landings = [gate_land, up_land, down_land, rest_land]
    totals = [gate_total, up_total, down_total, rest_total]
    ring = Ring(count, works, landings, totals, sends, arrivals)
    barrier = pltpu.get_barrier_semaphore()
    for device in (ring.after, ring.before):
        pl.semaphore_signal(barrier, inc=1, device_id=device, device_id_type=MESH)
    for step in range(1, group):
        peer = lax.rem(fsdp + step, group)
        pl.semaphore_signal(barrier, inc=1, device_id=(peer, ctx), device_id_type=MESH)
    pl.semaphore_wait(barrier, 1 + group)
    per = gate_ref.shape[1]
    copies = []
    for which, (part, work) in enumerate(((gate_ref, gate_work), (up_ref, up_work))):
        mine = work.at[pl.ds(fsdp * per, per)]
        own = pltpu.make_async_copy(part.at[fsdp], mine, local_sems.at[which])
        own.start()
        copies.append(own)
        for step in range(1, group):
            peer = lax.rem(fsdp + step, group)
            copy = pltpu.make_async_remote_copy(
                src_ref=part.at[peer],
                dst_ref=mine,
                send_sem=part_sends.at[which, step - 1],
                recv_sem=part_arrivals.at[which, step - 1],
                device_id=(peer, ctx),
                device_id_type=MESH,
            )
            copy.start()
            copies.append(copy)
        if work.shape[0] > per * group:
            for row in range(per * group, work.shape[0]):
                work[row] = jnp.zeros(work.shape[1:], work.dtype)
    for which, (part, work) in enumerate(((down_ref, down_work), (rest_ref, rest_work))):
        own = pltpu.make_async_copy(part, work.at[pl.ds(0, part.shape[0])], local_sems.at[2 + which])
        own.start()
        copies.append(own)
        for row in range(part.shape[0], work.shape[0]):
            work[row] = jnp.zeros(work.shape[1:], work.dtype)
    for copy in copies:
        copy.wait()
    for stream in range(len(works)):
        ring.start(stream)

    def step(at, unused):
        ring.tick(at)
        return unused

    lax.fori_loop(0, ring.ticks, step, 0)
    ring.finish()


def padded(blocks, count):
    return -(-blocks // count) * count


def reduce_gradients(gate_part, up_part, down_part, rest_part):
    group, count = lax.axis_size("fsdp"), lax.axis_size("ctx")
    shapes = [
        (padded(group * gate_part.shape[1], count),) + gate_part.shape[2:],
        (padded(group * up_part.shape[1], count),) + up_part.shape[2:],
        (padded(down_part.shape[0], count),) + down_part.shape[1:],
        (padded(rest_part.shape[0], count),) + rest_part.shape[1:],
    ]
    return pl.pallas_call(
        reduce_kernel,
        out_shape=[jax.ShapeDtypeStruct(shape, jnp.bfloat16) for shape in shapes],
        in_specs=[pl.BlockSpec(memory_space=pl.ANY)] * 4,
        out_specs=[pl.BlockSpec(memory_space=pltpu.VMEM)] * 4,
        scratch_shapes=[pltpu.VMEM(shape, jnp.bfloat16) for shape in shapes]
        + [
            pltpu.VMEM((count - 1, shape[0] // count) + shape[1:], jnp.bfloat16) for shape in shapes
        ]
        + [
            pltpu.SemaphoreType.DMA((4, 2 * count - 2)),
            pltpu.SemaphoreType.DMA((4, 2 * count - 2)),
            pltpu.SemaphoreType.DMA((2, group - 1)),
            pltpu.SemaphoreType.DMA((2, group - 1)),
            pltpu.SemaphoreType.DMA((4,)),
        ],
        compiler_params=pltpu.CompilerParams(
            collective_id=0, has_side_effects=True, vmem_limit_bytes=56 << 20
        ),
    )(gate_part, up_part, down_part, rest_part)


def lane_blocks(matrix):
    rows, columns = matrix.shape
    return jnp.swapaxes(matrix.reshape(rows, columns // LANES, LANES), 0, 1)


def from_blocks(blocks, first, count):
    part = jnp.swapaxes(blocks[first : first + count], 0, 1)
    return part.reshape(part.shape[0], count * LANES).astype(jnp.float32)


def call(kernel, outs, *args):
    return pl.pallas_call(
        kernel,
        out_shape=outs,
        in_specs=[pl.BlockSpec(memory_space=pltpu.VMEM)] * len(args),
        out_specs=[pl.BlockSpec(memory_space=pltpu.VMEM)] * len(outs),
        compiler_params=pltpu.CompilerParams(vmem_limit_bytes=56 << 20),
    )(*args)


def unit_columns(rows, seq_count, block_len):
    groups = H // KVH
    split = rows.reshape(block_len, seq_count, KVH, groups, HD)
    return jnp.transpose(split, (1, 2, 4, 3, 0)).reshape(
        seq_count * KVH, HD, groups * block_len
    )


def unit_rows(columns, seq_count, block_len):
    groups = H // KVH
    split = columns.reshape(seq_count, KVH, HD, groups, block_len)
    return jnp.transpose(split, (4, 0, 1, 3, 2)).reshape(block_len * seq_count, H * HD)


def on_device(
    tokens, w_query, w_key, w_value, w_out, w_gate, w_up, w_down, gain_attn, gain_ffn, cotangent
):
    block_len, seq_count, width = tokens.shape
    rows_count = block_len * seq_count
    groups = H // KVH
    kv_width = KVH * HD
    own_weights = (w_query, w_key, w_value, w_out, w_gate, w_up, w_down, gain_attn, gain_ffn)
    (
        full_query,
        full_key,
        full_value,
        full_out,
        my_gate,
        my_up,
        my_down,
        full_gain_attn,
        full_gain_ffn,
    ) = (
        lax.all_gather(own_weights[0], "fsdp", axis=0, tiled=True),
        lax.all_gather(own_weights[1], "fsdp", axis=0, tiled=True),
        lax.all_gather(own_weights[2], "fsdp", axis=0, tiled=True),
        lax.all_gather(own_weights[3], "fsdp", axis=0, tiled=True),
        lax.all_to_all(own_weights[4], "fsdp", 1, 0, tiled=True),
        lax.all_to_all(own_weights[5], "fsdp", 1, 0, tiled=True),
        w_down,
        lax.all_gather(own_weights[7], "fsdp", axis=0, tiled=True),
        lax.all_gather(own_weights[8], "fsdp", axis=0, tiled=True),
    )
    my_start = lax.axis_index("ctx") * block_len
    positions = my_start + jnp.arange(block_len, dtype=jnp.int32)
    inputs = tokens.astype(jnp.float32).reshape(rows_count, width)
    scale_attn = norm_scale(inputs)
    normed_attn = (inputs * scale_attn * full_gain_attn.astype(jnp.float32)).astype(jnp.bfloat16)
    query_raw = forward_dot(normed_attn, full_query)
    key_raw = forward_dot(normed_attn, full_key)
    value_raw = forward_dot(normed_attn, full_value)
    units = seq_count * KVH
    wide = groups * block_len
    queries = (
        rotary(query_raw.reshape(block_len, seq_count, H, HD), positions, 1.0)
        .astype(jnp.bfloat16)
        .reshape(rows_count, width)
    )
    keys_local = rotary(
        key_raw.reshape(block_len, seq_count, KVH, HD), positions, 1.0
    ).astype(jnp.bfloat16)
    values_local = value_raw.astype(jnp.bfloat16).reshape(block_len, seq_count, KVH, HD)
    pairs = jnp.transpose(
        jnp.concatenate([keys_local, values_local], axis=-1), (1, 2, 0, 3)
    ).reshape(units, block_len, 2 * HD)
    all_pairs = lax.all_gather(pairs, "ctx", axis=0)
    q_unit = unit_columns(queries * jnp.bfloat16(HD ** (-0.5)), seq_count, block_len)
    q_wide = jnp.concatenate([q_unit, jnp.zeros_like(q_unit)], axis=1)
    mix_unit, log_total = call(
        attend_kernel,
        [
            jax.ShapeDtypeStruct((units, HD, wide), jnp.float32),
            jax.ShapeDtypeStruct((units, 1, wide), jnp.float32),
        ],
        q_wide,
        all_pairs,
    )
    attn_low = unit_rows(mix_unit.astype(jnp.bfloat16), seq_count, block_len)
    resid = inputs + forward_dot(attn_low, full_out)
    scale_ffn = norm_scale(resid)
    normed_ffn = (resid * scale_ffn * full_gain_ffn.astype(jnp.float32)).astype(jnp.bfloat16)
    all_normed = lax.all_gather(normed_ffn, "fsdp", axis=0, tiled=True)
    upstream_low = cotangent.reshape(rows_count, width)
    upstream = upstream_low.astype(jnp.float32)
    all_upstream = lax.all_gather(upstream_low, "fsdp", axis=0, tiled=True)
    gate = forward_dot(all_normed, my_gate)
    upward = forward_dot(all_normed, my_up)
    sigmoid_gate = jax.nn.sigmoid(gate)
    act_low = (gate * sigmoid_gate * upward).astype(jnp.bfloat16)
    ffn_out = lax.psum_scatter(
        forward_dot(act_low, my_down).astype(jnp.bfloat16), "fsdp", scatter_dimension=0, tiled=True
    ).astype(jnp.float32)
    layer_out = (resid + ffn_out).astype(jnp.bfloat16).reshape(block_len, seq_count, width)
    grad_act = backward_dot(all_upstream, my_down)
    grad_gate_low = (grad_act * upward * sigmoid_gate * (1.0 + gate * (1.0 - sigmoid_gate))).astype(
        jnp.bfloat16
    )
    grad_up_low = (grad_act * gate * sigmoid_gate).astype(jnp.bfloat16)
    grad_normed_ffn = lax.psum_scatter(
        (backward_dot(grad_gate_low, my_gate) + backward_dot(grad_up_low, my_up)).astype(
            jnp.bfloat16
        ),
        "fsdp",
        scatter_dimension=0,
        tiled=True,
    ).astype(jnp.float32)
    inward_ffn, gain_term_ffn = norm_back(
        resid, scale_ffn, full_gain_ffn.astype(jnp.float32), grad_normed_ffn
    )
    grad_resid = upstream + inward_ffn
    grad_branch = grad_resid.astype(jnp.bfloat16)
    grad_mix = backward_dot(grad_branch, full_out).astype(jnp.bfloat16)
    g_unit = unit_columns(grad_mix, seq_count, block_len)
    g_wide = jnp.concatenate([jnp.zeros_like(g_unit), g_unit], axis=1)
    q_rows, g_rows = jnp.swapaxes(q_unit, 1, 2), jnp.swapaxes(g_unit, 1, 2)
    blank = jnp.zeros_like(q_rows)
    qg = jnp.concatenate(
        [jnp.concatenate([q_rows, blank], axis=2), jnp.concatenate([blank, g_rows], axis=2)],
        axis=1,
    )
    grad_q_unit, grad_pairs = call(
        attend_back_kernel,
        [
            jax.ShapeDtypeStruct((units, HD, wide), jnp.float32),
            jax.ShapeDtypeStruct(all_pairs.shape, jnp.bfloat16),
        ],
        q_wide,
        g_wide,
        qg,
        all_pairs,
        mix_unit,
        log_total,
    )
    summed_pairs = lax.psum_scatter(grad_pairs, "ctx", scatter_dimension=0, tiled=True)
    summed_pairs = jnp.transpose(
        summed_pairs.reshape(seq_count, KVH, block_len, 2 * HD), (2, 0, 1, 3)
    )
    grad_query_low = (
        rotary(
            unit_rows(grad_q_unit, seq_count, block_len).reshape(block_len, seq_count, H, HD),
            positions,
            -1.0,
        )
        .astype(jnp.bfloat16)
        .reshape(rows_count, width)
    )
    grad_key_low = (
        rotary(summed_pairs[..., :HD].astype(jnp.float32), positions, -1.0)
        .astype(jnp.bfloat16)
        .reshape(rows_count, kv_width)
    )
    grad_value_low = summed_pairs[..., HD:].reshape(rows_count, kv_width)
    grad_normed_attn = (
        backward_dot(grad_query_low, full_query)
        + backward_dot(grad_key_low, full_key)
        + backward_dot(grad_value_low, full_value)
    )
    inward_attn, gain_term_attn = norm_back(
        inputs, scale_attn, full_gain_attn.astype(jnp.float32), grad_normed_attn
    )
    grad_tokens = (grad_resid + inward_attn).reshape(block_len, seq_count, width)

    def part(acts, grads):
        return jnp.einsum("rc,rn->cn", acts, grads, preferred_element_type=jnp.float32)

    group = lax.axis_size("fsdp")
    rest_part = lax.psum_scatter(
        jnp.concatenate(
            [
                part(normed_attn, grad_query_low),
                part(normed_attn, grad_key_low),
                part(normed_attn, grad_value_low),
                part(attn_low, grad_branch),
            ],
            axis=1,
        ).astype(jnp.bfloat16),
        "fsdp",
        scatter_dimension=0,
        tiled=True,
    )
    gate_part = part(all_normed, grad_gate_low).astype(jnp.bfloat16)
    up_part = part(all_normed, grad_up_low).astype(jnp.bfloat16)
    down_part = part(act_low, all_upstream).astype(jnp.bfloat16)

    def by_owner(matrix):
        rows, columns = matrix.shape
        split = matrix.reshape(group, rows // group, columns // LANES, LANES)
        return jnp.swapaxes(split, 1, 2)

    gate_sum, up_sum, down_sum, rest_sum = reduce_gradients(
        by_owner(gate_part),
        by_owner(up_part),
        down_part.reshape(-1, 16, width),
        lane_blocks(rest_part),
    )
    gains = lax.psum(jnp.stack([gain_term_attn, gain_term_ffn]), ("fsdp", "ctx"))
    own = gain_attn.shape[0]
    gains = lax.dynamic_slice_in_dim(gains, lax.axis_index("fsdp") * own, own, 1)
    edges = [0, width, width + kv_width, width + 2 * kv_width, 2 * width + 2 * kv_width]
    grad_query, grad_key, grad_value, grad_out = [
        from_blocks(rest_sum, first // LANES, (last - first) // LANES)
        for first, last in zip(edges[:-1], edges[1:])
    ]
    return (
        layer_out,
        grad_tokens,
        grad_query,
        grad_key,
        grad_value,
        grad_out,
        from_blocks(gate_sum, 0, FF // LANES),
        from_blocks(up_sum, 0, FF // LANES),
        down_sum.reshape(-1, width)[: w_down.shape[0]].astype(jnp.float32),
        gains[0],
        gains[1],
    )


def solution(mesh):
    return jax.shard_map(
        on_device,
        mesh=mesh,
        in_specs=(
            P("ctx", "fsdp", None),
            P("fsdp", None),
            P("fsdp", None),
            P("fsdp", None),
            P("fsdp", None),
            P("fsdp", None),
            P("fsdp", None),
            P("fsdp", None),
            P("fsdp"),
            P("fsdp"),
            P("ctx", "fsdp", None),
        ),
        out_specs=(
            P("ctx", "fsdp", None),
            P("ctx", "fsdp", None),
            P("fsdp", None),
            P("fsdp", None),
            P("fsdp", None),
            P("fsdp", None),
            P("fsdp", None),
            P("fsdp", None),
            P("fsdp", None),
            P("fsdp"),
            P("fsdp"),
        ),
        check_vma=False,
    )
```

```python
import jax
import jax.numpy as jnp
from jax import lax
from jax.experimental import pallas as pl
from jax.experimental.pallas import tpu as pltpu
from jax.sharding import PartitionSpec as P

H = 18
KVH = 6
HD = 64
FF = 3072


EPSILON = 1e-05
ROTARY_BASE = 10000.0
MASKED_SCORE = -1e30


def rotary(values, positions, direction):
    half = values.shape[-1] // 2
    freqs = ROTARY_BASE ** (-2.0 * jnp.arange(half, dtype=jnp.float32) / values.shape[-1])
    angles = positions.astype(jnp.float32)[:, None] * freqs[None, :]
    cosine = jnp.cos(angles)[:, None, :]
    sine = direction * jnp.sin(angles)[:, None, :]
    first = values[..., :half]
    second = values[..., half:]
    return jnp.concatenate(
        [first * cosine - second * sine, second * cosine + first * sine], axis=-1
    )


def norm_scale(rows):
    return lax.rsqrt(jnp.mean(rows * rows, axis=-1, keepdims=True) + EPSILON)


def norm_back(rows, scale, gain, upstream):
    scaled = upstream * gain
    inward = scale * scaled - rows * scale**3 * jnp.mean(scaled * rows, axis=-1, keepdims=True)
    return (inward, jnp.sum(upstream * rows * scale, axis=0))


def forward_dot(left, right):
    return jnp.dot(left, right, preferred_element_type=jnp.float32)


def backward_dot(grad, weight):
    return jnp.einsum("rn,cn->rc", grad, weight, preferred_element_type=jnp.float32)


def attend_back_kernel(q_ref, g_ref, qg_ref, kv_ref, mix_ref, log_ref, grad_q_ref, grad_kv_ref):
    me = lax.axis_index("ctx")
    units, deep, wide = q_ref.shape
    blocks, _, keys, _ = kv_ref.shape

    def clear(block, unused):
        grad_kv_ref[block] = jnp.zeros(grad_kv_ref.shape[1:], grad_kv_ref.dtype)
        return unused

    lax.fori_loop(me + 1, blocks, clear, 0)

    def unit_step(unit, unused):
        q, g, qg, log_total = q_ref[unit], g_ref[unit], qg_ref[unit], log_ref[unit]
        delta = jnp.sum(g[HD:].astype(jnp.float32) * mix_ref[unit], axis=0, keepdims=True)

        def back(block, grad_q, diagonal):
            kv = kv_ref[block, unit]
            scores = jnp.dot(kv, q, preferred_element_type=jnp.float32)
            probs = jnp.exp(scores - log_total)
            if diagonal:
                key_at = lax.broadcasted_iota(jnp.int32, scores.shape, 0)
                query_at = lax.rem(lax.broadcasted_iota(jnp.int32, scores.shape, 1), keys)
                probs = jnp.where(key_at <= query_at, probs, 0.0)
            grad_probs = jnp.dot(kv, g, preferred_element_type=jnp.float32)
            grad_scores = (probs * (grad_probs - delta)).astype(jnp.bfloat16)
            both = jnp.concatenate([grad_scores, probs.astype(jnp.bfloat16)], axis=1)
            grad_kv_ref[block, unit] = jnp.dot(
                both, qg, preferred_element_type=jnp.float32
            ).astype(grad_kv_ref.dtype)
            added = jnp.dot(kv.T, grad_scores, preferred_element_type=jnp.float32)
            return grad_q + added[:HD]

        grad_q = back(me, jnp.zeros((HD, wide), jnp.float32), True)
        grad_q = lax.fori_loop(0, me, lambda block, held: back(block, held, False), grad_q)
        grad_q_ref[unit] = grad_q * HD ** (-0.5)
        return unused

    lax.fori_loop(0, units, unit_step, 0)


MESH = pl.DeviceIdType.MESH
LANES = 128


def ring_place(ctx, fsdp, count):
    column, side = lax.div(ctx, 2), lax.rem(ctx, 2)
    place = column + side * (count - 1 - 2 * column)
    odd = lax.rem(fsdp, 2)
    return place + odd * (count - 1 - 2 * place)


def ring_ctx(place, fsdp, count):
    odd = lax.rem(fsdp, 2)
    place = place + odd * (count - 1 - 2 * place)
    late = lax.div(place, count // 2)
    return (1 - late) * 2 * place + late * (2 * (count - 1 - place) + 1)


def ring_neighbours(count):
    ctx, fsdp = lax.axis_index("ctx"), lax.axis_index("fsdp")
    place = ring_place(ctx, fsdp, count)
    after = ring_ctx(lax.rem(place + 1, count), fsdp, count)
    before = ring_ctx(lax.rem(place + count - 1, count), fsdp, count)
    return place, (fsdp, after), (fsdp, before)


class Ring:
    def __init__(self, count, works, landings, totals, sends, arrivals):
        self.count, self.works, self.landings, self.totals = count, works, landings, totals
        self.sends, self.arrivals = sends, arrivals
        self.place, self.after, self.before = ring_neighbours(count)
        self.ticks = 2 * count - 2

    def chunk(self, held, index):
        per = held.shape[0] // self.count
        return held.at[pl.ds(index * per, per)]

    def copy(self, stream, step, index, summing):
        source = self.chunk((self.works if summing else self.totals)[stream], index)
        target = self.landings[stream].at[step] if summing else source
        return pltpu.make_async_remote_copy(
            src_ref=source,
            dst_ref=target,
            send_sem=self.sends.at[stream, step],
            recv_sem=self.arrivals.at[stream, step],
            device_id=self.after,
            device_id_type=MESH,
        )

    def start(self, stream):
        self.copy(stream, 0, self.place, True).start()

    def tick(self, step):
        index = lax.rem(self.place + 3 * self.count - 1 - step, self.count)
        last = self.count - 2
        for stream in range(len(self.works)):
            self.copy(stream, step, index, False).wait_recv()

            def add(target, stream=stream):
                part = self.chunk(self.works[stream], index)
                landed = self.landings[stream].at[jnp.minimum(step, last)]
                for row in range(part.shape[0]):
                    target[row] = (
                        part[row].astype(jnp.float32) + landed[row].astype(jnp.float32)
                    ).astype(part.dtype)

            @pl.when(step < last)
            def _():
                add(self.chunk(self.works[stream], index))
                self.copy(stream, jnp.minimum(step + 1, last), index, True).start()

            @pl.when(step == last)
            def _():
                add(self.chunk(self.totals[stream], index))

            @pl.when(jnp.logical_and(step >= last, step < self.ticks - 1))
            def _():
                self.copy(stream, jnp.minimum(step + 1, self.ticks - 1), index, False).start()

    def finish(self):
        def wait(step, unused):
            for stream in range(len(self.works)):
                self.copy(stream, step, self.place, False).wait_send()
            return unused

        lax.fori_loop(0, self.ticks, wait, 0)


def reduce_kernel(
    gate_ref, up_ref, down_ref, rest_ref, gate_total, up_total, down_total, rest_total,
    gate_work, up_work, down_work, rest_work, gate_land, up_land, down_land, rest_land,
    sends, arrivals, part_sends, part_arrivals, local_sems,
):
    fsdp, ctx = lax.axis_index("fsdp"), lax.axis_index("ctx")
    group, count = lax.axis_size("fsdp"), lax.axis_size("ctx")
    works = [gate_work, up_work, down_work, rest_work]
    landings = [gate_land, up_land, down_land, rest_land]
    totals = [gate_total, up_total, down_total, rest_total]
    ring = Ring(count, works, landings, totals, sends, arrivals)
    barrier = pltpu.get_barrier_semaphore()
    for device in (ring.after, ring.before):
        pl.semaphore_signal(barrier, inc=1, device_id=device, device_id_type=MESH)
    for step in range(1, group):
        peer = lax.rem(fsdp + step, group)
        pl.semaphore_signal(barrier, inc=1, device_id=(peer, ctx), device_id_type=MESH)
    pl.semaphore_wait(barrier, 1 + group)
    per = gate_ref.shape[1]
    copies = []
    for which, (part, work) in enumerate(((gate_ref, gate_work), (up_ref, up_work))):
        mine = work.at[pl.ds(fsdp * per, per)]
        own = pltpu.make_async_copy(part.at[fsdp], mine, local_sems.at[which])
        own.start()
        copies.append(own)
        for step in range(1, group):
            peer = lax.rem(fsdp + step, group)
            copy = pltpu.make_async_remote_copy(
                src_ref=part.at[peer],
                dst_ref=mine,
                send_sem=part_sends.at[which, step - 1],
                recv_sem=part_arrivals.at[which, step - 1],
                device_id=(peer, ctx),
                device_id_type=MESH,
            )
            copy.start()
            copies.append(copy)
        if work.shape[0] > per * group:
            for row in range(per * group, work.shape[0]):
                work[row] = jnp.zeros(work.shape[1:], work.dtype)
    for which, (part, work) in enumerate(((down_ref, down_work), (rest_ref, rest_work))):
        own = pltpu.make_async_copy(part, work.at[pl.ds(0, part.shape[0])], local_sems.at[2 + which])
        own.start()
        copies.append(own)
        for row in range(part.shape[0], work.shape[0]):
            work[row] = jnp.zeros(work.shape[1:], work.dtype)
    for copy in copies:
        copy.wait()
    for stream in range(len(works)):
        ring.start(stream)

    def step(at, unused):
        ring.tick(at)
        return unused

    lax.fori_loop(0, ring.ticks, step, 0)
    ring.finish()


def padded(blocks, count):
    return -(-blocks // count) * count


def reduce_gradients(gate_part, up_part, down_part, rest_part):
    group, count = lax.axis_size("fsdp"), lax.axis_size("ctx")
    shapes = [
        (padded(group * gate_part.shape[1], count),) + gate_part.shape[2:],
        (padded(group * up_part.shape[1], count),) + up_part.shape[2:],
        (padded(down_part.shape[0], count),) + down_part.shape[1:],
        (padded(rest_part.shape[0], count),) + rest_part.shape[1:],
    ]
    return pl.pallas_call(
        reduce_kernel,
        out_shape=[jax.ShapeDtypeStruct(shape, jnp.bfloat16) for shape in shapes],
        in_specs=[pl.BlockSpec(memory_space=pl.ANY)] * 4,
        out_specs=[pl.BlockSpec(memory_space=pltpu.VMEM)] * 4,
        scratch_shapes=[pltpu.VMEM(shape, jnp.bfloat16) for shape in shapes]
        + [
            pltpu.VMEM((count - 1, shape[0] // count) + shape[1:], jnp.bfloat16) for shape in shapes
        ]
        + [
            pltpu.SemaphoreType.DMA((4, 2 * count - 2)),
            pltpu.SemaphoreType.DMA((4, 2 * count - 2)),
            pltpu.SemaphoreType.DMA((2, group - 1)),
            pltpu.SemaphoreType.DMA((2, group - 1)),
            pltpu.SemaphoreType.DMA((4,)),
        ],
        compiler_params=pltpu.CompilerParams(
            collective_id=0, has_side_effects=True, vmem_limit_bytes=56 << 20
        ),
    )(gate_part, up_part, down_part, rest_part)


def lane_blocks(matrix):
    rows, columns = matrix.shape
    return jnp.swapaxes(matrix.reshape(rows, columns // LANES, LANES), 0, 1)


def from_blocks(blocks, first, count):
    part = jnp.swapaxes(blocks[first : first + count], 0, 1)
    return part.reshape(part.shape[0], count * LANES).astype(jnp.float32)


class GroupGather:
    def __init__(self, shard_of, sends, arrivals):
        self.shard_of, self.sends, self.arrivals = shard_of, sends, arrivals
        self.fsdp, self.ctx = lax.axis_index("fsdp"), lax.axis_index("ctx")
        self.chips = lax.axis_size("fsdp") // 2
        self.chip, self.core = lax.div(self.fsdp, 2), lax.rem(self.fsdp, 2)
        self.sibling = 2 * self.chip + 1 - self.core

    def copy(self, source, shard, semaphore, device):
        return pltpu.make_async_remote_copy(
            src_ref=source,
            dst_ref=self.shard_of(shard),
            send_sem=self.sends.at[semaphore],
            recv_sem=self.arrivals.at[semaphore],
            device_id=(device, self.ctx),
            device_id_type=MESH,
        )

    def same_core(self, step):
        return 2 * lax.rem(self.chip + step, self.chips) + self.core

    def across(self, source):
        return self.copy(source, self.fsdp, 0, self.sibling)

    def out(self, source, step):
        return self.copy(source, self.fsdp, step, self.same_core(step))

    def onward(self, step):
        shard = self.same_core(self.chips - step)
        return self.copy(self.shard_of(shard), shard, self.chips - 1 + step, self.sibling)

    def start(self, source):
        for step in range(1, self.chips):
            self.out(source, step).start()
        self.across(source).start()

    def forward(self):
        own = self.shard_of(self.fsdp)
        for step in range(1, self.chips):
            self.out(own, step).wait_recv()
            self.onward(step).start()

    def sibling_here(self):
        self.across(self.shard_of(self.fsdp)).wait_recv()

    def crossed(self, step):
        self.onward(step).wait_recv()

    def sent(self):
        own = self.shard_of(self.fsdp)
        self.across(own).wait_send()
        for step in range(1, self.chips):
            self.out(own, step).wait_send()
            self.onward(step).wait_send()

    def finish(self):
        self.forward()
        self.sibling_here()
        for step in range(1, self.chips):
            self.crossed(step)
        self.sent()


def group_semaphores():
    return pltpu.SemaphoreType.DMA((lax.axis_size("fsdp") - 1,))


def greet_group(barrier):
    fsdp, ctx, group = lax.axis_index("fsdp"), lax.axis_index("ctx"), lax.axis_size("fsdp")
    for step in range(1, group):
        peer = lax.rem(fsdp + step, group)
        pl.semaphore_signal(barrier, inc=1, device_id=(peer, ctx), device_id_type=MESH)
    return group - 1


class Steps:
    def __init__(self):
        self.fsdp, self.ctx = lax.axis_index("fsdp"), lax.axis_index("ctx")
        self.levels = lax.axis_size("ctx") // 2
        self.level, self.side = lax.div(self.ctx, 2), lax.rem(self.ctx, 2)
        self.peer = (self.fsdp, 2 * self.level + 1 - self.side)
        self.above = (self.fsdp, lax.rem(self.ctx + 2, 2 * self.levels))
        self.below = (self.fsdp, lax.rem(self.ctx + 2 * self.levels - 2, 2 * self.levels))
        self.has_above = self.level + 1 < self.levels
        self.has_below = self.level > 0

    def greet(self, barrier):
        pl.semaphore_signal(barrier, inc=1, device_id=self.peer, device_id_type=MESH)

        @pl.when(self.has_above)
        def _():
            pl.semaphore_signal(barrier, inc=1, device_id=self.above, device_id_type=MESH)

        @pl.when(self.has_below)
        def _():
            pl.semaphore_signal(barrier, inc=1, device_id=self.below, device_id_type=MESH)

        return 1 + jnp.minimum(self.level, 1) + jnp.minimum(self.levels - 1 - self.level, 1)


PARTS = 2


def causal(keys, wide, shape):
    key_at = lax.broadcasted_iota(jnp.int32, shape, 0)
    query_at = lax.rem(lax.broadcasted_iota(jnp.int32, shape, 1), keys)
    return key_at <= query_at


def attend_kernel(
    q_ref, kv_ref, out_ref, gate_ref, up_ref,
    low_ref, mix_ref, log_ref, all_ref, full_out_ref, my_gate_ref, my_up_ref,
    top_ref, total_ref, chain_sends, chain_arrivals, peer_sends, peer_arrivals,
    out_sends, out_arrivals, part_sends, part_arrivals, local_sems,
):
    steps = Steps()
    fsdp, ctx, group = steps.fsdp, steps.ctx, lax.axis_size("fsdp")
    units, deep, wide = q_ref.shape
    keys = kv_ref.shape[1]
    per_part = units // PARTS
    barrier = pltpu.get_barrier_semaphore()
    greeted = steps.greet(barrier) + greet_group(barrier)
    all_ref[ctx] = kv_ref[...]
    pl.semaphore_wait(barrier, greeted)

    def block_copy(level, part, side, semaphores, arrivals, arrives, device):
        block = 2 * (steps.level - level) + side
        held = all_ref.at[block, pl.ds(part * per_part, per_part)]
        return pltpu.make_async_remote_copy(
            src_ref=held,
            dst_ref=held,
            send_sem=semaphores.at[level, part],
            recv_sem=arrivals.at[arrives, part],
            device_id=device,
            device_id_type=MESH,
        )

    def chain(level, part):
        return block_copy(
            level, part, steps.side, chain_sends, chain_arrivals, level + 1, steps.above
        )

    def across(level, part):
        return block_copy(
            level, part, steps.side, peer_sends, peer_arrivals, level, steps.peer
        )

    def pass_on(level, part):
        @pl.when(steps.has_above)
        def _():
            chain(level, part).start()

    for part in range(PARTS):
        pass_on(0, part)

        @pl.when(steps.side == 0)
        def _():
            across(0, part).start()

    rows = out_ref.shape[0]
    columns = my_gate_ref.shape[1]
    gathered = GroupGather(
        lambda shard: full_out_ref.at[pl.ds(shard * rows, rows)], out_sends, out_arrivals
    )
    gathered.start(out_ref)
    background = []
    own_rows = pl.ds(fsdp * rows, rows)
    own_out = pltpu.make_async_copy(out_ref, full_out_ref.at[own_rows], local_sems.at[2])
    own_out.start()
    background.append(own_out)
    for which, (source, target) in enumerate(((gate_ref, my_gate_ref), (up_ref, my_up_ref))):
        for step in range(1, group):
            peer = lax.rem(fsdp + step, group)
            copy = pltpu.make_async_remote_copy(
                src_ref=source.at[:, pl.ds(pl.multiple_of(peer * columns, LANES), columns)],
                dst_ref=target.at[own_rows],
                send_sem=part_sends.at[which, step - 1],
                recv_sem=part_arrivals.at[which, step - 1],
                device_id=(peer, ctx),
                device_id_type=MESH,
            )
            copy.start()
            background.append(copy)
        own = pltpu.make_async_copy(
            source.at[:, pl.ds(pl.multiple_of(fsdp * columns, LANES), columns)],
            target.at[own_rows],
            local_sems.at[which],
        )
        own.start()
        background.append(own)

    def add(unit, kv):
        scores = jnp.dot(kv, q_ref[unit], preferred_element_type=jnp.float32)
        top = top_ref[unit]
        new_top = jnp.maximum(top, jnp.max(scores, axis=0, keepdims=True))
        fade = jnp.exp(top - new_top)
        weights = jnp.exp(scores - new_top)
        top_ref[unit] = new_top
        total_ref[unit] = total_ref[unit] * fade + jnp.sum(weights, axis=0, keepdims=True)
        added = jnp.dot(kv.T, weights.astype(jnp.bfloat16), preferred_element_type=jnp.float32)
        mix_ref[unit] = mix_ref[unit] * fade + added[HD:]

    def over_units(body, first, count):
        def two(at, unused):
            body(first + 2 * at)
            body(first + 2 * at + 1)
            return unused

        lax.fori_loop(0, count // 2, two, 0)

    def diagonal(unit):
        kv = kv_ref[unit]
        scores = jnp.dot(kv, q_ref[unit], preferred_element_type=jnp.float32)
        scores = jnp.where(causal(keys, wide, scores.shape), scores, MASKED_SCORE)
        top = jnp.max(scores, axis=0, keepdims=True)
        weights = jnp.exp(scores - top)
        top_ref[unit] = top
        total_ref[unit] = jnp.sum(weights, axis=0, keepdims=True)
        added = jnp.dot(kv.T, weights.astype(jnp.bfloat16), preferred_element_type=jnp.float32)
        mix_ref[unit] = added[HD:]

    over_units(diagonal, 0, units)

    @pl.when(steps.side == 1)
    def _():
        for part in range(PARTS):
            across(0, part).wait_recv()
            over_units(lambda unit: add(unit, all_ref[ctx - 1, unit]), part * per_part, per_part)

    def level_step(level, unused):
        for part in range(PARTS):
            chain(level - 1, part).wait_recv()
            pass_on(level, part)
            across(level, part).start()
        first = 2 * (steps.level - level)
        for part in range(PARTS):
            across(level, part).wait_recv()
            over_units(
                lambda unit: add(unit, all_ref[pl.ds(first, 2), unit].reshape(2 * keys, deep)),
                part * per_part,
                per_part,
            )
        return unused

    lax.fori_loop(1, steps.level + 1, level_step, 0)

    def close(unit):
        total = total_ref[unit]
        mix_ref[unit] = mix_ref[unit] / total
        log_ref[unit] = top_ref[unit] + jnp.log(total)

    over_units(close, 0, units)
    groups = wide // keys
    for sequence in range(units // KVH):
        for pair in range(H // 2):
            heads = []
            for head in (2 * pair, 2 * pair + 1):
                unit, member = sequence * KVH + head // groups, head % groups
                heads.append(mix_ref[unit, :, member * keys : (member + 1) * keys])
            tile = jnp.concatenate(heads, axis=0).T
            low_ref[
                sequence * keys : (sequence + 1) * keys, pair * 2 * HD : (pair + 1) * 2 * HD
            ] = tile.astype(low_ref.dtype)
    gathered.finish()
    for copy in background:
        copy.wait()

    def sent(level, unused):
        for part in range(PARTS):

            @pl.when(steps.has_above)
            def _():
                chain(level, part).wait_send()

            @pl.when(jnp.logical_or(level > 0, steps.side == 0))
            def _():
                across(level, part).wait_send()

        return unused

    lax.fori_loop(0, steps.level + 1, sent, 0)


ANY = pl.BlockSpec(memory_space=pl.ANY)
VMEM = pl.BlockSpec(memory_space=pltpu.VMEM)


def attend(q_wide, pairs, w_out, w_gate, w_up):
    group, count = lax.axis_size("fsdp"), lax.axis_size("ctx")
    units, deep, wide = q_wide.shape
    keys = pairs.shape[1]
    rows, width = w_out.shape
    hidden = w_gate.shape[1] // group
    dma = pltpu.SemaphoreType.DMA
    sequences = units // KVH
    return pl.pallas_call(
        attend_kernel,
        out_shape=[
            jax.ShapeDtypeStruct((sequences * keys, width), jnp.bfloat16),
            jax.ShapeDtypeStruct((units, HD, wide), jnp.float32),
            jax.ShapeDtypeStruct((units, 1, wide), jnp.float32),
            jax.ShapeDtypeStruct((count,) + pairs.shape, jnp.bfloat16),
            jax.ShapeDtypeStruct((group * rows, width), jnp.bfloat16),
            jax.ShapeDtypeStruct((group * rows, hidden), jnp.bfloat16),
            jax.ShapeDtypeStruct((group * rows, hidden), jnp.bfloat16),
        ],
        in_specs=[VMEM, VMEM, ANY, ANY, ANY],
        out_specs=[VMEM, VMEM, VMEM, VMEM, ANY, ANY, ANY],
        scratch_shapes=[
            pltpu.VMEM((units, 1, wide), jnp.float32),
            pltpu.VMEM((units, 1, wide), jnp.float32),
            dma((count // 2, PARTS)),
            dma((count // 2 + 1, PARTS)),
            dma((count // 2, PARTS)),
            dma((count // 2, PARTS)),
            group_semaphores(),
            group_semaphores(),
            dma((2, group - 1)),
            dma((2, group - 1)),
            dma((3,)),
        ],
        compiler_params=pltpu.CompilerParams(
            collective_id=1, has_side_effects=True, vmem_limit_bytes=56 << 20
        ),
    )(q_wide, pairs, w_out, w_gate, w_up)


def call(kernel, outs, *args):
    return pl.pallas_call(
        kernel,
        out_shape=outs,
        in_specs=[pl.BlockSpec(memory_space=pltpu.VMEM)] * len(args),
        out_specs=[pl.BlockSpec(memory_space=pltpu.VMEM)] * len(outs),
        compiler_params=pltpu.CompilerParams(vmem_limit_bytes=56 << 20),
    )(*args)


def unit_columns(rows, seq_count, block_len):
    groups = H // KVH
    split = rows.reshape(seq_count, block_len, KVH, groups, HD)
    return jnp.transpose(split, (0, 2, 4, 3, 1)).reshape(
        seq_count * KVH, HD, groups * block_len
    )


def unit_rows(columns, seq_count, block_len):
    groups = H // KVH
    split = columns.reshape(seq_count, KVH, HD, groups, block_len)
    return jnp.transpose(split, (0, 4, 1, 3, 2)).reshape(seq_count * block_len, H * HD)


def on_device(
    tokens, w_query, w_key, w_value, w_out, w_gate, w_up, w_down, gain_attn, gain_ffn, cotangent
):
    block_len, seq_count, width = tokens.shape
    rows_count = block_len * seq_count
    kv_width = KVH * HD
    full_query, full_key, full_value = [
        lax.all_gather(weight, "fsdp", axis=0, tiled=True) for weight in (w_query, w_key, w_value)
    ]
    full_gain_attn, full_gain_ffn = [
        lax.all_gather(gain, "fsdp", axis=0, tiled=True) for gain in (gain_attn, gain_ffn)
    ]
    my_down = w_down
    my_start = lax.axis_index("ctx") * block_len
    positions = my_start + jnp.arange(block_len, dtype=jnp.int32)
    inputs = jnp.swapaxes(tokens, 0, 1).reshape(rows_count, width).astype(jnp.float32)
    scale_attn = norm_scale(inputs)
    normed_attn = (inputs * scale_attn * full_gain_attn.astype(jnp.float32)).astype(jnp.bfloat16)
    query_raw = forward_dot(normed_attn, full_query)
    key_raw = forward_dot(normed_attn, full_key)
    value_raw = forward_dot(normed_attn, full_value)
    units = seq_count * KVH
    wide = H // KVH * block_len
    queries = (
        rotary(query_raw.reshape(seq_count, block_len, H, HD), positions, 1.0)
        .astype(jnp.bfloat16)
        .reshape(rows_count, width)
    )
    keys_local = rotary(
        key_raw.reshape(seq_count, block_len, KVH, HD), positions, 1.0
    ).astype(jnp.bfloat16)
    values_local = value_raw.astype(jnp.bfloat16).reshape(seq_count, block_len, KVH, HD)
    pairs = jnp.swapaxes(
        jnp.concatenate([keys_local, values_local], axis=-1), 1, 2
    ).reshape(units, block_len, 2 * HD)
    q_unit = unit_columns(queries * jnp.bfloat16(HD ** (-0.5)), seq_count, block_len)
    q_wide = jnp.concatenate([q_unit, jnp.zeros_like(q_unit)], axis=1)
    attn_low, mix_unit, log_total, all_pairs, full_out, my_gate, my_up = attend(
        q_wide, pairs, w_out, w_gate, w_up
    )
    resid = inputs + forward_dot(attn_low, full_out)
    scale_ffn = norm_scale(resid)
    normed_ffn = (resid * scale_ffn * full_gain_ffn.astype(jnp.float32)).astype(jnp.bfloat16)
    all_normed = lax.all_gather(normed_ffn, "fsdp", axis=0, tiled=True)
    upstream_low = jnp.swapaxes(cotangent, 0, 1).reshape(rows_count, width)
    upstream = upstream_low.astype(jnp.float32)
    all_upstream = lax.all_gather(upstream_low, "fsdp", axis=0, tiled=True)
    gate = forward_dot(all_normed, my_gate)
    upward = forward_dot(all_normed, my_up)
    sigmoid_gate = jax.nn.sigmoid(gate)
    act_low = (gate * sigmoid_gate * upward).astype(jnp.bfloat16)
    ffn_out = lax.psum_scatter(
        forward_dot(act_low, my_down).astype(jnp.bfloat16), "fsdp", scatter_dimension=0, tiled=True
    ).astype(jnp.float32)
    layer_out = (resid + ffn_out).astype(jnp.bfloat16).reshape(seq_count, block_len, width)
    grad_act = backward_dot(all_upstream, my_down)
    grad_gate_low = (grad_act * upward * sigmoid_gate * (1.0 + gate * (1.0 - sigmoid_gate))).astype(
        jnp.bfloat16
    )
    grad_up_low = (grad_act * gate * sigmoid_gate).astype(jnp.bfloat16)
    grad_normed_ffn = lax.psum_scatter(
        (backward_dot(grad_gate_low, my_gate) + backward_dot(grad_up_low, my_up)).astype(
            jnp.bfloat16
        ),
        "fsdp",
        scatter_dimension=0,
        tiled=True,
    ).astype(jnp.float32)
    inward_ffn, gain_term_ffn = norm_back(
        resid, scale_ffn, full_gain_ffn.astype(jnp.float32), grad_normed_ffn
    )
    grad_resid = upstream + inward_ffn
    grad_branch = grad_resid.astype(jnp.bfloat16)
    grad_mix = backward_dot(grad_branch, full_out).astype(jnp.bfloat16)
    g_unit = unit_columns(grad_mix, seq_count, block_len)
    g_wide = jnp.concatenate([jnp.zeros_like(g_unit), g_unit], axis=1)
    q_rows, g_rows = jnp.swapaxes(q_unit, 1, 2), jnp.swapaxes(g_unit, 1, 2)
    blank = jnp.zeros_like(q_rows)
    qg = jnp.concatenate(
        [jnp.concatenate([q_rows, blank], axis=2), jnp.concatenate([blank, g_rows], axis=2)],
        axis=1,
    )
    grad_q_unit, grad_pairs = call(
        attend_back_kernel,
        [
            jax.ShapeDtypeStruct((units, HD, wide), jnp.float32),
            jax.ShapeDtypeStruct(all_pairs.shape, jnp.bfloat16),
        ],
        q_wide,
        g_wide,
        qg,
        all_pairs,
        mix_unit,
        log_total,
    )
    summed_pairs = lax.psum_scatter(grad_pairs, "ctx", scatter_dimension=0, tiled=True)
    summed_pairs = jnp.transpose(
        summed_pairs.reshape(seq_count, KVH, block_len, 2 * HD), (0, 2, 1, 3)
    )
    grad_query_low = (
        rotary(
            unit_rows(grad_q_unit, seq_count, block_len).reshape(seq_count, block_len, H, HD),
            positions,
            -1.0,
        )
        .astype(jnp.bfloat16)
        .reshape(rows_count, width)
    )
    grad_key_low = (
        rotary(summed_pairs[..., :HD].astype(jnp.float32), positions, -1.0)
        .astype(jnp.bfloat16)
        .reshape(rows_count, kv_width)
    )
    grad_value_low = summed_pairs[..., HD:].reshape(rows_count, kv_width)
    grad_normed_attn = (
        backward_dot(grad_query_low, full_query)
        + backward_dot(grad_key_low, full_key)
        + backward_dot(grad_value_low, full_value)
    )
    inward_attn, gain_term_attn = norm_back(
        inputs, scale_attn, full_gain_attn.astype(jnp.float32), grad_normed_attn
    )
    grad_tokens = (grad_resid + inward_attn).reshape(seq_count, block_len, width)

    def part(acts, grads):
        return jnp.einsum("rc,rn->cn", acts, grads, preferred_element_type=jnp.float32)

    group = lax.axis_size("fsdp")
    rest_part = lax.psum_scatter(
        jnp.concatenate(
            [
                part(normed_attn, grad_query_low),
                part(normed_attn, grad_key_low),
                part(normed_attn, grad_value_low),
                part(attn_low, grad_branch),
            ],
            axis=1,
        ).astype(jnp.bfloat16),
        "fsdp",
        scatter_dimension=0,
        tiled=True,
    )
    gate_part = part(all_normed, grad_gate_low).astype(jnp.bfloat16)
    up_part = part(all_normed, grad_up_low).astype(jnp.bfloat16)
    down_part = part(act_low, all_upstream).astype(jnp.bfloat16)

    def by_owner(matrix):
        rows, columns = matrix.shape
        split = matrix.reshape(group, rows // group, columns // LANES, LANES)
        return jnp.swapaxes(split, 1, 2)

    gate_sum, up_sum, down_sum, rest_sum = reduce_gradients(
        by_owner(gate_part),
        by_owner(up_part),
        down_part.reshape(-1, 16, width),
        lane_blocks(rest_part),
    )
    gains = lax.psum(jnp.stack([gain_term_attn, gain_term_ffn]), ("fsdp", "ctx"))
    own = gain_attn.shape[0]
    gains = lax.dynamic_slice_in_dim(gains, lax.axis_index("fsdp") * own, own, 1)
    edges = [0, width, width + kv_width, width + 2 * kv_width, 2 * width + 2 * kv_width]
    grad_query, grad_key, grad_value, grad_out = [
        from_blocks(rest_sum, first // LANES, (last - first) // LANES)
        for first, last in zip(edges[:-1], edges[1:])
    ]
    return (
        jnp.swapaxes(layer_out, 0, 1),
        jnp.swapaxes(grad_tokens, 0, 1),
        grad_query,
        grad_key,
        grad_value,
        grad_out,
        from_blocks(gate_sum, 0, FF // LANES),
        from_blocks(up_sum, 0, FF // LANES),
        down_sum.reshape(-1, width)[: w_down.shape[0]].astype(jnp.float32),
        gains[0],
        gains[1],
    )


def solution(mesh):
    return jax.shard_map(
        on_device,
        mesh=mesh,
        in_specs=(
            P("ctx", "fsdp", None),
            P("fsdp", None),
            P("fsdp", None),
            P("fsdp", None),
            P("fsdp", None),
            P("fsdp", None),
            P("fsdp", None),
            P("fsdp", None),
            P("fsdp"),
            P("fsdp"),
            P("ctx", "fsdp", None),
        ),
        out_specs=(
            P("ctx", "fsdp", None),
            P("ctx", "fsdp", None),
            P("fsdp", None),
            P("fsdp", None),
            P("fsdp", None),
            P("fsdp", None),
            P("fsdp", None),
            P("fsdp", None),
            P("fsdp", None),
            P("fsdp"),
            P("fsdp"),
        ),
        check_vma=False,
    )
```

```python
import jax
import jax.numpy as jnp
from jax import lax
from jax.experimental import pallas as pl
from jax.experimental.pallas import tpu as pltpu
from jax.sharding import PartitionSpec as P

H = 18
KVH = 6
HD = 64
FF = 3072


EPSILON = 1e-05
ROTARY_BASE = 10000.0
MASKED_SCORE = -1e30


def rotary(values, positions, direction):
    half = values.shape[-1] // 2
    freqs = ROTARY_BASE ** (-2.0 * jnp.arange(half, dtype=jnp.float32) / values.shape[-1])
    angles = positions.astype(jnp.float32)[:, None] * freqs[None, :]
    cosine = jnp.cos(angles)[:, None, :]
    sine = direction * jnp.sin(angles)[:, None, :]
    first = values[..., :half]
    second = values[..., half:]
    return jnp.concatenate(
        [first * cosine - second * sine, second * cosine + first * sine], axis=-1
    )


def norm_scale(rows):
    return lax.rsqrt(jnp.mean(rows * rows, axis=-1, keepdims=True) + EPSILON)


def norm_back(rows, scale, gain, upstream):
    scaled = upstream * gain
    inward = scale * scaled - rows * scale**3 * jnp.mean(scaled * rows, axis=-1, keepdims=True)
    return (inward, jnp.sum(upstream * rows * scale, axis=0))


def forward_dot(left, right):
    return jnp.dot(left, right, preferred_element_type=jnp.float32)


def backward_dot(grad, weight):
    return jnp.einsum("rn,cn->rc", grad, weight, preferred_element_type=jnp.float32)


def attend_back_kernel(q_ref, g_ref, qg_ref, kv_ref, mix_ref, log_ref, grad_q_ref, grad_kv_ref):
    me = lax.axis_index("ctx")
    units, deep, wide = q_ref.shape
    blocks, _, keys, _ = kv_ref.shape

    def clear(block, unused):
        grad_kv_ref[block] = jnp.zeros(grad_kv_ref.shape[1:], grad_kv_ref.dtype)
        return unused

    lax.fori_loop(me + 1, blocks, clear, 0)

    def unit_step(unit, unused):
        q, g, qg, log_total = q_ref[unit], g_ref[unit], qg_ref[unit], log_ref[unit]
        delta = jnp.sum(g[HD:].astype(jnp.float32) * mix_ref[unit], axis=0, keepdims=True)

        def back(block, grad_q, diagonal):
            kv = kv_ref[block, unit]
            scores = jnp.dot(kv, q, preferred_element_type=jnp.float32)
            probs = jnp.exp(scores - log_total)
            if diagonal:
                key_at = lax.broadcasted_iota(jnp.int32, scores.shape, 0)
                query_at = lax.rem(lax.broadcasted_iota(jnp.int32, scores.shape, 1), keys)
                probs = jnp.where(key_at <= query_at, probs, 0.0)
            grad_probs = jnp.dot(kv, g, preferred_element_type=jnp.float32)
            grad_scores = (probs * (grad_probs - delta)).astype(jnp.bfloat16)
            both = jnp.concatenate([grad_scores, probs.astype(jnp.bfloat16)], axis=1)
            grad_kv_ref[block, unit] = jnp.dot(
                both, qg, preferred_element_type=jnp.float32
            ).astype(grad_kv_ref.dtype)
            added = jnp.dot(kv.T, grad_scores, preferred_element_type=jnp.float32)
            return grad_q + added[:HD]

        grad_q = back(me, jnp.zeros((HD, wide), jnp.float32), True)
        grad_q = lax.fori_loop(0, me, lambda block, held: back(block, held, False), grad_q)
        grad_q_ref[unit] = grad_q * HD ** (-0.5)
        return unused

    lax.fori_loop(0, units, unit_step, 0)


MESH = pl.DeviceIdType.MESH
LANES = 128


def ring_place(ctx, fsdp, count):
    column, side = lax.div(ctx, 2), lax.rem(ctx, 2)
    place = column + side * (count - 1 - 2 * column)
    odd = lax.rem(fsdp, 2)
    return place + odd * (count - 1 - 2 * place)


def ring_ctx(place, fsdp, count):
    odd = lax.rem(fsdp, 2)
    place = place + odd * (count - 1 - 2 * place)
    late = lax.div(place, count // 2)
    return (1 - late) * 2 * place + late * (2 * (count - 1 - place) + 1)


def ring_neighbours(count):
    ctx, fsdp = lax.axis_index("ctx"), lax.axis_index("fsdp")
    place = ring_place(ctx, fsdp, count)
    after = ring_ctx(lax.rem(place + 1, count), fsdp, count)
    before = ring_ctx(lax.rem(place + count - 1, count), fsdp, count)
    return place, (fsdp, after), (fsdp, before)


class Ring:
    def __init__(self, count, works, landings, totals, sends, arrivals):
        self.count, self.works, self.landings, self.totals = count, works, landings, totals
        self.sends, self.arrivals = sends, arrivals
        self.place, self.after, self.before = ring_neighbours(count)
        self.ticks = 2 * count - 2

    def chunk(self, held, index):
        per = held.shape[0] // self.count
        return held.at[pl.ds(index * per, per)]

    def copy(self, stream, step, index, summing):
        source = self.chunk((self.works if summing else self.totals)[stream], index)
        target = self.landings[stream].at[step] if summing else source
        return pltpu.make_async_remote_copy(
            src_ref=source,
            dst_ref=target,
            send_sem=self.sends.at[stream, step],
            recv_sem=self.arrivals.at[stream, step],
            device_id=self.after,
            device_id_type=MESH,
        )

    def start(self, stream):
        self.copy(stream, 0, self.place, True).start()

    def tick(self, step):
        index = lax.rem(self.place + 3 * self.count - 1 - step, self.count)
        last = self.count - 2
        for stream in range(len(self.works)):
            self.copy(stream, step, index, False).wait_recv()

            def add(target, stream=stream):
                part = self.chunk(self.works[stream], index)
                landed = self.landings[stream].at[jnp.minimum(step, last)]
                for row in range(part.shape[0]):
                    target[row] = (
                        part[row].astype(jnp.float32) + landed[row].astype(jnp.float32)
                    ).astype(part.dtype)

            @pl.when(step < last)
            def _():
                add(self.chunk(self.works[stream], index))
                self.copy(stream, jnp.minimum(step + 1, last), index, True).start()

            @pl.when(step == last)
            def _():
                add(self.chunk(self.totals[stream], index))

            @pl.when(jnp.logical_and(step >= last, step < self.ticks - 1))
            def _():
                self.copy(stream, jnp.minimum(step + 1, self.ticks - 1), index, False).start()

    def finish(self):
        def wait(step, unused):
            for stream in range(len(self.works)):
                self.copy(stream, step, self.place, False).wait_send()
            return unused

        lax.fori_loop(0, self.ticks, wait, 0)


def reduce_kernel(
    gate_ref, up_ref, down_ref, rest_ref, gate_total, up_total, down_total, rest_total,
    gate_work, up_work, down_work, rest_work, gate_land, up_land, down_land, rest_land,
    sends, arrivals, part_sends, part_arrivals, local_sems,
):
    fsdp, ctx = lax.axis_index("fsdp"), lax.axis_index("ctx")
    group, count = lax.axis_size("fsdp"), lax.axis_size("ctx")
    works = [gate_work, up_work, down_work, rest_work]
    landings = [gate_land, up_land, down_land, rest_land]
    totals = [gate_total, up_total, down_total, rest_total]
    ring = Ring(count, works, landings, totals, sends, arrivals)
    barrier = pltpu.get_barrier_semaphore()
    for device in (ring.after, ring.before):
        pl.semaphore_signal(barrier, inc=1, device_id=device, device_id_type=MESH)
    for step in range(1, group):
        peer = lax.rem(fsdp + step, group)
        pl.semaphore_signal(barrier, inc=1, device_id=(peer, ctx), device_id_type=MESH)
    pl.semaphore_wait(barrier, 1 + group)
    per = gate_ref.shape[1]
    copies = []
    for which, (part, work) in enumerate(((gate_ref, gate_work), (up_ref, up_work))):
        mine = work.at[pl.ds(fsdp * per, per)]
        own = pltpu.make_async_copy(part.at[fsdp], mine, local_sems.at[which])
        own.start()
        copies.append(own)
        for step in range(1, group):
            peer = lax.rem(fsdp + step, group)
            copy = pltpu.make_async_remote_copy(
                src_ref=part.at[peer],
                dst_ref=mine,
                send_sem=part_sends.at[which, step - 1],
                recv_sem=part_arrivals.at[which, step - 1],
                device_id=(peer, ctx),
                device_id_type=MESH,
            )
            copy.start()
            copies.append(copy)
        if work.shape[0] > per * group:
            for row in range(per * group, work.shape[0]):
                work[row] = jnp.zeros(work.shape[1:], work.dtype)
    for which, (part, work) in enumerate(((down_ref, down_work), (rest_ref, rest_work))):
        own = pltpu.make_async_copy(part, work.at[pl.ds(0, part.shape[0])], local_sems.at[2 + which])
        own.start()
        copies.append(own)
        for row in range(part.shape[0], work.shape[0]):
            work[row] = jnp.zeros(work.shape[1:], work.dtype)
    for copy in copies:
        copy.wait()
    for stream in range(len(works)):
        ring.start(stream)

    def step(at, unused):
        ring.tick(at)
        return unused

    lax.fori_loop(0, ring.ticks, step, 0)
    ring.finish()


def padded(blocks, count):
    return -(-blocks // count) * count


def reduce_gradients(gate_part, up_part, down_part, rest_part):
    group, count = lax.axis_size("fsdp"), lax.axis_size("ctx")
    shapes = [
        (padded(group * gate_part.shape[1], count),) + gate_part.shape[2:],
        (padded(group * up_part.shape[1], count),) + up_part.shape[2:],
        (padded(down_part.shape[0], count),) + down_part.shape[1:],
        (padded(rest_part.shape[0], count),) + rest_part.shape[1:],
    ]
    return pl.pallas_call(
        reduce_kernel,
        out_shape=[jax.ShapeDtypeStruct(shape, jnp.bfloat16) for shape in shapes],
        in_specs=[pl.BlockSpec(memory_space=pl.ANY)] * 4,
        out_specs=[pl.BlockSpec(memory_space=pltpu.VMEM)] * 4,
        scratch_shapes=[pltpu.VMEM(shape, jnp.bfloat16) for shape in shapes]
        + [
            pltpu.VMEM((count - 1, shape[0] // count) + shape[1:], jnp.bfloat16) for shape in shapes
        ]
        + [
            pltpu.SemaphoreType.DMA((4, 2 * count - 2)),
            pltpu.SemaphoreType.DMA((4, 2 * count - 2)),
            pltpu.SemaphoreType.DMA((2, group - 1)),
            pltpu.SemaphoreType.DMA((2, group - 1)),
            pltpu.SemaphoreType.DMA((4,)),
        ],
        compiler_params=pltpu.CompilerParams(
            collective_id=0, has_side_effects=True, vmem_limit_bytes=56 << 20
        ),
    )(gate_part, up_part, down_part, rest_part)


def lane_blocks(matrix):
    rows, columns = matrix.shape
    return jnp.swapaxes(matrix.reshape(rows, columns // LANES, LANES), 0, 1)


def from_parts(parts, rows, columns):
    group = lax.axis_size("fsdp")
    wide = columns // group // LANES
    split = parts.reshape(group, -1, 16, LANES)[:, : wide * (rows // 16)]
    split = split.reshape(group, wide, rows // 16, 16, LANES)
    return jnp.transpose(split, (2, 3, 0, 1, 4)).reshape(rows, columns).astype(jnp.float32)


def from_blocks(blocks, first, count):
    part = jnp.swapaxes(blocks[first : first + count], 0, 1)
    return part.reshape(part.shape[0], count * LANES).astype(jnp.float32)


class GroupGather:
    def __init__(self, shard_of, sends, arrivals):
        self.shard_of, self.sends, self.arrivals = shard_of, sends, arrivals
        self.fsdp, self.ctx = lax.axis_index("fsdp"), lax.axis_index("ctx")
        self.chips = lax.axis_size("fsdp") // 2
        self.chip, self.core = lax.div(self.fsdp, 2), lax.rem(self.fsdp, 2)
        self.sibling = 2 * self.chip + 1 - self.core

    def copy(self, source, shard, semaphore, device):
        return pltpu.make_async_remote_copy(
            src_ref=source,
            dst_ref=self.shard_of(shard),
            send_sem=self.sends.at[semaphore],
            recv_sem=self.arrivals.at[semaphore],
            device_id=(device, self.ctx),
            device_id_type=MESH,
        )

    def same_core(self, step):
        return 2 * lax.rem(self.chip + step, self.chips) + self.core

    def across(self, source):
        return self.copy(source, self.fsdp, 0, self.sibling)

    def out(self, source, step):
        return self.copy(source, self.fsdp, step, self.same_core(step))

    def onward(self, step):
        shard = self.same_core(self.chips - step)
        return self.copy(self.shard_of(shard), shard, self.chips - 1 + step, self.sibling)

    def start(self, source):
        for step in range(1, self.chips):
            self.out(source, step).start()
        self.across(source).start()

    def forward(self):
        own = self.shard_of(self.fsdp)
        for step in range(1, self.chips):
            self.out(own, step).wait_recv()
            self.onward(step).start()

    def sibling_here(self):
        self.across(self.shard_of(self.fsdp)).wait_recv()

    def crossed(self, step):
        self.onward(step).wait_recv()

    def sent(self):
        own = self.shard_of(self.fsdp)
        self.across(own).wait_send()
        for step in range(1, self.chips):
            self.out(own, step).wait_send()
            self.onward(step).wait_send()

    def finish(self):
        self.forward()
        self.sibling_here()
        for step in range(1, self.chips):
            self.crossed(step)
        self.sent()


def group_semaphores():
    return pltpu.SemaphoreType.DMA((lax.axis_size("fsdp") - 1,))


def greet_group(barrier):
    fsdp, ctx, group = lax.axis_index("fsdp"), lax.axis_index("ctx"), lax.axis_size("fsdp")
    for step in range(1, group):
        peer = lax.rem(fsdp + step, group)
        pl.semaphore_signal(barrier, inc=1, device_id=(peer, ctx), device_id_type=MESH)
    return group - 1


class Steps:
    def __init__(self):
        self.fsdp, self.ctx = lax.axis_index("fsdp"), lax.axis_index("ctx")
        self.levels = lax.axis_size("ctx") // 2
        self.level, self.side = lax.div(self.ctx, 2), lax.rem(self.ctx, 2)
        self.peer = (self.fsdp, 2 * self.level + 1 - self.side)
        self.above = (self.fsdp, lax.rem(self.ctx + 2, 2 * self.levels))
        self.below = (self.fsdp, lax.rem(self.ctx + 2 * self.levels - 2, 2 * self.levels))
        self.has_above = self.level + 1 < self.levels
        self.has_below = self.level > 0

    def greet(self, barrier):
        pl.semaphore_signal(barrier, inc=1, device_id=self.peer, device_id_type=MESH)

        @pl.when(self.has_above)
        def _():
            pl.semaphore_signal(barrier, inc=1, device_id=self.above, device_id_type=MESH)

        @pl.when(self.has_below)
        def _():
            pl.semaphore_signal(barrier, inc=1, device_id=self.below, device_id_type=MESH)

        return 1 + jnp.minimum(self.level, 1) + jnp.minimum(self.levels - 1 - self.level, 1)


PARTS = 2


def causal(keys, wide, shape):
    key_at = lax.broadcasted_iota(jnp.int32, shape, 0)
    query_at = lax.rem(lax.broadcasted_iota(jnp.int32, shape, 1), keys)
    return key_at <= query_at


def attend_kernel(
    q_ref, kv_ref, out_ref, gate_ref, up_ref, g_ref,
    low_ref, mix_ref, log_ref, all_ref, full_out_ref, my_gate_ref, my_up_ref, all_g_ref,
    top_ref, total_ref, chain_sends, chain_arrivals, peer_sends, peer_arrivals,
    out_sends, out_arrivals, g_sends, g_arrivals, part_sends, part_arrivals, local_sems,
):
    steps = Steps()
    fsdp, ctx, group = steps.fsdp, steps.ctx, lax.axis_size("fsdp")
    units, deep, wide = q_ref.shape
    keys = kv_ref.shape[1]
    per_part = units // PARTS
    barrier = pltpu.get_barrier_semaphore()
    greeted = steps.greet(barrier) + greet_group(barrier)
    all_ref[ctx] = kv_ref[...]
    pl.semaphore_wait(barrier, greeted)

    def block_copy(level, part, side, semaphores, arrivals, arrives, device):
        block = 2 * (steps.level - level) + side
        held = all_ref.at[block, pl.ds(part * per_part, per_part)]
        return pltpu.make_async_remote_copy(
            src_ref=held,
            dst_ref=held,
            send_sem=semaphores.at[level, part],
            recv_sem=arrivals.at[arrives, part],
            device_id=device,
            device_id_type=MESH,
        )

    def chain(level, part):
        return block_copy(
            level, part, steps.side, chain_sends, chain_arrivals, level + 1, steps.above
        )

    def across(level, part):
        return block_copy(
            level, part, steps.side, peer_sends, peer_arrivals, level, steps.peer
        )

    def pass_on(level, part):
        @pl.when(steps.has_above)
        def _():
            chain(level, part).start()

    for part in range(PARTS):
        pass_on(0, part)

        @pl.when(steps.side == 0)
        def _():
            across(0, part).start()

    rows = out_ref.shape[0]
    columns = my_gate_ref.shape[1]
    gathered = GroupGather(
        lambda shard: full_out_ref.at[pl.ds(shard * rows, rows)], out_sends, out_arrivals
    )
    gathered.start(out_ref)
    gathered_g = GroupGather(lambda shard: all_g_ref.at[shard], g_sends, g_arrivals)
    gathered_g.start(g_ref)
    own_g = pltpu.make_async_copy(g_ref, all_g_ref.at[fsdp], local_sems.at[3])
    own_g.start()
    background = [own_g]
    own_rows = pl.ds(fsdp * rows, rows)
    own_out = pltpu.make_async_copy(out_ref, full_out_ref.at[own_rows], local_sems.at[2])
    own_out.start()
    background.append(own_out)
    for which, (source, target) in enumerate(((gate_ref, my_gate_ref), (up_ref, my_up_ref))):
        for step in range(1, group):
            peer = lax.rem(fsdp + step, group)
            copy = pltpu.make_async_remote_copy(
                src_ref=source.at[:, pl.ds(pl.multiple_of(peer * columns, LANES), columns)],
                dst_ref=target.at[own_rows],
                send_sem=part_sends.at[which, step - 1],
                recv_sem=part_arrivals.at[which, step - 1],
                device_id=(peer, ctx),
                device_id_type=MESH,
            )
            copy.start()
            background.append(copy)
        own = pltpu.make_async_copy(
            source.at[:, pl.ds(pl.multiple_of(fsdp * columns, LANES), columns)],
            target.at[own_rows],
            local_sems.at[which],
        )
        own.start()
        background.append(own)

    def add(unit, kv):
        scores = jnp.dot(kv, q_ref[unit], preferred_element_type=jnp.float32)
        top = top_ref[unit]
        new_top = jnp.maximum(top, jnp.max(scores, axis=0, keepdims=True))
        fade = jnp.exp(top - new_top)
        weights = jnp.exp(scores - new_top)
        top_ref[unit] = new_top
        total_ref[unit] = total_ref[unit] * fade + jnp.sum(weights, axis=0, keepdims=True)
        added = jnp.dot(kv.T, weights.astype(jnp.bfloat16), preferred_element_type=jnp.float32)
        mix_ref[unit] = mix_ref[unit] * fade + added[HD:]

    def over_units(body, first, count):
        def two(at, unused):
            body(first + 2 * at)
            body(first + 2 * at + 1)
            return unused

        lax.fori_loop(0, count // 2, two, 0)

    def diagonal(unit):
        kv = kv_ref[unit]
        scores = jnp.dot(kv, q_ref[unit], preferred_element_type=jnp.float32)
        scores = jnp.where(causal(keys, wide, scores.shape), scores, MASKED_SCORE)
        top = jnp.max(scores, axis=0, keepdims=True)
        weights = jnp.exp(scores - top)
        top_ref[unit] = top
        total_ref[unit] = jnp.sum(weights, axis=0, keepdims=True)
        added = jnp.dot(kv.T, weights.astype(jnp.bfloat16), preferred_element_type=jnp.float32)
        mix_ref[unit] = added[HD:]

    over_units(diagonal, 0, units)

    @pl.when(steps.side == 1)
    def _():
        for part in range(PARTS):
            across(0, part).wait_recv()
            over_units(lambda unit: add(unit, all_ref[ctx - 1, unit]), part * per_part, per_part)

    def level_step(level, unused):
        for part in range(PARTS):
            chain(level - 1, part).wait_recv()
            pass_on(level, part)
            across(level, part).start()
        first = 2 * (steps.level - level)
        for part in range(PARTS):
            across(level, part).wait_recv()
            over_units(
                lambda unit: add(unit, all_ref[pl.ds(first, 2), unit].reshape(2 * keys, deep)),
                part * per_part,
                per_part,
            )
        return unused

    lax.fori_loop(1, steps.level + 1, level_step, 0)

    def close(unit):
        total = total_ref[unit]
        mix_ref[unit] = mix_ref[unit] / total
        log_ref[unit] = top_ref[unit] + jnp.log(total)

    over_units(close, 0, units)
    groups = wide // keys
    for sequence in range(units // KVH):
        for pair in range(H // 2):
            heads = []
            for head in (2 * pair, 2 * pair + 1):
                unit, member = sequence * KVH + head // groups, head % groups
                heads.append(mix_ref[unit, :, member * keys : (member + 1) * keys])
            tile = jnp.concatenate(heads, axis=0).T
            low_ref[
                sequence * keys : (sequence + 1) * keys, pair * 2 * HD : (pair + 1) * 2 * HD
            ] = tile.astype(low_ref.dtype)
    gathered.finish()
    gathered_g.finish()
    for copy in background:
        copy.wait()

    def sent(level, unused):
        for part in range(PARTS):

            @pl.when(steps.has_above)
            def _():
                chain(level, part).wait_send()

            @pl.when(jnp.logical_or(level > 0, steps.side == 0))
            def _():
                across(level, part).wait_send()

        return unused

    lax.fori_loop(0, steps.level + 1, sent, 0)


ANY = pl.BlockSpec(memory_space=pl.ANY)
VMEM = pl.BlockSpec(memory_space=pltpu.VMEM)


def attend(q_wide, pairs, w_out, w_gate, w_up, g_rows):
    group, count = lax.axis_size("fsdp"), lax.axis_size("ctx")
    units, deep, wide = q_wide.shape
    keys = pairs.shape[1]
    rows, width = w_out.shape
    hidden = w_gate.shape[1] // group
    dma = pltpu.SemaphoreType.DMA
    sequences = units // KVH
    return pl.pallas_call(
        attend_kernel,
        out_shape=[
            jax.ShapeDtypeStruct((sequences * keys, width), jnp.bfloat16),
            jax.ShapeDtypeStruct((units, HD, wide), jnp.float32),
            jax.ShapeDtypeStruct((units, 1, wide), jnp.float32),
            jax.ShapeDtypeStruct((count,) + pairs.shape, jnp.bfloat16),
            jax.ShapeDtypeStruct((group * rows, width), jnp.bfloat16),
            jax.ShapeDtypeStruct((group * rows, hidden), jnp.bfloat16),
            jax.ShapeDtypeStruct((group * rows, hidden), jnp.bfloat16),
            jax.ShapeDtypeStruct((group,) + g_rows.shape, jnp.bfloat16),
        ],
        in_specs=[VMEM, VMEM, ANY, ANY, ANY, ANY],
        out_specs=[VMEM, VMEM, VMEM, VMEM, ANY, ANY, ANY, ANY],
        scratch_shapes=[
            pltpu.VMEM((units, 1, wide), jnp.float32),
            pltpu.VMEM((units, 1, wide), jnp.float32),
            dma((count // 2, PARTS)),
            dma((count // 2 + 1, PARTS)),
            dma((count // 2, PARTS)),
            dma((count // 2, PARTS)),
            *[group_semaphores()] * 4,
            dma((2, group - 1)),
            dma((2, group - 1)),
            dma((4,)),
        ],
        compiler_params=pltpu.CompilerParams(
            collective_id=1, has_side_effects=True, vmem_limit_bytes=56 << 20
        ),
    )(q_wide, pairs, w_out, w_gate, w_up, g_rows)


class GroupScatter:
    def __init__(self, give_sib, got_sib, give_cross, got_cross, far, got_far, sends, arrivals):
        self.give_sib, self.got_sib = give_sib, got_sib
        self.give_cross, self.got_cross = give_cross, got_cross
        self.far, self.got_far = far, got_far
        self.sends, self.arrivals = sends, arrivals
        self.fsdp, self.ctx = lax.axis_index("fsdp"), lax.axis_index("ctx")
        self.chips = lax.axis_size("fsdp") // 2
        self.chip, self.core = lax.div(self.fsdp, 2), lax.rem(self.fsdp, 2)
        self.sibling = 2 * self.chip + 1 - self.core

    def copy(self, source, target, semaphore, device):
        return pltpu.make_async_remote_copy(
            src_ref=source,
            dst_ref=target,
            send_sem=self.sends.at[semaphore],
            recv_sem=self.arrivals.at[semaphore],
            device_id=(device, self.ctx),
            device_id_type=MESH,
        )

    def to_sibling(self):
        return self.copy(self.give_sib, self.got_sib, 0, self.sibling)

    def to_cross(self, step):
        return self.copy(
            self.give_cross.at[step - 1], self.got_cross.at[step - 1], step, self.sibling
        )

    def to_far(self, step):
        chip = lax.rem(self.chip + self.chips - step, self.chips)
        return self.copy(
            self.far.at[step - 1],
            self.got_far.at[step - 1],
            self.chips - 1 + step,
            2 * chip + self.core,
        )

    def add_cross(self, step):
        self.to_cross(step).wait_recv()
        held = self.far.at[step - 1]
        held[...] = (
            held[...].astype(jnp.float32) + self.got_cross[step - 1].astype(jnp.float32)
        ).astype(held.dtype)
        self.to_far(step).start()

    def total(self, own):
        self.to_sibling().wait_recv()
        value = own + self.got_sib[...].astype(jnp.float32)
        for step in range(1, self.chips):
            self.to_far(step).wait_recv()
            value = value + self.got_far[step - 1].astype(jnp.float32)
        return value

    def sent(self):
        self.to_sibling().wait_send()
        for step in range(1, self.chips):
            self.to_cross(step).wait_send()
            self.to_far(step).wait_send()


def scatter_scratch(rows, width):
    far = lax.axis_size("fsdp") // 2 - 1
    one, many = (rows, width), (far, rows, width)
    return [pltpu.VMEM(shape, jnp.bfloat16) for shape in (one, one, many, many, many, many)]


def dot_columns(left, right):
    return lax.dot_general(
        left, right, (((1,), (1,)), ((), ())), preferred_element_type=jnp.float32
    )


def tiles(count, body):
    def step(at, unused):
        body(at)
        return unused

    lax.fori_loop(0, count, step, 0)


def lane_tile(at, size):
    return pl.ds(pl.multiple_of(at * size, LANES), size)


def width_tile(width):
    return 384 if width % 384 == 0 else width


def hidden_tile(hidden):
    return 256 if hidden % 256 == 0 else 128


def transpose_into(target, source):
    rows, columns = source.shape

    def body(at):
        part = source[:, lane_tile(at, LANES)]
        target[pl.ds(pl.multiple_of(at * LANES, LANES), LANES), :] = part.T

    tiles(columns // LANES, body)


def ffn_kernel(
    x_ref, low_ref, out_ref, gate_ref, up_ref, down_ref, all_g_ref, gain_ref,
    layer_ref, resid_grad_ref, branch_ref, g_wide_ref, gate_part_ref, up_part_ref, down_part_ref,
    gain_grad_ref,
    all_n_ref, turned_n, turned_act, act_ref, gate_grad, up_grad, resid_ref, layer_own, grad_own,
    *rest,
):
    down_scratch, grad_scratch = rest[:6], rest[6:12]
    n_sends, n_arrivals, down_sends, down_arrivals, grad_sends, grad_arrivals = rest[12:]
    group = lax.axis_size("fsdp")
    rows, width = x_ref.shape
    hidden = gate_ref.shape[1]
    barrier = pltpu.get_barrier_semaphore()
    greeted = greet_group(barrier)
    step_in, step_out = hidden_tile(hidden), width_tile(width)

    def branch(at):
        columns = lane_tile(at, step_out)
        resid_ref[:, columns] = x_ref[:, columns].astype(jnp.float32) + forward_dot(
            low_ref[...], out_ref[:, columns]
        )

    tiles(width // step_out, branch)
    gain = gain_ref[...]
    scale = norm_scale(resid_ref[...])
    gathered = GroupGather(lambda shard: all_n_ref.at[shard], n_sends, n_arrivals)
    fsdp, chips = gathered.fsdp, gathered.chips
    all_n_ref[fsdp] = (resid_ref[...] * scale * gain).astype(jnp.bfloat16)
    pl.semaphore_wait(barrier, greeted)
    gathered.start(all_n_ref.at[fsdp])
    layer_sum = GroupScatter(*down_scratch, down_sends, down_arrivals)
    grad_sum = GroupScatter(*grad_scratch, grad_sends, grad_arrivals)

    def hidden_part(shard):
        def body(at):
            columns = lane_tile(at, step_in)
            normed = all_n_ref[shard]
            gate = forward_dot(normed, gate_ref[:, columns])
            upward = forward_dot(normed, up_ref[:, columns])
            grad_act = dot_columns(
                all_g_ref[shard], down_ref[pl.ds(pl.multiple_of(at * step_in, LANES), step_in), :]
            )
            sigmoid = jax.nn.sigmoid(gate)
            silu = gate * sigmoid
            act_ref[shard, :, columns] = (silu * upward).astype(jnp.bfloat16)
            gate_grad[shard, :, columns] = (
                grad_act * upward * (sigmoid * (1.0 + gate * (1.0 - sigmoid)))
            ).astype(jnp.bfloat16)
            up_grad[shard, :, columns] = (grad_act * silu).astype(jnp.bfloat16)

        tiles(hidden // step_in, body)

    def grad_part(shard, target):
        def body(at):
            columns = pl.ds(pl.multiple_of(at * step_out, LANES), step_out)
            target[:, columns] = (
                dot_columns(gate_grad[shard], gate_ref[columns, :])
                + dot_columns(up_grad[shard], up_ref[columns, :])
            ).astype(target.dtype)

        tiles(width // step_out, body)

    def layer_part(shard, target):
        def body(at):
            columns = lane_tile(at, step_out)
            target[:, columns] = forward_dot(act_ref[shard], down_ref[:, columns]).astype(
                target.dtype
            )

        tiles(width // step_out, body)

    hidden_part(fsdp)
    gathered.sibling_here()
    sibling = gathered.sibling
    hidden_part(sibling)
    grad_part(sibling, grad_sum.give_sib)
    grad_sum.to_sibling().start()
    layer_part(sibling, layer_sum.give_sib)
    layer_sum.to_sibling().start()
    gathered.forward()
    grad_part(fsdp, grad_own)
    layer_part(fsdp, layer_own)
    for step in range(1, chips):
        ours = gathered.same_core(chips - step)
        theirs = ours + sibling - fsdp
        gathered.crossed(step)
        hidden_part(theirs)
        grad_part(theirs, grad_sum.give_cross.at[step - 1])
        grad_sum.to_cross(step).start()
        hidden_part(ours)
        grad_part(ours, grad_sum.far.at[step - 1])
        grad_sum.add_cross(step)
        layer_part(theirs, layer_sum.give_cross.at[step - 1])
        layer_sum.to_cross(step).start()
        layer_part(ours, layer_sum.far.at[step - 1])
        layer_sum.add_cross(step)

    for shard in range(group):
        span = slice(shard * rows, (shard + 1) * rows)
        transpose_into(turned_n.at[:, span], all_n_ref.at[shard])
        transpose_into(turned_act.at[:, span], act_ref.at[shard])

    def down_tile(at):
        columns = lane_tile(at, step_out)
        down_part_ref[:, columns] = forward_dot(
            turned_act[...], all_g_ref[:, :, columns].reshape(group * rows, step_out)
        ).astype(jnp.bfloat16)

    tiles(width // step_out, down_tile)
    own = width // group
    row_blocks = own // 16
    for source, target in ((gate_grad, gate_part_ref), (up_grad, up_part_ref)):

        def weight_tile(at):
            columns = lane_tile(at, step_in)
            part = forward_dot(
                turned_n[...], source[:, :, columns].reshape(group * rows, step_in)
            ).astype(jnp.bfloat16)
            for block in range(step_in // LANES):
                first = (at * (step_in // LANES) + block) * row_blocks
                for owner in range(group):
                    target[owner, pl.ds(first, row_blocks)] = part[
                        owner * own : (owner + 1) * own, block * LANES : (block + 1) * LANES
                    ].reshape(row_blocks, 16, LANES)

        tiles(hidden // step_in, weight_tile)
        filled = hidden // LANES * row_blocks
        for spare in range(filled, target.shape[1]):
            for owner in range(group):
                target[owner, spare] = jnp.zeros(target.shape[2:], target.dtype)

    upstream = grad_sum.total(grad_own[...])
    resid = resid_ref[...]
    scaled = upstream * gain
    grad_resid = (
        all_g_ref[fsdp].astype(jnp.float32)
        + scale * scaled
        - resid * scale**3 * jnp.mean(scaled * resid, axis=-1, keepdims=True)
    )
    gain_grad_ref[...] = jnp.sum(upstream * resid * scale, axis=0, keepdims=True)
    resid_grad_ref[...] = grad_resid
    branch_ref[...] = grad_resid.astype(jnp.bfloat16)
    units, _, wide = g_wide_ref.shape
    sequences = units // KVH
    keys = rows // sequences
    groups = wide // keys
    g_wide_ref[:, :HD, :] = jnp.zeros((units, HD, wide), g_wide_ref.dtype)
    for pair in range(H // 2):
        columns = slice(pair * 2 * HD, (pair + 1) * 2 * HD)
        mixed = dot_columns(branch_ref[...], out_ref[columns, :]).astype(jnp.bfloat16)
        for sequence in range(sequences):
            turned = mixed[sequence * keys : (sequence + 1) * keys].T
            for half in range(2):
                head = 2 * pair + half
                unit, member = sequence * KVH + head // groups, head % groups
                g_wide_ref[unit, HD:, member * keys : (member + 1) * keys] = turned[
                    half * HD : (half + 1) * HD
                ]
    layer_ref[...] = (resid + layer_sum.total(layer_own[...])).astype(jnp.bfloat16)
    gathered.sent()
    grad_sum.sent()
    layer_sum.sent()


def spread(blocks, count):
    return -(-blocks // count) * count


def feed_forward(x, low, full_out, my_gate, my_up, my_down, all_g, gain, units, wide):
    group, count = lax.axis_size("fsdp"), lax.axis_size("ctx")
    rows, width = x.shape
    hidden = my_gate.shape[1]
    blocks = spread(hidden // LANES * (width // group // 16), count)
    chips = group // 2
    dma = pltpu.SemaphoreType.DMA((2 * chips - 1,))
    bf16 = jnp.bfloat16
    return pl.pallas_call(
        ffn_kernel,
        out_shape=[
            jax.ShapeDtypeStruct((rows, width), bf16),
            jax.ShapeDtypeStruct((rows, width), jnp.float32),
            jax.ShapeDtypeStruct((rows, width), bf16),
            jax.ShapeDtypeStruct((units, 2 * HD, wide), bf16),
            jax.ShapeDtypeStruct((group, blocks, 16, LANES), bf16),
            jax.ShapeDtypeStruct((group, blocks, 16, LANES), bf16),
            jax.ShapeDtypeStruct((hidden, width), bf16),
            jax.ShapeDtypeStruct((1, width), jnp.float32),
        ],
        in_specs=[VMEM] * 8,
        out_specs=[VMEM] * 8,
        scratch_shapes=[
            pltpu.VMEM((group, rows, width), bf16),
            pltpu.VMEM((width, group * rows), bf16),
            pltpu.VMEM((hidden, group * rows), bf16),
            pltpu.VMEM((group, rows, hidden), bf16),
            pltpu.VMEM((group, rows, hidden), bf16),
            pltpu.VMEM((group, rows, hidden), bf16),
            pltpu.VMEM((rows, width), jnp.float32),
            pltpu.VMEM((rows, width), jnp.float32),
            pltpu.VMEM((rows, width), jnp.float32),
            *scatter_scratch(rows, width),
            *scatter_scratch(rows, width),
            *[dma] * 6,
        ],
        compiler_params=pltpu.CompilerParams(
            collective_id=2, has_side_effects=True, vmem_limit_bytes=60 << 20
        ),
    )(x, low, full_out, my_gate, my_up, my_down, all_g, gain)


def call(kernel, outs, *args):
    return pl.pallas_call(
        kernel,
        out_shape=outs,
        in_specs=[pl.BlockSpec(memory_space=pltpu.VMEM)] * len(args),
        out_specs=[pl.BlockSpec(memory_space=pltpu.VMEM)] * len(outs),
        compiler_params=pltpu.CompilerParams(vmem_limit_bytes=56 << 20),
    )(*args)


def unit_columns(rows, seq_count, block_len):
    groups = H // KVH
    split = rows.reshape(seq_count, block_len, KVH, groups, HD)
    return jnp.transpose(split, (0, 2, 4, 3, 1)).reshape(
        seq_count * KVH, HD, groups * block_len
    )


def unit_rows(columns, seq_count, block_len):
    groups = H // KVH
    split = columns.reshape(seq_count, KVH, HD, groups, block_len)
    return jnp.transpose(split, (0, 4, 1, 3, 2)).reshape(seq_count * block_len, H * HD)


def on_device(
    tokens, w_query, w_key, w_value, w_out, w_gate, w_up, w_down, gain_attn, gain_ffn, cotangent
):
    block_len, seq_count, width = tokens.shape
    rows_count = block_len * seq_count
    kv_width = KVH * HD
    full_query, full_key, full_value = [
        lax.all_gather(weight, "fsdp", axis=0, tiled=True) for weight in (w_query, w_key, w_value)
    ]
    full_gain_attn, full_gain_ffn = [
        lax.all_gather(gain, "fsdp", axis=0, tiled=True) for gain in (gain_attn, gain_ffn)
    ]
    my_down = w_down
    my_start = lax.axis_index("ctx") * block_len
    positions = my_start + jnp.arange(block_len, dtype=jnp.int32)
    x_rows = jnp.swapaxes(tokens, 0, 1).reshape(rows_count, width)
    g_rows = jnp.swapaxes(cotangent, 0, 1).reshape(rows_count, width)
    inputs = x_rows.astype(jnp.float32)
    scale_attn = norm_scale(inputs)
    normed_attn = (inputs * scale_attn * full_gain_attn.astype(jnp.float32)).astype(jnp.bfloat16)
    query_raw = forward_dot(normed_attn, full_query)
    key_raw = forward_dot(normed_attn, full_key)
    value_raw = forward_dot(normed_attn, full_value)
    units = seq_count * KVH
    wide = H // KVH * block_len
    queries = (
        rotary(query_raw.reshape(seq_count, block_len, H, HD), positions, 1.0)
        .astype(jnp.bfloat16)
        .reshape(rows_count, width)
    )
    keys_local = rotary(
        key_raw.reshape(seq_count, block_len, KVH, HD), positions, 1.0
    ).astype(jnp.bfloat16)
    values_local = value_raw.astype(jnp.bfloat16).reshape(seq_count, block_len, KVH, HD)
    pairs = jnp.swapaxes(
        jnp.concatenate([keys_local, values_local], axis=-1), 1, 2
    ).reshape(units, block_len, 2 * HD)
    q_unit = unit_columns(queries * jnp.bfloat16(HD ** (-0.5)), seq_count, block_len)
    q_wide = jnp.concatenate([q_unit, jnp.zeros_like(q_unit)], axis=1)
    attn_low, mix_unit, log_total, all_pairs, full_out, my_gate, my_up, all_g = attend(
        q_wide, pairs, w_out, w_gate, w_up, g_rows
    )
    layer_out, grad_resid, grad_branch, g_wide, gate_part, up_part, down_part, gain_term_ffn = (
        feed_forward(
            x_rows,
            attn_low,
            full_out,
            my_gate,
            my_up,
            w_down,
            all_g,
            full_gain_ffn.astype(jnp.float32)[None],
            units,
            wide,
        )
    )
    qg = jnp.concatenate([jnp.swapaxes(q_wide, 1, 2), jnp.swapaxes(g_wide, 1, 2)], axis=1)
    grad_q_unit, grad_pairs = call(
        attend_back_kernel,
        [
            jax.ShapeDtypeStruct((units, HD, wide), jnp.float32),
            jax.ShapeDtypeStruct(all_pairs.shape, jnp.bfloat16),
        ],
        q_wide,
        g_wide,
        qg,
        all_pairs,
        mix_unit,
        log_total,
    )
    summed_pairs = lax.psum_scatter(grad_pairs, "ctx", scatter_dimension=0, tiled=True)
    summed_pairs = jnp.transpose(
        summed_pairs.reshape(seq_count, KVH, block_len, 2 * HD), (0, 2, 1, 3)
    )
    grad_query_low = (
        rotary(
            unit_rows(grad_q_unit, seq_count, block_len).reshape(seq_count, block_len, H, HD),
            positions,
            -1.0,
        )
        .astype(jnp.bfloat16)
        .reshape(rows_count, width)
    )
    grad_key_low = (
        rotary(summed_pairs[..., :HD].astype(jnp.float32), positions, -1.0)
        .astype(jnp.bfloat16)
        .reshape(rows_count, kv_width)
    )
    grad_value_low = summed_pairs[..., HD:].reshape(rows_count, kv_width)
    grad_normed_attn = (
        backward_dot(grad_query_low, full_query)
        + backward_dot(grad_key_low, full_key)
        + backward_dot(grad_value_low, full_value)
    )
    inward_attn, gain_term_attn = norm_back(
        inputs, scale_attn, full_gain_attn.astype(jnp.float32), grad_normed_attn
    )
    layer_out = layer_out.reshape(seq_count, block_len, width)
    grad_tokens = (grad_resid + inward_attn).reshape(seq_count, block_len, width)

    def part(acts, grads):
        return jnp.einsum("rc,rn->cn", acts, grads, preferred_element_type=jnp.float32)

    group = lax.axis_size("fsdp")
    rest_part = lax.psum_scatter(
        jnp.concatenate(
            [
                part(normed_attn, grad_query_low),
                part(normed_attn, grad_key_low),
                part(normed_attn, grad_value_low),
                part(attn_low, grad_branch),
            ],
            axis=1,
        ).astype(jnp.bfloat16),
        "fsdp",
        scatter_dimension=0,
        tiled=True,
    )
    gate_sum, up_sum, down_sum, rest_sum = reduce_gradients(
        gate_part,
        up_part,
        down_part.reshape(-1, 16, width),
        lane_blocks(rest_part),
    )
    gains = lax.psum(jnp.stack([gain_term_attn, gain_term_ffn[0]]), ("fsdp", "ctx"))
    own = gain_attn.shape[0]
    gains = lax.dynamic_slice_in_dim(gains, lax.axis_index("fsdp") * own, own, 1)
    edges = [0, width, width + kv_width, width + 2 * kv_width, 2 * width + 2 * kv_width]
    grad_query, grad_key, grad_value, grad_out = [
        from_blocks(rest_sum, first // LANES, (last - first) // LANES)
        for first, last in zip(edges[:-1], edges[1:])
    ]
    return (
        jnp.swapaxes(layer_out, 0, 1),
        jnp.swapaxes(grad_tokens, 0, 1),
        grad_query,
        grad_key,
        grad_value,
        grad_out,
        from_parts(gate_sum, gain_attn.shape[0], FF),
        from_parts(up_sum, gain_attn.shape[0], FF),
        down_sum.reshape(-1, width)[: w_down.shape[0]].astype(jnp.float32),
        gains[0],
        gains[1],
    )


def solution(mesh):
    return jax.shard_map(
        on_device,
        mesh=mesh,
        in_specs=(
            P("ctx", "fsdp", None),
            P("fsdp", None),
            P("fsdp", None),
            P("fsdp", None),
            P("fsdp", None),
            P("fsdp", None),
            P("fsdp", None),
            P("fsdp", None),
            P("fsdp"),
            P("fsdp"),
            P("ctx", "fsdp", None),
        ),
        out_specs=(
            P("ctx", "fsdp", None),
            P("ctx", "fsdp", None),
            P("fsdp", None),
            P("fsdp", None),
            P("fsdp", None),
            P("fsdp", None),
            P("fsdp", None),
            P("fsdp", None),
            P("fsdp", None),
            P("fsdp"),
            P("fsdp"),
        ),
        check_vma=False,
    )
```

```python
import jax
import jax.numpy as jnp
from jax import lax
from jax.experimental import pallas as pl
from jax.experimental.pallas import tpu as pltpu
from jax.sharding import PartitionSpec as P

H = 18
KVH = 6
HD = 64
FF = 3072


EPSILON = 1e-05
ROTARY_BASE = 10000.0
MASKED_SCORE = -1e30


def rotary(values, positions, direction):
    half = values.shape[-1] // 2
    freqs = ROTARY_BASE ** (-2.0 * jnp.arange(half, dtype=jnp.float32) / values.shape[-1])
    angles = positions.astype(jnp.float32)[:, None] * freqs[None, :]
    cosine = jnp.cos(angles)[:, None, :]
    sine = direction * jnp.sin(angles)[:, None, :]
    first = values[..., :half]
    second = values[..., half:]
    return jnp.concatenate(
        [first * cosine - second * sine, second * cosine + first * sine], axis=-1
    )


def norm_scale(rows):
    return lax.rsqrt(jnp.mean(rows * rows, axis=-1, keepdims=True) + EPSILON)


def forward_dot(left, right):
    return jnp.dot(left, right, preferred_element_type=jnp.float32)


MESH = pl.DeviceIdType.MESH
LANES = 128


def ring_place(ctx, fsdp, count):
    column, side = lax.div(ctx, 2), lax.rem(ctx, 2)
    place = column + side * (count - 1 - 2 * column)
    odd = lax.rem(fsdp, 2)
    return place + odd * (count - 1 - 2 * place)


def ring_ctx(place, fsdp, count):
    odd = lax.rem(fsdp, 2)
    place = place + odd * (count - 1 - 2 * place)
    late = lax.div(place, count // 2)
    return (1 - late) * 2 * place + late * (2 * (count - 1 - place) + 1)


class GroupGather:
    def __init__(self, shard_of, sends, arrivals):
        self.shard_of, self.sends, self.arrivals = shard_of, sends, arrivals
        self.fsdp, self.ctx = lax.axis_index("fsdp"), lax.axis_index("ctx")
        self.chips = lax.axis_size("fsdp") // 2
        self.chip, self.core = lax.div(self.fsdp, 2), lax.rem(self.fsdp, 2)
        self.sibling = 2 * self.chip + 1 - self.core

    def copy(self, source, shard, semaphore, device):
        return pltpu.make_async_remote_copy(
            src_ref=source,
            dst_ref=self.shard_of(shard),
            send_sem=self.sends.at[semaphore],
            recv_sem=self.arrivals.at[semaphore],
            device_id=(device, self.ctx),
            device_id_type=MESH,
        )

    def same_core(self, step):
        return 2 * lax.rem(self.chip + step, self.chips) + self.core

    def across(self, source):
        return self.copy(source, self.fsdp, 0, self.sibling)

    def out(self, source, step):
        return self.copy(source, self.fsdp, step, self.same_core(step))

    def onward(self, step):
        shard = self.same_core(self.chips - step)
        return self.copy(self.shard_of(shard), shard, self.chips - 1 + step, self.sibling)

    def start(self, source):
        for step in range(1, self.chips):
            self.out(source, step).start()
        self.across(source).start()

    def forward(self):
        own = self.shard_of(self.fsdp)
        for step in range(1, self.chips):
            self.out(own, step).wait_recv()
            self.onward(step).start()

    def sibling_here(self):
        self.across(self.shard_of(self.fsdp)).wait_recv()

    def crossed(self, step):
        self.onward(step).wait_recv()

    def sent(self):
        own = self.shard_of(self.fsdp)
        self.across(own).wait_send()
        for step in range(1, self.chips):
            self.out(own, step).wait_send()
            self.onward(step).wait_send()

    def finish(self):
        self.forward()
        self.sibling_here()
        for step in range(1, self.chips):
            self.crossed(step)
        self.sent()


def group_semaphores():
    return pltpu.SemaphoreType.DMA((lax.axis_size("fsdp") - 1,))


def greet_group(barrier):
    fsdp, ctx, group = lax.axis_index("fsdp"), lax.axis_index("ctx"), lax.axis_size("fsdp")
    for step in range(1, group):
        peer = lax.rem(fsdp + step, group)
        pl.semaphore_signal(barrier, inc=1, device_id=(peer, ctx), device_id_type=MESH)
    return group - 1


class Steps:
    def __init__(self):
        self.fsdp, self.ctx = lax.axis_index("fsdp"), lax.axis_index("ctx")
        self.levels = lax.axis_size("ctx") // 2
        self.level, self.side = lax.div(self.ctx, 2), lax.rem(self.ctx, 2)
        self.peer = (self.fsdp, 2 * self.level + 1 - self.side)
        self.above = (self.fsdp, lax.rem(self.ctx + 2, 2 * self.levels))
        self.below = (self.fsdp, lax.rem(self.ctx + 2 * self.levels - 2, 2 * self.levels))
        self.has_above = self.level + 1 < self.levels
        self.has_below = self.level > 0

    def greet(self, barrier):
        pl.semaphore_signal(barrier, inc=1, device_id=self.peer, device_id_type=MESH)

        @pl.when(self.has_above)
        def _():
            pl.semaphore_signal(barrier, inc=1, device_id=self.above, device_id_type=MESH)

        @pl.when(self.has_below)
        def _():
            pl.semaphore_signal(barrier, inc=1, device_id=self.below, device_id_type=MESH)

        return 1 + jnp.minimum(self.level, 1) + jnp.minimum(self.levels - 1 - self.level, 1)


PARTS = 2


def causal(keys, wide, shape):
    key_at = lax.broadcasted_iota(jnp.int32, shape, 0)
    query_at = lax.rem(lax.broadcasted_iota(jnp.int32, shape, 1), keys)
    return key_at <= query_at


def attend_kernel(
    q_ref, kv_ref, out_ref, gate_ref, up_ref, g_ref,
    low_ref, low_t_ref, mix_ref, log_ref, all_ref, full_out_ref, my_gate_ref, my_up_ref, all_g_ref,
    top_ref, total_ref, chain_sends, chain_arrivals, peer_sends, peer_arrivals,
    out_sends, out_arrivals, g_sends, g_arrivals, part_sends, part_arrivals, local_sems,
):
    steps = Steps()
    fsdp, ctx, group = steps.fsdp, steps.ctx, lax.axis_size("fsdp")
    units, deep, wide = q_ref.shape
    keys = kv_ref.shape[1]
    per_part = units // PARTS
    barrier = pltpu.get_barrier_semaphore()
    greeted = steps.greet(barrier) + greet_group(barrier)
    all_ref[ctx] = kv_ref[...]
    pl.semaphore_wait(barrier, greeted)

    def block_copy(level, part, side, semaphores, arrivals, arrives, device):
        block = 2 * (steps.level - level) + side
        held = all_ref.at[block, pl.ds(part * per_part, per_part)]
        return pltpu.make_async_remote_copy(
            src_ref=held,
            dst_ref=held,
            send_sem=semaphores.at[level, part],
            recv_sem=arrivals.at[arrives, part],
            device_id=device,
            device_id_type=MESH,
        )

    def chain(level, part):
        return block_copy(
            level, part, steps.side, chain_sends, chain_arrivals, level + 1, steps.above
        )

    def across(level, part):
        return block_copy(
            level, part, steps.side, peer_sends, peer_arrivals, level, steps.peer
        )

    def pass_on(level, part):
        @pl.when(steps.has_above)
        def _():
            chain(level, part).start()

    for part in range(PARTS):
        pass_on(0, part)

        @pl.when(steps.side == 0)
        def _():
            across(0, part).start()

    rows = out_ref.shape[0]
    columns = my_gate_ref.shape[1]
    gathered = GroupGather(
        lambda shard: full_out_ref.at[pl.ds(shard * rows, rows)], out_sends, out_arrivals
    )
    gathered.start(out_ref)
    gathered_g = GroupGather(lambda shard: all_g_ref.at[shard], g_sends, g_arrivals)
    gathered_g.start(g_ref)
    own_g = pltpu.make_async_copy(g_ref, all_g_ref.at[fsdp], local_sems.at[3])
    own_g.start()
    background = [own_g]
    own_rows = pl.ds(fsdp * rows, rows)
    own_out = pltpu.make_async_copy(out_ref, full_out_ref.at[own_rows], local_sems.at[2])
    own_out.start()
    background.append(own_out)
    for which, (source, target) in enumerate(((gate_ref, my_gate_ref), (up_ref, my_up_ref))):
        for step in range(1, group):
            peer = lax.rem(fsdp + step, group)
            copy = pltpu.make_async_remote_copy(
                src_ref=source.at[:, pl.ds(pl.multiple_of(peer * columns, LANES), columns)],
                dst_ref=target.at[own_rows],
                send_sem=part_sends.at[which, step - 1],
                recv_sem=part_arrivals.at[which, step - 1],
                device_id=(peer, ctx),
                device_id_type=MESH,
            )
            copy.start()
            background.append(copy)
        own = pltpu.make_async_copy(
            source.at[:, pl.ds(pl.multiple_of(fsdp * columns, LANES), columns)],
            target.at[own_rows],
            local_sems.at[which],
        )
        own.start()
        background.append(own)

    def add(unit, kv):
        scores = jnp.dot(kv, q_ref[unit], preferred_element_type=jnp.float32)
        top = top_ref[unit]
        new_top = jnp.maximum(top, jnp.max(scores, axis=0, keepdims=True))
        fade = jnp.exp(top - new_top)
        weights = jnp.exp(scores - new_top)
        top_ref[unit] = new_top
        total_ref[unit] = total_ref[unit] * fade + jnp.sum(weights, axis=0, keepdims=True)
        added = jnp.dot(kv.T, weights.astype(jnp.bfloat16), preferred_element_type=jnp.float32)
        mix_ref[unit] = mix_ref[unit] * fade + added[HD:]

    def over_units(body, first, count):
        def two(at, unused):
            body(first + 2 * at)
            body(first + 2 * at + 1)
            return unused

        lax.fori_loop(0, count // 2, two, 0)

    def diagonal(unit):
        kv = kv_ref[unit]
        scores = jnp.dot(kv, q_ref[unit], preferred_element_type=jnp.float32)
        scores = jnp.where(causal(keys, wide, scores.shape), scores, MASKED_SCORE)
        top = jnp.max(scores, axis=0, keepdims=True)
        weights = jnp.exp(scores - top)
        top_ref[unit] = top
        total_ref[unit] = jnp.sum(weights, axis=0, keepdims=True)
        added = jnp.dot(kv.T, weights.astype(jnp.bfloat16), preferred_element_type=jnp.float32)
        mix_ref[unit] = added[HD:]

    over_units(diagonal, 0, units)

    @pl.when(steps.side == 1)
    def _():
        for part in range(PARTS):
            across(0, part).wait_recv()
            over_units(lambda unit: add(unit, all_ref[ctx - 1, unit]), part * per_part, per_part)

    def level_step(level, unused):
        for part in range(PARTS):
            chain(level - 1, part).wait_recv()
            pass_on(level, part)
            across(level, part).start()
        first = 2 * (steps.level - level)
        for part in range(PARTS):
            across(level, part).wait_recv()
            over_units(
                lambda unit: add(unit, all_ref[pl.ds(first, 2), unit].reshape(2 * keys, deep)),
                part * per_part,
                per_part,
            )
        return unused

    lax.fori_loop(1, steps.level + 1, level_step, 0)

    def close(unit):
        total = total_ref[unit]
        mix_ref[unit] = mix_ref[unit] / total
        log_ref[unit] = top_ref[unit] + jnp.log(total)

    over_units(close, 0, units)
    groups = wide // keys
    for sequence in range(units // KVH):
        for pair in range(H // 2):
            heads = []
            for head in (2 * pair, 2 * pair + 1):
                unit, member = sequence * KVH + head // groups, head % groups
                heads.append(mix_ref[unit, :, member * keys : (member + 1) * keys])
            tile = jnp.concatenate(heads, axis=0).astype(low_ref.dtype)
            span = slice(sequence * keys, (sequence + 1) * keys)
            columns = slice(pair * 2 * HD, (pair + 1) * 2 * HD)
            low_t_ref[columns, span] = tile
            low_ref[span, columns] = tile.T
    gathered.finish()
    gathered_g.finish()
    for copy in background:
        copy.wait()

    def sent(level, unused):
        for part in range(PARTS):

            @pl.when(steps.has_above)
            def _():
                chain(level, part).wait_send()

            @pl.when(jnp.logical_or(level > 0, steps.side == 0))
            def _():
                across(level, part).wait_send()

        return unused

    lax.fori_loop(0, steps.level + 1, sent, 0)


ANY = pl.BlockSpec(memory_space=pl.ANY)
VMEM = pl.BlockSpec(memory_space=pltpu.VMEM)


def attend(q_wide, pairs, w_out, w_gate, w_up, g_rows):
    group, count = lax.axis_size("fsdp"), lax.axis_size("ctx")
    units, deep, wide = q_wide.shape
    keys = pairs.shape[1]
    rows, width = w_out.shape
    hidden = w_gate.shape[1] // group
    dma = pltpu.SemaphoreType.DMA
    sequences = units // KVH
    return pl.pallas_call(
        attend_kernel,
        out_shape=[
            jax.ShapeDtypeStruct((sequences * keys, width), jnp.bfloat16),
            jax.ShapeDtypeStruct((width, sequences * keys), jnp.bfloat16),
            jax.ShapeDtypeStruct((units, HD, wide), jnp.float32),
            jax.ShapeDtypeStruct((units, 1, wide), jnp.float32),
            jax.ShapeDtypeStruct((count,) + pairs.shape, jnp.bfloat16),
            jax.ShapeDtypeStruct((group * rows, width), jnp.bfloat16),
            jax.ShapeDtypeStruct((group * rows, hidden), jnp.bfloat16),
            jax.ShapeDtypeStruct((group * rows, hidden), jnp.bfloat16),
            jax.ShapeDtypeStruct((group,) + g_rows.shape, jnp.bfloat16),
        ],
        in_specs=[VMEM, VMEM, ANY, ANY, ANY, ANY],
        out_specs=[VMEM] * 5 + [ANY] * 4,
        scratch_shapes=[
            pltpu.VMEM((units, 1, wide), jnp.float32),
            pltpu.VMEM((units, 1, wide), jnp.float32),
            dma((count // 2, PARTS)),
            dma((count // 2 + 1, PARTS)),
            dma((count // 2, PARTS)),
            dma((count // 2, PARTS)),
            *[group_semaphores()] * 4,
            dma((2, group - 1)),
            dma((2, group - 1)),
            dma((4,)),
        ],
        compiler_params=pltpu.CompilerParams(
            collective_id=1, has_side_effects=True, vmem_limit_bytes=56 << 20
        ),
    )(q_wide, pairs, w_out, w_gate, w_up, g_rows)


class GroupScatter:
    def __init__(self, give_sib, got_sib, give_cross, got_cross, far, got_far, sends, arrivals):
        self.give_sib, self.got_sib = give_sib, got_sib
        self.give_cross, self.got_cross = give_cross, got_cross
        self.far, self.got_far = far, got_far
        self.sends, self.arrivals = sends, arrivals
        self.fsdp, self.ctx = lax.axis_index("fsdp"), lax.axis_index("ctx")
        self.chips = lax.axis_size("fsdp") // 2
        self.chip, self.core = lax.div(self.fsdp, 2), lax.rem(self.fsdp, 2)
        self.sibling = 2 * self.chip + 1 - self.core

    def copy(self, source, target, semaphore, device):
        return pltpu.make_async_remote_copy(
            src_ref=source,
            dst_ref=target,
            send_sem=self.sends.at[semaphore],
            recv_sem=self.arrivals.at[semaphore],
            device_id=(device, self.ctx),
            device_id_type=MESH,
        )

    def to_sibling(self):
        return self.copy(self.give_sib, self.got_sib, 0, self.sibling)

    def to_cross(self, step):
        return self.copy(
            self.give_cross.at[step - 1], self.got_cross.at[step - 1], step, self.sibling
        )

    def to_far(self, step):
        chip = lax.rem(self.chip + self.chips - step, self.chips)
        return self.copy(
            self.far.at[step - 1],
            self.got_far.at[step - 1],
            self.chips - 1 + step,
            2 * chip + self.core,
        )

    def add_cross(self, step):
        self.to_cross(step).wait_recv()
        held = self.far.at[step - 1]
        held[...] = (
            held[...].astype(jnp.float32) + self.got_cross[step - 1].astype(jnp.float32)
        ).astype(held.dtype)
        self.to_far(step).start()

    def total(self, own):
        self.to_sibling().wait_recv()
        value = own + self.got_sib[...].astype(jnp.float32)
        for step in range(1, self.chips):
            self.to_far(step).wait_recv()
            value = value + self.got_far[step - 1].astype(jnp.float32)
        return value

    def sent(self):
        self.to_sibling().wait_send()
        for step in range(1, self.chips):
            self.to_cross(step).wait_send()
            self.to_far(step).wait_send()


def scatter_scratch(rows, width):
    far = lax.axis_size("fsdp") // 2 - 1
    one, many = (rows, width), (far, rows, width)
    return [pltpu.VMEM(shape, jnp.bfloat16) for shape in (one, one, many, many, many, many)]


def dot_columns(left, right):
    return lax.dot_general(
        left, right, (((1,), (1,)), ((), ())), preferred_element_type=jnp.float32
    )


def tiles(count, body):
    def step(at, unused):
        body(at)
        return unused

    lax.fori_loop(0, count, step, 0)


def lane_tile(at, size):
    return pl.ds(pl.multiple_of(at * size, LANES), size)


def width_tile(width):
    return 384 if width % 384 == 0 else width


def hidden_tile(hidden):
    return 256 if hidden % 256 == 0 else 128


def transpose_into(target, source):
    rows, columns = source.shape

    def body(at):
        part = source[:, lane_tile(at, LANES)]
        target[pl.ds(pl.multiple_of(at * LANES, LANES), LANES), :] = part.T

    tiles(columns // LANES, body)


def ffn_kernel(
    x_ref, low_ref, out_ref, gate_ref, up_ref, down_ref, all_g_ref, gain_ref,
    layer_ref, resid_grad_ref, branch_ref, g_wide_ref, gate_part_ref, up_part_ref, down_part_ref,
    gain_grad_ref,
    all_n_ref, turned_n, turned_act, act_ref, gate_grad, up_grad, resid_ref, layer_own, grad_own,
    *rest,
):
    down_scratch, grad_scratch = rest[:6], rest[6:12]
    n_sends, n_arrivals, down_sends, down_arrivals, grad_sends, grad_arrivals = rest[12:]
    group = lax.axis_size("fsdp")
    rows, width = x_ref.shape
    hidden = gate_ref.shape[1]
    barrier = pltpu.get_barrier_semaphore()
    greeted = greet_group(barrier)
    step_in, step_out = hidden_tile(hidden), width_tile(width)

    def branch(at):
        columns = lane_tile(at, step_out)
        resid_ref[:, columns] = x_ref[:, columns].astype(jnp.float32) + forward_dot(
            low_ref[...], out_ref[:, columns]
        )

    tiles(width // step_out, branch)
    gain = gain_ref[...]
    scale = norm_scale(resid_ref[...])
    gathered = GroupGather(lambda shard: all_n_ref.at[shard], n_sends, n_arrivals)
    fsdp, chips = gathered.fsdp, gathered.chips
    all_n_ref[fsdp] = (resid_ref[...] * scale * gain).astype(jnp.bfloat16)
    pl.semaphore_wait(barrier, greeted)
    gathered.start(all_n_ref.at[fsdp])
    layer_sum = GroupScatter(*down_scratch, down_sends, down_arrivals)
    grad_sum = GroupScatter(*grad_scratch, grad_sends, grad_arrivals)

    def hidden_part(shard):
        def body(at):
            columns = lane_tile(at, step_in)
            normed = all_n_ref[shard]
            gate = forward_dot(normed, gate_ref[:, columns])
            upward = forward_dot(normed, up_ref[:, columns])
            grad_act = dot_columns(
                all_g_ref[shard], down_ref[pl.ds(pl.multiple_of(at * step_in, LANES), step_in), :]
            )
            sigmoid = jax.nn.sigmoid(gate)
            silu = gate * sigmoid
            act_ref[shard, :, columns] = (silu * upward).astype(jnp.bfloat16)
            gate_grad[shard, :, columns] = (
                grad_act * upward * (sigmoid * (1.0 + gate * (1.0 - sigmoid)))
            ).astype(jnp.bfloat16)
            up_grad[shard, :, columns] = (grad_act * silu).astype(jnp.bfloat16)

        tiles(hidden // step_in, body)

    def grad_part(shard, target):
        def body(at):
            columns = pl.ds(pl.multiple_of(at * step_out, LANES), step_out)
            target[:, columns] = (
                dot_columns(gate_grad[shard], gate_ref[columns, :])
                + dot_columns(up_grad[shard], up_ref[columns, :])
            ).astype(target.dtype)

        tiles(width // step_out, body)

    def layer_part(shard, target):
        def body(at):
            columns = lane_tile(at, step_out)
            target[:, columns] = forward_dot(act_ref[shard], down_ref[:, columns]).astype(
                target.dtype
            )

        tiles(width // step_out, body)

    hidden_part(fsdp)
    gathered.sibling_here()
    sibling = gathered.sibling
    hidden_part(sibling)
    grad_part(sibling, grad_sum.give_sib)
    grad_sum.to_sibling().start()
    layer_part(sibling, layer_sum.give_sib)
    layer_sum.to_sibling().start()
    gathered.forward()
    grad_part(fsdp, grad_own)
    layer_part(fsdp, layer_own)
    for step in range(1, chips):
        ours = gathered.same_core(chips - step)
        theirs = ours + sibling - fsdp
        gathered.crossed(step)
        hidden_part(theirs)
        grad_part(theirs, grad_sum.give_cross.at[step - 1])
        grad_sum.to_cross(step).start()
        hidden_part(ours)
        grad_part(ours, grad_sum.far.at[step - 1])
        grad_sum.add_cross(step)
        layer_part(theirs, layer_sum.give_cross.at[step - 1])
        layer_sum.to_cross(step).start()
        layer_part(ours, layer_sum.far.at[step - 1])
        layer_sum.add_cross(step)

    for shard in range(group):
        span = slice(shard * rows, (shard + 1) * rows)
        transpose_into(turned_n.at[:, span], all_n_ref.at[shard])
        transpose_into(turned_act.at[:, span], act_ref.at[shard])

    def down_tile(at):
        columns = lane_tile(at, step_out)
        down_part_ref[:, columns] = forward_dot(
            turned_act[...], all_g_ref[:, :, columns].reshape(group * rows, step_out)
        ).astype(jnp.bfloat16)

    tiles(width // step_out, down_tile)
    own = width // group
    row_blocks = own // 16
    for source, target in ((gate_grad, gate_part_ref), (up_grad, up_part_ref)):

        def weight_tile(at):
            columns = lane_tile(at, step_in)
            part = forward_dot(
                turned_n[...], source[:, :, columns].reshape(group * rows, step_in)
            ).astype(jnp.bfloat16)
            for block in range(step_in // LANES):
                first = (at * (step_in // LANES) + block) * row_blocks
                for owner in range(group):
                    target[owner, pl.ds(first, row_blocks)] = part[
                        owner * own : (owner + 1) * own, block * LANES : (block + 1) * LANES
                    ].reshape(row_blocks, 16, LANES)

        tiles(hidden // step_in, weight_tile)
        filled = hidden // LANES * row_blocks
        for spare in range(filled, target.shape[1]):
            for owner in range(group):
                target[owner, spare] = jnp.zeros(target.shape[2:], target.dtype)

    upstream = grad_sum.total(grad_own[...])
    resid = resid_ref[...]
    scaled = upstream * gain
    grad_resid = (
        all_g_ref[fsdp].astype(jnp.float32)
        + scale * scaled
        - resid * scale**3 * jnp.mean(scaled * resid, axis=-1, keepdims=True)
    )
    gain_grad_ref[...] = jnp.sum(upstream * resid * scale, axis=0, keepdims=True)
    resid_grad_ref[...] = grad_resid
    branch_ref[...] = grad_resid.astype(jnp.bfloat16)
    units, _, wide = g_wide_ref.shape
    sequences = units // KVH
    keys = rows // sequences
    groups = wide // keys
    g_wide_ref[:, :HD, :] = jnp.zeros((units, HD, wide), g_wide_ref.dtype)
    for pair in range(H // 2):
        columns = slice(pair * 2 * HD, (pair + 1) * 2 * HD)
        mixed = dot_columns(branch_ref[...], out_ref[columns, :]).astype(jnp.bfloat16)
        for sequence in range(sequences):
            turned = mixed[sequence * keys : (sequence + 1) * keys].T
            for half in range(2):
                head = 2 * pair + half
                unit, member = sequence * KVH + head // groups, head % groups
                g_wide_ref[unit, HD:, member * keys : (member + 1) * keys] = turned[
                    half * HD : (half + 1) * HD
                ]
    layer_ref[...] = (resid + layer_sum.total(layer_own[...])).astype(jnp.bfloat16)
    gathered.sent()
    grad_sum.sent()
    layer_sum.sent()


def spread(blocks, count):
    return -(-blocks // count) * count


def feed_forward(x, low, full_out, my_gate, my_up, my_down, all_g, gain, units, wide):
    group, count = lax.axis_size("fsdp"), lax.axis_size("ctx")
    rows, width = x.shape
    hidden = my_gate.shape[1]
    blocks = spread(hidden // LANES * (width // group // 16), count)
    chips = group // 2
    dma = pltpu.SemaphoreType.DMA((2 * chips - 1,))
    bf16 = jnp.bfloat16
    return pl.pallas_call(
        ffn_kernel,
        out_shape=[
            jax.ShapeDtypeStruct((rows, width), bf16),
            jax.ShapeDtypeStruct((rows, width), jnp.float32),
            jax.ShapeDtypeStruct((rows, width), bf16),
            jax.ShapeDtypeStruct((units, 2 * HD, wide), bf16),
            jax.ShapeDtypeStruct((group, blocks, 16, LANES), bf16),
            jax.ShapeDtypeStruct((group, blocks, 16, LANES), bf16),
            jax.ShapeDtypeStruct((hidden, width), bf16),
            jax.ShapeDtypeStruct((1, width), jnp.float32),
        ],
        in_specs=[VMEM] * 8,
        out_specs=[VMEM] * 8,
        scratch_shapes=[
            pltpu.VMEM((group, rows, width), bf16),
            pltpu.VMEM((width, group * rows), bf16),
            pltpu.VMEM((hidden, group * rows), bf16),
            pltpu.VMEM((group, rows, hidden), bf16),
            pltpu.VMEM((group, rows, hidden), bf16),
            pltpu.VMEM((group, rows, hidden), bf16),
            pltpu.VMEM((rows, width), jnp.float32),
            pltpu.VMEM((rows, width), jnp.float32),
            pltpu.VMEM((rows, width), jnp.float32),
            *scatter_scratch(rows, width),
            *scatter_scratch(rows, width),
            *[dma] * 6,
        ],
        compiler_params=pltpu.CompilerParams(
            collective_id=2, has_side_effects=True, vmem_limit_bytes=60 << 20
        ),
    )(x, low, full_out, my_gate, my_up, my_down, all_g, gain)


class Ring:
    def __init__(self, work, landing, total, semaphores, forward, exchange=False):
        self.fsdp, self.ctx = lax.axis_index("fsdp"), lax.axis_index("ctx")
        self.group, self.count = lax.axis_size("fsdp"), lax.axis_size("ctx")
        self.work, self.landing, self.total = work, landing, total
        self.sends, self.arrivals = semaphores[:2]
        self.part_sends, self.part_arrivals, self.own_sem = semaphores[2:] if exchange else (None,) * 3
        self.exchange = exchange
        side = 0 if forward else 1
        self.place = ring_place(self.ctx, side, self.count)
        self.after = (self.fsdp, ring_ctx(lax.rem(self.place + 1, self.count), side, self.count))
        self.ticks = 2 * self.count - 2 + int(exchange)

    def chunk(self, held, index):
        if self.exchange:
            return held.at[index]
        per = held.shape[0] // self.count
        return held.at[pl.ds(index * per, per)]

    def summing(self, step, index):
        return self.copy(self.chunk(self.work, index), self.landing.at[step], step)

    def handing(self, step, index):
        held = self.chunk(self.total, index)
        return self.copy(held, held, step)

    def copy(self, source, target, step):
        return pltpu.make_async_remote_copy(
            src_ref=source,
            dst_ref=target,
            send_sem=self.sends.at[step],
            recv_sem=self.arrivals.at[step],
            device_id=self.after,
            device_id_type=MESH,
        )

    def part(self, index, step):
        peer = lax.rem(self.fsdp + step, self.group)
        return pltpu.make_async_remote_copy(
            src_ref=self.work.at[index, peer],
            dst_ref=self.total.at[index, self.fsdp],
            send_sem=self.part_sends.at[step - 1],
            recv_sem=self.part_arrivals.at[step - 1],
            device_id=(peer, self.ctx),
            device_id_type=MESH,
        )

    def own_part(self, index):
        return pltpu.make_async_copy(
            self.work.at[index, self.fsdp], self.total.at[index, self.fsdp], self.own_sem
        )

    def start(self):
        self.summing(0, self.place).start()

    def tick(self, at):
        last = self.count - 2
        gap = int(self.exchange)
        step = at - gap * jnp.where(at > last, 1, 0) if self.exchange else at
        index = lax.rem(self.place + 3 * self.count - 1 - step, self.count)

        def add(target):
            part, landed = self.chunk(self.work, index), self.landing.at[jnp.minimum(at, last)]
            for row in range(part.shape[0]):
                target[row] = (
                    part[row].astype(jnp.float32) + landed[row].astype(jnp.float32)
                ).astype(part.dtype)

        @pl.when(at <= last)
        def _():
            self.summing(jnp.minimum(at, last), index).wait_recv()

        @pl.when(at < last)
        def _():
            add(self.chunk(self.work, index))
            self.summing(jnp.minimum(at + 1, last), index).start()

        if self.exchange:

            @pl.when(at == last)
            def _():
                add(self.chunk(self.work, index))
                for peer in range(1, self.group):
                    self.part(index, peer).start()
                self.own_part(index).start()

            @pl.when(at == last + 1)
            def _():
                done = lax.rem(self.place + 1, self.count)
                self.own_part(done).wait()
                for peer in range(1, self.group):
                    self.part(done, peer).wait_recv()
                self.handing(last + 1, done).start()

        else:

            @pl.when(at == last)
            def _():
                add(self.chunk(self.total, index))
                self.handing(last + 1, index).start()

        @pl.when(at > last + gap)
        def _():
            here = jnp.maximum(step, last + 1)
            self.handing(here, index).wait_recv()

            @pl.when(here < 2 * self.count - 3)
            def _():
                self.handing(jnp.minimum(here + 1, 2 * self.count - 3), index).start()

    def finish(self):
        def wait(step, unused):
            self.handing(step, self.place).wait_send()
            return unused

        lax.fori_loop(0, 2 * self.count - 2, wait, 0)
        if self.exchange:
            for peer in range(1, self.group):
                self.part(lax.rem(self.place + 1, self.count), peer).wait_send()


def ring_scratch(chunk, exchange=False):
    count = lax.axis_size("ctx")
    work = (count,) + chunk if exchange else (count * chunk[0],) + chunk[1:]
    return [pltpu.VMEM(work, jnp.bfloat16), pltpu.VMEM((count - 1,) + chunk, jnp.bfloat16)]


def ring_total(chunk, exchange=False):
    count = lax.axis_size("ctx")
    work = (count,) + chunk if exchange else (count * chunk[0],) + chunk[1:]
    return jax.ShapeDtypeStruct(work, jnp.bfloat16)


def ring_semaphores(exchange=False):
    dma, steps = pltpu.SemaphoreType.DMA, 2 * lax.axis_size("ctx") - 2
    parts = lax.axis_size("fsdp") - 1
    return [dma((steps,))] * 2 + ([dma((parts,))] * 2 + [dma] if exchange else [])


def back_kernel(
    q_ref, g_ref, pairs_ref, mix_ref, log_ref, gate_ref, up_ref, down_ref, gain_grad_ref,
    branch_ref, low_t_ref, normed_t_ref, w_query_ref, w_key_ref, w_value_ref, x_ref, gain_ref,
    resid_grad_ref, cos_ref, sin_ref,
    tokens_ref, gate_total, up_total, down_a_total, down_b_total, rest_a_total, rest_b_total,
    peer_got, chain_got,
    kv_ref, stage_ref, final_ref, qg_ref, delta_ref, grad_q_ref,
    gate_work, gate_land, up_work, up_land, down_a_work, down_a_land, down_b_work, down_b_land,
    rest_a_work, rest_a_land, rest_b_work, rest_b_land,
    low_all, normed_all, branch_all, query_all, pair_all, upstream_ref, gain_give, gain_got,
    *semaphores,
):
    steps = Steps()
    fsdp, ctx, group, count = steps.fsdp, steps.ctx, lax.axis_size("fsdp"), lax.axis_size("ctx")
    units, deep, wide = q_ref.shape
    keys = pairs_ref.shape[2]
    rows, width = x_ref.shape
    own = width // group
    taken = iter(semaphores)

    def take(number):
        return [next(taken) for _ in range(number)]

    gate_ring = Ring(gate_work, gate_land, gate_total, take(5), True, True)
    up_ring = Ring(up_work, up_land, up_total, take(5), False, True)
    down_a = Ring(down_a_work, down_a_land, down_a_total, take(2), True)
    down_b = Ring(down_b_work, down_b_land, down_b_total, take(2), False)
    rest_a = Ring(rest_a_work, rest_a_land, rest_a_total, take(2), True)
    rest_b = Ring(rest_b_work, rest_b_land, rest_b_total, take(2), False)
    first_rings = (gate_ring, up_ring, down_a, down_b)
    peer_sends, peer_arrivals, chain_sends, chain_arrivals = take(4)
    branch_gather = GroupGather(lambda shard: branch_all.at[shard], *take(2))
    query_gather = GroupGather(lambda shard: query_all.at[shard], *take(2))
    pair_gather = GroupGather(lambda shard: pair_all.at[shard], *take(2))
    low_sends, low_arrivals, normed_sends, normed_arrivals, gain_sends, gain_arrivals = take(6)
    local_sems, stage_sems = take(2)

    barrier = pltpu.get_barrier_semaphore()
    greeted = steps.greet(barrier) + greet_group(barrier) + 2
    for device in (gate_ring.after, up_ring.after):
        pl.semaphore_signal(barrier, inc=1, device_id=device, device_id_type=MESH)

    loads = []

    def load(source, target):
        copy = pltpu.make_async_copy(source, target, local_sems.at[len(loads)])
        copy.start()
        loads.append(copy)

    load(pairs_ref, kv_ref)
    load(branch_ref, branch_all.at[fsdp])
    load(low_t_ref.at[pl.ds(fsdp * own, own)], low_all.at[:, lane_tile(fsdp, rows)])
    load(normed_t_ref.at[pl.ds(fsdp * own, own)], normed_all.at[:, lane_tile(fsdp, rows)])
    for which in range(2):
        target = (down_a_work, down_b_work)[which]
        load(down_ref.at[which], target)
    n = gate_work.shape[2]
    chunk_loads = []
    for which, (source, target) in enumerate(((gate_ref, gate_work), (up_ref, up_work))):
        for chunk in range(count):
            copy = pltpu.make_async_copy(
                source.at[:, pl.ds(chunk * n, n)],
                target.at[chunk],
                local_sems.at[len(loads) + which * count + chunk],
            )
            copy.start()
            chunk_loads.append(copy)

    def prepare(unit):
        q, g = q_ref[unit], g_ref[unit]
        qg_ref[unit, :wide] = q.T
        qg_ref[unit, wide:] = g.T
        delta_ref[unit] = jnp.sum(
            g[HD:].astype(jnp.float32) * mix_ref[unit], axis=0, keepdims=True
        )
        grad_q_ref[unit] = jnp.zeros((HD, wide), jnp.float32)

    tiles(units, prepare)

    for copy in loads + chunk_loads:
        copy.wait()
    pl.semaphore_wait(barrier, greeted)
    for ring in first_rings:
        ring.start()
    branch_gather.start(branch_ref)

    def slices(source, target, sends, arrivals, step):
        peer = lax.rem(fsdp + step, group)
        return pltpu.make_async_remote_copy(
            src_ref=source.at[pl.ds(peer * own, own)],
            dst_ref=target.at[:, lane_tile(fsdp, rows)],
            send_sem=sends.at[step - 1],
            recv_sem=arrivals.at[step - 1],
            device_id=(peer, ctx),
            device_id_type=MESH,
        )

    turned = [
        slices(*ends, step)
        for ends in (
            (low_t_ref, low_all, low_sends, low_arrivals),
            (normed_t_ref, normed_all, normed_sends, normed_arrivals),
        )
        for step in range(1, group)
    ]
    for copy in turned:
        copy.start()

    def tick(at):
        for ring in first_rings:
            if ring.exchange:
                ring.tick(at)
            else:

                @pl.when(at < ring.ticks)
                def _():
                    ring.tick(jnp.minimum(at, ring.ticks - 1))

    def back(unit, first, blocks, diagonal):
        kv = kv_ref[pl.ds(first, blocks), unit].reshape(blocks * keys, deep)
        scores = jnp.dot(kv, q_ref[unit], preferred_element_type=jnp.float32)
        probs = jnp.exp(scores - log_ref[unit])
        if diagonal:
            probs = jnp.where(causal(keys, wide, scores.shape), probs, 0.0)
        grad_probs = jnp.dot(kv, g_ref[unit], preferred_element_type=jnp.float32)
        grad_scores = (probs * (grad_probs - delta_ref[unit])).astype(jnp.bfloat16)
        both = jnp.concatenate([grad_scores, probs.astype(jnp.bfloat16)], axis=1)
        grad_kv = jnp.dot(both, qg_ref[unit], preferred_element_type=jnp.float32)
        added = jnp.dot(kv.T, grad_scores, preferred_element_type=jnp.float32)
        grad_q_ref[unit] = grad_q_ref[unit] + added[:HD]
        kv_ref[pl.ds(first, blocks), unit] = grad_kv.astype(kv_ref.dtype).reshape(
            blocks, keys, deep
        )

    def over_units(body):
        def two(at):
            body(2 * at)
            body(2 * at + 1)

        tiles(units // 2, two)

    def across(pair):
        return pltpu.make_async_remote_copy(
            src_ref=kv_ref.at[2 * pair + 1 - steps.side],
            dst_ref=peer_got.at[pair],
            send_sem=peer_sends.at[pair],
            recv_sem=peer_arrivals.at[pair],
            device_id=steps.peer,
            device_id_type=MESH,
        )

    def down_chain(pair):
        return pltpu.make_async_remote_copy(
            src_ref=kv_ref.at[2 * pair + steps.side],
            dst_ref=chain_got.at[pair],
            send_sem=chain_sends.at[pair],
            recv_sem=chain_arrivals.at[pair],
            device_id=steps.below,
            device_id_type=MESH,
        )

    def combine(time):
        pair = time - steps.levels + steps.level

        @pl.when(jnp.logical_and(pair >= 0, pair <= steps.level))
        def _():
            for slot, expected, arrival, source in (
                (0, jnp.logical_or(pair < steps.level, steps.side == 0), across, peer_got),
                (1, steps.has_above, down_chain, chain_got),
            ):

                @pl.when(expected)
                def _():
                    arrival(pair).wait_recv()
                    copy = pltpu.make_async_copy(
                        source.at[pair], stage_ref.at[slot], stage_sems.at[slot]
                    )
                    copy.start()
                    copy.wait()

                @pl.when(jnp.logical_not(expected))
                def _():
                    stage_ref[slot] = jnp.zeros(stage_ref.shape[1:], stage_ref.dtype)

            def add(unit):
                final_ref[unit] = (
                    kv_ref[2 * pair + steps.side, unit].astype(jnp.float32)
                    + stage_ref[0, unit].astype(jnp.float32)
                    + stage_ref[1, unit].astype(jnp.float32)
                )

            tiles(units, add)

            @pl.when(pair < steps.level)
            def _():
                kv_ref[2 * pair + steps.side] = final_ref[...].astype(kv_ref.dtype)
                down_chain(pair).start()

    def slot(pair):
        @pl.when(pair < steps.level)
        def _():
            over_units(lambda unit: back(unit, 2 * pair, 2, False))
            across(pair).start()

        @pl.when(pair == steps.level)
        def _():
            over_units(lambda unit: back(unit, ctx, 1, True))

            @pl.when(steps.side == 1)
            def _():
                over_units(lambda unit: back(unit, ctx - 1, 1, False))
                across(steps.level).start()

        tick(pair)
        combine(pair)

    tiles(steps.levels, slot)
    done = steps.levels
    cosine, sine = cos_ref[...], sin_ref[...]

    def unturn(columns):
        first, second = columns[: HD // 2], columns[HD // 2 :]
        return jnp.concatenate(
            [first * cosine + second * sine, second * cosine - first * sine], axis=0
        )

    sequences = units // KVH
    groups = wide // keys
    for sequence in range(sequences):
        span = slice(sequence * keys, (sequence + 1) * keys)
        for pair in range(H // 2):
            heads = []
            for head in (2 * pair, 2 * pair + 1):
                unit, member = sequence * KVH + head // groups, head % groups
                part = grad_q_ref[unit, :, member * keys : (member + 1) * keys]
                heads.append(unturn(part * HD ** (-0.5)))
            query_all[fsdp, span, pair * 2 * HD : (pair + 1) * 2 * HD] = (
                jnp.concatenate(heads, axis=0).astype(jnp.bfloat16).T
            )
    query_gather.start(query_all.at[fsdp])
    tick(done)
    combine(steps.levels)
    kv_width = KVH * HD
    for sequence in range(sequences):
        span = slice(sequence * keys, (sequence + 1) * keys)
        for pair in range(KVH // 2):
            turned_keys, turned_values = [], []
            for unit in (sequence * KVH + 2 * pair, sequence * KVH + 2 * pair + 1):
                part = final_ref[unit].T
                turned_keys.append(unturn(part[:HD]))
                turned_values.append(part[HD:])
            for start, parts in ((0, turned_keys), (kv_width, turned_values)):
                pair_all[fsdp, span, start + pair * 2 * HD : start + (pair + 1) * 2 * HD] = (
                    jnp.concatenate(parts, axis=0).astype(jnp.bfloat16).T
                )
    pair_gather.start(pair_all.at[fsdp])
    branch_gather.forward()
    query_gather.forward()

    step_out = width_tile(width)

    def upstream_tile(at):
        columns = pl.ds(pl.multiple_of(at * step_out, LANES), step_out)
        upstream_ref[:, columns] = (
            dot_columns(query_all[fsdp], w_query_ref[columns, :])
            + dot_columns(pair_all[fsdp, :, :kv_width], w_key_ref[columns, :])
            + dot_columns(pair_all[fsdp, :, kv_width:], w_value_ref[columns, :])
        )

    tiles(width // step_out, upstream_tile)
    inputs = x_ref[...].astype(jnp.float32)
    scale = norm_scale(inputs)
    upstream = upstream_ref[...]
    scaled = upstream * gain_ref[...]
    tokens_ref[...] = (
        resid_grad_ref[...]
        + scale * scaled
        - inputs * scale**3 * jnp.mean(scaled * inputs, axis=-1, keepdims=True)
    )
    gain_attn = jnp.sum(upstream * inputs * scale, axis=0, keepdims=True)
    lanes = width // LANES
    gain_give[...] = jnp.zeros(gain_give.shape, jnp.float32)
    for block in range(lanes):
        columns = slice(block * LANES, (block + 1) * LANES)
        gain_give[block : block + 1, :] = gain_attn[:, columns]
        gain_give[lanes + block : lanes + block + 1, :] = gain_grad_ref[:, columns]

    def gain_copy(step):
        peer = lax.rem(fsdp + step, group)
        return pltpu.make_async_remote_copy(
            src_ref=gain_give,
            dst_ref=gain_got.at[step - 1],
            send_sem=gain_sends.at[step - 1],
            recv_sem=gain_arrivals.at[step - 1],
            device_id=(peer, ctx),
            device_id_type=MESH,
        )

    for step in range(1, group):
        gain_copy(step).start()
    tick(done + 1)
    for copy in turned:
        copy.wait_recv()
    for gather in (branch_gather, query_gather):
        gather.sibling_here()
        for step in range(1, gather.chips):
            gather.crossed(step)
    row_blocks = own // 16

    def weight_grad(left, right, columns, target, first):
        span = 384 if columns % 384 == 0 else LANES

        def body(at):
            part = forward_dot(
                left[...], right[:, :, lane_tile(at, span)].reshape(group * rows, span)
            ).astype(jnp.bfloat16)
            for block in range(span // LANES):
                begin = first + (at * (span // LANES) + block) * row_blocks
                target[pl.ds(begin, row_blocks)] = part[
                    :, block * LANES : (block + 1) * LANES
                ].reshape(row_blocks, 16, LANES)

        tiles(columns // span, body)

    weight_grad(low_all, branch_all, width, rest_b_work, 0)
    weight_grad(normed_all, query_all, width, rest_a_work, 0)
    tick(done + 2)
    pair_gather.forward()
    pair_gather.sibling_here()
    for step in range(1, pair_gather.chips):
        pair_gather.crossed(step)
    blocks = width // LANES * row_blocks
    key_blocks = kv_width // LANES * row_blocks
    weight_grad(normed_all, pair_all.at[:, :, :kv_width], kv_width, rest_a_work, blocks)
    weight_grad(normed_all, pair_all.at[:, :, kv_width:], kv_width, rest_b_work, blocks)
    gains = gain_give[...]
    for step in range(1, group):
        gain_copy(step).wait_recv()
        gains = gains + gain_got[step - 1]
    filled = blocks + key_blocks
    gain_tiles = gains.shape[0] // 16
    rest_a_work[filled : filled + gain_tiles] = gains.astype(jnp.bfloat16).reshape(
        gain_tiles, 16, LANES
    )
    for spare in range(filled + gain_tiles, rest_a_work.shape[0]):
        rest_a_work[spare] = jnp.zeros((16, LANES), jnp.bfloat16)
    for spare in range(filled, rest_b_work.shape[0]):
        rest_b_work[spare] = jnp.zeros((16, LANES), jnp.bfloat16)
    rest_a.start()
    rest_b.start()
    begun = done + 3
    left = gate_ring.ticks - begun

    def last_ticks(at, unused):
        @pl.when(at < left)
        def _():
            tick(jnp.minimum(begun + at, gate_ring.ticks - 1))

        for ring in (rest_a, rest_b):
            ring.tick(at)
        return unused

    lax.fori_loop(0, rest_a.ticks, last_ticks, 0)

    def more_ticks(at, unused):
        tick(begun + at)
        return unused

    lax.fori_loop(rest_a.ticks, max(left, rest_a.ticks), more_ticks, 0)
    for ring in first_rings + (rest_a, rest_b):
        ring.finish()
    for copy in turned:
        copy.wait_send()
    for gather in (branch_gather, query_gather, pair_gather):
        gather.sent()
    for step in range(1, group):
        gain_copy(step).wait_send()

    def sent(pair):
        @pl.when(jnp.logical_or(pair < steps.level, steps.side == 1))
        def _():
            across(pair).wait_send()

        @pl.when(pair < steps.level)
        def _():
            down_chain(pair).wait_send()

    tiles(steps.level + 1, sent)


def layer_back(
    q_wide, g_wide, all_pairs, mix, log_total, gate_part, up_part, down_part, gain_grad, branch,
    low_t, normed_t, w_query, w_key, w_value, x, gain, resid_grad, cosine, sine,
):
    group, count = lax.axis_size("fsdp"), lax.axis_size("ctx")
    units, deep, wide = q_wide.shape
    keys = all_pairs.shape[2]
    rows, width = x.shape
    own, kv_width = width // group, w_key.shape[1]
    bf16, f32 = jnp.bfloat16, jnp.float32
    dma = pltpu.SemaphoreType.DMA
    wide_chunk = (group, gate_part.shape[1] // count, 16, LANES)
    down_chunk = (down_part.shape[1] // count,) + down_part.shape[2:]
    gain_rows = spread(2 * (width // LANES), 16)
    tiles_held = (width + kv_width) // LANES * (own // 16)
    a_chunk = (spread(tiles_held + gain_rows // 16, count) // count, 16, LANES)
    b_chunk = (spread(tiles_held, count) // count, 16, LANES)
    levels = count // 2
    return pl.pallas_call(
        back_kernel,
        out_shape=[
            jax.ShapeDtypeStruct((rows, width), f32),
            ring_total(wide_chunk, True),
            ring_total(wide_chunk, True),
            ring_total(down_chunk),
            ring_total(down_chunk),
            ring_total(a_chunk),
            ring_total(b_chunk),
            *[jax.ShapeDtypeStruct((levels, units, keys, deep), bf16)] * 2,
        ],
        in_specs=[VMEM, VMEM, ANY, VMEM, VMEM, ANY, ANY, ANY, VMEM, ANY, ANY, ANY] + [VMEM] * 8,
        out_specs=[VMEM] * 7 + [ANY] * 2,
        scratch_shapes=[
            pltpu.VMEM(all_pairs.shape, bf16),
            pltpu.VMEM((2, units, keys, deep), bf16),
            pltpu.VMEM((units, keys, deep), f32),
            pltpu.VMEM((units, 2 * wide, deep), bf16),
            pltpu.VMEM((units, 1, wide), f32),
            pltpu.VMEM((units, HD, wide), f32),
            *ring_scratch(wide_chunk, True),
            *ring_scratch(wide_chunk, True),
            *ring_scratch(down_chunk),
            *ring_scratch(down_chunk),
            *ring_scratch(a_chunk),
            *ring_scratch(b_chunk),
            pltpu.VMEM((own, group * rows), bf16),
            pltpu.VMEM((own, group * rows), bf16),
            pltpu.VMEM((group, rows, width), bf16),
            pltpu.VMEM((group, rows, width), bf16),
            pltpu.VMEM((group, rows, 2 * kv_width), bf16),
            pltpu.VMEM((rows, width), f32),
            pltpu.VMEM((gain_rows, LANES), f32),
            pltpu.VMEM((group - 1, gain_rows, LANES), f32),
            *ring_semaphores(True),
            *ring_semaphores(True),
            *ring_semaphores(),
            *ring_semaphores(),
            *ring_semaphores(),
            *ring_semaphores(),
            *[dma((levels,))] * 4,
            *[group_semaphores()] * 6,
            *[dma((group - 1,))] * 6,
            dma((6 + 2 * count,)),
            dma((2,)),
        ],
        compiler_params=pltpu.CompilerParams(
            collective_id=3, has_side_effects=True, vmem_limit_bytes=62 << 20
        ),
    )(
        q_wide, g_wide, all_pairs, mix, log_total, gate_part, up_part, down_part, gain_grad, branch,
        low_t, normed_t, w_query, w_key, w_value, x, gain, resid_grad, cosine, sine,
    )


def unit_columns(rows, seq_count, block_len):
    groups = H // KVH
    split = rows.reshape(seq_count, block_len, KVH, groups, HD)
    return jnp.transpose(split, (0, 2, 4, 3, 1)).reshape(
        seq_count * KVH, HD, groups * block_len
    )


def from_tiles(held, rows):
    blocks = held.shape[0] * 16 // rows
    split = held.reshape(blocks, rows, LANES)
    return jnp.swapaxes(split, 0, 1).reshape(rows, blocks * LANES).astype(jnp.float32)


def from_parts(total, rows, columns):
    count, group, n = total.shape[:3]
    wide = columns // group // LANES
    split = jnp.swapaxes(total, 0, 1).reshape(group, count * n, 16, LANES)
    split = split[:, : wide * (rows // 16)].reshape(group, wide, rows, LANES)
    return jnp.transpose(split, (2, 0, 1, 3)).reshape(rows, columns).astype(jnp.float32)


def on_device(
    tokens, w_query, w_key, w_value, w_out, w_gate, w_up, w_down, gain_attn, gain_ffn, cotangent
):
    block_len, seq_count, width = tokens.shape
    rows_count = block_len * seq_count
    kv_width = KVH * HD
    full_query, full_key, full_value = [
        lax.all_gather(weight, "fsdp", axis=0, tiled=True) for weight in (w_query, w_key, w_value)
    ]
    full_gain_attn, full_gain_ffn = [
        lax.all_gather(gain, "fsdp", axis=0, tiled=True) for gain in (gain_attn, gain_ffn)
    ]
    my_down = w_down
    my_start = lax.axis_index("ctx") * block_len
    positions = my_start + jnp.arange(block_len, dtype=jnp.int32)
    x_rows = jnp.swapaxes(tokens, 0, 1).reshape(rows_count, width)
    g_rows = jnp.swapaxes(cotangent, 0, 1).reshape(rows_count, width)
    inputs = x_rows.astype(jnp.float32)
    scale_attn = norm_scale(inputs)
    normed_attn = (inputs * scale_attn * full_gain_attn.astype(jnp.float32)).astype(jnp.bfloat16)
    query_raw = forward_dot(normed_attn, full_query)
    key_raw = forward_dot(normed_attn, full_key)
    value_raw = forward_dot(normed_attn, full_value)
    units = seq_count * KVH
    wide = H // KVH * block_len
    queries = (
        rotary(query_raw.reshape(seq_count, block_len, H, HD), positions, 1.0)
        .astype(jnp.bfloat16)
        .reshape(rows_count, width)
    )
    keys_local = rotary(
        key_raw.reshape(seq_count, block_len, KVH, HD), positions, 1.0
    ).astype(jnp.bfloat16)
    values_local = value_raw.astype(jnp.bfloat16).reshape(seq_count, block_len, KVH, HD)
    pairs = jnp.swapaxes(
        jnp.concatenate([keys_local, values_local], axis=-1), 1, 2
    ).reshape(units, block_len, 2 * HD)
    q_unit = unit_columns(queries * jnp.bfloat16(HD ** (-0.5)), seq_count, block_len)
    q_wide = jnp.concatenate([q_unit, jnp.zeros_like(q_unit)], axis=1)
    (attn_low, low_t, mix_unit, log_total, all_pairs, full_out, my_gate, my_up, all_g) = attend(
        q_wide, pairs, w_out, w_gate, w_up, g_rows
    )
    layer_out, grad_resid, grad_branch, g_wide, gate_part, up_part, down_part, gain_term_ffn = (
        feed_forward(
            x_rows,
            attn_low,
            full_out,
            my_gate,
            my_up,
            w_down,
            all_g,
            full_gain_ffn.astype(jnp.float32)[None],
            units,
            wide,
        )
    )
    count = lax.axis_size("ctx")
    down_blocks = down_part.reshape(-1, 16, width)
    spare = spread(down_blocks.shape[0], 2 * count) - down_blocks.shape[0]
    down_blocks = jnp.pad(down_blocks, ((0, spare), (0, 0), (0, 0)))
    freqs = ROTARY_BASE ** (-2.0 * jnp.arange(HD // 2, dtype=jnp.float32) / HD)
    angles = freqs[:, None] * positions.astype(jnp.float32)[None, :]
    grad_tokens, gate_total, up_total, down_a, down_b, rest_a, rest_b, _, _ = layer_back(
        q_wide,
        g_wide,
        all_pairs,
        mix_unit,
        log_total,
        gate_part,
        up_part,
        down_blocks.reshape(2, -1, 16, width),
        gain_term_ffn,
        grad_branch,
        low_t,
        normed_attn.T,
        full_query,
        full_key,
        full_value,
        x_rows,
        full_gain_attn.astype(jnp.float32)[None],
        grad_resid,
        jnp.cos(angles),
        jnp.sin(angles),
    )
    own = gain_attn.shape[0]
    down_rows = jnp.concatenate([down_a, down_b]).reshape(-1, width)[: w_down.shape[0]]
    blocks = width // LANES * (own // 16)
    filled = blocks + kv_width // LANES * (own // 16)
    gains = rest_a[filled:].reshape(-1, LANES)[: 2 * (width // LANES)].reshape(2, width)
    gains = lax.dynamic_slice_in_dim(gains, lax.axis_index("fsdp") * own, own, 1)
    gains = gains.astype(jnp.float32)
    return (
        jnp.swapaxes(layer_out.reshape(seq_count, block_len, width), 0, 1),
        jnp.swapaxes(grad_tokens.reshape(seq_count, block_len, width), 0, 1),
        from_tiles(rest_a[:blocks], own),
        from_tiles(rest_a[blocks:filled], own),
        from_tiles(rest_b[blocks:filled], own),
        from_tiles(rest_b[:blocks], own),
        from_parts(gate_total, own, FF),
        from_parts(up_total, own, FF),
        down_rows.astype(jnp.float32),
        gains[0],
        gains[1],
    )


def solution(mesh):
    return jax.shard_map(
        on_device,
        mesh=mesh,
        in_specs=(
            P("ctx", "fsdp", None),
            P("fsdp", None),
            P("fsdp", None),
            P("fsdp", None),
            P("fsdp", None),
            P("fsdp", None),
            P("fsdp", None),
            P("fsdp", None),
            P("fsdp"),
            P("fsdp"),
            P("ctx", "fsdp", None),
        ),
        out_specs=(
            P("ctx", "fsdp", None),
            P("ctx", "fsdp", None),
            P("fsdp", None),
            P("fsdp", None),
            P("fsdp", None),
            P("fsdp", None),
            P("fsdp", None),
            P("fsdp", None),
            P("fsdp", None),
            P("fsdp"),
            P("fsdp"),
        ),
        check_vma=False,
    )
```

```python
import jax
import jax.numpy as jnp
from jax import lax
from jax.experimental import pallas as pl
from jax.experimental.pallas import tpu as pltpu
from jax.sharding import PartitionSpec as P

H = 18
KVH = 6
HD = 64
FF = 3072


EPSILON = 1e-05
ROTARY_BASE = 10000.0
MASKED_SCORE = -1e30


def rotary(values, positions, direction):
    half = values.shape[-1] // 2
    freqs = ROTARY_BASE ** (-2.0 * jnp.arange(half, dtype=jnp.float32) / values.shape[-1])
    angles = positions.astype(jnp.float32)[:, None] * freqs[None, :]
    cosine = jnp.cos(angles)[:, None, :]
    sine = direction * jnp.sin(angles)[:, None, :]
    first = values[..., :half]
    second = values[..., half:]
    return jnp.concatenate(
        [first * cosine - second * sine, second * cosine + first * sine], axis=-1
    )


def norm_scale(rows):
    return lax.rsqrt(jnp.mean(rows * rows, axis=-1, keepdims=True) + EPSILON)


def forward_dot(left, right):
    return jnp.dot(left, right, preferred_element_type=jnp.float32)


MESH = pl.DeviceIdType.MESH
LANES = 128


def ring_place(ctx, fsdp, count):
    column, side = lax.div(ctx, 2), lax.rem(ctx, 2)
    place = column + side * (count - 1 - 2 * column)
    odd = lax.rem(fsdp, 2)
    return place + odd * (count - 1 - 2 * place)


def ring_ctx(place, fsdp, count):
    odd = lax.rem(fsdp, 2)
    place = place + odd * (count - 1 - 2 * place)
    late = lax.div(place, count // 2)
    return (1 - late) * 2 * place + late * (2 * (count - 1 - place) + 1)


class GroupGather:
    def __init__(self, shard_of, sends, arrivals):
        self.shard_of, self.sends, self.arrivals = shard_of, sends, arrivals
        self.fsdp, self.ctx = lax.axis_index("fsdp"), lax.axis_index("ctx")
        self.chips = lax.axis_size("fsdp") // 2
        self.chip, self.core = lax.div(self.fsdp, 2), lax.rem(self.fsdp, 2)
        self.sibling = 2 * self.chip + 1 - self.core

    def copy(self, source, shard, semaphore, device):
        return pltpu.make_async_remote_copy(
            src_ref=source,
            dst_ref=self.shard_of(shard),
            send_sem=self.sends.at[semaphore],
            recv_sem=self.arrivals.at[semaphore],
            device_id=(device, self.ctx),
            device_id_type=MESH,
        )

    def same_core(self, step):
        return 2 * lax.rem(self.chip + step, self.chips) + self.core

    def across(self, source):
        return self.copy(source, self.fsdp, 0, self.sibling)

    def out(self, source, step):
        return self.copy(source, self.fsdp, step, self.same_core(step))

    def onward(self, step):
        shard = self.same_core(self.chips - step)
        return self.copy(self.shard_of(shard), shard, self.chips - 1 + step, self.sibling)

    def start(self, source):
        for step in range(1, self.chips):
            self.out(source, step).start()
        self.across(source).start()

    def forward(self):
        own = self.shard_of(self.fsdp)
        for step in range(1, self.chips):
            self.out(own, step).wait_recv()
            self.onward(step).start()

    def sibling_here(self):
        self.across(self.shard_of(self.fsdp)).wait_recv()

    def crossed(self, step):
        self.onward(step).wait_recv()

    def sent(self):
        own = self.shard_of(self.fsdp)
        self.across(own).wait_send()
        for step in range(1, self.chips):
            self.out(own, step).wait_send()
            self.onward(step).wait_send()

    def finish(self):
        self.forward()
        self.sibling_here()
        for step in range(1, self.chips):
            self.crossed(step)
        self.sent()


def group_semaphores():
    return pltpu.SemaphoreType.DMA((lax.axis_size("fsdp") - 1,))


def greet_group(barrier):
    fsdp, ctx, group = lax.axis_index("fsdp"), lax.axis_index("ctx"), lax.axis_size("fsdp")
    for step in range(1, group):
        peer = lax.rem(fsdp + step, group)
        pl.semaphore_signal(barrier, inc=1, device_id=(peer, ctx), device_id_type=MESH)
    return group - 1


class Steps:
    def __init__(self):
        self.fsdp, self.ctx = lax.axis_index("fsdp"), lax.axis_index("ctx")
        self.levels = lax.axis_size("ctx") // 2
        self.level, self.side = lax.div(self.ctx, 2), lax.rem(self.ctx, 2)
        self.peer = (self.fsdp, 2 * self.level + 1 - self.side)
        self.above = (self.fsdp, lax.rem(self.ctx + 2, 2 * self.levels))
        self.below = (self.fsdp, lax.rem(self.ctx + 2 * self.levels - 2, 2 * self.levels))
        self.has_above = self.level + 1 < self.levels
        self.has_below = self.level > 0

    def greet(self, barrier):
        pl.semaphore_signal(barrier, inc=1, device_id=self.peer, device_id_type=MESH)

        @pl.when(self.has_above)
        def _():
            pl.semaphore_signal(barrier, inc=1, device_id=self.above, device_id_type=MESH)

        @pl.when(self.has_below)
        def _():
            pl.semaphore_signal(barrier, inc=1, device_id=self.below, device_id_type=MESH)

        return 1 + jnp.minimum(self.level, 1) + jnp.minimum(self.levels - 1 - self.level, 1)


PARTS = 2


def causal(keys, wide, shape):
    key_at = lax.broadcasted_iota(jnp.int32, shape, 0)
    query_at = lax.rem(lax.broadcasted_iota(jnp.int32, shape, 1), keys)
    return key_at <= query_at


def attend_kernel(
    q_ref, kv_ref, out_ref, gate_ref, up_ref, g_ref,
    low_ref, low_t_ref, mix_ref, log_ref, all_ref, full_out_ref, my_gate_ref, my_up_ref, all_g_ref,
    top_ref, total_ref, chain_sends, chain_arrivals, peer_sends, peer_arrivals,
    out_sends, out_arrivals, g_sends, g_arrivals, part_sends, part_arrivals, local_sems,
):
    steps = Steps()
    fsdp, ctx, group = steps.fsdp, steps.ctx, lax.axis_size("fsdp")
    units, deep, wide = q_ref.shape
    keys = kv_ref.shape[1]
    per_part = units // PARTS
    barrier = pltpu.get_barrier_semaphore()
    greeted = steps.greet(barrier) + greet_group(barrier)
    all_ref[ctx] = kv_ref[...]
    pl.semaphore_wait(barrier, greeted)

    def block_copy(level, part, side, semaphores, arrivals, arrives, device):
        block = 2 * (steps.level - level) + side
        held = all_ref.at[block, pl.ds(part * per_part, per_part)]
        return pltpu.make_async_remote_copy(
            src_ref=held,
            dst_ref=held,
            send_sem=semaphores.at[level, part],
            recv_sem=arrivals.at[arrives, part],
            device_id=device,
            device_id_type=MESH,
        )

    def chain(level, part):
        return block_copy(
            level, part, steps.side, chain_sends, chain_arrivals, level + 1, steps.above
        )

    def across(level, part):
        return block_copy(
            level, part, steps.side, peer_sends, peer_arrivals, level, steps.peer
        )

    def pass_on(level, part):
        @pl.when(steps.has_above)
        def _():
            chain(level, part).start()

    for part in range(PARTS):
        pass_on(0, part)

        @pl.when(steps.side == 0)
        def _():
            across(0, part).start()

    rows = out_ref.shape[0]
    columns = my_gate_ref.shape[1]
    gathered = GroupGather(
        lambda shard: full_out_ref.at[pl.ds(shard * rows, rows)], out_sends, out_arrivals
    )
    gathered.start(out_ref)
    gathered_g = GroupGather(lambda shard: all_g_ref.at[shard], g_sends, g_arrivals)
    gathered_g.start(g_ref)
    own_g = pltpu.make_async_copy(g_ref, all_g_ref.at[fsdp], local_sems.at[3])
    own_g.start()
    background = [own_g]
    own_rows = pl.ds(fsdp * rows, rows)
    own_out = pltpu.make_async_copy(out_ref, full_out_ref.at[own_rows], local_sems.at[2])
    own_out.start()
    background.append(own_out)
    for which, (source, target) in enumerate(((gate_ref, my_gate_ref), (up_ref, my_up_ref))):
        for step in range(1, group):
            peer = lax.rem(fsdp + step, group)
            copy = pltpu.make_async_remote_copy(
                src_ref=source.at[:, pl.ds(pl.multiple_of(peer * columns, LANES), columns)],
                dst_ref=target.at[own_rows],
                send_sem=part_sends.at[which, step - 1],
                recv_sem=part_arrivals.at[which, step - 1],
                device_id=(peer, ctx),
                device_id_type=MESH,
            )
            copy.start()
            background.append(copy)
        own = pltpu.make_async_copy(
            source.at[:, pl.ds(pl.multiple_of(fsdp * columns, LANES), columns)],
            target.at[own_rows],
            local_sems.at[which],
        )
        own.start()
        background.append(own)

    def add(unit, kv):
        scores = jnp.dot(kv, q_ref[unit], preferred_element_type=jnp.float32)
        top = top_ref[unit]
        new_top = jnp.maximum(top, jnp.max(scores, axis=0, keepdims=True))
        fade = jnp.exp(top - new_top)
        weights = jnp.exp(scores - new_top)
        top_ref[unit] = new_top
        total_ref[unit] = total_ref[unit] * fade + jnp.sum(weights, axis=0, keepdims=True)
        added = jnp.dot(kv.T, weights.astype(jnp.bfloat16), preferred_element_type=jnp.float32)
        mix_ref[unit] = mix_ref[unit] * fade + added[HD:]

    def over_units(body, first, count):
        def two(at, unused):
            body(first + 2 * at)
            body(first + 2 * at + 1)
            return unused

        lax.fori_loop(0, count // 2, two, 0)

    def diagonal(unit):
        kv = kv_ref[unit]
        scores = jnp.dot(kv, q_ref[unit], preferred_element_type=jnp.float32)
        scores = jnp.where(causal(keys, wide, scores.shape), scores, MASKED_SCORE)
        top = jnp.max(scores, axis=0, keepdims=True)
        weights = jnp.exp(scores - top)
        top_ref[unit] = top
        total_ref[unit] = jnp.sum(weights, axis=0, keepdims=True)
        added = jnp.dot(kv.T, weights.astype(jnp.bfloat16), preferred_element_type=jnp.float32)
        mix_ref[unit] = added[HD:]

    over_units(diagonal, 0, units)

    @pl.when(steps.side == 1)
    def _():
        for part in range(PARTS):
            across(0, part).wait_recv()
            over_units(lambda unit: add(unit, all_ref[ctx - 1, unit]), part * per_part, per_part)

    def level_step(level, unused):
        for part in range(PARTS):
            chain(level - 1, part).wait_recv()
            pass_on(level, part)
            across(level, part).start()
        first = 2 * (steps.level - level)
        for part in range(PARTS):
            across(level, part).wait_recv()
            over_units(
                lambda unit: add(unit, all_ref[pl.ds(first, 2), unit].reshape(2 * keys, deep)),
                part * per_part,
                per_part,
            )
        return unused

    lax.fori_loop(1, steps.level + 1, level_step, 0)

    def close(unit):
        total = total_ref[unit]
        mix_ref[unit] = mix_ref[unit] / total
        log_ref[unit] = top_ref[unit] + jnp.log(total)

    over_units(close, 0, units)
    groups = wide // keys
    for sequence in range(units // KVH):
        for pair in range(H // 2):
            heads = []
            for head in (2 * pair, 2 * pair + 1):
                unit, member = sequence * KVH + head // groups, head % groups
                heads.append(mix_ref[unit, :, member * keys : (member + 1) * keys])
            tile = jnp.concatenate(heads, axis=0).astype(low_ref.dtype)
            span = slice(sequence * keys, (sequence + 1) * keys)
            columns = slice(pair * 2 * HD, (pair + 1) * 2 * HD)
            low_t_ref[columns, span] = tile
            low_ref[span, columns] = tile.T
    gathered.finish()
    gathered_g.finish()
    for copy in background:
        copy.wait()

    def sent(level, unused):
        for part in range(PARTS):

            @pl.when(steps.has_above)
            def _():
                chain(level, part).wait_send()

            @pl.when(jnp.logical_or(level > 0, steps.side == 0))
            def _():
                across(level, part).wait_send()

        return unused

    lax.fori_loop(0, steps.level + 1, sent, 0)


ANY = pl.BlockSpec(memory_space=pl.ANY)
VMEM = pl.BlockSpec(memory_space=pltpu.VMEM)


def attend(q_wide, pairs, w_out, w_gate, w_up, g_rows):
    group, count = lax.axis_size("fsdp"), lax.axis_size("ctx")
    units, deep, wide = q_wide.shape
    keys = pairs.shape[1]
    rows, width = w_out.shape
    hidden = w_gate.shape[1] // group
    dma = pltpu.SemaphoreType.DMA
    sequences = units // KVH
    return pl.pallas_call(
        attend_kernel,
        out_shape=[
            jax.ShapeDtypeStruct((sequences * keys, width), jnp.bfloat16),
            jax.ShapeDtypeStruct((width, sequences * keys), jnp.bfloat16),
            jax.ShapeDtypeStruct((units, HD, wide), jnp.float32),
            jax.ShapeDtypeStruct((units, 1, wide), jnp.float32),
            jax.ShapeDtypeStruct((count,) + pairs.shape, jnp.bfloat16),
            jax.ShapeDtypeStruct((group * rows, width), jnp.bfloat16),
            jax.ShapeDtypeStruct((group * rows, hidden), jnp.bfloat16),
            jax.ShapeDtypeStruct((group * rows, hidden), jnp.bfloat16),
            jax.ShapeDtypeStruct((group,) + g_rows.shape, jnp.bfloat16),
        ],
        in_specs=[VMEM, VMEM, ANY, ANY, ANY, ANY],
        out_specs=[VMEM] * 5 + [ANY] * 4,
        scratch_shapes=[
            pltpu.VMEM((units, 1, wide), jnp.float32),
            pltpu.VMEM((units, 1, wide), jnp.float32),
            dma((count // 2, PARTS)),
            dma((count // 2 + 1, PARTS)),
            dma((count // 2, PARTS)),
            dma((count // 2, PARTS)),
            *[group_semaphores()] * 4,
            dma((2, group - 1)),
            dma((2, group - 1)),
            dma((4,)),
        ],
        compiler_params=pltpu.CompilerParams(
            collective_id=1, has_side_effects=True, vmem_limit_bytes=56 << 20
        ),
    )(q_wide, pairs, w_out, w_gate, w_up, g_rows)


class GroupScatter:
    def __init__(self, give_sib, got_sib, give_cross, got_cross, far, got_far, sends, arrivals):
        self.give_sib, self.got_sib = give_sib, got_sib
        self.give_cross, self.got_cross = give_cross, got_cross
        self.far, self.got_far = far, got_far
        self.sends, self.arrivals = sends, arrivals
        self.fsdp, self.ctx = lax.axis_index("fsdp"), lax.axis_index("ctx")
        self.chips = lax.axis_size("fsdp") // 2
        self.chip, self.core = lax.div(self.fsdp, 2), lax.rem(self.fsdp, 2)
        self.sibling = 2 * self.chip + 1 - self.core

    def copy(self, source, target, semaphore, device):
        return pltpu.make_async_remote_copy(
            src_ref=source,
            dst_ref=target,
            send_sem=self.sends.at[semaphore],
            recv_sem=self.arrivals.at[semaphore],
            device_id=(device, self.ctx),
            device_id_type=MESH,
        )

    def to_sibling(self):
        return self.copy(self.give_sib, self.got_sib, 0, self.sibling)

    def to_cross(self, step):
        return self.copy(
            self.give_cross.at[step - 1], self.got_cross.at[step - 1], step, self.sibling
        )

    def to_far(self, step):
        chip = lax.rem(self.chip + self.chips - step, self.chips)
        return self.copy(
            self.far.at[step - 1],
            self.got_far.at[step - 1],
            self.chips - 1 + step,
            2 * chip + self.core,
        )

    def add_cross(self, step):
        self.to_cross(step).wait_recv()
        held = self.far.at[step - 1]
        held[...] = (
            held[...].astype(jnp.float32) + self.got_cross[step - 1].astype(jnp.float32)
        ).astype(held.dtype)
        self.to_far(step).start()

    def total(self, own):
        self.to_sibling().wait_recv()
        value = own + self.got_sib[...].astype(jnp.float32)
        for step in range(1, self.chips):
            self.to_far(step).wait_recv()
            value = value + self.got_far[step - 1].astype(jnp.float32)
        return value

    def sent(self):
        self.to_sibling().wait_send()
        for step in range(1, self.chips):
            self.to_cross(step).wait_send()
            self.to_far(step).wait_send()


def scatter_scratch(rows, width):
    far = lax.axis_size("fsdp") // 2 - 1
    one, many = (rows, width), (far, rows, width)
    return [pltpu.VMEM(shape, jnp.bfloat16) for shape in (one, one, many, many, many, many)]


def dot_columns(left, right):
    return lax.dot_general(
        left, right, (((1,), (1,)), ((), ())), preferred_element_type=jnp.float32
    )


def tiles(count, body):
    def step(at, unused):
        body(at)
        return unused

    lax.fori_loop(0, count, step, 0)


def lane_tile(at, size):
    return pl.ds(pl.multiple_of(at * size, LANES), size)


def width_tile(width):
    return 384 if width % 384 == 0 else width


def hidden_tile(hidden):
    return 256 if hidden % 256 == 0 else 128


def transpose_into(target, source):
    rows, columns = source.shape

    def body(at):
        part = source[:, lane_tile(at, LANES)]
        target[pl.ds(pl.multiple_of(at * LANES, LANES), LANES), :] = part.T

    tiles(columns // LANES, body)


def ffn_kernel(
    x_ref, low_ref, out_ref, gate_ref, up_ref, down_ref, all_g_ref, gain_ref,
    layer_ref, resid_grad_ref, branch_ref, g_wide_ref, gate_part_ref, up_part_ref, down_part_ref,
    gain_grad_ref,
    all_n_ref, turned_n, turned_act, act_ref, gate_grad, up_grad, resid_ref, layer_own, grad_own,
    *rest,
):
    down_scratch, grad_scratch = rest[:6], rest[6:12]
    n_sends, n_arrivals, down_sends, down_arrivals, grad_sends, grad_arrivals = rest[12:]
    group = lax.axis_size("fsdp")
    rows, width = x_ref.shape
    hidden = gate_ref.shape[1]
    barrier = pltpu.get_barrier_semaphore()
    greeted = greet_group(barrier)
    step_in, step_out = hidden_tile(hidden), width_tile(width)

    def branch(at):
        columns = lane_tile(at, step_out)
        resid_ref[:, columns] = x_ref[:, columns].astype(jnp.float32) + forward_dot(
            low_ref[...], out_ref[:, columns]
        )

    tiles(width // step_out, branch)
    gain = gain_ref[...]
    scale = norm_scale(resid_ref[...])
    gathered = GroupGather(lambda shard: all_n_ref.at[shard], n_sends, n_arrivals)
    fsdp, chips = gathered.fsdp, gathered.chips
    all_n_ref[fsdp] = (resid_ref[...] * scale * gain).astype(jnp.bfloat16)
    pl.semaphore_wait(barrier, greeted)
    gathered.start(all_n_ref.at[fsdp])
    layer_sum = GroupScatter(*down_scratch, down_sends, down_arrivals)
    grad_sum = GroupScatter(*grad_scratch, grad_sends, grad_arrivals)

    def hidden_part(shard):
        def body(at):
            columns = lane_tile(at, step_in)
            normed = all_n_ref[shard]
            gate = forward_dot(normed, gate_ref[:, columns])
            upward = forward_dot(normed, up_ref[:, columns])
            grad_act = dot_columns(
                all_g_ref[shard], down_ref[pl.ds(pl.multiple_of(at * step_in, LANES), step_in), :]
            )
            sigmoid = jax.nn.sigmoid(gate)
            silu = gate * sigmoid
            act_ref[shard, :, columns] = (silu * upward).astype(jnp.bfloat16)
            gate_grad[shard, :, columns] = (
                grad_act * upward * (sigmoid * (1.0 + gate * (1.0 - sigmoid)))
            ).astype(jnp.bfloat16)
            up_grad[shard, :, columns] = (grad_act * silu).astype(jnp.bfloat16)

        tiles(hidden // step_in, body)

    def grad_part(shard, target):
        def body(at):
            columns = pl.ds(pl.multiple_of(at * step_out, LANES), step_out)
            target[:, columns] = (
                dot_columns(gate_grad[shard], gate_ref[columns, :])
                + dot_columns(up_grad[shard], up_ref[columns, :])
            ).astype(target.dtype)

        tiles(width // step_out, body)

    def layer_part(shard, target):
        def body(at):
            columns = lane_tile(at, step_out)
            target[:, columns] = forward_dot(act_ref[shard], down_ref[:, columns]).astype(
                target.dtype
            )

        tiles(width // step_out, body)

    hidden_part(fsdp)
    gathered.sibling_here()
    sibling = gathered.sibling
    hidden_part(sibling)
    grad_part(sibling, grad_sum.give_sib)
    grad_sum.to_sibling().start()
    layer_part(sibling, layer_sum.give_sib)
    layer_sum.to_sibling().start()
    gathered.forward()
    grad_part(fsdp, grad_own)
    layer_part(fsdp, layer_own)
    for step in range(1, chips):
        ours = gathered.same_core(chips - step)
        theirs = ours + sibling - fsdp
        gathered.crossed(step)
        hidden_part(theirs)
        grad_part(theirs, grad_sum.give_cross.at[step - 1])
        grad_sum.to_cross(step).start()
        hidden_part(ours)
        grad_part(ours, grad_sum.far.at[step - 1])
        grad_sum.add_cross(step)
        layer_part(theirs, layer_sum.give_cross.at[step - 1])
        layer_sum.to_cross(step).start()
        layer_part(ours, layer_sum.far.at[step - 1])
        layer_sum.add_cross(step)

    for shard in range(group):
        span = slice(shard * rows, (shard + 1) * rows)
        transpose_into(turned_n.at[:, span], all_n_ref.at[shard])
        transpose_into(turned_act.at[:, span], act_ref.at[shard])

    def down_tile(at):
        columns = lane_tile(at, step_out)
        down_part_ref[:, columns] = forward_dot(
            turned_act[...], all_g_ref[:, :, columns].reshape(group * rows, step_out)
        ).astype(jnp.bfloat16)

    tiles(width // step_out, down_tile)
    own = width // group
    row_blocks = own // 16
    for source, target in ((gate_grad, gate_part_ref), (up_grad, up_part_ref)):

        def weight_tile(at):
            columns = lane_tile(at, step_in)
            part = forward_dot(
                turned_n[...], source[:, :, columns].reshape(group * rows, step_in)
            ).astype(jnp.bfloat16)
            for block in range(step_in // LANES):
                first = (at * (step_in // LANES) + block) * row_blocks
                for owner in range(group):
                    target[owner, pl.ds(first, row_blocks)] = part[
                        owner * own : (owner + 1) * own, block * LANES : (block + 1) * LANES
                    ].reshape(row_blocks, 16, LANES)

        tiles(hidden // step_in, weight_tile)
        filled = hidden // LANES * row_blocks
        for spare in range(filled, target.shape[1]):
            for owner in range(group):
                target[owner, spare] = jnp.zeros(target.shape[2:], target.dtype)

    upstream = grad_sum.total(grad_own[...])
    resid = resid_ref[...]
    scaled = upstream * gain
    grad_resid = (
        all_g_ref[fsdp].astype(jnp.float32)
        + scale * scaled
        - resid * scale**3 * jnp.mean(scaled * resid, axis=-1, keepdims=True)
    )
    gain_grad_ref[...] = jnp.sum(upstream * resid * scale, axis=0, keepdims=True)
    resid_grad_ref[...] = grad_resid
    branch_ref[...] = grad_resid.astype(jnp.bfloat16)
    units, _, wide = g_wide_ref.shape
    sequences = units // KVH
    keys = rows // sequences
    groups = wide // keys
    g_wide_ref[:, :HD, :] = jnp.zeros((units, HD, wide), g_wide_ref.dtype)
    for pair in range(H // 2):
        columns = slice(pair * 2 * HD, (pair + 1) * 2 * HD)
        mixed = dot_columns(branch_ref[...], out_ref[columns, :]).astype(jnp.bfloat16)
        for sequence in range(sequences):
            turned = mixed[sequence * keys : (sequence + 1) * keys].T
            for half in range(2):
                head = 2 * pair + half
                unit, member = sequence * KVH + head // groups, head % groups
                g_wide_ref[unit, HD:, member * keys : (member + 1) * keys] = turned[
                    half * HD : (half + 1) * HD
                ]
    layer_ref[...] = (resid + layer_sum.total(layer_own[...])).astype(jnp.bfloat16)
    gathered.sent()
    grad_sum.sent()
    layer_sum.sent()


def spread(blocks, count):
    return -(-blocks // count) * count


def feed_forward(x, low, full_out, my_gate, my_up, my_down, all_g, gain, units, wide):
    group, count = lax.axis_size("fsdp"), lax.axis_size("ctx")
    rows, width = x.shape
    hidden = my_gate.shape[1]
    blocks = spread(hidden // LANES * (width // group // 16), count)
    chips = group // 2
    dma = pltpu.SemaphoreType.DMA((2 * chips - 1,))
    bf16 = jnp.bfloat16
    return pl.pallas_call(
        ffn_kernel,
        out_shape=[
            jax.ShapeDtypeStruct((rows, width), bf16),
            jax.ShapeDtypeStruct((rows, width), jnp.float32),
            jax.ShapeDtypeStruct((rows, width), bf16),
            jax.ShapeDtypeStruct((units, 2 * HD, wide), bf16),
            jax.ShapeDtypeStruct((group, blocks, 16, LANES), bf16),
            jax.ShapeDtypeStruct((group, blocks, 16, LANES), bf16),
            jax.ShapeDtypeStruct((hidden, width), bf16),
            jax.ShapeDtypeStruct((1, width), jnp.float32),
        ],
        in_specs=[VMEM] * 8,
        out_specs=[VMEM] * 8,
        scratch_shapes=[
            pltpu.VMEM((group, rows, width), bf16),
            pltpu.VMEM((width, group * rows), bf16),
            pltpu.VMEM((hidden, group * rows), bf16),
            pltpu.VMEM((group, rows, hidden), bf16),
            pltpu.VMEM((group, rows, hidden), bf16),
            pltpu.VMEM((group, rows, hidden), bf16),
            pltpu.VMEM((rows, width), jnp.float32),
            pltpu.VMEM((rows, width), jnp.float32),
            pltpu.VMEM((rows, width), jnp.float32),
            *scatter_scratch(rows, width),
            *scatter_scratch(rows, width),
            *[dma] * 6,
        ],
        compiler_params=pltpu.CompilerParams(
            collective_id=2, has_side_effects=True, vmem_limit_bytes=60 << 20
        ),
    )(x, low, full_out, my_gate, my_up, my_down, all_g, gain)


class Ring:
    def __init__(self, work, landing, total, semaphores, forward, exchange=False):
        self.fsdp, self.ctx = lax.axis_index("fsdp"), lax.axis_index("ctx")
        self.group, self.count = lax.axis_size("fsdp"), lax.axis_size("ctx")
        self.work, self.landing, self.total = work, landing, total
        self.sends, self.arrivals = semaphores[:2]
        self.part_sends, self.part_arrivals, self.own_sem = semaphores[2:] if exchange else (None,) * 3
        self.exchange = exchange
        side = 0 if forward else 1
        self.place = ring_place(self.ctx, side, self.count)
        self.after = (self.fsdp, ring_ctx(lax.rem(self.place + 1, self.count), side, self.count))
        self.ticks = 2 * self.count - 2 + int(exchange)

    def chunk(self, held, index):
        if self.exchange:
            return held.at[index]
        per = held.shape[0] // self.count
        return held.at[pl.ds(index * per, per)]

    def summing(self, step, index):
        return self.copy(self.chunk(self.work, index), self.landing.at[step], step)

    def handing(self, step, index):
        held = self.chunk(self.total, index)
        return self.copy(held, held, step)

    def copy(self, source, target, step):
        return pltpu.make_async_remote_copy(
            src_ref=source,
            dst_ref=target,
            send_sem=self.sends.at[step],
            recv_sem=self.arrivals.at[step],
            device_id=self.after,
            device_id_type=MESH,
        )

    def part(self, index, step):
        peer = lax.rem(self.fsdp + step, self.group)
        return pltpu.make_async_remote_copy(
            src_ref=self.work.at[index, peer],
            dst_ref=self.total.at[index, self.fsdp],
            send_sem=self.part_sends.at[step - 1],
            recv_sem=self.part_arrivals.at[step - 1],
            device_id=(peer, self.ctx),
            device_id_type=MESH,
        )

    def own_part(self, index):
        return pltpu.make_async_copy(
            self.work.at[index, self.fsdp], self.total.at[index, self.fsdp], self.own_sem
        )

    def start(self):
        self.summing(0, self.place).start()

    def tick(self, at):
        last = self.count - 2
        gap = int(self.exchange)
        step = at - gap * jnp.where(at > last, 1, 0) if self.exchange else at
        index = lax.rem(self.place + 3 * self.count - 1 - step, self.count)

        def add(target):
            part, landed = self.chunk(self.work, index), self.landing.at[jnp.minimum(at, last)]
            for row in range(part.shape[0]):
                target[row] = (
                    part[row].astype(jnp.float32) + landed[row].astype(jnp.float32)
                ).astype(part.dtype)

        @pl.when(at <= last)
        def _():
            self.summing(jnp.minimum(at, last), index).wait_recv()

        @pl.when(at < last)
        def _():
            add(self.chunk(self.work, index))
            self.summing(jnp.minimum(at + 1, last), index).start()

        if self.exchange:

            @pl.when(at == last)
            def _():
                add(self.chunk(self.work, index))
                for peer in range(1, self.group):
                    self.part(index, peer).start()
                self.own_part(index).start()

            @pl.when(at == last + 1)
            def _():
                done = lax.rem(self.place + 1, self.count)
                self.own_part(done).wait()
                for peer in range(1, self.group):
                    self.part(done, peer).wait_recv()
                self.handing(last + 1, done).start()

        else:

            @pl.when(at == last)
            def _():
                add(self.chunk(self.total, index))
                self.handing(last + 1, index).start()

        @pl.when(at > last + gap)
        def _():
            here = jnp.maximum(step, last + 1)
            self.handing(here, index).wait_recv()

            @pl.when(here < 2 * self.count - 3)
            def _():
                self.handing(jnp.minimum(here + 1, 2 * self.count - 3), index).start()

    def finish(self):
        def wait(step, unused):
            self.handing(step, self.place).wait_send()
            return unused

        lax.fori_loop(0, 2 * self.count - 2, wait, 0)
        if self.exchange:
            for peer in range(1, self.group):
                self.part(lax.rem(self.place + 1, self.count), peer).wait_send()


def ring_scratch(chunk, exchange=False):
    count = lax.axis_size("ctx")
    work = (count,) + chunk if exchange else (count * chunk[0],) + chunk[1:]
    return [pltpu.VMEM(work, jnp.bfloat16), pltpu.VMEM((count - 1,) + chunk, jnp.bfloat16)]


def ring_total(chunk, exchange=False):
    count = lax.axis_size("ctx")
    work = (count,) + chunk if exchange else (count * chunk[0],) + chunk[1:]
    return jax.ShapeDtypeStruct(work, jnp.bfloat16)


def ring_semaphores(exchange=False):
    dma, steps = pltpu.SemaphoreType.DMA, 2 * lax.axis_size("ctx") - 2
    parts = lax.axis_size("fsdp") - 1
    return [dma((steps,))] * 2 + ([dma((parts,))] * 2 + [dma] if exchange else [])


def back_kernel(
    q_ref, g_ref, pairs_ref, mix_ref, log_ref, gate_ref, up_ref, down_ref, gain_grad_ref,
    branch_ref, low_t_ref, normed_t_ref, w_query_ref, w_key_ref, w_value_ref, x_ref, gain_ref,
    resid_grad_ref, cos_ref, sin_ref,
    tokens_ref, gate_total, up_total, down_a_total, down_b_total, out_total, rest_a_total,
    rest_b_total, peer_got, chain_got,
    kv_ref, stage_ref, final_ref, qg_ref, delta_ref, grad_q_ref,
    gate_work, gate_land, up_work, up_land, down_a_work, down_a_land, down_b_work, down_b_land,
    out_work, out_land, rest_a_work, rest_a_land, rest_b_work, rest_b_land,
    low_all, normed_all, branch_all, query_all, pair_all, upstream_ref, gain_give, gain_got,
    *semaphores,
):
    steps = Steps()
    fsdp, ctx, group, count = steps.fsdp, steps.ctx, lax.axis_size("fsdp"), lax.axis_size("ctx")
    units, deep, wide = q_ref.shape
    keys = pairs_ref.shape[2]
    rows, width = x_ref.shape
    own = width // group
    taken = iter(semaphores)

    def take(number):
        return [next(taken) for _ in range(number)]

    gate_ring = Ring(gate_work, gate_land, gate_total, take(5), True, True)
    up_ring = Ring(up_work, up_land, up_total, take(5), False, True)
    down_a = Ring(down_a_work, down_a_land, down_a_total, take(2), True)
    down_b = Ring(down_b_work, down_b_land, down_b_total, take(2), False)
    out_ring = Ring(out_work, out_land, out_total, take(2), True)
    rest_a = Ring(rest_a_work, rest_a_land, rest_a_total, take(2), True)
    rest_b = Ring(rest_b_work, rest_b_land, rest_b_total, take(2), False)
    first_rings = (gate_ring, up_ring, down_a, down_b)
    peer_sends, peer_arrivals, chain_sends, chain_arrivals = take(4)
    branch_gather = GroupGather(lambda shard: branch_all.at[shard], *take(2))
    query_gather = GroupGather(lambda shard: query_all.at[shard], *take(2))
    pair_gather = GroupGather(lambda shard: pair_all.at[shard], *take(2))
    low_sends, low_arrivals, normed_sends, normed_arrivals, gain_sends, gain_arrivals = take(6)
    local_sems, stage_sems = take(2)

    barrier = pltpu.get_barrier_semaphore()
    greeted = steps.greet(barrier) + greet_group(barrier) + 2
    for device in (gate_ring.after, up_ring.after):
        pl.semaphore_signal(barrier, inc=1, device_id=device, device_id_type=MESH)

    loads = []

    def load(source, target):
        copy = pltpu.make_async_copy(source, target, local_sems.at[len(loads)])
        copy.start()
        loads.append(copy)

    n = gate_work.shape[2]
    for source, target in ((gate_ref, gate_work), (up_ref, up_work)):
        for chunk in range(count):
            load(source.at[:, pl.ds(chunk * n, n)], target.at[chunk])
    first = down_a_work.shape[0]
    load(down_ref.at[pl.ds(0, first)], down_a_work)
    load(down_ref.at[pl.ds(first, down_b_work.shape[0])], down_b_work)
    ring_loads = len(loads)
    load(pairs_ref, kv_ref)
    load(branch_ref, branch_all.at[fsdp])
    load(low_t_ref.at[pl.ds(fsdp * own, own)], low_all.at[:, lane_tile(fsdp, rows)])
    load(normed_t_ref.at[pl.ds(fsdp * own, own)], normed_all.at[:, lane_tile(fsdp, rows)])
    for copy in loads[:ring_loads]:
        copy.wait()
    pl.semaphore_wait(barrier, greeted)
    for ring in first_rings:
        ring.start()
    branch_gather.start(branch_ref)

    def slices(source, target, sends, arrivals, step):
        peer = lax.rem(fsdp + step, group)
        return pltpu.make_async_remote_copy(
            src_ref=source.at[pl.ds(peer * own, own)],
            dst_ref=target.at[:, lane_tile(fsdp, rows)],
            send_sem=sends.at[step - 1],
            recv_sem=arrivals.at[step - 1],
            device_id=(peer, ctx),
            device_id_type=MESH,
        )

    turned = [
        slices(*ends, step)
        for ends in (
            (low_t_ref, low_all, low_sends, low_arrivals),
            (normed_t_ref, normed_all, normed_sends, normed_arrivals),
        )
        for step in range(1, group)
    ]
    for copy in turned:
        copy.start()

    def prepare(unit):
        q, g = q_ref[unit], g_ref[unit]
        qg_ref[unit, :wide] = q.T
        qg_ref[unit, wide:] = g.T
        delta_ref[unit] = jnp.sum(
            g[HD:].astype(jnp.float32) * mix_ref[unit], axis=0, keepdims=True
        )
        grad_q_ref[unit] = jnp.zeros((HD, wide), jnp.float32)

    tiles(units, prepare)
    for copy in loads[ring_loads:]:
        copy.wait()

    def tick(ring, at):
        @pl.when(at < ring.ticks)
        def _():
            ring.tick(jnp.minimum(at, ring.ticks - 1))

    def pump(at):
        for turn, ring in enumerate(first_rings):

            @pl.when(lax.rem(at, len(first_rings)) == turn)
            def _():
                tick(ring, lax.div(at, len(first_rings)))

    def back(unit, first, blocks, diagonal):
        kv = kv_ref[pl.ds(first, blocks), unit].reshape(blocks * keys, deep)
        scores = jnp.dot(kv, q_ref[unit], preferred_element_type=jnp.float32)
        probs = jnp.exp(scores - log_ref[unit])
        if diagonal:
            probs = jnp.where(causal(keys, wide, scores.shape), probs, 0.0)
        grad_probs = jnp.dot(kv, g_ref[unit], preferred_element_type=jnp.float32)
        grad_scores = (probs * (grad_probs - delta_ref[unit])).astype(jnp.bfloat16)
        both = jnp.concatenate([grad_scores, probs.astype(jnp.bfloat16)], axis=1)
        grad_kv = jnp.dot(both, qg_ref[unit], preferred_element_type=jnp.float32)
        added = jnp.dot(kv.T, grad_scores, preferred_element_type=jnp.float32)
        grad_q_ref[unit] = grad_q_ref[unit] + added[:HD]
        kv_ref[pl.ds(first, blocks), unit] = grad_kv.astype(kv_ref.dtype).reshape(
            blocks, keys, deep
        )

    def across(pair):
        return pltpu.make_async_remote_copy(
            src_ref=kv_ref.at[2 * pair + 1 - steps.side],
            dst_ref=peer_got.at[pair],
            send_sem=peer_sends.at[pair],
            recv_sem=peer_arrivals.at[pair],
            device_id=steps.peer,
            device_id_type=MESH,
        )

    def down_chain(pair):
        return pltpu.make_async_remote_copy(
            src_ref=kv_ref.at[2 * pair + steps.side],
            dst_ref=chain_got.at[pair],
            send_sem=chain_sends.at[pair],
            recv_sem=chain_arrivals.at[pair],
            device_id=steps.below,
            device_id_type=MESH,
        )

    def combine(time):
        pair = time - steps.levels + steps.level

        @pl.when(jnp.logical_and(pair >= 0, pair <= steps.level))
        def _():
            for slot, expected, arrival, source in (
                (0, jnp.logical_or(pair < steps.level, steps.side == 0), across, peer_got),
                (1, steps.has_above, down_chain, chain_got),
            ):

                @pl.when(expected)
                def _():
                    arrival(pair).wait_recv()
                    copy = pltpu.make_async_copy(
                        source.at[pair], stage_ref.at[slot], stage_sems.at[slot]
                    )
                    copy.start()
                    copy.wait()

                @pl.when(jnp.logical_not(expected))
                def _():
                    stage_ref[slot] = jnp.zeros(stage_ref.shape[1:], stage_ref.dtype)

            def add(unit):
                final_ref[unit] = (
                    kv_ref[2 * pair + steps.side, unit].astype(jnp.float32)
                    + stage_ref[0, unit].astype(jnp.float32)
                    + stage_ref[1, unit].astype(jnp.float32)
                )

            tiles(units, add)

            @pl.when(pair < steps.level)
            def _():
                kv_ref[2 * pair + steps.side] = final_ref[...].astype(kv_ref.dtype)
                down_chain(pair).start()

    turns = units // 2

    def slot(pair):
        def turn(at):
            @pl.when(pair < steps.level)
            def _():
                for unit in (2 * at, 2 * at + 1):
                    back(unit, 2 * pair, 2, False)

            @pl.when(pair == steps.level)
            def _():
                for unit in (2 * at, 2 * at + 1):
                    back(unit, ctx, 1, True)

            @pl.when(jnp.logical_and(pair == steps.level, steps.side == 1))
            def _():
                for unit in (2 * at, 2 * at + 1):
                    back(unit, ctx - 1, 1, False)

            pump(pair * turns + at)

        tiles(turns, turn)

        @pl.when(jnp.logical_or(pair < steps.level, (pair == steps.level) & (steps.side == 1)))
        def _():
            across(pair).start()

        combine(pair)

    tiles(steps.levels, slot)
    pumped = [steps.levels * turns]

    def pump_next(times=1):
        def body(at, unused, begin=pumped[0]):
            pump(begin + at)
            return unused

        lax.fori_loop(0, times, body, 0)
        pumped[0] += times

    def pumping(times, body):
        begin = pumped[0]

        def step(at):
            body(at)
            pump(begin + at)

        tiles(times, step)
        pumped[0] += times

    cosine, sine = cos_ref[...], sin_ref[...]

    def unturn(columns):
        first, second = columns[: HD // 2], columns[HD // 2 :]
        return jnp.concatenate(
            [first * cosine + second * sine, second * cosine - first * sine], axis=0
        )

    sequences = units // KVH
    groups = wide // keys
    for sequence in range(sequences):
        span = slice(sequence * keys, (sequence + 1) * keys)
        for pair in range(H // 2):
            heads = []
            for head in (2 * pair, 2 * pair + 1):
                unit, member = sequence * KVH + head // groups, head % groups
                part = grad_q_ref[unit, :, member * keys : (member + 1) * keys]
                heads.append(unturn(part * HD ** (-0.5)))
            query_all[fsdp, span, pair * 2 * HD : (pair + 1) * 2 * HD] = (
                jnp.concatenate(heads, axis=0).astype(jnp.bfloat16).T
            )
        pump_next()
    query_gather.start(query_all.at[fsdp])
    combine(steps.levels)
    kv_width = KVH * HD
    for sequence in range(sequences):
        span = slice(sequence * keys, (sequence + 1) * keys)
        for pair in range(KVH // 2):
            turned_keys, turned_values = [], []
            for unit in (sequence * KVH + 2 * pair, sequence * KVH + 2 * pair + 1):
                part = final_ref[unit].T
                turned_keys.append(unturn(part[:HD]))
                turned_values.append(part[HD:])
            for start, parts in ((0, turned_keys), (kv_width, turned_values)):
                pair_all[fsdp, span, start + pair * 2 * HD : start + (pair + 1) * 2 * HD] = (
                    jnp.concatenate(parts, axis=0).astype(jnp.bfloat16).T
                )
    pair_gather.start(pair_all.at[fsdp])
    branch_gather.forward()
    pump_next(2)
    query_gather.forward()

    step_out = width_tile(width)

    def upstream_tile(at):
        columns = pl.ds(pl.multiple_of(at * step_out, LANES), step_out)
        upstream_ref[:, columns] = (
            dot_columns(query_all[fsdp], w_query_ref[columns, :])
            + dot_columns(pair_all[fsdp, :, :kv_width], w_key_ref[columns, :])
            + dot_columns(pair_all[fsdp, :, kv_width:], w_value_ref[columns, :])
        )

    pumping(width // step_out, upstream_tile)
    inputs = x_ref[...].astype(jnp.float32)
    scale = norm_scale(inputs)
    upstream = upstream_ref[...]
    scaled = upstream * gain_ref[...]
    tokens_ref[...] = (
        resid_grad_ref[...]
        + scale * scaled
        - inputs * scale**3 * jnp.mean(scaled * inputs, axis=-1, keepdims=True)
    )
    gain_attn = jnp.sum(upstream * inputs * scale, axis=0, keepdims=True)
    lanes = width // LANES
    gain_give[...] = jnp.zeros(gain_give.shape, jnp.float32)
    for block in range(lanes):
        columns = slice(block * LANES, (block + 1) * LANES)
        gain_give[block : block + 1, :] = gain_attn[:, columns]
        gain_give[lanes + block : lanes + block + 1, :] = gain_grad_ref[:, columns]

    def gain_copy(step):
        peer = lax.rem(fsdp + step, group)
        return pltpu.make_async_remote_copy(
            src_ref=gain_give,
            dst_ref=gain_got.at[step - 1],
            send_sem=gain_sends.at[step - 1],
            recv_sem=gain_arrivals.at[step - 1],
            device_id=(peer, ctx),
            device_id_type=MESH,
        )

    for step in range(1, group):
        gain_copy(step).start()
    pump_next()
    for copy in turned:
        copy.wait_recv()
    for gather in (branch_gather, query_gather):
        gather.sibling_here()
        for step in range(1, gather.chips):
            gather.crossed(step)
    row_blocks = own // 16

    def weight_grad(left, right, begin, end, target, first):
        span = LANES * next(n for n in (3, 2, 1) if (end - begin) % (n * LANES) == 0)

        def body(at):
            columns = pl.ds(pl.multiple_of(begin + at * span, LANES), span)
            part = forward_dot(
                left[...], right[:, :, columns].reshape(group * rows, span)
            ).astype(jnp.bfloat16)
            for block in range(span // LANES):
                here = first + (at * (span // LANES) + block) * row_blocks
                target[pl.ds(here, row_blocks)] = part[
                    :, block * LANES : (block + 1) * LANES
                ].reshape(row_blocks, 16, LANES)

        pumping((end - begin) // span, body)
        return first + (end - begin) // LANES * row_blocks

    def clear_from(target, first):
        for spare in range(first, target.shape[0]):
            target[spare] = jnp.zeros((16, LANES), jnp.bfloat16)

    clear_from(out_work, weight_grad(low_all, branch_all, 0, width, out_work, 0))
    out_ring.start()
    split = query_split(width)
    filled_a = weight_grad(normed_all, query_all, 0, split, rest_a_work, 0)
    filled_b = weight_grad(normed_all, query_all, split, width, rest_b_work, 0)
    pair_gather.forward()
    pump_next()
    pair_gather.sibling_here()
    for step in range(1, pair_gather.chips):
        pair_gather.crossed(step)
    filled_b = weight_grad(normed_all, pair_all, 0, 2 * kv_width, rest_b_work, filled_b)
    gains = gain_give[...]
    for step in range(1, group):
        gain_copy(step).wait_recv()
        gains = gains + gain_got[step - 1]
    gain_tiles = gains.shape[0] // 16
    rest_a_work[filled_a : filled_a + gain_tiles] = gains.astype(jnp.bfloat16).reshape(
        gain_tiles, 16, LANES
    )
    clear_from(rest_a_work, filled_a + gain_tiles)
    clear_from(rest_b_work, filled_b)
    rest_a.start()
    rest_b.start()
    begun = pumped[0]
    half = len(first_rings) // 2
    total_pumps = gate_ring.ticks * len(first_rings)

    def last_ticks(at, unused):
        for turn in range(half):
            pump(jnp.minimum(begun + half * at + turn, total_pumps))
        tick(out_ring, at)
        tick(rest_a, at)
        tick(rest_b, at)
        return unused

    rounds = max(out_ring.ticks, -(-(total_pumps - begun) // half))
    lax.fori_loop(0, rounds, last_ticks, 0)
    for ring in first_rings + (out_ring, rest_a, rest_b):
        ring.finish()
    for copy in turned:
        copy.wait_send()
    for gather in (branch_gather, query_gather, pair_gather):
        gather.sent()
    for step in range(1, group):
        gain_copy(step).wait_send()

    def sent(pair):
        @pl.when(jnp.logical_or(pair < steps.level, steps.side == 1))
        def _():
            across(pair).wait_send()

        @pl.when(pair < steps.level)
        def _():
            down_chain(pair).wait_send()

    tiles(steps.level + 1, sent)


def query_split(width):
    return width // LANES * 7 // 9 * LANES


def down_split(blocks, count):
    each = -(-blocks // count)
    first = max(1, each // 3)
    return first, max(1, each - first)


def layer_back(
    q_wide, g_wide, all_pairs, mix, log_total, gate_part, up_part, down_part, gain_grad, branch,
    low_t, normed_t, w_query, w_key, w_value, x, gain, resid_grad, cosine, sine,
):
    group, count = lax.axis_size("fsdp"), lax.axis_size("ctx")
    units, deep, wide = q_wide.shape
    keys = all_pairs.shape[2]
    rows, width = x.shape
    own, kv_width = width // group, w_key.shape[1]
    bf16, f32 = jnp.bfloat16, jnp.float32
    dma = pltpu.SemaphoreType.DMA
    wide_chunk = (group, gate_part.shape[1] // count, 16, LANES)
    down_chunks = [(per,) + down_part.shape[1:] for per in down_split(down_part.shape[0], count)]
    gain_rows = spread(2 * (width // LANES), 16)
    split, row_blocks = query_split(width), own // 16
    out_chunk, a_chunk, b_chunk = [
        (spread(held, count) // count, 16, LANES)
        for held in (
            width // LANES * row_blocks,
            split // LANES * row_blocks + gain_rows // 16,
            (width - split + 2 * kv_width) // LANES * row_blocks,
        )
    ]
    levels = count // 2
    return pl.pallas_call(
        back_kernel,
        out_shape=[
            jax.ShapeDtypeStruct((rows, width), f32),
            ring_total(wide_chunk, True),
            ring_total(wide_chunk, True),
            ring_total(down_chunks[0]),
            ring_total(down_chunks[1]),
            ring_total(out_chunk),
            ring_total(a_chunk),
            ring_total(b_chunk),
            *[jax.ShapeDtypeStruct((levels, units, keys, deep), bf16)] * 2,
        ],
        in_specs=[VMEM, VMEM, ANY, VMEM, VMEM, ANY, ANY, ANY, VMEM, ANY, ANY, ANY] + [VMEM] * 8,
        out_specs=[VMEM] * 8 + [ANY] * 2,
        scratch_shapes=[
            pltpu.VMEM(all_pairs.shape, bf16),
            pltpu.VMEM((2, units, keys, deep), bf16),
            pltpu.VMEM((units, keys, deep), f32),
            pltpu.VMEM((units, 2 * wide, deep), bf16),
            pltpu.VMEM((units, 1, wide), f32),
            pltpu.VMEM((units, HD, wide), f32),
            *ring_scratch(wide_chunk, True),
            *ring_scratch(wide_chunk, True),
            *ring_scratch(down_chunks[0]),
            *ring_scratch(down_chunks[1]),
            *ring_scratch(out_chunk),
            *ring_scratch(a_chunk),
            *ring_scratch(b_chunk),
            pltpu.VMEM((own, group * rows), bf16),
            pltpu.VMEM((own, group * rows), bf16),
            pltpu.VMEM((group, rows, width), bf16),
            pltpu.VMEM((group, rows, width), bf16),
            pltpu.VMEM((group, rows, 2 * kv_width), bf16),
            pltpu.VMEM((rows, width), f32),
            pltpu.VMEM((gain_rows, LANES), f32),
            pltpu.VMEM((group - 1, gain_rows, LANES), f32),
            *ring_semaphores(True),
            *ring_semaphores(True),
            *[kind for _ in range(5) for kind in ring_semaphores()],
            *[dma((levels,))] * 4,
            *[group_semaphores()] * 6,
            *[dma((group - 1,))] * 6,
            dma((6 + 2 * count,)),
            dma((2,)),
        ],
        compiler_params=pltpu.CompilerParams(
            collective_id=3, has_side_effects=True, vmem_limit_bytes=62 << 20
        ),
    )(
        q_wide, g_wide, all_pairs, mix, log_total, gate_part, up_part, down_part, gain_grad, branch,
        low_t, normed_t, w_query, w_key, w_value, x, gain, resid_grad, cosine, sine,
    )


def unit_columns(rows, seq_count, block_len):
    groups = H // KVH
    split = rows.reshape(seq_count, block_len, KVH, groups, HD)
    return jnp.transpose(split, (0, 2, 4, 3, 1)).reshape(
        seq_count * KVH, HD, groups * block_len
    )


def finish_kernel(
    gate_ref, up_ref, down_a_ref, down_b_ref, out_ref, rest_a_ref, rest_b_ref,
    query_grad, key_grad, value_grad, out_grad, gate_grad, up_grad, down_grad,
):
    rows = gate_grad.shape[0]
    row_blocks = rows // 16
    for source, target in ((gate_ref, gate_grad), (up_ref, up_grad)):
        held = source[...].reshape((-1,) + source.shape[3:])
        for block in range(target.shape[1] // LANES):
            target[:, block * LANES : (block + 1) * LANES] = (
                held[block * row_blocks : (block + 1) * row_blocks]
                .reshape(rows, LANES)
                .astype(jnp.float32)
            )

    @pl.when(pl.program_id(0) == 0)
    def _():
        def unpack(source, first, target, begin, end):
            for block in range(begin, end):
                here = first + (block - begin) * row_blocks
                target[:, block * LANES : (block + 1) * LANES] = (
                    source[here : here + row_blocks].reshape(rows, LANES).astype(jnp.float32)
                )
            return first + (end - begin) * row_blocks

        width, kv_width = query_grad.shape[1], key_grad.shape[1]
        split = query_split(width) // LANES
        unpack(out_ref, 0, out_grad, 0, width // LANES)
        unpack(rest_a_ref, 0, query_grad, 0, split)
        at = unpack(rest_b_ref, 0, query_grad, split, width // LANES)
        at = unpack(rest_b_ref, at, key_grad, 0, kv_width // LANES)
        unpack(rest_b_ref, at, value_grad, 0, kv_width // LANES)
        blocks = down_grad.shape[0] // 16
        first = min(down_a_ref.shape[0], blocks)
        for begin, end, source in ((0, first, down_a_ref), (first, blocks, down_b_ref)):
            if end > begin:
                down_grad[begin * 16 : end * 16, :] = (
                    source[: end - begin]
                    .reshape((end - begin) * 16, down_grad.shape[1])
                    .astype(jnp.float32)
                )


def finish(gate, up, down_a, down_b, out, rest_a, rest_b, own, width, kv_width, hidden):
    count, group, n = gate.shape[:3]

    def whole(array):
        return pl.BlockSpec(array.shape, lambda part, rank=len(array.shape): (0,) * rank)

    wide = pl.BlockSpec((count, 1, n, 16, LANES), lambda part: (0, part, 0, 0, 0))
    outs = [
        jax.ShapeDtypeStruct((own, columns), jnp.float32)
        for columns in (width, kv_width, kv_width, width, FF, FF)
    ] + [jax.ShapeDtypeStruct((hidden, width), jnp.float32)]
    slice_spec = pl.BlockSpec((own, FF // group), lambda part: (0, part))
    return pl.pallas_call(
        finish_kernel,
        grid=(group,),
        out_shape=outs,
        in_specs=[wide, wide] + [whole(a) for a in (down_a, down_b, out, rest_a, rest_b)],
        out_specs=[whole(a) for a in outs[:4]] + [slice_spec, slice_spec, whole(outs[6])],
        compiler_params=pltpu.CompilerParams(vmem_limit_bytes=60 << 20),
    )(gate, up, down_a, down_b, out, rest_a, rest_b)


def on_device(
    tokens, w_query, w_key, w_value, w_out, w_gate, w_up, w_down, gain_attn, gain_ffn, cotangent
):
    block_len, seq_count, width = tokens.shape
    rows_count = block_len * seq_count
    kv_width = KVH * HD
    full_query, full_key, full_value = [
        lax.all_gather(weight, "fsdp", axis=0, tiled=True) for weight in (w_query, w_key, w_value)
    ]
    full_gain_attn, full_gain_ffn = [
        lax.all_gather(gain, "fsdp", axis=0, tiled=True) for gain in (gain_attn, gain_ffn)
    ]
    my_down = w_down
    my_start = lax.axis_index("ctx") * block_len
    positions = my_start + jnp.arange(block_len, dtype=jnp.int32)
    x_rows = jnp.swapaxes(tokens, 0, 1).reshape(rows_count, width)
    g_rows = jnp.swapaxes(cotangent, 0, 1).reshape(rows_count, width)
    inputs = x_rows.astype(jnp.float32)
    scale_attn = norm_scale(inputs)
    normed_attn = (inputs * scale_attn * full_gain_attn.astype(jnp.float32)).astype(jnp.bfloat16)
    query_raw = forward_dot(normed_attn, full_query)
    key_raw = forward_dot(normed_attn, full_key)
    value_raw = forward_dot(normed_attn, full_value)
    units = seq_count * KVH
    wide = H // KVH * block_len
    queries = (
        rotary(query_raw.reshape(seq_count, block_len, H, HD), positions, 1.0)
        .astype(jnp.bfloat16)
        .reshape(rows_count, width)
    )
    keys_local = rotary(
        key_raw.reshape(seq_count, block_len, KVH, HD), positions, 1.0
    ).astype(jnp.bfloat16)
    values_local = value_raw.astype(jnp.bfloat16).reshape(seq_count, block_len, KVH, HD)
    pairs = jnp.swapaxes(
        jnp.concatenate([keys_local, values_local], axis=-1), 1, 2
    ).reshape(units, block_len, 2 * HD)
    q_unit = unit_columns(queries * jnp.bfloat16(HD ** (-0.5)), seq_count, block_len)
    q_wide = jnp.concatenate([q_unit, jnp.zeros_like(q_unit)], axis=1)
    (attn_low, low_t, mix_unit, log_total, all_pairs, full_out, my_gate, my_up, all_g) = attend(
        q_wide, pairs, w_out, w_gate, w_up, g_rows
    )
    layer_out, grad_resid, grad_branch, g_wide, gate_part, up_part, down_part, gain_term_ffn = (
        feed_forward(
            x_rows,
            attn_low,
            full_out,
            my_gate,
            my_up,
            w_down,
            all_g,
            full_gain_ffn.astype(jnp.float32)[None],
            units,
            wide,
        )
    )
    count = lax.axis_size("ctx")
    down_blocks = down_part.reshape(-1, 16, width)
    spare = count * sum(down_split(down_blocks.shape[0], count)) - down_blocks.shape[0]
    down_blocks = jnp.pad(down_blocks, ((0, spare), (0, 0), (0, 0)))
    freqs = ROTARY_BASE ** (-2.0 * jnp.arange(HD // 2, dtype=jnp.float32) / HD)
    angles = freqs[:, None] * positions.astype(jnp.float32)[None, :]
    grad_tokens, gate_total, up_total, down_a, down_b, out_sum, rest_a, rest_b, _, _ = layer_back(
        q_wide,
        g_wide,
        all_pairs,
        mix_unit,
        log_total,
        gate_part,
        up_part,
        down_blocks,
        gain_term_ffn,
        grad_branch,
        low_t,
        normed_attn.T,
        full_query,
        full_key,
        full_value,
        x_rows,
        full_gain_attn.astype(jnp.float32)[None],
        grad_resid,
        jnp.cos(angles),
        jnp.sin(angles),
    )
    own = gain_attn.shape[0]
    filled = query_split(width) // LANES * (own // 16)
    gains = rest_a[filled:].reshape(-1, LANES)[: 2 * (width // LANES)].reshape(2, width)
    gains = lax.dynamic_slice_in_dim(gains, lax.axis_index("fsdp") * own, own, 1)
    gains = gains.astype(jnp.float32)
    grads = finish(
        gate_total, up_total, down_a, down_b, out_sum, rest_a, rest_b,
        own, width, kv_width, w_down.shape[0],
    )
    return (
        jnp.swapaxes(layer_out.reshape(seq_count, block_len, width), 0, 1),
        jnp.swapaxes(grad_tokens.reshape(seq_count, block_len, width), 0, 1),
        *grads,
        gains[0],
        gains[1],
    )


def solution(mesh):
    return jax.shard_map(
        on_device,
        mesh=mesh,
        in_specs=(
            P("ctx", "fsdp", None),
            P("fsdp", None),
            P("fsdp", None),
            P("fsdp", None),
            P("fsdp", None),
            P("fsdp", None),
            P("fsdp", None),
            P("fsdp", None),
            P("fsdp"),
            P("fsdp"),
            P("ctx", "fsdp", None),
        ),
        out_specs=(
            P("ctx", "fsdp", None),
            P("ctx", "fsdp", None),
            P("fsdp", None),
            P("fsdp", None),
            P("fsdp", None),
            P("fsdp", None),
            P("fsdp", None),
            P("fsdp", None),
            P("fsdp", None),
            P("fsdp"),
            P("fsdp"),
        ),
        check_vma=False,
    )
```

```python
import jax
import jax.numpy as jnp
from jax import lax
from jax.experimental import pallas as pl
from jax.experimental.pallas import tpu as pltpu
from jax.sharding import PartitionSpec as P

H = 18
KVH = 6
HD = 64
FF = 3072


EPSILON = 1e-05
ROTARY_BASE = 10000.0
MASKED_SCORE = -1e30


def rotary(values, positions, direction):
    half = values.shape[-1] // 2
    freqs = ROTARY_BASE ** (-2.0 * jnp.arange(half, dtype=jnp.float32) / values.shape[-1])
    angles = positions.astype(jnp.float32)[:, None] * freqs[None, :]
    cosine = jnp.cos(angles)[:, None, :]
    sine = direction * jnp.sin(angles)[:, None, :]
    first = values[..., :half]
    second = values[..., half:]
    return jnp.concatenate(
        [first * cosine - second * sine, second * cosine + first * sine], axis=-1
    )


def norm_scale(rows):
    return lax.rsqrt(jnp.mean(rows * rows, axis=-1, keepdims=True) + EPSILON)


def forward_dot(left, right):
    return jnp.dot(left, right, preferred_element_type=jnp.float32)


MESH = pl.DeviceIdType.MESH
LANES = 128


def ring_place(ctx, fsdp, count):
    column, side = lax.div(ctx, 2), lax.rem(ctx, 2)
    place = column + side * (count - 1 - 2 * column)
    odd = lax.rem(fsdp, 2)
    return place + odd * (count - 1 - 2 * place)


def ring_ctx(place, fsdp, count):
    odd = lax.rem(fsdp, 2)
    place = place + odd * (count - 1 - 2 * place)
    late = lax.div(place, count // 2)
    return (1 - late) * 2 * place + late * (2 * (count - 1 - place) + 1)


class GroupGather:
    def __init__(self, shard_of, sends, arrivals):
        self.shard_of, self.sends, self.arrivals = shard_of, sends, arrivals
        self.fsdp, self.ctx = lax.axis_index("fsdp"), lax.axis_index("ctx")
        self.chips = lax.axis_size("fsdp") // 2
        self.chip, self.core = lax.div(self.fsdp, 2), lax.rem(self.fsdp, 2)
        self.sibling = 2 * self.chip + 1 - self.core

    def copy(self, source, shard, semaphore, device):
        return pltpu.make_async_remote_copy(
            src_ref=source,
            dst_ref=self.shard_of(shard),
            send_sem=self.sends.at[semaphore],
            recv_sem=self.arrivals.at[semaphore],
            device_id=(device, self.ctx),
            device_id_type=MESH,
        )

    def same_core(self, step):
        return 2 * lax.rem(self.chip + step, self.chips) + self.core

    def across(self, source):
        return self.copy(source, self.fsdp, 0, self.sibling)

    def out(self, source, step):
        return self.copy(source, self.fsdp, step, self.same_core(step))

    def onward(self, step):
        shard = self.same_core(self.chips - step)
        return self.copy(self.shard_of(shard), shard, self.chips - 1 + step, self.sibling)

    def start(self, source):
        for step in range(1, self.chips):
            self.out(source, step).start()
        self.across(source).start()

    def forward(self):
        own = self.shard_of(self.fsdp)
        for step in range(1, self.chips):
            self.out(own, step).wait_recv()
            self.onward(step).start()

    def sibling_here(self):
        self.across(self.shard_of(self.fsdp)).wait_recv()

    def crossed(self, step):
        self.onward(step).wait_recv()

    def sent(self):
        own = self.shard_of(self.fsdp)
        self.across(own).wait_send()
        for step in range(1, self.chips):
            self.out(own, step).wait_send()
            self.onward(step).wait_send()

    def finish(self):
        self.forward()
        self.sibling_here()
        for step in range(1, self.chips):
            self.crossed(step)
        self.sent()


def group_semaphores():
    return pltpu.SemaphoreType.DMA((lax.axis_size("fsdp") - 1,))


def greet_group(barrier):
    fsdp, ctx, group = lax.axis_index("fsdp"), lax.axis_index("ctx"), lax.axis_size("fsdp")
    for step in range(1, group):
        peer = lax.rem(fsdp + step, group)
        pl.semaphore_signal(barrier, inc=1, device_id=(peer, ctx), device_id_type=MESH)
    return group - 1


class Steps:
    def __init__(self):
        self.fsdp, self.ctx = lax.axis_index("fsdp"), lax.axis_index("ctx")
        self.levels = lax.axis_size("ctx") // 2
        self.level, self.side = lax.div(self.ctx, 2), lax.rem(self.ctx, 2)
        self.peer = (self.fsdp, 2 * self.level + 1 - self.side)
        self.above = (self.fsdp, lax.rem(self.ctx + 2, 2 * self.levels))
        self.below = (self.fsdp, lax.rem(self.ctx + 2 * self.levels - 2, 2 * self.levels))
        self.has_above = self.level + 1 < self.levels
        self.has_below = self.level > 0

    def greet(self, barrier):
        pl.semaphore_signal(barrier, inc=1, device_id=self.peer, device_id_type=MESH)

        @pl.when(self.has_above)
        def _():
            pl.semaphore_signal(barrier, inc=1, device_id=self.above, device_id_type=MESH)

        @pl.when(self.has_below)
        def _():
            pl.semaphore_signal(barrier, inc=1, device_id=self.below, device_id_type=MESH)

        return 1 + jnp.minimum(self.level, 1) + jnp.minimum(self.levels - 1 - self.level, 1)


PARTS = 2


def causal(keys, wide, shape):
    key_at = lax.broadcasted_iota(jnp.int32, shape, 0)
    query_at = lax.rem(lax.broadcasted_iota(jnp.int32, shape, 1), keys)
    return key_at <= query_at


def attend_kernel(
    q_ref, kv_ref, out_ref, gate_ref, up_ref, g_ref,
    low_ref, low_t_ref, mix_ref, log_ref, all_ref, full_out_ref, my_gate_ref, my_up_ref, all_g_ref,
    top_ref, total_ref, chain_sends, chain_arrivals, peer_sends, peer_arrivals,
    out_sends, out_arrivals, g_sends, g_arrivals, part_sends, part_arrivals, local_sems,
):
    steps = Steps()
    fsdp, ctx, group = steps.fsdp, steps.ctx, lax.axis_size("fsdp")
    units, deep, wide = q_ref.shape
    keys = kv_ref.shape[1]
    per_part = units // PARTS
    barrier = pltpu.get_barrier_semaphore()
    greeted = steps.greet(barrier) + greet_group(barrier)
    all_ref[ctx] = kv_ref[...]
    pl.semaphore_wait(barrier, greeted)

    def block_copy(level, part, side, semaphores, arrivals, arrives, device):
        block = 2 * (steps.level - level) + side
        held = all_ref.at[block, pl.ds(part * per_part, per_part)]
        return pltpu.make_async_remote_copy(
            src_ref=held,
            dst_ref=held,
            send_sem=semaphores.at[level, part],
            recv_sem=arrivals.at[arrives, part],
            device_id=device,
            device_id_type=MESH,
        )

    def chain(level, part):
        return block_copy(
            level, part, steps.side, chain_sends, chain_arrivals, level + 1, steps.above
        )

    def across(level, part):
        return block_copy(
            level, part, steps.side, peer_sends, peer_arrivals, level, steps.peer
        )

    def pass_on(level, part):
        @pl.when(steps.has_above)
        def _():
            chain(level, part).start()

    for part in range(PARTS):
        pass_on(0, part)

        @pl.when(steps.side == 0)
        def _():
            across(0, part).start()

    rows = out_ref.shape[0]
    columns = my_gate_ref.shape[1]
    gathered = GroupGather(
        lambda shard: full_out_ref.at[pl.ds(shard * rows, rows)], out_sends, out_arrivals
    )
    gathered.start(out_ref)
    gathered_g = GroupGather(lambda shard: all_g_ref.at[shard], g_sends, g_arrivals)
    gathered_g.start(g_ref)
    own_g = pltpu.make_async_copy(g_ref, all_g_ref.at[fsdp], local_sems.at[3])
    own_g.start()
    background = [own_g]
    own_rows = pl.ds(fsdp * rows, rows)
    own_out = pltpu.make_async_copy(out_ref, full_out_ref.at[own_rows], local_sems.at[2])
    own_out.start()
    background.append(own_out)
    for which, (source, target) in enumerate(((gate_ref, my_gate_ref), (up_ref, my_up_ref))):
        for step in range(1, group):
            peer = lax.rem(fsdp + step, group)
            copy = pltpu.make_async_remote_copy(
                src_ref=source.at[:, pl.ds(pl.multiple_of(peer * columns, LANES), columns)],
                dst_ref=target.at[own_rows],
                send_sem=part_sends.at[which, step - 1],
                recv_sem=part_arrivals.at[which, step - 1],
                device_id=(peer, ctx),
                device_id_type=MESH,
            )
            copy.start()
            background.append(copy)
        own = pltpu.make_async_copy(
            source.at[:, pl.ds(pl.multiple_of(fsdp * columns, LANES), columns)],
            target.at[own_rows],
            local_sems.at[which],
        )
        own.start()
        background.append(own)

    def add(unit, kv):
        scores = jnp.dot(kv, q_ref[unit], preferred_element_type=jnp.float32)
        top = top_ref[unit]
        new_top = jnp.maximum(top, jnp.max(scores, axis=0, keepdims=True))
        fade = jnp.exp(top - new_top)
        weights = jnp.exp(scores - new_top)
        top_ref[unit] = new_top
        total_ref[unit] = total_ref[unit] * fade + jnp.sum(weights, axis=0, keepdims=True)
        added = jnp.dot(kv.T, weights.astype(jnp.bfloat16), preferred_element_type=jnp.float32)
        mix_ref[unit] = mix_ref[unit] * fade + added[HD:]

    def over_units(body, first, count):
        def two(at, unused):
            body(first + 2 * at)
            body(first + 2 * at + 1)
            return unused

        lax.fori_loop(0, count // 2, two, 0)

    def diagonal(unit):
        kv = kv_ref[unit]
        scores = jnp.dot(kv, q_ref[unit], preferred_element_type=jnp.float32)
        scores = jnp.where(causal(keys, wide, scores.shape), scores, MASKED_SCORE)
        top = jnp.max(scores, axis=0, keepdims=True)
        weights = jnp.exp(scores - top)
        top_ref[unit] = top
        total_ref[unit] = jnp.sum(weights, axis=0, keepdims=True)
        added = jnp.dot(kv.T, weights.astype(jnp.bfloat16), preferred_element_type=jnp.float32)
        mix_ref[unit] = added[HD:]

    over_units(diagonal, 0, units)

    @pl.when(steps.side == 1)
    def _():
        for part in range(PARTS):
            across(0, part).wait_recv()
            over_units(lambda unit: add(unit, all_ref[ctx - 1, unit]), part * per_part, per_part)

    def level_step(level, unused):
        for part in range(PARTS):
            chain(level - 1, part).wait_recv()
            pass_on(level, part)
            across(level, part).start()
        first = 2 * (steps.level - level)
        for part in range(PARTS):
            across(level, part).wait_recv()
            over_units(
                lambda unit: add(unit, all_ref[pl.ds(first, 2), unit].reshape(2 * keys, deep)),
                part * per_part,
                per_part,
            )
        return unused

    lax.fori_loop(1, steps.level + 1, level_step, 0)

    def close(unit):
        total = total_ref[unit]
        mix_ref[unit] = mix_ref[unit] / total
        log_ref[unit] = top_ref[unit] + jnp.log(total)

    over_units(close, 0, units)
    groups = wide // keys
    for sequence in range(units // KVH):
        for pair in range(H // 2):
            heads = []
            for head in (2 * pair, 2 * pair + 1):
                unit, member = sequence * KVH + head // groups, head % groups
                heads.append(mix_ref[unit, :, member * keys : (member + 1) * keys])
            tile = jnp.concatenate(heads, axis=0).astype(low_ref.dtype)
            span = slice(sequence * keys, (sequence + 1) * keys)
            columns = slice(pair * 2 * HD, (pair + 1) * 2 * HD)
            low_t_ref[columns, span] = tile
            low_ref[span, columns] = tile.T
    gathered.finish()
    gathered_g.finish()
    for copy in background:
        copy.wait()

    def sent(level, unused):
        for part in range(PARTS):

            @pl.when(steps.has_above)
            def _():
                chain(level, part).wait_send()

            @pl.when(jnp.logical_or(level > 0, steps.side == 0))
            def _():
                across(level, part).wait_send()

        return unused

    lax.fori_loop(0, steps.level + 1, sent, 0)


ANY = pl.BlockSpec(memory_space=pl.ANY)
VMEM = pl.BlockSpec(memory_space=pltpu.VMEM)


def attend(q_wide, pairs, w_out, w_gate, w_up, g_rows):
    group, count = lax.axis_size("fsdp"), lax.axis_size("ctx")
    units, deep, wide = q_wide.shape
    keys = pairs.shape[1]
    rows, width = w_out.shape
    hidden = w_gate.shape[1] // group
    dma = pltpu.SemaphoreType.DMA
    sequences = units // KVH
    return pl.pallas_call(
        attend_kernel,
        out_shape=[
            jax.ShapeDtypeStruct((sequences * keys, width), jnp.bfloat16),
            jax.ShapeDtypeStruct((width, sequences * keys), jnp.bfloat16),
            jax.ShapeDtypeStruct((units, HD, wide), jnp.float32),
            jax.ShapeDtypeStruct((units, 1, wide), jnp.float32),
            jax.ShapeDtypeStruct((count,) + pairs.shape, jnp.bfloat16),
            jax.ShapeDtypeStruct((group * rows, width), jnp.bfloat16),
            jax.ShapeDtypeStruct((group * rows, hidden), jnp.bfloat16),
            jax.ShapeDtypeStruct((group * rows, hidden), jnp.bfloat16),
            jax.ShapeDtypeStruct((group,) + g_rows.shape, jnp.bfloat16),
        ],
        in_specs=[VMEM, VMEM, ANY, ANY, ANY, ANY],
        out_specs=[VMEM] * 5 + [ANY] * 4,
        scratch_shapes=[
            pltpu.VMEM((units, 1, wide), jnp.float32),
            pltpu.VMEM((units, 1, wide), jnp.float32),
            dma((count // 2, PARTS)),
            dma((count // 2 + 1, PARTS)),
            dma((count // 2, PARTS)),
            dma((count // 2, PARTS)),
            *[group_semaphores()] * 4,
            dma((2, group - 1)),
            dma((2, group - 1)),
            dma((4,)),
        ],
        compiler_params=pltpu.CompilerParams(
            collective_id=1, has_side_effects=True, vmem_limit_bytes=56 << 20
        ),
    )(q_wide, pairs, w_out, w_gate, w_up, g_rows)


class Ring:
    def __init__(self, work, landing, total, semaphores, forward, exchange=False):
        self.fsdp, self.ctx = lax.axis_index("fsdp"), lax.axis_index("ctx")
        self.group, self.count = lax.axis_size("fsdp"), lax.axis_size("ctx")
        self.work, self.landing, self.total = work, landing, total
        self.sends, self.arrivals = semaphores[:2]
        self.part_sends, self.part_arrivals, self.own_sem = semaphores[2:] if exchange else (None,) * 3
        self.exchange = exchange
        side = 0 if forward else 1
        self.place = ring_place(self.ctx, side, self.count)
        self.after = (self.fsdp, ring_ctx(lax.rem(self.place + 1, self.count), side, self.count))
        self.ticks = 2 * self.count - 2 + int(exchange)

    def chunk(self, held, index):
        if self.exchange:
            return held.at[index]
        per = held.shape[0] // self.count
        return held.at[pl.ds(index * per, per)]

    def summing(self, step, index):
        return self.copy(self.chunk(self.work, index), self.landing.at[step], step)

    def handing(self, step, index):
        held = self.chunk(self.total, index)
        return self.copy(held, held, step)

    def copy(self, source, target, step):
        return pltpu.make_async_remote_copy(
            src_ref=source,
            dst_ref=target,
            send_sem=self.sends.at[step],
            recv_sem=self.arrivals.at[step],
            device_id=self.after,
            device_id_type=MESH,
        )

    def part(self, index, step):
        peer = lax.rem(self.fsdp + step, self.group)
        return pltpu.make_async_remote_copy(
            src_ref=self.work.at[index, peer],
            dst_ref=self.total.at[index, self.fsdp],
            send_sem=self.part_sends.at[step - 1],
            recv_sem=self.part_arrivals.at[step - 1],
            device_id=(peer, self.ctx),
            device_id_type=MESH,
        )

    def own_part(self, index):
        return pltpu.make_async_copy(
            self.work.at[index, self.fsdp], self.total.at[index, self.fsdp], self.own_sem
        )

    def start(self):
        self.summing(0, self.place).start()

    def tick(self, at):
        last = self.count - 2
        gap = int(self.exchange)
        step = at - gap * jnp.where(at > last, 1, 0) if self.exchange else at
        index = lax.rem(self.place + 3 * self.count - 1 - step, self.count)

        def add(target):
            part, landed = self.chunk(self.work, index), self.landing.at[jnp.minimum(at, last)]
            for row in range(part.shape[0]):
                target[row] = (
                    part[row].astype(jnp.float32) + landed[row].astype(jnp.float32)
                ).astype(part.dtype)

        @pl.when(at <= last)
        def _():
            self.summing(jnp.minimum(at, last), index).wait_recv()

        @pl.when(at < last)
        def _():
            add(self.chunk(self.work, index))
            self.summing(jnp.minimum(at + 1, last), index).start()

        if self.exchange:

            @pl.when(at == last)
            def _():
                add(self.chunk(self.work, index))
                for peer in range(1, self.group):
                    self.part(index, peer).start()
                self.own_part(index).start()

            @pl.when(at == last + 1)
            def _():
                done = lax.rem(self.place + 1, self.count)
                self.own_part(done).wait()
                for peer in range(1, self.group):
                    self.part(done, peer).wait_recv()
                self.handing(last + 1, done).start()

        else:

            @pl.when(at == last)
            def _():
                add(self.chunk(self.total, index))
                self.handing(last + 1, index).start()

        @pl.when(at > last + gap)
        def _():
            here = jnp.maximum(step, last + 1)
            self.handing(here, index).wait_recv()

            @pl.when(here < 2 * self.count - 3)
            def _():
                self.handing(jnp.minimum(here + 1, 2 * self.count - 3), index).start()

    def finish(self):
        def wait(step, unused):
            self.handing(step, self.place).wait_send()
            return unused

        lax.fori_loop(0, 2 * self.count - 2, wait, 0)
        if self.exchange:
            for peer in range(1, self.group):
                self.part(lax.rem(self.place + 1, self.count), peer).wait_send()


class SumRing(Ring):
    def __init__(self, *args):
        super().__init__(*args)
        self.ticks = self.count - 1

    def tick(self, at):
        last = self.count - 2
        index = lax.rem(self.place + 2 * self.count - 1 - at, self.count)
        self.summing(at, index).wait_recv()
        work, landed = self.chunk(self.work, index), self.landing.at[at]

        def add(target):
            for row in range(work.shape[0]):
                target[row] = (
                    work[row].astype(jnp.float32) + landed[row].astype(jnp.float32)
                ).astype(work.dtype)

        @pl.when(at < last)
        def _():
            add(work)
            self.summing(jnp.minimum(at + 1, last), index).start()

        @pl.when(at == last)
        def _():
            add(self.total)

    def finish(self):
        def wait(step, unused):
            self.summing(step, self.place).wait_send()
            return unused

        lax.fori_loop(0, self.ticks, wait, 0)


class SpreadRing(Ring):
    def __init__(self, total, semaphores, forward):
        super().__init__(None, None, total, semaphores, forward)
        self.ticks = self.count - 1
        self.first = lax.rem(self.place + 1, self.count)

    def start(self):
        self.handing(0, self.first).start()

    def tick(self, at):
        index = lax.rem(self.place + self.count - at, self.count)
        self.handing(at, index).wait_recv()

        @pl.when(at < self.count - 2)
        def _():
            self.handing(jnp.minimum(at + 1, self.count - 2), index).start()

    def finish(self):
        def wait(step, unused):
            self.handing(step, self.place).wait_send()
            return unused

        lax.fori_loop(0, self.ticks, wait, 0)


def ring_scratch(chunk, exchange=False):
    count = lax.axis_size("ctx")
    work = (count,) + chunk if exchange else (count * chunk[0],) + chunk[1:]
    return [pltpu.VMEM(work, jnp.bfloat16), pltpu.VMEM((count - 1,) + chunk, jnp.bfloat16)]


def ring_total(chunk, exchange=False):
    count = lax.axis_size("ctx")
    work = (count,) + chunk if exchange else (count * chunk[0],) + chunk[1:]
    return jax.ShapeDtypeStruct(work, jnp.bfloat16)


def ring_semaphores(exchange=False):
    dma, steps = pltpu.SemaphoreType.DMA, 2 * lax.axis_size("ctx") - 2
    parts = lax.axis_size("fsdp") - 1
    return [dma((steps,))] * 2 + ([dma((parts,))] * 2 + [dma] if exchange else [])


def query_split(width):
    return width // LANES * 7 // 9 * LANES


def out_split(width):
    return (width // LANES + 1) // 2 * LANES


def down_split(blocks, count):
    each = -(-blocks // count)
    first = max(1, each // 2)
    return first, max(1, each - first)


class GroupScatter:
    def __init__(self, give_sib, got_sib, give_cross, got_cross, far, got_far, sends, arrivals):
        self.give_sib, self.got_sib = give_sib, got_sib
        self.give_cross, self.got_cross = give_cross, got_cross
        self.far, self.got_far = far, got_far
        self.sends, self.arrivals = sends, arrivals
        self.fsdp, self.ctx = lax.axis_index("fsdp"), lax.axis_index("ctx")
        self.chips = lax.axis_size("fsdp") // 2
        self.chip, self.core = lax.div(self.fsdp, 2), lax.rem(self.fsdp, 2)
        self.sibling = 2 * self.chip + 1 - self.core

    def copy(self, source, target, semaphore, device):
        return pltpu.make_async_remote_copy(
            src_ref=source,
            dst_ref=target,
            send_sem=self.sends.at[semaphore],
            recv_sem=self.arrivals.at[semaphore],
            device_id=(device, self.ctx),
            device_id_type=MESH,
        )

    def to_sibling(self):
        return self.copy(self.give_sib, self.got_sib, 0, self.sibling)

    def to_cross(self, step):
        return self.copy(
            self.give_cross(step), self.got_cross.at[step - 1], step, self.sibling
        )

    def to_far(self, step):
        chip = lax.rem(self.chip + self.chips - step, self.chips)
        return self.copy(
            self.far.at[step - 1],
            self.got_far.at[step - 1],
            self.chips - 1 + step,
            2 * chip + self.core,
        )

    def add_cross(self, step):
        self.to_cross(step).wait_recv()
        held = self.far.at[step - 1]
        held[...] = (
            held[...].astype(jnp.float32) + self.got_cross[step - 1].astype(jnp.float32)
        ).astype(held.dtype)
        self.to_far(step).start()

    def total(self, own):
        self.to_sibling().wait_recv()
        value = own + self.got_sib[...].astype(jnp.float32)
        for step in range(1, self.chips):
            self.to_far(step).wait_recv()
            value = value + self.got_far[step - 1].astype(jnp.float32)
        return value

    def sent(self):
        self.to_sibling().wait_send()
        for step in range(1, self.chips):
            self.to_cross(step).wait_send()
            self.to_far(step).wait_send()


def scatter_scratch(rows, width):
    far = lax.axis_size("fsdp") // 2 - 1
    one, many = (rows, width), (far, rows, width)
    return [pltpu.VMEM(shape, jnp.bfloat16) for shape in (one, one, many, many, many, many)]


def dot_columns(left, right):
    return lax.dot_general(
        left, right, (((1,), (1,)), ((), ())), preferred_element_type=jnp.float32
    )


def tiles(count, body):
    def step(at, unused):
        body(at)
        return unused

    lax.fori_loop(0, count, step, 0)


def lane_tile(at, size):
    return pl.ds(pl.multiple_of(at * size, LANES), size)


def width_tile(width):
    return 384 if width % 384 == 0 else width


def hidden_tile(hidden):
    return 256 if hidden % 256 == 0 else 128


def transpose_into(target, source):
    rows, columns = source.shape

    def body(at):
        part = source[:, lane_tile(at, LANES)]
        target[pl.ds(pl.multiple_of(at * LANES, LANES), LANES), :] = part.T

    tiles(columns // LANES, body)


def ffn_kernel(
    x_ref, low_ref, out_ref, gate_ref, up_ref, down_ref, all_g_ref, gain_ref,
    layer_ref, layer_part_ref, resid_grad_ref, branch_ref, g_wide_ref, gate_part_ref, up_part_ref,
    down_a_done, down_b_done, gain_grad_ref,
    all_n_ref, turned_n, turned_act, act_ref, gate_grad, up_grad, resid_ref, grad_own,
    down_a_work, down_a_land, down_b_work, down_b_land, *rest,
):
    give_sib, got_sib, give_cross, got_cross, far, got_far = rest[:6]
    n_sends, n_arrivals, grad_sends, grad_arrivals = rest[6:10]
    down_a = SumRing(down_a_work, down_a_land, down_a_done, rest[10:12], True)
    down_b = SumRing(down_b_work, down_b_land, down_b_done, rest[12:14], False)
    rings = (down_a, down_b)
    group = lax.axis_size("fsdp")
    rows, width = x_ref.shape
    hidden = gate_ref.shape[1]
    barrier = pltpu.get_barrier_semaphore()
    greeted = greet_group(barrier) + len(rings)
    for ring in rings:
        pl.semaphore_signal(barrier, inc=1, device_id=ring.after, device_id_type=MESH)
    step_in, step_out = hidden_tile(hidden), width_tile(width)

    def branch(at):
        columns = lane_tile(at, step_out)
        resid_ref[:, columns] = x_ref[:, columns].astype(jnp.float32) + forward_dot(
            low_ref[...], out_ref[:, columns]
        )

    tiles(width // step_out, branch)
    gain = gain_ref[...]
    scale = norm_scale(resid_ref[...])
    gathered = GroupGather(lambda shard: all_n_ref.at[shard], n_sends, n_arrivals)
    fsdp, chips = gathered.fsdp, gathered.chips
    all_n_ref[fsdp] = (resid_ref[...] * scale * gain).astype(jnp.bfloat16)
    pl.semaphore_wait(barrier, greeted)
    gathered.start(all_n_ref.at[fsdp])
    grad_sum = GroupScatter(
        give_sib,
        got_sib,
        lambda step: give_cross.at[step - 1],
        got_cross,
        far,
        got_far,
        grad_sends,
        grad_arrivals,
    )

    def hidden_part(shard):
        def body(at):
            columns = lane_tile(at, step_in)
            normed = all_n_ref[shard]
            gate = forward_dot(normed, gate_ref[:, columns])
            upward = forward_dot(normed, up_ref[:, columns])
            grad_act = dot_columns(
                all_g_ref[shard], down_ref[pl.ds(pl.multiple_of(at * step_in, LANES), step_in), :]
            )
            sigmoid = jax.nn.sigmoid(gate)
            silu = gate * sigmoid
            act_ref[shard, :, columns] = (silu * upward).astype(jnp.bfloat16)
            gate_grad[shard, :, columns] = (
                grad_act * upward * (sigmoid * (1.0 + gate * (1.0 - sigmoid)))
            ).astype(jnp.bfloat16)
            up_grad[shard, :, columns] = (grad_act * silu).astype(jnp.bfloat16)

        tiles(hidden // step_in, body)

    def grad_part(shard, target):
        def body(at):
            columns = pl.ds(pl.multiple_of(at * step_out, LANES), step_out)
            target[:, columns] = (
                dot_columns(gate_grad[shard], gate_ref[columns, :])
                + dot_columns(up_grad[shard], up_ref[columns, :])
            ).astype(target.dtype)

        tiles(width // step_out, body)

    hidden_part(fsdp)
    gathered.sibling_here()
    sibling = gathered.sibling
    hidden_part(sibling)
    grad_part(sibling, grad_sum.give_sib)
    grad_sum.to_sibling().start()
    gathered.forward()
    grad_part(fsdp, grad_own)
    for step in range(1, chips):
        ours = gathered.same_core(chips - step)
        theirs = ours + sibling - fsdp
        gathered.crossed(step)
        hidden_part(theirs)
        grad_part(theirs, give_cross.at[step - 1])
        grad_sum.to_cross(step).start()
        hidden_part(ours)
        grad_part(ours, far.at[step - 1])
        grad_sum.add_cross(step)
    for shard in range(group):
        span = slice(shard * rows, (shard + 1) * rows)
        transpose_into(turned_act.at[:, span], act_ref.at[shard])
    blocks = hidden // 16
    first = min(blocks, down_a_work.shape[0])

    def down_tile(at):
        columns = lane_tile(at, step_out)
        part = forward_dot(
            turned_act[...], all_g_ref[:, :, columns].reshape(group * rows, step_out)
        ).astype(jnp.bfloat16)
        for begin, end, work in ((0, first, down_a_work), (first, blocks, down_b_work)):
            if end > begin:
                work[: end - begin, :, columns] = part[begin * 16 : end * 16].reshape(
                    end - begin, 16, step_out
                )

    tiles(width // step_out, down_tile)
    for work, filled in ((down_a_work, first), (down_b_work, blocks - first)):
        for spare in range(filled, work.shape[0]):
            work[spare] = jnp.zeros(work.shape[1:], work.dtype)
    for ring in rings:
        ring.start()
    ticked = [0]

    def ring_tick(at):
        for ring in rings:

            @pl.when(at < ring.ticks)
            def _():
                ring.tick(jnp.minimum(at, ring.ticks - 1))

    def ticking(times, body):
        begin = ticked[0]

        def step(at):
            body(at)
            ring_tick(begin + at)

        tiles(times, step)
        ticked[0] += times

    for shard in range(group):
        span = slice(shard * rows, (shard + 1) * rows)
        transpose_into(turned_n.at[:, span], all_n_ref.at[shard])
    own = width // group
    row_blocks = own // 16
    for source, target in ((gate_grad, gate_part_ref), (up_grad, up_part_ref)):

        def weight_tile(at):
            columns = lane_tile(at, step_in)
            part = forward_dot(
                turned_n[...], source[:, :, columns].reshape(group * rows, step_in)
            ).astype(jnp.bfloat16)
            for block in range(step_in // LANES):
                first = (at * (step_in // LANES) + block) * row_blocks
                for owner in range(group):
                    target[owner, pl.ds(first, row_blocks)] = part[
                        owner * own : (owner + 1) * own, block * LANES : (block + 1) * LANES
                    ].reshape(row_blocks, 16, LANES)

        ticking(hidden // step_in, weight_tile)
        filled = hidden // LANES * row_blocks
        for spare in range(filled, target.shape[1]):
            for owner in range(group):
                target[owner, spare] = jnp.zeros(target.shape[2:], target.dtype)

    def layer_tile(at):
        columns = lane_tile(at, step_out)
        part = forward_dot(
            act_ref[...].reshape(group * rows, hidden), down_ref[:, columns]
        ).reshape(group, rows, step_out)
        layer_part_ref[:, :, columns] = part.astype(jnp.bfloat16)

    ticking(width // step_out, layer_tile)
    layer_ref[...] = resid_ref[...] + layer_part_ref[fsdp].astype(jnp.float32)
    upstream = grad_sum.total(grad_own[...])
    resid = resid_ref[...]
    scaled = upstream * gain
    grad_resid = (
        all_g_ref[fsdp].astype(jnp.float32)
        + scale * scaled
        - resid * scale**3 * jnp.mean(scaled * resid, axis=-1, keepdims=True)
    )
    gain_grad_ref[...] = jnp.sum(upstream * resid * scale, axis=0, keepdims=True)
    resid_grad_ref[...] = grad_resid
    branch_ref[...] = grad_resid.astype(jnp.bfloat16)
    units, _, wide = g_wide_ref.shape
    sequences = units // KVH
    keys = rows // sequences
    groups = wide // keys
    g_wide_ref[:, :HD, :] = jnp.zeros((units, HD, wide), g_wide_ref.dtype)
    for pair in range(H // 2):
        columns = slice(pair * 2 * HD, (pair + 1) * 2 * HD)
        mixed = dot_columns(branch_ref[...], out_ref[columns, :]).astype(jnp.bfloat16)
        for sequence in range(sequences):
            turned = mixed[sequence * keys : (sequence + 1) * keys].T
            for half in range(2):
                head = 2 * pair + half
                unit, member = sequence * KVH + head // groups, head % groups
                g_wide_ref[unit, HD:, member * keys : (member + 1) * keys] = turned[
                    half * HD : (half + 1) * HD
                ]
    begin = ticked[0]
    tiles(max(0, down_a.ticks - begin), lambda at: ring_tick(begin + at))
    gathered.sent()
    grad_sum.sent()
    for ring in rings:
        ring.finish()


def spread(blocks, count):
    return -(-blocks // count) * count


def feed_forward(x, low, full_out, my_gate, my_up, my_down, all_g, gain, units, wide):
    group, count = lax.axis_size("fsdp"), lax.axis_size("ctx")
    rows, width = x.shape
    hidden = my_gate.shape[1]
    blocks = spread(hidden // LANES * (width // group // 16), count)
    chips = group // 2
    dma = pltpu.SemaphoreType.DMA((2 * chips - 1,))
    bf16 = jnp.bfloat16
    down_chunks = [(per, 16, width) for per in down_split(hidden // 16, count)]
    return pl.pallas_call(
        ffn_kernel,
        out_shape=[
            jax.ShapeDtypeStruct((rows, width), jnp.float32),
            jax.ShapeDtypeStruct((group, rows, width), bf16),
            jax.ShapeDtypeStruct((rows, width), jnp.float32),
            jax.ShapeDtypeStruct((rows, width), bf16),
            jax.ShapeDtypeStruct((units, 2 * HD, wide), bf16),
            jax.ShapeDtypeStruct((group, blocks, 16, LANES), bf16),
            jax.ShapeDtypeStruct((group, blocks, 16, LANES), bf16),
            *[jax.ShapeDtypeStruct(chunk, bf16) for chunk in down_chunks],
            jax.ShapeDtypeStruct((1, width), jnp.float32),
        ],
        in_specs=[VMEM] * 8,
        out_specs=[VMEM] * 10,
        scratch_shapes=[
            pltpu.VMEM((group, rows, width), bf16),
            pltpu.VMEM((width, group * rows), bf16),
            pltpu.VMEM((hidden, group * rows), bf16),
            pltpu.VMEM((group, rows, hidden), bf16),
            pltpu.VMEM((group, rows, hidden), bf16),
            pltpu.VMEM((group, rows, hidden), bf16),
            pltpu.VMEM((rows, width), jnp.float32),
            pltpu.VMEM((rows, width), jnp.float32),
            *ring_scratch(down_chunks[0]),
            *ring_scratch(down_chunks[1]),
            *scatter_scratch(rows, width),
            *[dma] * 4,
            *ring_semaphores(),
            *ring_semaphores(),
        ],
        compiler_params=pltpu.CompilerParams(
            collective_id=2, has_side_effects=True, vmem_limit_bytes=60 << 20
        ),
    )(x, low, full_out, my_gate, my_up, my_down, all_g, gain)


def back_kernel(
    q_ref, g_ref, pairs_ref, mix_ref, log_ref, gate_ref, up_ref, down_a_ref, down_b_ref,
    layer_base_ref, layer_part_ref, gain_grad_ref, branch_ref, low_t_ref, normed_t_ref, w_query_ref, w_key_ref, w_value_ref, x_ref, gain_ref,
    resid_grad_ref, cos_ref, sin_ref,
    tokens_ref, layer_ref, gate_total, up_total, down_a_total, down_b_total, out_a_total,
    out_b_total, rest_a_total, rest_b_total, peer_got, chain_got, layer_sib, layer_cross, layer_far,
    kv_ref, stage_ref, final_ref, qg_ref, delta_ref, grad_q_ref,
    gate_work, gate_land, up_work, up_land, out_a_work, out_a_land, out_b_work, out_b_land,
    rest_a_work, rest_a_land, rest_b_work, rest_b_land,
    low_all, normed_all, branch_all, query_all, pair_all, upstream_ref, gain_give, gain_got,
    far_ref, layer_stage,
    *semaphores,
):
    steps = Steps()
    fsdp, ctx, group, count = steps.fsdp, steps.ctx, lax.axis_size("fsdp"), lax.axis_size("ctx")
    units, deep, wide = q_ref.shape
    keys = pairs_ref.shape[2]
    rows, width = x_ref.shape
    own = width // group
    taken = iter(semaphores)

    def take(number):
        return [next(taken) for _ in range(number)]

    gate_ring = Ring(gate_work, gate_land, gate_total, take(5), True, True)
    up_ring = Ring(up_work, up_land, up_total, take(5), False, True)
    down_a = SpreadRing(down_a_total, take(2), True)
    down_b = SpreadRing(down_b_total, take(2), False)
    out_a = Ring(out_a_work, out_a_land, out_a_total, take(2), True)
    out_b = Ring(out_b_work, out_b_land, out_b_total, take(2), False)
    layer_sum = GroupScatter(
        None,
        layer_sib,
        lambda step: layer_part_ref.at[
            2 * lax.rem(lax.div(fsdp, 2) + group // 2 - step, group // 2) + 1 - lax.rem(fsdp, 2)
        ],
        layer_cross,
        far_ref,
        layer_far,
        *take(2),
    )
    layer_sum.give_sib = layer_part_ref.at[layer_sum.sibling]
    rest_a = Ring(rest_a_work, rest_a_land, rest_a_total, take(2), True)
    rest_b = Ring(rest_b_work, rest_b_land, rest_b_total, take(2), False)
    first_rings = (gate_ring, up_ring, down_a, down_b, out_a, out_b)
    peer_sends, peer_arrivals, chain_sends, chain_arrivals = take(4)
    branch_gather = GroupGather(lambda shard: branch_all.at[shard], *take(2))
    query_gather = GroupGather(lambda shard: query_all.at[shard], *take(2))
    pair_gather = GroupGather(lambda shard: pair_all.at[shard], *take(2))
    low_sends, low_arrivals, normed_sends, normed_arrivals, gain_sends, gain_arrivals = take(6)
    local_sems, stage_sems = take(2)

    barrier = pltpu.get_barrier_semaphore()
    greeted = steps.greet(barrier) + greet_group(barrier) + 2
    for device in (gate_ring.after, up_ring.after):
        pl.semaphore_signal(barrier, inc=1, device_id=device, device_id_type=MESH)

    loads = []

    def load(source, target):
        copy = pltpu.make_async_copy(source, target, local_sems.at[len(loads)])
        copy.start()
        loads.append(copy)

    n = gate_work.shape[2]
    for source, target in ((gate_ref, gate_work), (up_ref, up_work)):
        for chunk in range(count):
            load(source.at[:, pl.ds(chunk * n, n)], target.at[chunk])
    for ring, source in ((down_a, down_a_ref), (down_b, down_b_ref)):
        load(source, ring.chunk(ring.total, ring.first))
    ring_loads = len(loads)
    load(pairs_ref, kv_ref)
    load(branch_ref, branch_all.at[fsdp])
    load(low_t_ref.at[pl.ds(fsdp * own, own)], low_all.at[:, lane_tile(fsdp, rows)])
    load(normed_t_ref.at[pl.ds(fsdp * own, own)], normed_all.at[:, lane_tile(fsdp, rows)])
    for copy in loads[:ring_loads]:
        copy.wait()
    pl.semaphore_wait(barrier, greeted)
    for ring in first_rings[:4]:
        ring.start()
    branch_gather.start(branch_ref)
    layer_sum.to_sibling().start()
    for step in range(1, group // 2):
        layer_sum.to_cross(step).start()

    def slices(source, target, sends, arrivals, step):
        peer = lax.rem(fsdp + step, group)
        return pltpu.make_async_remote_copy(
            src_ref=source.at[pl.ds(peer * own, own)],
            dst_ref=target.at[:, lane_tile(fsdp, rows)],
            send_sem=sends.at[step - 1],
            recv_sem=arrivals.at[step - 1],
            device_id=(peer, ctx),
            device_id_type=MESH,
        )

    turned = [
        slices(*ends, step)
        for ends in (
            (low_t_ref, low_all, low_sends, low_arrivals),
            (normed_t_ref, normed_all, normed_sends, normed_arrivals),
        )
        for step in range(1, group)
    ]
    for copy in turned:
        copy.start()

    def prepare(unit):
        q, g = q_ref[unit], g_ref[unit]
        qg_ref[unit, :wide] = q.T
        qg_ref[unit, wide:] = g.T
        delta_ref[unit] = jnp.sum(
            g[HD:].astype(jnp.float32) * mix_ref[unit], axis=0, keepdims=True
        )
        grad_q_ref[unit] = jnp.zeros((HD, wide), jnp.float32)

    tiles(units, prepare)
    for copy in loads[ring_loads:]:
        copy.wait()

    def tick(ring, at):
        @pl.when(jnp.logical_and(at >= 0, at < ring.ticks))
        def _():
            ring.tick(jnp.clip(at, 0, ring.ticks - 1))

    late = steps.levels // 2 + 1

    def pump(at):
        lag = (0, 0, 0, 0, late, late)
        for turn, ring in enumerate(first_rings):

            @pl.when(lax.rem(at, len(first_rings)) == turn)
            def _():
                tick(ring, lax.div(at, len(first_rings)) - lag[turn])

    def back(unit, first, blocks, diagonal):
        kv = kv_ref[pl.ds(first, blocks), unit].reshape(blocks * keys, deep)
        scores = jnp.dot(kv, q_ref[unit], preferred_element_type=jnp.float32)
        probs = jnp.exp(scores - log_ref[unit])
        if diagonal:
            probs = jnp.where(causal(keys, wide, scores.shape), probs, 0.0)
        grad_probs = jnp.dot(kv, g_ref[unit], preferred_element_type=jnp.float32)
        grad_scores = (probs * (grad_probs - delta_ref[unit])).astype(jnp.bfloat16)
        both = jnp.concatenate([grad_scores, probs.astype(jnp.bfloat16)], axis=1)
        grad_kv = jnp.dot(both, qg_ref[unit], preferred_element_type=jnp.float32)
        added = jnp.dot(kv.T, grad_scores, preferred_element_type=jnp.float32)
        grad_q_ref[unit] = grad_q_ref[unit] + added[:HD]
        kv_ref[pl.ds(first, blocks), unit] = grad_kv.astype(kv_ref.dtype).reshape(
            blocks, keys, deep
        )

    def across(pair):
        return pltpu.make_async_remote_copy(
            src_ref=kv_ref.at[2 * pair + 1 - steps.side],
            dst_ref=peer_got.at[pair],
            send_sem=peer_sends.at[pair],
            recv_sem=peer_arrivals.at[pair],
            device_id=steps.peer,
            device_id_type=MESH,
        )

    def down_chain(pair):
        return pltpu.make_async_remote_copy(
            src_ref=kv_ref.at[2 * pair + steps.side],
            dst_ref=chain_got.at[pair],
            send_sem=chain_sends.at[pair],
            recv_sem=chain_arrivals.at[pair],
            device_id=steps.below,
            device_id_type=MESH,
        )

    def combine(time):
        pair = time - steps.levels + steps.level

        @pl.when(jnp.logical_and(pair >= 0, pair <= steps.level))
        def _():
            for slot, expected, arrival, source in (
                (0, jnp.logical_or(pair < steps.level, steps.side == 0), across, peer_got),
                (1, steps.has_above, down_chain, chain_got),
            ):

                @pl.when(expected)
                def _():
                    arrival(pair).wait_recv()
                    copy = pltpu.make_async_copy(
                        source.at[pair], stage_ref.at[slot], stage_sems.at[slot]
                    )
                    copy.start()
                    copy.wait()

                @pl.when(jnp.logical_not(expected))
                def _():
                    stage_ref[slot] = jnp.zeros(stage_ref.shape[1:], stage_ref.dtype)

            def add(unit):
                final_ref[unit] = (
                    kv_ref[2 * pair + steps.side, unit].astype(jnp.float32)
                    + stage_ref[0, unit].astype(jnp.float32)
                    + stage_ref[1, unit].astype(jnp.float32)
                )

            tiles(units, add)

            @pl.when(pair < steps.level)
            def _():
                kv_ref[2 * pair + steps.side] = final_ref[...].astype(kv_ref.dtype)
                down_chain(pair).start()

    row_blocks = own // 16

    def weight_grad(left, right, begin, end, target, first, loop):
        span = LANES * next(n for n in (3, 2, 1) if (end - begin) % (n * LANES) == 0)

        def body(at):
            columns = pl.ds(pl.multiple_of(begin + at * span, LANES), span)
            part = forward_dot(
                left[...], right[:, :, columns].reshape(group * rows, span)
            ).astype(jnp.bfloat16)
            for block in range(span // LANES):
                here = first + (at * (span // LANES) + block) * row_blocks
                target[pl.ds(here, row_blocks)] = part[
                    :, block * LANES : (block + 1) * LANES
                ].reshape(row_blocks, 16, LANES)

        loop((end - begin) // span, body)
        return first + (end - begin) // LANES * row_blocks

    def clear_from(target, first):
        for spare in range(first, target.shape[0]):
            target[spare] = jnp.zeros((16, LANES), jnp.bfloat16)

    def out_grad():
        for copy in turned[: group - 1]:
            copy.wait_recv()
        branch_gather.forward()
        branch_gather.sibling_here()
        for step in range(1, branch_gather.chips):
            branch_gather.crossed(step)
        split = out_split(width)
        clear_from(out_a_work, weight_grad(low_all, branch_all, 0, split, out_a_work, 0, tiles))
        clear_from(out_b_work, weight_grad(low_all, branch_all, split, width, out_b_work, 0, tiles))
        out_a.start()
        out_b.start()

    turns = units // 2

    def slot(pair):
        def turn(at):
            @pl.when(pair < steps.level)
            def _():
                for unit in (2 * at, 2 * at + 1):
                    back(unit, 2 * pair, 2, False)

            @pl.when(pair == steps.level)
            def _():
                for unit in (2 * at, 2 * at + 1):
                    back(unit, ctx, 1, True)

            @pl.when(jnp.logical_and(pair == steps.level, steps.side == 1))
            def _():
                for unit in (2 * at, 2 * at + 1):
                    back(unit, ctx - 1, 1, False)

            pump(pair * turns + at)

        tiles(turns, turn)

        @pl.when(jnp.logical_or(pair < steps.level, (pair == steps.level) & (steps.side == 1)))
        def _():
            across(pair).start()

        combine(pair)

        @pl.when(pair == late - 1)
        def _():
            out_grad()

    tiles(steps.levels, slot)
    pumped = [steps.levels * turns]

    def pump_next(times=1):
        def body(at, unused, begin=pumped[0]):
            pump(begin + at)
            return unused

        lax.fori_loop(0, times, body, 0)
        pumped[0] += times

    def pumping(times, body):
        begin = pumped[0]

        def step(at):
            body(at)
            pump(begin + at)

        tiles(times, step)
        pumped[0] += times

    cosine, sine = cos_ref[...], sin_ref[...]

    def unturn(columns):
        first, second = columns[: HD // 2], columns[HD // 2 :]
        return jnp.concatenate(
            [first * cosine + second * sine, second * cosine - first * sine], axis=0
        )

    sequences = units // KVH
    groups = wide // keys
    for sequence in range(sequences):
        span = slice(sequence * keys, (sequence + 1) * keys)
        for pair in range(H // 2):
            heads = []
            for head in (2 * pair, 2 * pair + 1):
                unit, member = sequence * KVH + head // groups, head % groups
                part = grad_q_ref[unit, :, member * keys : (member + 1) * keys]
                heads.append(unturn(part * HD ** (-0.5)))
            query_all[fsdp, span, pair * 2 * HD : (pair + 1) * 2 * HD] = (
                jnp.concatenate(heads, axis=0).astype(jnp.bfloat16).T
            )
        pump_next()
    query_gather.start(query_all.at[fsdp])
    combine(steps.levels)
    kv_width = KVH * HD
    for sequence in range(sequences):
        span = slice(sequence * keys, (sequence + 1) * keys)
        for pair in range(KVH // 2):
            turned_keys, turned_values = [], []
            for unit in (sequence * KVH + 2 * pair, sequence * KVH + 2 * pair + 1):
                part = final_ref[unit].T
                turned_keys.append(unturn(part[:HD]))
                turned_values.append(part[HD:])
            for start, parts in ((0, turned_keys), (kv_width, turned_values)):
                pair_all[fsdp, span, start + pair * 2 * HD : start + (pair + 1) * 2 * HD] = (
                    jnp.concatenate(parts, axis=0).astype(jnp.bfloat16).T
                )
    pair_gather.start(pair_all.at[fsdp])
    pump_next(2)
    query_gather.forward()
    for step in range(1, layer_sum.chips):
        ours = layer_part_ref.at[2 * lax.rem(layer_sum.chip + layer_sum.chips - step, layer_sum.chips) + layer_sum.core]
        for source, target in ((ours, far_ref.at[step - 1]), (layer_cross.at[step - 1], layer_stage)):
            if source is not ours:
                layer_sum.to_cross(step).wait_recv()
            copy = pltpu.make_async_copy(source, target, stage_sems.at[0])
            copy.start()
            copy.wait()
        far_ref[step - 1] = (
            far_ref[step - 1].astype(jnp.float32) + layer_stage[...].astype(jnp.float32)
        ).astype(jnp.bfloat16)
        layer_sum.to_far(step).start()

    step_out = width_tile(width)

    def upstream_tile(at):
        columns = pl.ds(pl.multiple_of(at * step_out, LANES), step_out)
        upstream_ref[:, columns] = (
            dot_columns(query_all[fsdp], w_query_ref[columns, :])
            + dot_columns(pair_all[fsdp, :, :kv_width], w_key_ref[columns, :])
            + dot_columns(pair_all[fsdp, :, kv_width:], w_value_ref[columns, :])
        )

    pumping(width // step_out, upstream_tile)
    inputs = x_ref[...].astype(jnp.float32)
    scale = norm_scale(inputs)
    upstream = upstream_ref[...]
    scaled = upstream * gain_ref[...]
    tokens_ref[...] = (
        resid_grad_ref[...]
        + scale * scaled
        - inputs * scale**3 * jnp.mean(scaled * inputs, axis=-1, keepdims=True)
    )
    gain_attn = jnp.sum(upstream * inputs * scale, axis=0, keepdims=True)
    lanes = width // LANES
    gain_give[...] = jnp.zeros(gain_give.shape, jnp.float32)
    for block in range(lanes):
        columns = slice(block * LANES, (block + 1) * LANES)
        gain_give[block : block + 1, :] = gain_attn[:, columns]
        gain_give[lanes + block : lanes + block + 1, :] = gain_grad_ref[:, columns]

    def gain_copy(step):
        peer = lax.rem(fsdp + step, group)
        return pltpu.make_async_remote_copy(
            src_ref=gain_give,
            dst_ref=gain_got.at[step - 1],
            send_sem=gain_sends.at[step - 1],
            recv_sem=gain_arrivals.at[step - 1],
            device_id=(peer, ctx),
            device_id_type=MESH,
        )

    for step in range(1, group):
        gain_copy(step).start()
    pump_next()
    for copy in turned[group - 1 :]:
        copy.wait_recv()
    query_gather.sibling_here()
    for step in range(1, query_gather.chips):
        query_gather.crossed(step)
    split = query_split(width)
    filled_a = weight_grad(normed_all, query_all, 0, split, rest_a_work, 0, pumping)
    filled_b = weight_grad(normed_all, query_all, split, width, rest_b_work, 0, pumping)
    pair_gather.forward()
    pump_next()
    pair_gather.sibling_here()
    for step in range(1, pair_gather.chips):
        pair_gather.crossed(step)
    filled_b = weight_grad(normed_all, pair_all, 0, 2 * kv_width, rest_b_work, filled_b, pumping)
    gains = gain_give[...]
    for step in range(1, group):
        gain_copy(step).wait_recv()
        gains = gains + gain_got[step - 1]
    gain_tiles = gains.shape[0] // 16
    rest_a_work[filled_a : filled_a + gain_tiles] = gains.astype(jnp.bfloat16).reshape(
        gain_tiles, 16, LANES
    )
    clear_from(rest_a_work, filled_a + gain_tiles)
    clear_from(rest_b_work, filled_b)
    rest_a.start()
    rest_b.start()
    begun = pumped[0]
    half = len(first_rings) // 2
    total_pumps = max(gate_ring.ticks, late + out_a.ticks) * len(first_rings)

    def last_ticks(at, unused):
        for turn in range(half):
            pump(jnp.minimum(begun + half * at + turn, total_pumps))
        tick(rest_a, at)
        tick(rest_b, at)
        return unused

    rounds = max(rest_a.ticks, -(-(total_pumps - begun) // half))
    lax.fori_loop(0, rounds, last_ticks, 0)
    layer_sum.to_sibling().wait_recv()
    layer = layer_base_ref[...]
    arrived = [layer_sib]
    for step in range(1, layer_sum.chips):
        layer_sum.to_far(step).wait_recv()
        arrived.append(layer_far.at[step - 1])
    for source in arrived:
        copy = pltpu.make_async_copy(source, layer_stage, stage_sems.at[0])
        copy.start()
        copy.wait()
        layer = layer + layer_stage[...].astype(jnp.float32)
    layer_ref[...] = layer.astype(jnp.bfloat16)
    layer_sum.sent()
    for ring in first_rings + (rest_a, rest_b):
        ring.finish()
    for copy in turned:
        copy.wait_send()
    for gather in (branch_gather, query_gather, pair_gather):
        gather.sent()
    for step in range(1, group):
        gain_copy(step).wait_send()

    def sent(pair):
        @pl.when(jnp.logical_or(pair < steps.level, steps.side == 1))
        def _():
            across(pair).wait_send()

        @pl.when(pair < steps.level)
        def _():
            down_chain(pair).wait_send()

    tiles(steps.level + 1, sent)


def layer_back(
    q_wide, g_wide, all_pairs, mix, log_total, gate_part, up_part, down_a, down_b, layer_base,
    layer_parts, gain_grad, branch, low_t, normed_t, w_query, w_key, w_value, x, gain, resid_grad,
    cosine, sine,
):
    group, count = lax.axis_size("fsdp"), lax.axis_size("ctx")
    units, deep, wide = q_wide.shape
    keys = all_pairs.shape[2]
    rows, width = x.shape
    own, kv_width = width // group, w_key.shape[1]
    bf16, f32 = jnp.bfloat16, jnp.float32
    dma = pltpu.SemaphoreType.DMA
    wide_chunk = (group, gate_part.shape[1] // count, 16, LANES)
    gain_rows = spread(2 * (width // LANES), 16)
    split, row_blocks = query_split(width), own // 16
    out_first = out_split(width)
    chips = group // 2
    out_a_chunk, out_b_chunk, a_chunk, b_chunk = [
        (spread(held, count) // count, 16, LANES)
        for held in (
            out_first // LANES * row_blocks,
            (width - out_first) // LANES * row_blocks,
            split // LANES * row_blocks + gain_rows // 16,
            (width - split + 2 * kv_width) // LANES * row_blocks,
        )
    ]
    levels = count // 2
    return pl.pallas_call(
        back_kernel,
        out_shape=[
            jax.ShapeDtypeStruct((rows, width), f32),
            jax.ShapeDtypeStruct((rows, width), bf16),
            ring_total(wide_chunk, True),
            ring_total(wide_chunk, True),
            ring_total(down_a.shape),
            ring_total(down_b.shape),
            ring_total(out_a_chunk),
            ring_total(out_b_chunk),
            ring_total(a_chunk),
            ring_total(b_chunk),
            *[jax.ShapeDtypeStruct((levels, units, keys, deep), bf16)] * 2,
            jax.ShapeDtypeStruct((rows, width), bf16),
            *[jax.ShapeDtypeStruct((chips - 1, rows, width), bf16)] * 2,
        ],
        in_specs=[VMEM, VMEM, ANY, VMEM, VMEM, ANY, ANY, ANY, ANY, VMEM, ANY, VMEM, ANY, ANY, ANY]
        + [VMEM] * 8,
        out_specs=[VMEM] * 10 + [ANY] * 5,
        scratch_shapes=[
            pltpu.VMEM(all_pairs.shape, bf16),
            pltpu.VMEM((2, units, keys, deep), bf16),
            pltpu.VMEM((units, keys, deep), f32),
            pltpu.VMEM((units, 2 * wide, deep), bf16),
            pltpu.VMEM((units, 1, wide), f32),
            pltpu.VMEM((units, HD, wide), f32),
            *ring_scratch(wide_chunk, True),
            *ring_scratch(wide_chunk, True),
            *ring_scratch(out_a_chunk),
            *ring_scratch(out_b_chunk),
            *ring_scratch(a_chunk),
            *ring_scratch(b_chunk),
            pltpu.VMEM((own, group * rows), bf16),
            pltpu.VMEM((own, group * rows), bf16),
            pltpu.VMEM((group, rows, width), bf16),
            pltpu.VMEM((group, rows, width), bf16),
            pltpu.VMEM((group, rows, 2 * kv_width), bf16),
            pltpu.VMEM((rows, width), f32),
            pltpu.VMEM((gain_rows, LANES), f32),
            pltpu.VMEM((group - 1, gain_rows, LANES), f32),
            pltpu.VMEM((chips - 1, rows, width), bf16),
            pltpu.VMEM((rows, width), bf16),
            *ring_semaphores(True),
            *ring_semaphores(True),
            *[kind for _ in range(4) for kind in ring_semaphores()],
            *[dma((group - 1,))] * 2,
            *[kind for _ in range(2) for kind in ring_semaphores()],
            *[dma((levels,))] * 4,
            *[group_semaphores()] * 6,
            *[dma((group - 1,))] * 6,
            dma((6 + 2 * count,)),
            dma((2,)),
        ],
        compiler_params=pltpu.CompilerParams(
            collective_id=3, has_side_effects=True, vmem_limit_bytes=62 << 20
        ),
    )(
        q_wide, g_wide, all_pairs, mix, log_total, gate_part, up_part, down_a, down_b, layer_base,
        layer_parts, gain_grad, branch, low_t, normed_t, w_query, w_key, w_value, x, gain, resid_grad,
        cosine, sine,
    )


def unit_columns(rows, seq_count, block_len):
    groups = H // KVH
    split = rows.reshape(seq_count, block_len, KVH, groups, HD)
    return jnp.transpose(split, (0, 2, 4, 3, 1)).reshape(
        seq_count * KVH, HD, groups * block_len
    )


def finish_kernel(
    gate_ref, up_ref, down_a_ref, down_b_ref, out_a_ref, out_b_ref, rest_a_ref, rest_b_ref,
    query_grad, key_grad, value_grad, out_grad, gate_grad, up_grad, down_grad,
):
    rows = gate_grad.shape[0]
    row_blocks = rows // 16
    for source, target in ((gate_ref, gate_grad), (up_ref, up_grad)):
        held = source[...].reshape((-1,) + source.shape[3:])
        for block in range(target.shape[1] // LANES):
            target[:, block * LANES : (block + 1) * LANES] = (
                held[block * row_blocks : (block + 1) * row_blocks]
                .reshape(rows, LANES)
                .astype(jnp.float32)
            )

    @pl.when(pl.program_id(0) == 0)
    def _():
        def unpack(source, first, target, begin, end):
            for block in range(begin, end):
                here = first + (block - begin) * row_blocks
                target[:, block * LANES : (block + 1) * LANES] = (
                    source[here : here + row_blocks].reshape(rows, LANES).astype(jnp.float32)
                )
            return first + (end - begin) * row_blocks

        width, kv_width = query_grad.shape[1], key_grad.shape[1]
        split = query_split(width) // LANES
        middle = out_split(width) // LANES
        unpack(out_a_ref, 0, out_grad, 0, middle)
        unpack(out_b_ref, 0, out_grad, middle, width // LANES)
        unpack(rest_a_ref, 0, query_grad, 0, split)
        at = unpack(rest_b_ref, 0, query_grad, split, width // LANES)
        at = unpack(rest_b_ref, at, key_grad, 0, kv_width // LANES)
        unpack(rest_b_ref, at, value_grad, 0, kv_width // LANES)
        blocks = down_grad.shape[0] // 16
        first = min(down_a_ref.shape[0], blocks)
        for begin, end, source in ((0, first, down_a_ref), (first, blocks, down_b_ref)):
            if end > begin:
                down_grad[begin * 16 : end * 16, :] = (
                    source[: end - begin]
                    .reshape((end - begin) * 16, down_grad.shape[1])
                    .astype(jnp.float32)
                )


def finish(gate, up, down_a, down_b, out_a, out_b, rest_a, rest_b, own, width, kv_width, hidden):
    count, group, n = gate.shape[:3]

    def whole(array):
        return pl.BlockSpec(array.shape, lambda part, rank=len(array.shape): (0,) * rank)

    wide = pl.BlockSpec((count, 1, n, 16, LANES), lambda part: (0, part, 0, 0, 0))
    outs = [
        jax.ShapeDtypeStruct((own, columns), jnp.float32)
        for columns in (width, kv_width, kv_width, width, FF, FF)
    ] + [jax.ShapeDtypeStruct((hidden, width), jnp.float32)]
    slice_spec = pl.BlockSpec((own, FF // group), lambda part: (0, part))
    return pl.pallas_call(
        finish_kernel,
        grid=(group,),
        out_shape=outs,
        in_specs=[wide, wide] + [whole(a) for a in (down_a, down_b, out_a, out_b, rest_a, rest_b)],
        out_specs=[whole(a) for a in outs[:4]] + [slice_spec, slice_spec, whole(outs[6])],
        compiler_params=pltpu.CompilerParams(vmem_limit_bytes=60 << 20),
    )(gate, up, down_a, down_b, out_a, out_b, rest_a, rest_b)


def on_device(
    tokens, w_query, w_key, w_value, w_out, w_gate, w_up, w_down, gain_attn, gain_ffn, cotangent
):
    block_len, seq_count, width = tokens.shape
    rows_count = block_len * seq_count
    kv_width = KVH * HD
    full_query, full_key, full_value = [
        lax.all_gather(weight, "fsdp", axis=0, tiled=True) for weight in (w_query, w_key, w_value)
    ]
    full_gain_attn, full_gain_ffn = [
        lax.all_gather(gain, "fsdp", axis=0, tiled=True) for gain in (gain_attn, gain_ffn)
    ]
    my_down = w_down
    my_start = lax.axis_index("ctx") * block_len
    positions = my_start + jnp.arange(block_len, dtype=jnp.int32)
    x_rows = jnp.swapaxes(tokens, 0, 1).reshape(rows_count, width)
    g_rows = jnp.swapaxes(cotangent, 0, 1).reshape(rows_count, width)
    inputs = x_rows.astype(jnp.float32)
    scale_attn = norm_scale(inputs)
    normed_attn = (inputs * scale_attn * full_gain_attn.astype(jnp.float32)).astype(jnp.bfloat16)
    query_raw = forward_dot(normed_attn, full_query)
    key_raw = forward_dot(normed_attn, full_key)
    value_raw = forward_dot(normed_attn, full_value)
    units = seq_count * KVH
    wide = H // KVH * block_len
    queries = (
        rotary(query_raw.reshape(seq_count, block_len, H, HD), positions, 1.0)
        .astype(jnp.bfloat16)
        .reshape(rows_count, width)
    )
    keys_local = rotary(
        key_raw.reshape(seq_count, block_len, KVH, HD), positions, 1.0
    ).astype(jnp.bfloat16)
    values_local = value_raw.astype(jnp.bfloat16).reshape(seq_count, block_len, KVH, HD)
    pairs = jnp.swapaxes(
        jnp.concatenate([keys_local, values_local], axis=-1), 1, 2
    ).reshape(units, block_len, 2 * HD)
    q_unit = unit_columns(queries * jnp.bfloat16(HD ** (-0.5)), seq_count, block_len)
    q_wide = jnp.concatenate([q_unit, jnp.zeros_like(q_unit)], axis=1)
    (attn_low, low_t, mix_unit, log_total, all_pairs, full_out, my_gate, my_up, all_g) = attend(
        q_wide, pairs, w_out, w_gate, w_up, g_rows
    )
    (
        layer_base, layer_parts, grad_resid, grad_branch, g_wide, gate_part, up_part, down_a, down_b,
        gain_term_ffn,
    ) = (
        feed_forward(
            x_rows,
            attn_low,
            full_out,
            my_gate,
            my_up,
            w_down,
            all_g,
            full_gain_ffn.astype(jnp.float32)[None],
            units,
            wide,
        )
    )
    freqs = ROTARY_BASE ** (-2.0 * jnp.arange(HD // 2, dtype=jnp.float32) / HD)
    angles = freqs[:, None] * positions.astype(jnp.float32)[None, :]
    (
        grad_tokens, layer_out, gate_total, up_total, down_a, down_b, out_a, out_b, rest_a, rest_b,
        *_,
    ) = layer_back(
        q_wide,
        g_wide,
        all_pairs,
        mix_unit,
        log_total,
        gate_part,
        up_part,
        down_a,
        down_b,
        layer_base,
        layer_parts,
        gain_term_ffn,
        grad_branch,
        low_t,
        normed_attn.T,
        full_query,
        full_key,
        full_value,
        x_rows,
        full_gain_attn.astype(jnp.float32)[None],
        grad_resid,
        jnp.cos(angles),
        jnp.sin(angles),
    )
    own = gain_attn.shape[0]
    filled = query_split(width) // LANES * (own // 16)
    gains = rest_a[filled:].reshape(-1, LANES)[: 2 * (width // LANES)].reshape(2, width)
    gains = lax.dynamic_slice_in_dim(gains, lax.axis_index("fsdp") * own, own, 1)
    gains = gains.astype(jnp.float32)
    grads = finish(
        gate_total, up_total, down_a, down_b, out_a, out_b, rest_a, rest_b,
        own, width, kv_width, w_down.shape[0],
    )
    return (
        jnp.swapaxes(layer_out.reshape(seq_count, block_len, width), 0, 1),
        jnp.swapaxes(grad_tokens.reshape(seq_count, block_len, width), 0, 1),
        *grads,
        gains[0],
        gains[1],
    )


def solution(mesh):
    return jax.shard_map(
        on_device,
        mesh=mesh,
        in_specs=(
            P("ctx", "fsdp", None),
            P("fsdp", None),
            P("fsdp", None),
            P("fsdp", None),
            P("fsdp", None),
            P("fsdp", None),
            P("fsdp", None),
            P("fsdp", None),
            P("fsdp"),
            P("fsdp"),
            P("ctx", "fsdp", None),
        ),
        out_specs=(
            P("ctx", "fsdp", None),
            P("ctx", "fsdp", None),
            P("fsdp", None),
            P("fsdp", None),
            P("fsdp", None),
            P("fsdp", None),
            P("fsdp", None),
            P("fsdp", None),
            P("fsdp", None),
            P("fsdp"),
            P("fsdp"),
        ),
        check_vma=False,
    )
```

```python
import jax
import jax.numpy as jnp
from jax import lax
from jax.experimental import pallas as pl
from jax.experimental.pallas import tpu as pltpu
from jax.sharding import PartitionSpec as P

H = 18
KVH = 6
HD = 64
FF = 3072


EPSILON = 1e-05
ROTARY_BASE = 10000.0
MASKED_SCORE = -1e30


def norm_scale(rows):
    return lax.rsqrt(jnp.mean(rows * rows, axis=-1, keepdims=True) + EPSILON)


def forward_dot(left, right):
    return jnp.dot(left, right, preferred_element_type=jnp.float32)


MESH = pl.DeviceIdType.MESH
LANES = 128


def ring_place(ctx, fsdp, count):
    column, side = lax.div(ctx, 2), lax.rem(ctx, 2)
    place = column + side * (count - 1 - 2 * column)
    odd = lax.rem(fsdp, 2)
    return place + odd * (count - 1 - 2 * place)


def ring_ctx(place, fsdp, count):
    odd = lax.rem(fsdp, 2)
    place = place + odd * (count - 1 - 2 * place)
    late = lax.div(place, count // 2)
    return (1 - late) * 2 * place + late * (2 * (count - 1 - place) + 1)


class GroupGather:
    def __init__(self, shard_of, sends, arrivals):
        self.shard_of, self.sends, self.arrivals = shard_of, sends, arrivals
        self.fsdp, self.ctx = lax.axis_index("fsdp"), lax.axis_index("ctx")
        self.chips = lax.axis_size("fsdp") // 2
        self.chip, self.core = lax.div(self.fsdp, 2), lax.rem(self.fsdp, 2)
        self.sibling = 2 * self.chip + 1 - self.core

    def copy(self, source, shard, semaphore, device):
        return pltpu.make_async_remote_copy(
            src_ref=source,
            dst_ref=self.shard_of(shard),
            send_sem=self.sends.at[semaphore],
            recv_sem=self.arrivals.at[semaphore],
            device_id=(device, self.ctx),
            device_id_type=MESH,
        )

    def same_core(self, step):
        return 2 * lax.rem(self.chip + step, self.chips) + self.core

    def across(self, source):
        return self.copy(source, self.fsdp, 0, self.sibling)

    def out(self, source, step):
        return self.copy(source, self.fsdp, step, self.same_core(step))

    def onward(self, step):
        shard = self.same_core(self.chips - step)
        return self.copy(self.shard_of(shard), shard, self.chips - 1 + step, self.sibling)

    def start(self, source):
        for step in range(1, self.chips):
            self.out(source, step).start()
        self.across(source).start()

    def forward(self):
        own = self.shard_of(self.fsdp)
        for step in range(1, self.chips):
            self.out(own, step).wait_recv()
            self.onward(step).start()

    def sibling_here(self):
        self.across(self.shard_of(self.fsdp)).wait_recv()

    def crossed(self, step):
        self.onward(step).wait_recv()

    def sent(self):
        own = self.shard_of(self.fsdp)
        self.across(own).wait_send()
        for step in range(1, self.chips):
            self.out(own, step).wait_send()
            self.onward(step).wait_send()

    def finish(self):
        self.forward()
        self.sibling_here()
        for step in range(1, self.chips):
            self.crossed(step)
        self.sent()


class HalfGather:
    def __init__(self, held, own_rows, sends, arrivals):
        self.held, self.own = held, own_rows
        self.sends, self.arrivals = sends, arrivals
        self.fsdp, self.ctx = lax.axis_index("fsdp"), lax.axis_index("ctx")
        self.chips = lax.axis_size("fsdp") // 2
        self.chip, self.core = lax.div(self.fsdp, 2), lax.rem(self.fsdp, 2)
        self.sibling = 2 * self.chip + 1 - self.core
        self.side = lax.rem(self.ctx, 2)
        self.pair = self.ctx + 1 - 2 * self.side
        first = -(-own_rows // 32) * 16
        self.halves = ((0, first), (first, own_rows - first))

    def same_core(self, step):
        return 2 * lax.rem(self.chip + step, self.chips) + self.core

    def rows(self, shard, half=None):
        begin, size = (0, self.own) if half is None else self.halves[half]
        return self.held.at[pl.ds(shard * self.own + begin, size)]

    def copy(self, source, target, semaphore, device):
        return pltpu.make_async_remote_copy(
            src_ref=source,
            dst_ref=target,
            send_sem=self.sends.at[semaphore],
            recv_sem=self.arrivals.at[semaphore],
            device_id=device,
            device_id_type=MESH,
        )

    def on_side(self, body):
        for half in range(2):

            @pl.when(self.side == half)
            def _(half=half):
                body(half)

    def across(self, source):
        return self.copy(source, self.rows(self.fsdp), 0, (self.sibling, self.ctx))

    def out(self, source, step, half):
        begin, size = self.halves[half]
        return self.copy(
            source.at[pl.ds(begin, size)],
            self.rows(self.fsdp, half),
            step,
            (self.same_core(step), self.ctx),
        )

    def to_pair(self, step, half):
        part = self.rows(self.same_core(self.chips - step), half)
        return self.copy(part, part, self.chips - 1 + step, (self.fsdp, self.pair))

    def onward(self, step):
        part = self.rows(self.same_core(self.chips - step))
        return self.copy(part, part, 2 * self.chips - 2 + step, (self.sibling, self.ctx))

    def start(self, source):
        def send(half):
            for step in range(1, self.chips):
                self.out(source, step, half).start()

        self.on_side(send)
        self.across(source).start()

    def to_pairs(self):
        def forward(half):
            for step in range(1, self.chips):
                self.out(self.rows(self.fsdp), step, half).wait_recv()
                self.to_pair(step, half).start()

        self.on_side(forward)

    def to_sibling(self):
        def forward(half):
            for step in range(1, self.chips):
                self.to_pair(step, 1 - half).wait_recv()

        self.on_side(forward)
        for step in range(1, self.chips):
            self.onward(step).start()

    def arrived(self):
        self.across(self.rows(self.fsdp)).wait_recv()
        for step in range(1, self.chips):
            self.onward(step).wait_recv()

    def sent(self):
        def wait(half):
            for step in range(1, self.chips):
                self.out(self.rows(self.fsdp), step, half).wait_send()
                self.to_pair(step, half).wait_send()

        self.on_side(wait)
        self.across(self.rows(self.fsdp)).wait_send()
        for step in range(1, self.chips):
            self.onward(step).wait_send()


def half_semaphores(many):
    return pltpu.SemaphoreType.DMA((many, 3 * (lax.axis_size("fsdp") // 2) - 2))


def group_semaphores():
    return pltpu.SemaphoreType.DMA((lax.axis_size("fsdp") - 1,))


def greet_group(barrier):
    fsdp, ctx, group = lax.axis_index("fsdp"), lax.axis_index("ctx"), lax.axis_size("fsdp")
    for step in range(1, group):
        peer = lax.rem(fsdp + step, group)
        pl.semaphore_signal(barrier, inc=1, device_id=(peer, ctx), device_id_type=MESH)
    return group - 1


class Steps:
    def __init__(self):
        self.fsdp, self.ctx = lax.axis_index("fsdp"), lax.axis_index("ctx")
        self.levels = lax.axis_size("ctx") // 2
        self.level, self.side = lax.div(self.ctx, 2), lax.rem(self.ctx, 2)
        self.peer = (self.fsdp, 2 * self.level + 1 - self.side)
        self.above = (self.fsdp, lax.rem(self.ctx + 2, 2 * self.levels))
        self.below = (self.fsdp, lax.rem(self.ctx + 2 * self.levels - 2, 2 * self.levels))
        self.has_above = self.level + 1 < self.levels
        self.has_below = self.level > 0

    def greet(self, barrier):
        pl.semaphore_signal(barrier, inc=1, device_id=self.peer, device_id_type=MESH)

        @pl.when(self.has_above)
        def _():
            pl.semaphore_signal(barrier, inc=1, device_id=self.above, device_id_type=MESH)

        @pl.when(self.has_below)
        def _():
            pl.semaphore_signal(barrier, inc=1, device_id=self.below, device_id_type=MESH)

        return 1 + jnp.minimum(self.level, 1) + jnp.minimum(self.levels - 1 - self.level, 1)


PARTS = 2


def causal(keys, wide, shape):
    key_at = lax.broadcasted_iota(jnp.int32, shape, 0)
    query_at = lax.rem(lax.broadcasted_iota(jnp.int32, shape, 1), keys)
    return key_at <= query_at


def attend_kernel(
    x_ref, gain_ref, cos_ref, sin_ref, query_ref, key_ref, value_ref, out_ref, gate_ref, up_ref, g_ref,
    q_ref, normed_t_ref, gains_ref, full_query, full_key, full_value,
    low_ref, low_t_ref, mix_ref, log_ref, all_ref, full_out_ref, my_gate_ref, my_up_ref, all_g_ref,
    normed_ref, key_rows, gain_all,
    top_ref, total_ref, chain_sends, chain_arrivals, peer_sends, peer_arrivals,
    half_sends, half_arrivals, gain_sends, gain_arrivals,
    out_sends, out_arrivals, g_sends, g_arrivals, part_sends, part_arrivals, local_sems,
):
    steps = Steps()
    fsdp, ctx, group = steps.fsdp, steps.ctx, lax.axis_size("fsdp")
    units, deep, wide = q_ref.shape
    keys = all_ref.shape[2]
    per_part = units // PARTS
    rows_count, width = x_ref.shape
    own = query_ref.shape[0]
    sequences, groups = units // KVH, H // KVH
    barrier = pltpu.get_barrier_semaphore()
    greeted = steps.greet(barrier) + greet_group(barrier)
    span = KVH * HD
    pieces = [(key_ref, full_key, 0), (value_ref, full_value, 0)]
    pieces += [(query_ref, full_query, start) for start in range(0, width, span)]
    gathers = []
    for at, (source, target, start) in enumerate(pieces):
        columns = pl.ds(start, span)
        gather = HalfGather(
            target.at[:, columns], own, half_sends.at[at], half_arrivals.at[at]
        )
        gathers.append((gather, source.at[:, columns]))
    own_rows = pl.ds(fsdp * own, own)
    own_copies = [
        pltpu.make_async_copy(source, target.at[own_rows], local_sems.at[4 + at])
        for at, (source, target) in enumerate(
            ((key_ref, full_key), (value_ref, full_value), (query_ref, full_query))
        )
    ]
    for copy in own_copies:
        copy.start()
    gain_all[fsdp] = gain_ref[...]
    pl.semaphore_wait(barrier, greeted)

    def gain_copy(step):
        peer = lax.rem(fsdp + step, group)
        return pltpu.make_async_remote_copy(
            src_ref=gain_ref,
            dst_ref=gain_all.at[fsdp],
            send_sem=gain_sends.at[step - 1],
            recv_sem=gain_arrivals.at[step - 1],
            device_id=(peer, ctx),
            device_id_type=MESH,
        )

    for step in range(1, group):
        gain_copy(step).start()
    for gather, source in gathers:
        gather.start(source)
    inputs = x_ref[...].astype(jnp.float32)
    scale = norm_scale(inputs)
    q_ref[:, HD:, :] = jnp.zeros((units, HD, wide), q_ref.dtype)
    for step in range(1, group):
        gain_copy(step).wait_recv()
    gains = jnp.concatenate([gain_all[shard][:, :own] for shard in range(group)], axis=1)
    gains_ref[...] = gains
    normed_ref[...] = (inputs * scale * gains[:1]).astype(jnp.bfloat16)
    cosine, sine = cos_ref[...], sin_ref[...]

    def turn(columns):
        first, second = columns[: HD // 2], columns[HD // 2 :]
        return jnp.concatenate(
            [first * cosine - second * sine, second * cosine + first * sine], axis=0
        ).astype(jnp.bfloat16)

    def block_copy(level, part, side, semaphores, arrivals, arrives, device):
        block = 2 * (steps.level - level) + side
        held = all_ref.at[block, pl.ds(part * per_part, per_part)]
        return pltpu.make_async_remote_copy(
            src_ref=held,
            dst_ref=held,
            send_sem=semaphores.at[level, part],
            recv_sem=arrivals.at[arrives, part],
            device_id=device,
            device_id_type=MESH,
        )

    def chain(level, part):
        return block_copy(
            level, part, steps.side, chain_sends, chain_arrivals, level + 1, steps.above
        )

    def across(level, part):
        return block_copy(
            level, part, steps.side, peer_sends, peer_arrivals, level, steps.peer
        )

    def pass_on(level, part):
        @pl.when(steps.has_above)
        def _():
            chain(level, part).start()

    def project(at):
        _, weight, start = pieces[at]
        made = forward_dot(normed_ref[...], weight[:, start : start + span])
        if at == 0:
            key_rows[...] = made
            return
        for sequence in range(sequences):
            block = slice(sequence * keys, (sequence + 1) * keys)
            for pair in range(span // (2 * HD)):
                columns = slice(pair * 2 * HD, (pair + 1) * 2 * HD)
                turned = made[block, columns].T
                if at == 1:
                    turned_keys = key_rows[block, columns].T
                    for half in range(2):
                        held = slice(half * HD, (half + 1) * HD)
                        both = jnp.concatenate(
                            [turn(turned_keys[held]), turned[held].astype(jnp.bfloat16)], axis=0
                        )
                        all_ref[ctx, sequence * KVH + 2 * pair + half] = both.T
                else:
                    for half in range(2):
                        head = start // HD + 2 * pair + half
                        unit, member = sequence * KVH + head // groups, head % groups
                        part = turn(turned[half * HD : (half + 1) * HD])
                        q_ref[unit, :HD, member * keys : (member + 1) * keys] = part * jnp.bfloat16(
                            HD ** (-0.5)
                        )
        if at == 1:
            for part in range(PARTS):
                pass_on(0, part)

                @pl.when(steps.side == 0)
                def _():
                    across(0, part).start()

    last = len(pieces)
    for at in range(last + 2):
        if at < last:
            gathers[at][0].to_pairs()
        if 1 <= at <= last:
            gathers[at - 1][0].to_sibling()
        if at == 1:
            for column in range(width // LANES):
                columns = slice(column * LANES, (column + 1) * LANES)
                normed_t_ref[columns, :] = normed_ref[:, columns].T
            for copy in own_copies:
                copy.wait()
        if at >= 2:
            gathers[at - 2][0].arrived()
            project(at - 2)

    columns = my_gate_ref.shape[1]
    gathered = GroupGather(
        lambda shard: full_out_ref.at[pl.ds(shard * own, own)], out_sends, out_arrivals
    )
    gathered.start(out_ref)
    gathered_g = GroupGather(lambda shard: all_g_ref.at[shard], g_sends, g_arrivals)
    gathered_g.start(g_ref)
    own_g = pltpu.make_async_copy(g_ref, all_g_ref.at[fsdp], local_sems.at[3])
    own_g.start()
    background = [own_g]
    own_out = pltpu.make_async_copy(out_ref, full_out_ref.at[own_rows], local_sems.at[2])
    own_out.start()
    background.append(own_out)
    for which, (source, target) in enumerate(((gate_ref, my_gate_ref), (up_ref, my_up_ref))):
        for step in range(1, group):
            peer = lax.rem(fsdp + step, group)
            copy = pltpu.make_async_remote_copy(
                src_ref=source.at[:, pl.ds(pl.multiple_of(peer * columns, LANES), columns)],
                dst_ref=target.at[own_rows],
                send_sem=part_sends.at[which, step - 1],
                recv_sem=part_arrivals.at[which, step - 1],
                device_id=(peer, ctx),
                device_id_type=MESH,
            )
            copy.start()
            background.append(copy)
        own_part = pltpu.make_async_copy(
            source.at[:, pl.ds(pl.multiple_of(fsdp * columns, LANES), columns)],
            target.at[own_rows],
            local_sems.at[which],
        )
        own_part.start()
        background.append(own_part)

    def add(unit, kv):
        scores = jnp.dot(kv, q_ref[unit], preferred_element_type=jnp.float32)
        top = top_ref[unit]
        new_top = jnp.maximum(top, jnp.max(scores, axis=0, keepdims=True))
        fade = jnp.exp(top - new_top)
        weights = jnp.exp(scores - new_top)
        top_ref[unit] = new_top
        total_ref[unit] = total_ref[unit] * fade + jnp.sum(weights, axis=0, keepdims=True)
        added = jnp.dot(kv.T, weights.astype(jnp.bfloat16), preferred_element_type=jnp.float32)
        mix_ref[unit] = mix_ref[unit] * fade + added[HD:]

    def over_units(body, first, count):
        def two(at, unused):
            body(first + 2 * at)
            body(first + 2 * at + 1)
            return unused

        lax.fori_loop(0, count // 2, two, 0)

    def diagonal(unit):
        kv = all_ref[ctx, unit]
        scores = jnp.dot(kv, q_ref[unit], preferred_element_type=jnp.float32)
        scores = jnp.where(causal(keys, wide, scores.shape), scores, MASKED_SCORE)
        top = jnp.max(scores, axis=0, keepdims=True)
        weights = jnp.exp(scores - top)
        top_ref[unit] = top
        total_ref[unit] = jnp.sum(weights, axis=0, keepdims=True)
        added = jnp.dot(kv.T, weights.astype(jnp.bfloat16), preferred_element_type=jnp.float32)
        mix_ref[unit] = added[HD:]

    over_units(diagonal, 0, units)

    @pl.when(steps.side == 1)
    def _():
        for part in range(PARTS):
            across(0, part).wait_recv()
            over_units(lambda unit: add(unit, all_ref[ctx - 1, unit]), part * per_part, per_part)

    def level_step(level, unused):
        for part in range(PARTS):
            chain(level - 1, part).wait_recv()
            pass_on(level, part)
            across(level, part).start()
        first = 2 * (steps.level - level)
        for part in range(PARTS):
            across(level, part).wait_recv()
            over_units(
                lambda unit: add(unit, all_ref[pl.ds(first, 2), unit].reshape(2 * keys, deep)),
                part * per_part,
                per_part,
            )
        return unused

    lax.fori_loop(1, steps.level + 1, level_step, 0)

    def close(unit):
        total = total_ref[unit]
        mix_ref[unit] = mix_ref[unit] / total
        log_ref[unit] = top_ref[unit] + jnp.log(total)

    over_units(close, 0, units)
    for sequence in range(sequences):
        for pair in range(H // 2):
            heads = []
            for head in (2 * pair, 2 * pair + 1):
                unit, member = sequence * KVH + head // groups, head % groups
                heads.append(mix_ref[unit, :, member * keys : (member + 1) * keys])
            tile = jnp.concatenate(heads, axis=0).astype(low_ref.dtype)
            block = slice(sequence * keys, (sequence + 1) * keys)
            columns = slice(pair * 2 * HD, (pair + 1) * 2 * HD)
            low_t_ref[columns, block] = tile
            low_ref[block, columns] = tile.T
    for gather, _ in gathers:
        gather.sent()
    for step in range(1, group):
        gain_copy(step).wait_send()
    gathered.finish()
    gathered_g.finish()
    for copy in background:
        copy.wait()

    def sent(level, unused):
        for part in range(PARTS):

            @pl.when(steps.has_above)
            def _():
                chain(level, part).wait_send()

            @pl.when(jnp.logical_or(level > 0, steps.side == 0))
            def _():
                across(level, part).wait_send()

        return unused

    lax.fori_loop(0, steps.level + 1, sent, 0)


ANY = pl.BlockSpec(memory_space=pl.ANY)
VMEM = pl.BlockSpec(memory_space=pltpu.VMEM)


def attend(x, gains, cosine, sine, w_query, w_key, w_value, w_out, w_gate, w_up, g_rows, sequences):
    group, count = lax.axis_size("fsdp"), lax.axis_size("ctx")
    rows, width = x.shape
    own, hidden = w_query.shape[0], w_gate.shape[1] // group
    keys, units, deep = rows // sequences, sequences * KVH, 2 * HD
    wide = H // KVH * keys
    kv_width = KVH * HD
    dma = pltpu.SemaphoreType.DMA
    bf16, f32 = jnp.bfloat16, jnp.float32
    pieces = 2 + width // kv_width
    return pl.pallas_call(
        attend_kernel,
        out_shape=[
            jax.ShapeDtypeStruct((units, deep, wide), bf16),
            jax.ShapeDtypeStruct((width, rows), bf16),
            jax.ShapeDtypeStruct((gains.shape[0], width), f32),
            jax.ShapeDtypeStruct((width, width), bf16),
            jax.ShapeDtypeStruct((width, kv_width), bf16),
            jax.ShapeDtypeStruct((width, kv_width), bf16),
            jax.ShapeDtypeStruct((rows, width), bf16),
            jax.ShapeDtypeStruct((width, rows), bf16),
            jax.ShapeDtypeStruct((units, HD, wide), f32),
            jax.ShapeDtypeStruct((units, 1, wide), f32),
            jax.ShapeDtypeStruct((count, units, keys, deep), bf16),
            jax.ShapeDtypeStruct((width, width), bf16),
            jax.ShapeDtypeStruct((width, hidden), bf16),
            jax.ShapeDtypeStruct((width, hidden), bf16),
            jax.ShapeDtypeStruct((group, rows, width), bf16),
        ],
        in_specs=[VMEM] * 4 + [ANY] * 7,
        out_specs=[VMEM] * 11 + [ANY] * 4,
        scratch_shapes=[
            pltpu.VMEM((rows, width), bf16),
            pltpu.VMEM((rows, kv_width), f32),
            pltpu.VMEM((group,) + gains.shape, f32),
            pltpu.VMEM((units, 1, wide), f32),
            pltpu.VMEM((units, 1, wide), f32),
            dma((count // 2, PARTS)),
            dma((count // 2 + 1, PARTS)),
            dma((count // 2, PARTS)),
            dma((count // 2, PARTS)),
            half_semaphores(pieces),
            half_semaphores(pieces),
            *[dma((group - 1,))] * 2,
            *[group_semaphores()] * 4,
            dma((2, group - 1)),
            dma((2, group - 1)),
            dma((7,)),
        ],
        compiler_params=pltpu.CompilerParams(
            collective_id=1, has_side_effects=True, vmem_limit_bytes=60 << 20
        ),
    )(x, gains, cosine, sine, w_query, w_key, w_value, w_out, w_gate, w_up, g_rows)


class Ring:
    def __init__(self, work, landing, total, semaphores, forward, exchange=False):
        self.fsdp, self.ctx = lax.axis_index("fsdp"), lax.axis_index("ctx")
        self.group, self.count = lax.axis_size("fsdp"), lax.axis_size("ctx")
        self.work, self.landing, self.total = work, landing, total
        self.sends, self.arrivals = semaphores[:2]
        self.part_sends, self.part_arrivals, self.own_sem = semaphores[2:] if exchange else (None,) * 3
        self.exchange = exchange
        side = 0 if forward else 1
        self.place = ring_place(self.ctx, side, self.count)
        self.after = (self.fsdp, ring_ctx(lax.rem(self.place + 1, self.count), side, self.count))
        self.ticks = 2 * self.count - 2 + int(exchange)

    def chunk(self, held, index):
        if self.exchange:
            return held.at[index]
        per = held.shape[0] // self.count
        return held.at[pl.ds(index * per, per)]

    def summing(self, step, index):
        return self.copy(self.chunk(self.work, index), self.landing.at[step], step)

    def handing(self, step, index):
        held = self.chunk(self.total, index)
        return self.copy(held, held, step)

    def copy(self, source, target, step):
        return pltpu.make_async_remote_copy(
            src_ref=source,
            dst_ref=target,
            send_sem=self.sends.at[step],
            recv_sem=self.arrivals.at[step],
            device_id=self.after,
            device_id_type=MESH,
        )

    def part(self, index, step):
        peer = lax.rem(self.fsdp + step, self.group)
        return pltpu.make_async_remote_copy(
            src_ref=self.work.at[index, peer],
            dst_ref=self.total.at[index, self.fsdp],
            send_sem=self.part_sends.at[step - 1],
            recv_sem=self.part_arrivals.at[step - 1],
            device_id=(peer, self.ctx),
            device_id_type=MESH,
        )

    def own_part(self, index):
        return pltpu.make_async_copy(
            self.work.at[index, self.fsdp], self.total.at[index, self.fsdp], self.own_sem
        )

    def start(self):
        self.summing(0, self.place).start()

    def tick(self, at):
        last = self.count - 2
        gap = int(self.exchange)
        step = at - gap * jnp.where(at > last, 1, 0) if self.exchange else at
        index = lax.rem(self.place + 3 * self.count - 1 - step, self.count)

        def add(target):
            part, landed = self.chunk(self.work, index), self.landing.at[jnp.minimum(at, last)]
            for row in range(part.shape[0]):
                target[row] = (
                    part[row].astype(jnp.float32) + landed[row].astype(jnp.float32)
                ).astype(part.dtype)

        @pl.when(at <= last)
        def _():
            self.summing(jnp.minimum(at, last), index).wait_recv()

        @pl.when(at < last)
        def _():
            add(self.chunk(self.work, index))
            self.summing(jnp.minimum(at + 1, last), index).start()

        if self.exchange:

            @pl.when(at == last)
            def _():
                add(self.chunk(self.work, index))
                for peer in range(1, self.group):
                    self.part(index, peer).start()
                self.own_part(index).start()

            @pl.when(at == last + 1)
            def _():
                done = lax.rem(self.place + 1, self.count)
                self.own_part(done).wait()
                for peer in range(1, self.group):
                    self.part(done, peer).wait_recv()
                self.handing(last + 1, done).start()

        else:

            @pl.when(at == last)
            def _():
                add(self.chunk(self.total, index))
                self.handing(last + 1, index).start()

        @pl.when(at > last + gap)
        def _():
            here = jnp.maximum(step, last + 1)
            self.handing(here, index).wait_recv()

            @pl.when(here < 2 * self.count - 3)
            def _():
                self.handing(jnp.minimum(here + 1, 2 * self.count - 3), index).start()

    def finish(self):
        def wait(step, unused):
            self.handing(step, self.place).wait_send()
            return unused

        lax.fori_loop(0, 2 * self.count - 2, wait, 0)
        if self.exchange:
            for peer in range(1, self.group):
                self.part(lax.rem(self.place + 1, self.count), peer).wait_send()


class SumRing(Ring):
    def __init__(self, *args):
        super().__init__(*args)
        self.ticks = self.count - 1

    def tick(self, at):
        last = self.count - 2
        index = lax.rem(self.place + 2 * self.count - 1 - at, self.count)
        self.summing(at, index).wait_recv()
        work, landed = self.chunk(self.work, index), self.landing.at[at]

        def add(target):
            for row in range(work.shape[0]):
                target[row] = (
                    work[row].astype(jnp.float32) + landed[row].astype(jnp.float32)
                ).astype(work.dtype)

        @pl.when(at < last)
        def _():
            add(work)
            self.summing(jnp.minimum(at + 1, last), index).start()

        @pl.when(at == last)
        def _():
            add(self.total)

    def finish(self):
        def wait(step, unused):
            self.summing(step, self.place).wait_send()
            return unused

        lax.fori_loop(0, self.ticks, wait, 0)


class SpreadRing(Ring):
    def __init__(self, total, semaphores, forward):
        super().__init__(None, None, total, semaphores, forward)
        self.ticks = self.count - 1
        self.first = lax.rem(self.place + 1, self.count)

    def start(self):
        self.handing(0, self.first).start()

    def tick(self, at):
        index = lax.rem(self.place + self.count - at, self.count)
        self.handing(at, index).wait_recv()

        @pl.when(at < self.count - 2)
        def _():
            self.handing(jnp.minimum(at + 1, self.count - 2), index).start()

    def finish(self):
        def wait(step, unused):
            self.handing(step, self.place).wait_send()
            return unused

        lax.fori_loop(0, self.ticks, wait, 0)


def ring_scratch(chunk, exchange=False):
    count = lax.axis_size("ctx")
    work = (count,) + chunk if exchange else (count * chunk[0],) + chunk[1:]
    return [pltpu.VMEM(work, jnp.bfloat16), pltpu.VMEM((count - 1,) + chunk, jnp.bfloat16)]


def ring_total(chunk, exchange=False):
    count = lax.axis_size("ctx")
    work = (count,) + chunk if exchange else (count * chunk[0],) + chunk[1:]
    return jax.ShapeDtypeStruct(work, jnp.bfloat16)


def ring_semaphores(exchange=False):
    dma, steps = pltpu.SemaphoreType.DMA, 2 * lax.axis_size("ctx") - 2
    parts = lax.axis_size("fsdp") - 1
    return [dma((steps,))] * 2 + ([dma((parts,))] * 2 + [dma] if exchange else [])


def query_split(width):
    return width // LANES * 7 // 9 * LANES


def out_split(width):
    return (width // LANES + 1) // 2 * LANES


def down_split(blocks, count):
    each = -(-blocks // count)
    first = max(1, each // 2)
    return first, max(1, each - first)


class GroupScatter:
    def __init__(self, give_sib, got_sib, give_cross, got_cross, far, got_far, sends, arrivals):
        self.give_sib, self.got_sib = give_sib, got_sib
        self.give_cross, self.got_cross = give_cross, got_cross
        self.far, self.got_far = far, got_far
        self.sends, self.arrivals = sends, arrivals
        self.fsdp, self.ctx = lax.axis_index("fsdp"), lax.axis_index("ctx")
        self.chips = lax.axis_size("fsdp") // 2
        self.chip, self.core = lax.div(self.fsdp, 2), lax.rem(self.fsdp, 2)
        self.sibling = 2 * self.chip + 1 - self.core

    def copy(self, source, target, semaphore, device):
        return pltpu.make_async_remote_copy(
            src_ref=source,
            dst_ref=target,
            send_sem=self.sends.at[semaphore],
            recv_sem=self.arrivals.at[semaphore],
            device_id=(device, self.ctx),
            device_id_type=MESH,
        )

    def to_sibling(self):
        return self.copy(self.give_sib, self.got_sib, 0, self.sibling)

    def to_cross(self, step):
        return self.copy(
            self.give_cross(step), self.got_cross.at[step - 1], step, self.sibling
        )

    def to_far(self, step):
        chip = lax.rem(self.chip + self.chips - step, self.chips)
        return self.copy(
            self.far.at[step - 1],
            self.got_far.at[step - 1],
            self.chips - 1 + step,
            2 * chip + self.core,
        )

    def add_cross(self, step):
        self.to_cross(step).wait_recv()
        held = self.far.at[step - 1]
        held[...] = (
            held[...].astype(jnp.float32) + self.got_cross[step - 1].astype(jnp.float32)
        ).astype(held.dtype)
        self.to_far(step).start()

    def total(self, own):
        self.to_sibling().wait_recv()
        value = own + self.got_sib[...].astype(jnp.float32)
        for step in range(1, self.chips):
            self.to_far(step).wait_recv()
            value = value + self.got_far[step - 1].astype(jnp.float32)
        return value

    def sent(self):
        self.to_sibling().wait_send()
        for step in range(1, self.chips):
            self.to_cross(step).wait_send()
            self.to_far(step).wait_send()


def scatter_scratch(rows, width):
    far = lax.axis_size("fsdp") // 2 - 1
    one, many = (rows, width), (far, rows, width)
    return [pltpu.VMEM(shape, jnp.bfloat16) for shape in (one, one, many, many, many, many)]


def dot_columns(left, right):
    return lax.dot_general(
        left, right, (((1,), (1,)), ((), ())), preferred_element_type=jnp.float32
    )


def tiles(count, body):
    def step(at, unused):
        body(at)
        return unused

    lax.fori_loop(0, count, step, 0)


def lane_tile(at, size):
    return pl.ds(pl.multiple_of(at * size, LANES), size)


def width_tile(width):
    return 384 if width % 384 == 0 else width


def hidden_tile(hidden):
    return 256 if hidden % 256 == 0 else 128


def transpose_into(target, source):
    rows, columns = source.shape

    def body(at):
        part = source[:, lane_tile(at, LANES)]
        target[pl.ds(pl.multiple_of(at * LANES, LANES), LANES), :] = part.T

    tiles(columns // LANES, body)


def ffn_kernel(
    x_ref, low_ref, out_ref, gate_ref, up_ref, down_ref, all_g_ref, gain_ref,
    layer_ref, layer_part_ref, resid_grad_ref, branch_ref, g_wide_ref, gate_part_ref, up_part_ref,
    down_a_done, down_b_done, gain_grad_ref,
    all_n_ref, turned_n, turned_act, act_ref, gate_grad, up_grad, resid_ref, grad_own,
    down_a_work, down_a_land, down_b_work, down_b_land, *rest,
):
    give_sib, got_sib, give_cross, got_cross, far, got_far = rest[:6]
    n_sends, n_arrivals, grad_sends, grad_arrivals = rest[6:10]
    down_a = SumRing(down_a_work, down_a_land, down_a_done, rest[10:12], True)
    down_b = SumRing(down_b_work, down_b_land, down_b_done, rest[12:14], False)
    rings = (down_a, down_b)
    group = lax.axis_size("fsdp")
    rows, width = x_ref.shape
    hidden = gate_ref.shape[1]
    barrier = pltpu.get_barrier_semaphore()
    greeted = greet_group(barrier) + len(rings)
    for ring in rings:
        pl.semaphore_signal(barrier, inc=1, device_id=ring.after, device_id_type=MESH)
    step_in, step_out = hidden_tile(hidden), width_tile(width)

    def branch(at):
        columns = lane_tile(at, step_out)
        resid_ref[:, columns] = x_ref[:, columns].astype(jnp.float32) + forward_dot(
            low_ref[...], out_ref[:, columns]
        )

    tiles(width // step_out, branch)
    gain = gain_ref[...]
    scale = norm_scale(resid_ref[...])
    gathered = GroupGather(lambda shard: all_n_ref.at[shard], n_sends, n_arrivals)
    fsdp, chips = gathered.fsdp, gathered.chips
    all_n_ref[fsdp] = (resid_ref[...] * scale * gain).astype(jnp.bfloat16)
    pl.semaphore_wait(barrier, greeted)
    gathered.start(all_n_ref.at[fsdp])
    grad_sum = GroupScatter(
        give_sib,
        got_sib,
        lambda step: give_cross.at[step - 1],
        got_cross,
        far,
        got_far,
        grad_sends,
        grad_arrivals,
    )

    def hidden_part(shard):
        def body(at):
            columns = lane_tile(at, step_in)
            normed = all_n_ref[shard]
            gate = forward_dot(normed, gate_ref[:, columns])
            upward = forward_dot(normed, up_ref[:, columns])
            grad_act = dot_columns(
                all_g_ref[shard], down_ref[pl.ds(pl.multiple_of(at * step_in, LANES), step_in), :]
            )
            sigmoid = jax.nn.sigmoid(gate)
            silu = gate * sigmoid
            act_ref[shard, :, columns] = (silu * upward).astype(jnp.bfloat16)
            gate_grad[shard, :, columns] = (
                grad_act * upward * (sigmoid * (1.0 + gate * (1.0 - sigmoid)))
            ).astype(jnp.bfloat16)
            up_grad[shard, :, columns] = (grad_act * silu).astype(jnp.bfloat16)

        tiles(hidden // step_in, body)

    def grad_part(shard, target):
        def body(at):
            columns = pl.ds(pl.multiple_of(at * step_out, LANES), step_out)
            target[:, columns] = (
                dot_columns(gate_grad[shard], gate_ref[columns, :])
                + dot_columns(up_grad[shard], up_ref[columns, :])
            ).astype(target.dtype)

        tiles(width // step_out, body)

    hidden_part(fsdp)
    gathered.sibling_here()
    sibling = gathered.sibling
    hidden_part(sibling)
    grad_part(sibling, grad_sum.give_sib)
    grad_sum.to_sibling().start()
    gathered.forward()
    grad_part(fsdp, grad_own)
    for step in range(1, chips):
        ours = gathered.same_core(chips - step)
        theirs = ours + sibling - fsdp
        gathered.crossed(step)
        hidden_part(theirs)
        grad_part(theirs, give_cross.at[step - 1])
        grad_sum.to_cross(step).start()
        hidden_part(ours)
        grad_part(ours, far.at[step - 1])
        grad_sum.add_cross(step)
    for shard in range(group):
        span = slice(shard * rows, (shard + 1) * rows)
        transpose_into(turned_act.at[:, span], act_ref.at[shard])
    blocks = hidden // 16
    first = min(blocks, down_a_work.shape[0])

    def down_tile(at):
        columns = lane_tile(at, step_out)
        part = forward_dot(
            turned_act[...], all_g_ref[:, :, columns].reshape(group * rows, step_out)
        ).astype(jnp.bfloat16)
        for begin, end, work in ((0, first, down_a_work), (first, blocks, down_b_work)):
            if end > begin:
                work[: end - begin, :, columns] = part[begin * 16 : end * 16].reshape(
                    end - begin, 16, step_out
                )

    tiles(width // step_out, down_tile)
    for work, filled in ((down_a_work, first), (down_b_work, blocks - first)):
        for spare in range(filled, work.shape[0]):
            work[spare] = jnp.zeros(work.shape[1:], work.dtype)
    for ring in rings:
        ring.start()
    ticked = [0]

    def ring_tick(at):
        for ring in rings:

            @pl.when(at < ring.ticks)
            def _():
                ring.tick(jnp.minimum(at, ring.ticks - 1))

    def ticking(times, body):
        begin = ticked[0]

        def step(at):
            body(at)
            ring_tick(begin + at)

        tiles(times, step)
        ticked[0] += times

    for shard in range(group):
        span = slice(shard * rows, (shard + 1) * rows)
        transpose_into(turned_n.at[:, span], all_n_ref.at[shard])
    own = width // group
    row_blocks = own // 16
    for source, target in ((gate_grad, gate_part_ref), (up_grad, up_part_ref)):

        def weight_tile(at):
            columns = lane_tile(at, step_in)
            part = forward_dot(
                turned_n[...], source[:, :, columns].reshape(group * rows, step_in)
            ).astype(jnp.bfloat16)
            for block in range(step_in // LANES):
                first = (at * (step_in // LANES) + block) * row_blocks
                for owner in range(group):
                    target[owner, pl.ds(first, row_blocks)] = part[
                        owner * own : (owner + 1) * own, block * LANES : (block + 1) * LANES
                    ].reshape(row_blocks, 16, LANES)

        ticking(hidden // step_in, weight_tile)
        filled = hidden // LANES * row_blocks
        for spare in range(filled, target.shape[1]):
            for owner in range(group):
                target[owner, spare] = jnp.zeros(target.shape[2:], target.dtype)

    def layer_tile(at):
        columns = lane_tile(at, step_out)
        part = forward_dot(
            act_ref[...].reshape(group * rows, hidden), down_ref[:, columns]
        ).reshape(group, rows, step_out)
        layer_part_ref[:, :, columns] = part.astype(jnp.bfloat16)

    ticking(width // step_out, layer_tile)
    layer_ref[...] = resid_ref[...] + layer_part_ref[fsdp].astype(jnp.float32)
    upstream = grad_sum.total(grad_own[...])
    resid = resid_ref[...]
    scaled = upstream * gain
    grad_resid = (
        all_g_ref[fsdp].astype(jnp.float32)
        + scale * scaled
        - resid * scale**3 * jnp.mean(scaled * resid, axis=-1, keepdims=True)
    )
    gain_grad_ref[...] = jnp.sum(upstream * resid * scale, axis=0, keepdims=True)
    resid_grad_ref[...] = grad_resid
    branch_ref[...] = grad_resid.astype(jnp.bfloat16)
    units, _, wide = g_wide_ref.shape
    sequences = units // KVH
    keys = rows // sequences
    groups = wide // keys
    g_wide_ref[:, :HD, :] = jnp.zeros((units, HD, wide), g_wide_ref.dtype)
    for pair in range(H // 2):
        columns = slice(pair * 2 * HD, (pair + 1) * 2 * HD)
        mixed = dot_columns(branch_ref[...], out_ref[columns, :]).astype(jnp.bfloat16)
        for sequence in range(sequences):
            turned = mixed[sequence * keys : (sequence + 1) * keys].T
            for half in range(2):
                head = 2 * pair + half
                unit, member = sequence * KVH + head // groups, head % groups
                g_wide_ref[unit, HD:, member * keys : (member + 1) * keys] = turned[
                    half * HD : (half + 1) * HD
                ]
    begin = ticked[0]
    tiles(max(0, down_a.ticks - begin), lambda at: ring_tick(begin + at))
    gathered.sent()
    grad_sum.sent()
    for ring in rings:
        ring.finish()


def spread(blocks, count):
    return -(-blocks // count) * count


def feed_forward(x, low, full_out, my_gate, my_up, my_down, all_g, gain, units, wide):
    group, count = lax.axis_size("fsdp"), lax.axis_size("ctx")
    rows, width = x.shape
    hidden = my_gate.shape[1]
    blocks = spread(hidden // LANES * (width // group // 16), count)
    chips = group // 2
    dma = pltpu.SemaphoreType.DMA((2 * chips - 1,))
    bf16 = jnp.bfloat16
    down_chunks = [(per, 16, width) for per in down_split(hidden // 16, count)]
    return pl.pallas_call(
        ffn_kernel,
        out_shape=[
            jax.ShapeDtypeStruct((rows, width), jnp.float32),
            jax.ShapeDtypeStruct((group, rows, width), bf16),
            jax.ShapeDtypeStruct((rows, width), jnp.float32),
            jax.ShapeDtypeStruct((rows, width), bf16),
            jax.ShapeDtypeStruct((units, 2 * HD, wide), bf16),
            jax.ShapeDtypeStruct((group, blocks, 16, LANES), bf16),
            jax.ShapeDtypeStruct((group, blocks, 16, LANES), bf16),
            *[jax.ShapeDtypeStruct(chunk, bf16) for chunk in down_chunks],
            jax.ShapeDtypeStruct((1, width), jnp.float32),
        ],
        in_specs=[VMEM] * 8,
        out_specs=[VMEM] * 10,
        scratch_shapes=[
            pltpu.VMEM((group, rows, width), bf16),
            pltpu.VMEM((width, group * rows), bf16),
            pltpu.VMEM((hidden, group * rows), bf16),
            pltpu.VMEM((group, rows, hidden), bf16),
            pltpu.VMEM((group, rows, hidden), bf16),
            pltpu.VMEM((group, rows, hidden), bf16),
            pltpu.VMEM((rows, width), jnp.float32),
            pltpu.VMEM((rows, width), jnp.float32),
            *ring_scratch(down_chunks[0]),
            *ring_scratch(down_chunks[1]),
            *scatter_scratch(rows, width),
            *[dma] * 4,
            *ring_semaphores(),
            *ring_semaphores(),
        ],
        compiler_params=pltpu.CompilerParams(
            collective_id=2, has_side_effects=True, vmem_limit_bytes=60 << 20
        ),
    )(x, low, full_out, my_gate, my_up, my_down, all_g, gain)


def back_kernel(
    q_ref, g_ref, pairs_ref, mix_ref, log_ref, gate_ref, up_ref, down_a_ref, down_b_ref,
    layer_base_ref, layer_part_ref, gain_grad_ref, branch_ref, low_t_ref, normed_t_ref, w_query_ref, w_key_ref, w_value_ref, x_ref, gain_ref,
    resid_grad_ref, cos_ref, sin_ref,
    tokens_ref, layer_ref, gate_total, up_total, down_a_total, down_b_total, out_a_total,
    out_b_total, rest_a_total, rest_b_total, peer_got, chain_got, layer_sib, layer_cross, layer_far,
    kv_ref, stage_ref, final_ref, qg_ref, delta_ref, grad_q_ref,
    gate_work, gate_land, up_work, up_land, out_a_work, out_a_land, out_b_work, out_b_land,
    rest_a_work, rest_a_land, rest_b_work, rest_b_land,
    low_all, normed_all, branch_all, query_all, pair_all, upstream_ref, gain_give, gain_got,
    far_ref, layer_stage,
    *semaphores,
):
    steps = Steps()
    fsdp, ctx, group, count = steps.fsdp, steps.ctx, lax.axis_size("fsdp"), lax.axis_size("ctx")
    units, deep, wide = q_ref.shape
    keys = pairs_ref.shape[2]
    rows, width = x_ref.shape
    own = width // group
    taken = iter(semaphores)

    def take(number):
        return [next(taken) for _ in range(number)]

    gate_ring = Ring(gate_work, gate_land, gate_total, take(5), True, True)
    up_ring = Ring(up_work, up_land, up_total, take(5), False, True)
    down_a = SpreadRing(down_a_total, take(2), True)
    down_b = SpreadRing(down_b_total, take(2), False)
    out_a = Ring(out_a_work, out_a_land, out_a_total, take(2), True)
    out_b = Ring(out_b_work, out_b_land, out_b_total, take(2), False)
    layer_sum = GroupScatter(
        None,
        layer_sib,
        lambda step: layer_part_ref.at[
            2 * lax.rem(lax.div(fsdp, 2) + group // 2 - step, group // 2) + 1 - lax.rem(fsdp, 2)
        ],
        layer_cross,
        far_ref,
        layer_far,
        *take(2),
    )
    layer_sum.give_sib = layer_part_ref.at[layer_sum.sibling]
    rest_a = Ring(rest_a_work, rest_a_land, rest_a_total, take(2), True)
    rest_b = Ring(rest_b_work, rest_b_land, rest_b_total, take(2), False)
    first_rings = (gate_ring, up_ring, down_a, down_b, out_a, out_b)
    peer_sends, peer_arrivals, chain_sends, chain_arrivals = take(4)
    branch_gather = GroupGather(lambda shard: branch_all.at[shard], *take(2))
    query_gather = GroupGather(lambda shard: query_all.at[shard], *take(2))
    pair_gather = GroupGather(lambda shard: pair_all.at[shard], *take(2))
    low_sends, low_arrivals, normed_sends, normed_arrivals, gain_sends, gain_arrivals = take(6)
    local_sems, stage_sems = take(2)

    barrier = pltpu.get_barrier_semaphore()
    greeted = steps.greet(barrier) + greet_group(barrier) + 2
    for device in (gate_ring.after, up_ring.after):
        pl.semaphore_signal(barrier, inc=1, device_id=device, device_id_type=MESH)

    loads = []

    def load(source, target):
        copy = pltpu.make_async_copy(source, target, local_sems.at[len(loads)])
        copy.start()
        loads.append(copy)

    n = gate_work.shape[2]
    for source, target in ((gate_ref, gate_work), (up_ref, up_work)):
        for chunk in range(count):
            load(source.at[:, pl.ds(chunk * n, n)], target.at[chunk])
    for ring, source in ((down_a, down_a_ref), (down_b, down_b_ref)):
        load(source, ring.chunk(ring.total, ring.first))
    ring_loads = len(loads)
    load(pairs_ref, kv_ref)
    load(branch_ref, branch_all.at[fsdp])
    load(low_t_ref.at[pl.ds(fsdp * own, own)], low_all.at[:, lane_tile(fsdp, rows)])
    load(normed_t_ref.at[pl.ds(fsdp * own, own)], normed_all.at[:, lane_tile(fsdp, rows)])
    for copy in loads[:ring_loads]:
        copy.wait()
    pl.semaphore_wait(barrier, greeted)
    for ring in first_rings[:4]:
        ring.start()
    branch_gather.start(branch_ref)
    layer_sum.to_sibling().start()
    for step in range(1, group // 2):
        layer_sum.to_cross(step).start()

    def slices(source, target, sends, arrivals, step):
        peer = lax.rem(fsdp + step, group)
        return pltpu.make_async_remote_copy(
            src_ref=source.at[pl.ds(peer * own, own)],
            dst_ref=target.at[:, lane_tile(fsdp, rows)],
            send_sem=sends.at[step - 1],
            recv_sem=arrivals.at[step - 1],
            device_id=(peer, ctx),
            device_id_type=MESH,
        )

    turned = [
        slices(*ends, step)
        for ends in (
            (low_t_ref, low_all, low_sends, low_arrivals),
            (normed_t_ref, normed_all, normed_sends, normed_arrivals),
        )
        for step in range(1, group)
    ]
    for copy in turned:
        copy.start()

    def prepare(unit):
        q, g = q_ref[unit], g_ref[unit]
        qg_ref[unit, :wide] = q.T
        qg_ref[unit, wide:] = g.T
        delta_ref[unit] = jnp.sum(
            g[HD:].astype(jnp.float32) * mix_ref[unit], axis=0, keepdims=True
        )
        grad_q_ref[unit] = jnp.zeros((HD, wide), jnp.float32)

    tiles(units, prepare)
    for copy in loads[ring_loads:]:
        copy.wait()

    def tick(ring, at):
        @pl.when(jnp.logical_and(at >= 0, at < ring.ticks))
        def _():
            ring.tick(jnp.clip(at, 0, ring.ticks - 1))

    late = steps.levels // 2 + 1

    def pump(at):
        lag = (0, 0, 0, 0, late, late)
        for turn, ring in enumerate(first_rings):

            @pl.when(lax.rem(at, len(first_rings)) == turn)
            def _():
                tick(ring, lax.div(at, len(first_rings)) - lag[turn])

    def back(unit, first, blocks, diagonal):
        kv = kv_ref[pl.ds(first, blocks), unit].reshape(blocks * keys, deep)
        scores = jnp.dot(kv, q_ref[unit], preferred_element_type=jnp.float32)
        probs = jnp.exp(scores - log_ref[unit])
        if diagonal:
            probs = jnp.where(causal(keys, wide, scores.shape), probs, 0.0)
        grad_probs = jnp.dot(kv, g_ref[unit], preferred_element_type=jnp.float32)
        grad_scores = (probs * (grad_probs - delta_ref[unit])).astype(jnp.bfloat16)
        both = jnp.concatenate([grad_scores, probs.astype(jnp.bfloat16)], axis=1)
        grad_kv = jnp.dot(both, qg_ref[unit], preferred_element_type=jnp.float32)
        added = jnp.dot(kv.T, grad_scores, preferred_element_type=jnp.float32)
        grad_q_ref[unit] = grad_q_ref[unit] + added[:HD]
        kv_ref[pl.ds(first, blocks), unit] = grad_kv.astype(kv_ref.dtype).reshape(
            blocks, keys, deep
        )

    def across(pair):
        return pltpu.make_async_remote_copy(
            src_ref=kv_ref.at[2 * pair + 1 - steps.side],
            dst_ref=peer_got.at[pair],
            send_sem=peer_sends.at[pair],
            recv_sem=peer_arrivals.at[pair],
            device_id=steps.peer,
            device_id_type=MESH,
        )

    def down_chain(pair):
        return pltpu.make_async_remote_copy(
            src_ref=kv_ref.at[2 * pair + steps.side],
            dst_ref=chain_got.at[pair],
            send_sem=chain_sends.at[pair],
            recv_sem=chain_arrivals.at[pair],
            device_id=steps.below,
            device_id_type=MESH,
        )

    def combine(time):
        pair = time - steps.levels + steps.level

        @pl.when(jnp.logical_and(pair >= 0, pair <= steps.level))
        def _():
            for slot, expected, arrival, source in (
                (0, jnp.logical_or(pair < steps.level, steps.side == 0), across, peer_got),
                (1, steps.has_above, down_chain, chain_got),
            ):

                @pl.when(expected)
                def _():
                    arrival(pair).wait_recv()
                    copy = pltpu.make_async_copy(
                        source.at[pair], stage_ref.at[slot], stage_sems.at[slot]
                    )
                    copy.start()
                    copy.wait()

                @pl.when(jnp.logical_not(expected))
                def _():
                    stage_ref[slot] = jnp.zeros(stage_ref.shape[1:], stage_ref.dtype)

            def add(unit):
                final_ref[unit] = (
                    kv_ref[2 * pair + steps.side, unit].astype(jnp.float32)
                    + stage_ref[0, unit].astype(jnp.float32)
                    + stage_ref[1, unit].astype(jnp.float32)
                )

            tiles(units, add)

            @pl.when(pair < steps.level)
            def _():
                kv_ref[2 * pair + steps.side] = final_ref[...].astype(kv_ref.dtype)
                down_chain(pair).start()

    row_blocks = own // 16

    def weight_grad(left, right, begin, end, target, first, loop):
        span = LANES * next(n for n in (3, 2, 1) if (end - begin) % (n * LANES) == 0)

        def body(at):
            columns = pl.ds(pl.multiple_of(begin + at * span, LANES), span)
            part = forward_dot(
                left[...], right[:, :, columns].reshape(group * rows, span)
            ).astype(jnp.bfloat16)
            for block in range(span // LANES):
                here = first + (at * (span // LANES) + block) * row_blocks
                target[pl.ds(here, row_blocks)] = part[
                    :, block * LANES : (block + 1) * LANES
                ].reshape(row_blocks, 16, LANES)

        loop((end - begin) // span, body)
        return first + (end - begin) // LANES * row_blocks

    def clear_from(target, first):
        for spare in range(first, target.shape[0]):
            target[spare] = jnp.zeros((16, LANES), jnp.bfloat16)

    def out_grad():
        for copy in turned[: group - 1]:
            copy.wait_recv()
        branch_gather.forward()
        branch_gather.sibling_here()
        for step in range(1, branch_gather.chips):
            branch_gather.crossed(step)
        split = out_split(width)
        clear_from(out_a_work, weight_grad(low_all, branch_all, 0, split, out_a_work, 0, tiles))
        clear_from(out_b_work, weight_grad(low_all, branch_all, split, width, out_b_work, 0, tiles))
        out_a.start()
        out_b.start()

    turns = units // 2

    def slot(pair):
        def turn(at):
            @pl.when(pair < steps.level)
            def _():
                for unit in (2 * at, 2 * at + 1):
                    back(unit, 2 * pair, 2, False)

            @pl.when(pair == steps.level)
            def _():
                for unit in (2 * at, 2 * at + 1):
                    back(unit, ctx, 1, True)

            @pl.when(jnp.logical_and(pair == steps.level, steps.side == 1))
            def _():
                for unit in (2 * at, 2 * at + 1):
                    back(unit, ctx - 1, 1, False)

            pump(pair * turns + at)

        tiles(turns, turn)

        @pl.when(jnp.logical_or(pair < steps.level, (pair == steps.level) & (steps.side == 1)))
        def _():
            across(pair).start()

        combine(pair)

        @pl.when(pair == late - 1)
        def _():
            out_grad()

    tiles(steps.levels, slot)
    pumped = [steps.levels * turns]

    def pump_next(times=1):
        def body(at, unused, begin=pumped[0]):
            pump(begin + at)
            return unused

        lax.fori_loop(0, times, body, 0)
        pumped[0] += times

    def pumping(times, body):
        begin = pumped[0]

        def step(at):
            body(at)
            pump(begin + at)

        tiles(times, step)
        pumped[0] += times

    cosine, sine = cos_ref[...], sin_ref[...]

    def unturn(columns):
        first, second = columns[: HD // 2], columns[HD // 2 :]
        return jnp.concatenate(
            [first * cosine + second * sine, second * cosine - first * sine], axis=0
        )

    sequences = units // KVH
    groups = wide // keys
    for sequence in range(sequences):
        span = slice(sequence * keys, (sequence + 1) * keys)
        for pair in range(H // 2):
            heads = []
            for head in (2 * pair, 2 * pair + 1):
                unit, member = sequence * KVH + head // groups, head % groups
                part = grad_q_ref[unit, :, member * keys : (member + 1) * keys]
                heads.append(unturn(part * HD ** (-0.5)))
            query_all[fsdp, span, pair * 2 * HD : (pair + 1) * 2 * HD] = (
                jnp.concatenate(heads, axis=0).astype(jnp.bfloat16).T
            )
        pump_next()
    query_gather.start(query_all.at[fsdp])
    combine(steps.levels)
    kv_width = KVH * HD
    for sequence in range(sequences):
        span = slice(sequence * keys, (sequence + 1) * keys)
        for pair in range(KVH // 2):
            turned_keys, turned_values = [], []
            for unit in (sequence * KVH + 2 * pair, sequence * KVH + 2 * pair + 1):
                part = final_ref[unit].T
                turned_keys.append(unturn(part[:HD]))
                turned_values.append(part[HD:])
            for start, parts in ((0, turned_keys), (kv_width, turned_values)):
                pair_all[fsdp, span, start + pair * 2 * HD : start + (pair + 1) * 2 * HD] = (
                    jnp.concatenate(parts, axis=0).astype(jnp.bfloat16).T
                )
    pair_gather.start(pair_all.at[fsdp])
    pump_next(2)
    query_gather.forward()
    for step in range(1, layer_sum.chips):
        ours = layer_part_ref.at[2 * lax.rem(layer_sum.chip + layer_sum.chips - step, layer_sum.chips) + layer_sum.core]
        for source, target in ((ours, far_ref.at[step - 1]), (layer_cross.at[step - 1], layer_stage)):
            if source is not ours:
                layer_sum.to_cross(step).wait_recv()
            copy = pltpu.make_async_copy(source, target, stage_sems.at[0])
            copy.start()
            copy.wait()
        far_ref[step - 1] = (
            far_ref[step - 1].astype(jnp.float32) + layer_stage[...].astype(jnp.float32)
        ).astype(jnp.bfloat16)
        layer_sum.to_far(step).start()

    step_out = width_tile(width)

    def upstream_tile(at):
        columns = pl.ds(pl.multiple_of(at * step_out, LANES), step_out)
        upstream_ref[:, columns] = (
            dot_columns(query_all[fsdp], w_query_ref[columns, :])
            + dot_columns(pair_all[fsdp, :, :kv_width], w_key_ref[columns, :])
            + dot_columns(pair_all[fsdp, :, kv_width:], w_value_ref[columns, :])
        )

    pumping(width // step_out, upstream_tile)
    inputs = x_ref[...].astype(jnp.float32)
    scale = norm_scale(inputs)
    upstream = upstream_ref[...]
    scaled = upstream * gain_ref[...]
    tokens_ref[...] = (
        resid_grad_ref[...]
        + scale * scaled
        - inputs * scale**3 * jnp.mean(scaled * inputs, axis=-1, keepdims=True)
    )
    gain_attn = jnp.sum(upstream * inputs * scale, axis=0, keepdims=True)
    lanes = width // LANES
    gain_give[...] = jnp.zeros(gain_give.shape, jnp.float32)
    for block in range(lanes):
        columns = slice(block * LANES, (block + 1) * LANES)
        gain_give[block : block + 1, :] = gain_attn[:, columns]
        gain_give[lanes + block : lanes + block + 1, :] = gain_grad_ref[:, columns]

    def gain_copy(step):
        peer = lax.rem(fsdp + step, group)
        return pltpu.make_async_remote_copy(
            src_ref=gain_give,
            dst_ref=gain_got.at[step - 1],
            send_sem=gain_sends.at[step - 1],
            recv_sem=gain_arrivals.at[step - 1],
            device_id=(peer, ctx),
            device_id_type=MESH,
        )

    for step in range(1, group):
        gain_copy(step).start()
    pump_next()
    for copy in turned[group - 1 :]:
        copy.wait_recv()
    query_gather.sibling_here()
    for step in range(1, query_gather.chips):
        query_gather.crossed(step)
    split = query_split(width)
    filled_a = weight_grad(normed_all, query_all, 0, split, rest_a_work, 0, pumping)
    filled_b = weight_grad(normed_all, query_all, split, width, rest_b_work, 0, pumping)
    pair_gather.forward()
    pump_next()
    pair_gather.sibling_here()
    for step in range(1, pair_gather.chips):
        pair_gather.crossed(step)
    filled_b = weight_grad(normed_all, pair_all, 0, 2 * kv_width, rest_b_work, filled_b, pumping)
    gains = gain_give[...]
    for step in range(1, group):
        gain_copy(step).wait_recv()
        gains = gains + gain_got[step - 1]
    gain_tiles = gains.shape[0] // 16
    rest_a_work[filled_a : filled_a + gain_tiles] = gains.astype(jnp.bfloat16).reshape(
        gain_tiles, 16, LANES
    )
    clear_from(rest_a_work, filled_a + gain_tiles)
    clear_from(rest_b_work, filled_b)
    rest_a.start()
    rest_b.start()
    begun = pumped[0]
    half = len(first_rings) // 2
    total_pumps = max(gate_ring.ticks, late + out_a.ticks) * len(first_rings)

    def last_ticks(at, unused):
        for turn in range(half):
            pump(jnp.minimum(begun + half * at + turn, total_pumps))
        tick(rest_a, at)
        tick(rest_b, at)
        return unused

    rounds = max(rest_a.ticks, -(-(total_pumps - begun) // half))
    lax.fori_loop(0, rounds, last_ticks, 0)
    layer_sum.to_sibling().wait_recv()
    layer = layer_base_ref[...]
    arrived = [layer_sib]
    for step in range(1, layer_sum.chips):
        layer_sum.to_far(step).wait_recv()
        arrived.append(layer_far.at[step - 1])
    for source in arrived:
        copy = pltpu.make_async_copy(source, layer_stage, stage_sems.at[0])
        copy.start()
        copy.wait()
        layer = layer + layer_stage[...].astype(jnp.float32)
    layer_ref[...] = layer.astype(jnp.bfloat16)
    layer_sum.sent()
    for ring in first_rings + (rest_a, rest_b):
        ring.finish()
    for copy in turned:
        copy.wait_send()
    for gather in (branch_gather, query_gather, pair_gather):
        gather.sent()
    for step in range(1, group):
        gain_copy(step).wait_send()

    def sent(pair):
        @pl.when(jnp.logical_or(pair < steps.level, steps.side == 1))
        def _():
            across(pair).wait_send()

        @pl.when(pair < steps.level)
        def _():
            down_chain(pair).wait_send()

    tiles(steps.level + 1, sent)


def layer_back(
    q_wide, g_wide, all_pairs, mix, log_total, gate_part, up_part, down_a, down_b, layer_base,
    layer_parts, gain_grad, branch, low_t, normed_t, w_query, w_key, w_value, x, gain, resid_grad,
    cosine, sine,
):
    group, count = lax.axis_size("fsdp"), lax.axis_size("ctx")
    units, deep, wide = q_wide.shape
    keys = all_pairs.shape[2]
    rows, width = x.shape
    own, kv_width = width // group, w_key.shape[1]
    bf16, f32 = jnp.bfloat16, jnp.float32
    dma = pltpu.SemaphoreType.DMA
    wide_chunk = (group, gate_part.shape[1] // count, 16, LANES)
    gain_rows = spread(2 * (width // LANES), 16)
    split, row_blocks = query_split(width), own // 16
    out_first = out_split(width)
    chips = group // 2
    out_a_chunk, out_b_chunk, a_chunk, b_chunk = [
        (spread(held, count) // count, 16, LANES)
        for held in (
            out_first // LANES * row_blocks,
            (width - out_first) // LANES * row_blocks,
            split // LANES * row_blocks + gain_rows // 16,
            (width - split + 2 * kv_width) // LANES * row_blocks,
        )
    ]
    levels = count // 2
    return pl.pallas_call(
        back_kernel,
        out_shape=[
            jax.ShapeDtypeStruct((rows, width), f32),
            jax.ShapeDtypeStruct((rows, width), bf16),
            ring_total(wide_chunk, True),
            ring_total(wide_chunk, True),
            ring_total(down_a.shape),
            ring_total(down_b.shape),
            ring_total(out_a_chunk),
            ring_total(out_b_chunk),
            ring_total(a_chunk),
            ring_total(b_chunk),
            *[jax.ShapeDtypeStruct((levels, units, keys, deep), bf16)] * 2,
            jax.ShapeDtypeStruct((rows, width), bf16),
            *[jax.ShapeDtypeStruct((chips - 1, rows, width), bf16)] * 2,
        ],
        in_specs=[VMEM, VMEM, ANY, VMEM, VMEM, ANY, ANY, ANY, ANY, VMEM, ANY, VMEM, ANY, ANY, ANY]
        + [VMEM] * 8,
        out_specs=[VMEM] * 10 + [ANY] * 5,
        scratch_shapes=[
            pltpu.VMEM(all_pairs.shape, bf16),
            pltpu.VMEM((2, units, keys, deep), bf16),
            pltpu.VMEM((units, keys, deep), f32),
            pltpu.VMEM((units, 2 * wide, deep), bf16),
            pltpu.VMEM((units, 1, wide), f32),
            pltpu.VMEM((units, HD, wide), f32),
            *ring_scratch(wide_chunk, True),
            *ring_scratch(wide_chunk, True),
            *ring_scratch(out_a_chunk),
            *ring_scratch(out_b_chunk),
            *ring_scratch(a_chunk),
            *ring_scratch(b_chunk),
            pltpu.VMEM((own, group * rows), bf16),
            pltpu.VMEM((own, group * rows), bf16),
            pltpu.VMEM((group, rows, width), bf16),
            pltpu.VMEM((group, rows, width), bf16),
            pltpu.VMEM((group, rows, 2 * kv_width), bf16),
            pltpu.VMEM((rows, width), f32),
            pltpu.VMEM((gain_rows, LANES), f32),
            pltpu.VMEM((group - 1, gain_rows, LANES), f32),
            pltpu.VMEM((chips - 1, rows, width), bf16),
            pltpu.VMEM((rows, width), bf16),
            *ring_semaphores(True),
            *ring_semaphores(True),
            *[kind for _ in range(4) for kind in ring_semaphores()],
            *[dma((group - 1,))] * 2,
            *[kind for _ in range(2) for kind in ring_semaphores()],
            *[dma((levels,))] * 4,
            *[group_semaphores()] * 6,
            *[dma((group - 1,))] * 6,
            dma((6 + 2 * count,)),
            dma((2,)),
        ],
        compiler_params=pltpu.CompilerParams(
            collective_id=3, has_side_effects=True, vmem_limit_bytes=62 << 20
        ),
    )(
        q_wide, g_wide, all_pairs, mix, log_total, gate_part, up_part, down_a, down_b, layer_base,
        layer_parts, gain_grad, branch, low_t, normed_t, w_query, w_key, w_value, x, gain, resid_grad,
        cosine, sine,
    )


def finish_kernel(
    gate_ref, up_ref, down_a_ref, down_b_ref, out_a_ref, out_b_ref, rest_a_ref, rest_b_ref,
    query_grad, key_grad, value_grad, out_grad, gate_grad, up_grad, down_grad,
):
    rows = gate_grad.shape[0]
    row_blocks = rows // 16
    for source, target in ((gate_ref, gate_grad), (up_ref, up_grad)):
        held = source[...].reshape((-1,) + source.shape[3:])
        for block in range(target.shape[1] // LANES):
            target[:, block * LANES : (block + 1) * LANES] = (
                held[block * row_blocks : (block + 1) * row_blocks]
                .reshape(rows, LANES)
                .astype(jnp.float32)
            )

    @pl.when(pl.program_id(0) == 0)
    def _():
        def unpack(source, first, target, begin, end):
            for block in range(begin, end):
                here = first + (block - begin) * row_blocks
                target[:, block * LANES : (block + 1) * LANES] = (
                    source[here : here + row_blocks].reshape(rows, LANES).astype(jnp.float32)
                )
            return first + (end - begin) * row_blocks

        width, kv_width = query_grad.shape[1], key_grad.shape[1]
        split = query_split(width) // LANES
        middle = out_split(width) // LANES
        unpack(out_a_ref, 0, out_grad, 0, middle)
        unpack(out_b_ref, 0, out_grad, middle, width // LANES)
        unpack(rest_a_ref, 0, query_grad, 0, split)
        at = unpack(rest_b_ref, 0, query_grad, split, width // LANES)
        at = unpack(rest_b_ref, at, key_grad, 0, kv_width // LANES)
        unpack(rest_b_ref, at, value_grad, 0, kv_width // LANES)
        blocks = down_grad.shape[0] // 16
        first = min(down_a_ref.shape[0], blocks)
        for begin, end, source in ((0, first, down_a_ref), (first, blocks, down_b_ref)):
            if end > begin:
                down_grad[begin * 16 : end * 16, :] = (
                    source[: end - begin]
                    .reshape((end - begin) * 16, down_grad.shape[1])
                    .astype(jnp.float32)
                )


def finish(gate, up, down_a, down_b, out_a, out_b, rest_a, rest_b, own, width, kv_width, hidden):
    count, group, n = gate.shape[:3]

    def whole(array):
        return pl.BlockSpec(array.shape, lambda part, rank=len(array.shape): (0,) * rank)

    wide = pl.BlockSpec((count, 1, n, 16, LANES), lambda part: (0, part, 0, 0, 0))
    outs = [
        jax.ShapeDtypeStruct((own, columns), jnp.float32)
        for columns in (width, kv_width, kv_width, width, FF, FF)
    ] + [jax.ShapeDtypeStruct((hidden, width), jnp.float32)]
    slice_spec = pl.BlockSpec((own, FF // group), lambda part: (0, part))
    return pl.pallas_call(
        finish_kernel,
        grid=(group,),
        out_shape=outs,
        in_specs=[wide, wide] + [whole(a) for a in (down_a, down_b, out_a, out_b, rest_a, rest_b)],
        out_specs=[whole(a) for a in outs[:4]] + [slice_spec, slice_spec, whole(outs[6])],
        compiler_params=pltpu.CompilerParams(vmem_limit_bytes=60 << 20),
    )(gate, up, down_a, down_b, out_a, out_b, rest_a, rest_b)


def on_device(
    tokens, w_query, w_key, w_value, w_out, w_gate, w_up, w_down, gain_attn, gain_ffn, cotangent
):
    block_len, seq_count, width = tokens.shape
    rows_count = block_len * seq_count
    kv_width = KVH * HD
    positions = lax.axis_index("ctx") * block_len + jnp.arange(block_len, dtype=jnp.int32)
    freqs = ROTARY_BASE ** (-2.0 * jnp.arange(HD // 2, dtype=jnp.float32) / HD)
    angles = freqs[:, None] * positions.astype(jnp.float32)[None, :]
    cosine, sine = jnp.cos(angles), jnp.sin(angles)
    x_rows = jnp.swapaxes(tokens, 0, 1).reshape(rows_count, width)
    g_rows = jnp.swapaxes(cotangent, 0, 1).reshape(rows_count, width)
    own = gain_attn.shape[0]
    units = seq_count * KVH
    wide = H // KVH * block_len
    own_gains = jnp.pad(
        jnp.stack([gain_attn, gain_ffn]).astype(jnp.float32), ((0, 6), (0, spread(own, LANES) - own))
    )
    (
        q_wide, normed_t, gains, full_query, full_key, full_value, attn_low, low_t, mix_unit, log_total,
        all_pairs, full_out, my_gate, my_up, all_g,
    ) = attend(
        x_rows, own_gains, cosine, sine, w_query, w_key, w_value, w_out, w_gate, w_up, g_rows, seq_count
    )
    (
        layer_base, layer_parts, grad_resid, grad_branch, g_wide, gate_part, up_part, down_a, down_b,
        gain_term_ffn,
    ) = (
        feed_forward(
            x_rows,
            attn_low,
            full_out,
            my_gate,
            my_up,
            w_down,
            all_g,
            gains[1:2],
            units,
            wide,
        )
    )
    (
        grad_tokens, layer_out, gate_total, up_total, down_a, down_b, out_a, out_b, rest_a, rest_b,
        *_,
    ) = layer_back(
        q_wide,
        g_wide,
        all_pairs,
        mix_unit,
        log_total,
        gate_part,
        up_part,
        down_a,
        down_b,
        layer_base,
        layer_parts,
        gain_term_ffn,
        grad_branch,
        low_t,
        normed_t,
        full_query,
        full_key,
        full_value,
        x_rows,
        gains[:1],
        grad_resid,
        cosine,
        sine,
    )
    filled = query_split(width) // LANES * (own // 16)
    gain_grads = rest_a[filled:].reshape(-1, LANES)[: 2 * (width // LANES)].reshape(2, width)
    gain_grads = lax.dynamic_slice_in_dim(gain_grads, lax.axis_index("fsdp") * own, own, 1)
    gain_grads = gain_grads.astype(jnp.float32)
    grads = finish(
        gate_total, up_total, down_a, down_b, out_a, out_b, rest_a, rest_b,
        own, width, kv_width, w_down.shape[0],
    )
    return (
        jnp.swapaxes(layer_out.reshape(seq_count, block_len, width), 0, 1),
        jnp.swapaxes(grad_tokens.reshape(seq_count, block_len, width), 0, 1),
        *grads,
        gain_grads[0],
        gain_grads[1],
    )


def solution(mesh):
    return jax.shard_map(
        on_device,
        mesh=mesh,
        in_specs=(
            P("ctx", "fsdp", None),
            P("fsdp", None),
            P("fsdp", None),
            P("fsdp", None),
            P("fsdp", None),
            P("fsdp", None),
            P("fsdp", None),
            P("fsdp", None),
            P("fsdp"),
            P("fsdp"),
            P("ctx", "fsdp", None),
        ),
        out_specs=(
            P("ctx", "fsdp", None),
            P("ctx", "fsdp", None),
            P("fsdp", None),
            P("fsdp", None),
            P("fsdp", None),
            P("fsdp", None),
            P("fsdp", None),
            P("fsdp", None),
            P("fsdp", None),
            P("fsdp"),
            P("fsdp"),
        ),
        check_vma=False,
    )
```

```python
import functools

import jax
import jax.numpy as jnp
from jax import lax
from jax.experimental import pallas as pl
from jax.experimental.pallas import tpu as pltpu
from jax.sharding import PartitionSpec as P

H = 18
KVH = 6
HD = 64
FF = 3072


EPSILON = 1e-05
ROTARY_BASE = 10000.0
MASKED_SCORE = -1e30


def norm_scale(rows):
    return lax.rsqrt(jnp.mean(rows * rows, axis=-1, keepdims=True) + EPSILON)


def forward_dot(left, right):
    return jnp.dot(left, right, preferred_element_type=jnp.float32)


MESH = pl.DeviceIdType.MESH
LANES = 128


def ring_place(ctx, fsdp, count):
    column, side = lax.div(ctx, 2), lax.rem(ctx, 2)
    place = column + side * (count - 1 - 2 * column)
    odd = lax.rem(fsdp, 2)
    return place + odd * (count - 1 - 2 * place)


def ring_ctx(place, fsdp, count):
    odd = lax.rem(fsdp, 2)
    place = place + odd * (count - 1 - 2 * place)
    late = lax.div(place, count // 2)
    return (1 - late) * 2 * place + late * (2 * (count - 1 - place) + 1)


class GroupGather:
    def __init__(self, shard_of, sends, arrivals):
        self.shard_of, self.sends, self.arrivals = shard_of, sends, arrivals
        self.fsdp, self.ctx = lax.axis_index("fsdp"), lax.axis_index("ctx")
        self.chips = lax.axis_size("fsdp") // 2
        self.chip, self.core = lax.div(self.fsdp, 2), lax.rem(self.fsdp, 2)
        self.sibling = 2 * self.chip + 1 - self.core

    def copy(self, source, shard, semaphore, device):
        return pltpu.make_async_remote_copy(
            src_ref=source,
            dst_ref=self.shard_of(shard),
            send_sem=self.sends.at[semaphore],
            recv_sem=self.arrivals.at[semaphore],
            device_id=(device, self.ctx),
            device_id_type=MESH,
        )

    def same_core(self, step):
        return 2 * lax.rem(self.chip + step, self.chips) + self.core

    def across(self, source):
        return self.copy(source, self.fsdp, 0, self.sibling)

    def out(self, source, step):
        return self.copy(source, self.fsdp, step, self.same_core(step))

    def onward(self, step):
        shard = self.same_core(self.chips - step)
        return self.copy(self.shard_of(shard), shard, self.chips - 1 + step, self.sibling)

    def start(self, source):
        for step in range(1, self.chips):
            self.out(source, step).start()
        self.across(source).start()

    def forward(self):
        own = self.shard_of(self.fsdp)
        for step in range(1, self.chips):
            self.out(own, step).wait_recv()
            self.onward(step).start()

    def sibling_here(self):
        self.across(self.shard_of(self.fsdp)).wait_recv()

    def crossed(self, step):
        self.onward(step).wait_recv()

    def sent(self):
        own = self.shard_of(self.fsdp)
        self.across(own).wait_send()
        for step in range(1, self.chips):
            self.out(own, step).wait_send()
            self.onward(step).wait_send()

    def finish(self):
        self.forward()
        self.sibling_here()
        for step in range(1, self.chips):
            self.crossed(step)
        self.sent()


class HalfGather:
    def __init__(self, held, own_rows, sends, arrivals):
        self.held, self.own = held, own_rows
        self.sends, self.arrivals = sends, arrivals
        self.fsdp, self.ctx = lax.axis_index("fsdp"), lax.axis_index("ctx")
        self.chips = lax.axis_size("fsdp") // 2
        self.chip, self.core = lax.div(self.fsdp, 2), lax.rem(self.fsdp, 2)
        self.sibling = 2 * self.chip + 1 - self.core
        self.side = lax.rem(self.ctx, 2)
        self.pair = self.ctx + 1 - 2 * self.side
        first = -(-own_rows // 32) * 16
        self.halves = ((0, first), (first, own_rows - first))

    def same_core(self, step):
        return 2 * lax.rem(self.chip + step, self.chips) + self.core

    def rows(self, shard, half=None):
        begin, size = (0, self.own) if half is None else self.halves[half]
        return self.held.at[pl.ds(shard * self.own + begin, size)]

    def copy(self, source, target, semaphore, device):
        return pltpu.make_async_remote_copy(
            src_ref=source,
            dst_ref=target,
            send_sem=self.sends.at[semaphore],
            recv_sem=self.arrivals.at[semaphore],
            device_id=device,
            device_id_type=MESH,
        )

    def on_side(self, body):
        for half in range(2):

            @pl.when(self.side == half)
            def _(half=half):
                body(half)

    def across(self, source):
        return self.copy(source, self.rows(self.fsdp), 0, (self.sibling, self.ctx))

    def out(self, source, step, half):
        begin, size = self.halves[half]
        return self.copy(
            source.at[pl.ds(begin, size)],
            self.rows(self.fsdp, half),
            step,
            (self.same_core(step), self.ctx),
        )

    def to_pair(self, step, half):
        part = self.rows(self.same_core(self.chips - step), half)
        return self.copy(part, part, self.chips - 1 + step, (self.fsdp, self.pair))

    def onward(self, step):
        part = self.rows(self.same_core(self.chips - step))
        return self.copy(part, part, 2 * self.chips - 2 + step, (self.sibling, self.ctx))

    def start(self, source):
        def send(half):
            for step in range(1, self.chips):
                self.out(source, step, half).start()

        self.on_side(send)
        self.across(source).start()

    def to_pairs(self):
        def forward(half):
            for step in range(1, self.chips):
                self.out(self.rows(self.fsdp), step, half).wait_recv()
                self.to_pair(step, half).start()

        self.on_side(forward)

    def to_sibling(self):
        def forward(half):
            for step in range(1, self.chips):
                self.to_pair(step, 1 - half).wait_recv()

        self.on_side(forward)
        for step in range(1, self.chips):
            self.onward(step).start()

    def arrived(self):
        self.across(self.rows(self.fsdp)).wait_recv()
        for step in range(1, self.chips):
            self.onward(step).wait_recv()

    def sent(self):
        def wait(half):
            for step in range(1, self.chips):
                self.out(self.rows(self.fsdp), step, half).wait_send()
                self.to_pair(step, half).wait_send()

        self.on_side(wait)
        self.across(self.rows(self.fsdp)).wait_send()
        for step in range(1, self.chips):
            self.onward(step).wait_send()


def half_semaphores(many):
    return pltpu.SemaphoreType.DMA((many, 3 * (lax.axis_size("fsdp") // 2) - 2))


def group_semaphores():
    return pltpu.SemaphoreType.DMA((lax.axis_size("fsdp") - 1,))


def greet_group(barrier):
    fsdp, ctx, group = lax.axis_index("fsdp"), lax.axis_index("ctx"), lax.axis_size("fsdp")
    for step in range(1, group):
        peer = lax.rem(fsdp + step, group)
        pl.semaphore_signal(barrier, inc=1, device_id=(peer, ctx), device_id_type=MESH)
    return group - 1


class Steps:
    def __init__(self):
        self.fsdp, self.ctx = lax.axis_index("fsdp"), lax.axis_index("ctx")
        self.levels = lax.axis_size("ctx") // 2
        self.level, self.side = lax.div(self.ctx, 2), lax.rem(self.ctx, 2)
        self.peer = (self.fsdp, 2 * self.level + 1 - self.side)
        self.above = (self.fsdp, lax.rem(self.ctx + 2, 2 * self.levels))
        self.below = (self.fsdp, lax.rem(self.ctx + 2 * self.levels - 2, 2 * self.levels))
        self.has_above = self.level + 1 < self.levels
        self.has_below = self.level > 0

    def greet(self, barrier):
        pl.semaphore_signal(barrier, inc=1, device_id=self.peer, device_id_type=MESH)

        @pl.when(self.has_above)
        def _():
            pl.semaphore_signal(barrier, inc=1, device_id=self.above, device_id_type=MESH)

        @pl.when(self.has_below)
        def _():
            pl.semaphore_signal(barrier, inc=1, device_id=self.below, device_id_type=MESH)

        return 1 + jnp.minimum(self.level, 1) + jnp.minimum(self.levels - 1 - self.level, 1)


PARTS = 2


def causal(keys, wide, shape):
    key_at = lax.broadcasted_iota(jnp.int32, shape, 0)
    query_at = lax.rem(lax.broadcasted_iota(jnp.int32, shape, 1), keys)
    return key_at <= query_at


def attend_kernel(
    x_ref, gain_ref, cos_ref, sin_ref, query_ref, key_ref, value_ref, out_ref, gate_ref, up_ref, g_ref,
    q_ref, normed_t_ref, gains_ref, full_query, full_key, full_value,
    low_ref, low_t_ref, mix_ref, log_ref, all_ref, full_out_ref, my_gate_ref, my_up_ref, all_g_ref,
    normed_ref, key_rows, gain_all,
    top_ref, total_ref, chain_sends, chain_arrivals, peer_sends, peer_arrivals,
    half_sends, half_arrivals, gain_sends, gain_arrivals,
    out_sends, out_arrivals, g_sends, g_arrivals, part_sends, part_arrivals, local_sems,
):
    steps = Steps()
    fsdp, ctx, group = steps.fsdp, steps.ctx, lax.axis_size("fsdp")
    units, deep, wide = q_ref.shape
    keys = all_ref.shape[2]
    per_part = units // PARTS
    rows_count, width = x_ref.shape
    own = query_ref.shape[0]
    sequences, groups = units // KVH, H // KVH
    barrier = pltpu.get_barrier_semaphore()
    greeted = steps.greet(barrier) + greet_group(barrier)
    span = KVH * HD
    pieces = [(key_ref, full_key, 0), (value_ref, full_value, 0)]
    pieces += [(query_ref, full_query, start) for start in range(0, width, span)]
    gathers = []
    for at, (source, target, start) in enumerate(pieces):
        columns = pl.ds(start, span)
        gather = HalfGather(
            target.at[:, columns], own, half_sends.at[at], half_arrivals.at[at]
        )
        gathers.append((gather, source.at[:, columns]))
    own_rows = pl.ds(fsdp * own, own)
    own_copies = [
        pltpu.make_async_copy(source, target.at[own_rows], local_sems.at[4 + at])
        for at, (source, target) in enumerate(
            ((key_ref, full_key), (value_ref, full_value), (query_ref, full_query))
        )
    ]
    for copy in own_copies:
        copy.start()
    gain_all[fsdp] = gain_ref[...]
    pl.semaphore_wait(barrier, greeted)

    def gain_copy(step):
        peer = lax.rem(fsdp + step, group)
        return pltpu.make_async_remote_copy(
            src_ref=gain_ref,
            dst_ref=gain_all.at[fsdp],
            send_sem=gain_sends.at[step - 1],
            recv_sem=gain_arrivals.at[step - 1],
            device_id=(peer, ctx),
            device_id_type=MESH,
        )

    for step in range(1, group):
        gain_copy(step).start()
    for gather, source in gathers:
        gather.start(source)
    inputs = x_ref[...].astype(jnp.float32)
    scale = norm_scale(inputs)
    q_ref[:, HD:, :] = jnp.zeros((units, HD, wide), q_ref.dtype)
    for step in range(1, group):
        gain_copy(step).wait_recv()
    gains = jnp.concatenate([gain_all[shard][:, :own] for shard in range(group)], axis=1)
    gains_ref[...] = gains
    normed_ref[...] = (inputs * scale * gains[:1]).astype(jnp.bfloat16)
    cosine, sine = cos_ref[...], sin_ref[...]

    def turn(columns):
        first, second = columns[: HD // 2], columns[HD // 2 :]
        return jnp.concatenate(
            [first * cosine - second * sine, second * cosine + first * sine], axis=0
        ).astype(jnp.bfloat16)

    def block_copy(level, part, side, semaphores, arrivals, arrives, device):
        block = 2 * (steps.level - level) + side
        held = all_ref.at[block, pl.ds(part * per_part, per_part)]
        return pltpu.make_async_remote_copy(
            src_ref=held,
            dst_ref=held,
            send_sem=semaphores.at[level, part],
            recv_sem=arrivals.at[arrives, part],
            device_id=device,
            device_id_type=MESH,
        )

    def chain(level, part):
        return block_copy(
            level, part, steps.side, chain_sends, chain_arrivals, level + 1, steps.above
        )

    def across(level, part):
        return block_copy(
            level, part, steps.side, peer_sends, peer_arrivals, level, steps.peer
        )

    def pass_on(level, part):
        @pl.when(steps.has_above)
        def _():
            chain(level, part).start()

    def project(at):
        _, weight, start = pieces[at]
        made = forward_dot(normed_ref[...], weight[:, start : start + span])
        if at == 0:
            key_rows[...] = made
            return
        for sequence in range(sequences):
            block = slice(sequence * keys, (sequence + 1) * keys)
            for pair in range(span // (2 * HD)):
                columns = slice(pair * 2 * HD, (pair + 1) * 2 * HD)
                turned = made[block, columns].T
                if at == 1:
                    turned_keys = key_rows[block, columns].T
                    for half in range(2):
                        held = slice(half * HD, (half + 1) * HD)
                        both = jnp.concatenate(
                            [turn(turned_keys[held]), turned[held].astype(jnp.bfloat16)], axis=0
                        )
                        all_ref[ctx, sequence * KVH + 2 * pair + half] = both.T
                else:
                    for half in range(2):
                        head = start // HD + 2 * pair + half
                        unit, member = sequence * KVH + head // groups, head % groups
                        part = turn(turned[half * HD : (half + 1) * HD])
                        q_ref[unit, :HD, member * keys : (member + 1) * keys] = part * jnp.bfloat16(
                            HD ** (-0.5)
                        )
        if at == 1:
            for part in range(PARTS):
                pass_on(0, part)

                @pl.when(steps.side == 0)
                def _():
                    across(0, part).start()

    last = len(pieces)
    for at in range(last + 2):
        if at < last:
            gathers[at][0].to_pairs()
        if 1 <= at <= last:
            gathers[at - 1][0].to_sibling()
        if at == 1:
            for column in range(width // LANES):
                columns = slice(column * LANES, (column + 1) * LANES)
                normed_t_ref[columns, :] = normed_ref[:, columns].T
            for copy in own_copies:
                copy.wait()
        if at >= 2:
            gathers[at - 2][0].arrived()
            project(at - 2)

    columns = my_gate_ref.shape[1]
    gathered = GroupGather(
        lambda shard: full_out_ref.at[pl.ds(shard * own, own)], out_sends, out_arrivals
    )
    gathered.start(out_ref)
    gathered_g = GroupGather(lambda shard: all_g_ref.at[shard], g_sends, g_arrivals)
    gathered_g.start(g_ref)
    own_g = pltpu.make_async_copy(g_ref, all_g_ref.at[fsdp], local_sems.at[3])
    own_g.start()
    background = [own_g]
    own_out = pltpu.make_async_copy(out_ref, full_out_ref.at[own_rows], local_sems.at[2])
    own_out.start()
    background.append(own_out)
    for which, (source, target) in enumerate(((gate_ref, my_gate_ref), (up_ref, my_up_ref))):
        for step in range(1, group):
            peer = lax.rem(fsdp + step, group)
            copy = pltpu.make_async_remote_copy(
                src_ref=source.at[:, pl.ds(pl.multiple_of(peer * columns, LANES), columns)],
                dst_ref=target.at[own_rows],
                send_sem=part_sends.at[which, step - 1],
                recv_sem=part_arrivals.at[which, step - 1],
                device_id=(peer, ctx),
                device_id_type=MESH,
            )
            copy.start()
            background.append(copy)
        own_part = pltpu.make_async_copy(
            source.at[:, pl.ds(pl.multiple_of(fsdp * columns, LANES), columns)],
            target.at[own_rows],
            local_sems.at[which],
        )
        own_part.start()
        background.append(own_part)

    def add(unit, kv):
        scores = jnp.dot(kv, q_ref[unit], preferred_element_type=jnp.float32)
        top = top_ref[unit]
        new_top = jnp.maximum(top, jnp.max(scores, axis=0, keepdims=True))
        fade = jnp.exp(top - new_top)
        weights = jnp.exp(scores - new_top)
        top_ref[unit] = new_top
        total_ref[unit] = total_ref[unit] * fade + jnp.sum(weights, axis=0, keepdims=True)
        added = jnp.dot(kv.T, weights.astype(jnp.bfloat16), preferred_element_type=jnp.float32)
        mix_ref[unit] = mix_ref[unit] * fade + added[HD:]

    def over_units(body, first, count):
        def two(at, unused):
            body(first + 2 * at)
            body(first + 2 * at + 1)
            return unused

        lax.fori_loop(0, count // 2, two, 0)

    def diagonal(unit):
        kv = all_ref[ctx, unit]
        scores = jnp.dot(kv, q_ref[unit], preferred_element_type=jnp.float32)
        scores = jnp.where(causal(keys, wide, scores.shape), scores, MASKED_SCORE)
        top = jnp.max(scores, axis=0, keepdims=True)
        weights = jnp.exp(scores - top)
        top_ref[unit] = top
        total_ref[unit] = jnp.sum(weights, axis=0, keepdims=True)
        added = jnp.dot(kv.T, weights.astype(jnp.bfloat16), preferred_element_type=jnp.float32)
        mix_ref[unit] = added[HD:]

    over_units(diagonal, 0, units)

    @pl.when(steps.side == 1)
    def _():
        for part in range(PARTS):
            across(0, part).wait_recv()
            over_units(lambda unit: add(unit, all_ref[ctx - 1, unit]), part * per_part, per_part)

    def level_step(level, unused):
        for part in range(PARTS):
            chain(level - 1, part).wait_recv()
            pass_on(level, part)
            across(level, part).start()
        first = 2 * (steps.level - level)
        for part in range(PARTS):
            across(level, part).wait_recv()
            over_units(
                lambda unit: add(unit, all_ref[pl.ds(first, 2), unit].reshape(2 * keys, deep)),
                part * per_part,
                per_part,
            )
        return unused

    lax.fori_loop(1, steps.level + 1, level_step, 0)

    def close(unit):
        total = total_ref[unit]
        mix_ref[unit] = mix_ref[unit] / total
        log_ref[unit] = top_ref[unit] + jnp.log(total)

    over_units(close, 0, units)
    for sequence in range(sequences):
        for pair in range(H // 2):
            heads = []
            for head in (2 * pair, 2 * pair + 1):
                unit, member = sequence * KVH + head // groups, head % groups
                heads.append(mix_ref[unit, :, member * keys : (member + 1) * keys])
            tile = jnp.concatenate(heads, axis=0).astype(low_ref.dtype)
            block = slice(sequence * keys, (sequence + 1) * keys)
            columns = slice(pair * 2 * HD, (pair + 1) * 2 * HD)
            low_t_ref[columns, block] = tile
            low_ref[block, columns] = tile.T
    for gather, _ in gathers:
        gather.sent()
    for step in range(1, group):
        gain_copy(step).wait_send()
    gathered.finish()
    gathered_g.finish()
    for copy in background:
        copy.wait()

    def sent(level, unused):
        for part in range(PARTS):

            @pl.when(steps.has_above)
            def _():
                chain(level, part).wait_send()

            @pl.when(jnp.logical_or(level > 0, steps.side == 0))
            def _():
                across(level, part).wait_send()

        return unused

    lax.fori_loop(0, steps.level + 1, sent, 0)


ANY = pl.BlockSpec(memory_space=pl.ANY)
VMEM = pl.BlockSpec(memory_space=pltpu.VMEM)


def attend(x, gains, cosine, sine, w_query, w_key, w_value, w_out, w_gate, w_up, g_rows, sequences):
    group, count = lax.axis_size("fsdp"), lax.axis_size("ctx")
    rows, width = x.shape
    own, hidden = w_query.shape[0], w_gate.shape[1] // group
    keys, units, deep = rows // sequences, sequences * KVH, 2 * HD
    wide = H // KVH * keys
    kv_width = KVH * HD
    dma = pltpu.SemaphoreType.DMA
    bf16, f32 = jnp.bfloat16, jnp.float32
    pieces = 2 + width // kv_width
    return pl.pallas_call(
        attend_kernel,
        out_shape=[
            jax.ShapeDtypeStruct((units, deep, wide), bf16),
            jax.ShapeDtypeStruct((width, rows), bf16),
            jax.ShapeDtypeStruct((gains.shape[0], width), f32),
            jax.ShapeDtypeStruct((width, width), bf16),
            jax.ShapeDtypeStruct((width, kv_width), bf16),
            jax.ShapeDtypeStruct((width, kv_width), bf16),
            jax.ShapeDtypeStruct((rows, width), bf16),
            jax.ShapeDtypeStruct((width, rows), bf16),
            jax.ShapeDtypeStruct((units, HD, wide), f32),
            jax.ShapeDtypeStruct((units, 1, wide), f32),
            jax.ShapeDtypeStruct((count, units, keys, deep), bf16),
            jax.ShapeDtypeStruct((width, width), bf16),
            jax.ShapeDtypeStruct((width, hidden), bf16),
            jax.ShapeDtypeStruct((width, hidden), bf16),
            jax.ShapeDtypeStruct((group, rows, width), bf16),
        ],
        in_specs=[VMEM] * 4 + [ANY] * 7,
        out_specs=[VMEM] * 11 + [ANY] * 4,
        scratch_shapes=[
            pltpu.VMEM((rows, width), bf16),
            pltpu.VMEM((rows, kv_width), f32),
            pltpu.VMEM((group,) + gains.shape, f32),
            pltpu.VMEM((units, 1, wide), f32),
            pltpu.VMEM((units, 1, wide), f32),
            dma((count // 2, PARTS)),
            dma((count // 2 + 1, PARTS)),
            dma((count // 2, PARTS)),
            dma((count // 2, PARTS)),
            half_semaphores(pieces),
            half_semaphores(pieces),
            *[dma((group - 1,))] * 2,
            *[group_semaphores()] * 4,
            dma((2, group - 1)),
            dma((2, group - 1)),
            dma((7,)),
        ],
        compiler_params=pltpu.CompilerParams(
            collective_id=1, has_side_effects=True, vmem_limit_bytes=60 << 20
        ),
    )(x, gains, cosine, sine, w_query, w_key, w_value, w_out, w_gate, w_up, g_rows)


class Ring:
    def __init__(self, work, landing, total, semaphores, forward, exchange=False):
        self.fsdp, self.ctx = lax.axis_index("fsdp"), lax.axis_index("ctx")
        self.group, self.count = lax.axis_size("fsdp"), lax.axis_size("ctx")
        self.work, self.landing, self.total = work, landing, total
        self.sends, self.arrivals = semaphores[:2]
        self.part_sends, self.part_arrivals, self.own_sem = semaphores[2:] if exchange else (None,) * 3
        self.exchange = exchange
        side = 0 if forward else 1
        self.place = ring_place(self.ctx, side, self.count)
        self.after = (self.fsdp, ring_ctx(lax.rem(self.place + 1, self.count), side, self.count))
        self.ticks = 2 * self.count - 2 + int(exchange)

    def chunk(self, held, index):
        if self.exchange:
            return held.at[index]
        per = held.shape[0] // self.count
        return held.at[pl.ds(index * per, per)]

    def summing(self, step, index):
        return self.copy(self.chunk(self.work, index), self.landing.at[step], step)

    def handing(self, step, index):
        held = self.chunk(self.total, index)
        return self.copy(held, held, step)

    def copy(self, source, target, step):
        return pltpu.make_async_remote_copy(
            src_ref=source,
            dst_ref=target,
            send_sem=self.sends.at[step],
            recv_sem=self.arrivals.at[step],
            device_id=self.after,
            device_id_type=MESH,
        )

    def part(self, index, step):
        peer = lax.rem(self.fsdp + step, self.group)
        return pltpu.make_async_remote_copy(
            src_ref=self.work.at[index, peer],
            dst_ref=self.total.at[index, self.fsdp],
            send_sem=self.part_sends.at[step - 1],
            recv_sem=self.part_arrivals.at[step - 1],
            device_id=(peer, self.ctx),
            device_id_type=MESH,
        )

    def own_part(self, index):
        return pltpu.make_async_copy(
            self.work.at[index, self.fsdp], self.total.at[index, self.fsdp], self.own_sem
        )

    def start(self):
        self.summing(0, self.place).start()

    def tick(self, at):
        last = self.count - 2
        gap = int(self.exchange)
        step = at - gap * jnp.where(at > last, 1, 0) if self.exchange else at
        index = lax.rem(self.place + 3 * self.count - 1 - step, self.count)

        def add(target):
            part, landed = self.chunk(self.work, index), self.landing.at[jnp.minimum(at, last)]
            for row in range(part.shape[0]):
                target[row] = (
                    part[row].astype(jnp.float32) + landed[row].astype(jnp.float32)
                ).astype(part.dtype)

        @pl.when(at <= last)
        def _():
            self.summing(jnp.minimum(at, last), index).wait_recv()

        @pl.when(at < last)
        def _():
            add(self.chunk(self.work, index))
            self.summing(jnp.minimum(at + 1, last), index).start()

        if self.exchange:

            @pl.when(at == last)
            def _():
                add(self.chunk(self.work, index))
                for peer in range(1, self.group):
                    self.part(index, peer).start()
                self.own_part(index).start()

            @pl.when(at == last + 1)
            def _():
                done = lax.rem(self.place + 1, self.count)
                self.own_part(done).wait()
                for peer in range(1, self.group):
                    self.part(done, peer).wait_recv()
                self.handing(last + 1, done).start()

        else:

            @pl.when(at == last)
            def _():
                add(self.chunk(self.total, index))
                self.handing(last + 1, index).start()

        @pl.when(at > last + gap)
        def _():
            here = jnp.maximum(step, last + 1)
            self.handing(here, index).wait_recv()

            @pl.when(here < 2 * self.count - 3)
            def _():
                self.handing(jnp.minimum(here + 1, 2 * self.count - 3), index).start()

    def finish(self):
        def wait(step, unused):
            self.handing(step, self.place).wait_send()
            return unused

        lax.fori_loop(0, 2 * self.count - 2, wait, 0)
        if self.exchange:
            for peer in range(1, self.group):
                self.part(lax.rem(self.place + 1, self.count), peer).wait_send()


class SumRing(Ring):
    def __init__(self, *args):
        super().__init__(*args)
        self.ticks = self.count - 1

    def tick(self, at):
        last = self.count - 2
        index = lax.rem(self.place + 2 * self.count - 1 - at, self.count)
        self.summing(at, index).wait_recv()
        work, landed = self.chunk(self.work, index), self.landing.at[at]

        def add(target):
            for row in range(work.shape[0]):
                target[row] = (
                    work[row].astype(jnp.float32) + landed[row].astype(jnp.float32)
                ).astype(work.dtype)

        @pl.when(at < last)
        def _():
            add(work)
            self.summing(jnp.minimum(at + 1, last), index).start()

        @pl.when(at == last)
        def _():
            add(self.total)

    def finish(self):
        def wait(step, unused):
            self.summing(step, self.place).wait_send()
            return unused

        lax.fori_loop(0, self.ticks, wait, 0)


class SpreadRing(Ring):
    def __init__(self, total, semaphores, forward):
        super().__init__(None, None, total, semaphores, forward)
        self.ticks = self.count - 1
        self.first = lax.rem(self.place + 1, self.count)

    def start(self):
        self.handing(0, self.first).start()

    def tick(self, at):
        index = lax.rem(self.place + self.count - at, self.count)
        self.handing(at, index).wait_recv()

        @pl.when(at < self.count - 2)
        def _():
            self.handing(jnp.minimum(at + 1, self.count - 2), index).start()

    def finish(self):
        def wait(step, unused):
            self.handing(step, self.place).wait_send()
            return unused

        lax.fori_loop(0, self.ticks, wait, 0)


def ring_scratch(chunk, exchange=False):
    count = lax.axis_size("ctx")
    work = (count,) + chunk if exchange else (count * chunk[0],) + chunk[1:]
    return [pltpu.VMEM(work, jnp.bfloat16), pltpu.VMEM((count - 1,) + chunk, jnp.bfloat16)]


def ring_total(chunk, exchange=False):
    count = lax.axis_size("ctx")
    work = (count,) + chunk if exchange else (count * chunk[0],) + chunk[1:]
    return jax.ShapeDtypeStruct(work, jnp.bfloat16)


def ring_semaphores(exchange=False):
    dma, steps = pltpu.SemaphoreType.DMA, 2 * lax.axis_size("ctx") - 2
    parts = lax.axis_size("fsdp") - 1
    return [dma((steps,))] * 2 + ([dma((parts,))] * 2 + [dma] if exchange else [])


def wide_split(width):
    group, count = lax.axis_size("fsdp"), lax.axis_size("ctx")
    return 2 if FF // group // LANES * (width // group // 16) >= 4 * count else 1


def query_split(width):
    return width // LANES * 7 // 9 * LANES


def out_split(width):
    return (width // LANES + 1) // 2 * LANES


def down_split(blocks, count):
    each = -(-blocks // count)
    rings = 4 if each >= 4 else 2
    return [max(1, (each + at) // rings) for at in range(rings)]


class GroupScatter:
    def __init__(self, give_sib, got_sib, give_cross, got_cross, far, got_far, sends, arrivals):
        self.give_sib, self.got_sib = give_sib, got_sib
        self.give_cross, self.got_cross = give_cross, got_cross
        self.far, self.got_far = far, got_far
        self.sends, self.arrivals = sends, arrivals
        self.fsdp, self.ctx = lax.axis_index("fsdp"), lax.axis_index("ctx")
        self.chips = lax.axis_size("fsdp") // 2
        self.chip, self.core = lax.div(self.fsdp, 2), lax.rem(self.fsdp, 2)
        self.sibling = 2 * self.chip + 1 - self.core

    def copy(self, source, target, semaphore, device):
        return pltpu.make_async_remote_copy(
            src_ref=source,
            dst_ref=target,
            send_sem=self.sends.at[semaphore],
            recv_sem=self.arrivals.at[semaphore],
            device_id=(device, self.ctx),
            device_id_type=MESH,
        )

    def to_sibling(self):
        return self.copy(self.give_sib, self.got_sib, 0, self.sibling)

    def to_cross(self, step):
        return self.copy(
            self.give_cross(step), self.got_cross.at[step - 1], step, self.sibling
        )

    def to_far(self, step):
        chip = lax.rem(self.chip + self.chips - step, self.chips)
        return self.copy(
            self.far.at[step - 1],
            self.got_far.at[step - 1],
            self.chips - 1 + step,
            2 * chip + self.core,
        )

    def add_cross(self, step):
        self.to_cross(step).wait_recv()
        held = self.far.at[step - 1]
        held[...] = (
            held[...].astype(jnp.float32) + self.got_cross[step - 1].astype(jnp.float32)
        ).astype(held.dtype)
        self.to_far(step).start()

    def total(self, own):
        self.to_sibling().wait_recv()
        value = own + self.got_sib[...].astype(jnp.float32)
        for step in range(1, self.chips):
            self.to_far(step).wait_recv()
            value = value + self.got_far[step - 1].astype(jnp.float32)
        return value

    def sent(self):
        self.to_sibling().wait_send()
        for step in range(1, self.chips):
            self.to_cross(step).wait_send()
            self.to_far(step).wait_send()


def scatter_scratch(rows, width):
    far = lax.axis_size("fsdp") // 2 - 1
    one, many = (rows, width), (far, rows, width)
    return [pltpu.VMEM(shape, jnp.bfloat16) for shape in (one, one, many, many, many, many)]


def dot_columns(left, right):
    return lax.dot_general(
        left, right, (((1,), (1,)), ((), ())), preferred_element_type=jnp.float32
    )


def tiles(count, body):
    def step(at, unused):
        body(at)
        return unused

    lax.fori_loop(0, count, step, 0)


def lane_tile(at, size):
    return pl.ds(pl.multiple_of(at * size, LANES), size)


def width_tile(width):
    return 384 if width % 384 == 0 else width


def hidden_tile(hidden):
    return 256 if hidden % 256 == 0 else 128


def transpose_into(target, source):
    rows, columns = source.shape

    def body(at):
        part = source[:, lane_tile(at, LANES)]
        target[pl.ds(pl.multiple_of(at * LANES, LANES), LANES), :] = part.T

    tiles(columns // LANES, body)


def ffn_kernel(
    x_ref, low_ref, out_ref, gate_ref, up_ref, down_ref, all_g_ref, gain_ref,
    layer_ref, layer_part_ref, resid_grad_ref, branch_ref, g_wide_ref, gate_part_ref, up_part_ref,
    *rest,
):
    downs = len(down_split(gate_ref.shape[1] // 16, lax.axis_size("ctx")))
    taken = iter(rest)

    def take(number):
        return [next(taken) for _ in range(number)]

    down_done, (gain_grad_ref,) = take(downs), take(1)
    all_n_ref, turned_n, turned_act, act_ref, gate_grad, up_grad, resid_ref, grad_own = take(8)
    down_scratch = take(2 * downs)
    give_sib, got_sib, give_cross, got_cross, far, got_far = take(6)
    n_sends, n_arrivals, grad_sends, grad_arrivals = take(4)
    rings = [
        SumRing(*down_scratch[2 * at : 2 * at + 2], down_done[at], take(2), at % 2 == 0)
        for at in range(downs)
    ]
    group = lax.axis_size("fsdp")
    rows, width = x_ref.shape
    hidden = gate_ref.shape[1]
    barrier = pltpu.get_barrier_semaphore()
    greeted = greet_group(barrier) + 2
    for ring in rings[:2]:
        pl.semaphore_signal(barrier, inc=1, device_id=ring.after, device_id_type=MESH)
    step_in, step_out = hidden_tile(hidden), width_tile(width)

    def branch(at):
        columns = lane_tile(at, step_out)
        resid_ref[:, columns] = x_ref[:, columns].astype(jnp.float32) + forward_dot(
            low_ref[...], out_ref[:, columns]
        )

    tiles(width // step_out, branch)
    gain = gain_ref[...]
    scale = norm_scale(resid_ref[...])
    gathered = GroupGather(lambda shard: all_n_ref.at[shard], n_sends, n_arrivals)
    fsdp, chips = gathered.fsdp, gathered.chips
    all_n_ref[fsdp] = (resid_ref[...] * scale * gain).astype(jnp.bfloat16)
    pl.semaphore_wait(barrier, greeted)
    gathered.start(all_n_ref.at[fsdp])
    grad_sum = GroupScatter(
        give_sib,
        got_sib,
        lambda step: give_cross.at[step - 1],
        got_cross,
        far,
        got_far,
        grad_sends,
        grad_arrivals,
    )

    def hidden_part(shard):
        def body(at):
            columns = lane_tile(at, step_in)
            normed = all_n_ref[shard]
            gate = forward_dot(normed, gate_ref[:, columns])
            upward = forward_dot(normed, up_ref[:, columns])
            grad_act = dot_columns(
                all_g_ref[shard], down_ref[pl.ds(pl.multiple_of(at * step_in, LANES), step_in), :]
            )
            sigmoid = jax.nn.sigmoid(gate)
            silu = gate * sigmoid
            act_ref[shard, :, columns] = (silu * upward).astype(jnp.bfloat16)
            gate_grad[shard, :, columns] = (
                grad_act * upward * (sigmoid * (1.0 + gate * (1.0 - sigmoid)))
            ).astype(jnp.bfloat16)
            up_grad[shard, :, columns] = (grad_act * silu).astype(jnp.bfloat16)

        tiles(hidden // step_in, body)

    def grad_part(shard, target):
        def body(at):
            columns = pl.ds(pl.multiple_of(at * step_out, LANES), step_out)
            target[:, columns] = (
                dot_columns(gate_grad[shard], gate_ref[columns, :])
                + dot_columns(up_grad[shard], up_ref[columns, :])
            ).astype(target.dtype)

        tiles(width // step_out, body)

    hidden_part(fsdp)
    gathered.sibling_here()
    sibling = gathered.sibling
    hidden_part(sibling)
    grad_part(sibling, grad_sum.give_sib)
    grad_sum.to_sibling().start()
    gathered.forward()
    grad_part(fsdp, grad_own)
    def turn_act(shard):
        transpose_into(turned_act.at[:, lane_tile(shard, rows)], act_ref.at[shard])

    turn_act(fsdp)
    turn_act(sibling)
    for step in range(1, chips):
        ours = gathered.same_core(chips - step)
        theirs = ours + sibling - fsdp
        gathered.crossed(step)
        hidden_part(theirs)
        grad_part(theirs, give_cross.at[step - 1])
        grad_sum.to_cross(step).start()
        hidden_part(ours)
        grad_part(ours, far.at[step - 1])
        grad_sum.add_cross(step)
        turn_act(theirs)
        turn_act(ours)
    blocks = hidden // 16
    spans, first = [], 0
    for ring in rings:
        last = min(blocks, first + ring.work.shape[0])
        spans.append((first, last, ring.work))
        first = last

    def down_tile(at):
        columns = lane_tile(at, step_out)
        part = forward_dot(
            turned_act[...], all_g_ref[:, :, columns].reshape(group * rows, step_out)
        ).astype(jnp.bfloat16)
        for begin, end, work in spans:
            if end > begin:
                work[: end - begin, :, columns] = part[begin * 16 : end * 16].reshape(
                    end - begin, 16, step_out
                )

    tiles(width // step_out, down_tile)
    for begin, end, work in spans:
        for spare in range(end - begin, work.shape[0]):
            work[spare] = jnp.zeros(work.shape[1:], work.dtype)
    for ring in rings:
        ring.start()
    ticked = [0]

    def ring_tick(at):
        for ring in rings:

            @pl.when(at < ring.ticks)
            def _():
                ring.tick(jnp.minimum(at, ring.ticks - 1))

    def ticking(times, body):
        begin = ticked[0]

        def step(at):
            body(at)
            ring_tick(begin + at)

        tiles(times, step)
        ticked[0] += times

    for shard in range(group):
        span = slice(shard * rows, (shard + 1) * rows)
        transpose_into(turned_n.at[:, span], all_n_ref.at[shard])
    own = width // group
    row_blocks = own // 16
    for source, target in ((gate_grad, gate_part_ref), (up_grad, up_part_ref)):

        def weight_tile(at):
            columns = lane_tile(at, step_in)
            part = forward_dot(
                turned_n[...], source[:, :, columns].reshape(group * rows, step_in)
            ).astype(jnp.bfloat16)
            for block in range(step_in // LANES):
                first = (at * (step_in // LANES) + block) * row_blocks
                for owner in range(group):
                    target[owner, pl.ds(first, row_blocks)] = part[
                        owner * own : (owner + 1) * own, block * LANES : (block + 1) * LANES
                    ].reshape(row_blocks, 16, LANES)

        ticking(hidden // step_in, weight_tile)
        filled = hidden // LANES * row_blocks
        for spare in range(filled, target.shape[1]):
            for owner in range(group):
                target[owner, spare] = jnp.zeros(target.shape[2:], target.dtype)

    def layer_tile(at):
        columns = lane_tile(at, step_out)
        part = forward_dot(
            act_ref[...].reshape(group * rows, hidden), down_ref[:, columns]
        ).reshape(group, rows, step_out)
        layer_part_ref[:, :, columns] = part.astype(jnp.bfloat16)

    ticking(width // step_out, layer_tile)
    layer_ref[...] = resid_ref[...] + layer_part_ref[fsdp].astype(jnp.float32)
    upstream = grad_sum.total(grad_own[...])
    resid = resid_ref[...]
    scaled = upstream * gain
    grad_resid = (
        all_g_ref[fsdp].astype(jnp.float32)
        + scale * scaled
        - resid * scale**3 * jnp.mean(scaled * resid, axis=-1, keepdims=True)
    )
    gain_grad_ref[...] = jnp.sum(upstream * resid * scale, axis=0, keepdims=True)
    resid_grad_ref[...] = grad_resid
    branch_ref[...] = grad_resid.astype(jnp.bfloat16)
    units, _, wide = g_wide_ref.shape
    sequences = units // KVH
    keys = rows // sequences
    groups = wide // keys
    g_wide_ref[:, :HD, :] = jnp.zeros((units, HD, wide), g_wide_ref.dtype)
    for pair in range(H // 2):
        columns = slice(pair * 2 * HD, (pair + 1) * 2 * HD)
        mixed = dot_columns(branch_ref[...], out_ref[columns, :]).astype(jnp.bfloat16)
        for sequence in range(sequences):
            turned = mixed[sequence * keys : (sequence + 1) * keys].T
            for half in range(2):
                head = 2 * pair + half
                unit, member = sequence * KVH + head // groups, head % groups
                g_wide_ref[unit, HD:, member * keys : (member + 1) * keys] = turned[
                    half * HD : (half + 1) * HD
                ]
    begin = ticked[0]
    tiles(max(0, rings[0].ticks - begin), lambda at: ring_tick(begin + at))
    gathered.sent()
    grad_sum.sent()
    for ring in rings:
        ring.finish()


def spread(blocks, count):
    return -(-blocks // count) * count


def feed_forward(x, low, full_out, my_gate, my_up, my_down, all_g, gain, units, wide):
    group, count = lax.axis_size("fsdp"), lax.axis_size("ctx")
    rows, width = x.shape
    hidden = my_gate.shape[1]
    blocks = spread(hidden // LANES * (width // group // 16), wide_split(width) * count)
    chips = group // 2
    dma = pltpu.SemaphoreType.DMA((2 * chips - 1,))
    bf16 = jnp.bfloat16
    down_chunks = [(per, 16, width) for per in down_split(hidden // 16, count)]
    return pl.pallas_call(
        ffn_kernel,
        out_shape=[
            jax.ShapeDtypeStruct((rows, width), jnp.float32),
            jax.ShapeDtypeStruct((group, rows, width), bf16),
            jax.ShapeDtypeStruct((rows, width), jnp.float32),
            jax.ShapeDtypeStruct((rows, width), bf16),
            jax.ShapeDtypeStruct((units, 2 * HD, wide), bf16),
            jax.ShapeDtypeStruct((group, blocks, 16, LANES), bf16),
            jax.ShapeDtypeStruct((group, blocks, 16, LANES), bf16),
            *[jax.ShapeDtypeStruct(chunk, bf16) for chunk in down_chunks],
            jax.ShapeDtypeStruct((1, width), jnp.float32),
        ],
        in_specs=[VMEM] * 8,
        out_specs=[VMEM] * (8 + len(down_chunks)),
        scratch_shapes=[
            pltpu.VMEM((group, rows, width), bf16),
            pltpu.VMEM((width, group * rows), bf16),
            pltpu.VMEM((hidden, group * rows), bf16),
            pltpu.VMEM((group, rows, hidden), bf16),
            pltpu.VMEM((group, rows, hidden), bf16),
            pltpu.VMEM((group, rows, hidden), bf16),
            pltpu.VMEM((rows, width), jnp.float32),
            pltpu.VMEM((rows, width), jnp.float32),
            *[kind for chunk in down_chunks for kind in ring_scratch(chunk)],
            *scatter_scratch(rows, width),
            *[dma] * 4,
            *[kind for _ in down_chunks for kind in ring_semaphores()],
        ],
        compiler_params=pltpu.CompilerParams(
            collective_id=2, has_side_effects=True, vmem_limit_bytes=60 << 20
        ),
    )(x, low, full_out, my_gate, my_up, my_down, all_g, gain)


def back_kernel(
    down_blocks, q_ref, g_ref, log_ref, gain_grad_ref, gain_ref, cos_ref, sin_ref,
    pairs_ref, mix_in, gate_ref, up_ref, layer_base_in, layer_part_ref, branch_ref, low_t_ref,
    normed_t_ref, w_query_in, w_key_in, w_value_in, x_in, resid_grad_in, *rest,
):
    taken = iter(rest)

    def take(number):
        return [next(taken) for _ in range(number)]

    halves, downs = wide_split(x_in.shape[1]), len(down_blocks)
    down_refs = take(downs)
    tokens_ref, layer_ref = take(2)
    wide_totals, down_totals = take(2 * halves), take(downs)
    out_a_total, out_b_total, rest_a_total, rest_b_total = take(4)
    peer_got, chain_got, layer_sib, layer_cross, layer_far = take(5)
    kv_ref, stage_ref, final_ref, qg_ref, delta_ref, grad_q_ref = take(6)
    wide_scratch = take(4 * halves)
    out_a_work, out_a_land, out_b_work, out_b_land = take(4)
    rest_a_work, rest_a_land, rest_b_work, rest_b_land = take(4)
    low_all, normed_all, branch_all, query_all, pair_all, upstream_ref, gain_give, gain_got = take(8)
    far_ref, layer_stage = take(2)
    mix_ref, layer_base_ref, w_query_ref, w_key_ref, w_value_ref, x_ref, resid_grad_ref = take(7)
    steps = Steps()
    fsdp, ctx, group, count = steps.fsdp, steps.ctx, lax.axis_size("fsdp"), lax.axis_size("ctx")
    units, deep, wide = q_ref.shape
    keys = pairs_ref.shape[2]
    rows, width = x_ref.shape
    own = width // group
    wide_rings = [
        Ring(*wide_scratch[2 * at : 2 * at + 2], wide_totals[at], take(5), at < halves, True)
        for at in range(2 * halves)
    ]
    down_rings = [SpreadRing(total, take(2), at % 2 == 0) for at, total in enumerate(down_totals)]
    out_a = Ring(out_a_work, out_a_land, out_a_total, take(2), True)
    out_b = Ring(out_b_work, out_b_land, out_b_total, take(2), False)
    layer_sum = GroupScatter(
        None,
        layer_sib,
        lambda step: layer_part_ref.at[
            2 * lax.rem(lax.div(fsdp, 2) + group // 2 - step, group // 2) + 1 - lax.rem(fsdp, 2)
        ],
        layer_cross,
        far_ref,
        layer_far,
        *take(2),
    )
    layer_sum.give_sib = layer_part_ref.at[layer_sum.sibling]
    rest_a = Ring(rest_a_work, rest_a_land, rest_a_total, take(2), True)
    rest_b = Ring(rest_b_work, rest_b_land, rest_b_total, take(2), False)
    first_rings = []
    for at in range(halves):
        first_rings += [wide_rings[at], wide_rings[halves + at]]
        first_rings += down_rings[at * downs // halves : (at + 1) * downs // halves]
    begun_rings = len(first_rings)
    first_rings += [out_a, out_b]
    peer_sends, peer_arrivals, chain_sends, chain_arrivals = take(4)
    branch_gather = GroupGather(lambda shard: branch_all.at[shard], *take(2))
    query_gather = GroupGather(lambda shard: query_all.at[shard], *take(2))
    pair_gather = GroupGather(lambda shard: pair_all.at[shard], *take(2))
    low_sends, low_arrivals, normed_sends, normed_arrivals, gain_sends, gain_arrivals = take(6)
    local_sems, stage_sems = take(2)

    barrier = pltpu.get_barrier_semaphore()
    greeted = steps.greet(barrier) + greet_group(barrier) + 2
    for device in (out_a.after, out_b.after):
        pl.semaphore_signal(barrier, inc=1, device_id=device, device_id_type=MESH)

    loads = []

    def load(source, target):
        copy = pltpu.make_async_copy(source, target, local_sems.at[len(loads)])
        copy.start()
        loads.append(copy)

    n = wide_scratch[0].shape[2]
    for at, ring in enumerate(wide_rings):
        source = (gate_ref, up_ref)[at // halves]
        for chunk in range(count):
            load(source.at[:, pl.ds((at % halves * count + chunk) * n, n)], ring.work.at[chunk])
    for ring, source in zip(down_rings, down_refs):
        load(source, ring.chunk(ring.total, ring.first))
    ring_loads = len(loads)
    load(pairs_ref, kv_ref)
    load(mix_in, mix_ref)
    load(branch_ref, branch_all.at[fsdp])
    load(low_t_ref.at[pl.ds(fsdp * own, own)], low_all.at[:, lane_tile(fsdp, rows)])
    load(normed_t_ref.at[pl.ds(fsdp * own, own)], normed_all.at[:, lane_tile(fsdp, rows)])
    slot_loads = len(loads)
    for source, target in (
        (layer_base_in, layer_base_ref),
        (w_query_in, w_query_ref),
        (w_key_in, w_key_ref),
        (w_value_in, w_value_ref),
        (x_in, x_ref),
        (resid_grad_in, resid_grad_ref),
    ):
        load(source, target)
    for copy in loads[:ring_loads]:
        copy.wait()
    pl.semaphore_wait(barrier, greeted)
    for ring in first_rings[:begun_rings]:
        ring.start()
    branch_gather.start(branch_ref)
    layer_sum.to_sibling().start()
    for step in range(1, group // 2):
        layer_sum.to_cross(step).start()

    def slices(source, target, sends, arrivals, step):
        peer = lax.rem(fsdp + step, group)
        return pltpu.make_async_remote_copy(
            src_ref=source.at[pl.ds(peer * own, own)],
            dst_ref=target.at[:, lane_tile(fsdp, rows)],
            send_sem=sends.at[step - 1],
            recv_sem=arrivals.at[step - 1],
            device_id=(peer, ctx),
            device_id_type=MESH,
        )

    turned = [
        slices(*ends, step)
        for ends in (
            (low_t_ref, low_all, low_sends, low_arrivals),
            (normed_t_ref, normed_all, normed_sends, normed_arrivals),
        )
        for step in range(1, group)
    ]
    for copy in turned:
        copy.start()

    def prepare(unit):
        q, g = q_ref[unit], g_ref[unit]
        qg_ref[unit, :wide] = q.T
        qg_ref[unit, wide:] = g.T
        delta_ref[unit] = jnp.sum(
            g[HD:].astype(jnp.float32) * mix_ref[unit], axis=0, keepdims=True
        )
        grad_q_ref[unit] = jnp.zeros((HD, wide), jnp.float32)

    for copy in loads[ring_loads:slot_loads]:
        copy.wait()
    tiles(units, prepare)

    def tick(ring, at):
        @pl.when(jnp.logical_and(at >= 0, at < ring.ticks))
        def _():
            ring.tick(jnp.clip(at, 0, ring.ticks - 1))

    late = steps.levels // 2 + 1

    def pump(at):
        lag = [0] * begun_rings + [late, late]
        for turn, ring in enumerate(first_rings):

            @pl.when(lax.rem(at, len(first_rings)) == turn)
            def _():
                tick(ring, lax.div(at, len(first_rings)) - lag[turn])

    def back(unit, first, blocks, diagonal):
        kv = kv_ref[pl.ds(first, blocks), unit].reshape(blocks * keys, deep)
        scores = jnp.dot(kv, q_ref[unit], preferred_element_type=jnp.float32)
        probs = jnp.exp(scores - log_ref[unit])
        if diagonal:
            probs = jnp.where(causal(keys, wide, scores.shape), probs, 0.0)
        grad_probs = jnp.dot(kv, g_ref[unit], preferred_element_type=jnp.float32)
        grad_scores = (probs * (grad_probs - delta_ref[unit])).astype(jnp.bfloat16)
        both = jnp.concatenate([grad_scores, probs.astype(jnp.bfloat16)], axis=1)
        grad_kv = jnp.dot(both, qg_ref[unit], preferred_element_type=jnp.float32)
        added = jnp.dot(kv.T, grad_scores, preferred_element_type=jnp.float32)
        grad_q_ref[unit] = grad_q_ref[unit] + added[:HD]
        kv_ref[pl.ds(first, blocks), unit] = grad_kv.astype(kv_ref.dtype).reshape(
            blocks, keys, deep
        )

    def across(pair):
        return pltpu.make_async_remote_copy(
            src_ref=kv_ref.at[2 * pair + 1 - steps.side],
            dst_ref=peer_got.at[pair],
            send_sem=peer_sends.at[pair],
            recv_sem=peer_arrivals.at[pair],
            device_id=steps.peer,
            device_id_type=MESH,
        )

    def down_chain(pair):
        return pltpu.make_async_remote_copy(
            src_ref=kv_ref.at[2 * pair + steps.side],
            dst_ref=chain_got.at[pair],
            send_sem=chain_sends.at[pair],
            recv_sem=chain_arrivals.at[pair],
            device_id=steps.below,
            device_id_type=MESH,
        )

    def combine(time):
        pair = time - steps.levels + steps.level

        @pl.when(jnp.logical_and(pair >= 0, pair <= steps.level))
        def _():
            for slot, expected, arrival, source in (
                (0, jnp.logical_or(pair < steps.level, steps.side == 0), across, peer_got),
                (1, steps.has_above, down_chain, chain_got),
            ):

                @pl.when(expected)
                def _():
                    arrival(pair).wait_recv()
                    copy = pltpu.make_async_copy(
                        source.at[pair], stage_ref.at[slot], stage_sems.at[slot]
                    )
                    copy.start()
                    copy.wait()

                @pl.when(jnp.logical_not(expected))
                def _():
                    stage_ref[slot] = jnp.zeros(stage_ref.shape[1:], stage_ref.dtype)

            def add(unit):
                final_ref[unit] = (
                    kv_ref[2 * pair + steps.side, unit].astype(jnp.float32)
                    + stage_ref[0, unit].astype(jnp.float32)
                    + stage_ref[1, unit].astype(jnp.float32)
                )

            tiles(units, add)

            @pl.when(pair < steps.level)
            def _():
                kv_ref[2 * pair + steps.side] = final_ref[...].astype(kv_ref.dtype)
                down_chain(pair).start()

    row_blocks = own // 16

    def weight_grad(left, right, begin, end, target, first, loop):
        span = LANES * next(n for n in (3, 2, 1) if (end - begin) % (n * LANES) == 0)

        def body(at):
            columns = pl.ds(pl.multiple_of(begin + at * span, LANES), span)
            part = forward_dot(
                left[...], right[:, :, columns].reshape(group * rows, span)
            ).astype(jnp.bfloat16)
            for block in range(span // LANES):
                here = first + (at * (span // LANES) + block) * row_blocks
                target[pl.ds(here, row_blocks)] = part[
                    :, block * LANES : (block + 1) * LANES
                ].reshape(row_blocks, 16, LANES)

        loop((end - begin) // span, body)
        return first + (end - begin) // LANES * row_blocks

    def clear_from(target, first):
        for spare in range(first, target.shape[0]):
            target[spare] = jnp.zeros((16, LANES), jnp.bfloat16)

    def out_grad():
        for copy in turned[: group - 1]:
            copy.wait_recv()
        branch_gather.forward()
        branch_gather.sibling_here()
        for step in range(1, branch_gather.chips):
            branch_gather.crossed(step)
        split = out_split(width)
        clear_from(out_a_work, weight_grad(low_all, branch_all, 0, split, out_a_work, 0, tiles))
        clear_from(out_b_work, weight_grad(low_all, branch_all, split, width, out_b_work, 0, tiles))
        out_a.start()
        out_b.start()

    turns = units // 2
    rings = max(turns, len(first_rings))

    def slot(pair):
        def turn(at):
            @pl.when(pair < steps.level)
            def _():
                for unit in (2 * at, 2 * at + 1):
                    back(unit, 2 * pair, 2, False)

            @pl.when(pair == steps.level)
            def _():
                for unit in (2 * at, 2 * at + 1):
                    back(unit, ctx, 1, True)

            @pl.when(jnp.logical_and(pair == steps.level, steps.side == 1))
            def _():
                for unit in (2 * at, 2 * at + 1):
                    back(unit, ctx - 1, 1, False)

            pump(pair * rings + at)

        tiles(turns, turn)
        tiles(rings - turns, lambda at: pump(pair * rings + turns + at))

        @pl.when(jnp.logical_or(pair < steps.level, (pair == steps.level) & (steps.side == 1)))
        def _():
            across(pair).start()

        combine(pair)

        @pl.when(pair == late - 1)
        def _():
            out_grad()

    tiles(steps.levels, slot)
    pumped = [steps.levels * rings]

    def pump_next(times=1):
        def body(at, unused, begin=pumped[0]):
            pump(begin + at)
            return unused

        lax.fori_loop(0, times, body, 0)
        pumped[0] += times

    def pumping(times, body):
        begin = pumped[0]

        def step(at):
            body(at)
            pump(begin + at)

        tiles(times, step)
        pumped[0] += times

    cosine, sine = cos_ref[...], sin_ref[...]

    def unturn(columns):
        first, second = columns[: HD // 2], columns[HD // 2 :]
        return jnp.concatenate(
            [first * cosine + second * sine, second * cosine - first * sine], axis=0
        )

    sequences = units // KVH
    groups = wide // keys
    for sequence in range(sequences):
        span = slice(sequence * keys, (sequence + 1) * keys)
        for pair in range(H // 2):
            heads = []
            for head in (2 * pair, 2 * pair + 1):
                unit, member = sequence * KVH + head // groups, head % groups
                part = grad_q_ref[unit, :, member * keys : (member + 1) * keys]
                heads.append(unturn(part * HD ** (-0.5)))
            query_all[fsdp, span, pair * 2 * HD : (pair + 1) * 2 * HD] = (
                jnp.concatenate(heads, axis=0).astype(jnp.bfloat16).T
            )
            if pair % 3 == 2:
                pump_next()
    query_gather.start(query_all.at[fsdp])
    combine(steps.levels)
    kv_width = KVH * HD
    for sequence in range(sequences):
        span = slice(sequence * keys, (sequence + 1) * keys)
        for pair in range(KVH // 2):
            turned_keys, turned_values = [], []
            for unit in (sequence * KVH + 2 * pair, sequence * KVH + 2 * pair + 1):
                part = final_ref[unit].T
                turned_keys.append(unturn(part[:HD]))
                turned_values.append(part[HD:])
            for start, parts in ((0, turned_keys), (kv_width, turned_values)):
                pair_all[fsdp, span, start + pair * 2 * HD : start + (pair + 1) * 2 * HD] = (
                    jnp.concatenate(parts, axis=0).astype(jnp.bfloat16).T
                )
    pair_gather.start(pair_all.at[fsdp])
    pump_next(2)
    query_gather.forward()
    for step in range(1, layer_sum.chips):
        ours = layer_part_ref.at[2 * lax.rem(layer_sum.chip + layer_sum.chips - step, layer_sum.chips) + layer_sum.core]
        for source, target in ((ours, far_ref.at[step - 1]), (layer_cross.at[step - 1], layer_stage)):
            if source is not ours:
                layer_sum.to_cross(step).wait_recv()
            copy = pltpu.make_async_copy(source, target, stage_sems.at[0])
            copy.start()
            copy.wait()
        far_ref[step - 1] = (
            far_ref[step - 1].astype(jnp.float32) + layer_stage[...].astype(jnp.float32)
        ).astype(jnp.bfloat16)
        layer_sum.to_far(step).start()

    step_out = width_tile(width)

    def upstream_tile(at):
        columns = pl.ds(pl.multiple_of(at * step_out, LANES), step_out)
        upstream_ref[:, columns] = (
            dot_columns(query_all[fsdp], w_query_ref[columns, :])
            + dot_columns(pair_all[fsdp, :, :kv_width], w_key_ref[columns, :])
            + dot_columns(pair_all[fsdp, :, kv_width:], w_value_ref[columns, :])
        )

    for copy in loads[slot_loads:]:
        copy.wait()
    pumping(width // step_out, upstream_tile)
    inputs = x_ref[...].astype(jnp.float32)
    scale = norm_scale(inputs)
    upstream = upstream_ref[...]
    scaled = upstream * gain_ref[...]
    tokens_ref[...] = (
        resid_grad_ref[...]
        + scale * scaled
        - inputs * scale**3 * jnp.mean(scaled * inputs, axis=-1, keepdims=True)
    )
    gain_attn = jnp.sum(upstream * inputs * scale, axis=0, keepdims=True)
    lanes = width // LANES
    gain_give[...] = jnp.zeros(gain_give.shape, jnp.float32)
    for block in range(lanes):
        columns = slice(block * LANES, (block + 1) * LANES)
        gain_give[block : block + 1, :] = gain_attn[:, columns]
        gain_give[lanes + block : lanes + block + 1, :] = gain_grad_ref[:, columns]

    def gain_copy(step):
        peer = lax.rem(fsdp + step, group)
        return pltpu.make_async_remote_copy(
            src_ref=gain_give,
            dst_ref=gain_got.at[step - 1],
            send_sem=gain_sends.at[step - 1],
            recv_sem=gain_arrivals.at[step - 1],
            device_id=(peer, ctx),
            device_id_type=MESH,
        )

    for step in range(1, group):
        gain_copy(step).start()
    pump_next()
    for copy in turned[group - 1 :]:
        copy.wait_recv()
    query_gather.sibling_here()
    for step in range(1, query_gather.chips):
        query_gather.crossed(step)
    split = query_split(width)
    filled_a = weight_grad(normed_all, query_all, 0, split, rest_a_work, 0, pumping)
    filled_b = weight_grad(normed_all, query_all, split, width, rest_b_work, 0, pumping)
    pair_gather.forward()
    pump_next()
    pair_gather.sibling_here()
    for step in range(1, pair_gather.chips):
        pair_gather.crossed(step)
    filled_b = weight_grad(normed_all, pair_all, 0, 2 * kv_width, rest_b_work, filled_b, pumping)
    gains = gain_give[...]
    for step in range(1, group):
        gain_copy(step).wait_recv()
        gains = gains + gain_got[step - 1]
    gain_tiles = gains.shape[0] // 16
    rest_a_work[filled_a : filled_a + gain_tiles] = gains.astype(jnp.bfloat16).reshape(
        gain_tiles, 16, LANES
    )
    clear_from(rest_a_work, filled_a + gain_tiles)
    clear_from(rest_b_work, filled_b)
    rest_a.start()
    rest_b.start()
    begun = pumped[0]
    total_pumps = max(wide_rings[0].ticks, late + out_a.ticks) * len(first_rings)

    half = -(-(total_pumps - begun) // rest_a.ticks)

    def last_ticks(at, unused):
        for turn in range(half):
            pump(jnp.minimum(begun + half * at + turn, total_pumps))
        tick(rest_a, at)
        tick(rest_b, at)
        return unused

    lax.fori_loop(0, rest_a.ticks, last_ticks, 0)
    layer_sum.to_sibling().wait_recv()
    layer = layer_base_ref[...]
    arrived = [layer_sib]
    for step in range(1, layer_sum.chips):
        layer_sum.to_far(step).wait_recv()
        arrived.append(layer_far.at[step - 1])
    for source in arrived:
        copy = pltpu.make_async_copy(source, layer_stage, stage_sems.at[0])
        copy.start()
        copy.wait()
        layer = layer + layer_stage[...].astype(jnp.float32)
    layer_ref[...] = layer.astype(jnp.bfloat16)
    layer_sum.sent()
    for ring in first_rings + [rest_a, rest_b]:
        ring.finish()
    for copy in turned:
        copy.wait_send()
    for gather in (branch_gather, query_gather, pair_gather):
        gather.sent()
    for step in range(1, group):
        gain_copy(step).wait_send()

    def sent(pair):
        @pl.when(jnp.logical_or(pair < steps.level, steps.side == 1))
        def _():
            across(pair).wait_send()

        @pl.when(pair < steps.level)
        def _():
            down_chain(pair).wait_send()

    tiles(steps.level + 1, sent)


def layer_back(
    q_wide, g_wide, log_total, gain_grad, gain, cosine, sine, all_pairs, mix, gate_part, up_part,
    layer_base, layer_parts, branch, low_t, normed_t, w_query, w_key, w_value, x, resid_grad, downs,
):
    group, count = lax.axis_size("fsdp"), lax.axis_size("ctx")
    units, deep, wide = q_wide.shape
    keys = all_pairs.shape[2]
    rows, width = x.shape
    own, kv_width = width // group, w_key.shape[1]
    bf16, f32 = jnp.bfloat16, jnp.float32
    dma = pltpu.SemaphoreType.DMA
    halves = wide_split(width)
    wide_chunk = (group, gate_part.shape[1] // (halves * count), 16, LANES)
    gain_rows = spread(2 * (width // LANES), 16)
    split, row_blocks = query_split(width), own // 16
    out_first = out_split(width)
    chips = group // 2
    small_chunks = [
        (spread(held, count) // count, 16, LANES)
        for held in (
            out_first // LANES * row_blocks,
            (width - out_first) // LANES * row_blocks,
            split // LANES * row_blocks + gain_rows // 16,
            (width - split + 2 * kv_width) // LANES * row_blocks,
        )
    ]
    levels = count // 2
    loaded = [mix, layer_base, w_query, w_key, w_value, x, resid_grad]
    return pl.pallas_call(
        functools.partial(back_kernel, [part.shape[0] for part in downs]),
        out_shape=[
            jax.ShapeDtypeStruct((rows, width), f32),
            jax.ShapeDtypeStruct((rows, width), bf16),
            *[ring_total(wide_chunk, True)] * (2 * halves),
            *[ring_total(part.shape) for part in downs],
            *[ring_total(chunk) for chunk in small_chunks],
            *[jax.ShapeDtypeStruct((levels, units, keys, deep), bf16)] * 2,
            jax.ShapeDtypeStruct((rows, width), bf16),
            *[jax.ShapeDtypeStruct((chips - 1, rows, width), bf16)] * 2,
        ],
        in_specs=[VMEM] * 7 + [ANY] * (14 + len(downs)),
        out_specs=[VMEM] * (6 + 2 * halves + len(downs)) + [ANY] * 5,
        scratch_shapes=[
            pltpu.VMEM(all_pairs.shape, bf16),
            pltpu.VMEM((2, units, keys, deep), bf16),
            pltpu.VMEM((units, keys, deep), f32),
            pltpu.VMEM((units, 2 * wide, deep), bf16),
            pltpu.VMEM((units, 1, wide), f32),
            pltpu.VMEM((units, HD, wide), f32),
            *[kind for _ in range(2 * halves) for kind in ring_scratch(wide_chunk, True)],
            *[kind for chunk in small_chunks for kind in ring_scratch(chunk)],
            pltpu.VMEM((own, group * rows), bf16),
            pltpu.VMEM((own, group * rows), bf16),
            pltpu.VMEM((group, rows, width), bf16),
            pltpu.VMEM((group, rows, width), bf16),
            pltpu.VMEM((group, rows, 2 * kv_width), bf16),
            pltpu.VMEM((rows, width), f32),
            pltpu.VMEM((gain_rows, LANES), f32),
            pltpu.VMEM((group - 1, gain_rows, LANES), f32),
            pltpu.VMEM((chips - 1, rows, width), bf16),
            pltpu.VMEM((rows, width), bf16),
            *[pltpu.VMEM(array.shape, array.dtype) for array in loaded],
            *[kind for _ in range(2 * halves) for kind in ring_semaphores(True)],
            *[kind for _ in range(len(downs) + 2) for kind in ring_semaphores()],
            *[dma((group - 1,))] * 2,
            *[kind for _ in range(2) for kind in ring_semaphores()],
            *[dma((levels,))] * 4,
            *[group_semaphores()] * 6,
            *[dma((group - 1,))] * 6,
            dma((11 + len(downs) + 2 * halves * count,)),
            dma((2,)),
        ],
        compiler_params=pltpu.CompilerParams(
            collective_id=3, has_side_effects=True, vmem_limit_bytes=62 << 20
        ),
    )(
        q_wide, g_wide, log_total, gain_grad, gain, cosine, sine, all_pairs, mix, gate_part, up_part,
        layer_base, layer_parts, branch, low_t, normed_t, w_query, w_key, w_value, x, resid_grad,
        *downs,
    )


def finish_kernel(halves, downs, *refs):
    wides, refs = refs[: 2 * halves], refs[2 * halves :]
    down_refs, refs = refs[:downs], refs[downs:]
    out_a_ref, out_b_ref, rest_a_ref, rest_b_ref = refs[:4]
    query_grad, key_grad, value_grad, out_grad, gate_grad, up_grad, down_grad = refs[4:]
    rows = gate_grad.shape[0]
    row_blocks = rows // 16
    for sources, target in ((wides[:halves], gate_grad), (wides[halves:], up_grad)):
        held = jnp.concatenate(
            [source[...].reshape((-1,) + source.shape[3:]) for source in sources], axis=0
        )
        for block in range(target.shape[1] // LANES):
            target[:, block * LANES : (block + 1) * LANES] = (
                held[block * row_blocks : (block + 1) * row_blocks]
                .reshape(rows, LANES)
                .astype(jnp.float32)
            )

    @pl.when(pl.program_id(0) == 0)
    def _():
        def unpack(source, first, target, begin, end):
            for block in range(begin, end):
                here = first + (block - begin) * row_blocks
                target[:, block * LANES : (block + 1) * LANES] = (
                    source[here : here + row_blocks].reshape(rows, LANES).astype(jnp.float32)
                )
            return first + (end - begin) * row_blocks

        width, kv_width = query_grad.shape[1], key_grad.shape[1]
        split = query_split(width) // LANES
        middle = out_split(width) // LANES
        unpack(out_a_ref, 0, out_grad, 0, middle)
        unpack(out_b_ref, 0, out_grad, middle, width // LANES)
        unpack(rest_a_ref, 0, query_grad, 0, split)
        at = unpack(rest_b_ref, 0, query_grad, split, width // LANES)
        at = unpack(rest_b_ref, at, key_grad, 0, kv_width // LANES)
        unpack(rest_b_ref, at, value_grad, 0, kv_width // LANES)
        blocks, begin = down_grad.shape[0] // 16, 0
        for source in down_refs:
            end = min(blocks, begin + source.shape[0])
            if end > begin:
                down_grad[begin * 16 : end * 16, :] = (
                    source[: end - begin]
                    .reshape((end - begin) * 16, down_grad.shape[1])
                    .astype(jnp.float32)
                )
            begin = end


def finish(wides, downs, smalls, own, width, kv_width, hidden):
    count, group, n = wides[0].shape[:3]

    def whole(array):
        return pl.BlockSpec(array.shape, lambda part, rank=len(array.shape): (0,) * rank)

    wide = pl.BlockSpec((count, 1, n, 16, LANES), lambda part: (0, part, 0, 0, 0))
    outs = [
        jax.ShapeDtypeStruct((own, columns), jnp.float32)
        for columns in (width, kv_width, kv_width, width, FF, FF)
    ] + [jax.ShapeDtypeStruct((hidden, width), jnp.float32)]
    slice_spec = pl.BlockSpec((own, FF // group), lambda part: (0, part))
    return pl.pallas_call(
        functools.partial(finish_kernel, len(wides) // 2, len(downs)),
        grid=(group,),
        out_shape=outs,
        in_specs=[wide] * len(wides) + [whole(a) for a in (*downs, *smalls)],
        out_specs=[whole(a) for a in outs[:4]] + [slice_spec, slice_spec, whole(outs[6])],
        compiler_params=pltpu.CompilerParams(vmem_limit_bytes=60 << 20),
    )(*wides, *downs, *smalls)


def on_device(
    tokens, w_query, w_key, w_value, w_out, w_gate, w_up, w_down, gain_attn, gain_ffn, cotangent
):
    block_len, seq_count, width = tokens.shape
    rows_count = block_len * seq_count
    kv_width = KVH * HD
    positions = lax.axis_index("ctx") * block_len + jnp.arange(block_len, dtype=jnp.int32)
    freqs = ROTARY_BASE ** (-2.0 * jnp.arange(HD // 2, dtype=jnp.float32) / HD)
    angles = freqs[:, None] * positions.astype(jnp.float32)[None, :]
    cosine, sine = jnp.cos(angles), jnp.sin(angles)
    x_rows = jnp.swapaxes(tokens, 0, 1).reshape(rows_count, width)
    g_rows = jnp.swapaxes(cotangent, 0, 1).reshape(rows_count, width)
    own = gain_attn.shape[0]
    units = seq_count * KVH
    wide = H // KVH * block_len
    own_gains = jnp.pad(
        jnp.stack([gain_attn, gain_ffn]).astype(jnp.float32), ((0, 6), (0, spread(own, LANES) - own))
    )
    (
        q_wide, normed_t, gains, full_query, full_key, full_value, attn_low, low_t, mix_unit, log_total,
        all_pairs, full_out, my_gate, my_up, all_g,
    ) = attend(
        x_rows, own_gains, cosine, sine, w_query, w_key, w_value, w_out, w_gate, w_up, g_rows, seq_count
    )
    layer_base, layer_parts, grad_resid, grad_branch, g_wide, gate_part, up_part, *downs = (
        feed_forward(
            x_rows, attn_low, full_out, my_gate, my_up, w_down, all_g, gains[1:2], units, wide
        )
    )
    downs, gain_term_ffn = downs[:-1], downs[-1]
    grad_tokens, layer_out, *sums = layer_back(
        q_wide, g_wide, log_total, gain_term_ffn, gains[:1], cosine, sine, all_pairs, mix_unit,
        gate_part, up_part, layer_base, layer_parts, grad_branch, low_t, normed_t, full_query,
        full_key, full_value, x_rows, grad_resid, downs,
    )
    wides, sums = sums[: 2 * wide_split(width)], sums[2 * wide_split(width) :]
    smalls = sums[len(downs) : len(downs) + 4]
    filled = query_split(width) // LANES * (own // 16)
    gain_grads = smalls[2][filled:].reshape(-1, LANES)[: 2 * (width // LANES)].reshape(2, width)
    gain_grads = lax.dynamic_slice_in_dim(gain_grads, lax.axis_index("fsdp") * own, own, 1)
    gain_grads = gain_grads.astype(jnp.float32)
    grads = finish(wides, sums[: len(downs)], smalls, own, width, kv_width, w_down.shape[0])
    return (
        jnp.swapaxes(layer_out.reshape(seq_count, block_len, width), 0, 1),
        jnp.swapaxes(grad_tokens.reshape(seq_count, block_len, width), 0, 1),
        *grads,
        gain_grads[0],
        gain_grads[1],
    )


def solution(mesh):
    return jax.shard_map(
        on_device,
        mesh=mesh,
        in_specs=(
            P("ctx", "fsdp", None),
            P("fsdp", None),
            P("fsdp", None),
            P("fsdp", None),
            P("fsdp", None),
            P("fsdp", None),
            P("fsdp", None),
            P("fsdp", None),
            P("fsdp"),
            P("fsdp"),
            P("ctx", "fsdp", None),
        ),
        out_specs=(
            P("ctx", "fsdp", None),
            P("ctx", "fsdp", None),
            P("fsdp", None),
            P("fsdp", None),
            P("fsdp", None),
            P("fsdp", None),
            P("fsdp", None),
            P("fsdp", None),
            P("fsdp", None),
            P("fsdp"),
            P("fsdp"),
        ),
        check_vma=False,
    )
```

```python
import functools

import jax
import jax.numpy as jnp
from jax import lax
from jax.experimental import pallas as pl
from jax.experimental.pallas import tpu as pltpu
from jax.sharding import PartitionSpec as P

H = 18
KVH = 6
HD = 64
FF = 3072


EPSILON = 1e-05
ROTARY_BASE = 10000.0
MASKED_SCORE = -1e30


def norm_scale(rows):
    return lax.rsqrt(jnp.mean(rows * rows, axis=-1, keepdims=True) + EPSILON)


def forward_dot(left, right):
    return jnp.dot(left, right, preferred_element_type=jnp.float32)


MESH = pl.DeviceIdType.MESH
LANES = 128


def ring_place(ctx, fsdp, count):
    column, side = lax.div(ctx, 2), lax.rem(ctx, 2)
    place = column + side * (count - 1 - 2 * column)
    odd = lax.rem(fsdp, 2)
    return place + odd * (count - 1 - 2 * place)


def ring_ctx(place, fsdp, count):
    odd = lax.rem(fsdp, 2)
    place = place + odd * (count - 1 - 2 * place)
    late = lax.div(place, count // 2)
    return (1 - late) * 2 * place + late * (2 * (count - 1 - place) + 1)


class GroupGather:
    def __init__(self, shard_of, sends, arrivals):
        self.shard_of, self.sends, self.arrivals = shard_of, sends, arrivals
        self.fsdp, self.ctx = lax.axis_index("fsdp"), lax.axis_index("ctx")
        self.chips = lax.axis_size("fsdp") // 2
        self.chip, self.core = lax.div(self.fsdp, 2), lax.rem(self.fsdp, 2)
        self.sibling = 2 * self.chip + 1 - self.core

    def copy(self, source, shard, semaphore, device):
        return pltpu.make_async_remote_copy(
            src_ref=source,
            dst_ref=self.shard_of(shard),
            send_sem=self.sends.at[semaphore],
            recv_sem=self.arrivals.at[semaphore],
            device_id=(device, self.ctx),
            device_id_type=MESH,
        )

    def same_core(self, step):
        return 2 * lax.rem(self.chip + step, self.chips) + self.core

    def across(self, source):
        return self.copy(source, self.fsdp, 0, self.sibling)

    def out(self, source, step):
        return self.copy(source, self.fsdp, step, self.same_core(step))

    def onward(self, step):
        shard = self.same_core(self.chips - step)
        return self.copy(self.shard_of(shard), shard, self.chips - 1 + step, self.sibling)

    def start(self, source):
        for step in range(1, self.chips):
            self.out(source, step).start()
        self.across(source).start()

    def forward(self):
        own = self.shard_of(self.fsdp)
        for step in range(1, self.chips):
            self.out(own, step).wait_recv()
            self.onward(step).start()

    def sibling_here(self):
        self.across(self.shard_of(self.fsdp)).wait_recv()

    def crossed(self, step):
        self.onward(step).wait_recv()

    def sent(self):
        own = self.shard_of(self.fsdp)
        self.across(own).wait_send()
        for step in range(1, self.chips):
            self.out(own, step).wait_send()
            self.onward(step).wait_send()

    def finish(self):
        self.forward()
        self.sibling_here()
        for step in range(1, self.chips):
            self.crossed(step)
        self.sent()


class HalfGather:
    def __init__(self, held, own_rows, sends, arrivals):
        self.held, self.own = held, own_rows
        self.sends, self.arrivals = sends, arrivals
        self.fsdp, self.ctx = lax.axis_index("fsdp"), lax.axis_index("ctx")
        self.chips = lax.axis_size("fsdp") // 2
        self.chip, self.core = lax.div(self.fsdp, 2), lax.rem(self.fsdp, 2)
        self.sibling = 2 * self.chip + 1 - self.core
        self.side = lax.rem(self.ctx, 2)
        self.pair = self.ctx + 1 - 2 * self.side
        first = -(-own_rows // 32) * 16
        self.halves = ((0, first), (first, own_rows - first))

    def same_core(self, step):
        return 2 * lax.rem(self.chip + step, self.chips) + self.core

    def rows(self, shard, half=None):
        begin, size = (0, self.own) if half is None else self.halves[half]
        return self.held.at[pl.ds(shard * self.own + begin, size)]

    def copy(self, source, target, semaphore, device):
        return pltpu.make_async_remote_copy(
            src_ref=source,
            dst_ref=target,
            send_sem=self.sends.at[semaphore],
            recv_sem=self.arrivals.at[semaphore],
            device_id=device,
            device_id_type=MESH,
        )

    def on_side(self, body):
        for half in range(2):

            @pl.when(self.side == half)
            def _(half=half):
                body(half)

    def across(self, source):
        return self.copy(source, self.rows(self.fsdp), 0, (self.sibling, self.ctx))

    def out(self, source, step, half):
        begin, size = self.halves[half]
        return self.copy(
            source.at[pl.ds(begin, size)],
            self.rows(self.fsdp, half),
            step,
            (self.same_core(step), self.ctx),
        )

    def to_pair(self, step, half):
        part = self.rows(self.same_core(self.chips - step), half)
        return self.copy(part, part, self.chips - 1 + step, (self.fsdp, self.pair))

    def onward(self, step):
        part = self.rows(self.same_core(self.chips - step))
        return self.copy(part, part, 2 * self.chips - 2 + step, (self.sibling, self.ctx))

    def start(self, source):
        def send(half):
            for step in range(1, self.chips):
                self.out(source, step, half).start()

        self.on_side(send)
        self.across(source).start()

    def to_pairs(self):
        def forward(half):
            for step in range(1, self.chips):
                self.out(self.rows(self.fsdp), step, half).wait_recv()
                self.to_pair(step, half).start()

        self.on_side(forward)

    def to_sibling(self):
        def forward(half):
            for step in range(1, self.chips):
                self.to_pair(step, 1 - half).wait_recv()

        self.on_side(forward)
        for step in range(1, self.chips):
            self.onward(step).start()

    def arrived(self):
        self.across(self.rows(self.fsdp)).wait_recv()
        for step in range(1, self.chips):
            self.onward(step).wait_recv()

    def sent(self):
        def wait(half):
            for step in range(1, self.chips):
                self.out(self.rows(self.fsdp), step, half).wait_send()
                self.to_pair(step, half).wait_send()

        self.on_side(wait)
        self.across(self.rows(self.fsdp)).wait_send()
        for step in range(1, self.chips):
            self.onward(step).wait_send()


class HalfSpread(HalfGather):
    def __init__(self, source, held, sends, arrivals):
        super().__init__(held, source.shape[0], sends, arrivals)
        self.source, self.columns = source, held.shape[1]

    def slice_for(self, peer):
        return self.source.at[:, lane_tile(peer, self.columns)]

    def others(self):
        return [(step, other) for step in range(1, self.chips) for other in range(2)]

    def device(self, step, other):
        return 2 * lax.rem(self.chip + step, self.chips) + lax.rem(self.core + other, 2)

    def near(self):
        return self.copy(
            self.slice_for(self.sibling), self.rows(self.fsdp), 0, (self.sibling, self.ctx)
        )

    def far(self, step, other, half):
        peer = self.device(step, other)
        begin, size = self.halves[half]
        return self.copy(
            self.slice_for(peer).at[pl.ds(begin, size)],
            self.rows(self.fsdp, half),
            2 * step - 1 + other,
            (peer, self.ctx),
        )

    def onto_pair(self, step, other, half):
        part = self.rows(self.device(self.chips - step, other), half)
        return self.copy(part, part, 2 * (self.chips - 1 + step) - 1 + other, (self.fsdp, self.pair))

    def start(self):
        def send(half):
            for step, other in self.others():
                self.far(step, other, half).start()

        self.on_side(send)
        self.near().start()

    def to_pairs(self):
        def forward(half):
            for step, other in self.others():
                self.far(step, other, half).wait_recv()
                self.onto_pair(step, other, half).start()

        self.on_side(forward)

    def finish(self):
        def wait(half):
            for step, other in self.others():
                self.onto_pair(step, other, 1 - half).wait_recv()
                self.far(step, other, half).wait_send()
                self.onto_pair(step, other, half).wait_send()

        self.on_side(wait)
        self.near().wait()


def spread_semaphores():
    return pltpu.SemaphoreType.DMA((2 * lax.axis_size("fsdp") - 3,))


def half_semaphores(many):
    return pltpu.SemaphoreType.DMA((many, 3 * (lax.axis_size("fsdp") // 2) - 2))


def group_semaphores():
    return pltpu.SemaphoreType.DMA((lax.axis_size("fsdp") - 1,))


def greet_group(barrier):
    fsdp, ctx, group = lax.axis_index("fsdp"), lax.axis_index("ctx"), lax.axis_size("fsdp")
    for step in range(1, group):
        peer = lax.rem(fsdp + step, group)
        pl.semaphore_signal(barrier, inc=1, device_id=(peer, ctx), device_id_type=MESH)
    return group - 1


class Steps:
    def __init__(self):
        self.fsdp, self.ctx = lax.axis_index("fsdp"), lax.axis_index("ctx")
        self.levels = lax.axis_size("ctx") // 2
        self.level, self.side = lax.div(self.ctx, 2), lax.rem(self.ctx, 2)
        self.peer = (self.fsdp, 2 * self.level + 1 - self.side)
        self.above = (self.fsdp, lax.rem(self.ctx + 2, 2 * self.levels))
        self.below = (self.fsdp, lax.rem(self.ctx + 2 * self.levels - 2, 2 * self.levels))
        self.has_above = self.level + 1 < self.levels
        self.has_below = self.level > 0

    def greet(self, barrier):
        pl.semaphore_signal(barrier, inc=1, device_id=self.peer, device_id_type=MESH)

        @pl.when(self.has_above)
        def _():
            pl.semaphore_signal(barrier, inc=1, device_id=self.above, device_id_type=MESH)

        @pl.when(self.has_below)
        def _():
            pl.semaphore_signal(barrier, inc=1, device_id=self.below, device_id_type=MESH)

        return 1 + jnp.minimum(self.level, 1) + jnp.minimum(self.levels - 1 - self.level, 1)


PARTS = 2


def causal(keys, wide, shape):
    key_at = lax.broadcasted_iota(jnp.int32, shape, 0)
    query_at = lax.rem(lax.broadcasted_iota(jnp.int32, shape, 1), keys)
    return key_at <= query_at


def attend_kernel(
    x_ref, gain_ref, cos_ref, sin_ref, query_ref, key_ref, value_ref, out_ref, gate_ref, up_ref, g_ref,
    q_ref, normed_t_ref, gains_ref, full_query, full_key, full_value,
    low_ref, low_t_ref, mix_ref, log_ref, all_ref, full_out_ref, my_gate_ref, my_up_ref, all_g_ref,
    normed_ref, key_rows, gain_all,
    top_ref, total_ref, chain_sends, chain_arrivals, peer_sends, peer_arrivals,
    half_sends, half_arrivals, gain_sends, gain_arrivals,
    out_sends, out_arrivals, gate_sends, gate_arrivals, g_sends, g_arrivals,
    part_sends, part_arrivals, local_sems,
):
    steps = Steps()
    fsdp, ctx, group = steps.fsdp, steps.ctx, lax.axis_size("fsdp")
    units, deep, wide = q_ref.shape
    keys = all_ref.shape[2]
    per_part = units // PARTS
    rows_count, width = x_ref.shape
    own = query_ref.shape[0]
    sequences, groups = units // KVH, H // KVH
    barrier = pltpu.get_barrier_semaphore()
    greeted = steps.greet(barrier) + greet_group(barrier)
    span = KVH * HD
    pieces = [(key_ref, full_key, 0), (value_ref, full_value, 0)]
    pieces += [(query_ref, full_query, start) for start in range(0, width, span)]
    gathers = []
    for at, (source, target, start) in enumerate(pieces):
        columns = pl.ds(start, span)
        gather = HalfGather(
            target.at[:, columns], own, half_sends.at[at], half_arrivals.at[at]
        )
        gathers.append((gather, source.at[:, columns]))
    own_rows = pl.ds(fsdp * own, own)
    own_copies = [
        pltpu.make_async_copy(source, target.at[own_rows], local_sems.at[4 + at])
        for at, (source, target) in enumerate(
            ((key_ref, full_key), (value_ref, full_value), (query_ref, full_query))
        )
    ]
    for copy in own_copies:
        copy.start()
    gain_all[fsdp] = gain_ref[...]
    pl.semaphore_wait(barrier, greeted)

    def gain_copy(step):
        peer = lax.rem(fsdp + step, group)
        return pltpu.make_async_remote_copy(
            src_ref=gain_ref,
            dst_ref=gain_all.at[fsdp],
            send_sem=gain_sends.at[step - 1],
            recv_sem=gain_arrivals.at[step - 1],
            device_id=(peer, ctx),
            device_id_type=MESH,
        )

    for step in range(1, group):
        gain_copy(step).start()
    for gather, source in gathers:
        gather.start(source)
    inputs = x_ref[...].astype(jnp.float32)
    scale = norm_scale(inputs)
    q_ref[:, HD:, :] = jnp.zeros((units, HD, wide), q_ref.dtype)
    for step in range(1, group):
        gain_copy(step).wait_recv()
    gains = jnp.concatenate([gain_all[shard][:, :own] for shard in range(group)], axis=1)
    gains_ref[...] = gains
    normed_ref[...] = (inputs * scale * gains[:1]).astype(jnp.bfloat16)
    cosine, sine = cos_ref[...], sin_ref[...]

    def turn(columns):
        first, second = columns[: HD // 2], columns[HD // 2 :]
        return jnp.concatenate(
            [first * cosine - second * sine, second * cosine + first * sine], axis=0
        ).astype(jnp.bfloat16)

    def block_copy(level, part, side, semaphores, arrivals, arrives, device):
        block = 2 * (steps.level - level) + side
        held = all_ref.at[block, pl.ds(part * per_part, per_part)]
        return pltpu.make_async_remote_copy(
            src_ref=held,
            dst_ref=held,
            send_sem=semaphores.at[level, part],
            recv_sem=arrivals.at[arrives, part],
            device_id=device,
            device_id_type=MESH,
        )

    def chain(level, part):
        return block_copy(
            level, part, steps.side, chain_sends, chain_arrivals, level + 1, steps.above
        )

    def across(level, part):
        return block_copy(
            level, part, steps.side, peer_sends, peer_arrivals, level, steps.peer
        )

    def pass_on(level, part):
        @pl.when(steps.has_above)
        def _():
            chain(level, part).start()

    def project(at):
        _, weight, start = pieces[at]
        made = forward_dot(normed_ref[...], weight[:, start : start + span])
        if at == 0:
            key_rows[...] = made
            return
        for sequence in range(sequences):
            block = slice(sequence * keys, (sequence + 1) * keys)
            for pair in range(span // (2 * HD)):
                columns = slice(pair * 2 * HD, (pair + 1) * 2 * HD)
                turned = made[block, columns].T
                if at == 1:
                    turned_keys = key_rows[block, columns].T
                    for half in range(2):
                        held = slice(half * HD, (half + 1) * HD)
                        both = jnp.concatenate(
                            [turn(turned_keys[held]), turned[held].astype(jnp.bfloat16)], axis=0
                        )
                        all_ref[ctx, sequence * KVH + 2 * pair + half] = both.T
                else:
                    for half in range(2):
                        head = start // HD + 2 * pair + half
                        unit, member = sequence * KVH + head // groups, head % groups
                        part = turn(turned[half * HD : (half + 1) * HD])
                        q_ref[unit, :HD, member * keys : (member + 1) * keys] = part * jnp.bfloat16(
                            HD ** (-0.5)
                        )
        if at == 1:
            for part in range(PARTS):
                pass_on(0, part)

                @pl.when(steps.side == 0)
                def _():
                    across(0, part).start()

    last = len(pieces)
    for at in range(last + 2):
        if at < last:
            gathers[at][0].to_pairs()
        if 1 <= at <= last:
            gathers[at - 1][0].to_sibling()
        if at == 1:
            for column in range(width // LANES):
                columns = slice(column * LANES, (column + 1) * LANES)
                normed_t_ref[columns, :] = normed_ref[:, columns].T
            for copy in own_copies:
                copy.wait()
        if at >= 2:
            gathers[at - 2][0].arrived()
            project(at - 2)

    columns = my_gate_ref.shape[1]
    gathered = HalfGather(full_out_ref, own, out_sends.at[0], out_arrivals.at[0])
    gathered.start(out_ref)
    spread_gate = HalfSpread(gate_ref, my_gate_ref, gate_sends, gate_arrivals)
    spread_gate.start()
    gathered_g = GroupGather(lambda shard: all_g_ref.at[shard], g_sends, g_arrivals)
    mine = lane_tile(fsdp, columns)
    background = [
        pltpu.make_async_copy(out_ref, full_out_ref.at[own_rows], local_sems.at[0]),
        pltpu.make_async_copy(gate_ref.at[:, mine], my_gate_ref.at[own_rows], local_sems.at[1]),
        pltpu.make_async_copy(up_ref.at[:, mine], my_up_ref.at[own_rows], local_sems.at[2]),
        pltpu.make_async_copy(g_ref, all_g_ref.at[fsdp], local_sems.at[3]),
    ]
    for copy in background:
        copy.start()
    up_parts = []
    for step in range(1, group):
        peer = lax.rem(fsdp + step, group)
        up_parts.append(
            pltpu.make_async_remote_copy(
                src_ref=up_ref.at[:, lane_tile(peer, columns)],
                dst_ref=my_up_ref.at[own_rows],
                send_sem=part_sends.at[step - 1],
                recv_sem=part_arrivals.at[step - 1],
                device_id=(peer, ctx),
                device_id_type=MESH,
            )
        )

    def second_half():
        spread_gate.to_pairs()
        gathered.to_pairs()
        gathered_g.start(g_ref)
        for copy in up_parts:
            copy.start()

    def add(unit, kv):
        scores = jnp.dot(kv, q_ref[unit], preferred_element_type=jnp.float32)
        top = top_ref[unit]
        new_top = jnp.maximum(top, jnp.max(scores, axis=0, keepdims=True))
        fade = jnp.exp(top - new_top)
        weights = jnp.exp(scores - new_top)
        top_ref[unit] = new_top
        total_ref[unit] = total_ref[unit] * fade + jnp.sum(weights, axis=0, keepdims=True)
        added = jnp.dot(kv.T, weights.astype(jnp.bfloat16), preferred_element_type=jnp.float32)
        mix_ref[unit] = mix_ref[unit] * fade + added[HD:]

    def over_units(body, first, count):
        def two(at, unused):
            body(first + 2 * at)
            body(first + 2 * at + 1)
            return unused

        lax.fori_loop(0, count // 2, two, 0)

    def diagonal(unit):
        kv = all_ref[ctx, unit]
        scores = jnp.dot(kv, q_ref[unit], preferred_element_type=jnp.float32)
        scores = jnp.where(causal(keys, wide, scores.shape), scores, MASKED_SCORE)
        top = jnp.max(scores, axis=0, keepdims=True)
        weights = jnp.exp(scores - top)
        top_ref[unit] = top
        total_ref[unit] = jnp.sum(weights, axis=0, keepdims=True)
        added = jnp.dot(kv.T, weights.astype(jnp.bfloat16), preferred_element_type=jnp.float32)
        mix_ref[unit] = added[HD:]

    over_units(diagonal, 0, units)

    @pl.when(steps.side == 1)
    def _():
        for part in range(PARTS):
            across(0, part).wait_recv()
            over_units(lambda unit: add(unit, all_ref[ctx - 1, unit]), part * per_part, per_part)

    def level_step(level, unused):
        for part in range(PARTS):
            chain(level - 1, part).wait_recv()
            pass_on(level, part)
            across(level, part).start()
        first = 2 * (steps.level - level)
        for part in range(PARTS):
            across(level, part).wait_recv()
            over_units(
                lambda unit: add(unit, all_ref[pl.ds(first, 2), unit].reshape(2 * keys, deep)),
                part * per_part,
                per_part,
            )

        @pl.when(level == 1)
        def _():
            second_half()

        return unused

    @pl.when(steps.level == 0)
    def _():
        second_half()

    lax.fori_loop(1, steps.level + 1, level_step, 0)

    def close(unit):
        total = total_ref[unit]
        mix_ref[unit] = mix_ref[unit] / total
        log_ref[unit] = top_ref[unit] + jnp.log(total)

    over_units(close, 0, units)
    for sequence in range(sequences):
        for pair in range(H // 2):
            heads = []
            for head in (2 * pair, 2 * pair + 1):
                unit, member = sequence * KVH + head // groups, head % groups
                heads.append(mix_ref[unit, :, member * keys : (member + 1) * keys])
            tile = jnp.concatenate(heads, axis=0).astype(low_ref.dtype)
            block = slice(sequence * keys, (sequence + 1) * keys)
            columns = slice(pair * 2 * HD, (pair + 1) * 2 * HD)
            low_t_ref[columns, block] = tile
            low_ref[block, columns] = tile.T
    for gather, _ in gathers:
        gather.sent()
    for step in range(1, group):
        gain_copy(step).wait_send()
    gathered.to_sibling()
    gathered_g.forward()
    gathered.arrived()
    gathered.sent()
    gathered_g.sibling_here()
    for step in range(1, gathered_g.chips):
        gathered_g.crossed(step)
    gathered_g.sent()
    spread_gate.finish()
    for copy in up_parts:
        copy.wait()
    for copy in background:
        copy.wait()

    def sent(level, unused):
        for part in range(PARTS):

            @pl.when(steps.has_above)
            def _():
                chain(level, part).wait_send()

            @pl.when(jnp.logical_or(level > 0, steps.side == 0))
            def _():
                across(level, part).wait_send()

        return unused

    lax.fori_loop(0, steps.level + 1, sent, 0)


ANY = pl.BlockSpec(memory_space=pl.ANY)
VMEM = pl.BlockSpec(memory_space=pltpu.VMEM)


def attend(x, gains, cosine, sine, w_query, w_key, w_value, w_out, w_gate, w_up, g_rows, sequences):
    group, count = lax.axis_size("fsdp"), lax.axis_size("ctx")
    rows, width = x.shape
    own, hidden = w_query.shape[0], w_gate.shape[1] // group
    keys, units, deep = rows // sequences, sequences * KVH, 2 * HD
    wide = H // KVH * keys
    kv_width = KVH * HD
    dma = pltpu.SemaphoreType.DMA
    bf16, f32 = jnp.bfloat16, jnp.float32
    pieces = 2 + width // kv_width
    return pl.pallas_call(
        attend_kernel,
        out_shape=[
            jax.ShapeDtypeStruct((units, deep, wide), bf16),
            jax.ShapeDtypeStruct((width, rows), bf16),
            jax.ShapeDtypeStruct((gains.shape[0], width), f32),
            jax.ShapeDtypeStruct((width, width), bf16),
            jax.ShapeDtypeStruct((width, kv_width), bf16),
            jax.ShapeDtypeStruct((width, kv_width), bf16),
            jax.ShapeDtypeStruct((rows, width), bf16),
            jax.ShapeDtypeStruct((width, rows), bf16),
            jax.ShapeDtypeStruct((units, HD, wide), f32),
            jax.ShapeDtypeStruct((units, 1, wide), f32),
            jax.ShapeDtypeStruct((count, units, keys, deep), bf16),
            jax.ShapeDtypeStruct((width, width), bf16),
            jax.ShapeDtypeStruct((width, hidden), bf16),
            jax.ShapeDtypeStruct((width, hidden), bf16),
            jax.ShapeDtypeStruct((group, rows, width), bf16),
        ],
        in_specs=[VMEM] * 4 + [ANY] * 7,
        out_specs=[VMEM] * 11 + [ANY] * 4,
        scratch_shapes=[
            pltpu.VMEM((rows, width), bf16),
            pltpu.VMEM((rows, kv_width), f32),
            pltpu.VMEM((group,) + gains.shape, f32),
            pltpu.VMEM((units, 1, wide), f32),
            pltpu.VMEM((units, 1, wide), f32),
            dma((count // 2, PARTS)),
            dma((count // 2 + 1, PARTS)),
            dma((count // 2, PARTS)),
            dma((count // 2, PARTS)),
            half_semaphores(pieces),
            half_semaphores(pieces),
            *[dma((group - 1,))] * 2,
            *[half_semaphores(1)] * 2,
            *[spread_semaphores()] * 2,
            *[group_semaphores()] * 2,
            *[dma((group - 1,))] * 2,
            dma((7,)),
        ],
        compiler_params=pltpu.CompilerParams(
            collective_id=1, has_side_effects=True, vmem_limit_bytes=60 << 20
        ),
    )(x, gains, cosine, sine, w_query, w_key, w_value, w_out, w_gate, w_up, g_rows)


class Ring:
    def __init__(self, work, landing, total, semaphores, forward, exchange=False):
        self.fsdp, self.ctx = lax.axis_index("fsdp"), lax.axis_index("ctx")
        self.group, self.count = lax.axis_size("fsdp"), lax.axis_size("ctx")
        self.work, self.landing, self.total = work, landing, total
        self.sends, self.arrivals = semaphores[:2]
        self.part_sends, self.part_arrivals, self.own_sem = semaphores[2:] if exchange else (None,) * 3
        self.exchange = exchange
        side = 0 if forward else 1
        self.place = ring_place(self.ctx, side, self.count)
        self.after = (self.fsdp, ring_ctx(lax.rem(self.place + 1, self.count), side, self.count))
        self.ticks = 2 * self.count - 2 + int(exchange)

    def chunk(self, held, index):
        if self.exchange:
            return held.at[index]
        per = held.shape[0] // self.count
        return held.at[pl.ds(index * per, per)]

    def summing(self, step, index):
        return self.copy(self.chunk(self.work, index), self.landing.at[step], step)

    def handing(self, step, index):
        held = self.chunk(self.total, index)
        return self.copy(held, held, step)

    def copy(self, source, target, step):
        return pltpu.make_async_remote_copy(
            src_ref=source,
            dst_ref=target,
            send_sem=self.sends.at[step],
            recv_sem=self.arrivals.at[step],
            device_id=self.after,
            device_id_type=MESH,
        )

    def part(self, index, step):
        peer = lax.rem(self.fsdp + step, self.group)
        return pltpu.make_async_remote_copy(
            src_ref=self.work.at[index, peer],
            dst_ref=self.total.at[index, self.fsdp],
            send_sem=self.part_sends.at[step - 1],
            recv_sem=self.part_arrivals.at[step - 1],
            device_id=(peer, self.ctx),
            device_id_type=MESH,
        )

    def own_part(self, index):
        return pltpu.make_async_copy(
            self.work.at[index, self.fsdp], self.total.at[index, self.fsdp], self.own_sem
        )

    def start(self):
        self.summing(0, self.place).start()

    def tick(self, at):
        last = self.count - 2
        gap = int(self.exchange)
        step = at - gap * jnp.where(at > last, 1, 0) if self.exchange else at
        index = lax.rem(self.place + 3 * self.count - 1 - step, self.count)

        def add(target):
            part, landed = self.chunk(self.work, index), self.landing.at[jnp.minimum(at, last)]
            for row in range(part.shape[0]):
                target[row] = (
                    part[row].astype(jnp.float32) + landed[row].astype(jnp.float32)
                ).astype(part.dtype)

        @pl.when(at <= last)
        def _():
            self.summing(jnp.minimum(at, last), index).wait_recv()

        @pl.when(at < last)
        def _():
            add(self.chunk(self.work, index))
            self.summing(jnp.minimum(at + 1, last), index).start()

        if self.exchange:

            @pl.when(at == last)
            def _():
                add(self.chunk(self.work, index))
                for peer in range(1, self.group):
                    self.part(index, peer).start()
                self.own_part(index).start()

            @pl.when(at == last + 1)
            def _():
                done = lax.rem(self.place + 1, self.count)
                self.own_part(done).wait()
                for peer in range(1, self.group):
                    self.part(done, peer).wait_recv()
                self.handing(last + 1, done).start()

        else:

            @pl.when(at == last)
            def _():
                add(self.chunk(self.total, index))
                self.handing(last + 1, index).start()

        @pl.when(at > last + gap)
        def _():
            here = jnp.maximum(step, last + 1)
            self.handing(here, index).wait_recv()

            @pl.when(here < 2 * self.count - 3)
            def _():
                self.handing(jnp.minimum(here + 1, 2 * self.count - 3), index).start()

    def finish(self):
        def wait(step, unused):
            self.handing(step, self.place).wait_send()
            return unused

        lax.fori_loop(0, 2 * self.count - 2, wait, 0)
        if self.exchange:
            for peer in range(1, self.group):
                self.part(lax.rem(self.place + 1, self.count), peer).wait_send()


class SumRing(Ring):
    def __init__(self, *args):
        super().__init__(*args)
        self.ticks = self.count - 1

    def tick(self, at):
        last = self.count - 2
        index = lax.rem(self.place + 2 * self.count - 1 - at, self.count)
        self.summing(at, index).wait_recv()
        work, landed = self.chunk(self.work, index), self.landing.at[at]

        def add(target):
            for row in range(work.shape[0]):
                target[row] = (
                    work[row].astype(jnp.float32) + landed[row].astype(jnp.float32)
                ).astype(work.dtype)

        @pl.when(at < last)
        def _():
            add(work)
            self.summing(jnp.minimum(at + 1, last), index).start()

        @pl.when(at == last)
        def _():
            add(self.total)

    def finish(self):
        def wait(step, unused):
            self.summing(step, self.place).wait_send()
            return unused

        lax.fori_loop(0, self.ticks, wait, 0)


class SpreadRing(Ring):
    def __init__(self, total, semaphores, forward):
        super().__init__(None, None, total, semaphores, forward)
        self.ticks = self.count - 1
        self.first = lax.rem(self.place + 1, self.count)

    def start(self):
        self.handing(0, self.first).start()

    def tick(self, at):
        index = lax.rem(self.place + self.count - at, self.count)
        self.handing(at, index).wait_recv()

        @pl.when(at < self.count - 2)
        def _():
            self.handing(jnp.minimum(at + 1, self.count - 2), index).start()

    def finish(self):
        def wait(step, unused):
            self.handing(step, self.place).wait_send()
            return unused

        lax.fori_loop(0, self.ticks, wait, 0)


def ring_scratch(chunk, exchange=False):
    count = lax.axis_size("ctx")
    work = (count,) + chunk if exchange else (count * chunk[0],) + chunk[1:]
    return [pltpu.VMEM(work, jnp.bfloat16), pltpu.VMEM((count - 1,) + chunk, jnp.bfloat16)]


def ring_total(chunk, exchange=False):
    count = lax.axis_size("ctx")
    work = (count,) + chunk if exchange else (count * chunk[0],) + chunk[1:]
    return jax.ShapeDtypeStruct(work, jnp.bfloat16)


def ring_semaphores(exchange=False):
    dma, steps = pltpu.SemaphoreType.DMA, 2 * lax.axis_size("ctx") - 2
    parts = lax.axis_size("fsdp") - 1
    return [dma((steps,))] * 2 + ([dma((parts,))] * 2 + [dma] if exchange else [])


def wide_split(width):
    group, count = lax.axis_size("fsdp"), lax.axis_size("ctx")
    return 2 if FF // group // LANES * (width // group // 16) >= 4 * count else 1


def query_split(width):
    return width // LANES * 7 // 9 * LANES


def out_split(width):
    return (width // LANES + 1) // 2 * LANES


def down_split(blocks, count):
    each = -(-blocks // count)
    rings = 4 if each >= 4 else 2
    return [max(1, (each + at) // rings) for at in range(rings)]


class GroupScatter:
    def __init__(self, give_sib, got_sib, give_cross, got_cross, far, got_far, sends, arrivals):
        self.give_sib, self.got_sib = give_sib, got_sib
        self.give_cross, self.got_cross = give_cross, got_cross
        self.far, self.got_far = far, got_far
        self.sends, self.arrivals = sends, arrivals
        self.fsdp, self.ctx = lax.axis_index("fsdp"), lax.axis_index("ctx")
        self.chips = lax.axis_size("fsdp") // 2
        self.chip, self.core = lax.div(self.fsdp, 2), lax.rem(self.fsdp, 2)
        self.sibling = 2 * self.chip + 1 - self.core

    def copy(self, source, target, semaphore, device):
        return pltpu.make_async_remote_copy(
            src_ref=source,
            dst_ref=target,
            send_sem=self.sends.at[semaphore],
            recv_sem=self.arrivals.at[semaphore],
            device_id=(device, self.ctx),
            device_id_type=MESH,
        )

    def to_sibling(self):
        return self.copy(self.give_sib, self.got_sib, 0, self.sibling)

    def to_cross(self, step):
        return self.copy(
            self.give_cross(step), self.got_cross.at[step - 1], step, self.sibling
        )

    def to_far(self, step):
        chip = lax.rem(self.chip + self.chips - step, self.chips)
        return self.copy(
            self.far.at[step - 1],
            self.got_far.at[step - 1],
            self.chips - 1 + step,
            2 * chip + self.core,
        )

    def add_cross(self, step):
        self.to_cross(step).wait_recv()
        held = self.far.at[step - 1]
        held[...] = (
            held[...].astype(jnp.float32) + self.got_cross[step - 1].astype(jnp.float32)
        ).astype(held.dtype)
        self.to_far(step).start()

    def total(self, own):
        self.to_sibling().wait_recv()
        value = own + self.got_sib[...].astype(jnp.float32)
        for step in range(1, self.chips):
            self.to_far(step).wait_recv()
            value = value + self.got_far[step - 1].astype(jnp.float32)
        return value

    def sent(self):
        self.to_sibling().wait_send()
        for step in range(1, self.chips):
            self.to_cross(step).wait_send()
            self.to_far(step).wait_send()


def scatter_scratch(rows, width):
    far = lax.axis_size("fsdp") // 2 - 1
    one, many = (rows, width), (far, rows, width)
    return [pltpu.VMEM(shape, jnp.bfloat16) for shape in (one, one, many, many, many, many)]


def dot_columns(left, right):
    return lax.dot_general(
        left, right, (((1,), (1,)), ((), ())), preferred_element_type=jnp.float32
    )


def tiles(count, body):
    def step(at, unused):
        body(at)
        return unused

    lax.fori_loop(0, count, step, 0)


def lane_tile(at, size):
    return pl.ds(pl.multiple_of(at * size, LANES), size)


def width_tile(width):
    return 384 if width % 384 == 0 else width


def hidden_tile(hidden):
    return 256 if hidden % 256 == 0 else 128


def transpose_into(target, source):
    rows, columns = source.shape

    def body(at):
        part = source[:, lane_tile(at, LANES)]
        target[pl.ds(pl.multiple_of(at * LANES, LANES), LANES), :] = part.T

    tiles(columns // LANES, body)


def ffn_kernel(
    x_ref, low_ref, out_ref, gate_ref, up_ref, down_ref, all_g_ref, gain_ref,
    layer_ref, layer_part_ref, resid_grad_ref, branch_ref, g_wide_ref, gate_part_ref, up_part_ref,
    *rest,
):
    downs = len(down_split(gate_ref.shape[1] // 16, lax.axis_size("ctx")))
    taken = iter(rest)

    def take(number):
        return [next(taken) for _ in range(number)]

    down_done, (gain_grad_ref,) = take(downs), take(1)
    all_n_ref, turned_n, turned_act, act_ref, gate_grad, up_grad, resid_ref, grad_own = take(8)
    down_scratch = take(2 * downs)
    give_sib, got_sib, give_cross, got_cross, far, got_far = take(6)
    n_sends, n_arrivals, grad_sends, grad_arrivals = take(4)
    rings = [
        SumRing(*down_scratch[2 * at : 2 * at + 2], down_done[at], take(2), at % 2 == 0)
        for at in range(downs)
    ]
    group = lax.axis_size("fsdp")
    rows, width = x_ref.shape
    hidden = gate_ref.shape[1]
    barrier = pltpu.get_barrier_semaphore()
    greeted = greet_group(barrier) + 2
    for ring in rings[:2]:
        pl.semaphore_signal(barrier, inc=1, device_id=ring.after, device_id_type=MESH)
    step_in, step_out = hidden_tile(hidden), width_tile(width)

    def branch(at):
        columns = lane_tile(at, step_out)
        resid_ref[:, columns] = x_ref[:, columns].astype(jnp.float32) + forward_dot(
            low_ref[...], out_ref[:, columns]
        )

    tiles(width // step_out, branch)
    gain = gain_ref[...]
    scale = norm_scale(resid_ref[...])
    gathered = GroupGather(lambda shard: all_n_ref.at[shard], n_sends, n_arrivals)
    fsdp, chips = gathered.fsdp, gathered.chips
    all_n_ref[fsdp] = (resid_ref[...] * scale * gain).astype(jnp.bfloat16)
    pl.semaphore_wait(barrier, greeted)
    gathered.start(all_n_ref.at[fsdp])
    grad_sum = GroupScatter(
        give_sib,
        got_sib,
        lambda step: give_cross.at[step - 1],
        got_cross,
        far,
        got_far,
        grad_sends,
        grad_arrivals,
    )

    def hidden_part(shard):
        def body(at):
            columns = lane_tile(at, step_in)
            normed = all_n_ref[shard]
            gate = forward_dot(normed, gate_ref[:, columns])
            upward = forward_dot(normed, up_ref[:, columns])
            grad_act = dot_columns(
                all_g_ref[shard], down_ref[pl.ds(pl.multiple_of(at * step_in, LANES), step_in), :]
            )
            sigmoid = jax.nn.sigmoid(gate)
            silu = gate * sigmoid
            act_ref[shard, :, columns] = (silu * upward).astype(jnp.bfloat16)
            gate_grad[shard, :, columns] = (
                grad_act * upward * (sigmoid * (1.0 + gate * (1.0 - sigmoid)))
            ).astype(jnp.bfloat16)
            up_grad[shard, :, columns] = (grad_act * silu).astype(jnp.bfloat16)

        tiles(hidden // step_in, body)

    def grad_part(shard, target):
        def body(at):
            columns = pl.ds(pl.multiple_of(at * step_out, LANES), step_out)
            target[:, columns] = (
                dot_columns(gate_grad[shard], gate_ref[columns, :])
                + dot_columns(up_grad[shard], up_ref[columns, :])
            ).astype(target.dtype)

        tiles(width // step_out, body)

    hidden_part(fsdp)
    gathered.sibling_here()
    sibling = gathered.sibling
    hidden_part(sibling)
    grad_part(sibling, grad_sum.give_sib)
    grad_sum.to_sibling().start()
    gathered.forward()
    grad_part(fsdp, grad_own)
    def turn_act(shard):
        transpose_into(turned_act.at[:, lane_tile(shard, rows)], act_ref.at[shard])

    turn_act(fsdp)
    turn_act(sibling)
    for step in range(1, chips):
        ours = gathered.same_core(chips - step)
        theirs = ours + sibling - fsdp
        gathered.crossed(step)
        hidden_part(theirs)
        grad_part(theirs, give_cross.at[step - 1])
        grad_sum.to_cross(step).start()
        hidden_part(ours)
        grad_part(ours, far.at[step - 1])
        grad_sum.add_cross(step)
        turn_act(theirs)
        turn_act(ours)
    blocks = hidden // 16
    spans, first = [], 0
    for ring in rings:
        last = min(blocks, first + ring.work.shape[0])
        spans.append((first, last, ring.work))
        first = last

    def down_tile(at):
        columns = lane_tile(at, step_out)
        part = forward_dot(
            turned_act[...], all_g_ref[:, :, columns].reshape(group * rows, step_out)
        ).astype(jnp.bfloat16)
        for begin, end, work in spans:
            if end > begin:
                work[: end - begin, :, columns] = part[begin * 16 : end * 16].reshape(
                    end - begin, 16, step_out
                )

    tiles(width // step_out, down_tile)
    for begin, end, work in spans:
        for spare in range(end - begin, work.shape[0]):
            work[spare] = jnp.zeros(work.shape[1:], work.dtype)
    for ring in rings:
        ring.start()
    ticked = [0]

    def ring_tick(at):
        for ring in rings:

            @pl.when(at < ring.ticks)
            def _():
                ring.tick(jnp.minimum(at, ring.ticks - 1))

    def ticking(times, body):
        begin = ticked[0]

        def step(at):
            body(at)
            ring_tick(begin + at)

        tiles(times, step)
        ticked[0] += times

    for shard in range(group):
        span = slice(shard * rows, (shard + 1) * rows)
        transpose_into(turned_n.at[:, span], all_n_ref.at[shard])
    own = width // group
    row_blocks = own // 16
    for source, target in ((gate_grad, gate_part_ref), (up_grad, up_part_ref)):

        def weight_tile(at):
            columns = lane_tile(at, step_in)
            part = forward_dot(
                turned_n[...], source[:, :, columns].reshape(group * rows, step_in)
            ).astype(jnp.bfloat16)
            for block in range(step_in // LANES):
                first = (at * (step_in // LANES) + block) * row_blocks
                for owner in range(group):
                    target[owner, pl.ds(first, row_blocks)] = part[
                        owner * own : (owner + 1) * own, block * LANES : (block + 1) * LANES
                    ].reshape(row_blocks, 16, LANES)

        ticking(hidden // step_in, weight_tile)
        filled = hidden // LANES * row_blocks
        for spare in range(filled, target.shape[1]):
            for owner in range(group):
                target[owner, spare] = jnp.zeros(target.shape[2:], target.dtype)

    def layer_tile(at):
        columns = lane_tile(at, step_out)
        part = forward_dot(
            act_ref[...].reshape(group * rows, hidden), down_ref[:, columns]
        ).reshape(group, rows, step_out)
        layer_part_ref[:, :, columns] = part.astype(jnp.bfloat16)

    ticking(width // step_out, layer_tile)
    layer_ref[...] = resid_ref[...] + layer_part_ref[fsdp].astype(jnp.float32)
    upstream = grad_sum.total(grad_own[...])
    resid = resid_ref[...]
    scaled = upstream * gain
    grad_resid = (
        all_g_ref[fsdp].astype(jnp.float32)
        + scale * scaled
        - resid * scale**3 * jnp.mean(scaled * resid, axis=-1, keepdims=True)
    )
    gain_grad_ref[...] = jnp.sum(upstream * resid * scale, axis=0, keepdims=True)
    resid_grad_ref[...] = grad_resid
    branch_ref[...] = grad_resid.astype(jnp.bfloat16)
    units, _, wide = g_wide_ref.shape
    sequences = units // KVH
    keys = rows // sequences
    groups = wide // keys
    g_wide_ref[:, :HD, :] = jnp.zeros((units, HD, wide), g_wide_ref.dtype)
    for pair in range(H // 2):
        columns = slice(pair * 2 * HD, (pair + 1) * 2 * HD)
        mixed = dot_columns(branch_ref[...], out_ref[columns, :]).astype(jnp.bfloat16)
        for sequence in range(sequences):
            turned = mixed[sequence * keys : (sequence + 1) * keys].T
            for half in range(2):
                head = 2 * pair + half
                unit, member = sequence * KVH + head // groups, head % groups
                g_wide_ref[unit, HD:, member * keys : (member + 1) * keys] = turned[
                    half * HD : (half + 1) * HD
                ]
    begin = ticked[0]
    tiles(max(0, rings[0].ticks - begin), lambda at: ring_tick(begin + at))
    gathered.sent()
    grad_sum.sent()
    for ring in rings:
        ring.finish()


def spread(blocks, count):
    return -(-blocks // count) * count


def feed_forward(x, low, full_out, my_gate, my_up, my_down, all_g, gain, units, wide):
    group, count = lax.axis_size("fsdp"), lax.axis_size("ctx")
    rows, width = x.shape
    hidden = my_gate.shape[1]
    blocks = spread(hidden // LANES * (width // group // 16), wide_split(width) * count)
    chips = group // 2
    dma = pltpu.SemaphoreType.DMA((2 * chips - 1,))
    bf16 = jnp.bfloat16
    down_chunks = [(per, 16, width) for per in down_split(hidden // 16, count)]
    return pl.pallas_call(
        ffn_kernel,
        out_shape=[
            jax.ShapeDtypeStruct((rows, width), jnp.float32),
            jax.ShapeDtypeStruct((group, rows, width), bf16),
            jax.ShapeDtypeStruct((rows, width), jnp.float32),
            jax.ShapeDtypeStruct((rows, width), bf16),
            jax.ShapeDtypeStruct((units, 2 * HD, wide), bf16),
            jax.ShapeDtypeStruct((group, blocks, 16, LANES), bf16),
            jax.ShapeDtypeStruct((group, blocks, 16, LANES), bf16),
            *[jax.ShapeDtypeStruct(chunk, bf16) for chunk in down_chunks],
            jax.ShapeDtypeStruct((1, width), jnp.float32),
        ],
        in_specs=[VMEM] * 8,
        out_specs=[VMEM] * (8 + len(down_chunks)),
        scratch_shapes=[
            pltpu.VMEM((group, rows, width), bf16),
            pltpu.VMEM((width, group * rows), bf16),
            pltpu.VMEM((hidden, group * rows), bf16),
            pltpu.VMEM((group, rows, hidden), bf16),
            pltpu.VMEM((group, rows, hidden), bf16),
            pltpu.VMEM((group, rows, hidden), bf16),
            pltpu.VMEM((rows, width), jnp.float32),
            pltpu.VMEM((rows, width), jnp.float32),
            *[kind for chunk in down_chunks for kind in ring_scratch(chunk)],
            *scatter_scratch(rows, width),
            *[dma] * 4,
            *[kind for _ in down_chunks for kind in ring_semaphores()],
        ],
        compiler_params=pltpu.CompilerParams(
            collective_id=2, has_side_effects=True, vmem_limit_bytes=60 << 20
        ),
    )(x, low, full_out, my_gate, my_up, my_down, all_g, gain)


def back_kernel(
    down_blocks, q_ref, g_ref, log_ref, gain_grad_ref, gain_ref, cos_ref, sin_ref,
    pairs_ref, mix_in, gate_ref, up_ref, layer_base_in, layer_part_ref, branch_ref, low_t_ref,
    normed_t_ref, w_query_in, w_key_in, w_value_in, x_in, resid_grad_in, *rest,
):
    taken = iter(rest)

    def take(number):
        return [next(taken) for _ in range(number)]

    halves, downs = wide_split(x_in.shape[1]), len(down_blocks)
    down_refs = take(downs)
    tokens_ref, layer_ref = take(2)
    wide_totals, down_totals = take(2 * halves), take(downs)
    out_a_total, out_b_total, rest_a_total, rest_b_total = take(4)
    peer_got, chain_got, layer_sib, layer_cross, layer_far = take(5)
    kv_ref, stage_ref, final_ref, qg_ref, delta_ref, grad_q_ref = take(6)
    wide_scratch = take(4 * halves)
    out_a_work, out_a_land, out_b_work, out_b_land = take(4)
    rest_a_work, rest_a_land, rest_b_work, rest_b_land = take(4)
    low_all, normed_all, branch_all, query_all, pair_all, upstream_ref, gain_give, gain_got = take(8)
    far_ref, layer_stage = take(2)
    mix_ref, layer_base_ref, w_query_ref, w_key_ref, w_value_ref, x_ref, resid_grad_ref = take(7)
    steps = Steps()
    fsdp, ctx, group, count = steps.fsdp, steps.ctx, lax.axis_size("fsdp"), lax.axis_size("ctx")
    units, deep, wide = q_ref.shape
    keys = pairs_ref.shape[2]
    rows, width = x_ref.shape
    own = width // group
    wide_rings = [
        Ring(*wide_scratch[2 * at : 2 * at + 2], wide_totals[at], take(5), at < halves, True)
        for at in range(2 * halves)
    ]
    down_rings = [SpreadRing(total, take(2), at % 2 == 0) for at, total in enumerate(down_totals)]
    out_a = Ring(out_a_work, out_a_land, out_a_total, take(2), True)
    out_b = Ring(out_b_work, out_b_land, out_b_total, take(2), False)
    layer_sum = GroupScatter(
        None,
        layer_sib,
        lambda step: layer_part_ref.at[
            2 * lax.rem(lax.div(fsdp, 2) + group // 2 - step, group // 2) + 1 - lax.rem(fsdp, 2)
        ],
        layer_cross,
        far_ref,
        layer_far,
        *take(2),
    )
    layer_sum.give_sib = layer_part_ref.at[layer_sum.sibling]
    rest_a = Ring(rest_a_work, rest_a_land, rest_a_total, take(2), True)
    rest_b = Ring(rest_b_work, rest_b_land, rest_b_total, take(2), False)
    first_rings = []
    for at in range(halves):
        first_rings += [wide_rings[at], wide_rings[halves + at]]
        first_rings += down_rings[at * downs // halves : (at + 1) * downs // halves]
    begun_rings = len(first_rings)
    first_rings += [out_a, out_b]
    peer_sends, peer_arrivals, chain_sends, chain_arrivals = take(4)
    branch_gather = GroupGather(lambda shard: branch_all.at[shard], *take(2))
    query_gather = GroupGather(lambda shard: query_all.at[shard], *take(2))
    pair_gather = GroupGather(lambda shard: pair_all.at[shard], *take(2))
    low_sends, low_arrivals, normed_sends, normed_arrivals, gain_sends, gain_arrivals = take(6)
    local_sems, stage_sems = take(2)

    barrier = pltpu.get_barrier_semaphore()
    greeted = steps.greet(barrier) + greet_group(barrier) + 2
    for device in (out_a.after, out_b.after):
        pl.semaphore_signal(barrier, inc=1, device_id=device, device_id_type=MESH)

    loads = []

    def load(source, target):
        copy = pltpu.make_async_copy(source, target, local_sems.at[len(loads)])
        copy.start()
        loads.append(copy)

    n = wide_scratch[0].shape[2]
    for at, ring in enumerate(wide_rings):
        source = (gate_ref, up_ref)[at // halves]
        for chunk in range(count):
            load(source.at[:, pl.ds((at % halves * count + chunk) * n, n)], ring.work.at[chunk])
    for ring, source in zip(down_rings, down_refs):
        load(source, ring.chunk(ring.total, ring.first))
    ring_loads = len(loads)
    load(pairs_ref, kv_ref)
    load(mix_in, mix_ref)
    load(branch_ref, branch_all.at[fsdp])
    load(low_t_ref.at[pl.ds(fsdp * own, own)], low_all.at[:, lane_tile(fsdp, rows)])
    load(normed_t_ref.at[pl.ds(fsdp * own, own)], normed_all.at[:, lane_tile(fsdp, rows)])
    slot_loads = len(loads)
    for source, target in (
        (layer_base_in, layer_base_ref),
        (w_query_in, w_query_ref),
        (w_key_in, w_key_ref),
        (w_value_in, w_value_ref),
        (x_in, x_ref),
        (resid_grad_in, resid_grad_ref),
    ):
        load(source, target)
    for copy in loads[:ring_loads]:
        copy.wait()
    pl.semaphore_wait(barrier, greeted)
    for ring in first_rings[:begun_rings]:
        ring.start()
    branch_gather.start(branch_ref)
    layer_sum.to_sibling().start()
    for step in range(1, group // 2):
        layer_sum.to_cross(step).start()

    def slices(source, target, sends, arrivals, step):
        peer = lax.rem(fsdp + step, group)
        return pltpu.make_async_remote_copy(
            src_ref=source.at[pl.ds(peer * own, own)],
            dst_ref=target.at[:, lane_tile(fsdp, rows)],
            send_sem=sends.at[step - 1],
            recv_sem=arrivals.at[step - 1],
            device_id=(peer, ctx),
            device_id_type=MESH,
        )

    turned = [
        slices(*ends, step)
        for ends in (
            (low_t_ref, low_all, low_sends, low_arrivals),
            (normed_t_ref, normed_all, normed_sends, normed_arrivals),
        )
        for step in range(1, group)
    ]
    for copy in turned:
        copy.start()

    def prepare(unit):
        q, g = q_ref[unit], g_ref[unit]
        qg_ref[unit, :wide] = q.T
        qg_ref[unit, wide:] = g.T
        delta_ref[unit] = jnp.sum(
            g[HD:].astype(jnp.float32) * mix_ref[unit], axis=0, keepdims=True
        )
        grad_q_ref[unit] = jnp.zeros((HD, wide), jnp.float32)

    for copy in loads[ring_loads:slot_loads]:
        copy.wait()
    tiles(units, prepare)

    def tick(ring, at):
        @pl.when(jnp.logical_and(at >= 0, at < ring.ticks))
        def _():
            ring.tick(jnp.clip(at, 0, ring.ticks - 1))

    late = steps.levels // 2 + 1

    def pump(at):
        lag = [0] * begun_rings + [late, late]
        for turn, ring in enumerate(first_rings):

            @pl.when(lax.rem(at, len(first_rings)) == turn)
            def _():
                tick(ring, lax.div(at, len(first_rings)) - lag[turn])

    def back(unit, first, blocks, diagonal):
        kv = kv_ref[pl.ds(first, blocks), unit].reshape(blocks * keys, deep)
        scores = jnp.dot(kv, q_ref[unit], preferred_element_type=jnp.float32)
        probs = jnp.exp(scores - log_ref[unit])
        if diagonal:
            probs = jnp.where(causal(keys, wide, scores.shape), probs, 0.0)
        grad_probs = jnp.dot(kv, g_ref[unit], preferred_element_type=jnp.float32)
        grad_scores = (probs * (grad_probs - delta_ref[unit])).astype(jnp.bfloat16)
        both = jnp.concatenate([grad_scores, probs.astype(jnp.bfloat16)], axis=1)
        grad_kv = jnp.dot(both, qg_ref[unit], preferred_element_type=jnp.float32)
        added = jnp.dot(kv.T, grad_scores, preferred_element_type=jnp.float32)
        grad_q_ref[unit] = grad_q_ref[unit] + added[:HD]
        kv_ref[pl.ds(first, blocks), unit] = grad_kv.astype(kv_ref.dtype).reshape(
            blocks, keys, deep
        )

    def across(pair):
        return pltpu.make_async_remote_copy(
            src_ref=kv_ref.at[2 * pair + 1 - steps.side],
            dst_ref=peer_got.at[pair],
            send_sem=peer_sends.at[pair],
            recv_sem=peer_arrivals.at[pair],
            device_id=steps.peer,
            device_id_type=MESH,
        )

    def down_chain(pair):
        return pltpu.make_async_remote_copy(
            src_ref=kv_ref.at[2 * pair + steps.side],
            dst_ref=chain_got.at[pair],
            send_sem=chain_sends.at[pair],
            recv_sem=chain_arrivals.at[pair],
            device_id=steps.below,
            device_id_type=MESH,
        )

    def combine(time):
        pair = time - steps.levels + steps.level

        @pl.when(jnp.logical_and(pair >= 0, pair <= steps.level))
        def _():
            for slot, expected, arrival, source in (
                (0, jnp.logical_or(pair < steps.level, steps.side == 0), across, peer_got),
                (1, steps.has_above, down_chain, chain_got),
            ):

                @pl.when(expected)
                def _():
                    arrival(pair).wait_recv()
                    copy = pltpu.make_async_copy(
                        source.at[pair], stage_ref.at[slot], stage_sems.at[slot]
                    )
                    copy.start()
                    copy.wait()

                @pl.when(jnp.logical_not(expected))
                def _():
                    stage_ref[slot] = jnp.zeros(stage_ref.shape[1:], stage_ref.dtype)

            def add(unit):
                final_ref[unit] = (
                    kv_ref[2 * pair + steps.side, unit].astype(jnp.float32)
                    + stage_ref[0, unit].astype(jnp.float32)
                    + stage_ref[1, unit].astype(jnp.float32)
                )

            tiles(units, add)

            @pl.when(pair < steps.level)
            def _():
                kv_ref[2 * pair + steps.side] = final_ref[...].astype(kv_ref.dtype)
                down_chain(pair).start()

    row_blocks = own // 16

    def weight_grad(left, right, begin, end, target, first, loop):
        span = LANES * next(n for n in (3, 2, 1) if (end - begin) % (n * LANES) == 0)

        def body(at):
            columns = pl.ds(pl.multiple_of(begin + at * span, LANES), span)
            part = forward_dot(
                left[...], right[:, :, columns].reshape(group * rows, span)
            ).astype(jnp.bfloat16)
            for block in range(span // LANES):
                here = first + (at * (span // LANES) + block) * row_blocks
                target[pl.ds(here, row_blocks)] = part[
                    :, block * LANES : (block + 1) * LANES
                ].reshape(row_blocks, 16, LANES)

        loop((end - begin) // span, body)
        return first + (end - begin) // LANES * row_blocks

    def clear_from(target, first):
        for spare in range(first, target.shape[0]):
            target[spare] = jnp.zeros((16, LANES), jnp.bfloat16)

    def out_grad():
        for copy in turned[: group - 1]:
            copy.wait_recv()
        branch_gather.forward()
        branch_gather.sibling_here()
        for step in range(1, branch_gather.chips):
            branch_gather.crossed(step)
        split = out_split(width)
        clear_from(out_a_work, weight_grad(low_all, branch_all, 0, split, out_a_work, 0, tiles))
        clear_from(out_b_work, weight_grad(low_all, branch_all, split, width, out_b_work, 0, tiles))
        out_a.start()
        out_b.start()

    turns = units // 2
    rings = max(turns, len(first_rings))

    def slot(pair):
        def turn(at):
            @pl.when(pair < steps.level)
            def _():
                for unit in (2 * at, 2 * at + 1):
                    back(unit, 2 * pair, 2, False)

            @pl.when(pair == steps.level)
            def _():
                for unit in (2 * at, 2 * at + 1):
                    back(unit, ctx, 1, True)

            @pl.when(jnp.logical_and(pair == steps.level, steps.side == 1))
            def _():
                for unit in (2 * at, 2 * at + 1):
                    back(unit, ctx - 1, 1, False)

            pump(pair * rings + at)

        tiles(turns, turn)
        tiles(rings - turns, lambda at: pump(pair * rings + turns + at))

        @pl.when(jnp.logical_or(pair < steps.level, (pair == steps.level) & (steps.side == 1)))
        def _():
            across(pair).start()

        combine(pair)

        @pl.when(pair == late - 1)
        def _():
            out_grad()

    tiles(steps.levels, slot)
    pumped = [steps.levels * rings]

    def pump_next(times=1):
        def body(at, unused, begin=pumped[0]):
            pump(begin + at)
            return unused

        lax.fori_loop(0, times, body, 0)
        pumped[0] += times

    def pumping(times, body):
        begin = pumped[0]

        def step(at):
            body(at)
            pump(begin + 2 * at)
            pump(begin + 2 * at + 1)

        tiles(times, step)
        pumped[0] += 2 * times

    cosine, sine = cos_ref[...], sin_ref[...]

    def unturn(columns):
        first, second = columns[: HD // 2], columns[HD // 2 :]
        return jnp.concatenate(
            [first * cosine + second * sine, second * cosine - first * sine], axis=0
        )

    sequences = units // KVH
    groups = wide // keys
    for sequence in range(sequences):
        span = slice(sequence * keys, (sequence + 1) * keys)
        for pair in range(H // 2):
            heads = []
            for head in (2 * pair, 2 * pair + 1):
                unit, member = sequence * KVH + head // groups, head % groups
                part = grad_q_ref[unit, :, member * keys : (member + 1) * keys]
                heads.append(unturn(part * HD ** (-0.5)))
            query_all[fsdp, span, pair * 2 * HD : (pair + 1) * 2 * HD] = (
                jnp.concatenate(heads, axis=0).astype(jnp.bfloat16).T
            )
            if pair % 3 == 2:
                pump_next()
    query_gather.start(query_all.at[fsdp])
    combine(steps.levels)
    kv_width = KVH * HD
    for sequence in range(sequences):
        span = slice(sequence * keys, (sequence + 1) * keys)
        for pair in range(KVH // 2):
            turned_keys, turned_values = [], []
            for unit in (sequence * KVH + 2 * pair, sequence * KVH + 2 * pair + 1):
                part = final_ref[unit].T
                turned_keys.append(unturn(part[:HD]))
                turned_values.append(part[HD:])
            for start, parts in ((0, turned_keys), (kv_width, turned_values)):
                pair_all[fsdp, span, start + pair * 2 * HD : start + (pair + 1) * 2 * HD] = (
                    jnp.concatenate(parts, axis=0).astype(jnp.bfloat16).T
                )
    pair_gather.start(pair_all.at[fsdp])
    pump_next(2)
    query_gather.forward()
    step_out = width_tile(width)

    def upstream_tile(at):
        columns = pl.ds(pl.multiple_of(at * step_out, LANES), step_out)
        upstream_ref[:, columns] = (
            dot_columns(query_all[fsdp], w_query_ref[columns, :])
            + dot_columns(pair_all[fsdp, :, :kv_width], w_key_ref[columns, :])
            + dot_columns(pair_all[fsdp, :, kv_width:], w_value_ref[columns, :])
        )

    for copy in loads[slot_loads:]:
        copy.wait()
    pumping(width // step_out, upstream_tile)
    inputs = x_ref[...].astype(jnp.float32)
    scale = norm_scale(inputs)
    upstream = upstream_ref[...]
    scaled = upstream * gain_ref[...]
    tokens_ref[...] = (
        resid_grad_ref[...]
        + scale * scaled
        - inputs * scale**3 * jnp.mean(scaled * inputs, axis=-1, keepdims=True)
    )
    gain_attn = jnp.sum(upstream * inputs * scale, axis=0, keepdims=True)
    lanes = width // LANES
    gain_give[...] = jnp.zeros(gain_give.shape, jnp.float32)
    for block in range(lanes):
        columns = slice(block * LANES, (block + 1) * LANES)
        gain_give[block : block + 1, :] = gain_attn[:, columns]
        gain_give[lanes + block : lanes + block + 1, :] = gain_grad_ref[:, columns]

    def gain_copy(step):
        peer = lax.rem(fsdp + step, group)
        return pltpu.make_async_remote_copy(
            src_ref=gain_give,
            dst_ref=gain_got.at[step - 1],
            send_sem=gain_sends.at[step - 1],
            recv_sem=gain_arrivals.at[step - 1],
            device_id=(peer, ctx),
            device_id_type=MESH,
        )

    for step in range(1, group):
        gain_copy(step).start()
    pump_next()
    for copy in turned[group - 1 :]:
        copy.wait_recv()
    query_gather.sibling_here()
    for step in range(1, query_gather.chips):
        query_gather.crossed(step)
    split = query_split(width)
    filled_a = weight_grad(normed_all, query_all, 0, split, rest_a_work, 0, pumping)
    filled_b = weight_grad(normed_all, query_all, split, width, rest_b_work, 0, pumping)
    pair_gather.forward()
    pump_next()
    pair_gather.sibling_here()
    for step in range(1, pair_gather.chips):
        pair_gather.crossed(step)
    filled_b = weight_grad(normed_all, pair_all, 0, 2 * kv_width, rest_b_work, filled_b, pumping)
    for step in range(1, layer_sum.chips):
        ours = layer_part_ref.at[2 * lax.rem(layer_sum.chip + layer_sum.chips - step, layer_sum.chips) + layer_sum.core]
        for source, target in ((ours, far_ref.at[step - 1]), (layer_cross.at[step - 1], layer_stage)):
            if source is not ours:
                layer_sum.to_cross(step).wait_recv()
            copy = pltpu.make_async_copy(source, target, stage_sems.at[0])
            copy.start()
            copy.wait()
        far_ref[step - 1] = (
            far_ref[step - 1].astype(jnp.float32) + layer_stage[...].astype(jnp.float32)
        ).astype(jnp.bfloat16)
        layer_sum.to_far(step).start()
    gains = gain_give[...]
    for step in range(1, group):
        gain_copy(step).wait_recv()
        gains = gains + gain_got[step - 1]
    gain_tiles = gains.shape[0] // 16
    rest_a_work[filled_a : filled_a + gain_tiles] = gains.astype(jnp.bfloat16).reshape(
        gain_tiles, 16, LANES
    )
    clear_from(rest_a_work, filled_a + gain_tiles)
    clear_from(rest_b_work, filled_b)
    rest_a.start()
    rest_b.start()
    begun = pumped[0]
    total_pumps = max(wide_rings[0].ticks, late + out_a.ticks) * len(first_rings)

    half = -(-(total_pumps - begun) // rest_a.ticks)

    def last_ticks(at, unused):
        for turn in range(half):
            pump(jnp.minimum(begun + half * at + turn, total_pumps))
        tick(rest_a, at)
        tick(rest_b, at)
        return unused

    lax.fori_loop(0, rest_a.ticks, last_ticks, 0)
    layer_sum.to_sibling().wait_recv()
    layer = layer_base_ref[...]
    arrived = [layer_sib]
    for step in range(1, layer_sum.chips):
        layer_sum.to_far(step).wait_recv()
        arrived.append(layer_far.at[step - 1])
    for source in arrived:
        copy = pltpu.make_async_copy(source, layer_stage, stage_sems.at[0])
        copy.start()
        copy.wait()
        layer = layer + layer_stage[...].astype(jnp.float32)
    layer_ref[...] = layer.astype(jnp.bfloat16)
    layer_sum.sent()
    for ring in first_rings + [rest_a, rest_b]:
        ring.finish()
    for copy in turned:
        copy.wait_send()
    for gather in (branch_gather, query_gather, pair_gather):
        gather.sent()
    for step in range(1, group):
        gain_copy(step).wait_send()

    def sent(pair):
        @pl.when(jnp.logical_or(pair < steps.level, steps.side == 1))
        def _():
            across(pair).wait_send()

        @pl.when(pair < steps.level)
        def _():
            down_chain(pair).wait_send()

    tiles(steps.level + 1, sent)


def layer_back(
    q_wide, g_wide, log_total, gain_grad, gain, cosine, sine, all_pairs, mix, gate_part, up_part,
    layer_base, layer_parts, branch, low_t, normed_t, w_query, w_key, w_value, x, resid_grad, downs,
):
    group, count = lax.axis_size("fsdp"), lax.axis_size("ctx")
    units, deep, wide = q_wide.shape
    keys = all_pairs.shape[2]
    rows, width = x.shape
    own, kv_width = width // group, w_key.shape[1]
    bf16, f32 = jnp.bfloat16, jnp.float32
    dma = pltpu.SemaphoreType.DMA
    halves = wide_split(width)
    wide_chunk = (group, gate_part.shape[1] // (halves * count), 16, LANES)
    gain_rows = spread(2 * (width // LANES), 16)
    split, row_blocks = query_split(width), own // 16
    out_first = out_split(width)
    chips = group // 2
    small_chunks = [
        (spread(held, count) // count, 16, LANES)
        for held in (
            out_first // LANES * row_blocks,
            (width - out_first) // LANES * row_blocks,
            split // LANES * row_blocks + gain_rows // 16,
            (width - split + 2 * kv_width) // LANES * row_blocks,
        )
    ]
    levels = count // 2
    loaded = [mix, layer_base, w_query, w_key, w_value, x, resid_grad]
    return pl.pallas_call(
        functools.partial(back_kernel, [part.shape[0] for part in downs]),
        out_shape=[
            jax.ShapeDtypeStruct((rows, width), f32),
            jax.ShapeDtypeStruct((rows, width), bf16),
            *[ring_total(wide_chunk, True)] * (2 * halves),
            *[ring_total(part.shape) for part in downs],
            *[ring_total(chunk) for chunk in small_chunks],
            *[jax.ShapeDtypeStruct((levels, units, keys, deep), bf16)] * 2,
            jax.ShapeDtypeStruct((rows, width), bf16),
            *[jax.ShapeDtypeStruct((chips - 1, rows, width), bf16)] * 2,
        ],
        in_specs=[VMEM] * 7 + [ANY] * (14 + len(downs)),
        out_specs=[VMEM] * (6 + 2 * halves + len(downs)) + [ANY] * 5,
        scratch_shapes=[
            pltpu.VMEM(all_pairs.shape, bf16),
            pltpu.VMEM((2, units, keys, deep), bf16),
            pltpu.VMEM((units, keys, deep), f32),
            pltpu.VMEM((units, 2 * wide, deep), bf16),
            pltpu.VMEM((units, 1, wide), f32),
            pltpu.VMEM((units, HD, wide), f32),
            *[kind for _ in range(2 * halves) for kind in ring_scratch(wide_chunk, True)],
            *[kind for chunk in small_chunks for kind in ring_scratch(chunk)],
            pltpu.VMEM((own, group * rows), bf16),
            pltpu.VMEM((own, group * rows), bf16),
            pltpu.VMEM((group, rows, width), bf16),
            pltpu.VMEM((group, rows, width), bf16),
            pltpu.VMEM((group, rows, 2 * kv_width), bf16),
            pltpu.VMEM((rows, width), f32),
            pltpu.VMEM((gain_rows, LANES), f32),
            pltpu.VMEM((group - 1, gain_rows, LANES), f32),
            pltpu.VMEM((chips - 1, rows, width), bf16),
            pltpu.VMEM((rows, width), bf16),
            *[pltpu.VMEM(array.shape, array.dtype) for array in loaded],
            *[kind for _ in range(2 * halves) for kind in ring_semaphores(True)],
            *[kind for _ in range(len(downs) + 2) for kind in ring_semaphores()],
            *[dma((group - 1,))] * 2,
            *[kind for _ in range(2) for kind in ring_semaphores()],
            *[dma((levels,))] * 4,
            *[group_semaphores()] * 6,
            *[dma((group - 1,))] * 6,
            dma((11 + len(downs) + 2 * halves * count,)),
            dma((2,)),
        ],
        compiler_params=pltpu.CompilerParams(
            collective_id=3, has_side_effects=True, vmem_limit_bytes=62 << 20
        ),
    )(
        q_wide, g_wide, log_total, gain_grad, gain, cosine, sine, all_pairs, mix, gate_part, up_part,
        layer_base, layer_parts, branch, low_t, normed_t, w_query, w_key, w_value, x, resid_grad,
        *downs,
    )


def finish_kernel(halves, downs, *refs):
    wides, refs = refs[: 2 * halves], refs[2 * halves :]
    down_refs, refs = refs[:downs], refs[downs:]
    out_a_ref, out_b_ref, rest_a_ref, rest_b_ref = refs[:4]
    query_grad, key_grad, value_grad, out_grad, gate_grad, up_grad, down_grad = refs[4:]
    rows = gate_grad.shape[0]
    row_blocks = rows // 16
    for sources, target in ((wides[:halves], gate_grad), (wides[halves:], up_grad)):
        held = jnp.concatenate(
            [source[...].reshape((-1,) + source.shape[3:]) for source in sources], axis=0
        )
        for block in range(target.shape[1] // LANES):
            target[:, block * LANES : (block + 1) * LANES] = (
                held[block * row_blocks : (block + 1) * row_blocks]
                .reshape(rows, LANES)
                .astype(jnp.float32)
            )

    @pl.when(pl.program_id(0) == 0)
    def _():
        def unpack(source, first, target, begin, end):
            for block in range(begin, end):
                here = first + (block - begin) * row_blocks
                target[:, block * LANES : (block + 1) * LANES] = (
                    source[here : here + row_blocks].reshape(rows, LANES).astype(jnp.float32)
                )
            return first + (end - begin) * row_blocks

        width, kv_width = query_grad.shape[1], key_grad.shape[1]
        split = query_split(width) // LANES
        middle = out_split(width) // LANES
        unpack(out_a_ref, 0, out_grad, 0, middle)
        unpack(out_b_ref, 0, out_grad, middle, width // LANES)
        unpack(rest_a_ref, 0, query_grad, 0, split)
        at = unpack(rest_b_ref, 0, query_grad, split, width // LANES)
        at = unpack(rest_b_ref, at, key_grad, 0, kv_width // LANES)
        unpack(rest_b_ref, at, value_grad, 0, kv_width // LANES)
        blocks, begin = down_grad.shape[0] // 16, 0
        for source in down_refs:
            end = min(blocks, begin + source.shape[0])
            if end > begin:
                down_grad[begin * 16 : end * 16, :] = (
                    source[: end - begin]
                    .reshape((end - begin) * 16, down_grad.shape[1])
                    .astype(jnp.float32)
                )
            begin = end


def finish(wides, downs, smalls, own, width, kv_width, hidden):
    count, group, n = wides[0].shape[:3]

    def whole(array):
        return pl.BlockSpec(array.shape, lambda part, rank=len(array.shape): (0,) * rank)

    wide = pl.BlockSpec((count, 1, n, 16, LANES), lambda part: (0, part, 0, 0, 0))
    outs = [
        jax.ShapeDtypeStruct((own, columns), jnp.float32)
        for columns in (width, kv_width, kv_width, width, FF, FF)
    ] + [jax.ShapeDtypeStruct((hidden, width), jnp.float32)]
    slice_spec = pl.BlockSpec((own, FF // group), lambda part: (0, part))
    return pl.pallas_call(
        functools.partial(finish_kernel, len(wides) // 2, len(downs)),
        grid=(group,),
        out_shape=outs,
        in_specs=[wide] * len(wides) + [whole(a) for a in (*downs, *smalls)],
        out_specs=[whole(a) for a in outs[:4]] + [slice_spec, slice_spec, whole(outs[6])],
        compiler_params=pltpu.CompilerParams(vmem_limit_bytes=60 << 20),
    )(*wides, *downs, *smalls)


def on_device(
    tokens, w_query, w_key, w_value, w_out, w_gate, w_up, w_down, gain_attn, gain_ffn, cotangent
):
    block_len, seq_count, width = tokens.shape
    rows_count = block_len * seq_count
    kv_width = KVH * HD
    positions = lax.axis_index("ctx") * block_len + jnp.arange(block_len, dtype=jnp.int32)
    freqs = ROTARY_BASE ** (-2.0 * jnp.arange(HD // 2, dtype=jnp.float32) / HD)
    angles = freqs[:, None] * positions.astype(jnp.float32)[None, :]
    cosine, sine = jnp.cos(angles), jnp.sin(angles)
    x_rows = jnp.swapaxes(tokens, 0, 1).reshape(rows_count, width)
    g_rows = jnp.swapaxes(cotangent, 0, 1).reshape(rows_count, width)
    own = gain_attn.shape[0]
    units = seq_count * KVH
    wide = H // KVH * block_len
    own_gains = jnp.pad(
        jnp.stack([gain_attn, gain_ffn]).astype(jnp.float32), ((0, 6), (0, spread(own, LANES) - own))
    )
    (
        q_wide, normed_t, gains, full_query, full_key, full_value, attn_low, low_t, mix_unit, log_total,
        all_pairs, full_out, my_gate, my_up, all_g,
    ) = attend(
        x_rows, own_gains, cosine, sine, w_query, w_key, w_value, w_out, w_gate, w_up, g_rows, seq_count
    )
    layer_base, layer_parts, grad_resid, grad_branch, g_wide, gate_part, up_part, *downs = (
        feed_forward(
            x_rows, attn_low, full_out, my_gate, my_up, w_down, all_g, gains[1:2], units, wide
        )
    )
    downs, gain_term_ffn = downs[:-1], downs[-1]
    grad_tokens, layer_out, *sums = layer_back(
        q_wide, g_wide, log_total, gain_term_ffn, gains[:1], cosine, sine, all_pairs, mix_unit,
        gate_part, up_part, layer_base, layer_parts, grad_branch, low_t, normed_t, full_query,
        full_key, full_value, x_rows, grad_resid, downs,
    )
    wides, sums = sums[: 2 * wide_split(width)], sums[2 * wide_split(width) :]
    smalls = sums[len(downs) : len(downs) + 4]
    filled = query_split(width) // LANES * (own // 16)
    gain_grads = smalls[2][filled:].reshape(-1, LANES)[: 2 * (width // LANES)].reshape(2, width)
    gain_grads = lax.dynamic_slice_in_dim(gain_grads, lax.axis_index("fsdp") * own, own, 1)
    gain_grads = gain_grads.astype(jnp.float32)
    grads = finish(wides, sums[: len(downs)], smalls, own, width, kv_width, w_down.shape[0])
    return (
        jnp.swapaxes(layer_out.reshape(seq_count, block_len, width), 0, 1),
        jnp.swapaxes(grad_tokens.reshape(seq_count, block_len, width), 0, 1),
        *grads,
        gain_grads[0],
        gain_grads[1],
    )


def solution(mesh):
    return jax.shard_map(
        on_device,
        mesh=mesh,
        in_specs=(
            P("ctx", "fsdp", None),
            P("fsdp", None),
            P("fsdp", None),
            P("fsdp", None),
            P("fsdp", None),
            P("fsdp", None),
            P("fsdp", None),
            P("fsdp", None),
            P("fsdp"),
            P("fsdp"),
            P("ctx", "fsdp", None),
        ),
        out_specs=(
            P("ctx", "fsdp", None),
            P("ctx", "fsdp", None),
            P("fsdp", None),
            P("fsdp", None),
            P("fsdp", None),
            P("fsdp", None),
            P("fsdp", None),
            P("fsdp", None),
            P("fsdp", None),
            P("fsdp"),
            P("fsdp"),
        ),
        check_vma=False,
    )
```

```python
import functools

import jax
import jax.numpy as jnp
from jax import lax
from jax.experimental import pallas as pl
from jax.experimental.pallas import tpu as pltpu
from jax.sharding import PartitionSpec as P

H = 18
KVH = 6
HD = 64
FF = 3072


EPSILON = 1e-05
ROTARY_BASE = 10000.0
MASKED_SCORE = -1e30


def norm_scale(rows):
    return lax.rsqrt(jnp.mean(rows * rows, axis=-1, keepdims=True) + EPSILON)


def forward_dot(left, right):
    return jnp.dot(left, right, preferred_element_type=jnp.float32)


MESH = pl.DeviceIdType.MESH
LANES = 128


def ring_place(ctx, fsdp, count):
    column, side = lax.div(ctx, 2), lax.rem(ctx, 2)
    place = column + side * (count - 1 - 2 * column)
    odd = lax.rem(fsdp, 2)
    return place + odd * (count - 1 - 2 * place)


def ring_ctx(place, fsdp, count):
    odd = lax.rem(fsdp, 2)
    place = place + odd * (count - 1 - 2 * place)
    late = lax.div(place, count // 2)
    return (1 - late) * 2 * place + late * (2 * (count - 1 - place) + 1)


class GroupGather:
    def __init__(self, shard_of, sends, arrivals):
        self.shard_of, self.sends, self.arrivals = shard_of, sends, arrivals
        self.fsdp, self.ctx = lax.axis_index("fsdp"), lax.axis_index("ctx")
        self.chips = lax.axis_size("fsdp") // 2
        self.chip, self.core = lax.div(self.fsdp, 2), lax.rem(self.fsdp, 2)
        self.sibling = 2 * self.chip + 1 - self.core

    def copy(self, source, shard, semaphore, device):
        return pltpu.make_async_remote_copy(
            src_ref=source,
            dst_ref=self.shard_of(shard),
            send_sem=self.sends.at[semaphore],
            recv_sem=self.arrivals.at[semaphore],
            device_id=(device, self.ctx),
            device_id_type=MESH,
        )

    def same_core(self, step):
        return 2 * lax.rem(self.chip + step, self.chips) + self.core

    def across(self, source):
        return self.copy(source, self.fsdp, 0, self.sibling)

    def out(self, source, step):
        return self.copy(source, self.fsdp, step, self.same_core(step))

    def onward(self, step):
        shard = self.same_core(self.chips - step)
        return self.copy(self.shard_of(shard), shard, self.chips - 1 + step, self.sibling)

    def start(self, source):
        for step in range(1, self.chips):
            self.out(source, step).start()
        self.across(source).start()

    def forward(self):
        own = self.shard_of(self.fsdp)
        for step in range(1, self.chips):
            self.out(own, step).wait_recv()
            self.onward(step).start()

    def sibling_here(self):
        self.across(self.shard_of(self.fsdp)).wait_recv()

    def crossed(self, step):
        self.onward(step).wait_recv()

    def sent(self):
        own = self.shard_of(self.fsdp)
        self.across(own).wait_send()
        for step in range(1, self.chips):
            self.out(own, step).wait_send()
            self.onward(step).wait_send()

    def finish(self):
        self.forward()
        self.sibling_here()
        for step in range(1, self.chips):
            self.crossed(step)
        self.sent()


class HalfGather:
    def __init__(self, held, own_rows, sends, arrivals):
        self.held, self.own = held, own_rows
        self.sends, self.arrivals = sends, arrivals
        self.fsdp, self.ctx = lax.axis_index("fsdp"), lax.axis_index("ctx")
        self.chips = lax.axis_size("fsdp") // 2
        self.chip, self.core = lax.div(self.fsdp, 2), lax.rem(self.fsdp, 2)
        self.sibling = 2 * self.chip + 1 - self.core
        self.side = lax.rem(self.ctx, 2)
        self.pair = self.ctx + 1 - 2 * self.side
        first = -(-own_rows // 32) * 16
        self.halves = ((0, first), (first, own_rows - first))

    def same_core(self, step):
        return 2 * lax.rem(self.chip + step, self.chips) + self.core

    def rows(self, shard, half=None):
        begin, size = (0, self.own) if half is None else self.halves[half]
        return self.held.at[pl.ds(shard * self.own + begin, size)]

    def copy(self, source, target, semaphore, device):
        return pltpu.make_async_remote_copy(
            src_ref=source,
            dst_ref=target,
            send_sem=self.sends.at[semaphore],
            recv_sem=self.arrivals.at[semaphore],
            device_id=device,
            device_id_type=MESH,
        )

    def on_side(self, body):
        for half in range(2):

            @pl.when(self.side == half)
            def _(half=half):
                body(half)

    def across(self, source):
        return self.copy(source, self.rows(self.fsdp), 0, (self.sibling, self.ctx))

    def out(self, source, step, half):
        begin, size = self.halves[half]
        return self.copy(
            source.at[pl.ds(begin, size)],
            self.rows(self.fsdp, half),
            step,
            (self.same_core(step), self.ctx),
        )

    def to_pair(self, step, half):
        part = self.rows(self.same_core(self.chips - step), half)
        return self.copy(part, part, self.chips - 1 + step, (self.fsdp, self.pair))

    def onward(self, step):
        part = self.rows(self.same_core(self.chips - step))
        return self.copy(part, part, 2 * self.chips - 2 + step, (self.sibling, self.ctx))

    def start(self, source):
        def send(half):
            for step in range(1, self.chips):
                self.out(source, step, half).start()

        self.on_side(send)
        self.across(source).start()

    def to_pairs(self):
        def forward(half):
            for step in range(1, self.chips):
                self.out(self.rows(self.fsdp), step, half).wait_recv()
                self.to_pair(step, half).start()

        self.on_side(forward)

    def to_sibling(self):
        def forward(half):
            for step in range(1, self.chips):
                self.to_pair(step, 1 - half).wait_recv()

        self.on_side(forward)
        for step in range(1, self.chips):
            self.onward(step).start()

    def arrived(self):
        self.across(self.rows(self.fsdp)).wait_recv()
        for step in range(1, self.chips):
            self.onward(step).wait_recv()

    def sent(self):
        def wait(half):
            for step in range(1, self.chips):
                self.out(self.rows(self.fsdp), step, half).wait_send()
                self.to_pair(step, half).wait_send()

        self.on_side(wait)
        self.across(self.rows(self.fsdp)).wait_send()
        for step in range(1, self.chips):
            self.onward(step).wait_send()


class HalfSpread(HalfGather):
    def __init__(self, source, held, sends, arrivals):
        super().__init__(held, source.shape[0], sends, arrivals)
        self.source, self.columns = source, held.shape[1]

    def slice_for(self, peer):
        return self.source.at[:, lane_tile(peer, self.columns)]

    def others(self):
        return [(step, other) for step in range(1, self.chips) for other in range(2)]

    def device(self, step, other):
        return 2 * lax.rem(self.chip + step, self.chips) + lax.rem(self.core + other, 2)

    def near(self):
        return self.copy(
            self.slice_for(self.sibling), self.rows(self.fsdp), 0, (self.sibling, self.ctx)
        )

    def far(self, step, other, half):
        peer = self.device(step, other)
        begin, size = self.halves[half]
        return self.copy(
            self.slice_for(peer).at[pl.ds(begin, size)],
            self.rows(self.fsdp, half),
            2 * step - 1 + other,
            (peer, self.ctx),
        )

    def onto_pair(self, step, other, half):
        part = self.rows(self.device(self.chips - step, other), half)
        return self.copy(part, part, 2 * (self.chips - 1 + step) - 1 + other, (self.fsdp, self.pair))

    def start(self):
        def send(half):
            for step, other in self.others():
                self.far(step, other, half).start()

        self.on_side(send)
        self.near().start()

    def to_pairs(self):
        def forward(half):
            for step, other in self.others():
                self.far(step, other, half).wait_recv()
                self.onto_pair(step, other, half).start()

        self.on_side(forward)

    def finish(self):
        def wait(half):
            for step, other in self.others():
                self.onto_pair(step, other, 1 - half).wait_recv()
                self.far(step, other, half).wait_send()
                self.onto_pair(step, other, half).wait_send()

        self.on_side(wait)
        self.near().wait()


def spread_semaphores():
    return pltpu.SemaphoreType.DMA((2 * lax.axis_size("fsdp") - 3,))


def half_semaphores(many):
    return pltpu.SemaphoreType.DMA((many, 3 * (lax.axis_size("fsdp") // 2) - 2))


def group_semaphores():
    return pltpu.SemaphoreType.DMA((lax.axis_size("fsdp") - 1,))


def greet_group(barrier):
    fsdp, ctx, group = lax.axis_index("fsdp"), lax.axis_index("ctx"), lax.axis_size("fsdp")
    for step in range(1, group):
        peer = lax.rem(fsdp + step, group)
        pl.semaphore_signal(barrier, inc=1, device_id=(peer, ctx), device_id_type=MESH)
    return group - 1


class Steps:
    def __init__(self):
        self.fsdp, self.ctx = lax.axis_index("fsdp"), lax.axis_index("ctx")
        self.levels = lax.axis_size("ctx") // 2
        self.level, self.side = lax.div(self.ctx, 2), lax.rem(self.ctx, 2)
        self.peer = (self.fsdp, 2 * self.level + 1 - self.side)
        self.above = (self.fsdp, lax.rem(self.ctx + 2, 2 * self.levels))
        self.below = (self.fsdp, lax.rem(self.ctx + 2 * self.levels - 2, 2 * self.levels))
        self.has_above = self.level + 1 < self.levels
        self.has_below = self.level > 0

    def greet(self, barrier):
        pl.semaphore_signal(barrier, inc=1, device_id=self.peer, device_id_type=MESH)

        @pl.when(self.has_above)
        def _():
            pl.semaphore_signal(barrier, inc=1, device_id=self.above, device_id_type=MESH)

        @pl.when(self.has_below)
        def _():
            pl.semaphore_signal(barrier, inc=1, device_id=self.below, device_id_type=MESH)

        return 1 + jnp.minimum(self.level, 1) + jnp.minimum(self.levels - 1 - self.level, 1)


PARTS = 2


def causal(keys, wide, shape):
    key_at = lax.broadcasted_iota(jnp.int32, shape, 0)
    query_at = lax.rem(lax.broadcasted_iota(jnp.int32, shape, 1), keys)
    return key_at <= query_at


def attend_kernel(
    x_ref, gain_ref, cos_ref, sin_ref, query_ref, key_ref, value_ref, out_ref, gate_ref, up_ref, g_ref,
    q_ref, normed_t_ref, gains_ref, full_query, full_key, full_value,
    low_ref, low_t_ref, mix_ref, log_ref, all_ref, full_out_ref, my_gate_ref, my_up_ref, all_g_ref,
    normed_ref, key_rows, gain_all, own_out, own_gate, own_up, own_g,
    top_ref, total_ref, chain_sends, chain_arrivals, peer_sends, peer_arrivals,
    half_sends, half_arrivals, gain_sends, gain_arrivals,
    out_sends, out_arrivals, gate_sends, gate_arrivals, g_sends, g_arrivals,
    part_sends, part_arrivals, local_sems,
):
    steps = Steps()
    fsdp, ctx, group = steps.fsdp, steps.ctx, lax.axis_size("fsdp")
    units, deep, wide = q_ref.shape
    keys = all_ref.shape[2]
    per_part = units // PARTS
    rows_count, width = x_ref.shape
    own = query_ref.shape[0]
    sequences, groups = units // KVH, H // KVH
    barrier = pltpu.get_barrier_semaphore()
    greeted = steps.greet(barrier) + greet_group(barrier)
    span = KVH * HD
    pieces = [(key_ref, full_key, 0), (value_ref, full_value, 0)]
    pieces += [(query_ref, full_query, start) for start in range(0, width, span)]
    gathers = []
    for at, (source, target, start) in enumerate(pieces):
        columns = pl.ds(start, span)
        gather = HalfGather(
            target.at[:, columns], own, half_sends.at[at], half_arrivals.at[at]
        )
        gathers.append((gather, source.at[:, columns]))
    own_rows = pl.ds(fsdp * own, own)
    own_copies = [
        pltpu.make_async_copy(source, target.at[own_rows], local_sems.at[4 + at])
        for at, (source, target) in enumerate(
            ((key_ref, full_key), (value_ref, full_value), (query_ref, full_query))
        )
    ]
    for copy in own_copies:
        copy.start()
    gain_all[fsdp] = gain_ref[...]
    pl.semaphore_wait(barrier, greeted)

    def gain_copy(step):
        peer = lax.rem(fsdp + step, group)
        return pltpu.make_async_remote_copy(
            src_ref=gain_ref,
            dst_ref=gain_all.at[fsdp],
            send_sem=gain_sends.at[step - 1],
            recv_sem=gain_arrivals.at[step - 1],
            device_id=(peer, ctx),
            device_id_type=MESH,
        )

    for step in range(1, group):
        gain_copy(step).start()
    for gather, source in gathers:
        gather.start(source)
    inputs = x_ref[...].astype(jnp.float32)
    scale = norm_scale(inputs)
    q_ref[:, HD:, :] = jnp.zeros((units, HD, wide), q_ref.dtype)
    for step in range(1, group):
        gain_copy(step).wait_recv()
    gains = jnp.concatenate([gain_all[shard][:, :own] for shard in range(group)], axis=1)
    gains_ref[...] = gains
    normed_ref[...] = (inputs * scale * gains[:1]).astype(jnp.bfloat16)
    cosine, sine = cos_ref[...], sin_ref[...]

    def turn(columns):
        first, second = columns[: HD // 2], columns[HD // 2 :]
        return jnp.concatenate(
            [first * cosine - second * sine, second * cosine + first * sine], axis=0
        ).astype(jnp.bfloat16)

    def block_copy(level, part, side, semaphores, arrivals, arrives, device):
        block = 2 * (steps.level - level) + side
        held = all_ref.at[block, pl.ds(part * per_part, per_part)]
        return pltpu.make_async_remote_copy(
            src_ref=held,
            dst_ref=held,
            send_sem=semaphores.at[level, part],
            recv_sem=arrivals.at[arrives, part],
            device_id=device,
            device_id_type=MESH,
        )

    def chain(level, part):
        return block_copy(
            level, part, steps.side, chain_sends, chain_arrivals, level + 1, steps.above
        )

    def across(level, part):
        return block_copy(
            level, part, steps.side, peer_sends, peer_arrivals, level, steps.peer
        )

    def pass_on(level, part):
        @pl.when(steps.has_above)
        def _():
            chain(level, part).start()

    def project(at):
        _, weight, start = pieces[at]
        made = forward_dot(normed_ref[...], weight[:, start : start + span])
        if at == 0:
            key_rows[...] = made
            return
        for sequence in range(sequences):
            block = slice(sequence * keys, (sequence + 1) * keys)
            for pair in range(span // (2 * HD)):
                columns = slice(pair * 2 * HD, (pair + 1) * 2 * HD)
                turned = made[block, columns].T
                if at == 1:
                    turned_keys = key_rows[block, columns].T
                    for half in range(2):
                        held = slice(half * HD, (half + 1) * HD)
                        both = jnp.concatenate(
                            [turn(turned_keys[held]), turned[held].astype(jnp.bfloat16)], axis=0
                        )
                        all_ref[ctx, sequence * KVH + 2 * pair + half] = both.T
                else:
                    for half in range(2):
                        head = start // HD + 2 * pair + half
                        unit, member = sequence * KVH + head // groups, head % groups
                        part = turn(turned[half * HD : (half + 1) * HD])
                        q_ref[unit, :HD, member * keys : (member + 1) * keys] = part * jnp.bfloat16(
                            HD ** (-0.5)
                        )
        if at == 1:
            for part in range(PARTS):
                pass_on(0, part)

                @pl.when(steps.side == 0)
                def _():
                    across(0, part).start()

    columns = my_gate_ref.shape[1]
    gathered = HalfGather(full_out_ref, own, out_sends.at[0], out_arrivals.at[0])
    spread_gate = HalfSpread(gate_ref, my_gate_ref, gate_sends, gate_arrivals)
    gathered_g = GroupGather(lambda shard: all_g_ref.at[shard], g_sends, g_arrivals)
    mine = lane_tile(fsdp, columns)
    own_parts = (
        (out_ref, own_out, full_out_ref.at[own_rows]),
        (gate_ref.at[:, mine], own_gate, my_gate_ref.at[own_rows]),
        (up_ref.at[:, mine], own_up, my_up_ref.at[own_rows]),
        (g_ref, own_g, all_g_ref.at[fsdp]),
    )
    loads = [
        pltpu.make_async_copy(source, held, local_sems.at[at])
        for at, (source, held, _) in enumerate(own_parts)
    ]
    background = [
        pltpu.make_async_copy(held, target, local_sems.at[at])
        for at, (_, held, target) in enumerate(own_parts)
    ]
    up_parts = []
    for step in range(1, group):
        peer = lax.rem(fsdp + step, group)
        up_parts.append(
            pltpu.make_async_remote_copy(
                src_ref=up_ref.at[:, lane_tile(peer, columns)],
                dst_ref=my_up_ref.at[own_rows],
                send_sem=part_sends.at[step - 1],
                recv_sem=part_arrivals.at[step - 1],
                device_id=(peer, ctx),
                device_id_type=MESH,
            )
        )

    def start_background():
        for copy in loads:
            copy.start()
        gathered.start(out_ref)
        spread_gate.start()
        for copy in up_parts:
            copy.start()
        gathered_g.start(g_ref)

    last = len(pieces)
    for at in range(last + 2):
        if at < last:
            gathers[at][0].to_pairs()
        if at == last - 1:
            start_background()
        if 1 <= at <= last:
            gathers[at - 1][0].to_sibling()
        if at == 1:
            for column in range(width // LANES):
                columns = slice(column * LANES, (column + 1) * LANES)
                normed_t_ref[columns, :] = normed_ref[:, columns].T
            for copy in own_copies:
                copy.wait()
        if at >= 2:
            gathers[at - 2][0].arrived()
            project(at - 2)

    def second_half():
        gathered.to_pairs()
        spread_gate.to_pairs()
        for load, copy in zip(loads, background):
            load.wait()
            copy.start()

    def add(unit, kv):
        scores = jnp.dot(kv, q_ref[unit], preferred_element_type=jnp.float32)
        top = top_ref[unit]
        new_top = jnp.maximum(top, jnp.max(scores, axis=0, keepdims=True))
        fade = jnp.exp(top - new_top)
        weights = jnp.exp(scores - new_top)
        top_ref[unit] = new_top
        total_ref[unit] = total_ref[unit] * fade + jnp.sum(weights, axis=0, keepdims=True)
        added = jnp.dot(kv.T, weights.astype(jnp.bfloat16), preferred_element_type=jnp.float32)
        mix_ref[unit] = mix_ref[unit] * fade + added[HD:]

    def over_units(body, first, count):
        def two(at, unused):
            body(first + 2 * at)
            body(first + 2 * at + 1)
            return unused

        lax.fori_loop(0, count // 2, two, 0)

    def diagonal(unit):
        kv = all_ref[ctx, unit]
        scores = jnp.dot(kv, q_ref[unit], preferred_element_type=jnp.float32)
        scores = jnp.where(causal(keys, wide, scores.shape), scores, MASKED_SCORE)
        top = jnp.max(scores, axis=0, keepdims=True)
        weights = jnp.exp(scores - top)
        top_ref[unit] = top
        total_ref[unit] = jnp.sum(weights, axis=0, keepdims=True)
        added = jnp.dot(kv.T, weights.astype(jnp.bfloat16), preferred_element_type=jnp.float32)
        mix_ref[unit] = added[HD:]

    over_units(diagonal, 0, units)

    def forward(level, part):
        chain(level - 1, part).wait_recv()
        pass_on(level, part)
        across(level, part).start()

    @pl.when(steps.level >= 1)
    def _():
        for part in range(PARTS):
            forward(1, part)

    @pl.when(steps.side == 1)
    def _():
        for part in range(PARTS):
            across(0, part).wait_recv()
            over_units(lambda unit: add(unit, all_ref[ctx - 1, unit]), part * per_part, per_part)

    def level_step(level, unused):
        first = 2 * (steps.level - level)
        for part in range(PARTS):

            @pl.when(level < steps.level)
            def _():
                forward(level + 1, part)

            across(level, part).wait_recv()
            over_units(
                lambda unit: add(unit, all_ref[pl.ds(first, 2), unit].reshape(2 * keys, deep)),
                part * per_part,
                per_part,
            )

        @pl.when(level == 1)
        def _():
            second_half()

        return unused

    @pl.when(steps.level == 0)
    def _():
        second_half()

    lax.fori_loop(1, steps.level + 1, level_step, 0)

    def close(unit):
        total = total_ref[unit]
        mix_ref[unit] = mix_ref[unit] / total
        log_ref[unit] = top_ref[unit] + jnp.log(total)

    over_units(close, 0, units)
    for sequence in range(sequences):
        for pair in range(H // 2):
            heads = []
            for head in (2 * pair, 2 * pair + 1):
                unit, member = sequence * KVH + head // groups, head % groups
                heads.append(mix_ref[unit, :, member * keys : (member + 1) * keys])
            tile = jnp.concatenate(heads, axis=0).astype(low_ref.dtype)
            block = slice(sequence * keys, (sequence + 1) * keys)
            columns = slice(pair * 2 * HD, (pair + 1) * 2 * HD)
            low_t_ref[columns, block] = tile
            low_ref[block, columns] = tile.T
    for gather, _ in gathers:
        gather.sent()
    for step in range(1, group):
        gain_copy(step).wait_send()
    gathered.to_sibling()
    gathered_g.forward()
    gathered.arrived()
    gathered.sent()
    gathered_g.sibling_here()
    for step in range(1, gathered_g.chips):
        gathered_g.crossed(step)
    gathered_g.sent()
    spread_gate.finish()
    for copy in up_parts:
        copy.wait()
    for copy in background:
        copy.wait()

    def sent(level, unused):
        for part in range(PARTS):

            @pl.when(steps.has_above)
            def _():
                chain(level, part).wait_send()

            @pl.when(jnp.logical_or(level > 0, steps.side == 0))
            def _():
                across(level, part).wait_send()

        return unused

    lax.fori_loop(0, steps.level + 1, sent, 0)


ANY = pl.BlockSpec(memory_space=pl.ANY)
VMEM = pl.BlockSpec(memory_space=pltpu.VMEM)


def attend(x, gains, cosine, sine, w_query, w_key, w_value, w_out, w_gate, w_up, g_rows, sequences):
    group, count = lax.axis_size("fsdp"), lax.axis_size("ctx")
    rows, width = x.shape
    own, hidden = w_query.shape[0], w_gate.shape[1] // group
    keys, units, deep = rows // sequences, sequences * KVH, 2 * HD
    wide = H // KVH * keys
    kv_width = KVH * HD
    dma = pltpu.SemaphoreType.DMA
    bf16, f32 = jnp.bfloat16, jnp.float32
    pieces = 2 + width // kv_width
    return pl.pallas_call(
        attend_kernel,
        out_shape=[
            jax.ShapeDtypeStruct((units, deep, wide), bf16),
            jax.ShapeDtypeStruct((width, rows), bf16),
            jax.ShapeDtypeStruct((gains.shape[0], width), f32),
            jax.ShapeDtypeStruct((width, width), bf16),
            jax.ShapeDtypeStruct((width, kv_width), bf16),
            jax.ShapeDtypeStruct((width, kv_width), bf16),
            jax.ShapeDtypeStruct((rows, width), bf16),
            jax.ShapeDtypeStruct((width, rows), bf16),
            jax.ShapeDtypeStruct((units, HD, wide), f32),
            jax.ShapeDtypeStruct((units, 1, wide), f32),
            jax.ShapeDtypeStruct((count, units, keys, deep), bf16),
            jax.ShapeDtypeStruct((width, width), bf16),
            jax.ShapeDtypeStruct((width, hidden), bf16),
            jax.ShapeDtypeStruct((width, hidden), bf16),
            jax.ShapeDtypeStruct((group, rows, width), bf16),
        ],
        in_specs=[VMEM] * 4 + [ANY] * 7,
        out_specs=[VMEM] * 11 + [ANY] * 4,
        scratch_shapes=[
            pltpu.VMEM((rows, width), bf16),
            pltpu.VMEM((rows, kv_width), f32),
            pltpu.VMEM((group,) + gains.shape, f32),
            pltpu.VMEM((own, width), bf16),
            pltpu.VMEM((own, hidden), bf16),
            pltpu.VMEM((own, hidden), bf16),
            pltpu.VMEM((rows, width), bf16),
            pltpu.VMEM((units, 1, wide), f32),
            pltpu.VMEM((units, 1, wide), f32),
            dma((count // 2, PARTS)),
            dma((count // 2 + 1, PARTS)),
            dma((count // 2, PARTS)),
            dma((count // 2, PARTS)),
            half_semaphores(pieces),
            half_semaphores(pieces),
            *[dma((group - 1,))] * 2,
            *[half_semaphores(1)] * 2,
            *[spread_semaphores()] * 2,
            *[group_semaphores()] * 2,
            *[dma((group - 1,))] * 2,
            dma((7,)),
        ],
        compiler_params=pltpu.CompilerParams(
            collective_id=1, has_side_effects=True, vmem_limit_bytes=60 << 20
        ),
    )(x, gains, cosine, sine, w_query, w_key, w_value, w_out, w_gate, w_up, g_rows)


class Ring:
    def __init__(self, work, landing, total, semaphores, forward, exchange=False):
        self.fsdp, self.ctx = lax.axis_index("fsdp"), lax.axis_index("ctx")
        self.group, self.count = lax.axis_size("fsdp"), lax.axis_size("ctx")
        self.work, self.landing, self.total = work, landing, total
        self.sends, self.arrivals = semaphores[:2]
        self.part_sends, self.part_arrivals, self.own_sem = semaphores[2:] if exchange else (None,) * 3
        self.exchange = exchange
        side = 0 if forward else 1
        self.place = ring_place(self.ctx, side, self.count)
        self.after = (self.fsdp, ring_ctx(lax.rem(self.place + 1, self.count), side, self.count))
        self.ticks = 2 * self.count - 2 + int(exchange)

    def chunk(self, held, index):
        if self.exchange:
            return held.at[index]
        per = held.shape[0] // self.count
        return held.at[pl.ds(index * per, per)]

    def summing(self, step, index):
        return self.copy(self.chunk(self.work, index), self.landing.at[step], step)

    def handing(self, step, index):
        held = self.chunk(self.total, index)
        return self.copy(held, held, step)

    def copy(self, source, target, step):
        return pltpu.make_async_remote_copy(
            src_ref=source,
            dst_ref=target,
            send_sem=self.sends.at[step],
            recv_sem=self.arrivals.at[step],
            device_id=self.after,
            device_id_type=MESH,
        )

    def part(self, index, step):
        peer = lax.rem(self.fsdp + step, self.group)
        return pltpu.make_async_remote_copy(
            src_ref=self.work.at[index, peer],
            dst_ref=self.total.at[index, self.fsdp],
            send_sem=self.part_sends.at[step - 1],
            recv_sem=self.part_arrivals.at[step - 1],
            device_id=(peer, self.ctx),
            device_id_type=MESH,
        )

    def own_part(self, index):
        return pltpu.make_async_copy(
            self.work.at[index, self.fsdp], self.total.at[index, self.fsdp], self.own_sem
        )

    def start(self):
        self.summing(0, self.place).start()

    def tick(self, at):
        last = self.count - 2
        gap = int(self.exchange)
        step = at - gap * jnp.where(at > last, 1, 0) if self.exchange else at
        index = lax.rem(self.place + 3 * self.count - 1 - step, self.count)

        def add(target):
            part, landed = self.chunk(self.work, index), self.landing.at[jnp.minimum(at, last)]
            for row in range(part.shape[0]):
                target[row] = (
                    part[row].astype(jnp.float32) + landed[row].astype(jnp.float32)
                ).astype(part.dtype)

        @pl.when(at <= last)
        def _():
            self.summing(jnp.minimum(at, last), index).wait_recv()

        @pl.when(at < last)
        def _():
            add(self.chunk(self.work, index))
            self.summing(jnp.minimum(at + 1, last), index).start()

        if self.exchange:

            @pl.when(at == last)
            def _():
                add(self.chunk(self.work, index))
                for peer in range(1, self.group):
                    self.part(index, peer).start()
                self.own_part(index).start()

            @pl.when(at == last + 1)
            def _():
                done = lax.rem(self.place + 1, self.count)
                self.own_part(done).wait()
                for peer in range(1, self.group):
                    self.part(done, peer).wait_recv()
                self.handing(last + 1, done).start()

        else:

            @pl.when(at == last)
            def _():
                add(self.chunk(self.total, index))
                self.handing(last + 1, index).start()

        @pl.when(at > last + gap)
        def _():
            here = jnp.maximum(step, last + 1)
            self.handing(here, index).wait_recv()

            @pl.when(here < 2 * self.count - 3)
            def _():
                self.handing(jnp.minimum(here + 1, 2 * self.count - 3), index).start()

    def finish(self):
        def wait(step, unused):
            self.handing(step, self.place).wait_send()
            return unused

        lax.fori_loop(0, 2 * self.count - 2, wait, 0)
        if self.exchange:
            for peer in range(1, self.group):
                self.part(lax.rem(self.place + 1, self.count), peer).wait_send()


class SumRing(Ring):
    def __init__(self, *args):
        super().__init__(*args)
        self.ticks = self.count - 1

    def tick(self, at):
        last = self.count - 2
        index = lax.rem(self.place + 2 * self.count - 1 - at, self.count)
        self.summing(at, index).wait_recv()
        work, landed = self.chunk(self.work, index), self.landing.at[at]

        def add(target):
            for row in range(work.shape[0]):
                target[row] = (
                    work[row].astype(jnp.float32) + landed[row].astype(jnp.float32)
                ).astype(work.dtype)

        @pl.when(at < last)
        def _():
            add(work)
            self.summing(jnp.minimum(at + 1, last), index).start()

        @pl.when(at == last)
        def _():
            add(self.total)

    def finish(self):
        def wait(step, unused):
            self.summing(step, self.place).wait_send()
            return unused

        lax.fori_loop(0, self.ticks, wait, 0)


class SpreadRing(Ring):
    def __init__(self, total, semaphores, forward):
        super().__init__(None, None, total, semaphores, forward)
        self.ticks = self.count - 1
        self.first = lax.rem(self.place + 1, self.count)

    def start(self):
        self.handing(0, self.first).start()

    def tick(self, at):
        index = lax.rem(self.place + self.count - at, self.count)
        self.handing(at, index).wait_recv()

        @pl.when(at < self.count - 2)
        def _():
            self.handing(jnp.minimum(at + 1, self.count - 2), index).start()

    def finish(self):
        def wait(step, unused):
            self.handing(step, self.place).wait_send()
            return unused

        lax.fori_loop(0, self.ticks, wait, 0)


def ring_scratch(chunk, exchange=False):
    count = lax.axis_size("ctx")
    work = (count,) + chunk if exchange else (count * chunk[0],) + chunk[1:]
    return [pltpu.VMEM(work, jnp.bfloat16), pltpu.VMEM((count - 1,) + chunk, jnp.bfloat16)]


def ring_total(chunk, exchange=False):
    count = lax.axis_size("ctx")
    work = (count,) + chunk if exchange else (count * chunk[0],) + chunk[1:]
    return jax.ShapeDtypeStruct(work, jnp.bfloat16)


def ring_semaphores(exchange=False):
    dma, steps = pltpu.SemaphoreType.DMA, 2 * lax.axis_size("ctx") - 2
    parts = lax.axis_size("fsdp") - 1
    return [dma((steps,))] * 2 + ([dma((parts,))] * 2 + [dma] if exchange else [])


def wide_split(width):
    group, count = lax.axis_size("fsdp"), lax.axis_size("ctx")
    return 2 if FF // group // LANES * (width // group // 16) >= 4 * count else 1


def query_split(width):
    return width // LANES * 7 // 9 * LANES


def out_split(width):
    return (width // LANES + 1) // 2 * LANES


def down_split(blocks, count):
    each = -(-blocks // count)
    rings = 4 if each >= 4 else 2
    return [max(1, (each + at) // rings) for at in range(rings)]


class GroupScatter:
    def __init__(self, give_sib, got_sib, give_cross, got_cross, far, got_far, sends, arrivals):
        self.give_sib, self.got_sib = give_sib, got_sib
        self.give_cross, self.got_cross = give_cross, got_cross
        self.far, self.got_far = far, got_far
        self.sends, self.arrivals = sends, arrivals
        self.fsdp, self.ctx = lax.axis_index("fsdp"), lax.axis_index("ctx")
        self.chips = lax.axis_size("fsdp") // 2
        self.chip, self.core = lax.div(self.fsdp, 2), lax.rem(self.fsdp, 2)
        self.sibling = 2 * self.chip + 1 - self.core

    def copy(self, source, target, semaphore, device):
        return pltpu.make_async_remote_copy(
            src_ref=source,
            dst_ref=target,
            send_sem=self.sends.at[semaphore],
            recv_sem=self.arrivals.at[semaphore],
            device_id=(device, self.ctx),
            device_id_type=MESH,
        )

    def to_sibling(self):
        return self.copy(self.give_sib, self.got_sib, 0, self.sibling)

    def to_cross(self, step):
        return self.copy(
            self.give_cross(step), self.got_cross.at[step - 1], step, self.sibling
        )

    def to_far(self, step):
        chip = lax.rem(self.chip + self.chips - step, self.chips)
        return self.copy(
            self.far.at[step - 1],
            self.got_far.at[step - 1],
            self.chips - 1 + step,
            2 * chip + self.core,
        )

    def add_cross(self, step):
        self.to_cross(step).wait_recv()
        held = self.far.at[step - 1]
        held[...] = (
            held[...].astype(jnp.float32) + self.got_cross[step - 1].astype(jnp.float32)
        ).astype(held.dtype)
        self.to_far(step).start()

    def total(self, own):
        self.to_sibling().wait_recv()
        value = own + self.got_sib[...].astype(jnp.float32)
        for step in range(1, self.chips):
            self.to_far(step).wait_recv()
            value = value + self.got_far[step - 1].astype(jnp.float32)
        return value

    def sent(self):
        self.to_sibling().wait_send()
        for step in range(1, self.chips):
            self.to_cross(step).wait_send()
            self.to_far(step).wait_send()


def scatter_scratch(rows, width):
    far = lax.axis_size("fsdp") // 2 - 1
    one, many = (rows, width), (far, rows, width)
    return [pltpu.VMEM(shape, jnp.bfloat16) for shape in (one, one, many, many, many, many)]


def dot_columns(left, right):
    return lax.dot_general(
        left, right, (((1,), (1,)), ((), ())), preferred_element_type=jnp.float32
    )


def tiles(count, body):
    def step(at, unused):
        body(at)
        return unused

    lax.fori_loop(0, count, step, 0)


def lane_tile(at, size):
    return pl.ds(pl.multiple_of(at * size, LANES), size)


def width_tile(width):
    return 384 if width % 384 == 0 else width


def hidden_tile(hidden):
    return 256 if hidden % 256 == 0 else 128


def transpose_into(target, source):
    rows, columns = source.shape

    def body(at):
        part = source[:, lane_tile(at, LANES)]
        target[pl.ds(pl.multiple_of(at * LANES, LANES), LANES), :] = part.T

    tiles(columns // LANES, body)


def ffn_kernel(
    x_ref, low_ref, out_ref, gain_ref, gate_in, up_in, down_in, all_g_in,
    layer_ref, resid_grad_ref, branch_ref, g_wide_ref, gate_part_out, up_part_out, layer_part_out,
    *rest,
):
    downs = len(down_split(gate_in.shape[1] // 16, lax.axis_size("ctx")))
    taken = iter(rest)

    def take(number):
        return [next(taken) for _ in range(number)]

    down_done, (gain_grad_ref,) = take(downs), take(1)
    all_n_ref, turned_n, turned_act, act_ref, gate_grad, up_grad, resid_ref, grad_own = take(8)
    down_scratch = take(2 * downs)
    give_sib, got_sib, give_cross, got_cross, far, got_far = take(6)
    n_sends, n_arrivals, grad_sends, grad_arrivals = take(4)
    gate_ref, up_ref, down_ref, all_g_ref, gate_part_ref, up_part_ref, layer_part_ref = take(7)
    (local_sems,) = take(1)
    loads = [
        pltpu.make_async_copy(source, target, local_sems.at[at])
        for at, (source, target) in enumerate(
            ((gate_in, gate_ref), (up_in, up_ref), (all_g_in, all_g_ref), (down_in, down_ref))
        )
    ]
    for copy in loads:
        copy.start()
    stores = []

    def store(source, target):
        copy = pltpu.make_async_copy(source, target, local_sems.at[len(loads) + len(stores)])
        copy.start()
        stores.append(copy)

    rings = [
        SumRing(*down_scratch[2 * at : 2 * at + 2], down_done[at], take(2), at % 2 == 0)
        for at in range(downs)
    ]
    group = lax.axis_size("fsdp")
    rows, width = x_ref.shape
    hidden = gate_ref.shape[1]
    barrier = pltpu.get_barrier_semaphore()
    greeted = greet_group(barrier) + 2
    for ring in rings[:2]:
        pl.semaphore_signal(barrier, inc=1, device_id=ring.after, device_id_type=MESH)
    step_in, step_out = hidden_tile(hidden), width_tile(width)

    def branch(at):
        columns = lane_tile(at, step_out)
        resid_ref[:, columns] = x_ref[:, columns].astype(jnp.float32) + forward_dot(
            low_ref[...], out_ref[:, columns]
        )

    tiles(width // step_out, branch)
    gain = gain_ref[...]
    scale = norm_scale(resid_ref[...])
    gathered = GroupGather(lambda shard: all_n_ref.at[shard], n_sends, n_arrivals)
    fsdp, chips = gathered.fsdp, gathered.chips
    all_n_ref[fsdp] = (resid_ref[...] * scale * gain).astype(jnp.bfloat16)
    pl.semaphore_wait(barrier, greeted)
    gathered.start(all_n_ref.at[fsdp])
    grad_sum = GroupScatter(
        give_sib,
        got_sib,
        lambda step: give_cross.at[step - 1],
        got_cross,
        far,
        got_far,
        grad_sends,
        grad_arrivals,
    )

    def hidden_part(shard):
        def body(at):
            columns = lane_tile(at, step_in)
            normed = all_n_ref[shard]
            gate = forward_dot(normed, gate_ref[:, columns])
            upward = forward_dot(normed, up_ref[:, columns])
            grad_act = dot_columns(
                all_g_ref[shard], down_ref[pl.ds(pl.multiple_of(at * step_in, LANES), step_in), :]
            )
            sigmoid = jax.nn.sigmoid(gate)
            silu = gate * sigmoid
            act_ref[shard, :, columns] = (silu * upward).astype(jnp.bfloat16)
            gate_grad[shard, :, columns] = (
                grad_act * upward * (sigmoid * (1.0 + gate * (1.0 - sigmoid)))
            ).astype(jnp.bfloat16)
            up_grad[shard, :, columns] = (grad_act * silu).astype(jnp.bfloat16)

        tiles(hidden // step_in, body)

    def grad_part(shard, target):
        def body(at):
            columns = pl.ds(pl.multiple_of(at * step_out, LANES), step_out)
            target[:, columns] = (
                dot_columns(gate_grad[shard], gate_ref[columns, :])
                + dot_columns(up_grad[shard], up_ref[columns, :])
            ).astype(target.dtype)

        tiles(width // step_out, body)

    for copy in loads:
        copy.wait()
    hidden_part(fsdp)
    gathered.sibling_here()
    sibling = gathered.sibling
    hidden_part(sibling)
    grad_part(sibling, grad_sum.give_sib)
    grad_sum.to_sibling().start()
    gathered.forward()
    grad_part(fsdp, grad_own)
    def turn_act(shard):
        transpose_into(turned_act.at[:, lane_tile(shard, rows)], act_ref.at[shard])

    turn_act(fsdp)
    turn_act(sibling)
    far_shards = []
    for step in range(1, chips):
        ours = gathered.same_core(chips - step)
        theirs = ours + sibling - fsdp
        far_shards.append((step, ours, theirs))
        gathered.crossed(step)
        hidden_part(theirs)
        hidden_part(ours)
        turn_act(theirs)
        turn_act(ours)
    blocks = hidden // 16
    spans, first = [], 0
    for ring in rings:
        last = min(blocks, first + ring.work.shape[0])
        spans.append((first, last, ring.work))
        first = last

    def down_tile(at):
        columns = lane_tile(at, step_out)
        part = forward_dot(
            turned_act[...], all_g_ref[:, :, columns].reshape(group * rows, step_out)
        ).astype(jnp.bfloat16)
        for begin, end, work in spans:
            if end > begin:
                work[: end - begin, :, columns] = part[begin * 16 : end * 16].reshape(
                    end - begin, 16, step_out
                )

    tiles(width // step_out, down_tile)
    for begin, end, work in spans:
        for spare in range(end - begin, work.shape[0]):
            work[spare] = jnp.zeros(work.shape[1:], work.dtype)
    for ring in rings:
        ring.start()
    for step, ours, theirs in far_shards:
        grad_part(theirs, give_cross.at[step - 1])
        grad_sum.to_cross(step).start()
        grad_part(ours, far.at[step - 1])
        grad_sum.add_cross(step)
    ticked = [0]

    def ring_tick(at):
        for ring in rings:

            @pl.when(at < ring.ticks)
            def _():
                ring.tick(jnp.minimum(at, ring.ticks - 1))

    def ticking(times, body):
        begin = ticked[0]

        def step(at):
            body(at)
            ring_tick(begin + at)

        tiles(times, step)
        ticked[0] += times

    for shard in range(group):
        span = slice(shard * rows, (shard + 1) * rows)
        transpose_into(turned_n.at[:, span], all_n_ref.at[shard])
    own = width // group
    row_blocks = own // 16
    for source, target in ((gate_grad, gate_part_ref), (up_grad, up_part_ref)):

        def weight_tile(at):
            columns = lane_tile(at, step_in)
            part = forward_dot(
                turned_n[...], source[:, :, columns].reshape(group * rows, step_in)
            ).astype(jnp.bfloat16)
            for block in range(step_in // LANES):
                first = (at * (step_in // LANES) + block) * row_blocks
                for owner in range(group):
                    target[owner, pl.ds(first, row_blocks)] = part[
                        owner * own : (owner + 1) * own, block * LANES : (block + 1) * LANES
                    ].reshape(row_blocks, 16, LANES)

        ticking(hidden // step_in, weight_tile)
        filled = hidden // LANES * row_blocks
        for spare in range(filled, target.shape[1]):
            for owner in range(group):
                target[owner, spare] = jnp.zeros(target.shape[2:], target.dtype)
        store(target, gate_part_out if source is gate_grad else up_part_out)

    def layer_tile(at):
        columns = lane_tile(at, step_out)
        part = forward_dot(
            act_ref[...].reshape(group * rows, hidden), down_ref[:, columns]
        ).reshape(group, rows, step_out)
        layer_part_ref[:, :, columns] = part.astype(jnp.bfloat16)

    ticking(width // step_out, layer_tile)
    store(layer_part_ref, layer_part_out)
    layer_ref[...] = resid_ref[...] + layer_part_ref[fsdp].astype(jnp.float32)
    upstream = grad_sum.total(grad_own[...])
    resid = resid_ref[...]
    scaled = upstream * gain
    grad_resid = (
        all_g_ref[fsdp].astype(jnp.float32)
        + scale * scaled
        - resid * scale**3 * jnp.mean(scaled * resid, axis=-1, keepdims=True)
    )
    gain_grad_ref[...] = jnp.sum(upstream * resid * scale, axis=0, keepdims=True)
    resid_grad_ref[...] = grad_resid
    branch_ref[...] = grad_resid.astype(jnp.bfloat16)
    units, _, wide = g_wide_ref.shape
    sequences = units // KVH
    keys = rows // sequences
    groups = wide // keys
    g_wide_ref[:, :HD, :] = jnp.zeros((units, HD, wide), g_wide_ref.dtype)
    for pair in range(H // 2):
        columns = slice(pair * 2 * HD, (pair + 1) * 2 * HD)
        mixed = dot_columns(branch_ref[...], out_ref[columns, :]).astype(jnp.bfloat16)
        for sequence in range(sequences):
            turned = mixed[sequence * keys : (sequence + 1) * keys].T
            for half in range(2):
                head = 2 * pair + half
                unit, member = sequence * KVH + head // groups, head % groups
                g_wide_ref[unit, HD:, member * keys : (member + 1) * keys] = turned[
                    half * HD : (half + 1) * HD
                ]
    begin = ticked[0]
    tiles(max(0, rings[0].ticks - begin), lambda at: ring_tick(begin + at))
    gathered.sent()
    grad_sum.sent()
    for ring in rings:
        ring.finish()
    for copy in stores:
        copy.wait()


def spread(blocks, count):
    return -(-blocks // count) * count


def feed_forward(x, low, full_out, my_gate, my_up, my_down, all_g, gain, units, wide):
    group, count = lax.axis_size("fsdp"), lax.axis_size("ctx")
    rows, width = x.shape
    hidden = my_gate.shape[1]
    blocks = spread(hidden // LANES * (width // group // 16), wide_split(width) * count)
    chips = group // 2
    dma = pltpu.SemaphoreType.DMA((2 * chips - 1,))
    bf16 = jnp.bfloat16
    down_chunks = [(per, 16, width) for per in down_split(hidden // 16, count)]
    return pl.pallas_call(
        ffn_kernel,
        out_shape=[
            jax.ShapeDtypeStruct((rows, width), jnp.float32),
            jax.ShapeDtypeStruct((rows, width), jnp.float32),
            jax.ShapeDtypeStruct((rows, width), bf16),
            jax.ShapeDtypeStruct((units, 2 * HD, wide), bf16),
            jax.ShapeDtypeStruct((group, blocks, 16, LANES), bf16),
            jax.ShapeDtypeStruct((group, blocks, 16, LANES), bf16),
            jax.ShapeDtypeStruct((group, rows, width), bf16),
            *[jax.ShapeDtypeStruct(chunk, bf16) for chunk in down_chunks],
            jax.ShapeDtypeStruct((1, width), jnp.float32),
        ],
        in_specs=[VMEM] * 4 + [ANY] * 4,
        out_specs=[VMEM] * 4 + [ANY] * 3 + [VMEM] * (1 + len(down_chunks)),
        scratch_shapes=[
            pltpu.VMEM((group, rows, width), bf16),
            pltpu.VMEM((width, group * rows), bf16),
            pltpu.VMEM((hidden, group * rows), bf16),
            pltpu.VMEM((group, rows, hidden), bf16),
            pltpu.VMEM((group, rows, hidden), bf16),
            pltpu.VMEM((group, rows, hidden), bf16),
            pltpu.VMEM((rows, width), jnp.float32),
            pltpu.VMEM((rows, width), jnp.float32),
            *[kind for chunk in down_chunks for kind in ring_scratch(chunk)],
            *scatter_scratch(rows, width),
            *[dma] * 4,
            pltpu.VMEM(my_gate.shape, bf16),
            pltpu.VMEM(my_up.shape, bf16),
            pltpu.VMEM(my_down.shape, bf16),
            pltpu.VMEM(all_g.shape, bf16),
            pltpu.VMEM((group, blocks, 16, LANES), bf16),
            pltpu.VMEM((group, blocks, 16, LANES), bf16),
            pltpu.VMEM((group, rows, width), bf16),
            pltpu.SemaphoreType.DMA((7,)),
            *[kind for _ in down_chunks for kind in ring_semaphores()],
        ],
        compiler_params=pltpu.CompilerParams(
            collective_id=2, has_side_effects=True, vmem_limit_bytes=60 << 20
        ),
    )(x, low, full_out, gain, my_gate, my_up, my_down, all_g)


def back_kernel(
    down_blocks, q_ref, g_ref, log_ref, gain_grad_ref, gain_ref, cos_ref, sin_ref,
    pairs_ref, mix_in, gate_ref, up_ref, layer_base_in, layer_part_ref, branch_ref, low_t_ref,
    normed_t_ref, w_query_in, w_key_in, w_value_in, x_in, resid_grad_in, *rest,
):
    taken = iter(rest)

    def take(number):
        return [next(taken) for _ in range(number)]

    halves, downs = wide_split(x_in.shape[1]), len(down_blocks)
    down_refs = take(downs)
    tokens_ref, layer_ref = take(2)
    wide_totals, down_totals = take(2 * halves), take(downs)
    out_a_total, out_b_total, rest_a_total, rest_b_total = take(4)
    peer_got, chain_got, layer_sib, layer_cross, layer_far = take(5)
    kv_ref, stage_ref, final_ref, qg_ref, delta_ref, grad_q_ref = take(6)
    wide_scratch = take(4 * halves)
    out_a_work, out_a_land, out_b_work, out_b_land = take(4)
    rest_a_work, rest_a_land, rest_b_work, rest_b_land = take(4)
    low_all, normed_all, branch_all, query_all, pair_all, upstream_ref, gain_give, gain_got = take(8)
    far_ref, layer_stage = take(2)
    mix_ref, layer_base_ref, w_query_ref, w_key_ref, w_value_ref, x_ref, resid_grad_ref = take(7)
    steps = Steps()
    fsdp, ctx, group, count = steps.fsdp, steps.ctx, lax.axis_size("fsdp"), lax.axis_size("ctx")
    units, deep, wide = q_ref.shape
    keys = pairs_ref.shape[2]
    rows, width = x_ref.shape
    own = width // group
    wide_rings = [
        Ring(*wide_scratch[2 * at : 2 * at + 2], wide_totals[at], take(5), at < halves, True)
        for at in range(2 * halves)
    ]
    down_rings = [SpreadRing(total, take(2), at % 2 == 0) for at, total in enumerate(down_totals)]
    out_a = Ring(out_a_work, out_a_land, out_a_total, take(2), True)
    out_b = Ring(out_b_work, out_b_land, out_b_total, take(2), False)
    layer_sum = GroupScatter(
        None,
        layer_sib,
        lambda step: layer_part_ref.at[
            2 * lax.rem(lax.div(fsdp, 2) + group // 2 - step, group // 2) + 1 - lax.rem(fsdp, 2)
        ],
        layer_cross,
        far_ref,
        layer_far,
        *take(2),
    )
    layer_sum.give_sib = layer_part_ref.at[layer_sum.sibling]
    rest_a = Ring(rest_a_work, rest_a_land, rest_a_total, take(2), True)
    rest_b = Ring(rest_b_work, rest_b_land, rest_b_total, take(2), False)
    first_rings = []
    for at in range(halves):
        first_rings += [wide_rings[at], wide_rings[halves + at]]
        first_rings += down_rings[at * downs // halves : (at + 1) * downs // halves]
    begun_rings = len(first_rings)
    first_rings += [out_a, out_b]
    peer_sends, peer_arrivals, chain_sends, chain_arrivals = take(4)
    branch_gather = GroupGather(lambda shard: branch_all.at[shard], *take(2))
    query_gather = GroupGather(lambda shard: query_all.at[shard], *take(2))
    pair_gather = GroupGather(lambda shard: pair_all.at[shard], *take(2))
    low_sends, low_arrivals, normed_sends, normed_arrivals, gain_sends, gain_arrivals = take(6)
    local_sems, stage_sems = take(2)

    barrier = pltpu.get_barrier_semaphore()
    greeted = steps.greet(barrier) + greet_group(barrier) + 2
    for device in (out_a.after, out_b.after):
        pl.semaphore_signal(barrier, inc=1, device_id=device, device_id_type=MESH)

    loads = []

    def load(source, target):
        copy = pltpu.make_async_copy(source, target, local_sems.at[len(loads)])
        copy.start()
        loads.append(copy)

    n = wide_scratch[0].shape[2]
    for at, ring in enumerate(wide_rings):
        source = (gate_ref, up_ref)[at // halves]
        for chunk in range(count):
            load(source.at[:, pl.ds((at % halves * count + chunk) * n, n)], ring.work.at[chunk])
    for ring, source in zip(down_rings, down_refs):
        load(source, ring.chunk(ring.total, ring.first))
    ring_loads = len(loads)
    load(pairs_ref, kv_ref)
    load(mix_in, mix_ref)
    load(branch_ref, branch_all.at[fsdp])
    load(low_t_ref.at[pl.ds(fsdp * own, own)], low_all.at[:, lane_tile(fsdp, rows)])
    load(normed_t_ref.at[pl.ds(fsdp * own, own)], normed_all.at[:, lane_tile(fsdp, rows)])
    slot_loads = len(loads)
    for source, target in (
        (layer_base_in, layer_base_ref),
        (w_query_in, w_query_ref),
        (w_key_in, w_key_ref),
        (w_value_in, w_value_ref),
        (x_in, x_ref),
        (resid_grad_in, resid_grad_ref),
    ):
        load(source, target)
    for copy in loads[:ring_loads]:
        copy.wait()
    pl.semaphore_wait(barrier, greeted)
    for ring in first_rings[:begun_rings]:
        ring.start()
    branch_gather.start(branch_ref)
    layer_sum.to_sibling().start()
    for step in range(1, group // 2):
        layer_sum.to_cross(step).start()

    def slices(source, target, sends, arrivals, step):
        peer = lax.rem(fsdp + step, group)
        return pltpu.make_async_remote_copy(
            src_ref=source.at[pl.ds(peer * own, own)],
            dst_ref=target.at[:, lane_tile(fsdp, rows)],
            send_sem=sends.at[step - 1],
            recv_sem=arrivals.at[step - 1],
            device_id=(peer, ctx),
            device_id_type=MESH,
        )

    turned = [
        slices(*ends, step)
        for ends in (
            (low_t_ref, low_all, low_sends, low_arrivals),
            (normed_t_ref, normed_all, normed_sends, normed_arrivals),
        )
        for step in range(1, group)
    ]
    for copy in turned:
        copy.start()

    def prepare(unit):
        q, g = q_ref[unit], g_ref[unit]
        qg_ref[unit, :wide] = q.T
        qg_ref[unit, wide:] = g.T
        delta_ref[unit] = jnp.sum(
            g[HD:].astype(jnp.float32) * mix_ref[unit], axis=0, keepdims=True
        )
        grad_q_ref[unit] = jnp.zeros((HD, wide), jnp.float32)

    for copy in loads[ring_loads:slot_loads]:
        copy.wait()
    tiles(units, prepare)

    def tick(ring, at):
        @pl.when(jnp.logical_and(at >= 0, at < ring.ticks))
        def _():
            ring.tick(jnp.clip(at, 0, ring.ticks - 1))

    late = steps.levels // 2 + 1

    def pump(at):
        lag = [0] * begun_rings + [late, late]
        for turn, ring in enumerate(first_rings):

            @pl.when(lax.rem(at, len(first_rings)) == turn)
            def _():
                tick(ring, lax.div(at, len(first_rings)) - lag[turn])

    def back(unit, first, blocks, diagonal):
        kv = kv_ref[pl.ds(first, blocks), unit].reshape(blocks * keys, deep)
        scores = jnp.dot(kv, q_ref[unit], preferred_element_type=jnp.float32)
        probs = jnp.exp(scores - log_ref[unit])
        if diagonal:
            probs = jnp.where(causal(keys, wide, scores.shape), probs, 0.0)
        grad_probs = jnp.dot(kv, g_ref[unit], preferred_element_type=jnp.float32)
        grad_scores = (probs * (grad_probs - delta_ref[unit])).astype(jnp.bfloat16)
        both = jnp.concatenate([grad_scores, probs.astype(jnp.bfloat16)], axis=1)
        grad_kv = jnp.dot(both, qg_ref[unit], preferred_element_type=jnp.float32)
        added = jnp.dot(kv.T, grad_scores, preferred_element_type=jnp.float32)
        grad_q_ref[unit] = grad_q_ref[unit] + added[:HD]
        kv_ref[pl.ds(first, blocks), unit] = grad_kv.astype(kv_ref.dtype).reshape(
            blocks, keys, deep
        )

    def across(pair):
        return pltpu.make_async_remote_copy(
            src_ref=kv_ref.at[2 * pair + 1 - steps.side],
            dst_ref=peer_got.at[pair],
            send_sem=peer_sends.at[pair],
            recv_sem=peer_arrivals.at[pair],
            device_id=steps.peer,
            device_id_type=MESH,
        )

    def down_chain(pair):
        return pltpu.make_async_remote_copy(
            src_ref=kv_ref.at[2 * pair + steps.side],
            dst_ref=chain_got.at[pair],
            send_sem=chain_sends.at[pair],
            recv_sem=chain_arrivals.at[pair],
            device_id=steps.below,
            device_id_type=MESH,
        )

    def combine(time):
        pair = time - steps.levels + steps.level

        @pl.when(jnp.logical_and(pair >= 0, pair <= steps.level))
        def _():
            for slot, expected, arrival, source in (
                (0, jnp.logical_or(pair < steps.level, steps.side == 0), across, peer_got),
                (1, steps.has_above, down_chain, chain_got),
            ):

                @pl.when(expected)
                def _():
                    arrival(pair).wait_recv()
                    copy = pltpu.make_async_copy(
                        source.at[pair], stage_ref.at[slot], stage_sems.at[slot]
                    )
                    copy.start()
                    copy.wait()

                @pl.when(jnp.logical_not(expected))
                def _():
                    stage_ref[slot] = jnp.zeros(stage_ref.shape[1:], stage_ref.dtype)

            def add(unit):
                final_ref[unit] = (
                    kv_ref[2 * pair + steps.side, unit].astype(jnp.float32)
                    + stage_ref[0, unit].astype(jnp.float32)
                    + stage_ref[1, unit].astype(jnp.float32)
                )

            tiles(units, add)

            @pl.when(pair < steps.level)
            def _():
                kv_ref[2 * pair + steps.side] = final_ref[...].astype(kv_ref.dtype)
                down_chain(pair).start()

    row_blocks = own // 16

    def weight_grad(left, right, begin, end, target, first, loop):
        span = LANES * next(n for n in (3, 2, 1) if (end - begin) % (n * LANES) == 0)

        def body(at):
            columns = pl.ds(pl.multiple_of(begin + at * span, LANES), span)
            part = forward_dot(
                left[...], right[:, :, columns].reshape(group * rows, span)
            ).astype(jnp.bfloat16)
            for block in range(span // LANES):
                here = first + (at * (span // LANES) + block) * row_blocks
                target[pl.ds(here, row_blocks)] = part[
                    :, block * LANES : (block + 1) * LANES
                ].reshape(row_blocks, 16, LANES)

        loop((end - begin) // span, body)
        return first + (end - begin) // LANES * row_blocks

    def clear_from(target, first):
        for spare in range(first, target.shape[0]):
            target[spare] = jnp.zeros((16, LANES), jnp.bfloat16)

    def out_grad():
        for copy in turned[: group - 1]:
            copy.wait_recv()
        branch_gather.forward()
        branch_gather.sibling_here()
        for step in range(1, branch_gather.chips):
            branch_gather.crossed(step)
        split = out_split(width)
        clear_from(out_a_work, weight_grad(low_all, branch_all, 0, split, out_a_work, 0, tiles))
        clear_from(out_b_work, weight_grad(low_all, branch_all, split, width, out_b_work, 0, tiles))
        out_a.start()
        out_b.start()

    turns = units // 2
    rings = max(turns, len(first_rings))

    def slot(pair):
        def turn(at):
            @pl.when(pair < steps.level)
            def _():
                for unit in (2 * at, 2 * at + 1):
                    back(unit, 2 * pair, 2, False)

            @pl.when(pair == steps.level)
            def _():
                for unit in (2 * at, 2 * at + 1):
                    back(unit, ctx, 1, True)

            @pl.when(jnp.logical_and(pair == steps.level, steps.side == 1))
            def _():
                for unit in (2 * at, 2 * at + 1):
                    back(unit, ctx - 1, 1, False)

            pump(pair * rings + at)

        tiles(turns, turn)
        tiles(rings - turns, lambda at: pump(pair * rings + turns + at))

        @pl.when(jnp.logical_or(pair < steps.level, (pair == steps.level) & (steps.side == 1)))
        def _():
            across(pair).start()

        combine(pair)

        @pl.when(pair == late - 1)
        def _():
            out_grad()

    tiles(steps.levels, slot)
    pumped = [steps.levels * rings]

    def pump_next(times=1):
        def body(at, unused, begin=pumped[0]):
            pump(begin + at)
            return unused

        lax.fori_loop(0, times, body, 0)
        pumped[0] += times

    def pumping(times, body):
        begin = pumped[0]

        def step(at):
            body(at)
            pump(begin + 2 * at)
            pump(begin + 2 * at + 1)

        tiles(times, step)
        pumped[0] += 2 * times

    cosine, sine = cos_ref[...], sin_ref[...]

    def unturn(columns):
        first, second = columns[: HD // 2], columns[HD // 2 :]
        return jnp.concatenate(
            [first * cosine + second * sine, second * cosine - first * sine], axis=0
        )

    sequences = units // KVH
    groups = wide // keys
    for sequence in range(sequences):
        span = slice(sequence * keys, (sequence + 1) * keys)
        for pair in range(H // 2):
            heads = []
            for head in (2 * pair, 2 * pair + 1):
                unit, member = sequence * KVH + head // groups, head % groups
                part = grad_q_ref[unit, :, member * keys : (member + 1) * keys]
                heads.append(unturn(part * HD ** (-0.5)))
            query_all[fsdp, span, pair * 2 * HD : (pair + 1) * 2 * HD] = (
                jnp.concatenate(heads, axis=0).astype(jnp.bfloat16).T
            )
            if pair % 3 == 2:
                pump_next()
    query_gather.start(query_all.at[fsdp])
    combine(steps.levels)
    kv_width = KVH * HD
    for sequence in range(sequences):
        span = slice(sequence * keys, (sequence + 1) * keys)
        for pair in range(KVH // 2):
            turned_keys, turned_values = [], []
            for unit in (sequence * KVH + 2 * pair, sequence * KVH + 2 * pair + 1):
                part = final_ref[unit].T
                turned_keys.append(unturn(part[:HD]))
                turned_values.append(part[HD:])
            for start, parts in ((0, turned_keys), (kv_width, turned_values)):
                pair_all[fsdp, span, start + pair * 2 * HD : start + (pair + 1) * 2 * HD] = (
                    jnp.concatenate(parts, axis=0).astype(jnp.bfloat16).T
                )
    pair_gather.start(pair_all.at[fsdp])
    pump_next(2)
    query_gather.forward()
    step_out = width_tile(width)

    def upstream_tile(at):
        columns = pl.ds(pl.multiple_of(at * step_out, LANES), step_out)
        upstream_ref[:, columns] = (
            dot_columns(query_all[fsdp], w_query_ref[columns, :])
            + dot_columns(pair_all[fsdp, :, :kv_width], w_key_ref[columns, :])
            + dot_columns(pair_all[fsdp, :, kv_width:], w_value_ref[columns, :])
        )

    for copy in loads[slot_loads:]:
        copy.wait()
    pumping(width // step_out, upstream_tile)
    inputs = x_ref[...].astype(jnp.float32)
    scale = norm_scale(inputs)
    upstream = upstream_ref[...]
    scaled = upstream * gain_ref[...]
    tokens_ref[...] = (
        resid_grad_ref[...]
        + scale * scaled
        - inputs * scale**3 * jnp.mean(scaled * inputs, axis=-1, keepdims=True)
    )
    gain_attn = jnp.sum(upstream * inputs * scale, axis=0, keepdims=True)
    lanes = width // LANES
    gain_give[...] = jnp.zeros(gain_give.shape, jnp.float32)
    for block in range(lanes):
        columns = slice(block * LANES, (block + 1) * LANES)
        gain_give[block : block + 1, :] = gain_attn[:, columns]
        gain_give[lanes + block : lanes + block + 1, :] = gain_grad_ref[:, columns]

    def gain_copy(step):
        peer = lax.rem(fsdp + step, group)
        return pltpu.make_async_remote_copy(
            src_ref=gain_give,
            dst_ref=gain_got.at[step - 1],
            send_sem=gain_sends.at[step - 1],
            recv_sem=gain_arrivals.at[step - 1],
            device_id=(peer, ctx),
            device_id_type=MESH,
        )

    for step in range(1, group):
        gain_copy(step).start()
    pump_next()
    for copy in turned[group - 1 :]:
        copy.wait_recv()
    query_gather.sibling_here()
    for step in range(1, query_gather.chips):
        query_gather.crossed(step)
    split = query_split(width)
    filled_a = weight_grad(normed_all, query_all, 0, split, rest_a_work, 0, pumping)
    filled_b = weight_grad(normed_all, query_all, split, width, rest_b_work, 0, pumping)
    pair_gather.forward()
    pump_next()
    pair_gather.sibling_here()
    for step in range(1, pair_gather.chips):
        pair_gather.crossed(step)
    filled_b = weight_grad(normed_all, pair_all, 0, 2 * kv_width, rest_b_work, filled_b, pumping)
    for step in range(1, layer_sum.chips):
        ours = layer_part_ref.at[2 * lax.rem(layer_sum.chip + layer_sum.chips - step, layer_sum.chips) + layer_sum.core]
        for source, target in ((ours, far_ref.at[step - 1]), (layer_cross.at[step - 1], layer_stage)):
            if source is not ours:
                layer_sum.to_cross(step).wait_recv()
            copy = pltpu.make_async_copy(source, target, stage_sems.at[0])
            copy.start()
            copy.wait()
        far_ref[step - 1] = (
            far_ref[step - 1].astype(jnp.float32) + layer_stage[...].astype(jnp.float32)
        ).astype(jnp.bfloat16)
        layer_sum.to_far(step).start()
    gains = gain_give[...]
    for step in range(1, group):
        gain_copy(step).wait_recv()
        gains = gains + gain_got[step - 1]
    gain_tiles = gains.shape[0] // 16
    rest_a_work[filled_a : filled_a + gain_tiles] = gains.astype(jnp.bfloat16).reshape(
        gain_tiles, 16, LANES
    )
    clear_from(rest_a_work, filled_a + gain_tiles)
    clear_from(rest_b_work, filled_b)
    rest_a.start()
    rest_b.start()
    begun = pumped[0]
    total_pumps = max(wide_rings[0].ticks, late + out_a.ticks) * len(first_rings)

    half = -(-(total_pumps - begun) // rest_a.ticks)

    def last_ticks(at, unused):
        for turn in range(half):
            pump(jnp.minimum(begun + half * at + turn, total_pumps))
        tick(rest_a, at)
        tick(rest_b, at)
        return unused

    lax.fori_loop(0, rest_a.ticks, last_ticks, 0)
    layer_sum.to_sibling().wait_recv()
    layer = layer_base_ref[...]
    arrived = [layer_sib]
    for step in range(1, layer_sum.chips):
        layer_sum.to_far(step).wait_recv()
        arrived.append(layer_far.at[step - 1])
    for source in arrived:
        copy = pltpu.make_async_copy(source, layer_stage, stage_sems.at[0])
        copy.start()
        copy.wait()
        layer = layer + layer_stage[...].astype(jnp.float32)
    layer_ref[...] = layer.astype(jnp.bfloat16)
    layer_sum.sent()
    for ring in first_rings + [rest_a, rest_b]:
        ring.finish()
    for copy in turned:
        copy.wait_send()
    for gather in (branch_gather, query_gather, pair_gather):
        gather.sent()
    for step in range(1, group):
        gain_copy(step).wait_send()

    def sent(pair):
        @pl.when(jnp.logical_or(pair < steps.level, steps.side == 1))
        def _():
            across(pair).wait_send()

        @pl.when(pair < steps.level)
        def _():
            down_chain(pair).wait_send()

    tiles(steps.level + 1, sent)


def layer_back(
    q_wide, g_wide, log_total, gain_grad, gain, cosine, sine, all_pairs, mix, gate_part, up_part,
    layer_base, layer_parts, branch, low_t, normed_t, w_query, w_key, w_value, x, resid_grad, downs,
):
    group, count = lax.axis_size("fsdp"), lax.axis_size("ctx")
    units, deep, wide = q_wide.shape
    keys = all_pairs.shape[2]
    rows, width = x.shape
    own, kv_width = width // group, w_key.shape[1]
    bf16, f32 = jnp.bfloat16, jnp.float32
    dma = pltpu.SemaphoreType.DMA
    halves = wide_split(width)
    wide_chunk = (group, gate_part.shape[1] // (halves * count), 16, LANES)
    gain_rows = spread(2 * (width // LANES), 16)
    split, row_blocks = query_split(width), own // 16
    out_first = out_split(width)
    chips = group // 2
    small_chunks = [
        (spread(held, count) // count, 16, LANES)
        for held in (
            out_first // LANES * row_blocks,
            (width - out_first) // LANES * row_blocks,
            split // LANES * row_blocks + gain_rows // 16,
            (width - split + 2 * kv_width) // LANES * row_blocks,
        )
    ]
    levels = count // 2
    loaded = [mix, layer_base, w_query, w_key, w_value, x, resid_grad]
    return pl.pallas_call(
        functools.partial(back_kernel, [part.shape[0] for part in downs]),
        out_shape=[
            jax.ShapeDtypeStruct((rows, width), f32),
            jax.ShapeDtypeStruct((rows, width), bf16),
            *[ring_total(wide_chunk, True)] * (2 * halves),
            *[ring_total(part.shape) for part in downs],
            *[ring_total(chunk) for chunk in small_chunks],
            *[jax.ShapeDtypeStruct((levels, units, keys, deep), bf16)] * 2,
            jax.ShapeDtypeStruct((rows, width), bf16),
            *[jax.ShapeDtypeStruct((chips - 1, rows, width), bf16)] * 2,
        ],
        in_specs=[VMEM] * 7 + [ANY] * (14 + len(downs)),
        out_specs=[VMEM] * (6 + 2 * halves + len(downs)) + [ANY] * 5,
        scratch_shapes=[
            pltpu.VMEM(all_pairs.shape, bf16),
            pltpu.VMEM((2, units, keys, deep), bf16),
            pltpu.VMEM((units, keys, deep), f32),
            pltpu.VMEM((units, 2 * wide, deep), bf16),
            pltpu.VMEM((units, 1, wide), f32),
            pltpu.VMEM((units, HD, wide), f32),
            *[kind for _ in range(2 * halves) for kind in ring_scratch(wide_chunk, True)],
            *[kind for chunk in small_chunks for kind in ring_scratch(chunk)],
            pltpu.VMEM((own, group * rows), bf16),
            pltpu.VMEM((own, group * rows), bf16),
            pltpu.VMEM((group, rows, width), bf16),
            pltpu.VMEM((group, rows, width), bf16),
            pltpu.VMEM((group, rows, 2 * kv_width), bf16),
            pltpu.VMEM((rows, width), f32),
            pltpu.VMEM((gain_rows, LANES), f32),
            pltpu.VMEM((group - 1, gain_rows, LANES), f32),
            pltpu.VMEM((chips - 1, rows, width), bf16),
            pltpu.VMEM((rows, width), bf16),
            *[pltpu.VMEM(array.shape, array.dtype) for array in loaded],
            *[kind for _ in range(2 * halves) for kind in ring_semaphores(True)],
            *[kind for _ in range(len(downs) + 2) for kind in ring_semaphores()],
            *[dma((group - 1,))] * 2,
            *[kind for _ in range(2) for kind in ring_semaphores()],
            *[dma((levels,))] * 4,
            *[group_semaphores()] * 6,
            *[dma((group - 1,))] * 6,
            dma((11 + len(downs) + 2 * halves * count,)),
            dma((2,)),
        ],
        compiler_params=pltpu.CompilerParams(
            collective_id=3, has_side_effects=True, vmem_limit_bytes=62 << 20
        ),
    )(
        q_wide, g_wide, log_total, gain_grad, gain, cosine, sine, all_pairs, mix, gate_part, up_part,
        layer_base, layer_parts, branch, low_t, normed_t, w_query, w_key, w_value, x, resid_grad,
        *downs,
    )


def finish_kernel(halves, downs, *refs):
    wides, refs = refs[: 2 * halves], refs[2 * halves :]
    down_refs, refs = refs[:downs], refs[downs:]
    out_a_ref, out_b_ref, rest_a_ref, rest_b_ref = refs[:4]
    query_grad, key_grad, value_grad, out_grad, gate_grad, up_grad, down_grad = refs[4:]
    rows = gate_grad.shape[0]
    row_blocks = rows // 16
    for sources, target in ((wides[:halves], gate_grad), (wides[halves:], up_grad)):
        held = jnp.concatenate(
            [source[...].reshape((-1,) + source.shape[3:]) for source in sources], axis=0
        )
        for block in range(target.shape[1] // LANES):
            target[:, block * LANES : (block + 1) * LANES] = (
                held[block * row_blocks : (block + 1) * row_blocks]
                .reshape(rows, LANES)
                .astype(jnp.float32)
            )

    @pl.when(pl.program_id(0) == 0)
    def _():
        def unpack(source, first, target, begin, end):
            for block in range(begin, end):
                here = first + (block - begin) * row_blocks
                target[:, block * LANES : (block + 1) * LANES] = (
                    source[here : here + row_blocks].reshape(rows, LANES).astype(jnp.float32)
                )
            return first + (end - begin) * row_blocks

        width, kv_width = query_grad.shape[1], key_grad.shape[1]
        split = query_split(width) // LANES
        middle = out_split(width) // LANES
        unpack(out_a_ref, 0, out_grad, 0, middle)
        unpack(out_b_ref, 0, out_grad, middle, width // LANES)
        unpack(rest_a_ref, 0, query_grad, 0, split)
        at = unpack(rest_b_ref, 0, query_grad, split, width // LANES)
        at = unpack(rest_b_ref, at, key_grad, 0, kv_width // LANES)
        unpack(rest_b_ref, at, value_grad, 0, kv_width // LANES)
        blocks, begin = down_grad.shape[0] // 16, 0
        for source in down_refs:
            end = min(blocks, begin + source.shape[0])
            if end > begin:
                down_grad[begin * 16 : end * 16, :] = (
                    source[: end - begin]
                    .reshape((end - begin) * 16, down_grad.shape[1])
                    .astype(jnp.float32)
                )
            begin = end


def finish(wides, downs, smalls, own, width, kv_width, hidden):
    count, group, n = wides[0].shape[:3]

    def whole(array):
        return pl.BlockSpec(array.shape, lambda part, rank=len(array.shape): (0,) * rank)

    wide = pl.BlockSpec((count, 1, n, 16, LANES), lambda part: (0, part, 0, 0, 0))
    outs = [
        jax.ShapeDtypeStruct((own, columns), jnp.float32)
        for columns in (width, kv_width, kv_width, width, FF, FF)
    ] + [jax.ShapeDtypeStruct((hidden, width), jnp.float32)]
    slice_spec = pl.BlockSpec((own, FF // group), lambda part: (0, part))
    return pl.pallas_call(
        functools.partial(finish_kernel, len(wides) // 2, len(downs)),
        grid=(group,),
        out_shape=outs,
        in_specs=[wide] * len(wides) + [whole(a) for a in (*downs, *smalls)],
        out_specs=[whole(a) for a in outs[:4]] + [slice_spec, slice_spec, whole(outs[6])],
        compiler_params=pltpu.CompilerParams(vmem_limit_bytes=60 << 20),
    )(*wides, *downs, *smalls)


def on_device(
    tokens, w_query, w_key, w_value, w_out, w_gate, w_up, w_down, gain_attn, gain_ffn, cotangent
):
    block_len, seq_count, width = tokens.shape
    rows_count = block_len * seq_count
    kv_width = KVH * HD
    positions = lax.axis_index("ctx") * block_len + jnp.arange(block_len, dtype=jnp.int32)
    freqs = ROTARY_BASE ** (-2.0 * jnp.arange(HD // 2, dtype=jnp.float32) / HD)
    angles = freqs[:, None] * positions.astype(jnp.float32)[None, :]
    cosine, sine = jnp.cos(angles), jnp.sin(angles)
    x_rows = jnp.swapaxes(tokens, 0, 1).reshape(rows_count, width)
    g_rows = jnp.swapaxes(cotangent, 0, 1).reshape(rows_count, width)
    own = gain_attn.shape[0]
    units = seq_count * KVH
    wide = H // KVH * block_len
    own_gains = jnp.pad(
        jnp.stack([gain_attn, gain_ffn]).astype(jnp.float32), ((0, 6), (0, spread(own, LANES) - own))
    )
    (
        q_wide, normed_t, gains, full_query, full_key, full_value, attn_low, low_t, mix_unit, log_total,
        all_pairs, full_out, my_gate, my_up, all_g,
    ) = attend(
        x_rows, own_gains, cosine, sine, w_query, w_key, w_value, w_out, w_gate, w_up, g_rows, seq_count
    )
    layer_base, grad_resid, grad_branch, g_wide, gate_part, up_part, layer_parts, *downs = (
        feed_forward(
            x_rows, attn_low, full_out, my_gate, my_up, w_down, all_g, gains[1:2], units, wide
        )
    )
    downs, gain_term_ffn = downs[:-1], downs[-1]
    grad_tokens, layer_out, *sums = layer_back(
        q_wide, g_wide, log_total, gain_term_ffn, gains[:1], cosine, sine, all_pairs, mix_unit,
        gate_part, up_part, layer_base, layer_parts, grad_branch, low_t, normed_t, full_query,
        full_key, full_value, x_rows, grad_resid, downs,
    )
    wides, sums = sums[: 2 * wide_split(width)], sums[2 * wide_split(width) :]
    smalls = sums[len(downs) : len(downs) + 4]
    filled = query_split(width) // LANES * (own // 16)
    gain_grads = smalls[2][filled:].reshape(-1, LANES)[: 2 * (width // LANES)].reshape(2, width)
    gain_grads = lax.dynamic_slice_in_dim(gain_grads, lax.axis_index("fsdp") * own, own, 1)
    gain_grads = gain_grads.astype(jnp.float32)
    grads = finish(wides, sums[: len(downs)], smalls, own, width, kv_width, w_down.shape[0])
    return (
        jnp.swapaxes(layer_out.reshape(seq_count, block_len, width), 0, 1),
        jnp.swapaxes(grad_tokens.reshape(seq_count, block_len, width), 0, 1),
        *grads,
        gain_grads[0],
        gain_grads[1],
    )


def solution(mesh):
    return jax.shard_map(
        on_device,
        mesh=mesh,
        in_specs=(
            P("ctx", "fsdp", None),
            P("fsdp", None),
            P("fsdp", None),
            P("fsdp", None),
            P("fsdp", None),
            P("fsdp", None),
            P("fsdp", None),
            P("fsdp", None),
            P("fsdp"),
            P("fsdp"),
            P("ctx", "fsdp", None),
        ),
        out_specs=(
            P("ctx", "fsdp", None),
            P("ctx", "fsdp", None),
            P("fsdp", None),
            P("fsdp", None),
            P("fsdp", None),
            P("fsdp", None),
            P("fsdp", None),
            P("fsdp", None),
            P("fsdp", None),
            P("fsdp"),
            P("fsdp"),
        ),
        check_vma=False,
    )
```

```python
import functools

import jax
import jax.numpy as jnp
from jax import lax
from jax.experimental import pallas as pl
from jax.experimental.pallas import tpu as pltpu
from jax.sharding import PartitionSpec as P

H = 18
KVH = 6
HD = 64
FF = 3072


EPSILON = 1e-05
ROTARY_BASE = 10000.0
MASKED_SCORE = -1e30


def norm_scale(rows):
    return lax.rsqrt(jnp.mean(rows * rows, axis=-1, keepdims=True) + EPSILON)


def forward_dot(left, right):
    return jnp.dot(left, right, preferred_element_type=jnp.float32)


MESH = pl.DeviceIdType.MESH
LANES = 128


def ring_place(ctx, fsdp, count):
    column, side = lax.div(ctx, 2), lax.rem(ctx, 2)
    place = column + side * (count - 1 - 2 * column)
    odd = lax.rem(fsdp, 2)
    return place + odd * (count - 1 - 2 * place)


def ring_ctx(place, fsdp, count):
    odd = lax.rem(fsdp, 2)
    place = place + odd * (count - 1 - 2 * place)
    late = lax.div(place, count // 2)
    return (1 - late) * 2 * place + late * (2 * (count - 1 - place) + 1)


class GroupGather:
    def __init__(self, shard_of, sends, arrivals):
        self.shard_of, self.sends, self.arrivals = shard_of, sends, arrivals
        self.fsdp, self.ctx = lax.axis_index("fsdp"), lax.axis_index("ctx")
        self.chips = lax.axis_size("fsdp") // 2
        self.chip, self.core = lax.div(self.fsdp, 2), lax.rem(self.fsdp, 2)
        self.sibling = 2 * self.chip + 1 - self.core

    def copy(self, source, shard, semaphore, device):
        return pltpu.make_async_remote_copy(
            src_ref=source,
            dst_ref=self.shard_of(shard),
            send_sem=self.sends.at[semaphore],
            recv_sem=self.arrivals.at[semaphore],
            device_id=(device, self.ctx),
            device_id_type=MESH,
        )

    def same_core(self, step):
        return 2 * lax.rem(self.chip + step, self.chips) + self.core

    def across(self, source):
        return self.copy(source, self.fsdp, 0, self.sibling)

    def out(self, source, step):
        return self.copy(source, self.fsdp, step, self.same_core(step))

    def onward(self, step):
        shard = self.same_core(self.chips - step)
        return self.copy(self.shard_of(shard), shard, self.chips - 1 + step, self.sibling)

    def start(self, source):
        for step in range(1, self.chips):
            self.out(source, step).start()
        self.across(source).start()

    def forward(self):
        own = self.shard_of(self.fsdp)
        for step in range(1, self.chips):
            self.out(own, step).wait_recv()
            self.onward(step).start()

    def sibling_here(self):
        self.across(self.shard_of(self.fsdp)).wait_recv()

    def crossed(self, step):
        self.onward(step).wait_recv()

    def sent(self):
        own = self.shard_of(self.fsdp)
        self.across(own).wait_send()
        for step in range(1, self.chips):
            self.out(own, step).wait_send()
            self.onward(step).wait_send()

    def finish(self):
        self.forward()
        self.sibling_here()
        for step in range(1, self.chips):
            self.crossed(step)
        self.sent()


class HalfGather:
    def __init__(self, held, own_rows, sends, arrivals):
        self.held, self.own = held, own_rows
        self.sends, self.arrivals = sends, arrivals
        self.fsdp, self.ctx = lax.axis_index("fsdp"), lax.axis_index("ctx")
        self.chips = lax.axis_size("fsdp") // 2
        self.chip, self.core = lax.div(self.fsdp, 2), lax.rem(self.fsdp, 2)
        self.sibling = 2 * self.chip + 1 - self.core
        self.side = lax.rem(self.ctx, 2)
        self.pair = self.ctx + 1 - 2 * self.side
        first = -(-own_rows // 32) * 16
        self.halves = ((0, first), (first, own_rows - first))

    def same_core(self, step):
        return 2 * lax.rem(self.chip + step, self.chips) + self.core

    def rows(self, shard, half=None):
        begin, size = (0, self.own) if half is None else self.halves[half]
        return self.held.at[pl.ds(shard * self.own + begin, size)]

    def copy(self, source, target, semaphore, device):
        return pltpu.make_async_remote_copy(
            src_ref=source,
            dst_ref=target,
            send_sem=self.sends.at[semaphore],
            recv_sem=self.arrivals.at[semaphore],
            device_id=device,
            device_id_type=MESH,
        )

    def on_side(self, body):
        for half in range(2):

            @pl.when(self.side == half)
            def _(half=half):
                body(half)

    def across(self, source):
        return self.copy(source, self.rows(self.fsdp), 0, (self.sibling, self.ctx))

    def out(self, source, step, half):
        begin, size = self.halves[half]
        return self.copy(
            source.at[pl.ds(begin, size)],
            self.rows(self.fsdp, half),
            step,
            (self.same_core(step), self.ctx),
        )

    def to_pair(self, step, half):
        part = self.rows(self.same_core(self.chips - step), half)
        return self.copy(part, part, self.chips - 1 + step, (self.fsdp, self.pair))

    def onward(self, step):
        part = self.rows(self.same_core(self.chips - step))
        return self.copy(part, part, 2 * self.chips - 2 + step, (self.sibling, self.ctx))

    def start(self, source):
        def send(half):
            for step in range(1, self.chips):
                self.out(source, step, half).start()

        self.on_side(send)
        self.across(source).start()

    def to_pairs(self):
        def forward(half):
            for step in range(1, self.chips):
                self.out(self.rows(self.fsdp), step, half).wait_recv()
                self.to_pair(step, half).start()

        self.on_side(forward)

    def to_sibling(self):
        def forward(half):
            for step in range(1, self.chips):
                self.to_pair(step, 1 - half).wait_recv()

        self.on_side(forward)
        for step in range(1, self.chips):
            self.onward(step).start()

    def arrived(self):
        self.across(self.rows(self.fsdp)).wait_recv()
        for step in range(1, self.chips):
            self.onward(step).wait_recv()

    def sent(self):
        def wait(half):
            for step in range(1, self.chips):
                self.out(self.rows(self.fsdp), step, half).wait_send()
                self.to_pair(step, half).wait_send()

        self.on_side(wait)
        self.across(self.rows(self.fsdp)).wait_send()
        for step in range(1, self.chips):
            self.onward(step).wait_send()


def half_semaphores(many):
    return pltpu.SemaphoreType.DMA((many, 3 * (lax.axis_size("fsdp") // 2) - 2))


def group_semaphores():
    return pltpu.SemaphoreType.DMA((lax.axis_size("fsdp") - 1,))


def greet_group(barrier):
    fsdp, ctx, group = lax.axis_index("fsdp"), lax.axis_index("ctx"), lax.axis_size("fsdp")
    for step in range(1, group):
        peer = lax.rem(fsdp + step, group)
        pl.semaphore_signal(barrier, inc=1, device_id=(peer, ctx), device_id_type=MESH)
    return group - 1


class Steps:
    def __init__(self):
        self.fsdp, self.ctx = lax.axis_index("fsdp"), lax.axis_index("ctx")
        self.levels = lax.axis_size("ctx") // 2
        self.level, self.side = lax.div(self.ctx, 2), lax.rem(self.ctx, 2)
        self.peer = (self.fsdp, 2 * self.level + 1 - self.side)
        self.above = (self.fsdp, lax.rem(self.ctx + 2, 2 * self.levels))
        self.below = (self.fsdp, lax.rem(self.ctx + 2 * self.levels - 2, 2 * self.levels))
        self.has_above = self.level + 1 < self.levels
        self.has_below = self.level > 0

    def greet(self, barrier):
        pl.semaphore_signal(barrier, inc=1, device_id=self.peer, device_id_type=MESH)

        @pl.when(self.has_above)
        def _():
            pl.semaphore_signal(barrier, inc=1, device_id=self.above, device_id_type=MESH)

        @pl.when(self.has_below)
        def _():
            pl.semaphore_signal(barrier, inc=1, device_id=self.below, device_id_type=MESH)

        return 1 + jnp.minimum(self.level, 1) + jnp.minimum(self.levels - 1 - self.level, 1)


PARTS = 2


def causal(keys, wide, shape):
    key_at = lax.broadcasted_iota(jnp.int32, shape, 0)
    query_at = lax.rem(lax.broadcasted_iota(jnp.int32, shape, 1), keys)
    return key_at <= query_at


def attend_kernel(
    x_ref, gain_ref, cos_ref, sin_ref, query_ref, key_ref, value_ref, out_ref, gate_ref, up_ref, g_ref,
    q_ref, normed_t_ref, gains_ref, full_query, full_key, full_value,
    low_ref, low_t_ref, mix_ref, log_ref, all_ref, full_out_ref, my_gate_ref, my_up_ref, all_g_ref,
    normed_ref, key_rows, gain_all, own_out, own_gate, own_up, own_g,
    top_ref, total_ref, chain_sends, chain_arrivals, peer_sends, peer_arrivals,
    half_sends, half_arrivals, gain_sends, gain_arrivals,
    out_sends, out_arrivals, g_sends, g_arrivals,
    part_sends, part_arrivals, local_sems,
):
    steps = Steps()
    fsdp, ctx, group = steps.fsdp, steps.ctx, lax.axis_size("fsdp")
    units, deep, wide = q_ref.shape
    keys = all_ref.shape[2]
    per_part = units // PARTS
    rows_count, width = x_ref.shape
    own = query_ref.shape[0]
    sequences, groups = units // KVH, H // KVH
    barrier = pltpu.get_barrier_semaphore()
    greeted = steps.greet(barrier) + greet_group(barrier)
    span = KVH * HD
    pieces = [(key_ref, full_key, 0), (value_ref, full_value, 0)]
    pieces += [(query_ref, full_query, start) for start in range(0, width, span)]
    gathers = []
    for at, (source, target, start) in enumerate(pieces):
        columns = pl.ds(start, span)
        gather = HalfGather(
            target.at[:, columns], own, half_sends.at[at], half_arrivals.at[at]
        )
        gathers.append((gather, source.at[:, columns]))
    own_rows = pl.ds(fsdp * own, own)
    own_copies = [
        pltpu.make_async_copy(source, target.at[own_rows], local_sems.at[4 + at])
        for at, (source, target) in enumerate(
            ((key_ref, full_key), (value_ref, full_value), (query_ref, full_query))
        )
    ]
    for copy in own_copies:
        copy.start()
    gain_all[fsdp] = gain_ref[...]
    pl.semaphore_wait(barrier, greeted)

    def gain_copy(step):
        peer = lax.rem(fsdp + step, group)
        return pltpu.make_async_remote_copy(
            src_ref=gain_ref,
            dst_ref=gain_all.at[fsdp],
            send_sem=gain_sends.at[step - 1],
            recv_sem=gain_arrivals.at[step - 1],
            device_id=(peer, ctx),
            device_id_type=MESH,
        )

    for step in range(1, group):
        gain_copy(step).start()
    for gather, source in gathers:
        gather.start(source)
    inputs = x_ref[...].astype(jnp.float32)
    scale = norm_scale(inputs)
    q_ref[:, HD:, :] = jnp.zeros((units, HD, wide), q_ref.dtype)
    for step in range(1, group):
        gain_copy(step).wait_recv()
    gains = jnp.concatenate([gain_all[shard][:, :own] for shard in range(group)], axis=1)
    gains_ref[...] = gains
    normed_ref[...] = (inputs * scale * gains[:1]).astype(jnp.bfloat16)
    cosine, sine = cos_ref[...], sin_ref[...]

    def turn(columns):
        first, second = columns[: HD // 2], columns[HD // 2 :]
        return jnp.concatenate(
            [first * cosine - second * sine, second * cosine + first * sine], axis=0
        ).astype(jnp.bfloat16)

    def block_copy(level, part, side, semaphores, arrivals, arrives, device):
        block = 2 * (steps.level - level) + side
        held = all_ref.at[block, pl.ds(part * per_part, per_part)]
        return pltpu.make_async_remote_copy(
            src_ref=held,
            dst_ref=held,
            send_sem=semaphores.at[level, part],
            recv_sem=arrivals.at[arrives, part],
            device_id=device,
            device_id_type=MESH,
        )

    def chain(level, part):
        return block_copy(
            level, part, steps.side, chain_sends, chain_arrivals, level + 1, steps.above
        )

    def across(level, part):
        return block_copy(
            level, part, steps.side, peer_sends, peer_arrivals, level, steps.peer
        )

    def pass_on(level, part):
        @pl.when(steps.has_above)
        def _():
            chain(level, part).start()

    def project(at):
        _, weight, start = pieces[at]
        made = forward_dot(normed_ref[...], weight[:, start : start + span])
        if at == 0:
            key_rows[...] = made
            return
        for sequence in range(sequences):
            block = slice(sequence * keys, (sequence + 1) * keys)
            for pair in range(span // (2 * HD)):
                columns = slice(pair * 2 * HD, (pair + 1) * 2 * HD)
                turned = made[block, columns].T
                if at == 1:
                    turned_keys = key_rows[block, columns].T
                    for half in range(2):
                        held = slice(half * HD, (half + 1) * HD)
                        both = jnp.concatenate(
                            [turn(turned_keys[held]), turned[held].astype(jnp.bfloat16)], axis=0
                        )
                        all_ref[ctx, sequence * KVH + 2 * pair + half] = both.T
                else:
                    for half in range(2):
                        head = start // HD + 2 * pair + half
                        unit, member = sequence * KVH + head // groups, head % groups
                        part = turn(turned[half * HD : (half + 1) * HD])
                        q_ref[unit, :HD, member * keys : (member + 1) * keys] = part * jnp.bfloat16(
                            HD ** (-0.5)
                        )
        if at == 1:
            for part in range(PARTS):
                pass_on(0, part)

                @pl.when(steps.side == 0)
                def _():
                    across(0, part).start()

    columns = my_gate_ref.shape[1]
    gathered = HalfGather(full_out_ref, own, out_sends.at[0], out_arrivals.at[0])
    gathered_g = GroupGather(lambda shard: all_g_ref.at[shard], g_sends, g_arrivals)
    mine = lane_tile(fsdp, columns)
    own_parts = (
        (out_ref, own_out, full_out_ref.at[own_rows]),
        (gate_ref.at[:, mine], own_gate, my_gate_ref.at[own_rows]),
        (up_ref.at[:, mine], own_up, my_up_ref.at[own_rows]),
        (g_ref, own_g, all_g_ref.at[fsdp]),
    )
    loads = [
        pltpu.make_async_copy(source, held, local_sems.at[at])
        for at, (source, held, _) in enumerate(own_parts)
    ]
    background = [
        pltpu.make_async_copy(held, target, local_sems.at[at])
        for at, (_, held, target) in enumerate(own_parts)
    ]
    slices = []
    for which, (source, target) in enumerate(((gate_ref, my_gate_ref), (up_ref, my_up_ref))):
        for step in range(1, group):
            peer = lax.rem(fsdp + step, group)
            slices.append(
                pltpu.make_async_remote_copy(
                    src_ref=source.at[:, lane_tile(peer, columns)],
                    dst_ref=target.at[own_rows],
                    send_sem=part_sends.at[which, step - 1],
                    recv_sem=part_arrivals.at[which, step - 1],
                    device_id=(peer, ctx),
                    device_id_type=MESH,
                )
            )

    def start_background():
        for copy in loads:
            copy.start()
        gathered.start(out_ref)
        for copy in slices:
            copy.start()
        gathered_g.start(g_ref)

    last = len(pieces)
    for at in range(last + 2):
        if at < last:
            gathers[at][0].to_pairs()
        if at == last - 1:
            start_background()
        if 1 <= at <= last:
            gathers[at - 1][0].to_sibling()
        if at == 1:
            for column in range(width // LANES):
                columns = slice(column * LANES, (column + 1) * LANES)
                normed_t_ref[columns, :] = normed_ref[:, columns].T
            for copy in own_copies:
                copy.wait()
        if at >= 2:
            gathers[at - 2][0].arrived()
            project(at - 2)

    def second_half():
        gathered.to_pairs()
        for load, copy in zip(loads, background):
            load.wait()
            copy.start()

    def add(unit, kv):
        scores = jnp.dot(kv, q_ref[unit], preferred_element_type=jnp.float32)
        top = top_ref[unit]
        new_top = jnp.maximum(top, jnp.max(scores, axis=0, keepdims=True))
        fade = jnp.exp(top - new_top)
        weights = jnp.exp(scores - new_top)
        top_ref[unit] = new_top
        total_ref[unit] = total_ref[unit] * fade + jnp.sum(weights, axis=0, keepdims=True)
        added = jnp.dot(kv.T, weights.astype(jnp.bfloat16), preferred_element_type=jnp.float32)
        mix_ref[unit] = mix_ref[unit] * fade + added[HD:]

    def over_units(body, first, count):
        def two(at, unused):
            body(first + 2 * at)
            body(first + 2 * at + 1)
            return unused

        lax.fori_loop(0, count // 2, two, 0)

    def diagonal(unit):
        kv = all_ref[ctx, unit]
        scores = jnp.dot(kv, q_ref[unit], preferred_element_type=jnp.float32)
        scores = jnp.where(causal(keys, wide, scores.shape), scores, MASKED_SCORE)
        top = jnp.max(scores, axis=0, keepdims=True)
        weights = jnp.exp(scores - top)
        top_ref[unit] = top
        total_ref[unit] = jnp.sum(weights, axis=0, keepdims=True)
        added = jnp.dot(kv.T, weights.astype(jnp.bfloat16), preferred_element_type=jnp.float32)
        mix_ref[unit] = added[HD:]

    over_units(diagonal, 0, units)

    def forward(level, part):
        chain(level - 1, part).wait_recv()
        pass_on(level, part)
        across(level, part).start()

    @pl.when(steps.level >= 1)
    def _():
        for part in range(PARTS):
            forward(1, part)

    @pl.when(steps.side == 1)
    def _():
        for part in range(PARTS):
            across(0, part).wait_recv()
            over_units(lambda unit: add(unit, all_ref[ctx - 1, unit]), part * per_part, per_part)

    def level_step(level, unused):
        first = 2 * (steps.level - level)
        for part in range(PARTS):

            @pl.when(level < steps.level)
            def _():
                forward(level + 1, part)

            across(level, part).wait_recv()
            over_units(
                lambda unit: add(unit, all_ref[pl.ds(first, 2), unit].reshape(2 * keys, deep)),
                part * per_part,
                per_part,
            )

        @pl.when(level == 1)
        def _():
            second_half()

        return unused

    @pl.when(steps.level == 0)
    def _():
        second_half()

    lax.fori_loop(1, steps.level + 1, level_step, 0)

    def close(unit):
        total = total_ref[unit]
        mix_ref[unit] = mix_ref[unit] / total
        log_ref[unit] = top_ref[unit] + jnp.log(total)

    over_units(close, 0, units)
    for sequence in range(sequences):
        for pair in range(H // 2):
            heads = []
            for head in (2 * pair, 2 * pair + 1):
                unit, member = sequence * KVH + head // groups, head % groups
                heads.append(mix_ref[unit, :, member * keys : (member + 1) * keys])
            tile = jnp.concatenate(heads, axis=0).astype(low_ref.dtype)
            block = slice(sequence * keys, (sequence + 1) * keys)
            columns = slice(pair * 2 * HD, (pair + 1) * 2 * HD)
            low_t_ref[columns, block] = tile
            low_ref[block, columns] = tile.T
    for gather, _ in gathers:
        gather.sent()
    for step in range(1, group):
        gain_copy(step).wait_send()
    gathered.to_sibling()
    gathered_g.forward()
    gathered.arrived()
    gathered.sent()
    gathered_g.sibling_here()
    for step in range(1, gathered_g.chips):
        gathered_g.crossed(step)
    gathered_g.sent()
    for copy in slices:
        copy.wait()
    for copy in background:
        copy.wait()

    def sent(level, unused):
        for part in range(PARTS):

            @pl.when(steps.has_above)
            def _():
                chain(level, part).wait_send()

            @pl.when(jnp.logical_or(level > 0, steps.side == 0))
            def _():
                across(level, part).wait_send()

        return unused

    lax.fori_loop(0, steps.level + 1, sent, 0)


ANY = pl.BlockSpec(memory_space=pl.ANY)
VMEM = pl.BlockSpec(memory_space=pltpu.VMEM)


def attend(x, gains, cosine, sine, w_query, w_key, w_value, w_out, w_gate, w_up, g_rows, sequences):
    group, count = lax.axis_size("fsdp"), lax.axis_size("ctx")
    rows, width = x.shape
    own, hidden = w_query.shape[0], w_gate.shape[1] // group
    keys, units, deep = rows // sequences, sequences * KVH, 2 * HD
    wide = H // KVH * keys
    kv_width = KVH * HD
    dma = pltpu.SemaphoreType.DMA
    bf16, f32 = jnp.bfloat16, jnp.float32
    pieces = 2 + width // kv_width
    return pl.pallas_call(
        attend_kernel,
        out_shape=[
            jax.ShapeDtypeStruct((units, deep, wide), bf16),
            jax.ShapeDtypeStruct((width, rows), bf16),
            jax.ShapeDtypeStruct((gains.shape[0], width), f32),
            jax.ShapeDtypeStruct((width, width), bf16),
            jax.ShapeDtypeStruct((width, kv_width), bf16),
            jax.ShapeDtypeStruct((width, kv_width), bf16),
            jax.ShapeDtypeStruct((rows, width), bf16),
            jax.ShapeDtypeStruct((width, rows), bf16),
            jax.ShapeDtypeStruct((units, HD, wide), f32),
            jax.ShapeDtypeStruct((units, 1, wide), f32),
            jax.ShapeDtypeStruct((count, units, keys, deep), bf16),
            jax.ShapeDtypeStruct((width, width), bf16),
            jax.ShapeDtypeStruct((width, hidden), bf16),
            jax.ShapeDtypeStruct((width, hidden), bf16),
            jax.ShapeDtypeStruct((group, rows, width), bf16),
        ],
        in_specs=[VMEM] * 4 + [ANY] * 7,
        out_specs=[VMEM] * 11 + [ANY] * 4,
        scratch_shapes=[
            pltpu.VMEM((rows, width), bf16),
            pltpu.VMEM((rows, kv_width), f32),
            pltpu.VMEM((group,) + gains.shape, f32),
            pltpu.VMEM((own, width), bf16),
            pltpu.VMEM((own, hidden), bf16),
            pltpu.VMEM((own, hidden), bf16),
            pltpu.VMEM((rows, width), bf16),
            pltpu.VMEM((units, 1, wide), f32),
            pltpu.VMEM((units, 1, wide), f32),
            dma((count // 2, PARTS)),
            dma((count // 2 + 1, PARTS)),
            dma((count // 2, PARTS)),
            dma((count // 2, PARTS)),
            half_semaphores(pieces),
            half_semaphores(pieces),
            *[dma((group - 1,))] * 2,
            *[half_semaphores(1)] * 2,
            *[group_semaphores()] * 2,
            *[dma((2, group - 1))] * 2,
            dma((7,)),
        ],
        compiler_params=pltpu.CompilerParams(
            collective_id=1, has_side_effects=True, vmem_limit_bytes=60 << 20
        ),
    )(x, gains, cosine, sine, w_query, w_key, w_value, w_out, w_gate, w_up, g_rows)


class Ring:
    def __init__(self, work, landing, total, semaphores, forward, exchange=False):
        self.fsdp, self.ctx = lax.axis_index("fsdp"), lax.axis_index("ctx")
        self.group, self.count = lax.axis_size("fsdp"), lax.axis_size("ctx")
        self.work, self.landing, self.total = work, landing, total
        self.sends, self.arrivals = semaphores[:2]
        self.part_sends, self.part_arrivals, self.own_sem = semaphores[2:] if exchange else (None,) * 3
        self.exchange = exchange
        side = 0 if forward else 1
        self.place = ring_place(self.ctx, side, self.count)
        self.after = (self.fsdp, ring_ctx(lax.rem(self.place + 1, self.count), side, self.count))
        self.ticks = 2 * self.count - 2 + int(exchange)

    def chunk(self, held, index):
        if self.exchange:
            return held.at[index]
        per = held.shape[0] // self.count
        return held.at[pl.ds(index * per, per)]

    def summing(self, step, index):
        return self.copy(self.chunk(self.work, index), self.landing.at[step], step)

    def handing(self, step, index):
        held = self.chunk(self.total, index)
        return self.copy(held, held, step)

    def copy(self, source, target, step):
        return pltpu.make_async_remote_copy(
            src_ref=source,
            dst_ref=target,
            send_sem=self.sends.at[step],
            recv_sem=self.arrivals.at[step],
            device_id=self.after,
            device_id_type=MESH,
        )

    def part(self, index, step):
        peer = lax.rem(self.fsdp + step, self.group)
        return pltpu.make_async_remote_copy(
            src_ref=self.work.at[index, peer],
            dst_ref=self.total.at[index, self.fsdp],
            send_sem=self.part_sends.at[step - 1],
            recv_sem=self.part_arrivals.at[step - 1],
            device_id=(peer, self.ctx),
            device_id_type=MESH,
        )

    def own_part(self, index):
        return pltpu.make_async_copy(
            self.work.at[index, self.fsdp], self.total.at[index, self.fsdp], self.own_sem
        )

    def start(self):
        self.summing(0, self.place).start()

    def tick(self, at):
        last = self.count - 2
        gap = int(self.exchange)
        step = at - gap * jnp.where(at > last, 1, 0) if self.exchange else at
        index = lax.rem(self.place + 3 * self.count - 1 - step, self.count)

        def add(target):
            part, landed = self.chunk(self.work, index), self.landing.at[jnp.minimum(at, last)]
            for row in range(part.shape[0]):
                target[row] = (
                    part[row].astype(jnp.float32) + landed[row].astype(jnp.float32)
                ).astype(part.dtype)

        @pl.when(at <= last)
        def _():
            self.summing(jnp.minimum(at, last), index).wait_recv()

        @pl.when(at < last)
        def _():
            add(self.chunk(self.work, index))
            self.summing(jnp.minimum(at + 1, last), index).start()

        if self.exchange:

            @pl.when(at == last)
            def _():
                add(self.chunk(self.work, index))
                for peer in range(1, self.group):
                    self.part(index, peer).start()
                self.own_part(index).start()

            @pl.when(at == last + 1)
            def _():
                done = lax.rem(self.place + 1, self.count)
                self.own_part(done).wait()
                for peer in range(1, self.group):
                    self.part(done, peer).wait_recv()
                self.handing(last + 1, done).start()

        else:

            @pl.when(at == last)
            def _():
                add(self.chunk(self.total, index))
                self.handing(last + 1, index).start()

        @pl.when(at > last + gap)
        def _():
            here = jnp.maximum(step, last + 1)
            self.handing(here, index).wait_recv()

            @pl.when(here < 2 * self.count - 3)
            def _():
                self.handing(jnp.minimum(here + 1, 2 * self.count - 3), index).start()

    def finish(self):
        def wait(step, unused):
            self.handing(step, self.place).wait_send()
            return unused

        lax.fori_loop(0, 2 * self.count - 2, wait, 0)
        if self.exchange:
            for peer in range(1, self.group):
                self.part(lax.rem(self.place + 1, self.count), peer).wait_send()


class SumRing(Ring):
    def __init__(self, *args):
        super().__init__(*args)
        self.ticks = self.count - 1

    def tick(self, at):
        last = self.count - 2
        index = lax.rem(self.place + 2 * self.count - 1 - at, self.count)
        self.summing(at, index).wait_recv()
        work, landed = self.chunk(self.work, index), self.landing.at[at]

        def add(target):
            for row in range(work.shape[0]):
                target[row] = (
                    work[row].astype(jnp.float32) + landed[row].astype(jnp.float32)
                ).astype(work.dtype)

        @pl.when(at < last)
        def _():
            add(work)
            self.summing(jnp.minimum(at + 1, last), index).start()

        @pl.when(at == last)
        def _():
            add(self.total)

    def finish(self):
        def wait(step, unused):
            self.summing(step, self.place).wait_send()
            return unused

        lax.fori_loop(0, self.ticks, wait, 0)


class SpreadRing(Ring):
    def __init__(self, total, semaphores, forward):
        super().__init__(None, None, total, semaphores, forward)
        self.ticks = self.count - 1
        self.first = lax.rem(self.place + 1, self.count)

    def start(self):
        self.handing(0, self.first).start()

    def tick(self, at):
        index = lax.rem(self.place + self.count - at, self.count)
        self.handing(at, index).wait_recv()

        @pl.when(at < self.count - 2)
        def _():
            self.handing(jnp.minimum(at + 1, self.count - 2), index).start()

    def finish(self):
        def wait(step, unused):
            self.handing(step, self.place).wait_send()
            return unused

        lax.fori_loop(0, self.ticks, wait, 0)


def ring_scratch(chunk, exchange=False):
    count = lax.axis_size("ctx")
    work = (count,) + chunk if exchange else (count * chunk[0],) + chunk[1:]
    return [pltpu.VMEM(work, jnp.bfloat16), pltpu.VMEM((count - 1,) + chunk, jnp.bfloat16)]


def ring_total(chunk, exchange=False):
    count = lax.axis_size("ctx")
    work = (count,) + chunk if exchange else (count * chunk[0],) + chunk[1:]
    return jax.ShapeDtypeStruct(work, jnp.bfloat16)


def ring_semaphores(exchange=False):
    dma, steps = pltpu.SemaphoreType.DMA, 2 * lax.axis_size("ctx") - 2
    parts = lax.axis_size("fsdp") - 1
    return [dma((steps,))] * 2 + ([dma((parts,))] * 2 + [dma] if exchange else [])


def wide_split(width):
    group, count = lax.axis_size("fsdp"), lax.axis_size("ctx")
    return 2 if FF // group // LANES * (width // group // 16) >= 4 * count else 1


def query_split(width):
    return width // LANES * 7 // 9 * LANES


def out_split(width):
    return (width // LANES + 1) // 2 * LANES


def down_split(blocks, count):
    each = -(-blocks // count)
    rings = 4 if each >= 4 else 2
    return [max(1, (each + at) // rings) for at in range(rings)]


class GroupScatter:
    def __init__(self, give_sib, got_sib, give_cross, got_cross, far, got_far, sends, arrivals):
        self.give_sib, self.got_sib = give_sib, got_sib
        self.give_cross, self.got_cross = give_cross, got_cross
        self.far, self.got_far = far, got_far
        self.sends, self.arrivals = sends, arrivals
        self.fsdp, self.ctx = lax.axis_index("fsdp"), lax.axis_index("ctx")
        self.chips = lax.axis_size("fsdp") // 2
        self.chip, self.core = lax.div(self.fsdp, 2), lax.rem(self.fsdp, 2)
        self.sibling = 2 * self.chip + 1 - self.core

    def copy(self, source, target, semaphore, device):
        return pltpu.make_async_remote_copy(
            src_ref=source,
            dst_ref=target,
            send_sem=self.sends.at[semaphore],
            recv_sem=self.arrivals.at[semaphore],
            device_id=(device, self.ctx),
            device_id_type=MESH,
        )

    def to_sibling(self):
        return self.copy(self.give_sib, self.got_sib, 0, self.sibling)

    def to_cross(self, step):
        return self.copy(
            self.give_cross(step), self.got_cross.at[step - 1], step, self.sibling
        )

    def to_far(self, step):
        chip = lax.rem(self.chip + self.chips - step, self.chips)
        return self.copy(
            self.far.at[step - 1],
            self.got_far.at[step - 1],
            self.chips - 1 + step,
            2 * chip + self.core,
        )

    def add_cross(self, step):
        self.to_cross(step).wait_recv()
        held = self.far.at[step - 1]
        held[...] = (
            held[...].astype(jnp.float32) + self.got_cross[step - 1].astype(jnp.float32)
        ).astype(held.dtype)
        self.to_far(step).start()

    def total(self, own):
        self.to_sibling().wait_recv()
        value = own + self.got_sib[...].astype(jnp.float32)
        for step in range(1, self.chips):
            self.to_far(step).wait_recv()
            value = value + self.got_far[step - 1].astype(jnp.float32)
        return value

    def sent(self):
        self.to_sibling().wait_send()
        for step in range(1, self.chips):
            self.to_cross(step).wait_send()
            self.to_far(step).wait_send()


def scatter_scratch(rows, width):
    far = lax.axis_size("fsdp") // 2 - 1
    one, many = (rows, width), (far, rows, width)
    return [pltpu.VMEM(shape, jnp.bfloat16) for shape in (one, one, many, many, many, many)]


def dot_columns(left, right):
    return lax.dot_general(
        left, right, (((1,), (1,)), ((), ())), preferred_element_type=jnp.float32
    )


def tiles(count, body):
    def step(at, unused):
        body(at)
        return unused

    lax.fori_loop(0, count, step, 0)


def lane_tile(at, size):
    return pl.ds(pl.multiple_of(at * size, LANES), size)


def width_tile(width):
    return 384 if width % 384 == 0 else width


def hidden_tile(hidden):
    return 256 if hidden % 256 == 0 else 128


def transpose_into(target, source):
    rows, columns = source.shape

    def body(at):
        part = source[:, lane_tile(at, LANES)]
        target[pl.ds(pl.multiple_of(at * LANES, LANES), LANES), :] = part.T

    tiles(columns // LANES, body)


def ffn_kernel(
    x_ref, low_ref, out_ref, gain_ref, gate_in, up_in, down_in, all_g_in,
    layer_ref, resid_grad_ref, branch_ref, g_wide_ref, gate_part_out, up_part_out, layer_part_out,
    *rest,
):
    downs = len(down_split(gate_in.shape[1] // 16, lax.axis_size("ctx")))
    taken = iter(rest)

    def take(number):
        return [next(taken) for _ in range(number)]

    down_done, (gain_grad_ref,) = take(downs), take(1)
    all_n_ref, turned_n, turned_act, act_ref, gate_grad, up_grad, resid_ref, grad_own = take(8)
    down_scratch = take(2 * downs)
    give_sib, got_sib, give_cross, got_cross, far, got_far = take(6)
    n_sends, n_arrivals, grad_sends, grad_arrivals = take(4)
    gate_ref, up_ref, down_ref, all_g_ref, gate_part_ref, up_part_ref, layer_part_ref = take(7)
    (local_sems,) = take(1)
    loads = [
        pltpu.make_async_copy(source, target, local_sems.at[at])
        for at, (source, target) in enumerate(
            ((gate_in, gate_ref), (up_in, up_ref), (all_g_in, all_g_ref), (down_in, down_ref))
        )
    ]
    for copy in loads:
        copy.start()
    stores = []

    def store(source, target):
        copy = pltpu.make_async_copy(source, target, local_sems.at[len(loads) + len(stores)])
        copy.start()
        stores.append(copy)

    rings = [
        SumRing(*down_scratch[2 * at : 2 * at + 2], down_done[at], take(2), at % 2 == 0)
        for at in range(downs)
    ]
    group = lax.axis_size("fsdp")
    rows, width = x_ref.shape
    hidden = gate_ref.shape[1]
    barrier = pltpu.get_barrier_semaphore()
    greeted = greet_group(barrier) + 2
    for ring in rings[:2]:
        pl.semaphore_signal(barrier, inc=1, device_id=ring.after, device_id_type=MESH)
    step_in, step_out = hidden_tile(hidden), width_tile(width)

    def branch(at):
        columns = lane_tile(at, step_out)
        resid_ref[:, columns] = x_ref[:, columns].astype(jnp.float32) + forward_dot(
            low_ref[...], out_ref[:, columns]
        )

    tiles(width // step_out, branch)
    gain = gain_ref[...]
    scale = norm_scale(resid_ref[...])
    gathered = GroupGather(lambda shard: all_n_ref.at[shard], n_sends, n_arrivals)
    fsdp, chips = gathered.fsdp, gathered.chips
    all_n_ref[fsdp] = (resid_ref[...] * scale * gain).astype(jnp.bfloat16)
    pl.semaphore_wait(barrier, greeted)
    gathered.start(all_n_ref.at[fsdp])
    grad_sum = GroupScatter(
        give_sib,
        got_sib,
        lambda step: give_cross.at[step - 1],
        got_cross,
        far,
        got_far,
        grad_sends,
        grad_arrivals,
    )

    def hidden_part(shard):
        def body(at):
            columns = lane_tile(at, step_in)
            normed = all_n_ref[shard]
            gate = forward_dot(normed, gate_ref[:, columns])
            upward = forward_dot(normed, up_ref[:, columns])
            grad_act = dot_columns(
                all_g_ref[shard], down_ref[pl.ds(pl.multiple_of(at * step_in, LANES), step_in), :]
            )
            sigmoid = jax.nn.sigmoid(gate)
            silu = gate * sigmoid
            act_ref[shard, :, columns] = (silu * upward).astype(jnp.bfloat16)
            gate_grad[shard, :, columns] = (
                grad_act * upward * (sigmoid * (1.0 + gate * (1.0 - sigmoid)))
            ).astype(jnp.bfloat16)
            up_grad[shard, :, columns] = (grad_act * silu).astype(jnp.bfloat16)

        tiles(hidden // step_in, body)

    def grad_part(shard, target):
        def body(at):
            columns = pl.ds(pl.multiple_of(at * step_out, LANES), step_out)
            target[:, columns] = (
                dot_columns(gate_grad[shard], gate_ref[columns, :])
                + dot_columns(up_grad[shard], up_ref[columns, :])
            ).astype(target.dtype)

        tiles(width // step_out, body)

    for copy in loads:
        copy.wait()
    hidden_part(fsdp)
    gathered.sibling_here()
    sibling = gathered.sibling
    hidden_part(sibling)
    grad_part(sibling, grad_sum.give_sib)
    grad_sum.to_sibling().start()
    gathered.forward()
    grad_part(fsdp, grad_own)
    def turn_act(shard):
        transpose_into(turned_act.at[:, lane_tile(shard, rows)], act_ref.at[shard])

    turn_act(fsdp)
    turn_act(sibling)
    far_shards = []
    for step in range(1, chips):
        ours = gathered.same_core(chips - step)
        theirs = ours + sibling - fsdp
        far_shards.append((step, ours, theirs))
        gathered.crossed(step)
        hidden_part(theirs)
        hidden_part(ours)
        turn_act(theirs)
        turn_act(ours)
    blocks = hidden // 16
    spans, first = [], 0
    for ring in rings:
        last = min(blocks, first + ring.work.shape[0])
        spans.append((first, last, ring.work))
        first = last

    def down_tile(at):
        columns = lane_tile(at, step_out)
        part = forward_dot(
            turned_act[...], all_g_ref[:, :, columns].reshape(group * rows, step_out)
        ).astype(jnp.bfloat16)
        for begin, end, work in spans:
            if end > begin:
                work[: end - begin, :, columns] = part[begin * 16 : end * 16].reshape(
                    end - begin, 16, step_out
                )

    tiles(width // step_out, down_tile)
    for begin, end, work in spans:
        for spare in range(end - begin, work.shape[0]):
            work[spare] = jnp.zeros(work.shape[1:], work.dtype)
    for ring in rings:
        ring.start()
    for step, ours, theirs in far_shards:
        grad_part(theirs, give_cross.at[step - 1])
        grad_sum.to_cross(step).start()
        grad_part(ours, far.at[step - 1])
        grad_sum.add_cross(step)
    ticked = [0]

    def ring_tick(at):
        for ring in rings:

            @pl.when(at < ring.ticks)
            def _():
                ring.tick(jnp.minimum(at, ring.ticks - 1))

    def ticking(times, body):
        begin = ticked[0]

        def step(at):
            body(at)
            ring_tick(begin + at)

        tiles(times, step)
        ticked[0] += times

    for shard in range(group):
        span = slice(shard * rows, (shard + 1) * rows)
        transpose_into(turned_n.at[:, span], all_n_ref.at[shard])
    own = width // group
    row_blocks = own // 16
    for source, target in ((gate_grad, gate_part_ref), (up_grad, up_part_ref)):

        def weight_tile(at):
            columns = lane_tile(at, step_in)
            part = forward_dot(
                turned_n[...], source[:, :, columns].reshape(group * rows, step_in)
            ).astype(jnp.bfloat16)
            for block in range(step_in // LANES):
                first = (at * (step_in // LANES) + block) * row_blocks
                for owner in range(group):
                    target[owner, pl.ds(first, row_blocks)] = part[
                        owner * own : (owner + 1) * own, block * LANES : (block + 1) * LANES
                    ].reshape(row_blocks, 16, LANES)

        ticking(hidden // step_in, weight_tile)
        filled = hidden // LANES * row_blocks
        for spare in range(filled, target.shape[1]):
            for owner in range(group):
                target[owner, spare] = jnp.zeros(target.shape[2:], target.dtype)
        store(target, gate_part_out if source is gate_grad else up_part_out)

    def layer_tile(at):
        columns = lane_tile(at, step_out)
        part = forward_dot(
            act_ref[...].reshape(group * rows, hidden), down_ref[:, columns]
        ).reshape(group, rows, step_out)
        layer_part_ref[:, :, columns] = part.astype(jnp.bfloat16)

    ticking(width // step_out, layer_tile)
    store(layer_part_ref, layer_part_out)
    layer_ref[...] = resid_ref[...] + layer_part_ref[fsdp].astype(jnp.float32)
    upstream = grad_sum.total(grad_own[...])
    resid = resid_ref[...]
    scaled = upstream * gain
    grad_resid = (
        all_g_ref[fsdp].astype(jnp.float32)
        + scale * scaled
        - resid * scale**3 * jnp.mean(scaled * resid, axis=-1, keepdims=True)
    )
    gain_grad_ref[...] = jnp.sum(upstream * resid * scale, axis=0, keepdims=True)
    resid_grad_ref[...] = grad_resid
    branch_ref[...] = grad_resid.astype(jnp.bfloat16)
    units, _, wide = g_wide_ref.shape
    sequences = units // KVH
    keys = rows // sequences
    groups = wide // keys
    g_wide_ref[:, :HD, :] = jnp.zeros((units, HD, wide), g_wide_ref.dtype)
    for pair in range(H // 2):
        columns = slice(pair * 2 * HD, (pair + 1) * 2 * HD)
        mixed = dot_columns(branch_ref[...], out_ref[columns, :]).astype(jnp.bfloat16)
        for sequence in range(sequences):
            turned = mixed[sequence * keys : (sequence + 1) * keys].T
            for half in range(2):
                head = 2 * pair + half
                unit, member = sequence * KVH + head // groups, head % groups
                g_wide_ref[unit, HD:, member * keys : (member + 1) * keys] = turned[
                    half * HD : (half + 1) * HD
                ]
    begin = ticked[0]
    tiles(max(0, rings[0].ticks - begin), lambda at: ring_tick(begin + at))
    gathered.sent()
    grad_sum.sent()
    for ring in rings:
        ring.finish()
    for copy in stores:
        copy.wait()


def spread(blocks, count):
    return -(-blocks // count) * count


def feed_forward(x, low, full_out, my_gate, my_up, my_down, all_g, gain, units, wide):
    group, count = lax.axis_size("fsdp"), lax.axis_size("ctx")
    rows, width = x.shape
    hidden = my_gate.shape[1]
    blocks = spread(hidden // LANES * (width // group // 16), wide_split(width) * count)
    chips = group // 2
    dma = pltpu.SemaphoreType.DMA((2 * chips - 1,))
    bf16 = jnp.bfloat16
    down_chunks = [(per, 16, width) for per in down_split(hidden // 16, count)]
    return pl.pallas_call(
        ffn_kernel,
        out_shape=[
            jax.ShapeDtypeStruct((rows, width), jnp.float32),
            jax.ShapeDtypeStruct((rows, width), jnp.float32),
            jax.ShapeDtypeStruct((rows, width), bf16),
            jax.ShapeDtypeStruct((units, 2 * HD, wide), bf16),
            jax.ShapeDtypeStruct((group, blocks, 16, LANES), bf16),
            jax.ShapeDtypeStruct((group, blocks, 16, LANES), bf16),
            jax.ShapeDtypeStruct((group, rows, width), bf16),
            *[jax.ShapeDtypeStruct(chunk, bf16) for chunk in down_chunks],
            jax.ShapeDtypeStruct((1, width), jnp.float32),
        ],
        in_specs=[VMEM] * 4 + [ANY] * 4,
        out_specs=[VMEM] * 4 + [ANY] * 3 + [VMEM] * (1 + len(down_chunks)),
        scratch_shapes=[
            pltpu.VMEM((group, rows, width), bf16),
            pltpu.VMEM((width, group * rows), bf16),
            pltpu.VMEM((hidden, group * rows), bf16),
            pltpu.VMEM((group, rows, hidden), bf16),
            pltpu.VMEM((group, rows, hidden), bf16),
            pltpu.VMEM((group, rows, hidden), bf16),
            pltpu.VMEM((rows, width), jnp.float32),
            pltpu.VMEM((rows, width), jnp.float32),
            *[kind for chunk in down_chunks for kind in ring_scratch(chunk)],
            *scatter_scratch(rows, width),
            *[dma] * 4,
            pltpu.VMEM(my_gate.shape, bf16),
            pltpu.VMEM(my_up.shape, bf16),
            pltpu.VMEM(my_down.shape, bf16),
            pltpu.VMEM(all_g.shape, bf16),
            pltpu.VMEM((group, blocks, 16, LANES), bf16),
            pltpu.VMEM((group, blocks, 16, LANES), bf16),
            pltpu.VMEM((group, rows, width), bf16),
            pltpu.SemaphoreType.DMA((7,)),
            *[kind for _ in down_chunks for kind in ring_semaphores()],
        ],
        compiler_params=pltpu.CompilerParams(
            collective_id=2, has_side_effects=True, vmem_limit_bytes=60 << 20
        ),
    )(x, low, full_out, gain, my_gate, my_up, my_down, all_g)


def back_kernel(
    down_blocks, q_ref, g_ref, log_ref, gain_grad_ref, gain_ref, cos_ref, sin_ref,
    pairs_ref, mix_in, gate_ref, up_ref, layer_base_in, layer_part_ref, branch_ref, low_t_ref,
    normed_t_ref, w_query_in, w_key_in, w_value_in, x_in, resid_grad_in, *rest,
):
    taken = iter(rest)

    def take(number):
        return [next(taken) for _ in range(number)]

    halves, downs = wide_split(x_in.shape[1]), len(down_blocks)
    down_refs = take(downs)
    tokens_ref, layer_ref = take(2)
    wide_totals, down_totals = take(2 * halves), take(downs)
    out_a_total, out_b_total, rest_a_total, rest_b_total = take(4)
    peer_got, chain_got, layer_sib, layer_cross, layer_far = take(5)
    kv_ref, stage_ref, final_ref, qg_ref, delta_ref, grad_q_ref = take(6)
    wide_scratch = take(4 * halves)
    out_a_work, out_a_land, out_b_work, out_b_land = take(4)
    rest_a_work, rest_a_land, rest_b_work, rest_b_land = take(4)
    low_all, normed_all, branch_all, query_all, pair_all, upstream_ref, gain_give, gain_got = take(8)
    far_ref, layer_stage = take(2)
    mix_ref, layer_base_ref, w_query_ref, w_key_ref, w_value_ref, x_ref, resid_grad_ref = take(7)
    steps = Steps()
    fsdp, ctx, group, count = steps.fsdp, steps.ctx, lax.axis_size("fsdp"), lax.axis_size("ctx")
    units, deep, wide = q_ref.shape
    keys = pairs_ref.shape[2]
    rows, width = x_ref.shape
    own = width // group
    wide_rings = [
        Ring(*wide_scratch[2 * at : 2 * at + 2], wide_totals[at], take(5), at < halves, True)
        for at in range(2 * halves)
    ]
    down_rings = [SpreadRing(total, take(2), at % 2 == 0) for at, total in enumerate(down_totals)]
    out_a = Ring(out_a_work, out_a_land, out_a_total, take(2), True)
    out_b = Ring(out_b_work, out_b_land, out_b_total, take(2), False)
    layer_sum = GroupScatter(
        None,
        layer_sib,
        lambda step: layer_part_ref.at[
            2 * lax.rem(lax.div(fsdp, 2) + group // 2 - step, group // 2) + 1 - lax.rem(fsdp, 2)
        ],
        layer_cross,
        far_ref,
        layer_far,
        *take(2),
    )
    layer_sum.give_sib = layer_part_ref.at[layer_sum.sibling]
    rest_a = Ring(rest_a_work, rest_a_land, rest_a_total, take(2), True)
    rest_b = Ring(rest_b_work, rest_b_land, rest_b_total, take(2), False)
    first_rings = []
    for at in range(halves):
        first_rings += [wide_rings[at], wide_rings[halves + at]]
        first_rings += down_rings[at * downs // halves : (at + 1) * downs // halves]
    begun_rings = len(first_rings)
    first_rings += [out_a, out_b]
    peer_sends, peer_arrivals, chain_sends, chain_arrivals = take(4)
    branch_gather = GroupGather(lambda shard: branch_all.at[shard], *take(2))
    query_gather = GroupGather(lambda shard: query_all.at[shard], *take(2))
    pair_gather = GroupGather(lambda shard: pair_all.at[shard], *take(2))
    low_sends, low_arrivals, normed_sends, normed_arrivals, gain_sends, gain_arrivals = take(6)
    local_sems, stage_sems = take(2)

    barrier = pltpu.get_barrier_semaphore()
    greeted = steps.greet(barrier) + greet_group(barrier) + 2
    for device in (out_a.after, out_b.after):
        pl.semaphore_signal(barrier, inc=1, device_id=device, device_id_type=MESH)

    loads = []

    def load(source, target):
        copy = pltpu.make_async_copy(source, target, local_sems.at[len(loads)])
        copy.start()
        loads.append(copy)

    n = wide_scratch[0].shape[2]
    for at, ring in enumerate(wide_rings):
        source = (gate_ref, up_ref)[at // halves]
        for chunk in range(count):
            load(source.at[:, pl.ds((at % halves * count + chunk) * n, n)], ring.work.at[chunk])
    for ring, source in zip(down_rings, down_refs):
        load(source, ring.chunk(ring.total, ring.first))
    ring_loads = len(loads)
    load(pairs_ref, kv_ref)
    load(mix_in, mix_ref)
    load(branch_ref, branch_all.at[fsdp])
    load(low_t_ref.at[pl.ds(fsdp * own, own)], low_all.at[:, lane_tile(fsdp, rows)])
    load(normed_t_ref.at[pl.ds(fsdp * own, own)], normed_all.at[:, lane_tile(fsdp, rows)])
    slot_loads = len(loads)
    for source, target in (
        (layer_base_in, layer_base_ref),
        (w_query_in, w_query_ref),
        (w_key_in, w_key_ref),
        (w_value_in, w_value_ref),
        (x_in, x_ref),
        (resid_grad_in, resid_grad_ref),
    ):
        load(source, target)
    for copy in loads[:ring_loads]:
        copy.wait()
    pl.semaphore_wait(barrier, greeted)
    for ring in first_rings[:begun_rings]:
        ring.start()
    branch_gather.start(branch_ref)
    layer_sum.to_sibling().start()
    for step in range(1, group // 2):
        layer_sum.to_cross(step).start()

    def slices(source, target, sends, arrivals, step):
        peer = lax.rem(fsdp + step, group)
        return pltpu.make_async_remote_copy(
            src_ref=source.at[pl.ds(peer * own, own)],
            dst_ref=target.at[:, lane_tile(fsdp, rows)],
            send_sem=sends.at[step - 1],
            recv_sem=arrivals.at[step - 1],
            device_id=(peer, ctx),
            device_id_type=MESH,
        )

    turned = [
        slices(*ends, step)
        for ends in (
            (low_t_ref, low_all, low_sends, low_arrivals),
            (normed_t_ref, normed_all, normed_sends, normed_arrivals),
        )
        for step in range(1, group)
    ]
    for copy in turned:
        copy.start()

    def prepare(unit):
        q, g = q_ref[unit], g_ref[unit]
        qg_ref[unit, :wide] = q.T
        qg_ref[unit, wide:] = g.T
        delta_ref[unit] = jnp.sum(
            g[HD:].astype(jnp.float32) * mix_ref[unit], axis=0, keepdims=True
        )
        grad_q_ref[unit] = jnp.zeros((HD, wide), jnp.float32)

    for copy in loads[ring_loads:slot_loads]:
        copy.wait()
    tiles(units, prepare)

    def tick(ring, at):
        @pl.when(jnp.logical_and(at >= 0, at < ring.ticks))
        def _():
            ring.tick(jnp.clip(at, 0, ring.ticks - 1))

    late = steps.levels // 2 + 1

    def pump(at):
        lag = [0] * begun_rings + [late, late]
        for turn, ring in enumerate(first_rings):

            @pl.when(lax.rem(at, len(first_rings)) == turn)
            def _():
                tick(ring, lax.div(at, len(first_rings)) - lag[turn])

    def back(unit, first, blocks, diagonal):
        kv = kv_ref[pl.ds(first, blocks), unit].reshape(blocks * keys, deep)
        scores = jnp.dot(kv, q_ref[unit], preferred_element_type=jnp.float32)
        probs = jnp.exp(scores - log_ref[unit])
        if diagonal:
            probs = jnp.where(causal(keys, wide, scores.shape), probs, 0.0)
        grad_probs = jnp.dot(kv, g_ref[unit], preferred_element_type=jnp.float32)
        grad_scores = (probs * (grad_probs - delta_ref[unit])).astype(jnp.bfloat16)
        both = jnp.concatenate([grad_scores, probs.astype(jnp.bfloat16)], axis=1)
        grad_kv = jnp.dot(both, qg_ref[unit], preferred_element_type=jnp.float32)
        added = jnp.dot(kv.T, grad_scores, preferred_element_type=jnp.float32)
        grad_q_ref[unit] = grad_q_ref[unit] + added[:HD]
        kv_ref[pl.ds(first, blocks), unit] = grad_kv.astype(kv_ref.dtype).reshape(
            blocks, keys, deep
        )

    def across(pair):
        return pltpu.make_async_remote_copy(
            src_ref=kv_ref.at[2 * pair + 1 - steps.side],
            dst_ref=peer_got.at[pair],
            send_sem=peer_sends.at[pair],
            recv_sem=peer_arrivals.at[pair],
            device_id=steps.peer,
            device_id_type=MESH,
        )

    def down_chain(pair):
        return pltpu.make_async_remote_copy(
            src_ref=kv_ref.at[2 * pair + steps.side],
            dst_ref=chain_got.at[pair],
            send_sem=chain_sends.at[pair],
            recv_sem=chain_arrivals.at[pair],
            device_id=steps.below,
            device_id_type=MESH,
        )

    def combine(time):
        pair = time - steps.levels + steps.level

        @pl.when(jnp.logical_and(pair >= 0, pair <= steps.level))
        def _():
            for slot, expected, arrival, source in (
                (0, jnp.logical_or(pair < steps.level, steps.side == 0), across, peer_got),
                (1, steps.has_above, down_chain, chain_got),
            ):

                @pl.when(expected)
                def _():
                    arrival(pair).wait_recv()
                    copy = pltpu.make_async_copy(
                        source.at[pair], stage_ref.at[slot], stage_sems.at[slot]
                    )
                    copy.start()
                    copy.wait()

                @pl.when(jnp.logical_not(expected))
                def _():
                    stage_ref[slot] = jnp.zeros(stage_ref.shape[1:], stage_ref.dtype)

            def add(unit):
                final_ref[unit] = (
                    kv_ref[2 * pair + steps.side, unit].astype(jnp.float32)
                    + stage_ref[0, unit].astype(jnp.float32)
                    + stage_ref[1, unit].astype(jnp.float32)
                )

            tiles(units, add)

            @pl.when(pair < steps.level)
            def _():
                kv_ref[2 * pair + steps.side] = final_ref[...].astype(kv_ref.dtype)
                down_chain(pair).start()

    row_blocks = own // 16

    def weight_grad(left, right, begin, end, target, first, loop):
        span = LANES * next(n for n in (3, 2, 1) if (end - begin) % (n * LANES) == 0)

        def body(at):
            columns = pl.ds(pl.multiple_of(begin + at * span, LANES), span)
            part = forward_dot(
                left[...], right[:, :, columns].reshape(group * rows, span)
            ).astype(jnp.bfloat16)
            for block in range(span // LANES):
                here = first + (at * (span // LANES) + block) * row_blocks
                target[pl.ds(here, row_blocks)] = part[
                    :, block * LANES : (block + 1) * LANES
                ].reshape(row_blocks, 16, LANES)

        loop((end - begin) // span, body)
        return first + (end - begin) // LANES * row_blocks

    def clear_from(target, first):
        for spare in range(first, target.shape[0]):
            target[spare] = jnp.zeros((16, LANES), jnp.bfloat16)

    def out_grad():
        for copy in turned[: group - 1]:
            copy.wait_recv()
        branch_gather.forward()
        branch_gather.sibling_here()
        for step in range(1, branch_gather.chips):
            branch_gather.crossed(step)
        split = out_split(width)
        clear_from(out_a_work, weight_grad(low_all, branch_all, 0, split, out_a_work, 0, tiles))
        clear_from(out_b_work, weight_grad(low_all, branch_all, split, width, out_b_work, 0, tiles))
        out_a.start()
        out_b.start()

    turns = units // 2
    rings = max(turns, len(first_rings))

    def slot(pair):
        def turn(at):
            @pl.when(jnp.logical_and(pair < steps.level, at < turns))
            def _():
                for unit in (2 * at, 2 * at + 1):
                    back(unit, 2 * pair, 2, False)

            @pl.when(jnp.logical_and(pair == steps.level, at < turns))
            def _():
                for unit in (2 * at, 2 * at + 1):
                    back(unit, ctx, 1, True)

            @pl.when((pair == steps.level) & (steps.side == 1) & (at < turns))
            def _():
                for unit in (2 * at, 2 * at + 1):
                    back(unit, ctx - 1, 1, False)

            pump(pair * rings + at)

        tiles(rings, turn)

        @pl.when(jnp.logical_or(pair < steps.level, (pair == steps.level) & (steps.side == 1)))
        def _():
            across(pair).start()

        combine(pair)

        @pl.when(pair == late - 1)
        def _():
            out_grad()

    tiles(steps.levels, slot)
    pumped = [steps.levels * rings]

    def pump_next(times=1):
        def body(at, unused, begin=pumped[0]):
            pump(begin + at)
            return unused

        lax.fori_loop(0, times, body, 0)
        pumped[0] += times

    def pumping(times, body):
        begin = pumped[0]

        def step(at):
            body(at)
            tiles(2, lambda more: pump(begin + 2 * at + more))

        tiles(times, step)
        pumped[0] += 2 * times

    cosine, sine = cos_ref[...], sin_ref[...]

    def unturn(columns):
        first, second = columns[: HD // 2], columns[HD // 2 :]
        return jnp.concatenate(
            [first * cosine + second * sine, second * cosine - first * sine], axis=0
        )

    sequences = units // KVH
    groups = wide // keys
    for sequence in range(sequences):
        span = slice(sequence * keys, (sequence + 1) * keys)
        for pair in range(H // 2):
            heads = []
            for head in (2 * pair, 2 * pair + 1):
                unit, member = sequence * KVH + head // groups, head % groups
                part = grad_q_ref[unit, :, member * keys : (member + 1) * keys]
                heads.append(unturn(part * HD ** (-0.5)))
            query_all[fsdp, span, pair * 2 * HD : (pair + 1) * 2 * HD] = (
                jnp.concatenate(heads, axis=0).astype(jnp.bfloat16).T
            )
        pump_next(3)
    query_gather.start(query_all.at[fsdp])
    combine(steps.levels)
    kv_width = KVH * HD
    for sequence in range(sequences):
        span = slice(sequence * keys, (sequence + 1) * keys)
        for pair in range(KVH // 2):
            turned_keys, turned_values = [], []
            for unit in (sequence * KVH + 2 * pair, sequence * KVH + 2 * pair + 1):
                part = final_ref[unit].T
                turned_keys.append(unturn(part[:HD]))
                turned_values.append(part[HD:])
            for start, parts in ((0, turned_keys), (kv_width, turned_values)):
                pair_all[fsdp, span, start + pair * 2 * HD : start + (pair + 1) * 2 * HD] = (
                    jnp.concatenate(parts, axis=0).astype(jnp.bfloat16).T
                )
    pair_gather.start(pair_all.at[fsdp])
    pump_next(2)
    query_gather.forward()
    step_out = width_tile(width)

    def upstream_tile(at):
        columns = pl.ds(pl.multiple_of(at * step_out, LANES), step_out)
        upstream_ref[:, columns] = (
            dot_columns(query_all[fsdp], w_query_ref[columns, :])
            + dot_columns(pair_all[fsdp, :, :kv_width], w_key_ref[columns, :])
            + dot_columns(pair_all[fsdp, :, kv_width:], w_value_ref[columns, :])
        )

    for copy in loads[slot_loads:]:
        copy.wait()
    pumping(width // step_out, upstream_tile)
    inputs = x_ref[...].astype(jnp.float32)
    scale = norm_scale(inputs)
    upstream = upstream_ref[...]
    scaled = upstream * gain_ref[...]
    tokens_ref[...] = (
        resid_grad_ref[...]
        + scale * scaled
        - inputs * scale**3 * jnp.mean(scaled * inputs, axis=-1, keepdims=True)
    )
    gain_attn = jnp.sum(upstream * inputs * scale, axis=0, keepdims=True)
    lanes = width // LANES
    gain_give[...] = jnp.zeros(gain_give.shape, jnp.float32)
    for block in range(lanes):
        columns = slice(block * LANES, (block + 1) * LANES)
        gain_give[block : block + 1, :] = gain_attn[:, columns]
        gain_give[lanes + block : lanes + block + 1, :] = gain_grad_ref[:, columns]

    def gain_copy(step):
        peer = lax.rem(fsdp + step, group)
        return pltpu.make_async_remote_copy(
            src_ref=gain_give,
            dst_ref=gain_got.at[step - 1],
            send_sem=gain_sends.at[step - 1],
            recv_sem=gain_arrivals.at[step - 1],
            device_id=(peer, ctx),
            device_id_type=MESH,
        )

    for step in range(1, group):
        gain_copy(step).start()
    pump_next()
    for copy in turned[group - 1 :]:
        copy.wait_recv()
    query_gather.sibling_here()
    for step in range(1, query_gather.chips):
        query_gather.crossed(step)
    split = query_split(width)
    filled_a = weight_grad(normed_all, query_all, 0, split, rest_a_work, 0, pumping)
    filled_b = weight_grad(normed_all, query_all, split, width, rest_b_work, 0, pumping)
    pair_gather.forward()
    pump_next()
    pair_gather.sibling_here()
    for step in range(1, pair_gather.chips):
        pair_gather.crossed(step)
    filled_b = weight_grad(normed_all, pair_all, 0, 2 * kv_width, rest_b_work, filled_b, pumping)
    for step in range(1, layer_sum.chips):
        ours = layer_part_ref.at[2 * lax.rem(layer_sum.chip + layer_sum.chips - step, layer_sum.chips) + layer_sum.core]
        for source, target in ((ours, far_ref.at[step - 1]), (layer_cross.at[step - 1], layer_stage)):
            if source is not ours:
                layer_sum.to_cross(step).wait_recv()
            copy = pltpu.make_async_copy(source, target, stage_sems.at[0])
            copy.start()
            copy.wait()
        far_ref[step - 1] = (
            far_ref[step - 1].astype(jnp.float32) + layer_stage[...].astype(jnp.float32)
        ).astype(jnp.bfloat16)
        layer_sum.to_far(step).start()
    gains = gain_give[...]
    for step in range(1, group):
        gain_copy(step).wait_recv()
        gains = gains + gain_got[step - 1]
    gain_tiles = gains.shape[0] // 16
    rest_a_work[filled_a : filled_a + gain_tiles] = gains.astype(jnp.bfloat16).reshape(
        gain_tiles, 16, LANES
    )
    clear_from(rest_a_work, filled_a + gain_tiles)
    clear_from(rest_b_work, filled_b)
    rest_a.start()
    rest_b.start()
    begun = pumped[0]
    total_pumps = max(wide_rings[0].ticks, late + out_a.ticks) * len(first_rings)

    half = -(-(total_pumps - begun) // rest_a.ticks)

    def layer_close():
        layer_sum.to_sibling().wait_recv()
        arrived = [layer_sib]
        for step in range(1, layer_sum.chips):
            layer_sum.to_far(step).wait_recv()
            arrived.append(layer_far.at[step - 1])
        for source in arrived:
            copy = pltpu.make_async_copy(source, layer_stage, stage_sems.at[0])
            copy.start()
            copy.wait()

            def add(at):
                block = pl.ds(pl.multiple_of(at * 32, 32), 32)
                layer_base_ref[block] = layer_base_ref[block] + layer_stage[block].astype(
                    jnp.float32
                )

            tiles(rows // 32, add)

        def close(at):
            block = pl.ds(pl.multiple_of(at * 32, 32), 32)
            layer_ref[block] = layer_base_ref[block].astype(jnp.bfloat16)

        tiles(rows // 32, close)

    def last_ticks(at, unused):
        tiles(half, lambda turn: pump(jnp.minimum(begun + half * at + turn, total_pumps)))
        tick(rest_a, at)
        tick(rest_b, at)

        @pl.when(at == rest_a.ticks * 3 // 4)
        def _():
            layer_close()

        return unused

    lax.fori_loop(0, rest_a.ticks, last_ticks, 0)
    layer_sum.sent()
    for ring in first_rings + [rest_a, rest_b]:
        ring.finish()
    for copy in turned:
        copy.wait_send()
    for gather in (branch_gather, query_gather, pair_gather):
        gather.sent()
    for step in range(1, group):
        gain_copy(step).wait_send()

    def sent(pair):
        @pl.when(jnp.logical_or(pair < steps.level, steps.side == 1))
        def _():
            across(pair).wait_send()

        @pl.when(pair < steps.level)
        def _():
            down_chain(pair).wait_send()

    tiles(steps.level + 1, sent)


def layer_back(
    q_wide, g_wide, log_total, gain_grad, gain, cosine, sine, all_pairs, mix, gate_part, up_part,
    layer_base, layer_parts, branch, low_t, normed_t, w_query, w_key, w_value, x, resid_grad, downs,
):
    group, count = lax.axis_size("fsdp"), lax.axis_size("ctx")
    units, deep, wide = q_wide.shape
    keys = all_pairs.shape[2]
    rows, width = x.shape
    own, kv_width = width // group, w_key.shape[1]
    bf16, f32 = jnp.bfloat16, jnp.float32
    dma = pltpu.SemaphoreType.DMA
    halves = wide_split(width)
    wide_chunk = (group, gate_part.shape[1] // (halves * count), 16, LANES)
    gain_rows = spread(2 * (width // LANES), 16)
    split, row_blocks = query_split(width), own // 16
    out_first = out_split(width)
    chips = group // 2
    small_chunks = [
        (spread(held, count) // count, 16, LANES)
        for held in (
            out_first // LANES * row_blocks,
            (width - out_first) // LANES * row_blocks,
            split // LANES * row_blocks + gain_rows // 16,
            (width - split + 2 * kv_width) // LANES * row_blocks,
        )
    ]
    levels = count // 2
    loaded = [mix, layer_base, w_query, w_key, w_value, x, resid_grad]
    return pl.pallas_call(
        functools.partial(back_kernel, [part.shape[0] for part in downs]),
        out_shape=[
            jax.ShapeDtypeStruct((rows, width), f32),
            jax.ShapeDtypeStruct((rows, width), bf16),
            *[ring_total(wide_chunk, True)] * (2 * halves),
            *[ring_total(part.shape) for part in downs],
            *[ring_total(chunk) for chunk in small_chunks],
            *[jax.ShapeDtypeStruct((levels, units, keys, deep), bf16)] * 2,
            jax.ShapeDtypeStruct((rows, width), bf16),
            *[jax.ShapeDtypeStruct((chips - 1, rows, width), bf16)] * 2,
        ],
        in_specs=[VMEM] * 7 + [ANY] * (14 + len(downs)),
        out_specs=[VMEM] * (6 + 2 * halves + len(downs)) + [ANY] * 5,
        scratch_shapes=[
            pltpu.VMEM(all_pairs.shape, bf16),
            pltpu.VMEM((2, units, keys, deep), bf16),
            pltpu.VMEM((units, keys, deep), f32),
            pltpu.VMEM((units, 2 * wide, deep), bf16),
            pltpu.VMEM((units, 1, wide), f32),
            pltpu.VMEM((units, HD, wide), f32),
            *[kind for _ in range(2 * halves) for kind in ring_scratch(wide_chunk, True)],
            *[kind for chunk in small_chunks for kind in ring_scratch(chunk)],
            pltpu.VMEM((own, group * rows), bf16),
            pltpu.VMEM((own, group * rows), bf16),
            pltpu.VMEM((group, rows, width), bf16),
            pltpu.VMEM((group, rows, width), bf16),
            pltpu.VMEM((group, rows, 2 * kv_width), bf16),
            pltpu.VMEM((rows, width), f32),
            pltpu.VMEM((gain_rows, LANES), f32),
            pltpu.VMEM((group - 1, gain_rows, LANES), f32),
            pltpu.VMEM((chips - 1, rows, width), bf16),
            pltpu.VMEM((rows, width), bf16),
            *[pltpu.VMEM(array.shape, array.dtype) for array in loaded],
            *[kind for _ in range(2 * halves) for kind in ring_semaphores(True)],
            *[kind for _ in range(len(downs) + 2) for kind in ring_semaphores()],
            *[dma((group - 1,))] * 2,
            *[kind for _ in range(2) for kind in ring_semaphores()],
            *[dma((levels,))] * 4,
            *[group_semaphores()] * 6,
            *[dma((group - 1,))] * 6,
            dma((11 + len(downs) + 2 * halves * count,)),
            dma((2,)),
        ],
        compiler_params=pltpu.CompilerParams(
            collective_id=3, has_side_effects=True, vmem_limit_bytes=62 << 20
        ),
    )(
        q_wide, g_wide, log_total, gain_grad, gain, cosine, sine, all_pairs, mix, gate_part, up_part,
        layer_base, layer_parts, branch, low_t, normed_t, w_query, w_key, w_value, x, resid_grad,
        *downs,
    )


def finish_kernel(halves, downs, *refs):
    wides, refs = refs[: 2 * halves], refs[2 * halves :]
    down_refs, refs = refs[:downs], refs[downs:]
    out_a_ref, out_b_ref, rest_a_ref, rest_b_ref = refs[:4]
    query_grad, key_grad, value_grad, out_grad, gate_grad, up_grad, down_grad = refs[4:]
    rows = gate_grad.shape[0]
    row_blocks = rows // 16
    for sources, target in ((wides[:halves], gate_grad), (wides[halves:], up_grad)):
        held = jnp.concatenate(
            [source[...].reshape((-1,) + source.shape[3:]) for source in sources], axis=0
        )
        for block in range(target.shape[1] // LANES):
            target[:, block * LANES : (block + 1) * LANES] = (
                held[block * row_blocks : (block + 1) * row_blocks]
                .reshape(rows, LANES)
                .astype(jnp.float32)
            )

    @pl.when(pl.program_id(0) == 0)
    def _():
        def unpack(source, first, target, begin, end):
            for block in range(begin, end):
                here = first + (block - begin) * row_blocks
                target[:, block * LANES : (block + 1) * LANES] = (
                    source[here : here + row_blocks].reshape(rows, LANES).astype(jnp.float32)
                )
            return first + (end - begin) * row_blocks

        width, kv_width = query_grad.shape[1], key_grad.shape[1]
        split = query_split(width) // LANES
        middle = out_split(width) // LANES
        unpack(out_a_ref, 0, out_grad, 0, middle)
        unpack(out_b_ref, 0, out_grad, middle, width // LANES)
        unpack(rest_a_ref, 0, query_grad, 0, split)
        at = unpack(rest_b_ref, 0, query_grad, split, width // LANES)
        at = unpack(rest_b_ref, at, key_grad, 0, kv_width // LANES)
        unpack(rest_b_ref, at, value_grad, 0, kv_width // LANES)
        blocks, begin = down_grad.shape[0] // 16, 0
        for source in down_refs:
            end = min(blocks, begin + source.shape[0])
            if end > begin:
                down_grad[begin * 16 : end * 16, :] = (
                    source[: end - begin]
                    .reshape((end - begin) * 16, down_grad.shape[1])
                    .astype(jnp.float32)
                )
            begin = end


def finish(wides, downs, smalls, own, width, kv_width, hidden):
    count, group, n = wides[0].shape[:3]

    def whole(array):
        return pl.BlockSpec(array.shape, lambda part, rank=len(array.shape): (0,) * rank)

    wide = pl.BlockSpec((count, 1, n, 16, LANES), lambda part: (0, part, 0, 0, 0))
    outs = [
        jax.ShapeDtypeStruct((own, columns), jnp.float32)
        for columns in (width, kv_width, kv_width, width, FF, FF)
    ] + [jax.ShapeDtypeStruct((hidden, width), jnp.float32)]
    slice_spec = pl.BlockSpec((own, FF // group), lambda part: (0, part))
    return pl.pallas_call(
        functools.partial(finish_kernel, len(wides) // 2, len(downs)),
        grid=(group,),
        out_shape=outs,
        in_specs=[wide] * len(wides) + [whole(a) for a in (*downs, *smalls)],
        out_specs=[whole(a) for a in outs[:4]] + [slice_spec, slice_spec, whole(outs[6])],
        compiler_params=pltpu.CompilerParams(vmem_limit_bytes=60 << 20),
    )(*wides, *downs, *smalls)


def on_device(
    tokens, w_query, w_key, w_value, w_out, w_gate, w_up, w_down, gain_attn, gain_ffn, cotangent
):
    block_len, seq_count, width = tokens.shape
    rows_count = block_len * seq_count
    kv_width = KVH * HD
    positions = lax.axis_index("ctx") * block_len + jnp.arange(block_len, dtype=jnp.int32)
    freqs = ROTARY_BASE ** (-2.0 * jnp.arange(HD // 2, dtype=jnp.float32) / HD)
    angles = freqs[:, None] * positions.astype(jnp.float32)[None, :]
    cosine, sine = jnp.cos(angles), jnp.sin(angles)
    x_rows = jnp.swapaxes(tokens, 0, 1).reshape(rows_count, width)
    g_rows = jnp.swapaxes(cotangent, 0, 1).reshape(rows_count, width)
    own = gain_attn.shape[0]
    units = seq_count * KVH
    wide = H // KVH * block_len
    own_gains = jnp.pad(
        jnp.stack([gain_attn, gain_ffn]).astype(jnp.float32), ((0, 6), (0, spread(own, LANES) - own))
    )
    (
        q_wide, normed_t, gains, full_query, full_key, full_value, attn_low, low_t, mix_unit, log_total,
        all_pairs, full_out, my_gate, my_up, all_g,
    ) = attend(
        x_rows, own_gains, cosine, sine, w_query, w_key, w_value, w_out, w_gate, w_up, g_rows, seq_count
    )
    layer_base, grad_resid, grad_branch, g_wide, gate_part, up_part, layer_parts, *downs = (
        feed_forward(
            x_rows, attn_low, full_out, my_gate, my_up, w_down, all_g, gains[1:2], units, wide
        )
    )
    downs, gain_term_ffn = downs[:-1], downs[-1]
    grad_tokens, layer_out, *sums = layer_back(
        q_wide, g_wide, log_total, gain_term_ffn, gains[:1], cosine, sine, all_pairs, mix_unit,
        gate_part, up_part, layer_base, layer_parts, grad_branch, low_t, normed_t, full_query,
        full_key, full_value, x_rows, grad_resid, downs,
    )
    wides, sums = sums[: 2 * wide_split(width)], sums[2 * wide_split(width) :]
    smalls = sums[len(downs) : len(downs) + 4]
    filled = query_split(width) // LANES * (own // 16)
    gain_grads = smalls[2][filled:].reshape(-1, LANES)[: 2 * (width // LANES)].reshape(2, width)
    gain_grads = lax.dynamic_slice_in_dim(gain_grads, lax.axis_index("fsdp") * own, own, 1)
    gain_grads = gain_grads.astype(jnp.float32)
    grads = finish(wides, sums[: len(downs)], smalls, own, width, kv_width, w_down.shape[0])
    return (
        jnp.swapaxes(layer_out.reshape(seq_count, block_len, width), 0, 1),
        jnp.swapaxes(grad_tokens.reshape(seq_count, block_len, width), 0, 1),
        *grads,
        gain_grads[0],
        gain_grads[1],
    )


def solution(mesh):
    return jax.shard_map(
        on_device,
        mesh=mesh,
        in_specs=(
            P("ctx", "fsdp", None),
            P("fsdp", None),
            P("fsdp", None),
            P("fsdp", None),
            P("fsdp", None),
            P("fsdp", None),
            P("fsdp", None),
            P("fsdp", None),
            P("fsdp"),
            P("fsdp"),
            P("ctx", "fsdp", None),
        ),
        out_specs=(
            P("ctx", "fsdp", None),
            P("ctx", "fsdp", None),
            P("fsdp", None),
            P("fsdp", None),
            P("fsdp", None),
            P("fsdp", None),
            P("fsdp", None),
            P("fsdp", None),
            P("fsdp", None),
            P("fsdp"),
            P("fsdp"),
        ),
        check_vma=False,
    )
```

```python
import functools

import jax
import jax.numpy as jnp
from jax import lax
from jax.experimental import pallas as pl
from jax.experimental.pallas import tpu as pltpu
from jax.sharding import PartitionSpec as P

H = 18
KVH = 6
HD = 64
FF = 3072


EPSILON = 1e-05
ROTARY_BASE = 10000.0
MASKED_SCORE = -1e30


def norm_scale(rows):
    return lax.rsqrt(jnp.mean(rows * rows, axis=-1, keepdims=True) + EPSILON)


def forward_dot(left, right):
    return jnp.dot(left, right, preferred_element_type=jnp.float32)


MESH = pl.DeviceIdType.MESH
LANES = 128


def ring_place(ctx, fsdp, count):
    column, side = lax.div(ctx, 2), lax.rem(ctx, 2)
    place = column + side * (count - 1 - 2 * column)
    odd = lax.rem(fsdp, 2)
    return place + odd * (count - 1 - 2 * place)


def ring_ctx(place, fsdp, count):
    odd = lax.rem(fsdp, 2)
    place = place + odd * (count - 1 - 2 * place)
    late = lax.div(place, count // 2)
    return (1 - late) * 2 * place + late * (2 * (count - 1 - place) + 1)


class GroupGather:
    def __init__(self, shard_of, sends, arrivals):
        self.shard_of, self.sends, self.arrivals = shard_of, sends, arrivals
        self.fsdp, self.ctx = lax.axis_index("fsdp"), lax.axis_index("ctx")
        self.chips = lax.axis_size("fsdp") // 2
        self.chip, self.core = lax.div(self.fsdp, 2), lax.rem(self.fsdp, 2)
        self.sibling = 2 * self.chip + 1 - self.core

    def copy(self, source, shard, semaphore, device):
        return pltpu.make_async_remote_copy(
            src_ref=source,
            dst_ref=self.shard_of(shard),
            send_sem=self.sends.at[semaphore],
            recv_sem=self.arrivals.at[semaphore],
            device_id=(device, self.ctx),
            device_id_type=MESH,
        )

    def same_core(self, step):
        return 2 * lax.rem(self.chip + step, self.chips) + self.core

    def across(self, source):
        return self.copy(source, self.fsdp, 0, self.sibling)

    def out(self, source, step):
        return self.copy(source, self.fsdp, step, self.same_core(step))

    def onward(self, step):
        shard = self.same_core(self.chips - step)
        return self.copy(self.shard_of(shard), shard, self.chips - 1 + step, self.sibling)

    def start(self, source):
        for step in range(1, self.chips):
            self.out(source, step).start()
        self.across(source).start()

    def forward(self):
        own = self.shard_of(self.fsdp)
        for step in range(1, self.chips):
            self.out(own, step).wait_recv()
            self.onward(step).start()

    def sibling_here(self):
        self.across(self.shard_of(self.fsdp)).wait_recv()

    def crossed(self, step):
        self.onward(step).wait_recv()

    def sent(self):
        own = self.shard_of(self.fsdp)
        self.across(own).wait_send()
        for step in range(1, self.chips):
            self.out(own, step).wait_send()
            self.onward(step).wait_send()

    def finish(self):
        self.forward()
        self.sibling_here()
        for step in range(1, self.chips):
            self.crossed(step)
        self.sent()


class HalfGather:
    def __init__(self, held, own_rows, sends, arrivals):
        self.held, self.own = held, own_rows
        self.sends, self.arrivals = sends, arrivals
        self.fsdp, self.ctx = lax.axis_index("fsdp"), lax.axis_index("ctx")
        self.chips = lax.axis_size("fsdp") // 2
        self.chip, self.core = lax.div(self.fsdp, 2), lax.rem(self.fsdp, 2)
        self.sibling = 2 * self.chip + 1 - self.core
        self.side = lax.rem(self.ctx, 2)
        self.pair = self.ctx + 1 - 2 * self.side
        first = -(-own_rows // 32) * 16
        self.halves = ((0, first), (first, own_rows - first))

    def same_core(self, step):
        return 2 * lax.rem(self.chip + step, self.chips) + self.core

    def rows(self, shard, half=None):
        begin, size = (0, self.own) if half is None else self.halves[half]
        return self.held.at[pl.ds(shard * self.own + begin, size)]

    def copy(self, source, target, semaphore, device):
        return pltpu.make_async_remote_copy(
            src_ref=source,
            dst_ref=target,
            send_sem=self.sends.at[semaphore],
            recv_sem=self.arrivals.at[semaphore],
            device_id=device,
            device_id_type=MESH,
        )

    def on_side(self, body):
        for half in range(2):

            @pl.when(self.side == half)
            def _(half=half):
                body(half)

    def across(self, source):
        return self.copy(source, self.rows(self.fsdp), 0, (self.sibling, self.ctx))

    def out(self, source, step, half):
        begin, size = self.halves[half]
        return self.copy(
            source.at[pl.ds(begin, size)],
            self.rows(self.fsdp, half),
            step,
            (self.same_core(step), self.ctx),
        )

    def to_pair(self, step, half):
        part = self.rows(self.same_core(self.chips - step), half)
        return self.copy(part, part, self.chips - 1 + step, (self.fsdp, self.pair))

    def onward(self, step):
        part = self.rows(self.same_core(self.chips - step))
        return self.copy(part, part, 2 * self.chips - 2 + step, (self.sibling, self.ctx))

    def start(self, source):
        def send(half):
            for step in range(1, self.chips):
                self.out(source, step, half).start()

        self.on_side(send)
        self.across(source).start()

    def to_pairs(self):
        def forward(half):
            for step in range(1, self.chips):
                self.out(self.rows(self.fsdp), step, half).wait_recv()
                self.to_pair(step, half).start()

        self.on_side(forward)

    def to_sibling(self):
        def forward(half):
            for step in range(1, self.chips):
                self.to_pair(step, 1 - half).wait_recv()

        self.on_side(forward)
        for step in range(1, self.chips):
            self.onward(step).start()

    def arrived(self):
        self.across(self.rows(self.fsdp)).wait_recv()
        for step in range(1, self.chips):
            self.onward(step).wait_recv()

    def sent(self):
        def wait(half):
            for step in range(1, self.chips):
                self.out(self.rows(self.fsdp), step, half).wait_send()
                self.to_pair(step, half).wait_send()

        self.on_side(wait)
        self.across(self.rows(self.fsdp)).wait_send()
        for step in range(1, self.chips):
            self.onward(step).wait_send()


def half_semaphores(many):
    return pltpu.SemaphoreType.DMA((many, 3 * (lax.axis_size("fsdp") // 2) - 2))


def group_semaphores():
    return pltpu.SemaphoreType.DMA((lax.axis_size("fsdp") - 1,))


def greet_group(barrier):
    fsdp, ctx, group = lax.axis_index("fsdp"), lax.axis_index("ctx"), lax.axis_size("fsdp")
    for step in range(1, group):
        peer = lax.rem(fsdp + step, group)
        pl.semaphore_signal(barrier, inc=1, device_id=(peer, ctx), device_id_type=MESH)
    return group - 1


class Steps:
    def __init__(self):
        self.fsdp, self.ctx = lax.axis_index("fsdp"), lax.axis_index("ctx")
        self.levels = lax.axis_size("ctx") // 2
        self.level, self.side = lax.div(self.ctx, 2), lax.rem(self.ctx, 2)
        self.peer = (self.fsdp, 2 * self.level + 1 - self.side)
        self.above = (self.fsdp, lax.rem(self.ctx + 2, 2 * self.levels))
        self.below = (self.fsdp, lax.rem(self.ctx + 2 * self.levels - 2, 2 * self.levels))
        self.has_above = self.level + 1 < self.levels
        self.has_below = self.level > 0

    def greet(self, barrier):
        pl.semaphore_signal(barrier, inc=1, device_id=self.peer, device_id_type=MESH)

        @pl.when(self.has_above)
        def _():
            pl.semaphore_signal(barrier, inc=1, device_id=self.above, device_id_type=MESH)

        @pl.when(self.has_below)
        def _():
            pl.semaphore_signal(barrier, inc=1, device_id=self.below, device_id_type=MESH)

        return 1 + jnp.minimum(self.level, 1) + jnp.minimum(self.levels - 1 - self.level, 1)


PARTS = 2


def causal(keys, wide, shape):
    key_at = lax.broadcasted_iota(jnp.int32, shape, 0)
    query_at = lax.rem(lax.broadcasted_iota(jnp.int32, shape, 1), keys)
    return key_at <= query_at


def attend_kernel(
    x_ref, gain_ref, cos_ref, sin_ref, query_ref, key_ref, value_ref, out_ref, gate_ref, up_ref, g_ref,
    q_ref, normed_t_ref, gain_attn_ref, gain_ffn_ref, full_query, full_key, full_value,
    low_ref, low_t_ref, mix_ref, log_ref, all_ref, full_out_ref, my_gate_ref, my_up_ref, all_g_ref,
    normed_ref, key_rows, gain_all, own_out, own_gate, own_up, own_g,
    top_ref, total_ref, chain_sends, chain_arrivals, peer_sends, peer_arrivals,
    half_sends, half_arrivals, gain_sends, gain_arrivals,
    out_sends, out_arrivals, g_sends, g_arrivals,
    part_sends, part_arrivals, local_sems,
):
    steps = Steps()
    fsdp, ctx, group = steps.fsdp, steps.ctx, lax.axis_size("fsdp")
    units, deep, wide = q_ref.shape
    keys = all_ref.shape[2]
    per_part = units // PARTS
    rows_count, width = x_ref.shape
    own = query_ref.shape[0]
    sequences, groups = units // KVH, H // KVH
    barrier = pltpu.get_barrier_semaphore()
    greeted = steps.greet(barrier) + greet_group(barrier)
    span = KVH * HD
    pieces = [(key_ref, full_key, 0), (value_ref, full_value, 0)]
    pieces += [(query_ref, full_query, start) for start in range(0, width, span)]
    gathers = []
    for at, (source, target, start) in enumerate(pieces):
        columns = pl.ds(start, span)
        gather = HalfGather(
            target.at[:, columns], own, half_sends.at[at], half_arrivals.at[at]
        )
        gathers.append((gather, source.at[:, columns]))
    own_rows = pl.ds(fsdp * own, own)
    own_copies = [
        pltpu.make_async_copy(source, target.at[own_rows], local_sems.at[4 + at])
        for at, (source, target) in enumerate(
            ((key_ref, full_key), (value_ref, full_value), (query_ref, full_query))
        )
    ]
    for copy in own_copies:
        copy.start()
    gain_all[fsdp] = gain_ref[...]
    pl.semaphore_wait(barrier, greeted)

    def gain_copy(step):
        peer = lax.rem(fsdp + step, group)
        return pltpu.make_async_remote_copy(
            src_ref=gain_ref,
            dst_ref=gain_all.at[fsdp],
            send_sem=gain_sends.at[step - 1],
            recv_sem=gain_arrivals.at[step - 1],
            device_id=(peer, ctx),
            device_id_type=MESH,
        )

    for step in range(1, group):
        gain_copy(step).start()
    for gather, source in gathers:
        gather.start(source)
    inputs = x_ref[...].astype(jnp.float32)
    scale = norm_scale(inputs)
    q_ref[:, HD:, :] = jnp.zeros((units, HD, wide), q_ref.dtype)
    for step in range(1, group):
        gain_copy(step).wait_recv()
    gains = jnp.concatenate([gain_all[shard][:, :own] for shard in range(group)], axis=1)
    gain_attn_ref[...] = gains[:1]
    gain_ffn_ref[...] = gains[1:2]
    normed_ref[...] = (inputs * scale * gains[:1]).astype(jnp.bfloat16)
    cosine, sine = cos_ref[...], sin_ref[...]

    def turn(columns):
        first, second = columns[: HD // 2], columns[HD // 2 :]
        return jnp.concatenate(
            [first * cosine - second * sine, second * cosine + first * sine], axis=0
        ).astype(jnp.bfloat16)

    def block_copy(level, part, side, semaphores, arrivals, arrives, device):
        block = 2 * (steps.level - level) + side
        held = all_ref.at[block, pl.ds(part * per_part, per_part)]
        return pltpu.make_async_remote_copy(
            src_ref=held,
            dst_ref=held,
            send_sem=semaphores.at[level, part],
            recv_sem=arrivals.at[arrives, part],
            device_id=device,
            device_id_type=MESH,
        )

    def chain(level, part):
        return block_copy(
            level, part, steps.side, chain_sends, chain_arrivals, level + 1, steps.above
        )

    def across(level, part):
        return block_copy(
            level, part, steps.side, peer_sends, peer_arrivals, level, steps.peer
        )

    def pass_on(level, part):
        @pl.when(steps.has_above)
        def _():
            chain(level, part).start()

    def project(at):
        _, weight, start = pieces[at]
        made = forward_dot(normed_ref[...], weight[:, start : start + span])
        if at == 0:
            key_rows[...] = made
            return
        for sequence in range(sequences):
            block = slice(sequence * keys, (sequence + 1) * keys)
            for pair in range(span // (2 * HD)):
                columns = slice(pair * 2 * HD, (pair + 1) * 2 * HD)
                turned = made[block, columns].T
                if at == 1:
                    turned_keys = key_rows[block, columns].T
                    for half in range(2):
                        held = slice(half * HD, (half + 1) * HD)
                        both = jnp.concatenate(
                            [turn(turned_keys[held]), turned[held].astype(jnp.bfloat16)], axis=0
                        )
                        all_ref[ctx, sequence * KVH + 2 * pair + half] = both.T
                else:
                    for half in range(2):
                        head = start // HD + 2 * pair + half
                        unit, member = sequence * KVH + head // groups, head % groups
                        part = turn(turned[half * HD : (half + 1) * HD])
                        q_ref[unit, :HD, member * keys : (member + 1) * keys] = part * jnp.bfloat16(
                            HD ** (-0.5)
                        )
        if at == 1:
            for part in range(PARTS):
                pass_on(0, part)

                @pl.when(steps.side == 0)
                def _():
                    across(0, part).start()

    columns = my_gate_ref.shape[1]
    gathered = HalfGather(full_out_ref, own, out_sends.at[0], out_arrivals.at[0])
    gathered_g = GroupGather(lambda shard: all_g_ref.at[shard], g_sends, g_arrivals)
    mine = lane_tile(fsdp, columns)
    own_parts = (
        (out_ref, own_out, full_out_ref.at[own_rows]),
        (gate_ref.at[:, mine], own_gate, my_gate_ref.at[own_rows]),
        (up_ref.at[:, mine], own_up, my_up_ref.at[own_rows]),
        (g_ref, own_g, all_g_ref.at[fsdp]),
    )
    loads = [
        pltpu.make_async_copy(source, held, local_sems.at[at])
        for at, (source, held, _) in enumerate(own_parts)
    ]
    background = [
        pltpu.make_async_copy(held, target, local_sems.at[at])
        for at, (_, held, target) in enumerate(own_parts)
    ]
    slices = []
    for which, (source, target) in enumerate(((gate_ref, my_gate_ref), (up_ref, my_up_ref))):
        for step in range(1, group):
            peer = lax.rem(fsdp + step, group)
            slices.append(
                pltpu.make_async_remote_copy(
                    src_ref=source.at[:, lane_tile(peer, columns)],
                    dst_ref=target.at[own_rows],
                    send_sem=part_sends.at[which, step - 1],
                    recv_sem=part_arrivals.at[which, step - 1],
                    device_id=(peer, ctx),
                    device_id_type=MESH,
                )
            )

    def start_background():
        for copy in loads:
            copy.start()
        gathered.start(out_ref)
        for copy in slices:
            copy.start()
        gathered_g.start(g_ref)

    last = len(pieces)
    for at in range(last + 2):
        if at < last:
            gathers[at][0].to_pairs()
        if at == last - 1:
            start_background()
        if 1 <= at <= last:
            gathers[at - 1][0].to_sibling()
        if at == 1:
            for column in range(width // LANES):
                columns = slice(column * LANES, (column + 1) * LANES)
                normed_t_ref[columns, :] = normed_ref[:, columns].T
            for copy in own_copies:
                copy.wait()
        if at >= 2:
            gathers[at - 2][0].arrived()
            project(at - 2)

    def second_half():
        gathered.to_pairs()
        for load, copy in zip(loads, background):
            load.wait()
            copy.start()

    def add(unit, kv):
        scores = jnp.dot(kv, q_ref[unit], preferred_element_type=jnp.float32)
        top = top_ref[unit]
        new_top = jnp.maximum(top, jnp.max(scores, axis=0, keepdims=True))
        fade = jnp.exp(top - new_top)
        weights = jnp.exp(scores - new_top)
        top_ref[unit] = new_top
        total_ref[unit] = total_ref[unit] * fade + jnp.sum(weights, axis=0, keepdims=True)
        added = jnp.dot(kv.T, weights.astype(jnp.bfloat16), preferred_element_type=jnp.float32)
        mix_ref[unit] = mix_ref[unit] * fade + added[HD:]

    def over_units(body, first, count):
        def two(at, unused):
            body(first + 2 * at)
            body(first + 2 * at + 1)
            return unused

        lax.fori_loop(0, count // 2, two, 0)

    def diagonal(unit):
        kv = all_ref[ctx, unit]
        scores = jnp.dot(kv, q_ref[unit], preferred_element_type=jnp.float32)
        scores = jnp.where(causal(keys, wide, scores.shape), scores, MASKED_SCORE)
        top = jnp.max(scores, axis=0, keepdims=True)
        weights = jnp.exp(scores - top)
        top_ref[unit] = top
        total_ref[unit] = jnp.sum(weights, axis=0, keepdims=True)
        added = jnp.dot(kv.T, weights.astype(jnp.bfloat16), preferred_element_type=jnp.float32)
        mix_ref[unit] = added[HD:]

    over_units(diagonal, 0, units)

    def forward(level, part):
        chain(level - 1, part).wait_recv()
        pass_on(level, part)
        across(level, part).start()

    @pl.when(steps.level >= 1)
    def _():
        for part in range(PARTS):
            forward(1, part)

    @pl.when(steps.side == 1)
    def _():
        for part in range(PARTS):
            across(0, part).wait_recv()
            over_units(lambda unit: add(unit, all_ref[ctx - 1, unit]), part * per_part, per_part)

    def level_step(level, unused):
        first = 2 * (steps.level - level)
        for part in range(PARTS):

            @pl.when(level < steps.level)
            def _():
                forward(level + 1, part)

            across(level, part).wait_recv()
            over_units(
                lambda unit: add(unit, all_ref[pl.ds(first, 2), unit].reshape(2 * keys, deep)),
                part * per_part,
                per_part,
            )

        @pl.when(level == 1)
        def _():
            second_half()

        return unused

    @pl.when(steps.level == 0)
    def _():
        second_half()

    lax.fori_loop(1, steps.level + 1, level_step, 0)

    def close(unit):
        total = total_ref[unit]
        mix_ref[unit] = mix_ref[unit] / total
        log_ref[unit] = top_ref[unit] + jnp.log(total)

    over_units(close, 0, units)
    for sequence in range(sequences):
        for pair in range(H // 2):
            heads = []
            for head in (2 * pair, 2 * pair + 1):
                unit, member = sequence * KVH + head // groups, head % groups
                heads.append(mix_ref[unit, :, member * keys : (member + 1) * keys])
            tile = jnp.concatenate(heads, axis=0).astype(low_ref.dtype)
            block = slice(sequence * keys, (sequence + 1) * keys)
            columns = slice(pair * 2 * HD, (pair + 1) * 2 * HD)
            low_t_ref[columns, block] = tile
            low_ref[block, columns] = tile.T
    for gather, _ in gathers:
        gather.sent()
    for step in range(1, group):
        gain_copy(step).wait_send()
    gathered.to_sibling()
    gathered_g.forward()
    gathered.arrived()
    gathered.sent()
    gathered_g.sibling_here()
    for step in range(1, gathered_g.chips):
        gathered_g.crossed(step)
    gathered_g.sent()
    for copy in slices:
        copy.wait()
    for copy in background:
        copy.wait()

    def sent(level, unused):
        for part in range(PARTS):

            @pl.when(steps.has_above)
            def _():
                chain(level, part).wait_send()

            @pl.when(jnp.logical_or(level > 0, steps.side == 0))
            def _():
                across(level, part).wait_send()

        return unused

    lax.fori_loop(0, steps.level + 1, sent, 0)


ANY = pl.BlockSpec(memory_space=pl.ANY)
VMEM = pl.BlockSpec(memory_space=pltpu.VMEM)


def attend(x, gains, cosine, sine, w_query, w_key, w_value, w_out, w_gate, w_up, g_rows, sequences):
    group, count = lax.axis_size("fsdp"), lax.axis_size("ctx")
    rows, width = x.shape
    own, hidden = w_query.shape[0], w_gate.shape[1] // group
    keys, units, deep = rows // sequences, sequences * KVH, 2 * HD
    wide = H // KVH * keys
    kv_width = KVH * HD
    dma = pltpu.SemaphoreType.DMA
    bf16, f32 = jnp.bfloat16, jnp.float32
    pieces = 2 + width // kv_width
    return pl.pallas_call(
        attend_kernel,
        out_shape=[
            jax.ShapeDtypeStruct((units, deep, wide), bf16),
            jax.ShapeDtypeStruct((width, rows), bf16),
            jax.ShapeDtypeStruct((1, width), f32),
            jax.ShapeDtypeStruct((1, width), f32),
            jax.ShapeDtypeStruct((width, width), bf16),
            jax.ShapeDtypeStruct((width, kv_width), bf16),
            jax.ShapeDtypeStruct((width, kv_width), bf16),
            jax.ShapeDtypeStruct((rows, width), bf16),
            jax.ShapeDtypeStruct((width, rows), bf16),
            jax.ShapeDtypeStruct((units, HD, wide), f32),
            jax.ShapeDtypeStruct((units, 1, wide), f32),
            jax.ShapeDtypeStruct((count, units, keys, deep), bf16),
            jax.ShapeDtypeStruct((width, width), bf16),
            jax.ShapeDtypeStruct((width, hidden), bf16),
            jax.ShapeDtypeStruct((width, hidden), bf16),
            jax.ShapeDtypeStruct((group, rows, width), bf16),
        ],
        in_specs=[VMEM] * 4 + [ANY] * 7,
        out_specs=[VMEM] * 12 + [ANY] * 4,
        scratch_shapes=[
            pltpu.VMEM((rows, width), bf16),
            pltpu.VMEM((rows, kv_width), f32),
            pltpu.VMEM((group,) + gains.shape, f32),
            pltpu.VMEM((own, width), bf16),
            pltpu.VMEM((own, hidden), bf16),
            pltpu.VMEM((own, hidden), bf16),
            pltpu.VMEM((rows, width), bf16),
            pltpu.VMEM((units, 1, wide), f32),
            pltpu.VMEM((units, 1, wide), f32),
            dma((count // 2, PARTS)),
            dma((count // 2 + 1, PARTS)),
            dma((count // 2, PARTS)),
            dma((count // 2, PARTS)),
            half_semaphores(pieces),
            half_semaphores(pieces),
            *[dma((group - 1,))] * 2,
            *[half_semaphores(1)] * 2,
            *[group_semaphores()] * 2,
            *[dma((2, group - 1))] * 2,
            dma((7,)),
        ],
        compiler_params=pltpu.CompilerParams(
            collective_id=1, has_side_effects=True, vmem_limit_bytes=60 << 20
        ),
    )(x, gains, cosine, sine, w_query, w_key, w_value, w_out, w_gate, w_up, g_rows)


class Ring:
    def __init__(self, work, landing, total, semaphores, forward, exchange=False):
        self.fsdp, self.ctx = lax.axis_index("fsdp"), lax.axis_index("ctx")
        self.group, self.count = lax.axis_size("fsdp"), lax.axis_size("ctx")
        self.work, self.landing, self.total = work, landing, total
        self.sends, self.arrivals = semaphores[:2]
        self.part_sends, self.part_arrivals, self.own_sem = semaphores[2:] if exchange else (None,) * 3
        self.exchange = exchange
        side = 0 if forward else 1
        self.place = ring_place(self.ctx, side, self.count)
        self.after = (self.fsdp, ring_ctx(lax.rem(self.place + 1, self.count), side, self.count))
        self.ticks = 2 * self.count - 2 + int(exchange)

    def chunk(self, held, index):
        if self.exchange:
            return held.at[index]
        per = held.shape[0] // self.count
        return held.at[pl.ds(index * per, per)]

    def summing(self, step, index):
        return self.copy(self.chunk(self.work, index), self.landing.at[step], step)

    def handing(self, step, index):
        held = self.chunk(self.total, index)
        return self.copy(held, held, step)

    def copy(self, source, target, step):
        return pltpu.make_async_remote_copy(
            src_ref=source,
            dst_ref=target,
            send_sem=self.sends.at[step],
            recv_sem=self.arrivals.at[step],
            device_id=self.after,
            device_id_type=MESH,
        )

    def part(self, index, step):
        peer = lax.rem(self.fsdp + step, self.group)
        return pltpu.make_async_remote_copy(
            src_ref=self.work.at[index, peer],
            dst_ref=self.total.at[index, self.fsdp],
            send_sem=self.part_sends.at[step - 1],
            recv_sem=self.part_arrivals.at[step - 1],
            device_id=(peer, self.ctx),
            device_id_type=MESH,
        )

    def own_part(self, index):
        return pltpu.make_async_copy(
            self.work.at[index, self.fsdp], self.total.at[index, self.fsdp], self.own_sem
        )

    def start(self):
        self.summing(0, self.place).start()

    def tick(self, at):
        last = self.count - 2
        gap = int(self.exchange)
        step = at - gap * jnp.where(at > last, 1, 0) if self.exchange else at
        index = lax.rem(self.place + 3 * self.count - 1 - step, self.count)

        def add(target):
            part, landed = self.chunk(self.work, index), self.landing.at[jnp.minimum(at, last)]
            for row in range(part.shape[0]):
                target[row] = (
                    part[row].astype(jnp.float32) + landed[row].astype(jnp.float32)
                ).astype(part.dtype)

        @pl.when(at <= last)
        def _():
            self.summing(jnp.minimum(at, last), index).wait_recv()

        @pl.when(at < last)
        def _():
            add(self.chunk(self.work, index))
            self.summing(jnp.minimum(at + 1, last), index).start()

        if self.exchange:

            @pl.when(at == last)
            def _():
                add(self.chunk(self.work, index))
                for peer in range(1, self.group):
                    self.part(index, peer).start()
                self.own_part(index).start()

            @pl.when(at == last + 1)
            def _():
                done = lax.rem(self.place + 1, self.count)
                self.own_part(done).wait()
                for peer in range(1, self.group):
                    self.part(done, peer).wait_recv()
                self.handing(last + 1, done).start()

        else:

            @pl.when(at == last)
            def _():
                add(self.chunk(self.total, index))
                self.handing(last + 1, index).start()

        @pl.when(at > last + gap)
        def _():
            here = jnp.maximum(step, last + 1)
            self.handing(here, index).wait_recv()

            @pl.when(here < 2 * self.count - 3)
            def _():
                self.handing(jnp.minimum(here + 1, 2 * self.count - 3), index).start()

    def finish(self):
        def wait(step, unused):
            self.handing(step, self.place).wait_send()
            return unused

        lax.fori_loop(0, 2 * self.count - 2, wait, 0)
        if self.exchange:
            for peer in range(1, self.group):
                self.part(lax.rem(self.place + 1, self.count), peer).wait_send()


class SumRing(Ring):
    def __init__(self, *args):
        super().__init__(*args)
        self.ticks = self.count - 1

    def tick(self, at):
        last = self.count - 2
        index = lax.rem(self.place + 2 * self.count - 1 - at, self.count)
        self.summing(at, index).wait_recv()
        work, landed = self.chunk(self.work, index), self.landing.at[at]

        def add(target):
            for row in range(work.shape[0]):
                target[row] = (
                    work[row].astype(jnp.float32) + landed[row].astype(jnp.float32)
                ).astype(work.dtype)

        @pl.when(at < last)
        def _():
            add(work)
            self.summing(jnp.minimum(at + 1, last), index).start()

        @pl.when(at == last)
        def _():
            add(self.total)

    def finish(self):
        def wait(step, unused):
            self.summing(step, self.place).wait_send()
            return unused

        lax.fori_loop(0, self.ticks, wait, 0)


class SpreadRing(Ring):
    def __init__(self, total, semaphores, forward):
        super().__init__(None, None, total, semaphores, forward)
        self.ticks = self.count - 1
        self.first = lax.rem(self.place + 1, self.count)

    def start(self):
        self.handing(0, self.first).start()

    def tick(self, at):
        index = lax.rem(self.place + self.count - at, self.count)
        self.handing(at, index).wait_recv()

        @pl.when(at < self.count - 2)
        def _():
            self.handing(jnp.minimum(at + 1, self.count - 2), index).start()

    def finish(self):
        def wait(step, unused):
            self.handing(step, self.place).wait_send()
            return unused

        lax.fori_loop(0, self.ticks, wait, 0)


def ring_scratch(chunk, exchange=False):
    count = lax.axis_size("ctx")
    work = (count,) + chunk if exchange else (count * chunk[0],) + chunk[1:]
    return [pltpu.VMEM(work, jnp.bfloat16), pltpu.VMEM((count - 1,) + chunk, jnp.bfloat16)]


def ring_total(chunk, exchange=False):
    count = lax.axis_size("ctx")
    work = (count,) + chunk if exchange else (count * chunk[0],) + chunk[1:]
    return jax.ShapeDtypeStruct(work, jnp.bfloat16)


def ring_semaphores(exchange=False):
    dma, steps = pltpu.SemaphoreType.DMA, 2 * lax.axis_size("ctx") - 2
    parts = lax.axis_size("fsdp") - 1
    return [dma((steps,))] * 2 + ([dma((parts,))] * 2 + [dma] if exchange else [])


def wide_split(width):
    group, count = lax.axis_size("fsdp"), lax.axis_size("ctx")
    return 2 if FF // group // LANES * (width // group // 16) >= 4 * count else 1


def query_split(width):
    return width // LANES * 7 // 9 * LANES


def out_split(width):
    return (width // LANES + 1) // 2 * LANES


def down_split(blocks, count):
    each = -(-blocks // count)
    rings = 4 if each >= 4 else 2
    return [max(1, (each + at) // rings) for at in range(rings)]


class GroupScatter:
    def __init__(self, give_sib, got_sib, give_cross, got_cross, far, got_far, sends, arrivals):
        self.give_sib, self.got_sib = give_sib, got_sib
        self.give_cross, self.got_cross = give_cross, got_cross
        self.far, self.got_far = far, got_far
        self.sends, self.arrivals = sends, arrivals
        self.fsdp, self.ctx = lax.axis_index("fsdp"), lax.axis_index("ctx")
        self.chips = lax.axis_size("fsdp") // 2
        self.chip, self.core = lax.div(self.fsdp, 2), lax.rem(self.fsdp, 2)
        self.sibling = 2 * self.chip + 1 - self.core

    def copy(self, source, target, semaphore, device):
        return pltpu.make_async_remote_copy(
            src_ref=source,
            dst_ref=target,
            send_sem=self.sends.at[semaphore],
            recv_sem=self.arrivals.at[semaphore],
            device_id=(device, self.ctx),
            device_id_type=MESH,
        )

    def to_sibling(self):
        return self.copy(self.give_sib, self.got_sib, 0, self.sibling)

    def to_cross(self, step):
        return self.copy(
            self.give_cross(step), self.got_cross.at[step - 1], step, self.sibling
        )

    def to_far(self, step):
        chip = lax.rem(self.chip + self.chips - step, self.chips)
        return self.copy(
            self.far.at[step - 1],
            self.got_far.at[step - 1],
            self.chips - 1 + step,
            2 * chip + self.core,
        )

    def add_cross(self, step):
        self.to_cross(step).wait_recv()
        held = self.far.at[step - 1]
        held[...] = (
            held[...].astype(jnp.float32) + self.got_cross[step - 1].astype(jnp.float32)
        ).astype(held.dtype)
        self.to_far(step).start()

    def total(self, own):
        self.to_sibling().wait_recv()
        value = own + self.got_sib[...].astype(jnp.float32)
        for step in range(1, self.chips):
            self.to_far(step).wait_recv()
            value = value + self.got_far[step - 1].astype(jnp.float32)
        return value

    def sent(self):
        self.to_sibling().wait_send()
        for step in range(1, self.chips):
            self.to_cross(step).wait_send()
            self.to_far(step).wait_send()


def scatter_scratch(rows, width):
    far = lax.axis_size("fsdp") // 2 - 1
    one, many = (rows, width), (far, rows, width)
    return [pltpu.VMEM(shape, jnp.bfloat16) for shape in (one, one, many, many, many, many)]


def dot_columns(left, right):
    return lax.dot_general(
        left, right, (((1,), (1,)), ((), ())), preferred_element_type=jnp.float32
    )


def tiles(count, body):
    def step(at, unused):
        body(at)
        return unused

    lax.fori_loop(0, count, step, 0)


def lane_tile(at, size):
    return pl.ds(pl.multiple_of(at * size, LANES), size)


def width_tile(width):
    return 384 if width % 384 == 0 else width


def hidden_tile(hidden):
    return 256 if hidden % 256 == 0 else 128


def transpose_into(target, source):
    rows, columns = source.shape

    def body(at):
        part = source[:, lane_tile(at, LANES)]
        target[pl.ds(pl.multiple_of(at * LANES, LANES), LANES), :] = part.T

    tiles(columns // LANES, body)


def ffn_kernel(
    x_ref, low_ref, out_ref, gain_ref, gate_in, up_in, down_in, all_g_in,
    layer_ref, resid_grad_ref, branch_ref, g_wide_ref, gate_part_out, up_part_out, layer_part_out,
    *rest,
):
    downs = len(down_split(gate_in.shape[1] // 16, lax.axis_size("ctx")))
    taken = iter(rest)

    def take(number):
        return [next(taken) for _ in range(number)]

    down_done, (gain_grad_ref,) = take(downs), take(1)
    all_n_ref, turned_n, turned_act, act_ref, gate_grad, up_grad, resid_ref, grad_own = take(8)
    down_scratch = take(2 * downs)
    give_sib, got_sib, give_cross, got_cross, far, got_far = take(6)
    n_sends, n_arrivals, grad_sends, grad_arrivals = take(4)
    gate_ref, up_ref, down_ref, all_g_ref, gate_part_ref, up_part_ref, layer_part_ref = take(7)
    (local_sems,) = take(1)
    loads = [
        pltpu.make_async_copy(source, target, local_sems.at[at])
        for at, (source, target) in enumerate(
            ((gate_in, gate_ref), (up_in, up_ref), (all_g_in, all_g_ref), (down_in, down_ref))
        )
    ]
    for copy in loads:
        copy.start()
    stores = []

    def store(source, target):
        copy = pltpu.make_async_copy(source, target, local_sems.at[len(loads) + len(stores)])
        copy.start()
        stores.append(copy)

    rings = [
        SumRing(*down_scratch[2 * at : 2 * at + 2], down_done[at], take(2), at % 2 == 0)
        for at in range(downs)
    ]
    group = lax.axis_size("fsdp")
    rows, width = x_ref.shape
    hidden = gate_ref.shape[1]
    barrier = pltpu.get_barrier_semaphore()
    greeted = greet_group(barrier) + 2
    for ring in rings[:2]:
        pl.semaphore_signal(barrier, inc=1, device_id=ring.after, device_id_type=MESH)
    step_in, step_out = hidden_tile(hidden), width_tile(width)

    def branch(at):
        columns = lane_tile(at, step_out)
        resid_ref[:, columns] = x_ref[:, columns].astype(jnp.float32) + forward_dot(
            low_ref[...], out_ref[:, columns]
        )

    tiles(width // step_out, branch)
    gain = gain_ref[...]
    scale = norm_scale(resid_ref[...])
    gathered = GroupGather(lambda shard: all_n_ref.at[shard], n_sends, n_arrivals)
    fsdp, chips = gathered.fsdp, gathered.chips
    all_n_ref[fsdp] = (resid_ref[...] * scale * gain).astype(jnp.bfloat16)
    pl.semaphore_wait(barrier, greeted)
    gathered.start(all_n_ref.at[fsdp])
    grad_sum = GroupScatter(
        give_sib,
        got_sib,
        lambda step: give_cross.at[step - 1],
        got_cross,
        far,
        got_far,
        grad_sends,
        grad_arrivals,
    )

    def hidden_part(shard):
        def body(at):
            columns = lane_tile(at, step_in)
            normed = all_n_ref[shard]
            gate = forward_dot(normed, gate_ref[:, columns])
            upward = forward_dot(normed, up_ref[:, columns])
            grad_act = dot_columns(
                all_g_ref[shard], down_ref[pl.ds(pl.multiple_of(at * step_in, LANES), step_in), :]
            )
            sigmoid = jax.nn.sigmoid(gate)
            silu = gate * sigmoid
            act_ref[shard, :, columns] = (silu * upward).astype(jnp.bfloat16)
            gate_grad[shard, :, columns] = (
                grad_act * upward * (sigmoid * (1.0 + gate * (1.0 - sigmoid)))
            ).astype(jnp.bfloat16)
            up_grad[shard, :, columns] = (grad_act * silu).astype(jnp.bfloat16)

        tiles(hidden // step_in, body)

    def grad_part(shard, target):
        def body(at):
            columns = pl.ds(pl.multiple_of(at * step_out, LANES), step_out)
            target[:, columns] = (
                dot_columns(gate_grad[shard], gate_ref[columns, :])
                + dot_columns(up_grad[shard], up_ref[columns, :])
            ).astype(target.dtype)

        tiles(width // step_out, body)

    for copy in loads:
        copy.wait()
    hidden_part(fsdp)
    gathered.sibling_here()
    sibling = gathered.sibling
    hidden_part(sibling)
    grad_part(sibling, grad_sum.give_sib)
    grad_sum.to_sibling().start()
    gathered.forward()
    grad_part(fsdp, grad_own)
    def turn_act(shard):
        transpose_into(turned_act.at[:, lane_tile(shard, rows)], act_ref.at[shard])

    turn_act(fsdp)
    turn_act(sibling)
    far_shards = []
    for step in range(1, chips):
        ours = gathered.same_core(chips - step)
        theirs = ours + sibling - fsdp
        far_shards.append((step, ours, theirs))
        gathered.crossed(step)
        hidden_part(theirs)
        hidden_part(ours)
        turn_act(theirs)
        turn_act(ours)
    blocks = hidden // 16
    spans, first = [], 0
    for ring in rings:
        last = min(blocks, first + ring.work.shape[0])
        spans.append((first, last, ring.work))
        first = last

    def down_tile(at):
        columns = lane_tile(at, step_out)
        part = forward_dot(
            turned_act[...], all_g_ref[:, :, columns].reshape(group * rows, step_out)
        ).astype(jnp.bfloat16)
        for begin, end, work in spans:
            if end > begin:
                work[: end - begin, :, columns] = part[begin * 16 : end * 16].reshape(
                    end - begin, 16, step_out
                )

    tiles(width // step_out, down_tile)
    for begin, end, work in spans:
        for spare in range(end - begin, work.shape[0]):
            work[spare] = jnp.zeros(work.shape[1:], work.dtype)
    for ring in rings:
        ring.start()
    for step, ours, theirs in far_shards:
        grad_part(theirs, give_cross.at[step - 1])
        grad_sum.to_cross(step).start()
        grad_part(ours, far.at[step - 1])
        grad_sum.add_cross(step)
    ticked = [0]

    def ring_tick(at):
        for ring in rings:

            @pl.when(at < ring.ticks)
            def _():
                ring.tick(jnp.minimum(at, ring.ticks - 1))

    def ticking(times, body):
        begin = ticked[0]

        def step(at):
            body(at)
            ring_tick(begin + at)

        tiles(times, step)
        ticked[0] += times

    for shard in range(group):
        span = slice(shard * rows, (shard + 1) * rows)
        transpose_into(turned_n.at[:, span], all_n_ref.at[shard])
    own = width // group
    row_blocks = own // 16
    for source, target in ((gate_grad, gate_part_ref), (up_grad, up_part_ref)):

        def weight_tile(at):
            columns = lane_tile(at, step_in)
            part = forward_dot(
                turned_n[...], source[:, :, columns].reshape(group * rows, step_in)
            ).astype(jnp.bfloat16)
            for block in range(step_in // LANES):
                first = (at * (step_in // LANES) + block) * row_blocks
                for owner in range(group):
                    target[owner, pl.ds(first, row_blocks)] = part[
                        owner * own : (owner + 1) * own, block * LANES : (block + 1) * LANES
                    ].reshape(row_blocks, 16, LANES)

        ticking(hidden // step_in, weight_tile)
        filled = hidden // LANES * row_blocks
        for spare in range(filled, target.shape[1]):
            for owner in range(group):
                target[owner, spare] = jnp.zeros(target.shape[2:], target.dtype)
        store(target, gate_part_out if source is gate_grad else up_part_out)

    def layer_tile(at):
        columns = lane_tile(at, step_out)
        part = forward_dot(
            act_ref[...].reshape(group * rows, hidden), down_ref[:, columns]
        ).reshape(group, rows, step_out)
        layer_part_ref[:, :, columns] = part.astype(jnp.bfloat16)

    ticking(width // step_out, layer_tile)
    store(layer_part_ref, layer_part_out)
    layer_ref[...] = resid_ref[...] + layer_part_ref[fsdp].astype(jnp.float32)
    upstream = grad_sum.total(grad_own[...])
    resid = resid_ref[...]
    scaled = upstream * gain
    grad_resid = (
        all_g_ref[fsdp].astype(jnp.float32)
        + scale * scaled
        - resid * scale**3 * jnp.mean(scaled * resid, axis=-1, keepdims=True)
    )
    gain_grad_ref[...] = jnp.sum(upstream * resid * scale, axis=0, keepdims=True)
    resid_grad_ref[...] = grad_resid
    branch_ref[...] = grad_resid.astype(jnp.bfloat16)
    units, _, wide = g_wide_ref.shape
    sequences = units // KVH
    keys = rows // sequences
    groups = wide // keys
    g_wide_ref[:, :HD, :] = jnp.zeros((units, HD, wide), g_wide_ref.dtype)
    for pair in range(H // 2):
        columns = slice(pair * 2 * HD, (pair + 1) * 2 * HD)
        mixed = dot_columns(branch_ref[...], out_ref[columns, :]).astype(jnp.bfloat16)
        for sequence in range(sequences):
            turned = mixed[sequence * keys : (sequence + 1) * keys].T
            for half in range(2):
                head = 2 * pair + half
                unit, member = sequence * KVH + head // groups, head % groups
                g_wide_ref[unit, HD:, member * keys : (member + 1) * keys] = turned[
                    half * HD : (half + 1) * HD
                ]
    begin = ticked[0]
    tiles(max(0, rings[0].ticks - begin), lambda at: ring_tick(begin + at))
    gathered.sent()
    grad_sum.sent()
    for ring in rings:
        ring.finish()
    for copy in stores:
        copy.wait()


def spread(blocks, count):
    return -(-blocks // count) * count


def feed_forward(x, low, full_out, my_gate, my_up, my_down, all_g, gain, units, wide):
    group, count = lax.axis_size("fsdp"), lax.axis_size("ctx")
    rows, width = x.shape
    hidden = my_gate.shape[1]
    blocks = spread(hidden // LANES * (width // group // 16), wide_split(width) * count)
    chips = group // 2
    dma = pltpu.SemaphoreType.DMA((2 * chips - 1,))
    bf16 = jnp.bfloat16
    down_chunks = [(per, 16, width) for per in down_split(hidden // 16, count)]
    return pl.pallas_call(
        ffn_kernel,
        out_shape=[
            jax.ShapeDtypeStruct((rows, width), jnp.float32),
            jax.ShapeDtypeStruct((rows, width), jnp.float32),
            jax.ShapeDtypeStruct((rows, width), bf16),
            jax.ShapeDtypeStruct((units, 2 * HD, wide), bf16),
            jax.ShapeDtypeStruct((group, blocks, 16, LANES), bf16),
            jax.ShapeDtypeStruct((group, blocks, 16, LANES), bf16),
            jax.ShapeDtypeStruct((group, rows, width), bf16),
            *[jax.ShapeDtypeStruct(chunk, bf16) for chunk in down_chunks],
            jax.ShapeDtypeStruct((1, width), jnp.float32),
        ],
        in_specs=[VMEM] * 4 + [ANY] * 4,
        out_specs=[VMEM] * 4 + [ANY] * 3 + [VMEM] * (1 + len(down_chunks)),
        scratch_shapes=[
            pltpu.VMEM((group, rows, width), bf16),
            pltpu.VMEM((width, group * rows), bf16),
            pltpu.VMEM((hidden, group * rows), bf16),
            pltpu.VMEM((group, rows, hidden), bf16),
            pltpu.VMEM((group, rows, hidden), bf16),
            pltpu.VMEM((group, rows, hidden), bf16),
            pltpu.VMEM((rows, width), jnp.float32),
            pltpu.VMEM((rows, width), jnp.float32),
            *[kind for chunk in down_chunks for kind in ring_scratch(chunk)],
            *scatter_scratch(rows, width),
            *[dma] * 4,
            pltpu.VMEM(my_gate.shape, bf16),
            pltpu.VMEM(my_up.shape, bf16),
            pltpu.VMEM(my_down.shape, bf16),
            pltpu.VMEM(all_g.shape, bf16),
            pltpu.VMEM((group, blocks, 16, LANES), bf16),
            pltpu.VMEM((group, blocks, 16, LANES), bf16),
            pltpu.VMEM((group, rows, width), bf16),
            pltpu.SemaphoreType.DMA((7,)),
            *[kind for _ in down_chunks for kind in ring_semaphores()],
        ],
        compiler_params=pltpu.CompilerParams(
            collective_id=2, has_side_effects=True, vmem_limit_bytes=60 << 20
        ),
    )(x, low, full_out, gain, my_gate, my_up, my_down, all_g)


def back_kernel(
    down_blocks, q_ref, g_ref, log_ref, gain_grad_ref, gain_ref, cos_ref, sin_ref,
    pairs_ref, mix_in, gate_ref, up_ref, layer_base_in, layer_part_ref, branch_ref, low_t_ref,
    normed_t_ref, w_query_in, w_key_in, w_value_in, x_in, resid_grad_in, *rest,
):
    taken = iter(rest)

    def take(number):
        return [next(taken) for _ in range(number)]

    halves, downs = wide_split(x_in.shape[1]), len(down_blocks)
    down_refs = take(downs)
    tokens_ref, layer_ref = take(2)
    wide_totals, down_totals = take(2 * halves), take(downs)
    out_a_total, out_b_total, rest_a_total, rest_b_total = take(4)
    peer_got, chain_got, layer_sib, layer_cross, layer_far = take(5)
    kv_ref, stage_ref, final_ref, qg_ref, delta_ref, grad_q_ref = take(6)
    wide_scratch = take(4 * halves)
    out_a_work, out_a_land, out_b_work, out_b_land = take(4)
    rest_a_work, rest_a_land, rest_b_work, rest_b_land = take(4)
    low_all, normed_all, branch_all, query_all, pair_all, upstream_ref, gain_give, gain_got = take(8)
    far_ref, layer_stage = take(2)
    mix_ref, layer_base_ref, w_query_ref, w_key_ref, w_value_ref, x_ref, resid_grad_ref = take(7)
    steps = Steps()
    fsdp, ctx, group, count = steps.fsdp, steps.ctx, lax.axis_size("fsdp"), lax.axis_size("ctx")
    units, deep, wide = q_ref.shape
    keys = pairs_ref.shape[2]
    rows, width = x_ref.shape
    own = width // group
    wide_rings = [
        Ring(*wide_scratch[2 * at : 2 * at + 2], wide_totals[at], take(5), at < halves, True)
        for at in range(2 * halves)
    ]
    down_rings = [SpreadRing(total, take(2), at % 2 == 0) for at, total in enumerate(down_totals)]
    out_a = Ring(out_a_work, out_a_land, out_a_total, take(2), True)
    out_b = Ring(out_b_work, out_b_land, out_b_total, take(2), False)
    layer_sum = GroupScatter(
        None,
        layer_sib,
        lambda step: layer_part_ref.at[
            2 * lax.rem(lax.div(fsdp, 2) + group // 2 - step, group // 2) + 1 - lax.rem(fsdp, 2)
        ],
        layer_cross,
        far_ref,
        layer_far,
        *take(2),
    )
    layer_sum.give_sib = layer_part_ref.at[layer_sum.sibling]
    rest_a = Ring(rest_a_work, rest_a_land, rest_a_total, take(2), True)
    rest_b = Ring(rest_b_work, rest_b_land, rest_b_total, take(2), False)
    first_rings = []
    for at in range(halves):
        first_rings += [wide_rings[at], wide_rings[halves + at]]
        first_rings += down_rings[at * downs // halves : (at + 1) * downs // halves]
    begun_rings = len(first_rings)
    first_rings += [out_a, out_b]
    peer_sends, peer_arrivals, chain_sends, chain_arrivals = take(4)
    branch_gather = GroupGather(lambda shard: branch_all.at[shard], *take(2))
    query_gather = GroupGather(lambda shard: query_all.at[shard], *take(2))
    pair_gather = GroupGather(lambda shard: pair_all.at[shard], *take(2))
    low_sends, low_arrivals, normed_sends, normed_arrivals, gain_sends, gain_arrivals = take(6)
    local_sems, stage_sems = take(2)

    barrier = pltpu.get_barrier_semaphore()
    greeted = steps.greet(barrier) + greet_group(barrier) + 2
    for device in (out_a.after, out_b.after):
        pl.semaphore_signal(barrier, inc=1, device_id=device, device_id_type=MESH)

    loads = []

    def load(source, target):
        copy = pltpu.make_async_copy(source, target, local_sems.at[len(loads)])
        copy.start()
        loads.append(copy)

    n = wide_scratch[0].shape[2]
    for at, ring in enumerate(wide_rings):
        source = (gate_ref, up_ref)[at // halves]
        for chunk in range(count):
            load(source.at[:, pl.ds((at % halves * count + chunk) * n, n)], ring.work.at[chunk])
    for ring, source in zip(down_rings, down_refs):
        load(source, ring.chunk(ring.total, ring.first))
    ring_loads = len(loads)
    load(pairs_ref, kv_ref)
    load(mix_in, mix_ref)
    load(branch_ref, branch_all.at[fsdp])
    load(low_t_ref.at[pl.ds(fsdp * own, own)], low_all.at[:, lane_tile(fsdp, rows)])
    load(normed_t_ref.at[pl.ds(fsdp * own, own)], normed_all.at[:, lane_tile(fsdp, rows)])
    slot_loads = len(loads)
    for source, target in (
        (layer_base_in, layer_base_ref),
        (w_query_in, w_query_ref),
        (w_key_in, w_key_ref),
        (w_value_in, w_value_ref),
        (x_in, x_ref),
        (resid_grad_in, resid_grad_ref),
    ):
        load(source, target)
    for copy in loads[:ring_loads]:
        copy.wait()
    pl.semaphore_wait(barrier, greeted)
    for ring in first_rings[:begun_rings]:
        ring.start()
    branch_gather.start(branch_ref)
    layer_sum.to_sibling().start()
    for step in range(1, group // 2):
        layer_sum.to_cross(step).start()

    def slices(source, target, sends, arrivals, step):
        peer = lax.rem(fsdp + step, group)
        return pltpu.make_async_remote_copy(
            src_ref=source.at[pl.ds(peer * own, own)],
            dst_ref=target.at[:, lane_tile(fsdp, rows)],
            send_sem=sends.at[step - 1],
            recv_sem=arrivals.at[step - 1],
            device_id=(peer, ctx),
            device_id_type=MESH,
        )

    turned = [
        slices(*ends, step)
        for ends in (
            (low_t_ref, low_all, low_sends, low_arrivals),
            (normed_t_ref, normed_all, normed_sends, normed_arrivals),
        )
        for step in range(1, group)
    ]
    for copy in turned:
        copy.start()

    def prepare(unit):
        q, g = q_ref[unit], g_ref[unit]
        qg_ref[unit, :wide] = q.T
        qg_ref[unit, wide:] = g.T
        delta_ref[unit] = jnp.sum(
            g[HD:].astype(jnp.float32) * mix_ref[unit], axis=0, keepdims=True
        )
        grad_q_ref[unit] = jnp.zeros((HD, wide), jnp.float32)

    for copy in loads[ring_loads:slot_loads]:
        copy.wait()
    tiles(units, prepare)

    def tick(ring, at):
        @pl.when(jnp.logical_and(at >= 0, at < ring.ticks))
        def _():
            ring.tick(jnp.clip(at, 0, ring.ticks - 1))

    late = steps.levels // 2 + 1

    def pump(at):
        lag = [0] * begun_rings + [late, late]
        for turn, ring in enumerate(first_rings):

            @pl.when(lax.rem(at, len(first_rings)) == turn)
            def _():
                tick(ring, lax.div(at, len(first_rings)) - lag[turn])

    def back(unit, first, blocks, diagonal):
        kv = kv_ref[pl.ds(first, blocks), unit].reshape(blocks * keys, deep)
        scores = jnp.dot(kv, q_ref[unit], preferred_element_type=jnp.float32)
        probs = jnp.exp(scores - log_ref[unit])
        if diagonal:
            probs = jnp.where(causal(keys, wide, scores.shape), probs, 0.0)
        grad_probs = jnp.dot(kv, g_ref[unit], preferred_element_type=jnp.float32)
        grad_scores = (probs * (grad_probs - delta_ref[unit])).astype(jnp.bfloat16)
        both = jnp.concatenate([grad_scores, probs.astype(jnp.bfloat16)], axis=1)
        grad_kv = jnp.dot(both, qg_ref[unit], preferred_element_type=jnp.float32)
        added = jnp.dot(kv.T, grad_scores, preferred_element_type=jnp.float32)
        grad_q_ref[unit] = grad_q_ref[unit] + added[:HD]
        kv_ref[pl.ds(first, blocks), unit] = grad_kv.astype(kv_ref.dtype).reshape(
            blocks, keys, deep
        )

    def across(pair):
        return pltpu.make_async_remote_copy(
            src_ref=kv_ref.at[2 * pair + 1 - steps.side],
            dst_ref=peer_got.at[pair],
            send_sem=peer_sends.at[pair],
            recv_sem=peer_arrivals.at[pair],
            device_id=steps.peer,
            device_id_type=MESH,
        )

    def down_chain(pair):
        return pltpu.make_async_remote_copy(
            src_ref=kv_ref.at[2 * pair + steps.side],
            dst_ref=chain_got.at[pair],
            send_sem=chain_sends.at[pair],
            recv_sem=chain_arrivals.at[pair],
            device_id=steps.below,
            device_id_type=MESH,
        )

    def combine(time):
        pair = time - steps.levels + steps.level

        @pl.when(jnp.logical_and(pair >= 0, pair <= steps.level))
        def _():
            for slot, expected, arrival, source in (
                (0, jnp.logical_or(pair < steps.level, steps.side == 0), across, peer_got),
                (1, steps.has_above, down_chain, chain_got),
            ):

                @pl.when(expected)
                def _():
                    arrival(pair).wait_recv()
                    copy = pltpu.make_async_copy(
                        source.at[pair], stage_ref.at[slot], stage_sems.at[slot]
                    )
                    copy.start()
                    copy.wait()

                @pl.when(jnp.logical_not(expected))
                def _():
                    stage_ref[slot] = jnp.zeros(stage_ref.shape[1:], stage_ref.dtype)

            def add(unit):
                final_ref[unit] = (
                    kv_ref[2 * pair + steps.side, unit].astype(jnp.float32)
                    + stage_ref[0, unit].astype(jnp.float32)
                    + stage_ref[1, unit].astype(jnp.float32)
                )

            tiles(units, add)

            @pl.when(pair < steps.level)
            def _():
                kv_ref[2 * pair + steps.side] = final_ref[...].astype(kv_ref.dtype)
                down_chain(pair).start()

    row_blocks = own // 16

    def weight_grad(left, right, begin, end, target, first, loop):
        span = LANES * next(n for n in (3, 2, 1) if (end - begin) % (n * LANES) == 0)

        def body(at):
            columns = pl.ds(pl.multiple_of(begin + at * span, LANES), span)
            part = forward_dot(
                left[...], right[:, :, columns].reshape(group * rows, span)
            ).astype(jnp.bfloat16)
            for block in range(span // LANES):
                here = first + (at * (span // LANES) + block) * row_blocks
                target[pl.ds(here, row_blocks)] = part[
                    :, block * LANES : (block + 1) * LANES
                ].reshape(row_blocks, 16, LANES)

        loop((end - begin) // span, body)
        return first + (end - begin) // LANES * row_blocks

    def clear_from(target, first):
        for spare in range(first, target.shape[0]):
            target[spare] = jnp.zeros((16, LANES), jnp.bfloat16)

    def out_grad():
        for copy in turned[: group - 1]:
            copy.wait_recv()
        branch_gather.forward()
        branch_gather.sibling_here()
        for step in range(1, branch_gather.chips):
            branch_gather.crossed(step)
        split = out_split(width)
        clear_from(out_a_work, weight_grad(low_all, branch_all, 0, split, out_a_work, 0, tiles))
        clear_from(out_b_work, weight_grad(low_all, branch_all, split, width, out_b_work, 0, tiles))
        out_a.start()
        out_b.start()

    turns = units // 2
    rings = max(turns, len(first_rings))

    def slot(pair):
        def turn(at):
            @pl.when(jnp.logical_and(pair < steps.level, at < turns))
            def _():
                for unit in (2 * at, 2 * at + 1):
                    back(unit, 2 * pair, 2, False)

            @pl.when(jnp.logical_and(pair == steps.level, at < turns))
            def _():
                for unit in (2 * at, 2 * at + 1):
                    back(unit, ctx, 1, True)

            @pl.when((pair == steps.level) & (steps.side == 1) & (at < turns))
            def _():
                for unit in (2 * at, 2 * at + 1):
                    back(unit, ctx - 1, 1, False)

            pump(pair * rings + at)

        tiles(rings, turn)

        @pl.when(jnp.logical_or(pair < steps.level, (pair == steps.level) & (steps.side == 1)))
        def _():
            across(pair).start()

        combine(pair)

        @pl.when(pair == late - 1)
        def _():
            out_grad()

    tiles(steps.levels, slot)
    pumped = [steps.levels * rings]

    def pump_next(times=1):
        def body(at, unused, begin=pumped[0]):
            pump(begin + at)
            return unused

        lax.fori_loop(0, times, body, 0)
        pumped[0] += times

    def pumping(times, body):
        begin = pumped[0]

        def step(at):
            body(at)
            tiles(2, lambda more: pump(begin + 2 * at + more))

        tiles(times, step)
        pumped[0] += 2 * times

    cosine, sine = cos_ref[...], sin_ref[...]

    def unturn(columns):
        first, second = columns[: HD // 2], columns[HD // 2 :]
        return jnp.concatenate(
            [first * cosine + second * sine, second * cosine - first * sine], axis=0
        )

    sequences = units // KVH
    groups = wide // keys
    for sequence in range(sequences):
        span = slice(sequence * keys, (sequence + 1) * keys)
        for pair in range(H // 2):
            heads = []
            for head in (2 * pair, 2 * pair + 1):
                unit, member = sequence * KVH + head // groups, head % groups
                part = grad_q_ref[unit, :, member * keys : (member + 1) * keys]
                heads.append(unturn(part * HD ** (-0.5)))
            query_all[fsdp, span, pair * 2 * HD : (pair + 1) * 2 * HD] = (
                jnp.concatenate(heads, axis=0).astype(jnp.bfloat16).T
            )
        pump_next(3)
    query_gather.start(query_all.at[fsdp])
    combine(steps.levels)
    kv_width = KVH * HD
    for sequence in range(sequences):
        span = slice(sequence * keys, (sequence + 1) * keys)
        for pair in range(KVH // 2):
            turned_keys, turned_values = [], []
            for unit in (sequence * KVH + 2 * pair, sequence * KVH + 2 * pair + 1):
                part = final_ref[unit].T
                turned_keys.append(unturn(part[:HD]))
                turned_values.append(part[HD:])
            for start, parts in ((0, turned_keys), (kv_width, turned_values)):
                pair_all[fsdp, span, start + pair * 2 * HD : start + (pair + 1) * 2 * HD] = (
                    jnp.concatenate(parts, axis=0).astype(jnp.bfloat16).T
                )
    pair_gather.start(pair_all.at[fsdp])
    pump_next(2)
    query_gather.forward()
    step_out = width_tile(width)

    def upstream_tile(at):
        columns = pl.ds(pl.multiple_of(at * step_out, LANES), step_out)
        upstream_ref[:, columns] = (
            dot_columns(query_all[fsdp], w_query_ref[columns, :])
            + dot_columns(pair_all[fsdp, :, :kv_width], w_key_ref[columns, :])
            + dot_columns(pair_all[fsdp, :, kv_width:], w_value_ref[columns, :])
        )

    for copy in loads[slot_loads:]:
        copy.wait()
    pumping(width // step_out, upstream_tile)
    inputs = x_ref[...].astype(jnp.float32)
    scale = norm_scale(inputs)
    upstream = upstream_ref[...]
    scaled = upstream * gain_ref[...]
    tokens_ref[...] = (
        resid_grad_ref[...]
        + scale * scaled
        - inputs * scale**3 * jnp.mean(scaled * inputs, axis=-1, keepdims=True)
    )
    gain_attn = jnp.sum(upstream * inputs * scale, axis=0, keepdims=True)
    lanes = width // LANES
    gain_give[...] = jnp.zeros(gain_give.shape, jnp.float32)
    for block in range(lanes):
        columns = slice(block * LANES, (block + 1) * LANES)
        gain_give[block : block + 1, :] = gain_attn[:, columns]
        gain_give[lanes + block : lanes + block + 1, :] = gain_grad_ref[:, columns]

    def gain_copy(step):
        peer = lax.rem(fsdp + step, group)
        return pltpu.make_async_remote_copy(
            src_ref=gain_give,
            dst_ref=gain_got.at[step - 1],
            send_sem=gain_sends.at[step - 1],
            recv_sem=gain_arrivals.at[step - 1],
            device_id=(peer, ctx),
            device_id_type=MESH,
        )

    for step in range(1, group):
        gain_copy(step).start()
    pump_next()
    for copy in turned[group - 1 :]:
        copy.wait_recv()
    query_gather.sibling_here()
    for step in range(1, query_gather.chips):
        query_gather.crossed(step)
    split = query_split(width)
    filled_a = weight_grad(normed_all, query_all, 0, split, rest_a_work, 0, pumping)
    filled_b = weight_grad(normed_all, query_all, split, width, rest_b_work, 0, pumping)
    pair_gather.forward()
    pump_next()
    pair_gather.sibling_here()
    for step in range(1, pair_gather.chips):
        pair_gather.crossed(step)
    filled_b = weight_grad(normed_all, pair_all, 0, 2 * kv_width, rest_b_work, filled_b, pumping)
    for step in range(1, layer_sum.chips):
        ours = layer_part_ref.at[2 * lax.rem(layer_sum.chip + layer_sum.chips - step, layer_sum.chips) + layer_sum.core]
        for source, target in ((ours, far_ref.at[step - 1]), (layer_cross.at[step - 1], layer_stage)):
            if source is not ours:
                layer_sum.to_cross(step).wait_recv()
            copy = pltpu.make_async_copy(source, target, stage_sems.at[0])
            copy.start()
            copy.wait()
        far_ref[step - 1] = (
            far_ref[step - 1].astype(jnp.float32) + layer_stage[...].astype(jnp.float32)
        ).astype(jnp.bfloat16)
        layer_sum.to_far(step).start()
    gains = gain_give[...]
    for step in range(1, group):
        gain_copy(step).wait_recv()
        gains = gains + gain_got[step - 1]
    gain_tiles = gains.shape[0] // 16
    rest_a_work[filled_a : filled_a + gain_tiles] = gains.astype(jnp.bfloat16).reshape(
        gain_tiles, 16, LANES
    )
    clear_from(rest_a_work, filled_a + gain_tiles)
    clear_from(rest_b_work, filled_b)
    rest_a.start()
    rest_b.start()
    begun = pumped[0]
    total_pumps = max(wide_rings[0].ticks, late + out_a.ticks) * len(first_rings)

    half = -(-(total_pumps - begun) // rest_a.ticks)

    def layer_close():
        layer_sum.to_sibling().wait_recv()
        arrived = [layer_sib]
        for step in range(1, layer_sum.chips):
            layer_sum.to_far(step).wait_recv()
            arrived.append(layer_far.at[step - 1])
        for source in arrived:
            copy = pltpu.make_async_copy(source, layer_stage, stage_sems.at[0])
            copy.start()
            copy.wait()

            def add(at):
                block = pl.ds(pl.multiple_of(at * 32, 32), 32)
                layer_base_ref[block] = layer_base_ref[block] + layer_stage[block].astype(
                    jnp.float32
                )

            tiles(rows // 32, add)

        def close(at):
            block = pl.ds(pl.multiple_of(at * 32, 32), 32)
            layer_ref[block] = layer_base_ref[block].astype(jnp.bfloat16)

        tiles(rows // 32, close)

    def last_ticks(at, unused):
        tiles(half, lambda turn: pump(jnp.minimum(begun + half * at + turn, total_pumps)))
        tick(rest_a, at)
        tick(rest_b, at)

        @pl.when(at == rest_a.ticks * 3 // 4)
        def _():
            layer_close()

        return unused

    lax.fori_loop(0, rest_a.ticks, last_ticks, 0)
    layer_sum.sent()
    for ring in first_rings + [rest_a, rest_b]:
        ring.finish()
    for copy in turned:
        copy.wait_send()
    for gather in (branch_gather, query_gather, pair_gather):
        gather.sent()
    for step in range(1, group):
        gain_copy(step).wait_send()

    def sent(pair):
        @pl.when(jnp.logical_or(pair < steps.level, steps.side == 1))
        def _():
            across(pair).wait_send()

        @pl.when(pair < steps.level)
        def _():
            down_chain(pair).wait_send()

    tiles(steps.level + 1, sent)


def layer_back(
    q_wide, g_wide, log_total, gain_grad, gain, cosine, sine, all_pairs, mix, gate_part, up_part,
    layer_base, layer_parts, branch, low_t, normed_t, w_query, w_key, w_value, x, resid_grad, downs,
):
    group, count = lax.axis_size("fsdp"), lax.axis_size("ctx")
    units, deep, wide = q_wide.shape
    keys = all_pairs.shape[2]
    rows, width = x.shape
    own, kv_width = width // group, w_key.shape[1]
    bf16, f32 = jnp.bfloat16, jnp.float32
    dma = pltpu.SemaphoreType.DMA
    halves = wide_split(width)
    wide_chunk = (group, gate_part.shape[1] // (halves * count), 16, LANES)
    gain_rows = spread(2 * (width // LANES), 16)
    split, row_blocks = query_split(width), own // 16
    out_first = out_split(width)
    chips = group // 2
    small_chunks = [
        (spread(held, count) // count, 16, LANES)
        for held in (
            out_first // LANES * row_blocks,
            (width - out_first) // LANES * row_blocks,
            split // LANES * row_blocks + gain_rows // 16,
            (width - split + 2 * kv_width) // LANES * row_blocks,
        )
    ]
    levels = count // 2
    loaded = [mix, layer_base, w_query, w_key, w_value, x, resid_grad]
    return pl.pallas_call(
        functools.partial(back_kernel, [part.shape[0] for part in downs]),
        out_shape=[
            jax.ShapeDtypeStruct((rows, width), f32),
            jax.ShapeDtypeStruct((rows, width), bf16),
            *[ring_total(wide_chunk, True)] * (2 * halves),
            *[ring_total(part.shape) for part in downs],
            *[ring_total(chunk) for chunk in small_chunks],
            *[jax.ShapeDtypeStruct((levels, units, keys, deep), bf16)] * 2,
            jax.ShapeDtypeStruct((rows, width), bf16),
            *[jax.ShapeDtypeStruct((chips - 1, rows, width), bf16)] * 2,
        ],
        in_specs=[VMEM] * 7 + [ANY] * (14 + len(downs)),
        out_specs=[VMEM] * (6 + 2 * halves + len(downs)) + [ANY] * 5,
        scratch_shapes=[
            pltpu.VMEM(all_pairs.shape, bf16),
            pltpu.VMEM((2, units, keys, deep), bf16),
            pltpu.VMEM((units, keys, deep), f32),
            pltpu.VMEM((units, 2 * wide, deep), bf16),
            pltpu.VMEM((units, 1, wide), f32),
            pltpu.VMEM((units, HD, wide), f32),
            *[kind for _ in range(2 * halves) for kind in ring_scratch(wide_chunk, True)],
            *[kind for chunk in small_chunks for kind in ring_scratch(chunk)],
            pltpu.VMEM((own, group * rows), bf16),
            pltpu.VMEM((own, group * rows), bf16),
            pltpu.VMEM((group, rows, width), bf16),
            pltpu.VMEM((group, rows, width), bf16),
            pltpu.VMEM((group, rows, 2 * kv_width), bf16),
            pltpu.VMEM((rows, width), f32),
            pltpu.VMEM((gain_rows, LANES), f32),
            pltpu.VMEM((group - 1, gain_rows, LANES), f32),
            pltpu.VMEM((chips - 1, rows, width), bf16),
            pltpu.VMEM((rows, width), bf16),
            *[pltpu.VMEM(array.shape, array.dtype) for array in loaded],
            *[kind for _ in range(2 * halves) for kind in ring_semaphores(True)],
            *[kind for _ in range(len(downs) + 2) for kind in ring_semaphores()],
            *[dma((group - 1,))] * 2,
            *[kind for _ in range(2) for kind in ring_semaphores()],
            *[dma((levels,))] * 4,
            *[group_semaphores()] * 6,
            *[dma((group - 1,))] * 6,
            dma((11 + len(downs) + 2 * halves * count,)),
            dma((2,)),
        ],
        compiler_params=pltpu.CompilerParams(
            collective_id=3, has_side_effects=True, vmem_limit_bytes=62 << 20
        ),
    )(
        q_wide, g_wide, log_total, gain_grad, gain, cosine, sine, all_pairs, mix, gate_part, up_part,
        layer_base, layer_parts, branch, low_t, normed_t, w_query, w_key, w_value, x, resid_grad,
        *downs,
    )


def finish_kernel(halves, downs, *refs):
    taken = iter(refs)

    def take(number):
        return [next(taken) for _ in range(number)]

    wides, down_refs, smalls, (rows_ref,) = take(2 * halves), take(downs), take(4), take(1)
    outs, (tokens_ref,) = take(7), take(1)
    wide_held, down_held, small_held = take(2 * halves), take(downs), take(4)
    made, (load_sems, store_sems) = take(7), take(2)
    sources = [*wides, *down_refs, *smalls]
    held = [*wide_held, *down_held, *small_held]
    loads = {}
    for at, (source, target) in enumerate(zip(sources, held)):
        loads[id(target)] = pltpu.make_async_copy(source, target, load_sems.at[at])
        loads[id(target)].start()
    stores = []

    def store(index, columns=None):
        source, target = made[index], outs[index]
        if columns is not None:
            source, target = source.at[:, columns], target.at[:, columns]
        copy = pltpu.make_async_copy(source, target, store_sems.at[len(stores)])
        copy.start()
        stores.append(copy)

    rows = made[4].shape[0]
    row_blocks = rows // 16
    group = wides[0].shape[1]

    def unpack(source, first, index, begin, end):
        target = made[index]
        for block in range(begin, end):
            here = first + (block - begin) * row_blocks
            target[:, block * LANES : (block + 1) * LANES] = (
                source[here : here + row_blocks].reshape(rows, LANES).astype(jnp.float32)
            )
        return first + (end - begin) * row_blocks

    for index, parts in ((4, wide_held[:halves]), (5, wide_held[halves:])):
        for part in parts:
            loads[id(part)].wait()
        target = made[index]
        columns = target.shape[1] // group
        for owner in range(group):
            tile_rows = jnp.concatenate(
                [part[:, owner].reshape((-1,) + part.shape[3:]) for part in parts], axis=0
            )
            for block in range(columns // LANES):
                begin = owner * columns + block * LANES
                target[:, begin : begin + LANES] = (
                    tile_rows[block * row_blocks : (block + 1) * row_blocks]
                    .reshape(rows, LANES)
                    .astype(jnp.float32)
                )
            store(index, pl.ds(owner * columns, columns))
    down_grad = made[6]
    blocks, begin = down_grad.shape[0] // 16, 0
    for source in down_held:
        loads[id(source)].wait()
        end = min(blocks, begin + source.shape[0])
        if end > begin:
            down_grad[begin * 16 : end * 16, :] = (
                source[: end - begin]
                .reshape((end - begin) * 16, down_grad.shape[1])
                .astype(jnp.float32)
            )
        begin = end
    store(6)
    for part in small_held:
        loads[id(part)].wait()
    out_a, out_b, rest_a, rest_b = small_held
    lanes, kv_lanes = made[0].shape[1] // LANES, made[1].shape[1] // LANES
    middle, split = out_split(made[0].shape[1]) // LANES, query_split(made[0].shape[1]) // LANES
    unpack(out_a, 0, 3, 0, middle)
    unpack(out_b, 0, 3, middle, lanes)
    store(3)
    unpack(rest_a, 0, 0, 0, split)
    at = unpack(rest_b, 0, 0, split, lanes)
    store(0)
    at = unpack(rest_b, at, 1, 0, kv_lanes)
    store(1)
    unpack(rest_b, at, 2, 0, kv_lanes)
    store(2)
    keys = tokens_ref.shape[0]
    for sequence in range(tokens_ref.shape[1]):
        tokens_ref[:, sequence, :] = rows_ref[sequence * keys : (sequence + 1) * keys]
    for copy in stores:
        copy.wait()


def finish(wides, downs, smalls, token_rows, own, kv_width, hidden, sequences):
    rows, width = token_rows.shape
    f32 = jnp.float32
    outs = [
        jax.ShapeDtypeStruct((own, columns), f32)
        for columns in (width, kv_width, kv_width, width, FF, FF)
    ] + [jax.ShapeDtypeStruct((hidden, width), f32)]
    sources = [*wides, *downs, *smalls]
    dma = pltpu.SemaphoreType.DMA
    return pl.pallas_call(
        functools.partial(finish_kernel, len(wides) // 2, len(downs)),
        out_shape=outs + [jax.ShapeDtypeStruct((rows // sequences, sequences, width), f32)],
        in_specs=[ANY] * len(sources) + [VMEM],
        out_specs=[ANY] * len(outs) + [VMEM],
        scratch_shapes=[pltpu.VMEM(array.shape, array.dtype) for array in sources]
        + [pltpu.VMEM(out.shape, f32) for out in outs]
        + [dma((len(sources),)), dma((5 + 2 * wides[0].shape[1],))],
        compiler_params=pltpu.CompilerParams(vmem_limit_bytes=60 << 20),
    )(*sources, token_rows)


def on_device(
    tokens, w_query, w_key, w_value, w_out, w_gate, w_up, w_down, gain_attn, gain_ffn, cotangent
):
    block_len, seq_count, width = tokens.shape
    rows_count = block_len * seq_count
    kv_width = KVH * HD
    positions = lax.axis_index("ctx") * block_len + jnp.arange(block_len, dtype=jnp.int32)
    freqs = ROTARY_BASE ** (-2.0 * jnp.arange(HD // 2, dtype=jnp.float32) / HD)
    angles = freqs[:, None] * positions.astype(jnp.float32)[None, :]
    cosine, sine = jnp.cos(angles), jnp.sin(angles)
    x_rows = jnp.swapaxes(tokens, 0, 1).reshape(rows_count, width)
    g_rows = jnp.swapaxes(cotangent, 0, 1).reshape(rows_count, width)
    own = gain_attn.shape[0]
    units = seq_count * KVH
    wide = H // KVH * block_len
    own_gains = jnp.pad(
        jnp.stack([gain_attn, gain_ffn]).astype(jnp.float32), ((0, 6), (0, spread(own, LANES) - own))
    )
    (
        q_wide, normed_t, full_gain_attn, full_gain_ffn, full_query, full_key, full_value, attn_low, low_t, mix_unit, log_total,
        all_pairs, full_out, my_gate, my_up, all_g,
    ) = attend(
        x_rows, own_gains, cosine, sine, w_query, w_key, w_value, w_out, w_gate, w_up, g_rows, seq_count
    )
    layer_base, grad_resid, grad_branch, g_wide, gate_part, up_part, layer_parts, *downs = (
        feed_forward(
            x_rows, attn_low, full_out, my_gate, my_up, w_down, all_g, full_gain_ffn, units, wide
        )
    )
    downs, gain_term_ffn = downs[:-1], downs[-1]
    grad_tokens, layer_out, *sums = layer_back(
        q_wide, g_wide, log_total, gain_term_ffn, full_gain_attn, cosine, sine, all_pairs, mix_unit,
        gate_part, up_part, layer_base, layer_parts, grad_branch, low_t, normed_t, full_query,
        full_key, full_value, x_rows, grad_resid, downs,
    )
    wides, sums = sums[: 2 * wide_split(width)], sums[2 * wide_split(width) :]
    smalls = sums[len(downs) : len(downs) + 4]
    filled = query_split(width) // LANES * (own // 16)
    gain_grads = smalls[2][filled:].reshape(-1, LANES)[: 2 * (width // LANES)].reshape(2, width)
    gain_grads = lax.dynamic_slice_in_dim(gain_grads, lax.axis_index("fsdp") * own, own, 1)
    gain_grads = gain_grads.astype(jnp.float32)
    *grads, tokens_grad = finish(
        wides, sums[: len(downs)], smalls, grad_tokens, own, kv_width, w_down.shape[0], seq_count
    )
    return (
        jnp.swapaxes(layer_out.reshape(seq_count, block_len, width), 0, 1),
        tokens_grad,
        *grads,
        gain_grads[0],
        gain_grads[1],
    )


def solution(mesh):
    return jax.shard_map(
        on_device,
        mesh=mesh,
        in_specs=(
            P("ctx", "fsdp", None),
            P("fsdp", None),
            P("fsdp", None),
            P("fsdp", None),
            P("fsdp", None),
            P("fsdp", None),
            P("fsdp", None),
            P("fsdp", None),
            P("fsdp"),
            P("fsdp"),
            P("ctx", "fsdp", None),
        ),
        out_specs=(
            P("ctx", "fsdp", None),
            P("ctx", "fsdp", None),
            P("fsdp", None),
            P("fsdp", None),
            P("fsdp", None),
            P("fsdp", None),
            P("fsdp", None),
            P("fsdp", None),
            P("fsdp", None),
            P("fsdp"),
            P("fsdp"),
        ),
        check_vma=False,
    )
```

```python
import functools

import jax
import jax.numpy as jnp
from jax import lax
from jax.experimental import pallas as pl
from jax.experimental.pallas import tpu as pltpu
from jax.sharding import PartitionSpec as P

H = 18
KVH = 6
HD = 64
FF = 3072


EPSILON = 1e-05
ROTARY_BASE = 10000.0
MASKED_SCORE = -1e30


def norm_scale(rows):
    return lax.rsqrt(jnp.mean(rows * rows, axis=-1, keepdims=True) + EPSILON)


def forward_dot(left, right):
    return jnp.dot(left, right, preferred_element_type=jnp.float32)


MESH = pl.DeviceIdType.MESH
LANES = 128


def ring_place(ctx, fsdp, count):
    column, side = lax.div(ctx, 2), lax.rem(ctx, 2)
    place = column + side * (count - 1 - 2 * column)
    odd = lax.rem(fsdp, 2)
    return place + odd * (count - 1 - 2 * place)


def ring_ctx(place, fsdp, count):
    odd = lax.rem(fsdp, 2)
    place = place + odd * (count - 1 - 2 * place)
    late = lax.div(place, count // 2)
    return (1 - late) * 2 * place + late * (2 * (count - 1 - place) + 1)


class GroupGather:
    def __init__(self, shard_of, sends, arrivals):
        self.shard_of, self.sends, self.arrivals = shard_of, sends, arrivals
        self.fsdp, self.ctx = lax.axis_index("fsdp"), lax.axis_index("ctx")
        self.chips = lax.axis_size("fsdp") // 2
        self.chip, self.core = lax.div(self.fsdp, 2), lax.rem(self.fsdp, 2)
        self.sibling = 2 * self.chip + 1 - self.core

    def copy(self, source, shard, semaphore, device):
        return pltpu.make_async_remote_copy(
            src_ref=source,
            dst_ref=self.shard_of(shard),
            send_sem=self.sends.at[semaphore],
            recv_sem=self.arrivals.at[semaphore],
            device_id=(device, self.ctx),
            device_id_type=MESH,
        )

    def same_core(self, step):
        return 2 * lax.rem(self.chip + step, self.chips) + self.core

    def across(self, source):
        return self.copy(source, self.fsdp, 0, self.sibling)

    def out(self, source, step):
        return self.copy(source, self.fsdp, step, self.same_core(step))

    def onward(self, step):
        shard = self.same_core(self.chips - step)
        return self.copy(self.shard_of(shard), shard, self.chips - 1 + step, self.sibling)

    def start(self, source):
        for step in range(1, self.chips):
            self.out(source, step).start()
        self.across(source).start()

    def forward(self):
        own = self.shard_of(self.fsdp)
        for step in range(1, self.chips):
            self.out(own, step).wait_recv()
            self.onward(step).start()

    def sibling_here(self):
        self.across(self.shard_of(self.fsdp)).wait_recv()

    def crossed(self, step):
        self.onward(step).wait_recv()

    def sent(self):
        own = self.shard_of(self.fsdp)
        self.across(own).wait_send()
        for step in range(1, self.chips):
            self.out(own, step).wait_send()
            self.onward(step).wait_send()

    def finish(self):
        self.forward()
        self.sibling_here()
        for step in range(1, self.chips):
            self.crossed(step)
        self.sent()


class HalfGather:
    def __init__(self, held, own_rows, sends, arrivals):
        self.held, self.own = held, own_rows
        self.sends, self.arrivals = sends, arrivals
        self.fsdp, self.ctx = lax.axis_index("fsdp"), lax.axis_index("ctx")
        self.chips = lax.axis_size("fsdp") // 2
        self.chip, self.core = lax.div(self.fsdp, 2), lax.rem(self.fsdp, 2)
        self.sibling = 2 * self.chip + 1 - self.core
        self.side = lax.rem(self.ctx, 2)
        self.pair = self.ctx + 1 - 2 * self.side
        first = -(-own_rows // 32) * 16
        self.halves = ((0, first), (first, own_rows - first))

    def same_core(self, step):
        return 2 * lax.rem(self.chip + step, self.chips) + self.core

    def rows(self, shard, half=None):
        begin, size = (0, self.own) if half is None else self.halves[half]
        return self.held.at[pl.ds(shard * self.own + begin, size)]

    def copy(self, source, target, semaphore, device):
        return pltpu.make_async_remote_copy(
            src_ref=source,
            dst_ref=target,
            send_sem=self.sends.at[semaphore],
            recv_sem=self.arrivals.at[semaphore],
            device_id=device,
            device_id_type=MESH,
        )

    def on_side(self, body):
        for half in range(2):

            @pl.when(self.side == half)
            def _(half=half):
                body(half)

    def across(self, source):
        return self.copy(source, self.rows(self.fsdp), 0, (self.sibling, self.ctx))

    def out(self, source, step, half):
        begin, size = self.halves[half]
        return self.copy(
            source.at[pl.ds(begin, size)],
            self.rows(self.fsdp, half),
            step,
            (self.same_core(step), self.ctx),
        )

    def to_pair(self, step, half):
        part = self.rows(self.same_core(self.chips - step), half)
        return self.copy(part, part, self.chips - 1 + step, (self.fsdp, self.pair))

    def onward(self, step):
        part = self.rows(self.same_core(self.chips - step))
        return self.copy(part, part, 2 * self.chips - 2 + step, (self.sibling, self.ctx))

    def start(self, source):
        def send(half):
            for step in range(1, self.chips):
                self.out(source, step, half).start()

        self.on_side(send)
        self.across(source).start()

    def to_pairs(self):
        def forward(half):
            for step in range(1, self.chips):
                self.out(self.rows(self.fsdp), step, half).wait_recv()
                self.to_pair(step, half).start()

        self.on_side(forward)

    def to_sibling(self):
        def forward(half):
            for step in range(1, self.chips):
                self.to_pair(step, 1 - half).wait_recv()

        self.on_side(forward)
        for step in range(1, self.chips):
            self.onward(step).start()

    def arrived(self):
        self.across(self.rows(self.fsdp)).wait_recv()
        for step in range(1, self.chips):
            self.onward(step).wait_recv()

    def sent(self):
        def wait(half):
            for step in range(1, self.chips):
                self.out(self.rows(self.fsdp), step, half).wait_send()
                self.to_pair(step, half).wait_send()

        self.on_side(wait)
        self.across(self.rows(self.fsdp)).wait_send()
        for step in range(1, self.chips):
            self.onward(step).wait_send()


def half_semaphores(many):
    return pltpu.SemaphoreType.DMA((many, 3 * (lax.axis_size("fsdp") // 2) - 2))


def group_semaphores():
    return pltpu.SemaphoreType.DMA((lax.axis_size("fsdp") - 1,))


def greet_group(barrier):
    fsdp, ctx, group = lax.axis_index("fsdp"), lax.axis_index("ctx"), lax.axis_size("fsdp")
    for step in range(1, group):
        peer = lax.rem(fsdp + step, group)
        pl.semaphore_signal(barrier, inc=1, device_id=(peer, ctx), device_id_type=MESH)
    return group - 1


class Steps:
    def __init__(self):
        self.fsdp, self.ctx = lax.axis_index("fsdp"), lax.axis_index("ctx")
        self.levels = lax.axis_size("ctx") // 2
        self.level, self.side = lax.div(self.ctx, 2), lax.rem(self.ctx, 2)
        self.peer = (self.fsdp, 2 * self.level + 1 - self.side)
        self.above = (self.fsdp, lax.rem(self.ctx + 2, 2 * self.levels))
        self.below = (self.fsdp, lax.rem(self.ctx + 2 * self.levels - 2, 2 * self.levels))
        self.has_above = self.level + 1 < self.levels
        self.has_below = self.level > 0

    def greet(self, barrier):
        pl.semaphore_signal(barrier, inc=1, device_id=self.peer, device_id_type=MESH)

        @pl.when(self.has_above)
        def _():
            pl.semaphore_signal(barrier, inc=1, device_id=self.above, device_id_type=MESH)

        @pl.when(self.has_below)
        def _():
            pl.semaphore_signal(barrier, inc=1, device_id=self.below, device_id_type=MESH)

        return 1 + jnp.minimum(self.level, 1) + jnp.minimum(self.levels - 1 - self.level, 1)


PARTS = 2


def causal(keys, wide, shape):
    key_at = lax.broadcasted_iota(jnp.int32, shape, 0)
    query_at = lax.rem(lax.broadcasted_iota(jnp.int32, shape, 1), keys)
    return key_at <= query_at


def attend_kernel(
    x_ref, gain_ref, cos_ref, sin_ref, query_ref, key_ref, value_ref, out_ref, gate_ref, up_ref, g_ref,
    q_ref, normed_t_ref, gain_attn_ref, gain_ffn_ref, full_query, full_key, full_value,
    low_ref, low_t_ref, mix_ref, log_ref, all_ref, full_out_ref, my_gate_ref, my_up_ref, all_g_ref,
    normed_ref, key_rows, gain_all, own_out, own_gate, own_up, own_g,
    top_ref, total_ref, chain_sends, chain_arrivals, peer_sends, peer_arrivals,
    half_sends, half_arrivals, gain_sends, gain_arrivals,
    out_sends, out_arrivals, g_sends, g_arrivals,
    part_sends, part_arrivals, local_sems,
):
    steps = Steps()
    fsdp, ctx, group = steps.fsdp, steps.ctx, lax.axis_size("fsdp")
    units, deep, wide = q_ref.shape
    keys = all_ref.shape[2]
    per_part = units // PARTS
    rows_count, width = x_ref.shape
    own = query_ref.shape[0]
    sequences, groups = units // KVH, H // KVH
    barrier = pltpu.get_barrier_semaphore()
    greeted = steps.greet(barrier) + greet_group(barrier)
    span = KVH * HD
    pieces = [(key_ref, full_key, 0), (value_ref, full_value, 0)]
    pieces += [(query_ref, full_query, start) for start in range(0, width, span)]
    gathers = []
    for at, (source, target, start) in enumerate(pieces):
        columns = pl.ds(start, span)
        gather = HalfGather(
            target.at[:, columns], own, half_sends.at[at], half_arrivals.at[at]
        )
        gathers.append((gather, source.at[:, columns]))
    own_rows = pl.ds(fsdp * own, own)
    own_copies = [
        pltpu.make_async_copy(source, target.at[own_rows], local_sems.at[4 + at])
        for at, (source, target) in enumerate(
            ((key_ref, full_key), (value_ref, full_value), (query_ref, full_query))
        )
    ]
    for copy in own_copies:
        copy.start()
    gain_all[fsdp] = gain_ref[...]
    pl.semaphore_wait(barrier, greeted)

    def gain_copy(step):
        peer = lax.rem(fsdp + step, group)
        return pltpu.make_async_remote_copy(
            src_ref=gain_ref,
            dst_ref=gain_all.at[fsdp],
            send_sem=gain_sends.at[step - 1],
            recv_sem=gain_arrivals.at[step - 1],
            device_id=(peer, ctx),
            device_id_type=MESH,
        )

    for step in range(1, group):
        gain_copy(step).start()
    for gather, source in gathers:
        gather.start(source)
    inputs = x_ref[...].astype(jnp.float32)
    scale = norm_scale(inputs)
    q_ref[:, HD:, :] = jnp.zeros((units, HD, wide), q_ref.dtype)
    for step in range(1, group):
        gain_copy(step).wait_recv()
    gains = jnp.concatenate([gain_all[shard][:, :own] for shard in range(group)], axis=1)
    gain_attn_ref[...] = gains[:1]
    gain_ffn_ref[...] = gains[1:2]
    normed_ref[...] = (inputs * scale * gains[:1]).astype(jnp.bfloat16)
    cosine, sine = cos_ref[...], sin_ref[...]

    def turn(columns):
        first, second = columns[: HD // 2], columns[HD // 2 :]
        return jnp.concatenate(
            [first * cosine - second * sine, second * cosine + first * sine], axis=0
        ).astype(jnp.bfloat16)

    def block_copy(level, part, side, semaphores, arrivals, arrives, device):
        block = 2 * (steps.level - level) + side
        held = all_ref.at[block, pl.ds(part * per_part, per_part)]
        return pltpu.make_async_remote_copy(
            src_ref=held,
            dst_ref=held,
            send_sem=semaphores.at[level, part],
            recv_sem=arrivals.at[arrives, part],
            device_id=device,
            device_id_type=MESH,
        )

    def chain(level, part):
        return block_copy(
            level, part, steps.side, chain_sends, chain_arrivals, level + 1, steps.above
        )

    def across(level, part):
        return block_copy(
            level, part, steps.side, peer_sends, peer_arrivals, level, steps.peer
        )

    def pass_on(level, part):
        @pl.when(steps.has_above)
        def _():
            chain(level, part).start()

    def project(at):
        _, weight, start = pieces[at]
        made = forward_dot(normed_ref[...], weight[:, start : start + span])
        if at == 0:
            key_rows[...] = made
            return
        for sequence in range(sequences):
            block = slice(sequence * keys, (sequence + 1) * keys)
            for pair in range(span // (2 * HD)):
                columns = slice(pair * 2 * HD, (pair + 1) * 2 * HD)
                turned = made[block, columns].T
                if at == 1:
                    turned_keys = key_rows[block, columns].T
                    for half in range(2):
                        held = slice(half * HD, (half + 1) * HD)
                        both = jnp.concatenate(
                            [turn(turned_keys[held]), turned[held].astype(jnp.bfloat16)], axis=0
                        )
                        all_ref[ctx, sequence * KVH + 2 * pair + half] = both.T
                else:
                    for half in range(2):
                        head = start // HD + 2 * pair + half
                        unit, member = sequence * KVH + head // groups, head % groups
                        part = turn(turned[half * HD : (half + 1) * HD])
                        q_ref[unit, :HD, member * keys : (member + 1) * keys] = part * jnp.bfloat16(
                            HD ** (-0.5)
                        )
        if at == 1:
            for part in range(PARTS):
                pass_on(0, part)

                @pl.when(steps.side == 0)
                def _():
                    across(0, part).start()

    columns = my_gate_ref.shape[1]
    gathered = HalfGather(full_out_ref, own, out_sends.at[0], out_arrivals.at[0])
    gathered_g = GroupGather(lambda shard: all_g_ref.at[shard], g_sends, g_arrivals)
    mine = lane_tile(fsdp, columns)
    own_parts = (
        (out_ref, own_out, full_out_ref.at[own_rows]),
        (gate_ref.at[:, mine], own_gate, my_gate_ref.at[own_rows]),
        (up_ref.at[:, mine], own_up, my_up_ref.at[own_rows]),
        (g_ref, own_g, all_g_ref.at[fsdp]),
    )
    loads = [
        pltpu.make_async_copy(source, held, local_sems.at[at])
        for at, (source, held, _) in enumerate(own_parts)
    ]
    background = [
        pltpu.make_async_copy(held, target, local_sems.at[at])
        for at, (_, held, target) in enumerate(own_parts)
    ]
    slices = []
    for which, (source, target) in enumerate(((gate_ref, my_gate_ref), (up_ref, my_up_ref))):
        for step in range(1, group):
            peer = lax.rem(fsdp + step, group)
            slices.append(
                pltpu.make_async_remote_copy(
                    src_ref=source.at[:, lane_tile(peer, columns)],
                    dst_ref=target.at[own_rows],
                    send_sem=part_sends.at[which, step - 1],
                    recv_sem=part_arrivals.at[which, step - 1],
                    device_id=(peer, ctx),
                    device_id_type=MESH,
                )
            )

    def start_background():
        for copy in loads:
            copy.start()
        gathered.start(out_ref)
        for copy in slices:
            copy.start()
        gathered_g.start(g_ref)

    last = len(pieces)
    for at in range(last + 2):
        if at < last:
            gathers[at][0].to_pairs()
        if at == 0:
            start_background()
        if 1 <= at <= last:
            gathers[at - 1][0].to_sibling()
        if at == 1:
            for column in range(width // LANES):
                columns = slice(column * LANES, (column + 1) * LANES)
                normed_t_ref[columns, :] = normed_ref[:, columns].T
            for copy in own_copies:
                copy.wait()
        if at >= 2:
            gathers[at - 2][0].arrived()
            project(at - 2)

    def second_half():
        gathered.to_pairs()
        for load, copy in zip(loads, background):
            load.wait()
            copy.start()

    def add(unit, kv):
        scores = jnp.dot(kv, q_ref[unit], preferred_element_type=jnp.float32)
        top = top_ref[unit]
        new_top = jnp.maximum(top, jnp.max(scores, axis=0, keepdims=True))
        fade = jnp.exp(top - new_top)
        weights = jnp.exp(scores - new_top)
        top_ref[unit] = new_top
        total_ref[unit] = total_ref[unit] * fade + jnp.sum(weights, axis=0, keepdims=True)
        added = jnp.dot(kv.T, weights.astype(jnp.bfloat16), preferred_element_type=jnp.float32)
        mix_ref[unit] = mix_ref[unit] * fade + added[HD:]

    def over_units(body, first, count):
        def two(at, unused):
            body(first + 2 * at)
            body(first + 2 * at + 1)
            return unused

        lax.fori_loop(0, count // 2, two, 0)

    def diagonal(unit):
        kv = all_ref[ctx, unit]
        scores = jnp.dot(kv, q_ref[unit], preferred_element_type=jnp.float32)
        scores = jnp.where(causal(keys, wide, scores.shape), scores, MASKED_SCORE)
        top = jnp.max(scores, axis=0, keepdims=True)
        weights = jnp.exp(scores - top)
        top_ref[unit] = top
        total_ref[unit] = jnp.sum(weights, axis=0, keepdims=True)
        added = jnp.dot(kv.T, weights.astype(jnp.bfloat16), preferred_element_type=jnp.float32)
        mix_ref[unit] = added[HD:]

    over_units(diagonal, 0, units)

    def forward(level, part):
        chain(level - 1, part).wait_recv()
        pass_on(level, part)
        across(level, part).start()

    @pl.when(steps.level >= 1)
    def _():
        for part in range(PARTS):
            forward(1, part)

    @pl.when(steps.side == 1)
    def _():
        for part in range(PARTS):
            across(0, part).wait_recv()
            over_units(lambda unit: add(unit, all_ref[ctx - 1, unit]), part * per_part, per_part)

    def level_step(level, unused):
        first = 2 * (steps.level - level)
        for part in range(PARTS):

            @pl.when(level < steps.level)
            def _():
                forward(level + 1, part)

            across(level, part).wait_recv()
            over_units(
                lambda unit: add(unit, all_ref[pl.ds(first, 2), unit].reshape(2 * keys, deep)),
                part * per_part,
                per_part,
            )

        @pl.when(level == 1)
        def _():
            second_half()

        return unused

    @pl.when(steps.level == 0)
    def _():
        second_half()

    lax.fori_loop(1, steps.level + 1, level_step, 0)

    def close(unit):
        total = total_ref[unit]
        mix_ref[unit] = mix_ref[unit] / total
        log_ref[unit] = top_ref[unit] + jnp.log(total)

    over_units(close, 0, units)
    for sequence in range(sequences):
        for pair in range(H // 2):
            heads = []
            for head in (2 * pair, 2 * pair + 1):
                unit, member = sequence * KVH + head // groups, head % groups
                heads.append(mix_ref[unit, :, member * keys : (member + 1) * keys])
            tile = jnp.concatenate(heads, axis=0).astype(low_ref.dtype)
            block = slice(sequence * keys, (sequence + 1) * keys)
            columns = slice(pair * 2 * HD, (pair + 1) * 2 * HD)
            low_t_ref[columns, block] = tile
            low_ref[block, columns] = tile.T
    for gather, _ in gathers:
        gather.sent()
    for step in range(1, group):
        gain_copy(step).wait_send()
    gathered.to_sibling()
    gathered_g.forward()
    gathered.arrived()
    gathered.sent()
    gathered_g.sibling_here()
    for step in range(1, gathered_g.chips):
        gathered_g.crossed(step)
    gathered_g.sent()
    for copy in slices:
        copy.wait()
    for copy in background:
        copy.wait()

    def sent(level, unused):
        for part in range(PARTS):

            @pl.when(steps.has_above)
            def _():
                chain(level, part).wait_send()

            @pl.when(jnp.logical_or(level > 0, steps.side == 0))
            def _():
                across(level, part).wait_send()

        return unused

    lax.fori_loop(0, steps.level + 1, sent, 0)


ANY = pl.BlockSpec(memory_space=pl.ANY)
VMEM = pl.BlockSpec(memory_space=pltpu.VMEM)


def attend(x, gains, cosine, sine, w_query, w_key, w_value, w_out, w_gate, w_up, g_rows, sequences):
    group, count = lax.axis_size("fsdp"), lax.axis_size("ctx")
    rows, width = x.shape
    own, hidden = w_query.shape[0], w_gate.shape[1] // group
    keys, units, deep = rows // sequences, sequences * KVH, 2 * HD
    wide = H // KVH * keys
    kv_width = KVH * HD
    dma = pltpu.SemaphoreType.DMA
    bf16, f32 = jnp.bfloat16, jnp.float32
    pieces = 2 + width // kv_width
    return pl.pallas_call(
        attend_kernel,
        out_shape=[
            jax.ShapeDtypeStruct((units, deep, wide), bf16),
            jax.ShapeDtypeStruct((width, rows), bf16),
            jax.ShapeDtypeStruct((1, width), f32),
            jax.ShapeDtypeStruct((1, width), f32),
            jax.ShapeDtypeStruct((width, width), bf16),
            jax.ShapeDtypeStruct((width, kv_width), bf16),
            jax.ShapeDtypeStruct((width, kv_width), bf16),
            jax.ShapeDtypeStruct((rows, width), bf16),
            jax.ShapeDtypeStruct((width, rows), bf16),
            jax.ShapeDtypeStruct((units, HD, wide), f32),
            jax.ShapeDtypeStruct((units, 1, wide), f32),
            jax.ShapeDtypeStruct((count, units, keys, deep), bf16),
            jax.ShapeDtypeStruct((width, width), bf16),
            jax.ShapeDtypeStruct((width, hidden), bf16),
            jax.ShapeDtypeStruct((width, hidden), bf16),
            jax.ShapeDtypeStruct((group, rows, width), bf16),
        ],
        in_specs=[VMEM] * 4 + [ANY] * 7,
        out_specs=[VMEM] * 12 + [ANY] * 4,
        scratch_shapes=[
            pltpu.VMEM((rows, width), bf16),
            pltpu.VMEM((rows, kv_width), f32),
            pltpu.VMEM((group,) + gains.shape, f32),
            pltpu.VMEM((own, width), bf16),
            pltpu.VMEM((own, hidden), bf16),
            pltpu.VMEM((own, hidden), bf16),
            pltpu.VMEM((rows, width), bf16),
            pltpu.VMEM((units, 1, wide), f32),
            pltpu.VMEM((units, 1, wide), f32),
            dma((count // 2, PARTS)),
            dma((count // 2 + 1, PARTS)),
            dma((count // 2, PARTS)),
            dma((count // 2, PARTS)),
            half_semaphores(pieces),
            half_semaphores(pieces),
            *[dma((group - 1,))] * 2,
            *[half_semaphores(1)] * 2,
            *[group_semaphores()] * 2,
            *[dma((2, group - 1))] * 2,
            dma((7,)),
        ],
        compiler_params=pltpu.CompilerParams(
            collective_id=1, has_side_effects=True, vmem_limit_bytes=60 << 20
        ),
    )(x, gains, cosine, sine, w_query, w_key, w_value, w_out, w_gate, w_up, g_rows)


class Ring:
    def __init__(self, work, landing, total, semaphores, forward, exchange=False):
        self.fsdp, self.ctx = lax.axis_index("fsdp"), lax.axis_index("ctx")
        self.group, self.count = lax.axis_size("fsdp"), lax.axis_size("ctx")
        self.work, self.landing, self.total = work, landing, total
        self.sends, self.arrivals = semaphores[:2]
        self.part_sends, self.part_arrivals, self.own_sem = semaphores[2:] if exchange else (None,) * 3
        self.exchange = exchange
        side = 0 if forward else 1
        self.place = ring_place(self.ctx, side, self.count)
        self.after = (self.fsdp, ring_ctx(lax.rem(self.place + 1, self.count), side, self.count))
        self.ticks = 2 * self.count - 2 + int(exchange)

    def chunk(self, held, index):
        if self.exchange:
            return held.at[index]
        per = held.shape[0] // self.count
        return held.at[pl.ds(index * per, per)]

    def summing(self, step, index):
        return self.copy(self.chunk(self.work, index), self.landing.at[step], step)

    def handing(self, step, index):
        held = self.chunk(self.total, index)
        return self.copy(held, held, step)

    def copy(self, source, target, step):
        return pltpu.make_async_remote_copy(
            src_ref=source,
            dst_ref=target,
            send_sem=self.sends.at[step],
            recv_sem=self.arrivals.at[step],
            device_id=self.after,
            device_id_type=MESH,
        )

    def part(self, index, step):
        peer = lax.rem(self.fsdp + step, self.group)
        return pltpu.make_async_remote_copy(
            src_ref=self.work.at[index, peer],
            dst_ref=self.total.at[index, self.fsdp],
            send_sem=self.part_sends.at[step - 1],
            recv_sem=self.part_arrivals.at[step - 1],
            device_id=(peer, self.ctx),
            device_id_type=MESH,
        )

    def own_part(self, index):
        return pltpu.make_async_copy(
            self.work.at[index, self.fsdp], self.total.at[index, self.fsdp], self.own_sem
        )

    def start(self):
        self.summing(0, self.place).start()

    def tick(self, at):
        last = self.count - 2
        gap = int(self.exchange)
        step = at - gap * jnp.where(at > last, 1, 0) if self.exchange else at
        index = lax.rem(self.place + 3 * self.count - 1 - step, self.count)

        def add(target):
            part, landed = self.chunk(self.work, index), self.landing.at[jnp.minimum(at, last)]
            for row in range(part.shape[0]):
                target[row] = (
                    part[row].astype(jnp.float32) + landed[row].astype(jnp.float32)
                ).astype(part.dtype)

        @pl.when(at <= last)
        def _():
            self.summing(jnp.minimum(at, last), index).wait_recv()

        @pl.when(at < last)
        def _():
            add(self.chunk(self.work, index))
            self.summing(jnp.minimum(at + 1, last), index).start()

        if self.exchange:

            @pl.when(at == last)
            def _():
                add(self.chunk(self.work, index))
                for peer in range(1, self.group):
                    self.part(index, peer).start()
                self.own_part(index).start()

            @pl.when(at == last + 1)
            def _():
                done = lax.rem(self.place + 1, self.count)
                self.own_part(done).wait()
                for peer in range(1, self.group):
                    self.part(done, peer).wait_recv()
                self.handing(last + 1, done).start()

        else:

            @pl.when(at == last)
            def _():
                add(self.chunk(self.total, index))
                self.handing(last + 1, index).start()

        @pl.when(at > last + gap)
        def _():
            here = jnp.maximum(step, last + 1)
            self.handing(here, index).wait_recv()

            @pl.when(here < 2 * self.count - 3)
            def _():
                self.handing(jnp.minimum(here + 1, 2 * self.count - 3), index).start()

    def finish(self):
        def wait(step, unused):
            self.handing(step, self.place).wait_send()
            return unused

        lax.fori_loop(0, 2 * self.count - 2, wait, 0)
        if self.exchange:
            for peer in range(1, self.group):
                self.part(lax.rem(self.place + 1, self.count), peer).wait_send()


class SumRing(Ring):
    def __init__(self, *args):
        super().__init__(*args)
        self.ticks = self.count - 1

    def tick(self, at):
        last = self.count - 2
        index = lax.rem(self.place + 2 * self.count - 1 - at, self.count)
        self.summing(at, index).wait_recv()
        work, landed = self.chunk(self.work, index), self.landing.at[at]

        def add(target):
            for row in range(work.shape[0]):
                target[row] = (
                    work[row].astype(jnp.float32) + landed[row].astype(jnp.float32)
                ).astype(work.dtype)

        @pl.when(at < last)
        def _():
            add(work)
            self.summing(jnp.minimum(at + 1, last), index).start()

        @pl.when(at == last)
        def _():
            add(self.total)

    def finish(self):
        def wait(step, unused):
            self.summing(step, self.place).wait_send()
            return unused

        lax.fori_loop(0, self.ticks, wait, 0)


class SpreadRing(Ring):
    def __init__(self, total, semaphores, forward):
        super().__init__(None, None, total, semaphores, forward)
        self.ticks = self.count - 1
        self.first = lax.rem(self.place + 1, self.count)

    def start(self):
        self.handing(0, self.first).start()

    def tick(self, at):
        index = lax.rem(self.place + self.count - at, self.count)
        self.handing(at, index).wait_recv()

        @pl.when(at < self.count - 2)
        def _():
            self.handing(jnp.minimum(at + 1, self.count - 2), index).start()

    def finish(self):
        def wait(step, unused):
            self.handing(step, self.place).wait_send()
            return unused

        lax.fori_loop(0, self.ticks, wait, 0)


def ring_scratch(chunk, exchange=False):
    count = lax.axis_size("ctx")
    work = (count,) + chunk if exchange else (count * chunk[0],) + chunk[1:]
    return [pltpu.VMEM(work, jnp.bfloat16), pltpu.VMEM((count - 1,) + chunk, jnp.bfloat16)]


def ring_total(chunk, exchange=False):
    count = lax.axis_size("ctx")
    work = (count,) + chunk if exchange else (count * chunk[0],) + chunk[1:]
    return jax.ShapeDtypeStruct(work, jnp.bfloat16)


def ring_semaphores(exchange=False):
    dma, steps = pltpu.SemaphoreType.DMA, 2 * lax.axis_size("ctx") - 2
    parts = lax.axis_size("fsdp") - 1
    return [dma((steps,))] * 2 + ([dma((parts,))] * 2 + [dma] if exchange else [])


def wide_split(width):
    group, count = lax.axis_size("fsdp"), lax.axis_size("ctx")
    return 2 if FF // group // LANES * (width // group // 16) >= 4 * count else 1


def query_split(width):
    return width // LANES * 7 // 9 * LANES


def out_split(width):
    return (width // LANES + 1) // 2 * LANES


def down_split(blocks, count):
    each = -(-blocks // count)
    rings = 4 if each >= 4 else 2
    return [max(1, (each + at) // rings) for at in range(rings)]


class GroupScatter:
    def __init__(self, give_sib, got_sib, give_cross, got_cross, far, got_far, sends, arrivals):
        self.give_sib, self.got_sib = give_sib, got_sib
        self.give_cross, self.got_cross = give_cross, got_cross
        self.far, self.got_far = far, got_far
        self.sends, self.arrivals = sends, arrivals
        self.fsdp, self.ctx = lax.axis_index("fsdp"), lax.axis_index("ctx")
        self.chips = lax.axis_size("fsdp") // 2
        self.chip, self.core = lax.div(self.fsdp, 2), lax.rem(self.fsdp, 2)
        self.sibling = 2 * self.chip + 1 - self.core

    def copy(self, source, target, semaphore, device):
        return pltpu.make_async_remote_copy(
            src_ref=source,
            dst_ref=target,
            send_sem=self.sends.at[semaphore],
            recv_sem=self.arrivals.at[semaphore],
            device_id=(device, self.ctx),
            device_id_type=MESH,
        )

    def to_sibling(self):
        return self.copy(self.give_sib, self.got_sib, 0, self.sibling)

    def to_cross(self, step):
        return self.copy(
            self.give_cross(step), self.got_cross.at[step - 1], step, self.sibling
        )

    def to_far(self, step):
        chip = lax.rem(self.chip + self.chips - step, self.chips)
        return self.copy(
            self.far.at[step - 1],
            self.got_far.at[step - 1],
            self.chips - 1 + step,
            2 * chip + self.core,
        )

    def add_cross(self, step):
        self.to_cross(step).wait_recv()
        held = self.far.at[step - 1]
        held[...] = (
            held[...].astype(jnp.float32) + self.got_cross[step - 1].astype(jnp.float32)
        ).astype(held.dtype)
        self.to_far(step).start()

    def total(self, own):
        self.to_sibling().wait_recv()
        value = own + self.got_sib[...].astype(jnp.float32)
        for step in range(1, self.chips):
            self.to_far(step).wait_recv()
            value = value + self.got_far[step - 1].astype(jnp.float32)
        return value

    def sent(self):
        self.to_sibling().wait_send()
        for step in range(1, self.chips):
            self.to_cross(step).wait_send()
            self.to_far(step).wait_send()


def scatter_scratch(rows, width):
    far = lax.axis_size("fsdp") // 2 - 1
    one, many = (rows, width), (far, rows, width)
    return [pltpu.VMEM(shape, jnp.bfloat16) for shape in (one, one, many, many, many, many)]


def dot_columns(left, right):
    return lax.dot_general(
        left, right, (((1,), (1,)), ((), ())), preferred_element_type=jnp.float32
    )


def tiles(count, body):
    def step(at, unused):
        body(at)
        return unused

    lax.fori_loop(0, count, step, 0)


def lane_tile(at, size):
    return pl.ds(pl.multiple_of(at * size, LANES), size)


def width_tile(width):
    return 384 if width % 384 == 0 else width


def hidden_tile(hidden):
    return 256 if hidden % 256 == 0 else 128


def transpose_into(target, source):
    rows, columns = source.shape

    def body(at):
        part = source[:, lane_tile(at, LANES)]
        target[pl.ds(pl.multiple_of(at * LANES, LANES), LANES), :] = part.T

    tiles(columns // LANES, body)


def ffn_kernel(
    x_ref, low_ref, out_ref, gain_ref, gate_in, up_in, down_in, all_g_in,
    layer_ref, resid_grad_ref, branch_ref, g_wide_ref, gate_part_out, up_part_out, layer_part_out,
    *rest,
):
    downs = len(down_split(gate_in.shape[1] // 16, lax.axis_size("ctx")))
    taken = iter(rest)

    def take(number):
        return [next(taken) for _ in range(number)]

    down_done, (gain_grad_ref,) = take(downs), take(1)
    all_n_ref, turned_n, turned_act, act_ref, gate_grad, up_grad, resid_ref, grad_own = take(8)
    down_scratch = take(2 * downs)
    give_sib, got_sib, give_cross, got_cross, far, got_far = take(6)
    n_sends, n_arrivals, grad_sends, grad_arrivals = take(4)
    gate_ref, up_ref, down_ref, all_g_ref, gate_part_ref, up_part_ref, layer_part_ref = take(7)
    (local_sems,) = take(1)
    loads = [
        pltpu.make_async_copy(source, target, local_sems.at[at])
        for at, (source, target) in enumerate(
            ((gate_in, gate_ref), (up_in, up_ref), (all_g_in, all_g_ref), (down_in, down_ref))
        )
    ]
    for copy in loads:
        copy.start()
    stores = []

    def store(source, target):
        copy = pltpu.make_async_copy(source, target, local_sems.at[len(loads) + len(stores)])
        copy.start()
        stores.append(copy)

    rings = [
        SumRing(*down_scratch[2 * at : 2 * at + 2], down_done[at], take(2), at % 2 == 0)
        for at in range(downs)
    ]
    group = lax.axis_size("fsdp")
    rows, width = x_ref.shape
    hidden = gate_ref.shape[1]
    barrier = pltpu.get_barrier_semaphore()
    greeted = greet_group(barrier) + 2
    for ring in rings[:2]:
        pl.semaphore_signal(barrier, inc=1, device_id=ring.after, device_id_type=MESH)
    step_in, step_out = hidden_tile(hidden), width_tile(width)

    def branch(at):
        columns = lane_tile(at, step_out)
        resid_ref[:, columns] = x_ref[:, columns].astype(jnp.float32) + forward_dot(
            low_ref[...], out_ref[:, columns]
        )

    tiles(width // step_out, branch)
    gain = gain_ref[...]
    scale = norm_scale(resid_ref[...])
    gathered = GroupGather(lambda shard: all_n_ref.at[shard], n_sends, n_arrivals)
    fsdp, chips = gathered.fsdp, gathered.chips
    all_n_ref[fsdp] = (resid_ref[...] * scale * gain).astype(jnp.bfloat16)
    pl.semaphore_wait(barrier, greeted)
    gathered.start(all_n_ref.at[fsdp])
    grad_sum = GroupScatter(
        give_sib,
        got_sib,
        lambda step: give_cross.at[step - 1],
        got_cross,
        far,
        got_far,
        grad_sends,
        grad_arrivals,
    )

    def hidden_part(shard):
        def body(at):
            columns = lane_tile(at, step_in)
            normed = all_n_ref[shard]
            gate = forward_dot(normed, gate_ref[:, columns])
            upward = forward_dot(normed, up_ref[:, columns])
            grad_act = dot_columns(
                all_g_ref[shard], down_ref[pl.ds(pl.multiple_of(at * step_in, LANES), step_in), :]
            )
            sigmoid = jax.nn.sigmoid(gate)
            silu = gate * sigmoid
            act_ref[shard, :, columns] = (silu * upward).astype(jnp.bfloat16)
            gate_grad[shard, :, columns] = (
                grad_act * upward * (sigmoid * (1.0 + gate * (1.0 - sigmoid)))
            ).astype(jnp.bfloat16)
            up_grad[shard, :, columns] = (grad_act * silu).astype(jnp.bfloat16)

        tiles(hidden // step_in, body)

    def grad_part(shard, target):
        def body(at):
            columns = pl.ds(pl.multiple_of(at * step_out, LANES), step_out)
            target[:, columns] = (
                dot_columns(gate_grad[shard], gate_ref[columns, :])
                + dot_columns(up_grad[shard], up_ref[columns, :])
            ).astype(target.dtype)

        tiles(width // step_out, body)

    for copy in loads:
        copy.wait()
    hidden_part(fsdp)
    gathered.sibling_here()
    sibling = gathered.sibling
    hidden_part(sibling)
    grad_part(sibling, grad_sum.give_sib)
    grad_sum.to_sibling().start()
    gathered.forward()
    grad_part(fsdp, grad_own)
    def turn_act(shard):
        transpose_into(turned_act.at[:, lane_tile(shard, rows)], act_ref.at[shard])

    turn_act(fsdp)
    turn_act(sibling)
    far_shards = []
    for step in range(1, chips):
        ours = gathered.same_core(chips - step)
        theirs = ours + sibling - fsdp
        far_shards.append((step, ours, theirs))
        gathered.crossed(step)
        hidden_part(theirs)
        hidden_part(ours)
        turn_act(theirs)
        turn_act(ours)
    blocks = hidden // 16
    spans, first = [], 0
    for ring in rings:
        last = min(blocks, first + ring.work.shape[0])
        spans.append((first, last, ring.work))
        first = last

    def down_tile(at):
        columns = lane_tile(at, step_out)
        part = forward_dot(
            turned_act[...], all_g_ref[:, :, columns].reshape(group * rows, step_out)
        ).astype(jnp.bfloat16)
        for begin, end, work in spans:
            if end > begin:
                work[: end - begin, :, columns] = part[begin * 16 : end * 16].reshape(
                    end - begin, 16, step_out
                )

    tiles(width // step_out, down_tile)
    for begin, end, work in spans:
        for spare in range(end - begin, work.shape[0]):
            work[spare] = jnp.zeros(work.shape[1:], work.dtype)
    for ring in rings:
        ring.start()
    for step, ours, theirs in far_shards:
        grad_part(theirs, give_cross.at[step - 1])
        grad_sum.to_cross(step).start()
        grad_part(ours, far.at[step - 1])
        grad_sum.add_cross(step)
    ticked = [0]

    def ring_tick(at):
        for ring in rings:

            @pl.when(at < ring.ticks)
            def _():
                ring.tick(jnp.minimum(at, ring.ticks - 1))

    def ticking(times, body):
        begin = ticked[0]

        def step(at):
            body(at)
            ring_tick(begin + at)

        tiles(times, step)
        ticked[0] += times

    for shard in range(group):
        span = slice(shard * rows, (shard + 1) * rows)
        transpose_into(turned_n.at[:, span], all_n_ref.at[shard])
    own = width // group
    row_blocks = own // 16
    for source, target in ((gate_grad, gate_part_ref), (up_grad, up_part_ref)):

        def weight_tile(at):
            columns = lane_tile(at, step_in)
            part = forward_dot(
                turned_n[...], source[:, :, columns].reshape(group * rows, step_in)
            ).astype(jnp.bfloat16)
            for block in range(step_in // LANES):
                first = (at * (step_in // LANES) + block) * row_blocks
                for owner in range(group):
                    target[owner, pl.ds(first, row_blocks)] = part[
                        owner * own : (owner + 1) * own, block * LANES : (block + 1) * LANES
                    ].reshape(row_blocks, 16, LANES)

        ticking(hidden // step_in, weight_tile)
        filled = hidden // LANES * row_blocks
        for spare in range(filled, target.shape[1]):
            for owner in range(group):
                target[owner, spare] = jnp.zeros(target.shape[2:], target.dtype)
        store(target, gate_part_out if source is gate_grad else up_part_out)

    def layer_tile(at):
        columns = lane_tile(at, step_out)
        part = forward_dot(
            act_ref[...].reshape(group * rows, hidden), down_ref[:, columns]
        ).reshape(group, rows, step_out)
        layer_part_ref[:, :, columns] = part.astype(jnp.bfloat16)

    ticking(width // step_out, layer_tile)
    store(layer_part_ref, layer_part_out)
    layer_ref[...] = resid_ref[...] + layer_part_ref[fsdp].astype(jnp.float32)
    upstream = grad_sum.total(grad_own[...])
    resid = resid_ref[...]
    scaled = upstream * gain
    grad_resid = (
        all_g_ref[fsdp].astype(jnp.float32)
        + scale * scaled
        - resid * scale**3 * jnp.mean(scaled * resid, axis=-1, keepdims=True)
    )
    gain_grad_ref[...] = jnp.sum(upstream * resid * scale, axis=0, keepdims=True)
    resid_grad_ref[...] = grad_resid
    branch_ref[...] = grad_resid.astype(jnp.bfloat16)
    units, _, wide = g_wide_ref.shape
    sequences = units // KVH
    keys = rows // sequences
    groups = wide // keys
    g_wide_ref[:, :HD, :] = jnp.zeros((units, HD, wide), g_wide_ref.dtype)
    for pair in range(H // 2):
        columns = slice(pair * 2 * HD, (pair + 1) * 2 * HD)
        mixed = dot_columns(branch_ref[...], out_ref[columns, :]).astype(jnp.bfloat16)
        for sequence in range(sequences):
            turned = mixed[sequence * keys : (sequence + 1) * keys].T
            for half in range(2):
                head = 2 * pair + half
                unit, member = sequence * KVH + head // groups, head % groups
                g_wide_ref[unit, HD:, member * keys : (member + 1) * keys] = turned[
                    half * HD : (half + 1) * HD
                ]
    begin = ticked[0]
    tiles(max(0, rings[0].ticks - begin), lambda at: ring_tick(begin + at))
    gathered.sent()
    grad_sum.sent()
    for ring in rings:
        ring.finish()
    for copy in stores:
        copy.wait()


def spread(blocks, count):
    return -(-blocks // count) * count


def feed_forward(x, low, full_out, my_gate, my_up, my_down, all_g, gain, units, wide):
    group, count = lax.axis_size("fsdp"), lax.axis_size("ctx")
    rows, width = x.shape
    hidden = my_gate.shape[1]
    blocks = spread(hidden // LANES * (width // group // 16), wide_split(width) * count)
    chips = group // 2
    dma = pltpu.SemaphoreType.DMA((2 * chips - 1,))
    bf16 = jnp.bfloat16
    down_chunks = [(per, 16, width) for per in down_split(hidden // 16, count)]
    return pl.pallas_call(
        ffn_kernel,
        out_shape=[
            jax.ShapeDtypeStruct((rows, width), jnp.float32),
            jax.ShapeDtypeStruct((rows, width), jnp.float32),
            jax.ShapeDtypeStruct((rows, width), bf16),
            jax.ShapeDtypeStruct((units, 2 * HD, wide), bf16),
            jax.ShapeDtypeStruct((group, blocks, 16, LANES), bf16),
            jax.ShapeDtypeStruct((group, blocks, 16, LANES), bf16),
            jax.ShapeDtypeStruct((group, rows, width), bf16),
            *[jax.ShapeDtypeStruct(chunk, bf16) for chunk in down_chunks],
            jax.ShapeDtypeStruct((1, width), jnp.float32),
        ],
        in_specs=[VMEM] * 4 + [ANY] * 4,
        out_specs=[VMEM] * 4 + [ANY] * 3 + [VMEM] * (1 + len(down_chunks)),
        scratch_shapes=[
            pltpu.VMEM((group, rows, width), bf16),
            pltpu.VMEM((width, group * rows), bf16),
            pltpu.VMEM((hidden, group * rows), bf16),
            pltpu.VMEM((group, rows, hidden), bf16),
            pltpu.VMEM((group, rows, hidden), bf16),
            pltpu.VMEM((group, rows, hidden), bf16),
            pltpu.VMEM((rows, width), jnp.float32),
            pltpu.VMEM((rows, width), jnp.float32),
            *[kind for chunk in down_chunks for kind in ring_scratch(chunk)],
            *scatter_scratch(rows, width),
            *[dma] * 4,
            pltpu.VMEM(my_gate.shape, bf16),
            pltpu.VMEM(my_up.shape, bf16),
            pltpu.VMEM(my_down.shape, bf16),
            pltpu.VMEM(all_g.shape, bf16),
            pltpu.VMEM((group, blocks, 16, LANES), bf16),
            pltpu.VMEM((group, blocks, 16, LANES), bf16),
            pltpu.VMEM((group, rows, width), bf16),
            pltpu.SemaphoreType.DMA((7,)),
            *[kind for _ in down_chunks for kind in ring_semaphores()],
        ],
        compiler_params=pltpu.CompilerParams(
            collective_id=2, has_side_effects=True, vmem_limit_bytes=60 << 20
        ),
    )(x, low, full_out, gain, my_gate, my_up, my_down, all_g)


def back_kernel(
    down_blocks, q_ref, g_ref, log_ref, gain_grad_ref, gain_ref, cos_ref, sin_ref,
    pairs_ref, mix_in, gate_ref, up_ref, layer_base_in, layer_part_ref, branch_ref, low_t_ref,
    normed_t_ref, w_query_in, w_key_in, w_value_in, x_in, resid_grad_in, *rest,
):
    taken = iter(rest)

    def take(number):
        return [next(taken) for _ in range(number)]

    halves, downs = wide_split(x_in.shape[1]), len(down_blocks)
    down_refs = take(downs)
    tokens_ref, layer_ref = take(2)
    wide_totals, down_totals = take(2 * halves), take(downs)
    out_a_total, out_b_total, rest_a_total, rest_b_total = take(4)
    peer_got, chain_got, layer_sib, layer_cross, layer_far = take(5)
    kv_ref, stage_ref, final_ref, qg_ref, delta_ref, grad_q_ref = take(6)
    wide_scratch = take(4 * halves)
    out_a_work, out_a_land, out_b_work, out_b_land = take(4)
    rest_a_work, rest_a_land, rest_b_work, rest_b_land = take(4)
    low_all, normed_all, branch_all, query_all, pair_all, upstream_ref, gain_give, gain_got = take(8)
    far_ref, layer_stage = take(2)
    mix_ref, layer_base_ref, w_query_ref, w_key_ref, w_value_ref, x_ref, resid_grad_ref = take(7)
    steps = Steps()
    fsdp, ctx, group, count = steps.fsdp, steps.ctx, lax.axis_size("fsdp"), lax.axis_size("ctx")
    units, deep, wide = q_ref.shape
    keys = pairs_ref.shape[2]
    rows, width = x_ref.shape
    own = width // group
    wide_rings = [
        Ring(*wide_scratch[2 * at : 2 * at + 2], wide_totals[at], take(5), at < halves, True)
        for at in range(2 * halves)
    ]
    down_rings = [SpreadRing(total, take(2), at % 2 == 0) for at, total in enumerate(down_totals)]
    out_a = Ring(out_a_work, out_a_land, out_a_total, take(2), True)
    out_b = Ring(out_b_work, out_b_land, out_b_total, take(2), False)
    layer_sum = GroupScatter(
        None,
        layer_sib,
        lambda step: layer_part_ref.at[
            2 * lax.rem(lax.div(fsdp, 2) + group // 2 - step, group // 2) + 1 - lax.rem(fsdp, 2)
        ],
        layer_cross,
        far_ref,
        layer_far,
        *take(2),
    )
    layer_sum.give_sib = layer_part_ref.at[layer_sum.sibling]
    rest_a = Ring(rest_a_work, rest_a_land, rest_a_total, take(2), True)
    rest_b = Ring(rest_b_work, rest_b_land, rest_b_total, take(2), False)
    first_rings = []
    for at in range(halves):
        first_rings += [wide_rings[at], wide_rings[halves + at]]
        first_rings += down_rings[at * downs // halves : (at + 1) * downs // halves]
    begun_rings = len(first_rings)
    first_rings += [out_a, out_b]
    peer_sends, peer_arrivals, chain_sends, chain_arrivals = take(4)
    branch_gather = GroupGather(lambda shard: branch_all.at[shard], *take(2))
    query_gather = GroupGather(lambda shard: query_all.at[shard], *take(2))
    pair_gather = GroupGather(lambda shard: pair_all.at[shard], *take(2))
    low_sends, low_arrivals, normed_sends, normed_arrivals, gain_sends, gain_arrivals = take(6)
    local_sems, stage_sems = take(2)

    barrier = pltpu.get_barrier_semaphore()
    greeted = steps.greet(barrier) + greet_group(barrier) + 2
    for device in (out_a.after, out_b.after):
        pl.semaphore_signal(barrier, inc=1, device_id=device, device_id_type=MESH)

    loads = []

    def load(source, target):
        copy = pltpu.make_async_copy(source, target, local_sems.at[len(loads)])
        copy.start()
        loads.append(copy)

    n = wide_scratch[0].shape[2]
    for at, ring in enumerate(wide_rings):
        source = (gate_ref, up_ref)[at // halves]
        for chunk in range(count):
            load(source.at[:, pl.ds((at % halves * count + chunk) * n, n)], ring.work.at[chunk])
    for ring, source in zip(down_rings, down_refs):
        load(source, ring.chunk(ring.total, ring.first))
    ring_loads = len(loads)
    load(pairs_ref, kv_ref)
    load(mix_in, mix_ref)
    load(branch_ref, branch_all.at[fsdp])
    load(low_t_ref.at[pl.ds(fsdp * own, own)], low_all.at[:, lane_tile(fsdp, rows)])
    load(normed_t_ref.at[pl.ds(fsdp * own, own)], normed_all.at[:, lane_tile(fsdp, rows)])
    slot_loads = len(loads)
    for source, target in (
        (layer_base_in, layer_base_ref),
        (w_query_in, w_query_ref),
        (w_key_in, w_key_ref),
        (w_value_in, w_value_ref),
        (x_in, x_ref),
        (resid_grad_in, resid_grad_ref),
    ):
        load(source, target)
    for copy in loads[:ring_loads]:
        copy.wait()
    pl.semaphore_wait(barrier, greeted)
    for ring in first_rings[:begun_rings]:
        ring.start()
    branch_gather.start(branch_ref)
    layer_sum.to_sibling().start()
    for step in range(1, group // 2):
        layer_sum.to_cross(step).start()

    def slices(source, target, sends, arrivals, step):
        peer = lax.rem(fsdp + step, group)
        return pltpu.make_async_remote_copy(
            src_ref=source.at[pl.ds(peer * own, own)],
            dst_ref=target.at[:, lane_tile(fsdp, rows)],
            send_sem=sends.at[step - 1],
            recv_sem=arrivals.at[step - 1],
            device_id=(peer, ctx),
            device_id_type=MESH,
        )

    turned = [
        slices(*ends, step)
        for ends in (
            (low_t_ref, low_all, low_sends, low_arrivals),
            (normed_t_ref, normed_all, normed_sends, normed_arrivals),
        )
        for step in range(1, group)
    ]
    for copy in turned:
        copy.start()

    def prepare(unit):
        q, g = q_ref[unit], g_ref[unit]
        qg_ref[unit, :wide] = q.T
        qg_ref[unit, wide:] = g.T
        delta_ref[unit] = jnp.sum(
            g[HD:].astype(jnp.float32) * mix_ref[unit], axis=0, keepdims=True
        )
        grad_q_ref[unit] = jnp.zeros((HD, wide), jnp.float32)

    for copy in loads[ring_loads:slot_loads]:
        copy.wait()
    tiles(units, prepare)

    def tick(ring, at):
        @pl.when(jnp.logical_and(at >= 0, at < ring.ticks))
        def _():
            ring.tick(jnp.clip(at, 0, ring.ticks - 1))

    late = steps.levels // 2 + 1

    def pump(at):
        lag = [0] * begun_rings + [late, late]
        for turn, ring in enumerate(first_rings):

            @pl.when(lax.rem(at, len(first_rings)) == turn)
            def _():
                tick(ring, lax.div(at, len(first_rings)) - lag[turn])

    def back(unit, first, blocks, diagonal):
        kv = kv_ref[pl.ds(first, blocks), unit].reshape(blocks * keys, deep)
        scores = jnp.dot(kv, q_ref[unit], preferred_element_type=jnp.float32)
        probs = jnp.exp(scores - log_ref[unit])
        if diagonal:
            probs = jnp.where(causal(keys, wide, scores.shape), probs, 0.0)
        grad_probs = jnp.dot(kv, g_ref[unit], preferred_element_type=jnp.float32)
        grad_scores = (probs * (grad_probs - delta_ref[unit])).astype(jnp.bfloat16)
        both = jnp.concatenate([grad_scores, probs.astype(jnp.bfloat16)], axis=1)
        grad_kv = jnp.dot(both, qg_ref[unit], preferred_element_type=jnp.float32)
        added = jnp.dot(kv.T, grad_scores, preferred_element_type=jnp.float32)
        grad_q_ref[unit] = grad_q_ref[unit] + added[:HD]
        kv_ref[pl.ds(first, blocks), unit] = grad_kv.astype(kv_ref.dtype).reshape(
            blocks, keys, deep
        )

    def across(pair):
        return pltpu.make_async_remote_copy(
            src_ref=kv_ref.at[2 * pair + 1 - steps.side],
            dst_ref=peer_got.at[pair],
            send_sem=peer_sends.at[pair],
            recv_sem=peer_arrivals.at[pair],
            device_id=steps.peer,
            device_id_type=MESH,
        )

    def down_chain(pair):
        return pltpu.make_async_remote_copy(
            src_ref=kv_ref.at[2 * pair + steps.side],
            dst_ref=chain_got.at[pair],
            send_sem=chain_sends.at[pair],
            recv_sem=chain_arrivals.at[pair],
            device_id=steps.below,
            device_id_type=MESH,
        )

    def combine(time):
        pair = time - steps.levels + steps.level

        @pl.when(jnp.logical_and(pair >= 0, pair <= steps.level))
        def _():
            for slot, expected, arrival, source in (
                (0, jnp.logical_or(pair < steps.level, steps.side == 0), across, peer_got),
                (1, steps.has_above, down_chain, chain_got),
            ):

                @pl.when(expected)
                def _():
                    arrival(pair).wait_recv()
                    copy = pltpu.make_async_copy(
                        source.at[pair], stage_ref.at[slot], stage_sems.at[slot]
                    )
                    copy.start()
                    copy.wait()

                @pl.when(jnp.logical_not(expected))
                def _():
                    stage_ref[slot] = jnp.zeros(stage_ref.shape[1:], stage_ref.dtype)

            def add(unit):
                final_ref[unit] = (
                    kv_ref[2 * pair + steps.side, unit].astype(jnp.float32)
                    + stage_ref[0, unit].astype(jnp.float32)
                    + stage_ref[1, unit].astype(jnp.float32)
                )

            tiles(units, add)

            @pl.when(pair < steps.level)
            def _():
                kv_ref[2 * pair + steps.side] = final_ref[...].astype(kv_ref.dtype)
                down_chain(pair).start()

    row_blocks = own // 16

    def weight_grad(left, right, begin, end, target, first, loop):
        span = LANES * next(n for n in (3, 2, 1) if (end - begin) % (n * LANES) == 0)

        def body(at):
            columns = pl.ds(pl.multiple_of(begin + at * span, LANES), span)
            part = forward_dot(
                left[...], right[:, :, columns].reshape(group * rows, span)
            ).astype(jnp.bfloat16)
            for block in range(span // LANES):
                here = first + (at * (span // LANES) + block) * row_blocks
                target[pl.ds(here, row_blocks)] = part[
                    :, block * LANES : (block + 1) * LANES
                ].reshape(row_blocks, 16, LANES)

        loop((end - begin) // span, body)
        return first + (end - begin) // LANES * row_blocks

    def clear_from(target, first):
        for spare in range(first, target.shape[0]):
            target[spare] = jnp.zeros((16, LANES), jnp.bfloat16)

    def out_grad():
        for copy in turned[: group - 1]:
            copy.wait_recv()
        branch_gather.forward()
        branch_gather.sibling_here()
        for step in range(1, branch_gather.chips):
            branch_gather.crossed(step)
        split = out_split(width)
        clear_from(out_a_work, weight_grad(low_all, branch_all, 0, split, out_a_work, 0, tiles))
        clear_from(out_b_work, weight_grad(low_all, branch_all, split, width, out_b_work, 0, tiles))
        out_a.start()
        out_b.start()

    turns = units // 2
    rings = max(turns, len(first_rings))

    def slot(pair):
        def turn(at):
            @pl.when(jnp.logical_and(pair < steps.level, at < turns))
            def _():
                for unit in (2 * at, 2 * at + 1):
                    back(unit, 2 * pair, 2, False)

            @pl.when(jnp.logical_and(pair == steps.level, at < turns))
            def _():
                for unit in (2 * at, 2 * at + 1):
                    back(unit, ctx, 1, True)

            @pl.when((pair == steps.level) & (steps.side == 1) & (at < turns))
            def _():
                for unit in (2 * at, 2 * at + 1):
                    back(unit, ctx - 1, 1, False)

            pump(pair * rings + at)

        tiles(rings, turn)

        @pl.when(jnp.logical_or(pair < steps.level, (pair == steps.level) & (steps.side == 1)))
        def _():
            across(pair).start()

        combine(pair)

        @pl.when(pair == late - 1)
        def _():
            out_grad()

    tiles(steps.levels, slot)
    pumped = [steps.levels * rings]

    def pump_next(times=1):
        def body(at, unused, begin=pumped[0]):
            pump(begin + at)
            return unused

        lax.fori_loop(0, times, body, 0)
        pumped[0] += times

    def pumping(times, body):
        begin = pumped[0]

        def step(at):
            body(at)
            tiles(2, lambda more: pump(begin + 2 * at + more))

        tiles(times, step)
        pumped[0] += 2 * times

    cosine, sine = cos_ref[...], sin_ref[...]

    def unturn(columns):
        first, second = columns[: HD // 2], columns[HD // 2 :]
        return jnp.concatenate(
            [first * cosine + second * sine, second * cosine - first * sine], axis=0
        )

    sequences = units // KVH
    groups = wide // keys
    begin = pumped[0]

    def query_rows(sequence):
        span = pl.ds(pl.multiple_of(sequence * keys, LANES), keys)
        for pair in range(H // 2):
            heads = []
            for head in (2 * pair, 2 * pair + 1):
                unit, member = sequence * KVH + head // groups, head % groups
                part = grad_q_ref[unit, :, member * keys : (member + 1) * keys]
                heads.append(unturn(part * HD ** (-0.5)))
            query_all[fsdp, span, pair * 2 * HD : (pair + 1) * 2 * HD] = (
                jnp.concatenate(heads, axis=0).astype(jnp.bfloat16).T
            )
        tiles(3, lambda more: pump(begin + 3 * sequence + more))

    tiles(sequences, query_rows)
    pumped[0] += 3 * sequences
    query_gather.start(query_all.at[fsdp])
    combine(steps.levels)
    kv_width = KVH * HD
    def pair_rows(sequence):
        span = pl.ds(pl.multiple_of(sequence * keys, LANES), keys)
        for pair in range(KVH // 2):
            turned_keys, turned_values = [], []
            for unit in (sequence * KVH + 2 * pair, sequence * KVH + 2 * pair + 1):
                part = final_ref[unit].T
                turned_keys.append(unturn(part[:HD]))
                turned_values.append(part[HD:])
            for start, parts in ((0, turned_keys), (kv_width, turned_values)):
                pair_all[fsdp, span, start + pair * 2 * HD : start + (pair + 1) * 2 * HD] = (
                    jnp.concatenate(parts, axis=0).astype(jnp.bfloat16).T
                )
    tiles(sequences, pair_rows)
    pair_gather.start(pair_all.at[fsdp])
    pump_next(2)
    query_gather.forward()
    step_out = width_tile(width)

    def upstream_tile(at):
        columns = pl.ds(pl.multiple_of(at * step_out, LANES), step_out)
        upstream_ref[:, columns] = (
            dot_columns(query_all[fsdp], w_query_ref[columns, :])
            + dot_columns(pair_all[fsdp, :, :kv_width], w_key_ref[columns, :])
            + dot_columns(pair_all[fsdp, :, kv_width:], w_value_ref[columns, :])
        )

    for copy in loads[slot_loads:]:
        copy.wait()
    pumping(width // step_out, upstream_tile)
    inputs = x_ref[...].astype(jnp.float32)
    scale = norm_scale(inputs)
    upstream = upstream_ref[...]
    scaled = upstream * gain_ref[...]
    tokens_ref[...] = (
        resid_grad_ref[...]
        + scale * scaled
        - inputs * scale**3 * jnp.mean(scaled * inputs, axis=-1, keepdims=True)
    )
    gain_attn = jnp.sum(upstream * inputs * scale, axis=0, keepdims=True)
    lanes = width // LANES
    gain_give[...] = jnp.zeros(gain_give.shape, jnp.float32)
    for block in range(lanes):
        columns = slice(block * LANES, (block + 1) * LANES)
        gain_give[block : block + 1, :] = gain_attn[:, columns]
        gain_give[lanes + block : lanes + block + 1, :] = gain_grad_ref[:, columns]

    def gain_copy(step):
        peer = lax.rem(fsdp + step, group)
        return pltpu.make_async_remote_copy(
            src_ref=gain_give,
            dst_ref=gain_got.at[step - 1],
            send_sem=gain_sends.at[step - 1],
            recv_sem=gain_arrivals.at[step - 1],
            device_id=(peer, ctx),
            device_id_type=MESH,
        )

    for step in range(1, group):
        gain_copy(step).start()
    pump_next()
    for copy in turned[group - 1 :]:
        copy.wait_recv()
    query_gather.sibling_here()
    for step in range(1, query_gather.chips):
        query_gather.crossed(step)
    split = query_split(width)
    filled_a = weight_grad(normed_all, query_all, 0, split, rest_a_work, 0, pumping)
    filled_b = weight_grad(normed_all, query_all, split, width, rest_b_work, 0, pumping)
    pair_gather.forward()
    pump_next()
    pair_gather.sibling_here()
    for step in range(1, pair_gather.chips):
        pair_gather.crossed(step)
    filled_b = weight_grad(normed_all, pair_all, 0, 2 * kv_width, rest_b_work, filled_b, pumping)
    for step in range(1, layer_sum.chips):
        ours = layer_part_ref.at[2 * lax.rem(layer_sum.chip + layer_sum.chips - step, layer_sum.chips) + layer_sum.core]
        for source, target in ((ours, far_ref.at[step - 1]), (layer_cross.at[step - 1], layer_stage)):
            if source is not ours:
                layer_sum.to_cross(step).wait_recv()
            copy = pltpu.make_async_copy(source, target, stage_sems.at[0])
            copy.start()
            copy.wait()
        far_ref[step - 1] = (
            far_ref[step - 1].astype(jnp.float32) + layer_stage[...].astype(jnp.float32)
        ).astype(jnp.bfloat16)
        layer_sum.to_far(step).start()
    gains = gain_give[...]
    for step in range(1, group):
        gain_copy(step).wait_recv()
        gains = gains + gain_got[step - 1]
    gain_tiles = gains.shape[0] // 16
    rest_a_work[filled_a : filled_a + gain_tiles] = gains.astype(jnp.bfloat16).reshape(
        gain_tiles, 16, LANES
    )
    clear_from(rest_a_work, filled_a + gain_tiles)
    clear_from(rest_b_work, filled_b)
    rest_a.start()
    rest_b.start()
    begun = pumped[0]
    total_pumps = max(wide_rings[0].ticks, late + out_a.ticks) * len(first_rings)

    half = -(-(total_pumps - begun) // rest_a.ticks)

    def layer_close():
        layer_sum.to_sibling().wait_recv()
        arrived = [layer_sib]
        for step in range(1, layer_sum.chips):
            layer_sum.to_far(step).wait_recv()
            arrived.append(layer_far.at[step - 1])
        for source in arrived:
            copy = pltpu.make_async_copy(source, layer_stage, stage_sems.at[0])
            copy.start()
            copy.wait()

            def add(at):
                block = pl.ds(pl.multiple_of(at * 32, 32), 32)
                layer_base_ref[block] = layer_base_ref[block] + layer_stage[block].astype(
                    jnp.float32
                )

            tiles(rows // 32, add)

        def close(at):
            block = pl.ds(pl.multiple_of(at * 32, 32), 32)
            layer_ref[block] = layer_base_ref[block].astype(jnp.bfloat16)

        tiles(rows // 32, close)

    def last_ticks(at, unused):
        tiles(half, lambda turn: pump(jnp.minimum(begun + half * at + turn, total_pumps)))
        tick(rest_a, at)
        tick(rest_b, at)

        @pl.when(at == rest_a.ticks * 3 // 4)
        def _():
            layer_close()

        return unused

    lax.fori_loop(0, rest_a.ticks, last_ticks, 0)
    layer_sum.sent()
    for ring in first_rings + [rest_a, rest_b]:
        ring.finish()
    for copy in turned:
        copy.wait_send()
    for gather in (branch_gather, query_gather, pair_gather):
        gather.sent()
    for step in range(1, group):
        gain_copy(step).wait_send()

    def sent(pair):
        @pl.when(jnp.logical_or(pair < steps.level, steps.side == 1))
        def _():
            across(pair).wait_send()

        @pl.when(pair < steps.level)
        def _():
            down_chain(pair).wait_send()

    tiles(steps.level + 1, sent)


def layer_back(
    q_wide, g_wide, log_total, gain_grad, gain, cosine, sine, all_pairs, mix, gate_part, up_part,
    layer_base, layer_parts, branch, low_t, normed_t, w_query, w_key, w_value, x, resid_grad, downs,
):
    group, count = lax.axis_size("fsdp"), lax.axis_size("ctx")
    units, deep, wide = q_wide.shape
    keys = all_pairs.shape[2]
    rows, width = x.shape
    own, kv_width = width // group, w_key.shape[1]
    bf16, f32 = jnp.bfloat16, jnp.float32
    dma = pltpu.SemaphoreType.DMA
    halves = wide_split(width)
    wide_chunk = (group, gate_part.shape[1] // (halves * count), 16, LANES)
    gain_rows = spread(2 * (width // LANES), 16)
    split, row_blocks = query_split(width), own // 16
    out_first = out_split(width)
    chips = group // 2
    small_chunks = [
        (spread(held, count) // count, 16, LANES)
        for held in (
            out_first // LANES * row_blocks,
            (width - out_first) // LANES * row_blocks,
            split // LANES * row_blocks + gain_rows // 16,
            (width - split + 2 * kv_width) // LANES * row_blocks,
        )
    ]
    levels = count // 2
    loaded = [mix, layer_base, w_query, w_key, w_value, x, resid_grad]
    return pl.pallas_call(
        functools.partial(back_kernel, [part.shape[0] for part in downs]),
        out_shape=[
            jax.ShapeDtypeStruct((rows, width), f32),
            jax.ShapeDtypeStruct((rows, width), bf16),
            *[ring_total(wide_chunk, True)] * (2 * halves),
            *[ring_total(part.shape) for part in downs],
            *[ring_total(chunk) for chunk in small_chunks],
            *[jax.ShapeDtypeStruct((levels, units, keys, deep), bf16)] * 2,
            jax.ShapeDtypeStruct((rows, width), bf16),
            *[jax.ShapeDtypeStruct((chips - 1, rows, width), bf16)] * 2,
        ],
        in_specs=[VMEM] * 7 + [ANY] * (14 + len(downs)),
        out_specs=[VMEM] * (6 + 2 * halves + len(downs)) + [ANY] * 5,
        scratch_shapes=[
            pltpu.VMEM(all_pairs.shape, bf16),
            pltpu.VMEM((2, units, keys, deep), bf16),
            pltpu.VMEM((units, keys, deep), f32),
            pltpu.VMEM((units, 2 * wide, deep), bf16),
            pltpu.VMEM((units, 1, wide), f32),
            pltpu.VMEM((units, HD, wide), f32),
            *[kind for _ in range(2 * halves) for kind in ring_scratch(wide_chunk, True)],
            *[kind for chunk in small_chunks for kind in ring_scratch(chunk)],
            pltpu.VMEM((own, group * rows), bf16),
            pltpu.VMEM((own, group * rows), bf16),
            pltpu.VMEM((group, rows, width), bf16),
            pltpu.VMEM((group, rows, width), bf16),
            pltpu.VMEM((group, rows, 2 * kv_width), bf16),
            pltpu.VMEM((rows, width), f32),
            pltpu.VMEM((gain_rows, LANES), f32),
            pltpu.VMEM((group - 1, gain_rows, LANES), f32),
            pltpu.VMEM((chips - 1, rows, width), bf16),
            pltpu.VMEM((rows, width), bf16),
            *[pltpu.VMEM(array.shape, array.dtype) for array in loaded],
            *[kind for _ in range(2 * halves) for kind in ring_semaphores(True)],
            *[kind for _ in range(len(downs) + 2) for kind in ring_semaphores()],
            *[dma((group - 1,))] * 2,
            *[kind for _ in range(2) for kind in ring_semaphores()],
            *[dma((levels,))] * 4,
            *[group_semaphores()] * 6,
            *[dma((group - 1,))] * 6,
            dma((11 + len(downs) + 2 * halves * count,)),
            dma((2,)),
        ],
        compiler_params=pltpu.CompilerParams(
            collective_id=3, has_side_effects=True, vmem_limit_bytes=62 << 20
        ),
    )(
        q_wide, g_wide, log_total, gain_grad, gain, cosine, sine, all_pairs, mix, gate_part, up_part,
        layer_base, layer_parts, branch, low_t, normed_t, w_query, w_key, w_value, x, resid_grad,
        *downs,
    )


def finish_kernel(halves, downs, *refs):
    taken = iter(refs)

    def take(number):
        return [next(taken) for _ in range(number)]

    wides, down_refs, smalls, (rows_ref,) = take(2 * halves), take(downs), take(4), take(1)
    outs, (tokens_ref,) = take(7), take(1)
    wide_held, down_held, small_held = take(2 * halves), take(downs), take(4)
    made, (load_sems, store_sems) = take(7), take(2)
    sources = [*wides, *down_refs, *smalls]
    held = [*wide_held, *down_held, *small_held]
    loads = {}
    for at, (source, target) in enumerate(zip(sources, held)):
        loads[id(target)] = pltpu.make_async_copy(source, target, load_sems.at[at])
        loads[id(target)].start()
    stores = []

    def store(index, columns=None):
        source, target = made[index], outs[index]
        if columns is not None:
            source, target = source.at[:, columns], target.at[:, columns]
        copy = pltpu.make_async_copy(source, target, store_sems.at[len(stores)])
        copy.start()
        stores.append(copy)

    rows = made[4].shape[0]
    row_blocks = rows // 16
    group = wides[0].shape[1]

    def unpack(source, first, index, begin, end):
        target = made[index]
        for block in range(begin, end):
            here = first + (block - begin) * row_blocks
            target[:, block * LANES : (block + 1) * LANES] = (
                source[here : here + row_blocks].reshape(rows, LANES).astype(jnp.float32)
            )
        return first + (end - begin) * row_blocks

    for index, parts in ((4, wide_held[:halves]), (5, wide_held[halves:])):
        for part in parts:
            loads[id(part)].wait()
        target = made[index]
        columns = target.shape[1] // group
        for owner in range(group):
            tile_rows = jnp.concatenate(
                [part[:, owner].reshape((-1,) + part.shape[3:]) for part in parts], axis=0
            )
            for block in range(columns // LANES):
                begin = owner * columns + block * LANES
                target[:, begin : begin + LANES] = (
                    tile_rows[block * row_blocks : (block + 1) * row_blocks]
                    .reshape(rows, LANES)
                    .astype(jnp.float32)
                )
            store(index, pl.ds(owner * columns, columns))
    down_grad = made[6]
    blocks, begin = down_grad.shape[0] // 16, 0
    for source in down_held:
        loads[id(source)].wait()
        end = min(blocks, begin + source.shape[0])
        if end > begin:
            down_grad[begin * 16 : end * 16, :] = (
                source[: end - begin]
                .reshape((end - begin) * 16, down_grad.shape[1])
                .astype(jnp.float32)
            )
        begin = end
    store(6)
    for part in small_held:
        loads[id(part)].wait()
    out_a, out_b, rest_a, rest_b = small_held
    lanes, kv_lanes = made[0].shape[1] // LANES, made[1].shape[1] // LANES
    middle, split = out_split(made[0].shape[1]) // LANES, query_split(made[0].shape[1]) // LANES
    unpack(out_a, 0, 3, 0, middle)
    unpack(out_b, 0, 3, middle, lanes)
    store(3)
    unpack(rest_a, 0, 0, 0, split)
    at = unpack(rest_b, 0, 0, split, lanes)
    store(0)
    at = unpack(rest_b, at, 1, 0, kv_lanes)
    store(1)
    unpack(rest_b, at, 2, 0, kv_lanes)
    store(2)
    keys = tokens_ref.shape[0]
    for sequence in range(tokens_ref.shape[1]):
        tokens_ref[:, sequence, :] = rows_ref[sequence * keys : (sequence + 1) * keys]
    for copy in stores:
        copy.wait()


def finish(wides, downs, smalls, token_rows, own, kv_width, hidden, sequences):
    rows, width = token_rows.shape
    f32 = jnp.float32
    outs = [
        jax.ShapeDtypeStruct((own, columns), f32)
        for columns in (width, kv_width, kv_width, width, FF, FF)
    ] + [jax.ShapeDtypeStruct((hidden, width), f32)]
    sources = [*wides, *downs, *smalls]
    dma = pltpu.SemaphoreType.DMA
    return pl.pallas_call(
        functools.partial(finish_kernel, len(wides) // 2, len(downs)),
        out_shape=outs + [jax.ShapeDtypeStruct((rows // sequences, sequences, width), f32)],
        in_specs=[ANY] * len(sources) + [VMEM],
        out_specs=[ANY] * len(outs) + [VMEM],
        scratch_shapes=[pltpu.VMEM(array.shape, array.dtype) for array in sources]
        + [pltpu.VMEM(out.shape, f32) for out in outs]
        + [dma((len(sources),)), dma((5 + 2 * wides[0].shape[1],))],
        compiler_params=pltpu.CompilerParams(vmem_limit_bytes=60 << 20),
    )(*sources, token_rows)


def on_device(
    tokens, w_query, w_key, w_value, w_out, w_gate, w_up, w_down, gain_attn, gain_ffn, cotangent
):
    block_len, seq_count, width = tokens.shape
    rows_count = block_len * seq_count
    kv_width = KVH * HD
    positions = lax.axis_index("ctx") * block_len + jnp.arange(block_len, dtype=jnp.int32)
    freqs = ROTARY_BASE ** (-2.0 * jnp.arange(HD // 2, dtype=jnp.float32) / HD)
    angles = freqs[:, None] * positions.astype(jnp.float32)[None, :]
    cosine, sine = jnp.cos(angles), jnp.sin(angles)
    x_rows = jnp.swapaxes(tokens, 0, 1).reshape(rows_count, width)
    g_rows = jnp.swapaxes(cotangent, 0, 1).reshape(rows_count, width)
    own = gain_attn.shape[0]
    units = seq_count * KVH
    wide = H // KVH * block_len
    own_gains = jnp.pad(
        jnp.stack([gain_attn, gain_ffn]).astype(jnp.float32), ((0, 6), (0, spread(own, LANES) - own))
    )
    (
        q_wide, normed_t, full_gain_attn, full_gain_ffn, full_query, full_key, full_value, attn_low, low_t, mix_unit, log_total,
        all_pairs, full_out, my_gate, my_up, all_g,
    ) = attend(
        x_rows, own_gains, cosine, sine, w_query, w_key, w_value, w_out, w_gate, w_up, g_rows, seq_count
    )
    layer_base, grad_resid, grad_branch, g_wide, gate_part, up_part, layer_parts, *downs = (
        feed_forward(
            x_rows, attn_low, full_out, my_gate, my_up, w_down, all_g, full_gain_ffn, units, wide
        )
    )
    downs, gain_term_ffn = downs[:-1], downs[-1]
    grad_tokens, layer_out, *sums = layer_back(
        q_wide, g_wide, log_total, gain_term_ffn, full_gain_attn, cosine, sine, all_pairs, mix_unit,
        gate_part, up_part, layer_base, layer_parts, grad_branch, low_t, normed_t, full_query,
        full_key, full_value, x_rows, grad_resid, downs,
    )
    wides, sums = sums[: 2 * wide_split(width)], sums[2 * wide_split(width) :]
    smalls = sums[len(downs) : len(downs) + 4]
    filled = query_split(width) // LANES * (own // 16)
    gain_grads = smalls[2][filled:].reshape(-1, LANES)[: 2 * (width // LANES)].reshape(2, width)
    gain_grads = lax.dynamic_slice_in_dim(gain_grads, lax.axis_index("fsdp") * own, own, 1)
    gain_grads = gain_grads.astype(jnp.float32)
    *grads, tokens_grad = finish(
        wides, sums[: len(downs)], smalls, grad_tokens, own, kv_width, w_down.shape[0], seq_count
    )
    return (
        jnp.swapaxes(layer_out.reshape(seq_count, block_len, width), 0, 1),
        tokens_grad,
        *grads,
        gain_grads[0],
        gain_grads[1],
    )


def solution(mesh):
    return jax.shard_map(
        on_device,
        mesh=mesh,
        in_specs=(
            P("ctx", "fsdp", None),
            P("fsdp", None),
            P("fsdp", None),
            P("fsdp", None),
            P("fsdp", None),
            P("fsdp", None),
            P("fsdp", None),
            P("fsdp", None),
            P("fsdp"),
            P("fsdp"),
            P("ctx", "fsdp", None),
        ),
        out_specs=(
            P("ctx", "fsdp", None),
            P("ctx", "fsdp", None),
            P("fsdp", None),
            P("fsdp", None),
            P("fsdp", None),
            P("fsdp", None),
            P("fsdp", None),
            P("fsdp", None),
            P("fsdp", None),
            P("fsdp"),
            P("fsdp"),
        ),
        check_vma=False,
    )
```

```python
import functools

import jax
import jax.numpy as jnp
from jax import lax
from jax.experimental import pallas as pl
from jax.experimental.pallas import tpu as pltpu
from jax.sharding import PartitionSpec as P

H = 18
KVH = 6
HD = 64
FF = 3072


EPSILON = 1e-05
ROTARY_BASE = 10000.0
MASKED_SCORE = -1e30


def norm_scale(rows):
    return lax.rsqrt(jnp.mean(rows * rows, axis=-1, keepdims=True) + EPSILON)


def forward_dot(left, right):
    return jnp.dot(left, right, preferred_element_type=jnp.float32)


MESH = pl.DeviceIdType.MESH
LANES = 128


def ring_place(ctx, fsdp, count):
    column, side = lax.div(ctx, 2), lax.rem(ctx, 2)
    place = column + side * (count - 1 - 2 * column)
    odd = lax.rem(fsdp, 2)
    return place + odd * (count - 1 - 2 * place)


def ring_ctx(place, fsdp, count):
    odd = lax.rem(fsdp, 2)
    place = place + odd * (count - 1 - 2 * place)
    late = lax.div(place, count // 2)
    return (1 - late) * 2 * place + late * (2 * (count - 1 - place) + 1)


class GroupGather:
    def __init__(self, shard_of, sends, arrivals):
        self.shard_of, self.sends, self.arrivals = shard_of, sends, arrivals
        self.fsdp, self.ctx = lax.axis_index("fsdp"), lax.axis_index("ctx")
        self.chips = lax.axis_size("fsdp") // 2
        self.chip, self.core = lax.div(self.fsdp, 2), lax.rem(self.fsdp, 2)
        self.sibling = 2 * self.chip + 1 - self.core

    def copy(self, source, shard, semaphore, device):
        return pltpu.make_async_remote_copy(
            src_ref=source,
            dst_ref=self.shard_of(shard),
            send_sem=self.sends.at[semaphore],
            recv_sem=self.arrivals.at[semaphore],
            device_id=(device, self.ctx),
            device_id_type=MESH,
        )

    def same_core(self, step):
        return 2 * lax.rem(self.chip + step, self.chips) + self.core

    def across(self, source):
        return self.copy(source, self.fsdp, 0, self.sibling)

    def out(self, source, step):
        return self.copy(source, self.fsdp, step, self.same_core(step))

    def onward(self, step):
        shard = self.same_core(self.chips - step)
        return self.copy(self.shard_of(shard), shard, self.chips - 1 + step, self.sibling)

    def start(self, source):
        for step in range(1, self.chips):
            self.out(source, step).start()
        self.across(source).start()

    def forward(self):
        own = self.shard_of(self.fsdp)
        for step in range(1, self.chips):
            self.out(own, step).wait_recv()
            self.onward(step).start()

    def sibling_here(self):
        self.across(self.shard_of(self.fsdp)).wait_recv()

    def crossed(self, step):
        self.onward(step).wait_recv()

    def sent(self):
        own = self.shard_of(self.fsdp)
        self.across(own).wait_send()
        for step in range(1, self.chips):
            self.out(own, step).wait_send()
            self.onward(step).wait_send()

    def finish(self):
        self.forward()
        self.sibling_here()
        for step in range(1, self.chips):
            self.crossed(step)
        self.sent()


class HalfGather:
    def __init__(self, held, own_rows, sends, arrivals):
        self.held, self.own = held, own_rows
        self.sends, self.arrivals = sends, arrivals
        self.fsdp, self.ctx = lax.axis_index("fsdp"), lax.axis_index("ctx")
        self.chips = lax.axis_size("fsdp") // 2
        self.chip, self.core = lax.div(self.fsdp, 2), lax.rem(self.fsdp, 2)
        self.sibling = 2 * self.chip + 1 - self.core
        self.side = lax.rem(self.ctx, 2)
        self.pair = self.ctx + 1 - 2 * self.side
        first = -(-own_rows // 32) * 16
        self.halves = ((0, first), (first, own_rows - first))

    def same_core(self, step):
        return 2 * lax.rem(self.chip + step, self.chips) + self.core

    def rows(self, shard, half=None):
        begin, size = (0, self.own) if half is None else self.halves[half]
        return self.held.at[pl.ds(shard * self.own + begin, size)]

    def copy(self, source, target, semaphore, device):
        return pltpu.make_async_remote_copy(
            src_ref=source,
            dst_ref=target,
            send_sem=self.sends.at[semaphore],
            recv_sem=self.arrivals.at[semaphore],
            device_id=device,
            device_id_type=MESH,
        )

    def on_side(self, body):
        for half in range(2):

            @pl.when(self.side == half)
            def _(half=half):
                body(half)

    def across(self, source):
        return self.copy(source, self.rows(self.fsdp), 0, (self.sibling, self.ctx))

    def out(self, source, step, half):
        begin, size = self.halves[half]
        return self.copy(
            source.at[pl.ds(begin, size)],
            self.rows(self.fsdp, half),
            step,
            (self.same_core(step), self.ctx),
        )

    def to_pair(self, step, half):
        part = self.rows(self.same_core(self.chips - step), half)
        return self.copy(part, part, self.chips - 1 + step, (self.fsdp, self.pair))

    def onward(self, step):
        part = self.rows(self.same_core(self.chips - step))
        return self.copy(part, part, 2 * self.chips - 2 + step, (self.sibling, self.ctx))

    def start(self, source):
        def send(half):
            for step in range(1, self.chips):
                self.out(source, step, half).start()

        self.on_side(send)
        self.across(source).start()

    def to_pairs(self):
        def forward(half):
            for step in range(1, self.chips):
                self.out(self.rows(self.fsdp), step, half).wait_recv()
                self.to_pair(step, half).start()

        self.on_side(forward)

    def to_sibling(self):
        def forward(half):
            for step in range(1, self.chips):
                self.to_pair(step, 1 - half).wait_recv()

        self.on_side(forward)
        for step in range(1, self.chips):
            self.onward(step).start()

    def arrived(self):
        self.across(self.rows(self.fsdp)).wait_recv()
        for step in range(1, self.chips):
            self.onward(step).wait_recv()

    def sent(self):
        def wait(half):
            for step in range(1, self.chips):
                self.out(self.rows(self.fsdp), step, half).wait_send()
                self.to_pair(step, half).wait_send()

        self.on_side(wait)
        self.across(self.rows(self.fsdp)).wait_send()
        for step in range(1, self.chips):
            self.onward(step).wait_send()


def half_semaphores(many):
    return pltpu.SemaphoreType.DMA((many, 3 * (lax.axis_size("fsdp") // 2) - 2))


def group_semaphores():
    return pltpu.SemaphoreType.DMA((lax.axis_size("fsdp") - 1,))


def greet_group(barrier):
    fsdp, ctx, group = lax.axis_index("fsdp"), lax.axis_index("ctx"), lax.axis_size("fsdp")
    for step in range(1, group):
        peer = lax.rem(fsdp + step, group)
        pl.semaphore_signal(barrier, inc=1, device_id=(peer, ctx), device_id_type=MESH)
    return group - 1


class Steps:
    def __init__(self):
        self.fsdp, self.ctx = lax.axis_index("fsdp"), lax.axis_index("ctx")
        self.levels = lax.axis_size("ctx") // 2
        self.level, self.side = lax.div(self.ctx, 2), lax.rem(self.ctx, 2)
        self.peer = (self.fsdp, 2 * self.level + 1 - self.side)
        self.above = (self.fsdp, lax.rem(self.ctx + 2, 2 * self.levels))
        self.below = (self.fsdp, lax.rem(self.ctx + 2 * self.levels - 2, 2 * self.levels))
        self.has_above = self.level + 1 < self.levels
        self.has_below = self.level > 0

    def greet(self, barrier):
        pl.semaphore_signal(barrier, inc=1, device_id=self.peer, device_id_type=MESH)

        @pl.when(self.has_above)
        def _():
            pl.semaphore_signal(barrier, inc=1, device_id=self.above, device_id_type=MESH)

        @pl.when(self.has_below)
        def _():
            pl.semaphore_signal(barrier, inc=1, device_id=self.below, device_id_type=MESH)

        return 1 + jnp.minimum(self.level, 1) + jnp.minimum(self.levels - 1 - self.level, 1)


PARTS = 2


def causal(keys, wide, shape):
    key_at = lax.broadcasted_iota(jnp.int32, shape, 0)
    query_at = lax.rem(lax.broadcasted_iota(jnp.int32, shape, 1), keys)
    return key_at <= query_at


def attend_kernel(
    token_ref, upstream_ref, gain_ref, cos_ref, sin_ref, query_ref, key_ref, value_ref, out_ref, gate_ref,
    up_ref, x_ref, q_ref, normed_t_ref, gain_attn_ref, gain_ffn_ref, full_query, full_key, full_value,
    low_ref, low_t_ref, mix_ref, log_ref, all_ref, full_out_ref, my_gate_ref, my_up_ref, all_g_ref,
    normed_ref, key_rows, gain_all, own_out, own_gate, own_up, own_g,
    top_ref, total_ref, chain_sends, chain_arrivals, peer_sends, peer_arrivals,
    half_sends, half_arrivals, gain_sends, gain_arrivals,
    out_sends, out_arrivals, g_sends, g_arrivals,
    part_sends, part_arrivals, local_sems,
):
    steps = Steps()
    fsdp, ctx, group = steps.fsdp, steps.ctx, lax.axis_size("fsdp")
    units, deep, wide = q_ref.shape
    keys = all_ref.shape[2]
    per_part = units // PARTS
    rows_count, width = x_ref.shape
    own = query_ref.shape[0]
    sequences, groups = units // KVH, H // KVH
    barrier = pltpu.get_barrier_semaphore()
    greeted = steps.greet(barrier) + greet_group(barrier)
    span = KVH * HD
    pieces = [(key_ref, full_key, 0), (value_ref, full_value, 0)]
    pieces += [(query_ref, full_query, start) for start in range(0, width, span)]
    gathers = []
    for at, (source, target, start) in enumerate(pieces):
        columns = pl.ds(start, span)
        gather = HalfGather(
            target.at[:, columns], own, half_sends.at[at], half_arrivals.at[at]
        )
        gathers.append((gather, source.at[:, columns]))
    own_rows = pl.ds(fsdp * own, own)
    own_copies = [
        pltpu.make_async_copy(source, target.at[own_rows], local_sems.at[4 + at])
        for at, (source, target) in enumerate(
            ((key_ref, full_key), (value_ref, full_value), (query_ref, full_query))
        )
    ]
    for copy in own_copies:
        copy.start()
    for sequence in range(sequences):
        x_ref[sequence * keys : (sequence + 1) * keys] = token_ref[:, sequence, :]
        own_g[sequence * keys : (sequence + 1) * keys] = upstream_ref[:, sequence, :]
    gain_all[fsdp] = gain_ref[...]
    pl.semaphore_wait(barrier, greeted)

    def gain_copy(step):
        peer = lax.rem(fsdp + step, group)
        return pltpu.make_async_remote_copy(
            src_ref=gain_ref,
            dst_ref=gain_all.at[fsdp],
            send_sem=gain_sends.at[step - 1],
            recv_sem=gain_arrivals.at[step - 1],
            device_id=(peer, ctx),
            device_id_type=MESH,
        )

    for step in range(1, group):
        gain_copy(step).start()
    for gather, source in gathers:
        gather.start(source)
    inputs = x_ref[...].astype(jnp.float32)
    scale = norm_scale(inputs)
    q_ref[:, HD:, :] = jnp.zeros((units, HD, wide), q_ref.dtype)
    for step in range(1, group):
        gain_copy(step).wait_recv()
    gains = jnp.concatenate([gain_all[shard][:, :own] for shard in range(group)], axis=1)
    gain_attn_ref[...] = gains[:1]
    gain_ffn_ref[...] = gains[1:2]
    normed_ref[...] = (inputs * scale * gains[:1]).astype(jnp.bfloat16)
    cosine, sine = cos_ref[...], sin_ref[...]

    def turn(columns):
        first, second = columns[: HD // 2], columns[HD // 2 :]
        return jnp.concatenate(
            [first * cosine - second * sine, second * cosine + first * sine], axis=0
        ).astype(jnp.bfloat16)

    def block_copy(level, part, side, semaphores, arrivals, arrives, device):
        block = 2 * (steps.level - level) + side
        held = all_ref.at[block, pl.ds(part * per_part, per_part)]
        return pltpu.make_async_remote_copy(
            src_ref=held,
            dst_ref=held,
            send_sem=semaphores.at[level, part],
            recv_sem=arrivals.at[arrives, part],
            device_id=device,
            device_id_type=MESH,
        )

    def chain(level, part):
        return block_copy(
            level, part, steps.side, chain_sends, chain_arrivals, level + 1, steps.above
        )

    def across(level, part):
        return block_copy(
            level, part, steps.side, peer_sends, peer_arrivals, level, steps.peer
        )

    def pass_on(level, part):
        @pl.when(steps.has_above)
        def _():
            chain(level, part).start()

    def project(at):
        _, weight, start = pieces[at]
        made = forward_dot(normed_ref[...], weight[:, start : start + span])
        if at == 0:
            key_rows[...] = made
            return
        for sequence in range(sequences):
            block = slice(sequence * keys, (sequence + 1) * keys)
            for pair in range(span // (2 * HD)):
                columns = slice(pair * 2 * HD, (pair + 1) * 2 * HD)
                turned = made[block, columns].T
                if at == 1:
                    turned_keys = key_rows[block, columns].T
                    for half in range(2):
                        held = slice(half * HD, (half + 1) * HD)
                        both = jnp.concatenate(
                            [turn(turned_keys[held]), turned[held].astype(jnp.bfloat16)], axis=0
                        )
                        all_ref[ctx, sequence * KVH + 2 * pair + half] = both.T
                else:
                    for half in range(2):
                        head = start // HD + 2 * pair + half
                        unit, member = sequence * KVH + head // groups, head % groups
                        part = turn(turned[half * HD : (half + 1) * HD])
                        q_ref[unit, :HD, member * keys : (member + 1) * keys] = part * jnp.bfloat16(
                            HD ** (-0.5)
                        )
        if at == 1:
            for part in range(PARTS):
                pass_on(0, part)

                @pl.when(steps.side == 0)
                def _():
                    across(0, part).start()

    columns = my_gate_ref.shape[1]
    gathered = HalfGather(full_out_ref, own, out_sends.at[0], out_arrivals.at[0])
    gathered_g = GroupGather(lambda shard: all_g_ref.at[shard], g_sends, g_arrivals)
    mine = lane_tile(fsdp, columns)
    own_parts = (
        (out_ref, own_out, full_out_ref.at[own_rows]),
        (gate_ref.at[:, mine], own_gate, my_gate_ref.at[own_rows]),
        (up_ref.at[:, mine], own_up, my_up_ref.at[own_rows]),
    )
    own_g_copy = pltpu.make_async_copy(own_g, all_g_ref.at[fsdp], local_sems.at[3])
    loads = [
        pltpu.make_async_copy(source, held, local_sems.at[at])
        for at, (source, held, _) in enumerate(own_parts)
    ]
    background = [
        pltpu.make_async_copy(held, target, local_sems.at[at])
        for at, (_, held, target) in enumerate(own_parts)
    ]
    slices = []
    for which, (source, target) in enumerate(((gate_ref, my_gate_ref), (up_ref, my_up_ref))):
        for step in range(1, group):
            peer = lax.rem(fsdp + step, group)
            slices.append(
                pltpu.make_async_remote_copy(
                    src_ref=source.at[:, lane_tile(peer, columns)],
                    dst_ref=target.at[own_rows],
                    send_sem=part_sends.at[which, step - 1],
                    recv_sem=part_arrivals.at[which, step - 1],
                    device_id=(peer, ctx),
                    device_id_type=MESH,
                )
            )

    def start_background():
        for copy in loads:
            copy.start()
        gathered.start(out_ref)
        for copy in slices:
            copy.start()
        gathered_g.start(own_g)
        own_g_copy.start()

    last = len(pieces)
    for at in range(last + 2):
        if at < last:
            gathers[at][0].to_pairs()
        if at == 0:
            start_background()
        if 1 <= at <= last:
            gathers[at - 1][0].to_sibling()
        if at == 1:
            for column in range(width // LANES):
                columns = slice(column * LANES, (column + 1) * LANES)
                normed_t_ref[columns, :] = normed_ref[:, columns].T
            for copy in own_copies:
                copy.wait()
        if at >= 2:
            gathers[at - 2][0].arrived()
            project(at - 2)

    def second_half():
        gathered.to_pairs()
        for load, copy in zip(loads, background):
            load.wait()
            copy.start()

    def add(unit, kv):
        scores = jnp.dot(kv, q_ref[unit], preferred_element_type=jnp.float32)
        top = top_ref[unit]
        new_top = jnp.maximum(top, jnp.max(scores, axis=0, keepdims=True))
        fade = jnp.exp(top - new_top)
        weights = jnp.exp(scores - new_top)
        top_ref[unit] = new_top
        total_ref[unit] = total_ref[unit] * fade + jnp.sum(weights, axis=0, keepdims=True)
        added = jnp.dot(kv.T, weights.astype(jnp.bfloat16), preferred_element_type=jnp.float32)
        mix_ref[unit] = mix_ref[unit] * fade + added[HD:]

    def over_units(body, first, count):
        def two(at, unused):
            body(first + 2 * at)
            body(first + 2 * at + 1)
            return unused

        lax.fori_loop(0, count // 2, two, 0)

    def diagonal(unit):
        kv = all_ref[ctx, unit]
        scores = jnp.dot(kv, q_ref[unit], preferred_element_type=jnp.float32)
        scores = jnp.where(causal(keys, wide, scores.shape), scores, MASKED_SCORE)
        top = jnp.max(scores, axis=0, keepdims=True)
        weights = jnp.exp(scores - top)
        top_ref[unit] = top
        total_ref[unit] = jnp.sum(weights, axis=0, keepdims=True)
        added = jnp.dot(kv.T, weights.astype(jnp.bfloat16), preferred_element_type=jnp.float32)
        mix_ref[unit] = added[HD:]

    over_units(diagonal, 0, units)

    def forward(level, part):
        chain(level - 1, part).wait_recv()
        pass_on(level, part)
        across(level, part).start()

    @pl.when(steps.level >= 1)
    def _():
        for part in range(PARTS):
            forward(1, part)

    @pl.when(steps.side == 1)
    def _():
        for part in range(PARTS):
            across(0, part).wait_recv()
            over_units(lambda unit: add(unit, all_ref[ctx - 1, unit]), part * per_part, per_part)

    def level_step(level, unused):
        first = 2 * (steps.level - level)
        for part in range(PARTS):

            @pl.when(level < steps.level)
            def _():
                forward(level + 1, part)

            across(level, part).wait_recv()
            over_units(
                lambda unit: add(unit, all_ref[pl.ds(first, 2), unit].reshape(2 * keys, deep)),
                part * per_part,
                per_part,
            )

        @pl.when(level == 1)
        def _():
            second_half()

        return unused

    @pl.when(steps.level == 0)
    def _():
        second_half()

    lax.fori_loop(1, steps.level + 1, level_step, 0)

    def close(unit):
        total = total_ref[unit]
        mix_ref[unit] = mix_ref[unit] / total
        log_ref[unit] = top_ref[unit] + jnp.log(total)

    over_units(close, 0, units)
    for sequence in range(sequences):
        for pair in range(H // 2):
            heads = []
            for head in (2 * pair, 2 * pair + 1):
                unit, member = sequence * KVH + head // groups, head % groups
                heads.append(mix_ref[unit, :, member * keys : (member + 1) * keys])
            tile = jnp.concatenate(heads, axis=0).astype(low_ref.dtype)
            block = slice(sequence * keys, (sequence + 1) * keys)
            columns = slice(pair * 2 * HD, (pair + 1) * 2 * HD)
            low_t_ref[columns, block] = tile
            low_ref[block, columns] = tile.T
    for gather, _ in gathers:
        gather.sent()
    for step in range(1, group):
        gain_copy(step).wait_send()
    gathered.to_sibling()
    gathered_g.forward()
    gathered.arrived()
    gathered.sent()
    gathered_g.sibling_here()
    for step in range(1, gathered_g.chips):
        gathered_g.crossed(step)
    gathered_g.sent()
    for copy in slices:
        copy.wait()
    own_g_copy.wait()
    for copy in background:
        copy.wait()

    def sent(level, unused):
        for part in range(PARTS):

            @pl.when(steps.has_above)
            def _():
                chain(level, part).wait_send()

            @pl.when(jnp.logical_or(level > 0, steps.side == 0))
            def _():
                across(level, part).wait_send()

        return unused

    lax.fori_loop(0, steps.level + 1, sent, 0)


ANY = pl.BlockSpec(memory_space=pl.ANY)
VMEM = pl.BlockSpec(memory_space=pltpu.VMEM)


def attend(tokens, upstream, gains, cosine, sine, w_query, w_key, w_value, w_out, w_gate, w_up):
    group, count = lax.axis_size("fsdp"), lax.axis_size("ctx")
    keys, sequences, width = tokens.shape
    own, hidden = w_query.shape[0], w_gate.shape[1] // group
    rows, units, deep = keys * sequences, sequences * KVH, 2 * HD
    wide = H // KVH * keys
    kv_width = KVH * HD
    dma = pltpu.SemaphoreType.DMA
    bf16, f32 = jnp.bfloat16, jnp.float32
    pieces = 2 + width // kv_width
    return pl.pallas_call(
        attend_kernel,
        out_shape=[
            jax.ShapeDtypeStruct((rows, width), bf16),
            jax.ShapeDtypeStruct((units, deep, wide), bf16),
            jax.ShapeDtypeStruct((width, rows), bf16),
            jax.ShapeDtypeStruct((1, width), f32),
            jax.ShapeDtypeStruct((1, width), f32),
            jax.ShapeDtypeStruct((width, width), bf16),
            jax.ShapeDtypeStruct((width, kv_width), bf16),
            jax.ShapeDtypeStruct((width, kv_width), bf16),
            jax.ShapeDtypeStruct((rows, width), bf16),
            jax.ShapeDtypeStruct((width, rows), bf16),
            jax.ShapeDtypeStruct((units, HD, wide), f32),
            jax.ShapeDtypeStruct((units, 1, wide), f32),
            jax.ShapeDtypeStruct((count, units, keys, deep), bf16),
            jax.ShapeDtypeStruct((width, width), bf16),
            jax.ShapeDtypeStruct((width, hidden), bf16),
            jax.ShapeDtypeStruct((width, hidden), bf16),
            jax.ShapeDtypeStruct((group, rows, width), bf16),
        ],
        in_specs=[VMEM] * 5 + [ANY] * 6,
        out_specs=[VMEM] * 13 + [ANY] * 4,
        scratch_shapes=[
            pltpu.VMEM((rows, width), bf16),
            pltpu.VMEM((rows, kv_width), f32),
            pltpu.VMEM((group,) + gains.shape, f32),
            pltpu.VMEM((own, width), bf16),
            pltpu.VMEM((own, hidden), bf16),
            pltpu.VMEM((own, hidden), bf16),
            pltpu.VMEM((rows, width), bf16),
            pltpu.VMEM((units, 1, wide), f32),
            pltpu.VMEM((units, 1, wide), f32),
            dma((count // 2, PARTS)),
            dma((count // 2 + 1, PARTS)),
            dma((count // 2, PARTS)),
            dma((count // 2, PARTS)),
            half_semaphores(pieces),
            half_semaphores(pieces),
            *[dma((group - 1,))] * 2,
            *[half_semaphores(1)] * 2,
            *[group_semaphores()] * 2,
            *[dma((2, group - 1))] * 2,
            dma((7,)),
        ],
        compiler_params=pltpu.CompilerParams(
            collective_id=1, has_side_effects=True, vmem_limit_bytes=60 << 20
        ),
    )(tokens, upstream, gains, cosine, sine, w_query, w_key, w_value, w_out, w_gate, w_up)


class Ring:
    def __init__(self, work, landing, total, semaphores, forward, exchange=False):
        self.fsdp, self.ctx = lax.axis_index("fsdp"), lax.axis_index("ctx")
        self.group, self.count = lax.axis_size("fsdp"), lax.axis_size("ctx")
        self.work, self.landing, self.total = work, landing, total
        self.sends, self.arrivals = semaphores[:2]
        self.part_sends, self.part_arrivals, self.own_sem = semaphores[2:] if exchange else (None,) * 3
        self.exchange = exchange
        side = 0 if forward else 1
        self.place = ring_place(self.ctx, side, self.count)
        self.after = (self.fsdp, ring_ctx(lax.rem(self.place + 1, self.count), side, self.count))
        self.ticks = 2 * self.count - 2 + int(exchange)

    def chunk(self, held, index):
        if self.exchange:
            return held.at[index]
        per = held.shape[0] // self.count
        return held.at[pl.ds(index * per, per)]

    def summing(self, step, index):
        return self.copy(self.chunk(self.work, index), self.landing.at[step], step)

    def handing(self, step, index):
        held = self.chunk(self.total, index)
        return self.copy(held, held, step)

    def copy(self, source, target, step):
        return pltpu.make_async_remote_copy(
            src_ref=source,
            dst_ref=target,
            send_sem=self.sends.at[step],
            recv_sem=self.arrivals.at[step],
            device_id=self.after,
            device_id_type=MESH,
        )

    def part(self, index, step):
        peer = lax.rem(self.fsdp + step, self.group)
        return pltpu.make_async_remote_copy(
            src_ref=self.work.at[index, peer],
            dst_ref=self.total.at[index, self.fsdp],
            send_sem=self.part_sends.at[step - 1],
            recv_sem=self.part_arrivals.at[step - 1],
            device_id=(peer, self.ctx),
            device_id_type=MESH,
        )

    def own_part(self, index):
        return pltpu.make_async_copy(
            self.work.at[index, self.fsdp], self.total.at[index, self.fsdp], self.own_sem
        )

    def start(self):
        self.summing(0, self.place).start()

    def tick(self, at):
        last = self.count - 2
        gap = int(self.exchange)
        step = at - gap * jnp.where(at > last, 1, 0) if self.exchange else at
        index = lax.rem(self.place + 3 * self.count - 1 - step, self.count)

        def add(target):
            part, landed = self.chunk(self.work, index), self.landing.at[jnp.minimum(at, last)]
            for row in range(part.shape[0]):
                target[row] = (
                    part[row].astype(jnp.float32) + landed[row].astype(jnp.float32)
                ).astype(part.dtype)

        @pl.when(at <= last)
        def _():
            self.summing(jnp.minimum(at, last), index).wait_recv()

        @pl.when(at < last)
        def _():
            add(self.chunk(self.work, index))
            self.summing(jnp.minimum(at + 1, last), index).start()

        if self.exchange:

            @pl.when(at == last)
            def _():
                add(self.chunk(self.work, index))
                for peer in range(1, self.group):
                    self.part(index, peer).start()
                self.own_part(index).start()

            @pl.when(at == last + 1)
            def _():
                done = lax.rem(self.place + 1, self.count)
                self.own_part(done).wait()
                for peer in range(1, self.group):
                    self.part(done, peer).wait_recv()
                self.handing(last + 1, done).start()

        else:

            @pl.when(at == last)
            def _():
                add(self.chunk(self.total, index))
                self.handing(last + 1, index).start()

        @pl.when(at > last + gap)
        def _():
            here = jnp.maximum(step, last + 1)
            self.handing(here, index).wait_recv()

            @pl.when(here < 2 * self.count - 3)
            def _():
                self.handing(jnp.minimum(here + 1, 2 * self.count - 3), index).start()

    def finish(self):
        def wait(step, unused):
            self.handing(step, self.place).wait_send()
            return unused

        lax.fori_loop(0, 2 * self.count - 2, wait, 0)
        if self.exchange:
            for peer in range(1, self.group):
                self.part(lax.rem(self.place + 1, self.count), peer).wait_send()


class SumRing(Ring):
    def __init__(self, *args):
        super().__init__(*args)
        self.ticks = self.count - 1

    def tick(self, at):
        last = self.count - 2
        index = lax.rem(self.place + 2 * self.count - 1 - at, self.count)
        self.summing(at, index).wait_recv()
        work, landed = self.chunk(self.work, index), self.landing.at[at]

        def add(target):
            for row in range(work.shape[0]):
                target[row] = (
                    work[row].astype(jnp.float32) + landed[row].astype(jnp.float32)
                ).astype(work.dtype)

        @pl.when(at < last)
        def _():
            add(work)
            self.summing(jnp.minimum(at + 1, last), index).start()

        @pl.when(at == last)
        def _():
            add(self.total)

    def finish(self):
        def wait(step, unused):
            self.summing(step, self.place).wait_send()
            return unused

        lax.fori_loop(0, self.ticks, wait, 0)


class SpreadRing(Ring):
    def __init__(self, total, semaphores, forward):
        super().__init__(None, None, total, semaphores, forward)
        self.ticks = self.count - 1
        self.first = lax.rem(self.place + 1, self.count)

    def start(self):
        self.handing(0, self.first).start()

    def tick(self, at):
        index = lax.rem(self.place + self.count - at, self.count)
        self.handing(at, index).wait_recv()

        @pl.when(at < self.count - 2)
        def _():
            self.handing(jnp.minimum(at + 1, self.count - 2), index).start()

    def finish(self):
        def wait(step, unused):
            self.handing(step, self.place).wait_send()
            return unused

        lax.fori_loop(0, self.ticks, wait, 0)


def ring_scratch(chunk, exchange=False):
    count = lax.axis_size("ctx")
    work = (count,) + chunk if exchange else (count * chunk[0],) + chunk[1:]
    return [pltpu.VMEM(work, jnp.bfloat16), pltpu.VMEM((count - 1,) + chunk, jnp.bfloat16)]


def ring_total(chunk, exchange=False):
    count = lax.axis_size("ctx")
    work = (count,) + chunk if exchange else (count * chunk[0],) + chunk[1:]
    return jax.ShapeDtypeStruct(work, jnp.bfloat16)


def ring_semaphores(exchange=False):
    dma, steps = pltpu.SemaphoreType.DMA, 2 * lax.axis_size("ctx") - 2
    parts = lax.axis_size("fsdp") - 1
    return [dma((steps,))] * 2 + ([dma((parts,))] * 2 + [dma] if exchange else [])


def wide_split(width):
    group, count = lax.axis_size("fsdp"), lax.axis_size("ctx")
    return 2 if FF // group // LANES * (width // group // 16) >= 4 * count else 1


def query_split(width):
    return width // LANES * 7 // 9 * LANES


def out_split(width):
    return (width // LANES + 1) // 2 * LANES


def down_split(blocks, count):
    each = -(-blocks // count)
    rings = 4 if each >= 4 else 2
    return [max(1, (each + at) // rings) for at in range(rings)]


class GroupScatter:
    def __init__(self, give_sib, got_sib, give_cross, got_cross, far, got_far, sends, arrivals):
        self.give_sib, self.got_sib = give_sib, got_sib
        self.give_cross, self.got_cross = give_cross, got_cross
        self.far, self.got_far = far, got_far
        self.sends, self.arrivals = sends, arrivals
        self.fsdp, self.ctx = lax.axis_index("fsdp"), lax.axis_index("ctx")
        self.chips = lax.axis_size("fsdp") // 2
        self.chip, self.core = lax.div(self.fsdp, 2), lax.rem(self.fsdp, 2)
        self.sibling = 2 * self.chip + 1 - self.core

    def copy(self, source, target, semaphore, device):
        return pltpu.make_async_remote_copy(
            src_ref=source,
            dst_ref=target,
            send_sem=self.sends.at[semaphore],
            recv_sem=self.arrivals.at[semaphore],
            device_id=(device, self.ctx),
            device_id_type=MESH,
        )

    def to_sibling(self):
        return self.copy(self.give_sib, self.got_sib, 0, self.sibling)

    def to_cross(self, step):
        return self.copy(
            self.give_cross(step), self.got_cross.at[step - 1], step, self.sibling
        )

    def to_far(self, step):
        chip = lax.rem(self.chip + self.chips - step, self.chips)
        return self.copy(
            self.far.at[step - 1],
            self.got_far.at[step - 1],
            self.chips - 1 + step,
            2 * chip + self.core,
        )

    def add_cross(self, step):
        self.to_cross(step).wait_recv()
        held = self.far.at[step - 1]
        held[...] = (
            held[...].astype(jnp.float32) + self.got_cross[step - 1].astype(jnp.float32)
        ).astype(held.dtype)
        self.to_far(step).start()

    def total(self, own):
        self.to_sibling().wait_recv()
        value = own + self.got_sib[...].astype(jnp.float32)
        for step in range(1, self.chips):
            self.to_far(step).wait_recv()
            value = value + self.got_far[step - 1].astype(jnp.float32)
        return value

    def sent(self):
        self.to_sibling().wait_send()
        for step in range(1, self.chips):
            self.to_cross(step).wait_send()
            self.to_far(step).wait_send()


def scatter_scratch(rows, width):
    far = lax.axis_size("fsdp") // 2 - 1
    one, many = (rows, width), (far, rows, width)
    return [pltpu.VMEM(shape, jnp.bfloat16) for shape in (one, one, many, many, many, many)]


def dot_columns(left, right):
    return lax.dot_general(
        left, right, (((1,), (1,)), ((), ())), preferred_element_type=jnp.float32
    )


def tiles(count, body):
    def step(at, unused):
        body(at)
        return unused

    lax.fori_loop(0, count, step, 0)


def lane_tile(at, size):
    return pl.ds(pl.multiple_of(at * size, LANES), size)


def width_tile(width):
    return 384 if width % 384 == 0 else width


def hidden_tile(hidden):
    return 256 if hidden % 256 == 0 else 128


def transpose_into(target, source):
    rows, columns = source.shape

    def body(at):
        part = source[:, lane_tile(at, LANES)]
        target[pl.ds(pl.multiple_of(at * LANES, LANES), LANES), :] = part.T

    tiles(columns // LANES, body)


def ffn_kernel(
    x_ref, low_ref, out_ref, gain_ref, gate_in, up_in, down_in, all_g_in,
    layer_ref, resid_grad_ref, branch_ref, g_wide_ref, gate_part_out, up_part_out, layer_part_out,
    *rest,
):
    downs = len(down_split(gate_in.shape[1] // 16, lax.axis_size("ctx")))
    taken = iter(rest)

    def take(number):
        return [next(taken) for _ in range(number)]

    down_done, (gain_grad_ref,) = take(downs), take(1)
    all_n_ref, turned_n, turned_act, act_ref, gate_grad, up_grad, resid_ref, grad_own = take(8)
    down_scratch = take(2 * downs)
    give_sib, got_sib, give_cross, got_cross, far, got_far = take(6)
    n_sends, n_arrivals, grad_sends, grad_arrivals = take(4)
    gate_ref, up_ref, down_ref, all_g_ref, gate_part_ref, up_part_ref, layer_part_ref = take(7)
    (local_sems,) = take(1)
    loads = [
        pltpu.make_async_copy(source, target, local_sems.at[at])
        for at, (source, target) in enumerate(
            ((gate_in, gate_ref), (up_in, up_ref), (all_g_in, all_g_ref), (down_in, down_ref))
        )
    ]
    for copy in loads:
        copy.start()
    stores = []

    def store(source, target):
        copy = pltpu.make_async_copy(source, target, local_sems.at[len(loads) + len(stores)])
        copy.start()
        stores.append(copy)

    rings = [
        SumRing(*down_scratch[2 * at : 2 * at + 2], down_done[at], take(2), at % 2 == 0)
        for at in range(downs)
    ]
    group = lax.axis_size("fsdp")
    rows, width = x_ref.shape
    hidden = gate_ref.shape[1]
    barrier = pltpu.get_barrier_semaphore()
    greeted = greet_group(barrier) + 2
    for ring in rings[:2]:
        pl.semaphore_signal(barrier, inc=1, device_id=ring.after, device_id_type=MESH)
    step_in, step_out = hidden_tile(hidden), width_tile(width)

    def branch(at):
        columns = lane_tile(at, step_out)
        resid_ref[:, columns] = x_ref[:, columns].astype(jnp.float32) + forward_dot(
            low_ref[...], out_ref[:, columns]
        )

    tiles(width // step_out, branch)
    gain = gain_ref[...]
    scale = norm_scale(resid_ref[...])
    gathered = GroupGather(lambda shard: all_n_ref.at[shard], n_sends, n_arrivals)
    fsdp, chips = gathered.fsdp, gathered.chips
    all_n_ref[fsdp] = (resid_ref[...] * scale * gain).astype(jnp.bfloat16)
    pl.semaphore_wait(barrier, greeted)
    gathered.start(all_n_ref.at[fsdp])
    grad_sum = GroupScatter(
        give_sib,
        got_sib,
        lambda step: give_cross.at[step - 1],
        got_cross,
        far,
        got_far,
        grad_sends,
        grad_arrivals,
    )

    def hidden_part(shard):
        def body(at):
            columns = lane_tile(at, step_in)
            normed = all_n_ref[shard]
            gate = forward_dot(normed, gate_ref[:, columns])
            upward = forward_dot(normed, up_ref[:, columns])
            grad_act = dot_columns(
                all_g_ref[shard], down_ref[pl.ds(pl.multiple_of(at * step_in, LANES), step_in), :]
            )
            sigmoid = jax.nn.sigmoid(gate)
            silu = gate * sigmoid
            act_ref[shard, :, columns] = (silu * upward).astype(jnp.bfloat16)
            gate_grad[shard, :, columns] = (
                grad_act * upward * (sigmoid * (1.0 + gate * (1.0 - sigmoid)))
            ).astype(jnp.bfloat16)
            up_grad[shard, :, columns] = (grad_act * silu).astype(jnp.bfloat16)

        tiles(hidden // step_in, body)

    def grad_part(shard, target):
        def body(at):
            columns = pl.ds(pl.multiple_of(at * step_out, LANES), step_out)
            target[:, columns] = (
                dot_columns(gate_grad[shard], gate_ref[columns, :])
                + dot_columns(up_grad[shard], up_ref[columns, :])
            ).astype(target.dtype)

        tiles(width // step_out, body)

    for copy in loads:
        copy.wait()
    hidden_part(fsdp)
    gathered.sibling_here()
    sibling = gathered.sibling
    hidden_part(sibling)
    grad_part(sibling, grad_sum.give_sib)
    grad_sum.to_sibling().start()
    gathered.forward()
    grad_part(fsdp, grad_own)
    def turn_act(shard):
        transpose_into(turned_act.at[:, lane_tile(shard, rows)], act_ref.at[shard])

    turn_act(fsdp)
    turn_act(sibling)
    far_shards = []
    for step in range(1, chips):
        ours = gathered.same_core(chips - step)
        theirs = ours + sibling - fsdp
        far_shards.append((step, ours, theirs))
        gathered.crossed(step)
        hidden_part(theirs)
        hidden_part(ours)
        turn_act(theirs)
        turn_act(ours)
    blocks = hidden // 16
    spans, first = [], 0
    for ring in rings:
        last = min(blocks, first + ring.work.shape[0])
        spans.append((first, last, ring.work))
        first = last

    def down_tile(at):
        columns = lane_tile(at, step_out)
        part = forward_dot(
            turned_act[...], all_g_ref[:, :, columns].reshape(group * rows, step_out)
        ).astype(jnp.bfloat16)
        for begin, end, work in spans:
            if end > begin:
                work[: end - begin, :, columns] = part[begin * 16 : end * 16].reshape(
                    end - begin, 16, step_out
                )

    tiles(width // step_out, down_tile)
    for begin, end, work in spans:
        for spare in range(end - begin, work.shape[0]):
            work[spare] = jnp.zeros(work.shape[1:], work.dtype)
    for ring in rings:
        ring.start()
    for step, ours, theirs in far_shards:
        grad_part(theirs, give_cross.at[step - 1])
        grad_sum.to_cross(step).start()
        grad_part(ours, far.at[step - 1])
        grad_sum.add_cross(step)
    ticked = [0]

    def ring_tick(at):
        for ring in rings:

            @pl.when(at < ring.ticks)
            def _():
                ring.tick(jnp.minimum(at, ring.ticks - 1))

    def ticking(times, body):
        begin = ticked[0]

        def step(at):
            body(at)
            ring_tick(begin + at)

        tiles(times, step)
        ticked[0] += times

    for shard in range(group):
        span = slice(shard * rows, (shard + 1) * rows)
        transpose_into(turned_n.at[:, span], all_n_ref.at[shard])
    own = width // group
    row_blocks = own // 16
    for source, target in ((gate_grad, gate_part_ref), (up_grad, up_part_ref)):

        def weight_tile(at):
            columns = lane_tile(at, step_in)
            part = forward_dot(
                turned_n[...], source[:, :, columns].reshape(group * rows, step_in)
            ).astype(jnp.bfloat16)
            for block in range(step_in // LANES):
                first = (at * (step_in // LANES) + block) * row_blocks
                for owner in range(group):
                    target[owner, pl.ds(first, row_blocks)] = part[
                        owner * own : (owner + 1) * own, block * LANES : (block + 1) * LANES
                    ].reshape(row_blocks, 16, LANES)

        ticking(hidden // step_in, weight_tile)
        filled = hidden // LANES * row_blocks
        for spare in range(filled, target.shape[1]):
            for owner in range(group):
                target[owner, spare] = jnp.zeros(target.shape[2:], target.dtype)
        store(target, gate_part_out if source is gate_grad else up_part_out)

    def layer_tile(at):
        columns = lane_tile(at, step_out)
        part = forward_dot(
            act_ref[...].reshape(group * rows, hidden), down_ref[:, columns]
        ).reshape(group, rows, step_out)
        layer_part_ref[:, :, columns] = part.astype(jnp.bfloat16)

    ticking(width // step_out, layer_tile)
    store(layer_part_ref, layer_part_out)
    layer_ref[...] = resid_ref[...] + layer_part_ref[fsdp].astype(jnp.float32)
    upstream = grad_sum.total(grad_own[...])
    resid = resid_ref[...]
    scaled = upstream * gain
    grad_resid = (
        all_g_ref[fsdp].astype(jnp.float32)
        + scale * scaled
        - resid * scale**3 * jnp.mean(scaled * resid, axis=-1, keepdims=True)
    )
    gain_grad_ref[...] = jnp.sum(upstream * resid * scale, axis=0, keepdims=True)
    resid_grad_ref[...] = grad_resid
    branch_ref[...] = grad_resid.astype(jnp.bfloat16)
    units, _, wide = g_wide_ref.shape
    sequences = units // KVH
    keys = rows // sequences
    groups = wide // keys
    g_wide_ref[:, :HD, :] = jnp.zeros((units, HD, wide), g_wide_ref.dtype)
    for pair in range(H // 2):
        columns = slice(pair * 2 * HD, (pair + 1) * 2 * HD)
        mixed = dot_columns(branch_ref[...], out_ref[columns, :]).astype(jnp.bfloat16)
        for sequence in range(sequences):
            turned = mixed[sequence * keys : (sequence + 1) * keys].T
            for half in range(2):
                head = 2 * pair + half
                unit, member = sequence * KVH + head // groups, head % groups
                g_wide_ref[unit, HD:, member * keys : (member + 1) * keys] = turned[
                    half * HD : (half + 1) * HD
                ]
    begin = ticked[0]
    tiles(max(0, rings[0].ticks - begin), lambda at: ring_tick(begin + at))
    gathered.sent()
    grad_sum.sent()
    for ring in rings:
        ring.finish()
    for copy in stores:
        copy.wait()


def spread(blocks, count):
    return -(-blocks // count) * count


def feed_forward(x, low, full_out, my_gate, my_up, my_down, all_g, gain, units, wide):
    group, count = lax.axis_size("fsdp"), lax.axis_size("ctx")
    rows, width = x.shape
    hidden = my_gate.shape[1]
    blocks = spread(hidden // LANES * (width // group // 16), wide_split(width) * count)
    chips = group // 2
    dma = pltpu.SemaphoreType.DMA((2 * chips - 1,))
    bf16 = jnp.bfloat16
    down_chunks = [(per, 16, width) for per in down_split(hidden // 16, count)]
    return pl.pallas_call(
        ffn_kernel,
        out_shape=[
            jax.ShapeDtypeStruct((rows, width), jnp.float32),
            jax.ShapeDtypeStruct((rows, width), jnp.float32),
            jax.ShapeDtypeStruct((rows, width), bf16),
            jax.ShapeDtypeStruct((units, 2 * HD, wide), bf16),
            jax.ShapeDtypeStruct((group, blocks, 16, LANES), bf16),
            jax.ShapeDtypeStruct((group, blocks, 16, LANES), bf16),
            jax.ShapeDtypeStruct((group, rows, width), bf16),
            *[jax.ShapeDtypeStruct(chunk, bf16) for chunk in down_chunks],
            jax.ShapeDtypeStruct((1, width), jnp.float32),
        ],
        in_specs=[VMEM] * 4 + [ANY] * 4,
        out_specs=[VMEM] * 4 + [ANY] * 3 + [VMEM] * (1 + len(down_chunks)),
        scratch_shapes=[
            pltpu.VMEM((group, rows, width), bf16),
            pltpu.VMEM((width, group * rows), bf16),
            pltpu.VMEM((hidden, group * rows), bf16),
            pltpu.VMEM((group, rows, hidden), bf16),
            pltpu.VMEM((group, rows, hidden), bf16),
            pltpu.VMEM((group, rows, hidden), bf16),
            pltpu.VMEM((rows, width), jnp.float32),
            pltpu.VMEM((rows, width), jnp.float32),
            *[kind for chunk in down_chunks for kind in ring_scratch(chunk)],
            *scatter_scratch(rows, width),
            *[dma] * 4,
            pltpu.VMEM(my_gate.shape, bf16),
            pltpu.VMEM(my_up.shape, bf16),
            pltpu.VMEM(my_down.shape, bf16),
            pltpu.VMEM(all_g.shape, bf16),
            pltpu.VMEM((group, blocks, 16, LANES), bf16),
            pltpu.VMEM((group, blocks, 16, LANES), bf16),
            pltpu.VMEM((group, rows, width), bf16),
            pltpu.SemaphoreType.DMA((7,)),
            *[kind for _ in down_chunks for kind in ring_semaphores()],
        ],
        compiler_params=pltpu.CompilerParams(
            collective_id=2, has_side_effects=True, vmem_limit_bytes=60 << 20
        ),
    )(x, low, full_out, gain, my_gate, my_up, my_down, all_g)


def back_kernel(
    down_blocks, q_ref, g_ref, log_ref, gain_grad_ref, gain_ref, cos_ref, sin_ref,
    pairs_ref, mix_in, gate_ref, up_ref, layer_base_in, layer_part_ref, branch_ref, low_t_ref,
    normed_t_ref, w_query_in, w_key_in, w_value_in, x_in, resid_grad_in, *rest,
):
    taken = iter(rest)

    def take(number):
        return [next(taken) for _ in range(number)]

    halves, downs = wide_split(x_in.shape[1]), len(down_blocks)
    down_refs = take(downs)
    tokens_ref, layer_ref = take(2)
    wide_totals, down_totals = take(2 * halves), take(downs)
    out_a_total, out_b_total, rest_a_total, rest_b_total = take(4)
    peer_got, chain_got, layer_sib, layer_cross, layer_far = take(5)
    kv_ref, stage_ref, final_ref, qg_ref, delta_ref, grad_q_ref = take(6)
    wide_scratch = take(4 * halves)
    out_a_work, out_a_land, out_b_work, out_b_land = take(4)
    rest_a_work, rest_a_land, rest_b_work, rest_b_land = take(4)
    low_all, normed_all, branch_all, query_all, pair_all, upstream_ref, gain_give, gain_got = take(8)
    far_ref, layer_stage = take(2)
    mix_ref, layer_base_ref, w_query_ref, w_key_ref, w_value_ref, x_ref, resid_grad_ref = take(7)
    steps = Steps()
    fsdp, ctx, group, count = steps.fsdp, steps.ctx, lax.axis_size("fsdp"), lax.axis_size("ctx")
    units, deep, wide = q_ref.shape
    keys = pairs_ref.shape[2]
    rows, width = x_ref.shape
    own = width // group
    wide_rings = [
        Ring(*wide_scratch[2 * at : 2 * at + 2], wide_totals[at], take(5), at < halves, True)
        for at in range(2 * halves)
    ]
    down_rings = [SpreadRing(total, take(2), at % 2 == 0) for at, total in enumerate(down_totals)]
    out_a = Ring(out_a_work, out_a_land, out_a_total, take(2), True)
    out_b = Ring(out_b_work, out_b_land, out_b_total, take(2), False)
    layer_sum = GroupScatter(
        None,
        layer_sib,
        lambda step: layer_part_ref.at[
            2 * lax.rem(lax.div(fsdp, 2) + group // 2 - step, group // 2) + 1 - lax.rem(fsdp, 2)
        ],
        layer_cross,
        far_ref,
        layer_far,
        *take(2),
    )
    layer_sum.give_sib = layer_part_ref.at[layer_sum.sibling]
    rest_a = Ring(rest_a_work, rest_a_land, rest_a_total, take(2), True)
    rest_b = Ring(rest_b_work, rest_b_land, rest_b_total, take(2), False)
    first_rings = []
    for at in range(halves):
        first_rings += [wide_rings[at], wide_rings[halves + at]]
        first_rings += down_rings[at * downs // halves : (at + 1) * downs // halves]
    begun_rings = len(first_rings)
    first_rings += [out_a, out_b]
    peer_sends, peer_arrivals, chain_sends, chain_arrivals = take(4)
    branch_gather = GroupGather(lambda shard: branch_all.at[shard], *take(2))
    query_gather = GroupGather(lambda shard: query_all.at[shard], *take(2))
    pair_gather = GroupGather(lambda shard: pair_all.at[shard], *take(2))
    low_sends, low_arrivals, normed_sends, normed_arrivals, gain_sends, gain_arrivals = take(6)
    local_sems, stage_sems = take(2)

    barrier = pltpu.get_barrier_semaphore()
    greeted = steps.greet(barrier) + greet_group(barrier) + 2
    for device in (out_a.after, out_b.after):
        pl.semaphore_signal(barrier, inc=1, device_id=device, device_id_type=MESH)

    loads = []

    def load(source, target):
        copy = pltpu.make_async_copy(source, target, local_sems.at[len(loads)])
        copy.start()
        loads.append(copy)

    n = wide_scratch[0].shape[2]
    for at, ring in enumerate(wide_rings):
        source = (gate_ref, up_ref)[at // halves]
        for chunk in range(count):
            load(source.at[:, pl.ds((at % halves * count + chunk) * n, n)], ring.work.at[chunk])
    for ring, source in zip(down_rings, down_refs):
        load(source, ring.chunk(ring.total, ring.first))
    ring_loads = len(loads)
    load(pairs_ref, kv_ref)
    load(mix_in, mix_ref)
    load(branch_ref, branch_all.at[fsdp])
    load(low_t_ref.at[pl.ds(fsdp * own, own)], low_all.at[:, lane_tile(fsdp, rows)])
    load(normed_t_ref.at[pl.ds(fsdp * own, own)], normed_all.at[:, lane_tile(fsdp, rows)])
    slot_loads = len(loads)
    for source, target in (
        (layer_base_in, layer_base_ref),
        (w_query_in, w_query_ref),
        (w_key_in, w_key_ref),
        (w_value_in, w_value_ref),
        (x_in, x_ref),
        (resid_grad_in, resid_grad_ref),
    ):
        load(source, target)
    for copy in loads[:ring_loads]:
        copy.wait()
    pl.semaphore_wait(barrier, greeted)
    for ring in first_rings[:begun_rings]:
        ring.start()
    branch_gather.start(branch_ref)
    layer_sum.to_sibling().start()
    for step in range(1, group // 2):
        layer_sum.to_cross(step).start()

    def slices(source, target, sends, arrivals, step):
        peer = lax.rem(fsdp + step, group)
        return pltpu.make_async_remote_copy(
            src_ref=source.at[pl.ds(peer * own, own)],
            dst_ref=target.at[:, lane_tile(fsdp, rows)],
            send_sem=sends.at[step - 1],
            recv_sem=arrivals.at[step - 1],
            device_id=(peer, ctx),
            device_id_type=MESH,
        )

    turned = [
        slices(*ends, step)
        for ends in (
            (low_t_ref, low_all, low_sends, low_arrivals),
            (normed_t_ref, normed_all, normed_sends, normed_arrivals),
        )
        for step in range(1, group)
    ]
    for copy in turned:
        copy.start()

    def prepare(unit):
        q, g = q_ref[unit], g_ref[unit]
        qg_ref[unit, :wide] = q.T
        qg_ref[unit, wide:] = g.T
        delta_ref[unit] = jnp.sum(
            g[HD:].astype(jnp.float32) * mix_ref[unit], axis=0, keepdims=True
        )
        grad_q_ref[unit] = jnp.zeros((HD, wide), jnp.float32)

    for copy in loads[ring_loads:slot_loads]:
        copy.wait()
    tiles(units, prepare)

    def tick(ring, at):
        @pl.when(jnp.logical_and(at >= 0, at < ring.ticks))
        def _():
            ring.tick(jnp.clip(at, 0, ring.ticks - 1))

    late = steps.levels // 2 + 1

    def pump(at):
        lag = [0] * begun_rings + [late, late]
        for turn, ring in enumerate(first_rings):

            @pl.when(lax.rem(at, len(first_rings)) == turn)
            def _():
                tick(ring, lax.div(at, len(first_rings)) - lag[turn])

    def back(unit, first, blocks, diagonal):
        kv = kv_ref[pl.ds(first, blocks), unit].reshape(blocks * keys, deep)
        scores = jnp.dot(kv, q_ref[unit], preferred_element_type=jnp.float32)
        probs = jnp.exp(scores - log_ref[unit])
        if diagonal:
            probs = jnp.where(causal(keys, wide, scores.shape), probs, 0.0)
        grad_probs = jnp.dot(kv, g_ref[unit], preferred_element_type=jnp.float32)
        grad_scores = (probs * (grad_probs - delta_ref[unit])).astype(jnp.bfloat16)
        both = jnp.concatenate([grad_scores, probs.astype(jnp.bfloat16)], axis=1)
        grad_kv = jnp.dot(both, qg_ref[unit], preferred_element_type=jnp.float32)
        added = jnp.dot(kv.T, grad_scores, preferred_element_type=jnp.float32)
        grad_q_ref[unit] = grad_q_ref[unit] + added[:HD]
        kv_ref[pl.ds(first, blocks), unit] = grad_kv.astype(kv_ref.dtype).reshape(
            blocks, keys, deep
        )

    def across(pair):
        return pltpu.make_async_remote_copy(
            src_ref=kv_ref.at[2 * pair + 1 - steps.side],
            dst_ref=peer_got.at[pair],
            send_sem=peer_sends.at[pair],
            recv_sem=peer_arrivals.at[pair],
            device_id=steps.peer,
            device_id_type=MESH,
        )

    def down_chain(pair):
        return pltpu.make_async_remote_copy(
            src_ref=kv_ref.at[2 * pair + steps.side],
            dst_ref=chain_got.at[pair],
            send_sem=chain_sends.at[pair],
            recv_sem=chain_arrivals.at[pair],
            device_id=steps.below,
            device_id_type=MESH,
        )

    def combine(time):
        pair = time - steps.levels + steps.level

        @pl.when(jnp.logical_and(pair >= 0, pair <= steps.level))
        def _():
            for slot, expected, arrival, source in (
                (0, jnp.logical_or(pair < steps.level, steps.side == 0), across, peer_got),
                (1, steps.has_above, down_chain, chain_got),
            ):

                @pl.when(expected)
                def _():
                    arrival(pair).wait_recv()
                    copy = pltpu.make_async_copy(
                        source.at[pair], stage_ref.at[slot], stage_sems.at[slot]
                    )
                    copy.start()
                    copy.wait()

                @pl.when(jnp.logical_not(expected))
                def _():
                    stage_ref[slot] = jnp.zeros(stage_ref.shape[1:], stage_ref.dtype)

            def add(unit):
                final_ref[unit] = (
                    kv_ref[2 * pair + steps.side, unit].astype(jnp.float32)
                    + stage_ref[0, unit].astype(jnp.float32)
                    + stage_ref[1, unit].astype(jnp.float32)
                )

            tiles(units, add)

            @pl.when(pair < steps.level)
            def _():
                kv_ref[2 * pair + steps.side] = final_ref[...].astype(kv_ref.dtype)
                down_chain(pair).start()

    row_blocks = own // 16

    def weight_grad(left, right, begin, end, target, first, loop):
        span = LANES * next(n for n in (3, 2, 1) if (end - begin) % (n * LANES) == 0)

        def body(at):
            columns = pl.ds(pl.multiple_of(begin + at * span, LANES), span)
            part = forward_dot(
                left[...], right[:, :, columns].reshape(group * rows, span)
            ).astype(jnp.bfloat16)
            for block in range(span // LANES):
                here = first + (at * (span // LANES) + block) * row_blocks
                target[pl.ds(here, row_blocks)] = part[
                    :, block * LANES : (block + 1) * LANES
                ].reshape(row_blocks, 16, LANES)

        loop((end - begin) // span, body)
        return first + (end - begin) // LANES * row_blocks

    def clear_from(target, first):
        for spare in range(first, target.shape[0]):
            target[spare] = jnp.zeros((16, LANES), jnp.bfloat16)

    def out_grad():
        for copy in turned[: group - 1]:
            copy.wait_recv()
        branch_gather.forward()
        branch_gather.sibling_here()
        for step in range(1, branch_gather.chips):
            branch_gather.crossed(step)
        split = out_split(width)
        clear_from(out_a_work, weight_grad(low_all, branch_all, 0, split, out_a_work, 0, tiles))
        clear_from(out_b_work, weight_grad(low_all, branch_all, split, width, out_b_work, 0, tiles))
        out_a.start()
        out_b.start()

    turns = units // 2
    rings = max(turns, len(first_rings))

    def slot(pair):
        def turn(at):
            @pl.when(jnp.logical_and(pair < steps.level, at < turns))
            def _():
                for unit in (2 * at, 2 * at + 1):
                    back(unit, 2 * pair, 2, False)

            @pl.when(jnp.logical_and(pair == steps.level, at < turns))
            def _():
                for unit in (2 * at, 2 * at + 1):
                    back(unit, ctx, 1, True)

            @pl.when((pair == steps.level) & (steps.side == 1) & (at < turns))
            def _():
                for unit in (2 * at, 2 * at + 1):
                    back(unit, ctx - 1, 1, False)

            pump(pair * rings + at)

        tiles(rings, turn)

        @pl.when(jnp.logical_or(pair < steps.level, (pair == steps.level) & (steps.side == 1)))
        def _():
            across(pair).start()

        combine(pair)

        @pl.when(pair == late - 1)
        def _():
            out_grad()

    tiles(steps.levels, slot)
    pumped = [steps.levels * rings]

    def pump_next(times=1):
        def body(at, unused, begin=pumped[0]):
            pump(begin + at)
            return unused

        lax.fori_loop(0, times, body, 0)
        pumped[0] += times

    def pumping(times, body):
        begin = pumped[0]

        def step(at):
            body(at)
            tiles(2, lambda more: pump(begin + 2 * at + more))

        tiles(times, step)
        pumped[0] += 2 * times

    cosine, sine = cos_ref[...], sin_ref[...]

    def unturn(columns):
        first, second = columns[: HD // 2], columns[HD // 2 :]
        return jnp.concatenate(
            [first * cosine + second * sine, second * cosine - first * sine], axis=0
        )

    sequences = units // KVH
    groups = wide // keys
    begin = pumped[0]

    def query_rows(sequence):
        span = pl.ds(pl.multiple_of(sequence * keys, LANES), keys)
        for pair in range(H // 2):
            heads = []
            for head in (2 * pair, 2 * pair + 1):
                unit, member = sequence * KVH + head // groups, head % groups
                part = grad_q_ref[unit, :, member * keys : (member + 1) * keys]
                heads.append(unturn(part * HD ** (-0.5)))
            query_all[fsdp, span, pair * 2 * HD : (pair + 1) * 2 * HD] = (
                jnp.concatenate(heads, axis=0).astype(jnp.bfloat16).T
            )
        tiles(3, lambda more: pump(begin + 3 * sequence + more))

    tiles(sequences, query_rows)
    pumped[0] += 3 * sequences
    query_gather.start(query_all.at[fsdp])
    combine(steps.levels)
    kv_width = KVH * HD
    def pair_rows(sequence):
        span = pl.ds(pl.multiple_of(sequence * keys, LANES), keys)
        for pair in range(KVH // 2):
            turned_keys, turned_values = [], []
            for unit in (sequence * KVH + 2 * pair, sequence * KVH + 2 * pair + 1):
                part = final_ref[unit].T
                turned_keys.append(unturn(part[:HD]))
                turned_values.append(part[HD:])
            for start, parts in ((0, turned_keys), (kv_width, turned_values)):
                pair_all[fsdp, span, start + pair * 2 * HD : start + (pair + 1) * 2 * HD] = (
                    jnp.concatenate(parts, axis=0).astype(jnp.bfloat16).T
                )
    tiles(sequences, pair_rows)
    pair_gather.start(pair_all.at[fsdp])
    pump_next(2)
    query_gather.forward()
    step_out = width_tile(width)

    def upstream_tile(at):
        columns = pl.ds(pl.multiple_of(at * step_out, LANES), step_out)
        upstream_ref[:, columns] = (
            dot_columns(query_all[fsdp], w_query_ref[columns, :])
            + dot_columns(pair_all[fsdp, :, :kv_width], w_key_ref[columns, :])
            + dot_columns(pair_all[fsdp, :, kv_width:], w_value_ref[columns, :])
        )

    for copy in loads[slot_loads:]:
        copy.wait()
    pumping(width // step_out, upstream_tile)
    inputs = x_ref[...].astype(jnp.float32)
    scale = norm_scale(inputs)
    upstream = upstream_ref[...]
    scaled = upstream * gain_ref[...]
    tokens_ref[...] = (
        resid_grad_ref[...]
        + scale * scaled
        - inputs * scale**3 * jnp.mean(scaled * inputs, axis=-1, keepdims=True)
    )
    gain_attn = jnp.sum(upstream * inputs * scale, axis=0, keepdims=True)
    lanes = width // LANES
    gain_give[...] = jnp.zeros(gain_give.shape, jnp.float32)
    for block in range(lanes):
        columns = slice(block * LANES, (block + 1) * LANES)
        gain_give[block : block + 1, :] = gain_attn[:, columns]
        gain_give[lanes + block : lanes + block + 1, :] = gain_grad_ref[:, columns]

    def gain_copy(step):
        peer = lax.rem(fsdp + step, group)
        return pltpu.make_async_remote_copy(
            src_ref=gain_give,
            dst_ref=gain_got.at[step - 1],
            send_sem=gain_sends.at[step - 1],
            recv_sem=gain_arrivals.at[step - 1],
            device_id=(peer, ctx),
            device_id_type=MESH,
        )

    for step in range(1, group):
        gain_copy(step).start()
    pump_next()
    for copy in turned[group - 1 :]:
        copy.wait_recv()
    query_gather.sibling_here()
    for step in range(1, query_gather.chips):
        query_gather.crossed(step)
    split = query_split(width)
    filled_a = weight_grad(normed_all, query_all, 0, split, rest_a_work, 0, pumping)
    filled_b = weight_grad(normed_all, query_all, split, width, rest_b_work, 0, pumping)
    pair_gather.forward()
    pump_next()
    pair_gather.sibling_here()
    for step in range(1, pair_gather.chips):
        pair_gather.crossed(step)
    filled_b = weight_grad(normed_all, pair_all, 0, 2 * kv_width, rest_b_work, filled_b, pumping)
    for step in range(1, layer_sum.chips):
        ours = layer_part_ref.at[2 * lax.rem(layer_sum.chip + layer_sum.chips - step, layer_sum.chips) + layer_sum.core]
        for source, target in ((ours, far_ref.at[step - 1]), (layer_cross.at[step - 1], layer_stage)):
            if source is not ours:
                layer_sum.to_cross(step).wait_recv()
            copy = pltpu.make_async_copy(source, target, stage_sems.at[0])
            copy.start()
            copy.wait()
        far_ref[step - 1] = (
            far_ref[step - 1].astype(jnp.float32) + layer_stage[...].astype(jnp.float32)
        ).astype(jnp.bfloat16)
        layer_sum.to_far(step).start()
    gains = gain_give[...]
    for step in range(1, group):
        gain_copy(step).wait_recv()
        gains = gains + gain_got[step - 1]
    gain_tiles = gains.shape[0] // 16
    rest_a_work[filled_a : filled_a + gain_tiles] = gains.astype(jnp.bfloat16).reshape(
        gain_tiles, 16, LANES
    )
    clear_from(rest_a_work, filled_a + gain_tiles)
    clear_from(rest_b_work, filled_b)
    rest_a.start()
    rest_b.start()
    begun = pumped[0]
    total_pumps = max(wide_rings[0].ticks, late + out_a.ticks) * len(first_rings)

    half = -(-(total_pumps - begun) // rest_a.ticks)

    def layer_close():
        layer_sum.to_sibling().wait_recv()
        arrived = [layer_sib]
        for step in range(1, layer_sum.chips):
            layer_sum.to_far(step).wait_recv()
            arrived.append(layer_far.at[step - 1])
        for source in arrived:
            copy = pltpu.make_async_copy(source, layer_stage, stage_sems.at[0])
            copy.start()
            copy.wait()

            def add(at):
                block = pl.ds(pl.multiple_of(at * 32, 32), 32)
                layer_base_ref[block] = layer_base_ref[block] + layer_stage[block].astype(
                    jnp.float32
                )

            tiles(rows // 32, add)

        def close(at):
            block = pl.ds(pl.multiple_of(at * 32, 32), 32)
            layer_ref[block] = layer_base_ref[block].astype(jnp.bfloat16)

        tiles(rows // 32, close)

    def last_ticks(at, unused):
        tiles(half, lambda turn: pump(jnp.minimum(begun + half * at + turn, total_pumps)))
        tick(rest_a, at)
        tick(rest_b, at)

        @pl.when(at == rest_a.ticks * 3 // 4)
        def _():
            layer_close()

        return unused

    lax.fori_loop(0, rest_a.ticks, last_ticks, 0)
    layer_sum.sent()
    for ring in first_rings + [rest_a, rest_b]:
        ring.finish()
    for copy in turned:
        copy.wait_send()
    for gather in (branch_gather, query_gather, pair_gather):
        gather.sent()
    for step in range(1, group):
        gain_copy(step).wait_send()

    def sent(pair):
        @pl.when(jnp.logical_or(pair < steps.level, steps.side == 1))
        def _():
            across(pair).wait_send()

        @pl.when(pair < steps.level)
        def _():
            down_chain(pair).wait_send()

    tiles(steps.level + 1, sent)


def layer_back(
    q_wide, g_wide, log_total, gain_grad, gain, cosine, sine, all_pairs, mix, gate_part, up_part,
    layer_base, layer_parts, branch, low_t, normed_t, w_query, w_key, w_value, x, resid_grad, downs,
):
    group, count = lax.axis_size("fsdp"), lax.axis_size("ctx")
    units, deep, wide = q_wide.shape
    keys = all_pairs.shape[2]
    rows, width = x.shape
    own, kv_width = width // group, w_key.shape[1]
    bf16, f32 = jnp.bfloat16, jnp.float32
    dma = pltpu.SemaphoreType.DMA
    halves = wide_split(width)
    wide_chunk = (group, gate_part.shape[1] // (halves * count), 16, LANES)
    gain_rows = spread(2 * (width // LANES), 16)
    split, row_blocks = query_split(width), own // 16
    out_first = out_split(width)
    chips = group // 2
    small_chunks = [
        (spread(held, count) // count, 16, LANES)
        for held in (
            out_first // LANES * row_blocks,
            (width - out_first) // LANES * row_blocks,
            split // LANES * row_blocks + gain_rows // 16,
            (width - split + 2 * kv_width) // LANES * row_blocks,
        )
    ]
    levels = count // 2
    loaded = [mix, layer_base, w_query, w_key, w_value, x, resid_grad]
    return pl.pallas_call(
        functools.partial(back_kernel, [part.shape[0] for part in downs]),
        out_shape=[
            jax.ShapeDtypeStruct((rows, width), f32),
            jax.ShapeDtypeStruct((rows, width), bf16),
            *[ring_total(wide_chunk, True)] * (2 * halves),
            *[ring_total(part.shape) for part in downs],
            *[ring_total(chunk) for chunk in small_chunks],
            *[jax.ShapeDtypeStruct((levels, units, keys, deep), bf16)] * 2,
            jax.ShapeDtypeStruct((rows, width), bf16),
            *[jax.ShapeDtypeStruct((chips - 1, rows, width), bf16)] * 2,
        ],
        in_specs=[VMEM] * 7 + [ANY] * (14 + len(downs)),
        out_specs=[VMEM] * (6 + 2 * halves + len(downs)) + [ANY] * 5,
        scratch_shapes=[
            pltpu.VMEM(all_pairs.shape, bf16),
            pltpu.VMEM((2, units, keys, deep), bf16),
            pltpu.VMEM((units, keys, deep), f32),
            pltpu.VMEM((units, 2 * wide, deep), bf16),
            pltpu.VMEM((units, 1, wide), f32),
            pltpu.VMEM((units, HD, wide), f32),
            *[kind for _ in range(2 * halves) for kind in ring_scratch(wide_chunk, True)],
            *[kind for chunk in small_chunks for kind in ring_scratch(chunk)],
            pltpu.VMEM((own, group * rows), bf16),
            pltpu.VMEM((own, group * rows), bf16),
            pltpu.VMEM((group, rows, width), bf16),
            pltpu.VMEM((group, rows, width), bf16),
            pltpu.VMEM((group, rows, 2 * kv_width), bf16),
            pltpu.VMEM((rows, width), f32),
            pltpu.VMEM((gain_rows, LANES), f32),
            pltpu.VMEM((group - 1, gain_rows, LANES), f32),
            pltpu.VMEM((chips - 1, rows, width), bf16),
            pltpu.VMEM((rows, width), bf16),
            *[pltpu.VMEM(array.shape, array.dtype) for array in loaded],
            *[kind for _ in range(2 * halves) for kind in ring_semaphores(True)],
            *[kind for _ in range(len(downs) + 2) for kind in ring_semaphores()],
            *[dma((group - 1,))] * 2,
            *[kind for _ in range(2) for kind in ring_semaphores()],
            *[dma((levels,))] * 4,
            *[group_semaphores()] * 6,
            *[dma((group - 1,))] * 6,
            dma((11 + len(downs) + 2 * halves * count,)),
            dma((2,)),
        ],
        compiler_params=pltpu.CompilerParams(
            collective_id=3, has_side_effects=True, vmem_limit_bytes=62 << 20
        ),
    )(
        q_wide, g_wide, log_total, gain_grad, gain, cosine, sine, all_pairs, mix, gate_part, up_part,
        layer_base, layer_parts, branch, low_t, normed_t, w_query, w_key, w_value, x, resid_grad,
        *downs,
    )


def finish_kernel(halves, downs, *refs):
    taken = iter(refs)

    def take(number):
        return [next(taken) for _ in range(number)]

    wides, down_refs, smalls, (rows_ref, layer_rows) = take(2 * halves), take(downs), take(4), take(2)
    outs, (tokens_ref, layer_ref) = take(7), take(2)
    wide_held, down_held, small_held = take(2 * halves), take(downs), take(4)
    made, (load_sems, store_sems) = take(7), take(2)
    sources = [*wides, *down_refs, *smalls]
    held = [*wide_held, *down_held, *small_held]
    loads = {}
    for at, (source, target) in enumerate(zip(sources, held)):
        loads[id(target)] = pltpu.make_async_copy(source, target, load_sems.at[at])
        loads[id(target)].start()
    stores = []

    def store(index, columns=None):
        source, target = made[index], outs[index]
        if columns is not None:
            source, target = source.at[:, columns], target.at[:, columns]
        copy = pltpu.make_async_copy(source, target, store_sems.at[len(stores)])
        copy.start()
        stores.append(copy)

    rows = made[4].shape[0]
    row_blocks = rows // 16
    group = wides[0].shape[1]

    def unpack(source, first, index, begin, end):
        target = made[index]
        for block in range(begin, end):
            here = first + (block - begin) * row_blocks
            target[:, block * LANES : (block + 1) * LANES] = (
                source[here : here + row_blocks].reshape(rows, LANES).astype(jnp.float32)
            )
        return first + (end - begin) * row_blocks

    for index, parts in ((4, wide_held[:halves]), (5, wide_held[halves:])):
        for part in parts:
            loads[id(part)].wait()
        target = made[index]
        columns = target.shape[1] // group
        for owner in range(group):
            tile_rows = jnp.concatenate(
                [part[:, owner].reshape((-1,) + part.shape[3:]) for part in parts], axis=0
            )
            for block in range(columns // LANES):
                begin = owner * columns + block * LANES
                target[:, begin : begin + LANES] = (
                    tile_rows[block * row_blocks : (block + 1) * row_blocks]
                    .reshape(rows, LANES)
                    .astype(jnp.float32)
                )
            store(index, pl.ds(owner * columns, columns))
    down_grad = made[6]
    blocks, begin = down_grad.shape[0] // 16, 0
    for source in down_held:
        loads[id(source)].wait()
        end = min(blocks, begin + source.shape[0])
        if end > begin:
            down_grad[begin * 16 : end * 16, :] = (
                source[: end - begin]
                .reshape((end - begin) * 16, down_grad.shape[1])
                .astype(jnp.float32)
            )
        begin = end
    store(6)
    for part in small_held:
        loads[id(part)].wait()
    out_a, out_b, rest_a, rest_b = small_held
    lanes, kv_lanes = made[0].shape[1] // LANES, made[1].shape[1] // LANES
    middle, split = out_split(made[0].shape[1]) // LANES, query_split(made[0].shape[1]) // LANES
    unpack(out_a, 0, 3, 0, middle)
    unpack(out_b, 0, 3, middle, lanes)
    store(3)
    unpack(rest_a, 0, 0, 0, split)
    at = unpack(rest_b, 0, 0, split, lanes)
    store(0)
    at = unpack(rest_b, at, 1, 0, kv_lanes)
    store(1)
    unpack(rest_b, at, 2, 0, kv_lanes)
    store(2)
    keys = tokens_ref.shape[0]
    for sequence in range(tokens_ref.shape[1]):
        block = slice(sequence * keys, (sequence + 1) * keys)
        tokens_ref[:, sequence, :] = rows_ref[block]
        layer_ref[:, sequence, :] = layer_rows[block]
    for copy in stores:
        copy.wait()


def finish(wides, downs, smalls, token_rows, layer_rows, own, kv_width, hidden, sequences):
    rows, width = token_rows.shape
    f32 = jnp.float32
    outs = [
        jax.ShapeDtypeStruct((own, columns), f32)
        for columns in (width, kv_width, kv_width, width, FF, FF)
    ] + [jax.ShapeDtypeStruct((hidden, width), f32)]
    sources = [*wides, *downs, *smalls]
    dma = pltpu.SemaphoreType.DMA
    return pl.pallas_call(
        functools.partial(finish_kernel, len(wides) // 2, len(downs)),
        out_shape=outs
        + [
            jax.ShapeDtypeStruct((rows // sequences, sequences, width), kind)
            for kind in (f32, layer_rows.dtype)
        ],
        in_specs=[ANY] * len(sources) + [VMEM] * 2,
        out_specs=[ANY] * len(outs) + [VMEM] * 2,
        scratch_shapes=[pltpu.VMEM(array.shape, array.dtype) for array in sources]
        + [pltpu.VMEM(out.shape, f32) for out in outs]
        + [dma((len(sources),)), dma((5 + 2 * wides[0].shape[1],))],
        compiler_params=pltpu.CompilerParams(vmem_limit_bytes=60 << 20),
    )(*sources, token_rows, layer_rows)


def on_device(
    tokens, w_query, w_key, w_value, w_out, w_gate, w_up, w_down, gain_attn, gain_ffn, cotangent
):
    block_len, seq_count, width = tokens.shape
    rows_count = block_len * seq_count
    kv_width = KVH * HD
    positions = lax.axis_index("ctx") * block_len + jnp.arange(block_len, dtype=jnp.int32)
    freqs = ROTARY_BASE ** (-2.0 * jnp.arange(HD // 2, dtype=jnp.float32) / HD)
    angles = freqs[:, None] * positions.astype(jnp.float32)[None, :]
    cosine, sine = jnp.cos(angles), jnp.sin(angles)
    own = gain_attn.shape[0]
    units = seq_count * KVH
    wide = H // KVH * block_len
    own_gains = jnp.pad(
        jnp.stack([gain_attn, gain_ffn]).astype(jnp.float32), ((0, 6), (0, spread(own, LANES) - own))
    )
    (
        x_rows, q_wide, normed_t, full_gain_attn, full_gain_ffn, full_query, full_key, full_value, attn_low, low_t, mix_unit, log_total,
        all_pairs, full_out, my_gate, my_up, all_g,
    ) = attend(
        tokens, cotangent, own_gains, cosine, sine, w_query, w_key, w_value, w_out, w_gate, w_up
    )
    layer_base, grad_resid, grad_branch, g_wide, gate_part, up_part, layer_parts, *downs = (
        feed_forward(
            x_rows, attn_low, full_out, my_gate, my_up, w_down, all_g, full_gain_ffn, units, wide
        )
    )
    downs, gain_term_ffn = downs[:-1], downs[-1]
    grad_tokens, layer_out, *sums = layer_back(
        q_wide, g_wide, log_total, gain_term_ffn, full_gain_attn, cosine, sine, all_pairs, mix_unit,
        gate_part, up_part, layer_base, layer_parts, grad_branch, low_t, normed_t, full_query,
        full_key, full_value, x_rows, grad_resid, downs,
    )
    wides, sums = sums[: 2 * wide_split(width)], sums[2 * wide_split(width) :]
    smalls = sums[len(downs) : len(downs) + 4]
    filled = query_split(width) // LANES * (own // 16)
    gain_grads = smalls[2][filled:].reshape(-1, LANES)[: 2 * (width // LANES)].reshape(2, width)
    gain_grads = lax.dynamic_slice_in_dim(gain_grads, lax.axis_index("fsdp") * own, own, 1)
    gain_grads = gain_grads.astype(jnp.float32)
    *grads, tokens_grad, layer_result = finish(
        wides, sums[: len(downs)], smalls, grad_tokens, layer_out, own, kv_width, w_down.shape[0],
        seq_count,
    )
    return (
        layer_result,
        tokens_grad,
        *grads,
        gain_grads[0],
        gain_grads[1],
    )


def solution(mesh):
    return jax.shard_map(
        on_device,
        mesh=mesh,
        in_specs=(
            P("ctx", "fsdp", None),
            P("fsdp", None),
            P("fsdp", None),
            P("fsdp", None),
            P("fsdp", None),
            P("fsdp", None),
            P("fsdp", None),
            P("fsdp", None),
            P("fsdp"),
            P("fsdp"),
            P("ctx", "fsdp", None),
        ),
        out_specs=(
            P("ctx", "fsdp", None),
            P("ctx", "fsdp", None),
            P("fsdp", None),
            P("fsdp", None),
            P("fsdp", None),
            P("fsdp", None),
            P("fsdp", None),
            P("fsdp", None),
            P("fsdp", None),
            P("fsdp"),
            P("fsdp"),
        ),
        check_vma=False,
    )
```

```python
import functools

import jax
import jax.numpy as jnp
from jax import lax
from jax.experimental import pallas as pl
from jax.experimental.pallas import tpu as pltpu
from jax.sharding import PartitionSpec as P

H = 18
KVH = 6
HD = 64
FF = 3072


EPSILON = 1e-05
ROTARY_BASE = 10000.0
MASKED_SCORE = -1e30


def norm_scale(rows):
    return lax.rsqrt(jnp.mean(rows * rows, axis=-1, keepdims=True) + EPSILON)


def forward_dot(left, right):
    return jnp.dot(left, right, preferred_element_type=jnp.float32)


MESH = pl.DeviceIdType.MESH
LANES = 128


def ring_place(ctx, fsdp, count):
    column, side = lax.div(ctx, 2), lax.rem(ctx, 2)
    place = column + side * (count - 1 - 2 * column)
    odd = lax.rem(fsdp, 2)
    return place + odd * (count - 1 - 2 * place)


def ring_ctx(place, fsdp, count):
    odd = lax.rem(fsdp, 2)
    place = place + odd * (count - 1 - 2 * place)
    late = lax.div(place, count // 2)
    return (1 - late) * 2 * place + late * (2 * (count - 1 - place) + 1)


class GroupGather:
    def __init__(self, shard_of, sends, arrivals):
        self.shard_of, self.sends, self.arrivals = shard_of, sends, arrivals
        self.fsdp, self.ctx = lax.axis_index("fsdp"), lax.axis_index("ctx")
        self.chips = lax.axis_size("fsdp") // 2
        self.chip, self.core = lax.div(self.fsdp, 2), lax.rem(self.fsdp, 2)
        self.sibling = 2 * self.chip + 1 - self.core

    def copy(self, source, shard, semaphore, device):
        return pltpu.make_async_remote_copy(
            src_ref=source,
            dst_ref=self.shard_of(shard),
            send_sem=self.sends.at[semaphore],
            recv_sem=self.arrivals.at[semaphore],
            device_id=(device, self.ctx),
            device_id_type=MESH,
        )

    def same_core(self, step):
        return 2 * lax.rem(self.chip + step, self.chips) + self.core

    def across(self, source):
        return self.copy(source, self.fsdp, 0, self.sibling)

    def out(self, source, step):
        return self.copy(source, self.fsdp, step, self.same_core(step))

    def onward(self, step):
        shard = self.same_core(self.chips - step)
        return self.copy(self.shard_of(shard), shard, self.chips - 1 + step, self.sibling)

    def start(self, source):
        for step in range(1, self.chips):
            self.out(source, step).start()
        self.across(source).start()

    def forward(self):
        own = self.shard_of(self.fsdp)
        for step in range(1, self.chips):
            self.out(own, step).wait_recv()
            self.onward(step).start()

    def sibling_here(self):
        self.across(self.shard_of(self.fsdp)).wait_recv()

    def crossed(self, step):
        self.onward(step).wait_recv()

    def sent(self):
        own = self.shard_of(self.fsdp)
        self.across(own).wait_send()
        for step in range(1, self.chips):
            self.out(own, step).wait_send()
            self.onward(step).wait_send()

    def finish(self):
        self.forward()
        self.sibling_here()
        for step in range(1, self.chips):
            self.crossed(step)
        self.sent()


class HalfGather:
    def __init__(self, held, own_rows, sends, arrivals):
        self.held, self.own = held, own_rows
        self.sends, self.arrivals = sends, arrivals
        self.fsdp, self.ctx = lax.axis_index("fsdp"), lax.axis_index("ctx")
        self.chips = lax.axis_size("fsdp") // 2
        self.chip, self.core = lax.div(self.fsdp, 2), lax.rem(self.fsdp, 2)
        self.sibling = 2 * self.chip + 1 - self.core
        self.side = lax.rem(self.ctx, 2)
        self.pair = self.ctx + 1 - 2 * self.side
        first = -(-own_rows // 32) * 16
        self.halves = ((0, first), (first, own_rows - first))

    def same_core(self, step):
        return 2 * lax.rem(self.chip + step, self.chips) + self.core

    def rows(self, shard, half=None):
        begin, size = (0, self.own) if half is None else self.halves[half]
        return self.held.at[pl.ds(shard * self.own + begin, size)]

    def copy(self, source, target, semaphore, device):
        return pltpu.make_async_remote_copy(
            src_ref=source,
            dst_ref=target,
            send_sem=self.sends.at[semaphore],
            recv_sem=self.arrivals.at[semaphore],
            device_id=device,
            device_id_type=MESH,
        )

    def on_side(self, body):
        for half in range(2):

            @pl.when(self.side == half)
            def _(half=half):
                body(half)

    def across(self, source):
        return self.copy(source, self.rows(self.fsdp), 0, (self.sibling, self.ctx))

    def out(self, source, step, half):
        begin, size = self.halves[half]
        return self.copy(
            source.at[pl.ds(begin, size)],
            self.rows(self.fsdp, half),
            step,
            (self.same_core(step), self.ctx),
        )

    def to_pair(self, step, half):
        part = self.rows(self.same_core(self.chips - step), half)
        return self.copy(part, part, self.chips - 1 + step, (self.fsdp, self.pair))

    def onward(self, step):
        part = self.rows(self.same_core(self.chips - step))
        return self.copy(part, part, 2 * self.chips - 2 + step, (self.sibling, self.ctx))

    def start(self, source):
        def send(half):
            for step in range(1, self.chips):
                self.out(source, step, half).start()

        self.on_side(send)
        self.across(source).start()

    def to_pairs(self):
        def forward(half):
            for step in range(1, self.chips):
                self.out(self.rows(self.fsdp), step, half).wait_recv()
                self.to_pair(step, half).start()

        self.on_side(forward)

    def to_sibling(self):
        def forward(half):
            for step in range(1, self.chips):
                self.to_pair(step, 1 - half).wait_recv()

        self.on_side(forward)
        for step in range(1, self.chips):
            self.onward(step).start()

    def arrived(self):
        self.across(self.rows(self.fsdp)).wait_recv()
        for step in range(1, self.chips):
            self.onward(step).wait_recv()

    def sent(self):
        def wait(half):
            for step in range(1, self.chips):
                self.out(self.rows(self.fsdp), step, half).wait_send()
                self.to_pair(step, half).wait_send()

        self.on_side(wait)
        self.across(self.rows(self.fsdp)).wait_send()
        for step in range(1, self.chips):
            self.onward(step).wait_send()


def half_semaphores(many):
    return pltpu.SemaphoreType.DMA((many, 3 * (lax.axis_size("fsdp") // 2) - 2))


def group_semaphores():
    return pltpu.SemaphoreType.DMA((lax.axis_size("fsdp") - 1,))


def greet_group(barrier):
    fsdp, ctx, group = lax.axis_index("fsdp"), lax.axis_index("ctx"), lax.axis_size("fsdp")
    for step in range(1, group):
        peer = lax.rem(fsdp + step, group)
        pl.semaphore_signal(barrier, inc=1, device_id=(peer, ctx), device_id_type=MESH)
    return group - 1


class Steps:
    def __init__(self):
        self.fsdp, self.ctx = lax.axis_index("fsdp"), lax.axis_index("ctx")
        self.levels = lax.axis_size("ctx") // 2
        self.level, self.side = lax.div(self.ctx, 2), lax.rem(self.ctx, 2)
        self.peer = (self.fsdp, 2 * self.level + 1 - self.side)
        self.above = (self.fsdp, lax.rem(self.ctx + 2, 2 * self.levels))
        self.below = (self.fsdp, lax.rem(self.ctx + 2 * self.levels - 2, 2 * self.levels))
        self.has_above = self.level + 1 < self.levels
        self.has_below = self.level > 0

    def greet(self, barrier):
        pl.semaphore_signal(barrier, inc=1, device_id=self.peer, device_id_type=MESH)

        @pl.when(self.has_above)
        def _():
            pl.semaphore_signal(barrier, inc=1, device_id=self.above, device_id_type=MESH)

        @pl.when(self.has_below)
        def _():
            pl.semaphore_signal(barrier, inc=1, device_id=self.below, device_id_type=MESH)

        return 1 + jnp.minimum(self.level, 1) + jnp.minimum(self.levels - 1 - self.level, 1)


PARTS = 2


def causal(keys, wide, shape):
    key_at = lax.broadcasted_iota(jnp.int32, shape, 0)
    query_at = lax.rem(lax.broadcasted_iota(jnp.int32, shape, 1), keys)
    return key_at <= query_at


def attend_kernel(
    token_ref, upstream_ref, gain_ref, cos_ref, sin_ref, query_ref, key_ref, value_ref, out_ref, gate_ref,
    up_ref, x_ref, q_ref, normed_t_ref, gain_attn_ref, gain_ffn_ref, full_query, full_key, full_value,
    low_ref, low_t_ref, mix_ref, log_ref, all_ref, full_out_ref, my_gate_ref, my_up_ref, all_g_ref,
    normed_ref, key_rows, gain_all, own_out, own_gate, own_up, own_g,
    top_ref, total_ref, chain_sends, chain_arrivals, peer_sends, peer_arrivals,
    half_sends, half_arrivals, gain_sends, gain_arrivals,
    out_sends, out_arrivals, g_sends, g_arrivals,
    part_sends, part_arrivals, local_sems,
):
    steps = Steps()
    fsdp, ctx, group = steps.fsdp, steps.ctx, lax.axis_size("fsdp")
    units, deep, wide = q_ref.shape
    keys = all_ref.shape[2]
    per_part = units // PARTS
    rows_count, width = x_ref.shape
    own = query_ref.shape[0]
    sequences, groups = units // KVH, H // KVH
    barrier = pltpu.get_barrier_semaphore()
    greeted = steps.greet(barrier) + greet_group(barrier)
    span = KVH * HD
    pieces = [(key_ref, full_key, 0), (value_ref, full_value, 0)]
    pieces += [(query_ref, full_query, start) for start in range(0, width, span)]
    gathers = []
    for at, (source, target, start) in enumerate(pieces):
        columns = pl.ds(start, span)
        gather = HalfGather(
            target.at[:, columns], own, half_sends.at[at], half_arrivals.at[at]
        )
        gathers.append((gather, source.at[:, columns]))
    own_rows = pl.ds(fsdp * own, own)
    own_copies = [
        pltpu.make_async_copy(source, target.at[own_rows], local_sems.at[4 + at])
        for at, (source, target) in enumerate(
            ((key_ref, full_key), (value_ref, full_value), (query_ref, full_query))
        )
    ]
    for copy in own_copies:
        copy.start()
    for sequence in range(sequences):
        x_ref[sequence * keys : (sequence + 1) * keys] = token_ref[:, sequence, :]
    gain_all[fsdp] = gain_ref[...]
    pl.semaphore_wait(barrier, greeted)

    def gain_copy(step):
        peer = lax.rem(fsdp + step, group)
        return pltpu.make_async_remote_copy(
            src_ref=gain_ref,
            dst_ref=gain_all.at[fsdp],
            send_sem=gain_sends.at[step - 1],
            recv_sem=gain_arrivals.at[step - 1],
            device_id=(peer, ctx),
            device_id_type=MESH,
        )

    for step in range(1, group):
        gain_copy(step).start()
    for gather, source in gathers:
        gather.start(source)
    for sequence in range(sequences):
        own_g[sequence * keys : (sequence + 1) * keys] = upstream_ref[:, sequence, :]
    inputs = x_ref[...].astype(jnp.float32)
    scale = norm_scale(inputs)
    q_ref[:, HD:, :] = jnp.zeros((units, HD, wide), q_ref.dtype)
    for step in range(1, group):
        gain_copy(step).wait_recv()
    gains = jnp.concatenate([gain_all[shard][:, :own] for shard in range(group)], axis=1)
    gain_attn_ref[...] = gains[:1]
    gain_ffn_ref[...] = gains[1:2]
    normed_ref[...] = (inputs * scale * gains[:1]).astype(jnp.bfloat16)
    cosine, sine = cos_ref[...], sin_ref[...]

    def turn(columns):
        first, second = columns[: HD // 2], columns[HD // 2 :]
        return jnp.concatenate(
            [first * cosine - second * sine, second * cosine + first * sine], axis=0
        ).astype(jnp.bfloat16)

    def block_copy(level, part, side, semaphores, arrivals, arrives, device):
        block = 2 * (steps.level - level) + side
        held = all_ref.at[block, pl.ds(part * per_part, per_part)]
        return pltpu.make_async_remote_copy(
            src_ref=held,
            dst_ref=held,
            send_sem=semaphores.at[level, part],
            recv_sem=arrivals.at[arrives, part],
            device_id=device,
            device_id_type=MESH,
        )

    def chain(level, part):
        return block_copy(
            level, part, steps.side, chain_sends, chain_arrivals, level + 1, steps.above
        )

    def across(level, part):
        return block_copy(
            level, part, steps.side, peer_sends, peer_arrivals, level, steps.peer
        )

    def pass_on(level, part):
        @pl.when(steps.has_above)
        def _():
            chain(level, part).start()

    def project(at):
        _, weight, start = pieces[at]
        made = forward_dot(normed_ref[...], weight[:, start : start + span])
        if at == 0:
            key_rows[...] = made
            return
        for sequence in range(sequences):
            block = slice(sequence * keys, (sequence + 1) * keys)
            for pair in range(span // (2 * HD)):
                columns = slice(pair * 2 * HD, (pair + 1) * 2 * HD)
                turned = made[block, columns].T
                if at == 1:
                    turned_keys = key_rows[block, columns].T
                    for half in range(2):
                        held = slice(half * HD, (half + 1) * HD)
                        both = jnp.concatenate(
                            [turn(turned_keys[held]), turned[held].astype(jnp.bfloat16)], axis=0
                        )
                        all_ref[ctx, sequence * KVH + 2 * pair + half] = both.T
                else:
                    for half in range(2):
                        head = start // HD + 2 * pair + half
                        unit, member = sequence * KVH + head // groups, head % groups
                        part = turn(turned[half * HD : (half + 1) * HD])
                        q_ref[unit, :HD, member * keys : (member + 1) * keys] = part * jnp.bfloat16(
                            HD ** (-0.5)
                        )
        if at == 1:
            for part in range(PARTS):
                pass_on(0, part)

                @pl.when(steps.side == 0)
                def _():
                    across(0, part).start()

    columns = my_gate_ref.shape[1]
    gathered = HalfGather(full_out_ref, own, out_sends.at[0], out_arrivals.at[0])
    gathered_g = GroupGather(lambda shard: all_g_ref.at[shard], g_sends, g_arrivals)
    mine = lane_tile(fsdp, columns)
    own_parts = (
        (out_ref, own_out, full_out_ref.at[own_rows]),
        (gate_ref.at[:, mine], own_gate, my_gate_ref.at[own_rows]),
        (up_ref.at[:, mine], own_up, my_up_ref.at[own_rows]),
    )
    own_g_copy = pltpu.make_async_copy(own_g, all_g_ref.at[fsdp], local_sems.at[3])
    loads = [
        pltpu.make_async_copy(source, held, local_sems.at[at])
        for at, (source, held, _) in enumerate(own_parts)
    ]
    background = [
        pltpu.make_async_copy(held, target, local_sems.at[at])
        for at, (_, held, target) in enumerate(own_parts)
    ]
    slices = []
    for which, (source, target) in enumerate(((gate_ref, my_gate_ref), (up_ref, my_up_ref))):
        for step in range(1, group):
            peer = lax.rem(fsdp + step, group)
            slices.append(
                pltpu.make_async_remote_copy(
                    src_ref=source.at[:, lane_tile(peer, columns)],
                    dst_ref=target.at[own_rows],
                    send_sem=part_sends.at[which, step - 1],
                    recv_sem=part_arrivals.at[which, step - 1],
                    device_id=(peer, ctx),
                    device_id_type=MESH,
                )
            )

    def start_background():
        for copy in loads:
            copy.start()
        gathered.start(out_ref)
        for copy in slices:
            copy.start()
        gathered_g.start(own_g)
        own_g_copy.start()

    last = len(pieces)
    for at in range(last + 2):
        if at < last:
            gathers[at][0].to_pairs()
        if at == 0:
            start_background()
        if 1 <= at <= last:
            gathers[at - 1][0].to_sibling()
        if at == 1:
            for column in range(width // LANES):
                columns = slice(column * LANES, (column + 1) * LANES)
                normed_t_ref[columns, :] = normed_ref[:, columns].T
            for copy in own_copies:
                copy.wait()
        if at >= 2:
            gathers[at - 2][0].arrived()
            project(at - 2)

    def second_half():
        gathered.to_pairs()
        for load, copy in zip(loads, background):
            load.wait()
            copy.start()

    def add(unit, kv):
        scores = jnp.dot(kv, q_ref[unit], preferred_element_type=jnp.float32)
        top = top_ref[unit]
        new_top = jnp.maximum(top, jnp.max(scores, axis=0, keepdims=True))
        fade = jnp.exp(top - new_top)
        weights = jnp.exp(scores - new_top)
        top_ref[unit] = new_top
        total_ref[unit] = total_ref[unit] * fade + jnp.sum(weights, axis=0, keepdims=True)
        added = jnp.dot(kv.T, weights.astype(jnp.bfloat16), preferred_element_type=jnp.float32)
        mix_ref[unit] = mix_ref[unit] * fade + added[HD:]

    def over_units(body, first, count):
        def two(at, unused):
            body(first + 2 * at)
            body(first + 2 * at + 1)
            return unused

        lax.fori_loop(0, count // 2, two, 0)

    def diagonal(unit):
        kv = all_ref[ctx, unit]
        scores = jnp.dot(kv, q_ref[unit], preferred_element_type=jnp.float32)
        scores = jnp.where(causal(keys, wide, scores.shape), scores, MASKED_SCORE)
        top = jnp.max(scores, axis=0, keepdims=True)
        weights = jnp.exp(scores - top)
        top_ref[unit] = top
        total_ref[unit] = jnp.sum(weights, axis=0, keepdims=True)
        added = jnp.dot(kv.T, weights.astype(jnp.bfloat16), preferred_element_type=jnp.float32)
        mix_ref[unit] = added[HD:]

    over_units(diagonal, 0, units)

    def forward(level, part):
        chain(level - 1, part).wait_recv()
        pass_on(level, part)
        across(level, part).start()

    @pl.when(steps.level >= 1)
    def _():
        for part in range(PARTS):
            forward(1, part)

    @pl.when(steps.side == 1)
    def _():
        for part in range(PARTS):
            across(0, part).wait_recv()
            over_units(lambda unit: add(unit, all_ref[ctx - 1, unit]), part * per_part, per_part)

    def level_step(level, unused):
        first = 2 * (steps.level - level)
        for part in range(PARTS):

            @pl.when(level < steps.level)
            def _():
                forward(level + 1, part)

            across(level, part).wait_recv()
            over_units(
                lambda unit: add(unit, all_ref[pl.ds(first, 2), unit].reshape(2 * keys, deep)),
                part * per_part,
                per_part,
            )

        @pl.when(level == 1)
        def _():
            second_half()

        return unused

    @pl.when(steps.level == 0)
    def _():
        second_half()

    lax.fori_loop(1, steps.level + 1, level_step, 0)

    def close(unit):
        total = total_ref[unit]
        mix_ref[unit] = mix_ref[unit] / total
        log_ref[unit] = top_ref[unit] + jnp.log(total)

    over_units(close, 0, units)
    for sequence in range(sequences):
        for pair in range(H // 2):
            heads = []
            for head in (2 * pair, 2 * pair + 1):
                unit, member = sequence * KVH + head // groups, head % groups
                heads.append(mix_ref[unit, :, member * keys : (member + 1) * keys])
            tile = jnp.concatenate(heads, axis=0).astype(low_ref.dtype)
            block = slice(sequence * keys, (sequence + 1) * keys)
            columns = slice(pair * 2 * HD, (pair + 1) * 2 * HD)
            low_t_ref[columns, block] = tile
            low_ref[block, columns] = tile.T
    for gather, _ in gathers:
        gather.sent()
    for step in range(1, group):
        gain_copy(step).wait_send()
    gathered.to_sibling()
    gathered_g.forward()
    gathered.arrived()
    gathered.sent()
    gathered_g.sibling_here()
    for step in range(1, gathered_g.chips):
        gathered_g.crossed(step)
    gathered_g.sent()
    for copy in slices:
        copy.wait()
    own_g_copy.wait()
    for copy in background:
        copy.wait()

    def sent(level, unused):
        for part in range(PARTS):

            @pl.when(steps.has_above)
            def _():
                chain(level, part).wait_send()

            @pl.when(jnp.logical_or(level > 0, steps.side == 0))
            def _():
                across(level, part).wait_send()

        return unused

    lax.fori_loop(0, steps.level + 1, sent, 0)


ANY = pl.BlockSpec(memory_space=pl.ANY)
VMEM = pl.BlockSpec(memory_space=pltpu.VMEM)


def attend(tokens, upstream, gains, cosine, sine, w_query, w_key, w_value, w_out, w_gate, w_up):
    group, count = lax.axis_size("fsdp"), lax.axis_size("ctx")
    keys, sequences, width = tokens.shape
    own, hidden = w_query.shape[0], w_gate.shape[1] // group
    rows, units, deep = keys * sequences, sequences * KVH, 2 * HD
    wide = H // KVH * keys
    kv_width = KVH * HD
    dma = pltpu.SemaphoreType.DMA
    bf16, f32 = jnp.bfloat16, jnp.float32
    pieces = 2 + width // kv_width
    return pl.pallas_call(
        attend_kernel,
        out_shape=[
            jax.ShapeDtypeStruct((rows, width), bf16),
            jax.ShapeDtypeStruct((units, deep, wide), bf16),
            jax.ShapeDtypeStruct((width, rows), bf16),
            jax.ShapeDtypeStruct((1, width), f32),
            jax.ShapeDtypeStruct((1, width), f32),
            jax.ShapeDtypeStruct((width, width), bf16),
            jax.ShapeDtypeStruct((width, kv_width), bf16),
            jax.ShapeDtypeStruct((width, kv_width), bf16),
            jax.ShapeDtypeStruct((rows, width), bf16),
            jax.ShapeDtypeStruct((width, rows), bf16),
            jax.ShapeDtypeStruct((units, HD, wide), f32),
            jax.ShapeDtypeStruct((units, 1, wide), f32),
            jax.ShapeDtypeStruct((count, units, keys, deep), bf16),
            jax.ShapeDtypeStruct((width, width), bf16),
            jax.ShapeDtypeStruct((width, hidden), bf16),
            jax.ShapeDtypeStruct((width, hidden), bf16),
            jax.ShapeDtypeStruct((group, rows, width), bf16),
        ],
        in_specs=[VMEM] * 5 + [ANY] * 6,
        out_specs=[VMEM] * 13 + [ANY] * 4,
        scratch_shapes=[
            pltpu.VMEM((rows, width), bf16),
            pltpu.VMEM((rows, kv_width), f32),
            pltpu.VMEM((group,) + gains.shape, f32),
            pltpu.VMEM((own, width), bf16),
            pltpu.VMEM((own, hidden), bf16),
            pltpu.VMEM((own, hidden), bf16),
            pltpu.VMEM((rows, width), bf16),
            pltpu.VMEM((units, 1, wide), f32),
            pltpu.VMEM((units, 1, wide), f32),
            dma((count // 2, PARTS)),
            dma((count // 2 + 1, PARTS)),
            dma((count // 2, PARTS)),
            dma((count // 2, PARTS)),
            half_semaphores(pieces),
            half_semaphores(pieces),
            *[dma((group - 1,))] * 2,
            *[half_semaphores(1)] * 2,
            *[group_semaphores()] * 2,
            *[dma((2, group - 1))] * 2,
            dma((7,)),
        ],
        compiler_params=pltpu.CompilerParams(
            collective_id=1, has_side_effects=True, vmem_limit_bytes=60 << 20
        ),
    )(tokens, upstream, gains, cosine, sine, w_query, w_key, w_value, w_out, w_gate, w_up)


class Ring:
    def __init__(self, work, landing, total, semaphores, forward, exchange=False):
        self.fsdp, self.ctx = lax.axis_index("fsdp"), lax.axis_index("ctx")
        self.group, self.count = lax.axis_size("fsdp"), lax.axis_size("ctx")
        self.work, self.landing, self.total = work, landing, total
        self.sends, self.arrivals = semaphores[:2]
        self.part_sends, self.part_arrivals, self.own_sem = semaphores[2:] if exchange else (None,) * 3
        self.exchange = exchange
        side = 0 if forward else 1
        self.place = ring_place(self.ctx, side, self.count)
        self.after = (self.fsdp, ring_ctx(lax.rem(self.place + 1, self.count), side, self.count))
        self.ticks = 2 * self.count - 2 + int(exchange)

    def chunk(self, held, index):
        if self.exchange:
            return held.at[index]
        per = held.shape[0] // self.count
        return held.at[pl.ds(index * per, per)]

    def summing(self, step, index):
        return self.copy(self.chunk(self.work, index), self.landing.at[step], step)

    def handing(self, step, index):
        held = self.chunk(self.total, index)
        return self.copy(held, held, step)

    def copy(self, source, target, step):
        return pltpu.make_async_remote_copy(
            src_ref=source,
            dst_ref=target,
            send_sem=self.sends.at[step],
            recv_sem=self.arrivals.at[step],
            device_id=self.after,
            device_id_type=MESH,
        )

    def part(self, index, step):
        peer = lax.rem(self.fsdp + step, self.group)
        return pltpu.make_async_remote_copy(
            src_ref=self.work.at[index, peer],
            dst_ref=self.total.at[index, self.fsdp],
            send_sem=self.part_sends.at[step - 1],
            recv_sem=self.part_arrivals.at[step - 1],
            device_id=(peer, self.ctx),
            device_id_type=MESH,
        )

    def own_part(self, index):
        return pltpu.make_async_copy(
            self.work.at[index, self.fsdp], self.total.at[index, self.fsdp], self.own_sem
        )

    def start(self):
        self.summing(0, self.place).start()

    def tick(self, at):
        last = self.count - 2
        gap = int(self.exchange)
        step = at - gap * jnp.where(at > last, 1, 0) if self.exchange else at
        index = lax.rem(self.place + 3 * self.count - 1 - step, self.count)

        def add(target):
            part, landed = self.chunk(self.work, index), self.landing.at[jnp.minimum(at, last)]
            for row in range(part.shape[0]):
                target[row] = (
                    part[row].astype(jnp.float32) + landed[row].astype(jnp.float32)
                ).astype(part.dtype)

        @pl.when(at <= last)
        def _():
            self.summing(jnp.minimum(at, last), index).wait_recv()

        @pl.when(at < last)
        def _():
            add(self.chunk(self.work, index))
            self.summing(jnp.minimum(at + 1, last), index).start()

        if self.exchange:

            @pl.when(at == last)
            def _():
                add(self.chunk(self.work, index))
                for peer in range(1, self.group):
                    self.part(index, peer).start()
                self.own_part(index).start()

            @pl.when(at == last + 1)
            def _():
                done = lax.rem(self.place + 1, self.count)
                self.own_part(done).wait()
                for peer in range(1, self.group):
                    self.part(done, peer).wait_recv()
                self.handing(last + 1, done).start()

        else:

            @pl.when(at == last)
            def _():
                add(self.chunk(self.total, index))
                self.handing(last + 1, index).start()

        @pl.when(at > last + gap)
        def _():
            here = jnp.maximum(step, last + 1)
            self.handing(here, index).wait_recv()

            @pl.when(here < 2 * self.count - 3)
            def _():
                self.handing(jnp.minimum(here + 1, 2 * self.count - 3), index).start()

    def finish(self):
        def wait(step, unused):
            self.handing(step, self.place).wait_send()
            return unused

        lax.fori_loop(0, 2 * self.count - 2, wait, 0)
        if self.exchange:
            for peer in range(1, self.group):
                self.part(lax.rem(self.place + 1, self.count), peer).wait_send()


class SumRing(Ring):
    def __init__(self, *args):
        super().__init__(*args)
        self.ticks = self.count - 1

    def tick(self, at):
        last = self.count - 2
        index = lax.rem(self.place + 2 * self.count - 1 - at, self.count)
        self.summing(at, index).wait_recv()
        work, landed = self.chunk(self.work, index), self.landing.at[at]

        def add(target):
            for row in range(work.shape[0]):
                target[row] = (
                    work[row].astype(jnp.float32) + landed[row].astype(jnp.float32)
                ).astype(work.dtype)

        @pl.when(at < last)
        def _():
            add(work)
            self.summing(jnp.minimum(at + 1, last), index).start()

        @pl.when(at == last)
        def _():
            add(self.total)

    def finish(self):
        def wait(step, unused):
            self.summing(step, self.place).wait_send()
            return unused

        lax.fori_loop(0, self.ticks, wait, 0)


class SpreadRing(Ring):
    def __init__(self, total, semaphores, forward):
        super().__init__(None, None, total, semaphores, forward)
        self.ticks = self.count - 1
        self.first = lax.rem(self.place + 1, self.count)

    def start(self):
        self.handing(0, self.first).start()

    def tick(self, at):
        index = lax.rem(self.place + self.count - at, self.count)
        self.handing(at, index).wait_recv()

        @pl.when(at < self.count - 2)
        def _():
            self.handing(jnp.minimum(at + 1, self.count - 2), index).start()

    def finish(self):
        def wait(step, unused):
            self.handing(step, self.place).wait_send()
            return unused

        lax.fori_loop(0, self.ticks, wait, 0)


def ring_scratch(chunk, exchange=False):
    count = lax.axis_size("ctx")
    work = (count,) + chunk if exchange else (count * chunk[0],) + chunk[1:]
    return [pltpu.VMEM(work, jnp.bfloat16), pltpu.VMEM((count - 1,) + chunk, jnp.bfloat16)]


def ring_total(chunk, exchange=False):
    count = lax.axis_size("ctx")
    work = (count,) + chunk if exchange else (count * chunk[0],) + chunk[1:]
    return jax.ShapeDtypeStruct(work, jnp.bfloat16)


def ring_semaphores(exchange=False):
    dma, steps = pltpu.SemaphoreType.DMA, 2 * lax.axis_size("ctx") - 2
    parts = lax.axis_size("fsdp") - 1
    return [dma((steps,))] * 2 + ([dma((parts,))] * 2 + [dma] if exchange else [])


def wide_split(width):
    group, count = lax.axis_size("fsdp"), lax.axis_size("ctx")
    return 2 if FF // group // LANES * (width // group // 16) >= 4 * count else 1


def query_split(width):
    return width // LANES * 7 // 9 * LANES


def out_split(width):
    return (width // LANES + 1) // 2 * LANES


def down_split(blocks, count):
    each = -(-blocks // count)
    rings = 4 if each >= 4 else 2
    return [max(1, (each + at) // rings) for at in range(rings)]


class GroupScatter:
    def __init__(self, give_sib, got_sib, give_cross, got_cross, far, got_far, sends, arrivals):
        self.give_sib, self.got_sib = give_sib, got_sib
        self.give_cross, self.got_cross = give_cross, got_cross
        self.far, self.got_far = far, got_far
        self.sends, self.arrivals = sends, arrivals
        self.fsdp, self.ctx = lax.axis_index("fsdp"), lax.axis_index("ctx")
        self.chips = lax.axis_size("fsdp") // 2
        self.chip, self.core = lax.div(self.fsdp, 2), lax.rem(self.fsdp, 2)
        self.sibling = 2 * self.chip + 1 - self.core

    def copy(self, source, target, semaphore, device):
        return pltpu.make_async_remote_copy(
            src_ref=source,
            dst_ref=target,
            send_sem=self.sends.at[semaphore],
            recv_sem=self.arrivals.at[semaphore],
            device_id=(device, self.ctx),
            device_id_type=MESH,
        )

    def to_sibling(self):
        return self.copy(self.give_sib, self.got_sib, 0, self.sibling)

    def to_cross(self, step):
        return self.copy(
            self.give_cross(step), self.got_cross.at[step - 1], step, self.sibling
        )

    def to_far(self, step):
        chip = lax.rem(self.chip + self.chips - step, self.chips)
        return self.copy(
            self.far.at[step - 1],
            self.got_far.at[step - 1],
            self.chips - 1 + step,
            2 * chip + self.core,
        )

    def add_cross(self, step):
        self.to_cross(step).wait_recv()
        held = self.far.at[step - 1]
        held[...] = (
            held[...].astype(jnp.float32) + self.got_cross[step - 1].astype(jnp.float32)
        ).astype(held.dtype)
        self.to_far(step).start()

    def total(self, own):
        self.to_sibling().wait_recv()
        value = own + self.got_sib[...].astype(jnp.float32)
        for step in range(1, self.chips):
            self.to_far(step).wait_recv()
            value = value + self.got_far[step - 1].astype(jnp.float32)
        return value

    def sent(self):
        self.to_sibling().wait_send()
        for step in range(1, self.chips):
            self.to_cross(step).wait_send()
            self.to_far(step).wait_send()


def scatter_scratch(rows, width):
    far = lax.axis_size("fsdp") // 2 - 1
    one, many = (rows, width), (far, rows, width)
    return [pltpu.VMEM(shape, jnp.bfloat16) for shape in (one, one, many, many, many, many)]


def dot_columns(left, right):
    return lax.dot_general(
        left, right, (((1,), (1,)), ((), ())), preferred_element_type=jnp.float32
    )


def tiles(count, body):
    def step(at, unused):
        body(at)
        return unused

    lax.fori_loop(0, count, step, 0)


def lane_tile(at, size):
    return pl.ds(pl.multiple_of(at * size, LANES), size)


def width_tile(width):
    return 384 if width % 384 == 0 else width


def hidden_tile(hidden):
    return 256 if hidden % 256 == 0 else 128


def transpose_into(target, source):
    rows, columns = source.shape

    def body(at):
        part = source[:, lane_tile(at, LANES)]
        target[pl.ds(pl.multiple_of(at * LANES, LANES), LANES), :] = part.T

    tiles(columns // LANES, body)


def ffn_kernel(
    x_ref, low_ref, out_ref, gain_ref, gate_in, up_in, down_in, all_g_in,
    layer_ref, resid_grad_ref, branch_ref, g_wide_ref, gate_part_out, up_part_out, layer_part_out,
    *rest,
):
    downs = len(down_split(gate_in.shape[1] // 16, lax.axis_size("ctx")))
    taken = iter(rest)

    def take(number):
        return [next(taken) for _ in range(number)]

    down_done, (gain_grad_ref,) = take(downs), take(1)
    all_n_ref, turned_n, turned_act, act_ref, gate_grad, up_grad, resid_ref, grad_own = take(8)
    down_scratch = take(2 * downs)
    give_sib, got_sib, give_cross, got_cross, far, got_far = take(6)
    n_sends, n_arrivals, grad_sends, grad_arrivals = take(4)
    gate_ref, up_ref, down_ref, all_g_ref, gate_part_ref, up_part_ref, layer_part_ref = take(7)
    (local_sems,) = take(1)
    loads = [
        pltpu.make_async_copy(source, target, local_sems.at[at])
        for at, (source, target) in enumerate(
            ((gate_in, gate_ref), (up_in, up_ref), (all_g_in, all_g_ref), (down_in, down_ref))
        )
    ]
    for copy in loads:
        copy.start()
    stores = []

    def store(source, target):
        copy = pltpu.make_async_copy(source, target, local_sems.at[len(loads) + len(stores)])
        copy.start()
        stores.append(copy)

    rings = [
        SumRing(*down_scratch[2 * at : 2 * at + 2], down_done[at], take(2), at % 2 == 0)
        for at in range(downs)
    ]
    group = lax.axis_size("fsdp")
    rows, width = x_ref.shape
    hidden = gate_ref.shape[1]
    barrier = pltpu.get_barrier_semaphore()
    greeted = greet_group(barrier) + 2
    for ring in rings[:2]:
        pl.semaphore_signal(barrier, inc=1, device_id=ring.after, device_id_type=MESH)
    step_in, step_out = hidden_tile(hidden), width_tile(width)

    def branch(at):
        columns = lane_tile(at, step_out)
        resid_ref[:, columns] = x_ref[:, columns].astype(jnp.float32) + forward_dot(
            low_ref[...], out_ref[:, columns]
        )

    tiles(width // step_out, branch)
    gain = gain_ref[...]
    scale = norm_scale(resid_ref[...])
    gathered = GroupGather(lambda shard: all_n_ref.at[shard], n_sends, n_arrivals)
    fsdp, chips = gathered.fsdp, gathered.chips
    all_n_ref[fsdp] = (resid_ref[...] * scale * gain).astype(jnp.bfloat16)
    pl.semaphore_wait(barrier, greeted)
    gathered.start(all_n_ref.at[fsdp])
    grad_sum = GroupScatter(
        give_sib,
        got_sib,
        lambda step: give_cross.at[step - 1],
        got_cross,
        far,
        got_far,
        grad_sends,
        grad_arrivals,
    )

    def hidden_part(shard):
        def body(at):
            columns = lane_tile(at, step_in)
            normed = all_n_ref[shard]
            gate = forward_dot(normed, gate_ref[:, columns])
            upward = forward_dot(normed, up_ref[:, columns])
            grad_act = dot_columns(
                all_g_ref[shard], down_ref[pl.ds(pl.multiple_of(at * step_in, LANES), step_in), :]
            )
            sigmoid = jax.nn.sigmoid(gate)
            silu = gate * sigmoid
            act_ref[shard, :, columns] = (silu * upward).astype(jnp.bfloat16)
            gate_grad[shard, :, columns] = (
                grad_act * upward * (sigmoid * (1.0 + gate * (1.0 - sigmoid)))
            ).astype(jnp.bfloat16)
            up_grad[shard, :, columns] = (grad_act * silu).astype(jnp.bfloat16)

        tiles(hidden // step_in, body)

    def grad_part(shard, target):
        def body(at):
            columns = pl.ds(pl.multiple_of(at * step_out, LANES), step_out)
            target[:, columns] = (
                dot_columns(gate_grad[shard], gate_ref[columns, :])
                + dot_columns(up_grad[shard], up_ref[columns, :])
            ).astype(target.dtype)

        tiles(width // step_out, body)

    for copy in loads:
        copy.wait()
    hidden_part(fsdp)
    gathered.sibling_here()
    sibling = gathered.sibling
    hidden_part(sibling)
    grad_part(sibling, grad_sum.give_sib)
    grad_sum.to_sibling().start()
    gathered.forward()
    grad_part(fsdp, grad_own)
    def turn_act(shard):
        transpose_into(turned_act.at[:, lane_tile(shard, rows)], act_ref.at[shard])

    turn_act(fsdp)
    turn_act(sibling)
    far_shards = []
    for step in range(1, chips):
        ours = gathered.same_core(chips - step)
        theirs = ours + sibling - fsdp
        far_shards.append((step, ours, theirs))
        gathered.crossed(step)
        hidden_part(theirs)
        hidden_part(ours)
        turn_act(theirs)
        turn_act(ours)
    blocks = hidden // 16
    spans, first = [], 0
    for ring in rings:
        last = min(blocks, first + ring.work.shape[0])
        spans.append((first, last, ring.work))
        first = last

    def down_tile(at):
        columns = lane_tile(at, step_out)
        part = forward_dot(
            turned_act[...], all_g_ref[:, :, columns].reshape(group * rows, step_out)
        ).astype(jnp.bfloat16)
        for begin, end, work in spans:
            if end > begin:
                work[: end - begin, :, columns] = part[begin * 16 : end * 16].reshape(
                    end - begin, 16, step_out
                )

    tiles(width // step_out, down_tile)
    for begin, end, work in spans:
        for spare in range(end - begin, work.shape[0]):
            work[spare] = jnp.zeros(work.shape[1:], work.dtype)
    for ring in rings:
        ring.start()
    for step, ours, theirs in far_shards:
        grad_part(theirs, give_cross.at[step - 1])
        grad_sum.to_cross(step).start()
        grad_part(ours, far.at[step - 1])
        grad_sum.add_cross(step)
    ticked = [0]

    def ring_tick(at):
        for ring in rings:

            @pl.when(at < ring.ticks)
            def _():
                ring.tick(jnp.minimum(at, ring.ticks - 1))

    def ticking(times, body):
        begin = ticked[0]

        def step(at):
            body(at)
            ring_tick(begin + at)

        tiles(times, step)
        ticked[0] += times

    for shard in range(group):
        span = slice(shard * rows, (shard + 1) * rows)
        transpose_into(turned_n.at[:, span], all_n_ref.at[shard])
    own = width // group
    row_blocks = own // 16
    for source, target in ((gate_grad, gate_part_ref), (up_grad, up_part_ref)):

        def weight_tile(at):
            columns = lane_tile(at, step_in)
            part = forward_dot(
                turned_n[...], source[:, :, columns].reshape(group * rows, step_in)
            ).astype(jnp.bfloat16)
            for block in range(step_in // LANES):
                first = (at * (step_in // LANES) + block) * row_blocks
                for owner in range(group):
                    target[owner, pl.ds(first, row_blocks)] = part[
                        owner * own : (owner + 1) * own, block * LANES : (block + 1) * LANES
                    ].reshape(row_blocks, 16, LANES)

        ticking(hidden // step_in, weight_tile)
        filled = hidden // LANES * row_blocks
        for spare in range(filled, target.shape[1]):
            for owner in range(group):
                target[owner, spare] = jnp.zeros(target.shape[2:], target.dtype)
        store(target, gate_part_out if source is gate_grad else up_part_out)

    def layer_tile(at):
        columns = lane_tile(at, step_out)
        part = forward_dot(
            act_ref[...].reshape(group * rows, hidden), down_ref[:, columns]
        ).reshape(group, rows, step_out)
        layer_part_ref[:, :, columns] = part.astype(jnp.bfloat16)

    ticking(width // step_out, layer_tile)
    store(layer_part_ref, layer_part_out)
    layer_ref[...] = resid_ref[...] + layer_part_ref[fsdp].astype(jnp.float32)
    upstream = grad_sum.total(grad_own[...])
    resid = resid_ref[...]
    scaled = upstream * gain
    grad_resid = (
        all_g_ref[fsdp].astype(jnp.float32)
        + scale * scaled
        - resid * scale**3 * jnp.mean(scaled * resid, axis=-1, keepdims=True)
    )
    gain_grad_ref[...] = jnp.sum(upstream * resid * scale, axis=0, keepdims=True)
    resid_grad_ref[...] = grad_resid
    branch_ref[...] = grad_resid.astype(jnp.bfloat16)
    units, _, wide = g_wide_ref.shape
    sequences = units // KVH
    keys = rows // sequences
    groups = wide // keys
    g_wide_ref[:, :HD, :] = jnp.zeros((units, HD, wide), g_wide_ref.dtype)
    for pair in range(H // 2):
        columns = slice(pair * 2 * HD, (pair + 1) * 2 * HD)
        mixed = dot_columns(branch_ref[...], out_ref[columns, :]).astype(jnp.bfloat16)
        for sequence in range(sequences):
            turned = mixed[sequence * keys : (sequence + 1) * keys].T
            for half in range(2):
                head = 2 * pair + half
                unit, member = sequence * KVH + head // groups, head % groups
                g_wide_ref[unit, HD:, member * keys : (member + 1) * keys] = turned[
                    half * HD : (half + 1) * HD
                ]
    begin = ticked[0]
    tiles(max(0, rings[0].ticks - begin), lambda at: ring_tick(begin + at))
    gathered.sent()
    grad_sum.sent()
    for ring in rings:
        ring.finish()
    for copy in stores:
        copy.wait()


def spread(blocks, count):
    return -(-blocks // count) * count


def feed_forward(x, low, full_out, my_gate, my_up, my_down, all_g, gain, units, wide):
    group, count = lax.axis_size("fsdp"), lax.axis_size("ctx")
    rows, width = x.shape
    hidden = my_gate.shape[1]
    blocks = spread(hidden // LANES * (width // group // 16), wide_split(width) * count)
    chips = group // 2
    dma = pltpu.SemaphoreType.DMA((2 * chips - 1,))
    bf16 = jnp.bfloat16
    down_chunks = [(per, 16, width) for per in down_split(hidden // 16, count)]
    return pl.pallas_call(
        ffn_kernel,
        out_shape=[
            jax.ShapeDtypeStruct((rows, width), jnp.float32),
            jax.ShapeDtypeStruct((rows, width), jnp.float32),
            jax.ShapeDtypeStruct((rows, width), bf16),
            jax.ShapeDtypeStruct((units, 2 * HD, wide), bf16),
            jax.ShapeDtypeStruct((group, blocks, 16, LANES), bf16),
            jax.ShapeDtypeStruct((group, blocks, 16, LANES), bf16),
            jax.ShapeDtypeStruct((group, rows, width), bf16),
            *[jax.ShapeDtypeStruct(chunk, bf16) for chunk in down_chunks],
            jax.ShapeDtypeStruct((1, width), jnp.float32),
        ],
        in_specs=[VMEM] * 4 + [ANY] * 4,
        out_specs=[VMEM] * 4 + [ANY] * 3 + [VMEM] * (1 + len(down_chunks)),
        scratch_shapes=[
            pltpu.VMEM((group, rows, width), bf16),
            pltpu.VMEM((width, group * rows), bf16),
            pltpu.VMEM((hidden, group * rows), bf16),
            pltpu.VMEM((group, rows, hidden), bf16),
            pltpu.VMEM((group, rows, hidden), bf16),
            pltpu.VMEM((group, rows, hidden), bf16),
            pltpu.VMEM((rows, width), jnp.float32),
            pltpu.VMEM((rows, width), jnp.float32),
            *[kind for chunk in down_chunks for kind in ring_scratch(chunk)],
            *scatter_scratch(rows, width),
            *[dma] * 4,
            pltpu.VMEM(my_gate.shape, bf16),
            pltpu.VMEM(my_up.shape, bf16),
            pltpu.VMEM(my_down.shape, bf16),
            pltpu.VMEM(all_g.shape, bf16),
            pltpu.VMEM((group, blocks, 16, LANES), bf16),
            pltpu.VMEM((group, blocks, 16, LANES), bf16),
            pltpu.VMEM((group, rows, width), bf16),
            pltpu.SemaphoreType.DMA((7,)),
            *[kind for _ in down_chunks for kind in ring_semaphores()],
        ],
        compiler_params=pltpu.CompilerParams(
            collective_id=2, has_side_effects=True, vmem_limit_bytes=60 << 20
        ),
    )(x, low, full_out, gain, my_gate, my_up, my_down, all_g)


def back_kernel(
    down_blocks, q_ref, g_ref, log_ref, gain_grad_ref, gain_ref, cos_ref, sin_ref,
    pairs_ref, mix_in, gate_ref, up_ref, layer_base_in, layer_part_ref, branch_ref, low_t_ref,
    normed_t_ref, w_query_in, w_key_in, w_value_in, x_in, resid_grad_in, *rest,
):
    taken = iter(rest)

    def take(number):
        return [next(taken) for _ in range(number)]

    halves, downs = wide_split(x_in.shape[1]), len(down_blocks)
    down_refs = take(downs)
    tokens_ref, layer_ref = take(2)
    wide_totals, down_totals = take(2 * halves), take(downs)
    out_a_total, out_b_total, rest_a_total, rest_b_total = take(4)
    peer_got, chain_got, layer_sib, layer_cross, layer_far = take(5)
    kv_ref, stage_ref, final_ref, qg_ref, delta_ref, grad_q_ref = take(6)
    wide_scratch = take(4 * halves)
    out_a_work, out_a_land, out_b_work, out_b_land = take(4)
    rest_a_work, rest_a_land, rest_b_work, rest_b_land = take(4)
    low_all, normed_all, branch_all, query_all, pair_all, upstream_ref, gain_give, gain_got = take(8)
    far_ref, layer_stage = take(2)
    mix_ref, layer_base_ref, w_query_ref, w_key_ref, w_value_ref, x_ref, resid_grad_ref = take(7)
    steps = Steps()
    fsdp, ctx, group, count = steps.fsdp, steps.ctx, lax.axis_size("fsdp"), lax.axis_size("ctx")
    units, deep, wide = q_ref.shape
    keys = pairs_ref.shape[2]
    rows, width = x_ref.shape
    own = width // group
    wide_rings = [
        Ring(*wide_scratch[2 * at : 2 * at + 2], wide_totals[at], take(5), at < halves, True)
        for at in range(2 * halves)
    ]
    down_rings = [SpreadRing(total, take(2), at % 2 == 0) for at, total in enumerate(down_totals)]
    out_a = Ring(out_a_work, out_a_land, out_a_total, take(2), True)
    out_b = Ring(out_b_work, out_b_land, out_b_total, take(2), False)
    layer_sum = GroupScatter(
        None,
        layer_sib,
        lambda step: layer_part_ref.at[
            2 * lax.rem(lax.div(fsdp, 2) + group // 2 - step, group // 2) + 1 - lax.rem(fsdp, 2)
        ],
        layer_cross,
        far_ref,
        layer_far,
        *take(2),
    )
    layer_sum.give_sib = layer_part_ref.at[layer_sum.sibling]
    rest_a = Ring(rest_a_work, rest_a_land, rest_a_total, take(2), True)
    rest_b = Ring(rest_b_work, rest_b_land, rest_b_total, take(2), False)
    first_rings = []
    for at in range(halves):
        first_rings += [wide_rings[at], wide_rings[halves + at]]
        first_rings += down_rings[at * downs // halves : (at + 1) * downs // halves]
    begun_rings = len(first_rings)
    first_rings += [out_a, out_b]
    peer_sends, peer_arrivals, chain_sends, chain_arrivals = take(4)
    branch_gather = GroupGather(lambda shard: branch_all.at[shard], *take(2))
    query_gather = GroupGather(lambda shard: query_all.at[shard], *take(2))
    pair_gather = GroupGather(lambda shard: pair_all.at[shard], *take(2))
    low_sends, low_arrivals, normed_sends, normed_arrivals, gain_sends, gain_arrivals = take(6)
    local_sems, stage_sems = take(2)

    barrier = pltpu.get_barrier_semaphore()
    greeted = steps.greet(barrier) + greet_group(barrier) + 2
    for device in (out_a.after, out_b.after):
        pl.semaphore_signal(barrier, inc=1, device_id=device, device_id_type=MESH)

    loads = []

    def load(source, target):
        copy = pltpu.make_async_copy(source, target, local_sems.at[len(loads)])
        copy.start()
        loads.append(copy)

    n = wide_scratch[0].shape[2]
    for at, ring in enumerate(wide_rings):
        source = (gate_ref, up_ref)[at // halves]
        for chunk in range(count):
            load(source.at[:, pl.ds((at % halves * count + chunk) * n, n)], ring.work.at[chunk])
    for ring, source in zip(down_rings, down_refs):
        load(source, ring.chunk(ring.total, ring.first))
    ring_loads = len(loads)
    load(pairs_ref, kv_ref)
    load(mix_in, mix_ref)
    load(branch_ref, branch_all.at[fsdp])
    load(low_t_ref.at[pl.ds(fsdp * own, own)], low_all.at[:, lane_tile(fsdp, rows)])
    load(normed_t_ref.at[pl.ds(fsdp * own, own)], normed_all.at[:, lane_tile(fsdp, rows)])
    slot_loads = len(loads)
    for source, target in (
        (layer_base_in, layer_base_ref),
        (w_query_in, w_query_ref),
        (w_key_in, w_key_ref),
        (w_value_in, w_value_ref),
        (x_in, x_ref),
        (resid_grad_in, resid_grad_ref),
    ):
        load(source, target)
    for copy in loads[:ring_loads]:
        copy.wait()
    pl.semaphore_wait(barrier, greeted)
    for ring in first_rings[:begun_rings]:
        ring.start()
    branch_gather.start(branch_ref)
    layer_sum.to_sibling().start()
    for step in range(1, group // 2):
        layer_sum.to_cross(step).start()

    def slices(source, target, sends, arrivals, step):
        peer = lax.rem(fsdp + step, group)
        return pltpu.make_async_remote_copy(
            src_ref=source.at[pl.ds(peer * own, own)],
            dst_ref=target.at[:, lane_tile(fsdp, rows)],
            send_sem=sends.at[step - 1],
            recv_sem=arrivals.at[step - 1],
            device_id=(peer, ctx),
            device_id_type=MESH,
        )

    turned = [
        slices(*ends, step)
        for ends in (
            (low_t_ref, low_all, low_sends, low_arrivals),
            (normed_t_ref, normed_all, normed_sends, normed_arrivals),
        )
        for step in range(1, group)
    ]
    for copy in turned:
        copy.start()

    def prepare(unit):
        q, g = q_ref[unit], g_ref[unit]
        qg_ref[unit, :wide] = q.T
        qg_ref[unit, wide:] = g.T
        delta_ref[unit] = jnp.sum(
            g[HD:].astype(jnp.float32) * mix_ref[unit], axis=0, keepdims=True
        )
        grad_q_ref[unit] = jnp.zeros((HD, wide), jnp.float32)

    for copy in loads[ring_loads:slot_loads]:
        copy.wait()
    tiles(units, prepare)

    def tick(ring, at):
        @pl.when(jnp.logical_and(at >= 0, at < ring.ticks))
        def _():
            ring.tick(jnp.clip(at, 0, ring.ticks - 1))

    late = steps.levels // 2 + 1

    def pump(at):
        lag = [0] * begun_rings + [late, late]
        for turn, ring in enumerate(first_rings):

            @pl.when(lax.rem(at, len(first_rings)) == turn)
            def _():
                tick(ring, lax.div(at, len(first_rings)) - lag[turn])

    def back(unit, first, blocks, diagonal):
        kv = kv_ref[pl.ds(first, blocks), unit].reshape(blocks * keys, deep)
        scores = jnp.dot(kv, q_ref[unit], preferred_element_type=jnp.float32)
        probs = jnp.exp(scores - log_ref[unit])
        if diagonal:
            probs = jnp.where(causal(keys, wide, scores.shape), probs, 0.0)
        grad_probs = jnp.dot(kv, g_ref[unit], preferred_element_type=jnp.float32)
        grad_scores = (probs * (grad_probs - delta_ref[unit])).astype(jnp.bfloat16)
        both = jnp.concatenate([grad_scores, probs.astype(jnp.bfloat16)], axis=1)
        grad_kv = jnp.dot(both, qg_ref[unit], preferred_element_type=jnp.float32)
        added = jnp.dot(kv.T, grad_scores, preferred_element_type=jnp.float32)
        grad_q_ref[unit] = grad_q_ref[unit] + added[:HD]
        kv_ref[pl.ds(first, blocks), unit] = grad_kv.astype(kv_ref.dtype).reshape(
            blocks, keys, deep
        )

    def across(pair):
        return pltpu.make_async_remote_copy(
            src_ref=kv_ref.at[2 * pair + 1 - steps.side],
            dst_ref=peer_got.at[pair],
            send_sem=peer_sends.at[pair],
            recv_sem=peer_arrivals.at[pair],
            device_id=steps.peer,
            device_id_type=MESH,
        )

    def down_chain(pair):
        return pltpu.make_async_remote_copy(
            src_ref=kv_ref.at[2 * pair + steps.side],
            dst_ref=chain_got.at[pair],
            send_sem=chain_sends.at[pair],
            recv_sem=chain_arrivals.at[pair],
            device_id=steps.below,
            device_id_type=MESH,
        )

    def combine(time):
        pair = time - steps.levels + steps.level

        @pl.when(jnp.logical_and(pair >= 0, pair <= steps.level))
        def _():
            for slot, expected, arrival, source in (
                (0, jnp.logical_or(pair < steps.level, steps.side == 0), across, peer_got),
                (1, steps.has_above, down_chain, chain_got),
            ):

                @pl.when(expected)
                def _():
                    arrival(pair).wait_recv()
                    copy = pltpu.make_async_copy(
                        source.at[pair], stage_ref.at[slot], stage_sems.at[slot]
                    )
                    copy.start()
                    copy.wait()

                @pl.when(jnp.logical_not(expected))
                def _():
                    stage_ref[slot] = jnp.zeros(stage_ref.shape[1:], stage_ref.dtype)

            def add(unit):
                final_ref[unit] = (
                    kv_ref[2 * pair + steps.side, unit].astype(jnp.float32)
                    + stage_ref[0, unit].astype(jnp.float32)
                    + stage_ref[1, unit].astype(jnp.float32)
                )

            tiles(units, add)

            @pl.when(pair < steps.level)
            def _():
                kv_ref[2 * pair + steps.side] = final_ref[...].astype(kv_ref.dtype)
                down_chain(pair).start()

    row_blocks = own // 16

    def weight_grad(left, right, begin, end, target, first, loop):
        span = LANES * next(n for n in (3, 2, 1) if (end - begin) % (n * LANES) == 0)

        def body(at):
            columns = pl.ds(pl.multiple_of(begin + at * span, LANES), span)
            part = forward_dot(
                left[...], right[:, :, columns].reshape(group * rows, span)
            ).astype(jnp.bfloat16)
            for block in range(span // LANES):
                here = first + (at * (span // LANES) + block) * row_blocks
                target[pl.ds(here, row_blocks)] = part[
                    :, block * LANES : (block + 1) * LANES
                ].reshape(row_blocks, 16, LANES)

        loop((end - begin) // span, body)
        return first + (end - begin) // LANES * row_blocks

    def clear_from(target, first):
        for spare in range(first, target.shape[0]):
            target[spare] = jnp.zeros((16, LANES), jnp.bfloat16)

    def out_grad():
        for copy in turned[: group - 1]:
            copy.wait_recv()
        branch_gather.forward()
        branch_gather.sibling_here()
        for step in range(1, branch_gather.chips):
            branch_gather.crossed(step)
        split = out_split(width)
        clear_from(out_a_work, weight_grad(low_all, branch_all, 0, split, out_a_work, 0, tiles))
        clear_from(out_b_work, weight_grad(low_all, branch_all, split, width, out_b_work, 0, tiles))
        out_a.start()
        out_b.start()

    turns = units // 2
    rings = max(turns, len(first_rings))

    def slot(pair):
        def turn(at):
            @pl.when(jnp.logical_and(pair < steps.level, at < turns))
            def _():
                for unit in (2 * at, 2 * at + 1):
                    back(unit, 2 * pair, 2, False)

            @pl.when(jnp.logical_and(pair == steps.level, at < turns))
            def _():
                for unit in (2 * at, 2 * at + 1):
                    back(unit, ctx, 1, True)

            @pl.when((pair == steps.level) & (steps.side == 1) & (at < turns))
            def _():
                for unit in (2 * at, 2 * at + 1):
                    back(unit, ctx - 1, 1, False)

            pump(pair * rings + at)

        tiles(rings, turn)

        @pl.when(jnp.logical_or(pair < steps.level, (pair == steps.level) & (steps.side == 1)))
        def _():
            across(pair).start()

        combine(pair)

        @pl.when(pair == late - 1)
        def _():
            out_grad()

    tiles(steps.levels, slot)
    pumped = [steps.levels * rings]

    def pump_next(times=1):
        def body(at, unused, begin=pumped[0]):
            pump(begin + at)
            return unused

        lax.fori_loop(0, times, body, 0)
        pumped[0] += times

    def pumping(times, body):
        begin = pumped[0]

        def step(at):
            body(at)
            tiles(2, lambda more: pump(begin + 2 * at + more))

        tiles(times, step)
        pumped[0] += 2 * times

    cosine, sine = cos_ref[...], sin_ref[...]

    def unturn(columns):
        first, second = columns[: HD // 2], columns[HD // 2 :]
        return jnp.concatenate(
            [first * cosine + second * sine, second * cosine - first * sine], axis=0
        )

    sequences = units // KVH
    groups = wide // keys
    begin = pumped[0]

    def query_rows(sequence):
        span = pl.ds(pl.multiple_of(sequence * keys, LANES), keys)
        for pair in range(H // 2):
            heads = []
            for head in (2 * pair, 2 * pair + 1):
                unit, member = sequence * KVH + head // groups, head % groups
                part = grad_q_ref[unit, :, member * keys : (member + 1) * keys]
                heads.append(unturn(part * HD ** (-0.5)))
            query_all[fsdp, span, pair * 2 * HD : (pair + 1) * 2 * HD] = (
                jnp.concatenate(heads, axis=0).astype(jnp.bfloat16).T
            )
        tiles(3, lambda more: pump(begin + 3 * sequence + more))

    tiles(sequences, query_rows)
    pumped[0] += 3 * sequences
    query_gather.start(query_all.at[fsdp])
    combine(steps.levels)
    kv_width = KVH * HD
    def pair_rows(sequence):
        span = pl.ds(pl.multiple_of(sequence * keys, LANES), keys)
        for pair in range(KVH // 2):
            turned_keys, turned_values = [], []
            for unit in (sequence * KVH + 2 * pair, sequence * KVH + 2 * pair + 1):
                part = final_ref[unit].T
                turned_keys.append(unturn(part[:HD]))
                turned_values.append(part[HD:])
            for start, parts in ((0, turned_keys), (kv_width, turned_values)):
                pair_all[fsdp, span, start + pair * 2 * HD : start + (pair + 1) * 2 * HD] = (
                    jnp.concatenate(parts, axis=0).astype(jnp.bfloat16).T
                )
    tiles(sequences, pair_rows)
    pair_gather.start(pair_all.at[fsdp])
    pump_next(2)
    query_gather.forward()
    step_out = width_tile(width)

    def upstream_tile(at):
        columns = pl.ds(pl.multiple_of(at * step_out, LANES), step_out)
        upstream_ref[:, columns] = (
            dot_columns(query_all[fsdp], w_query_ref[columns, :])
            + dot_columns(pair_all[fsdp, :, :kv_width], w_key_ref[columns, :])
            + dot_columns(pair_all[fsdp, :, kv_width:], w_value_ref[columns, :])
        )

    for copy in loads[slot_loads:]:
        copy.wait()
    pumping(width // step_out, upstream_tile)
    inputs = x_ref[...].astype(jnp.float32)
    scale = norm_scale(inputs)
    upstream = upstream_ref[...]
    scaled = upstream * gain_ref[...]
    tokens_ref[...] = (
        resid_grad_ref[...]
        + scale * scaled
        - inputs * scale**3 * jnp.mean(scaled * inputs, axis=-1, keepdims=True)
    )
    gain_attn = jnp.sum(upstream * inputs * scale, axis=0, keepdims=True)
    lanes = width // LANES
    gain_give[...] = jnp.zeros(gain_give.shape, jnp.float32)
    for block in range(lanes):
        columns = slice(block * LANES, (block + 1) * LANES)
        gain_give[block : block + 1, :] = gain_attn[:, columns]
        gain_give[lanes + block : lanes + block + 1, :] = gain_grad_ref[:, columns]

    def gain_copy(step):
        peer = lax.rem(fsdp + step, group)
        return pltpu.make_async_remote_copy(
            src_ref=gain_give,
            dst_ref=gain_got.at[step - 1],
            send_sem=gain_sends.at[step - 1],
            recv_sem=gain_arrivals.at[step - 1],
            device_id=(peer, ctx),
            device_id_type=MESH,
        )

    for step in range(1, group):
        gain_copy(step).start()
    pump_next()
    for copy in turned[group - 1 :]:
        copy.wait_recv()
    query_gather.sibling_here()
    for step in range(1, query_gather.chips):
        query_gather.crossed(step)
    split = query_split(width)
    filled_a = weight_grad(normed_all, query_all, 0, split, rest_a_work, 0, pumping)
    filled_b = weight_grad(normed_all, query_all, split, width, rest_b_work, 0, pumping)
    pair_gather.forward()
    pump_next()
    pair_gather.sibling_here()
    for step in range(1, pair_gather.chips):
        pair_gather.crossed(step)
    filled_b = weight_grad(normed_all, pair_all, 0, 2 * kv_width, rest_b_work, filled_b, pumping)
    for step in range(1, layer_sum.chips):
        ours = layer_part_ref.at[2 * lax.rem(layer_sum.chip + layer_sum.chips - step, layer_sum.chips) + layer_sum.core]
        for source, target in ((ours, far_ref.at[step - 1]), (layer_cross.at[step - 1], layer_stage)):
            if source is not ours:
                layer_sum.to_cross(step).wait_recv()
            copy = pltpu.make_async_copy(source, target, stage_sems.at[0])
            copy.start()
            copy.wait()
        far_ref[step - 1] = (
            far_ref[step - 1].astype(jnp.float32) + layer_stage[...].astype(jnp.float32)
        ).astype(jnp.bfloat16)
        layer_sum.to_far(step).start()
    gains = gain_give[...]
    for step in range(1, group):
        gain_copy(step).wait_recv()
        gains = gains + gain_got[step - 1]
    gain_tiles = gains.shape[0] // 16
    rest_a_work[filled_a : filled_a + gain_tiles] = gains.astype(jnp.bfloat16).reshape(
        gain_tiles, 16, LANES
    )
    clear_from(rest_a_work, filled_a + gain_tiles)
    clear_from(rest_b_work, filled_b)
    rest_a.start()
    rest_b.start()
    begun = pumped[0]
    total_pumps = max(wide_rings[0].ticks, late + out_a.ticks) * len(first_rings)

    half = -(-(total_pumps - begun) // rest_a.ticks)

    def layer_close():
        layer_sum.to_sibling().wait_recv()
        arrived = [layer_sib]
        for step in range(1, layer_sum.chips):
            layer_sum.to_far(step).wait_recv()
            arrived.append(layer_far.at[step - 1])
        for source in arrived:
            copy = pltpu.make_async_copy(source, layer_stage, stage_sems.at[0])
            copy.start()
            copy.wait()

            def add(at):
                block = pl.ds(pl.multiple_of(at * 32, 32), 32)
                layer_base_ref[block] = layer_base_ref[block] + layer_stage[block].astype(
                    jnp.float32
                )

            tiles(rows // 32, add)

        def close(at):
            block = pl.ds(pl.multiple_of(at * 32, 32), 32)
            layer_ref[block] = layer_base_ref[block].astype(jnp.bfloat16)

        tiles(rows // 32, close)

    def last_ticks(at, unused):
        tick(rest_a, at)
        tick(rest_b, at)
        tiles(half, lambda turn: pump(jnp.minimum(begun + half * at + turn, total_pumps)))

        @pl.when(at == rest_a.ticks * 3 // 4)
        def _():
            layer_close()

        return unused

    lax.fori_loop(0, rest_a.ticks, last_ticks, 0)
    layer_sum.sent()
    for ring in first_rings + [rest_a, rest_b]:
        ring.finish()
    for copy in turned:
        copy.wait_send()
    for gather in (branch_gather, query_gather, pair_gather):
        gather.sent()
    for step in range(1, group):
        gain_copy(step).wait_send()

    def sent(pair):
        @pl.when(jnp.logical_or(pair < steps.level, steps.side == 1))
        def _():
            across(pair).wait_send()

        @pl.when(pair < steps.level)
        def _():
            down_chain(pair).wait_send()

    tiles(steps.level + 1, sent)


def layer_back(
    q_wide, g_wide, log_total, gain_grad, gain, cosine, sine, all_pairs, mix, gate_part, up_part,
    layer_base, layer_parts, branch, low_t, normed_t, w_query, w_key, w_value, x, resid_grad, downs,
):
    group, count = lax.axis_size("fsdp"), lax.axis_size("ctx")
    units, deep, wide = q_wide.shape
    keys = all_pairs.shape[2]
    rows, width = x.shape
    own, kv_width = width // group, w_key.shape[1]
    bf16, f32 = jnp.bfloat16, jnp.float32
    dma = pltpu.SemaphoreType.DMA
    halves = wide_split(width)
    wide_chunk = (group, gate_part.shape[1] // (halves * count), 16, LANES)
    gain_rows = spread(2 * (width // LANES), 16)
    split, row_blocks = query_split(width), own // 16
    out_first = out_split(width)
    chips = group // 2
    small_chunks = [
        (spread(held, count) // count, 16, LANES)
        for held in (
            out_first // LANES * row_blocks,
            (width - out_first) // LANES * row_blocks,
            split // LANES * row_blocks + gain_rows // 16,
            (width - split + 2 * kv_width) // LANES * row_blocks,
        )
    ]
    levels = count // 2
    loaded = [mix, layer_base, w_query, w_key, w_value, x, resid_grad]
    return pl.pallas_call(
        functools.partial(back_kernel, [part.shape[0] for part in downs]),
        out_shape=[
            jax.ShapeDtypeStruct((rows, width), f32),
            jax.ShapeDtypeStruct((rows, width), bf16),
            *[ring_total(wide_chunk, True)] * (2 * halves),
            *[ring_total(part.shape) for part in downs],
            *[ring_total(chunk) for chunk in small_chunks],
            *[jax.ShapeDtypeStruct((levels, units, keys, deep), bf16)] * 2,
            jax.ShapeDtypeStruct((rows, width), bf16),
            *[jax.ShapeDtypeStruct((chips - 1, rows, width), bf16)] * 2,
        ],
        in_specs=[VMEM] * 7 + [ANY] * (14 + len(downs)),
        out_specs=[VMEM] * (6 + 2 * halves + len(downs)) + [ANY] * 5,
        scratch_shapes=[
            pltpu.VMEM(all_pairs.shape, bf16),
            pltpu.VMEM((2, units, keys, deep), bf16),
            pltpu.VMEM((units, keys, deep), f32),
            pltpu.VMEM((units, 2 * wide, deep), bf16),
            pltpu.VMEM((units, 1, wide), f32),
            pltpu.VMEM((units, HD, wide), f32),
            *[kind for _ in range(2 * halves) for kind in ring_scratch(wide_chunk, True)],
            *[kind for chunk in small_chunks for kind in ring_scratch(chunk)],
            pltpu.VMEM((own, group * rows), bf16),
            pltpu.VMEM((own, group * rows), bf16),
            pltpu.VMEM((group, rows, width), bf16),
            pltpu.VMEM((group, rows, width), bf16),
            pltpu.VMEM((group, rows, 2 * kv_width), bf16),
            pltpu.VMEM((rows, width), f32),
            pltpu.VMEM((gain_rows, LANES), f32),
            pltpu.VMEM((group - 1, gain_rows, LANES), f32),
            pltpu.VMEM((chips - 1, rows, width), bf16),
            pltpu.VMEM((rows, width), bf16),
            *[pltpu.VMEM(array.shape, array.dtype) for array in loaded],
            *[kind for _ in range(2 * halves) for kind in ring_semaphores(True)],
            *[kind for _ in range(len(downs) + 2) for kind in ring_semaphores()],
            *[dma((group - 1,))] * 2,
            *[kind for _ in range(2) for kind in ring_semaphores()],
            *[dma((levels,))] * 4,
            *[group_semaphores()] * 6,
            *[dma((group - 1,))] * 6,
            dma((11 + len(downs) + 2 * halves * count,)),
            dma((2,)),
        ],
        compiler_params=pltpu.CompilerParams(
            collective_id=3, has_side_effects=True, vmem_limit_bytes=62 << 20
        ),
    )(
        q_wide, g_wide, log_total, gain_grad, gain, cosine, sine, all_pairs, mix, gate_part, up_part,
        layer_base, layer_parts, branch, low_t, normed_t, w_query, w_key, w_value, x, resid_grad,
        *downs,
    )


def finish_kernel(halves, downs, *refs):
    taken = iter(refs)

    def take(number):
        return [next(taken) for _ in range(number)]

    wides, down_refs, smalls, (rows_ref, layer_rows) = take(2 * halves), take(downs), take(4), take(2)
    outs, (tokens_ref, layer_ref) = take(7), take(2)
    wide_held, down_held, small_held = take(2 * halves), take(downs), take(4)
    made, (load_sems, store_sems) = take(7), take(2)
    sources = [*wides, *down_refs, *smalls]
    held = [*wide_held, *down_held, *small_held]
    loads = {}
    for at, (source, target) in enumerate(zip(sources, held)):
        loads[id(target)] = pltpu.make_async_copy(source, target, load_sems.at[at])
        loads[id(target)].start()
    stores = []

    def store(index, columns=None):
        source, target = made[index], outs[index]
        if columns is not None:
            source, target = source.at[:, columns], target.at[:, columns]
        copy = pltpu.make_async_copy(source, target, store_sems.at[len(stores)])
        copy.start()
        stores.append(copy)

    rows = made[4].shape[0]
    row_blocks = rows // 16
    group = wides[0].shape[1]

    def unpack(source, first, index, begin, end):
        target = made[index]
        for block in range(begin, end):
            here = first + (block - begin) * row_blocks
            target[:, block * LANES : (block + 1) * LANES] = (
                source[here : here + row_blocks].reshape(rows, LANES).astype(jnp.float32)
            )
        return first + (end - begin) * row_blocks

    for index, parts in ((4, wide_held[:halves]), (5, wide_held[halves:])):
        for part in parts:
            loads[id(part)].wait()
        target = made[index]
        columns = target.shape[1] // group
        for owner in range(group):
            tile_rows = jnp.concatenate(
                [part[:, owner].reshape((-1,) + part.shape[3:]) for part in parts], axis=0
            )
            for block in range(columns // LANES):
                begin = owner * columns + block * LANES
                target[:, begin : begin + LANES] = (
                    tile_rows[block * row_blocks : (block + 1) * row_blocks]
                    .reshape(rows, LANES)
                    .astype(jnp.float32)
                )
            store(index, pl.ds(owner * columns, columns))
    down_grad = made[6]
    blocks, begin = down_grad.shape[0] // 16, 0
    for source in down_held:
        loads[id(source)].wait()
        end = min(blocks, begin + source.shape[0])
        if end > begin:
            down_grad[begin * 16 : end * 16, :] = (
                source[: end - begin]
                .reshape((end - begin) * 16, down_grad.shape[1])
                .astype(jnp.float32)
            )
        begin = end
    store(6)
    for part in small_held:
        loads[id(part)].wait()
    out_a, out_b, rest_a, rest_b = small_held
    lanes, kv_lanes = made[0].shape[1] // LANES, made[1].shape[1] // LANES
    middle, split = out_split(made[0].shape[1]) // LANES, query_split(made[0].shape[1]) // LANES
    unpack(out_a, 0, 3, 0, middle)
    unpack(out_b, 0, 3, middle, lanes)
    store(3)
    unpack(rest_a, 0, 0, 0, split)
    at = unpack(rest_b, 0, 0, split, lanes)
    store(0)
    at = unpack(rest_b, at, 1, 0, kv_lanes)
    store(1)
    unpack(rest_b, at, 2, 0, kv_lanes)
    store(2)
    keys = tokens_ref.shape[0]
    for sequence in range(tokens_ref.shape[1]):
        block = slice(sequence * keys, (sequence + 1) * keys)
        tokens_ref[:, sequence, :] = rows_ref[block]
        layer_ref[:, sequence, :] = layer_rows[block]
    for copy in stores:
        copy.wait()


def finish(wides, downs, smalls, token_rows, layer_rows, own, kv_width, hidden, sequences):
    rows, width = token_rows.shape
    f32 = jnp.float32
    outs = [
        jax.ShapeDtypeStruct((own, columns), f32)
        for columns in (width, kv_width, kv_width, width, FF, FF)
    ] + [jax.ShapeDtypeStruct((hidden, width), f32)]
    sources = [*wides, *downs, *smalls]
    dma = pltpu.SemaphoreType.DMA
    return pl.pallas_call(
        functools.partial(finish_kernel, len(wides) // 2, len(downs)),
        out_shape=outs
        + [
            jax.ShapeDtypeStruct((rows // sequences, sequences, width), kind)
            for kind in (f32, layer_rows.dtype)
        ],
        in_specs=[ANY] * len(sources) + [VMEM] * 2,
        out_specs=[ANY] * len(outs) + [VMEM] * 2,
        scratch_shapes=[pltpu.VMEM(array.shape, array.dtype) for array in sources]
        + [pltpu.VMEM(out.shape, f32) for out in outs]
        + [dma((len(sources),)), dma((5 + 2 * wides[0].shape[1],))],
        compiler_params=pltpu.CompilerParams(vmem_limit_bytes=60 << 20),
    )(*sources, token_rows, layer_rows)


def on_device(
    tokens, w_query, w_key, w_value, w_out, w_gate, w_up, w_down, gain_attn, gain_ffn, cotangent
):
    block_len, seq_count, width = tokens.shape
    rows_count = block_len * seq_count
    kv_width = KVH * HD
    positions = lax.axis_index("ctx") * block_len + jnp.arange(block_len, dtype=jnp.int32)
    freqs = ROTARY_BASE ** (-2.0 * jnp.arange(HD // 2, dtype=jnp.float32) / HD)
    angles = freqs[:, None] * positions.astype(jnp.float32)[None, :]
    cosine, sine = jnp.cos(angles), jnp.sin(angles)
    own = gain_attn.shape[0]
    units = seq_count * KVH
    wide = H // KVH * block_len
    own_gains = jnp.pad(
        jnp.stack([gain_attn, gain_ffn]).astype(jnp.float32), ((0, 6), (0, spread(own, LANES) - own))
    )
    (
        x_rows, q_wide, normed_t, full_gain_attn, full_gain_ffn, full_query, full_key, full_value, attn_low, low_t, mix_unit, log_total,
        all_pairs, full_out, my_gate, my_up, all_g,
    ) = attend(
        tokens, cotangent, own_gains, cosine, sine, w_query, w_key, w_value, w_out, w_gate, w_up
    )
    layer_base, grad_resid, grad_branch, g_wide, gate_part, up_part, layer_parts, *downs = (
        feed_forward(
            x_rows, attn_low, full_out, my_gate, my_up, w_down, all_g, full_gain_ffn, units, wide
        )
    )
    downs, gain_term_ffn = downs[:-1], downs[-1]
    grad_tokens, layer_out, *sums = layer_back(
        q_wide, g_wide, log_total, gain_term_ffn, full_gain_attn, cosine, sine, all_pairs, mix_unit,
        gate_part, up_part, layer_base, layer_parts, grad_branch, low_t, normed_t, full_query,
        full_key, full_value, x_rows, grad_resid, downs,
    )
    wides, sums = sums[: 2 * wide_split(width)], sums[2 * wide_split(width) :]
    smalls = sums[len(downs) : len(downs) + 4]
    filled = query_split(width) // LANES * (own // 16)
    gain_grads = smalls[2][filled:].reshape(-1, LANES)[: 2 * (width // LANES)].reshape(2, width)
    gain_grads = lax.dynamic_slice_in_dim(gain_grads, lax.axis_index("fsdp") * own, own, 1)
    gain_grads = gain_grads.astype(jnp.float32)
    *grads, tokens_grad, layer_result = finish(
        wides, sums[: len(downs)], smalls, grad_tokens, layer_out, own, kv_width, w_down.shape[0],
        seq_count,
    )
    return (
        layer_result,
        tokens_grad,
        *grads,
        gain_grads[0],
        gain_grads[1],
    )


def solution(mesh):
    return jax.shard_map(
        on_device,
        mesh=mesh,
        in_specs=(
            P("ctx", "fsdp", None),
            P("fsdp", None),
            P("fsdp", None),
            P("fsdp", None),
            P("fsdp", None),
            P("fsdp", None),
            P("fsdp", None),
            P("fsdp", None),
            P("fsdp"),
            P("fsdp"),
            P("ctx", "fsdp", None),
        ),
        out_specs=(
            P("ctx", "fsdp", None),
            P("ctx", "fsdp", None),
            P("fsdp", None),
            P("fsdp", None),
            P("fsdp", None),
            P("fsdp", None),
            P("fsdp", None),
            P("fsdp", None),
            P("fsdp", None),
            P("fsdp"),
            P("fsdp"),
        ),
        check_vma=False,
    )
```

```python
import functools

import jax
import jax.numpy as jnp
from jax import lax
from jax.experimental import pallas as pl
from jax.experimental.pallas import tpu as pltpu
from jax.sharding import PartitionSpec as P

H = 18
KVH = 6
HD = 64
FF = 3072


EPSILON = 1e-05
ROTARY_BASE = 10000.0
MASKED_SCORE = -1e30


def norm_scale(rows):
    return lax.rsqrt(jnp.mean(rows * rows, axis=-1, keepdims=True) + EPSILON)


def forward_dot(left, right):
    return jnp.dot(left, right, preferred_element_type=jnp.float32)


MESH = pl.DeviceIdType.MESH
LANES = 128


def ring_place(ctx, fsdp, count):
    column, side = lax.div(ctx, 2), lax.rem(ctx, 2)
    place = column + side * (count - 1 - 2 * column)
    odd = lax.rem(fsdp, 2)
    return place + odd * (count - 1 - 2 * place)


def ring_ctx(place, fsdp, count):
    odd = lax.rem(fsdp, 2)
    place = place + odd * (count - 1 - 2 * place)
    late = lax.div(place, count // 2)
    return (1 - late) * 2 * place + late * (2 * (count - 1 - place) + 1)


class GroupGather:
    def __init__(self, shard_of, sends, arrivals):
        self.shard_of, self.sends, self.arrivals = shard_of, sends, arrivals
        self.fsdp, self.ctx = lax.axis_index("fsdp"), lax.axis_index("ctx")
        self.chips = lax.axis_size("fsdp") // 2
        self.chip, self.core = lax.div(self.fsdp, 2), lax.rem(self.fsdp, 2)
        self.sibling = 2 * self.chip + 1 - self.core

    def copy(self, source, shard, semaphore, device):
        return pltpu.make_async_remote_copy(
            src_ref=source,
            dst_ref=self.shard_of(shard),
            send_sem=self.sends.at[semaphore],
            recv_sem=self.arrivals.at[semaphore],
            device_id=(device, self.ctx),
            device_id_type=MESH,
        )

    def same_core(self, step):
        return 2 * lax.rem(self.chip + step, self.chips) + self.core

    def across(self, source):
        return self.copy(source, self.fsdp, 0, self.sibling)

    def out(self, source, step):
        return self.copy(source, self.fsdp, step, self.same_core(step))

    def onward(self, step):
        shard = self.same_core(self.chips - step)
        return self.copy(self.shard_of(shard), shard, self.chips - 1 + step, self.sibling)

    def start(self, source):
        for step in range(1, self.chips):
            self.out(source, step).start()
        self.across(source).start()

    def forward(self):
        own = self.shard_of(self.fsdp)
        for step in range(1, self.chips):
            self.out(own, step).wait_recv()
            self.onward(step).start()

    def sibling_here(self):
        self.across(self.shard_of(self.fsdp)).wait_recv()

    def crossed(self, step):
        self.onward(step).wait_recv()

    def sent(self):
        own = self.shard_of(self.fsdp)
        self.across(own).wait_send()
        for step in range(1, self.chips):
            self.out(own, step).wait_send()
            self.onward(step).wait_send()

    def finish(self):
        self.forward()
        self.sibling_here()
        for step in range(1, self.chips):
            self.crossed(step)
        self.sent()


class HalfGather:
    def __init__(self, held, own_rows, sends, arrivals):
        self.held, self.own = held, own_rows
        self.sends, self.arrivals = sends, arrivals
        self.fsdp, self.ctx = lax.axis_index("fsdp"), lax.axis_index("ctx")
        self.chips = lax.axis_size("fsdp") // 2
        self.chip, self.core = lax.div(self.fsdp, 2), lax.rem(self.fsdp, 2)
        self.sibling = 2 * self.chip + 1 - self.core
        self.side = lax.rem(self.ctx, 2)
        self.pair = self.ctx + 1 - 2 * self.side
        first = -(-own_rows // 32) * 16
        self.halves = ((0, first), (first, own_rows - first))

    def same_core(self, step):
        return 2 * lax.rem(self.chip + step, self.chips) + self.core

    def rows(self, shard, half=None):
        begin, size = (0, self.own) if half is None else self.halves[half]
        return self.held.at[pl.ds(shard * self.own + begin, size)]

    def copy(self, source, target, semaphore, device):
        return pltpu.make_async_remote_copy(
            src_ref=source,
            dst_ref=target,
            send_sem=self.sends.at[semaphore],
            recv_sem=self.arrivals.at[semaphore],
            device_id=device,
            device_id_type=MESH,
        )

    def on_side(self, body):
        for half in range(2):

            @pl.when(self.side == half)
            def _(half=half):
                body(half)

    def across(self, source):
        return self.copy(source, self.rows(self.fsdp), 0, (self.sibling, self.ctx))

    def out(self, source, step, half):
        begin, size = self.halves[half]
        return self.copy(
            source.at[pl.ds(begin, size)],
            self.rows(self.fsdp, half),
            step,
            (self.same_core(step), self.ctx),
        )

    def to_pair(self, step, half):
        part = self.rows(self.same_core(self.chips - step), half)
        return self.copy(part, part, self.chips - 1 + step, (self.fsdp, self.pair))

    def onward(self, step):
        part = self.rows(self.same_core(self.chips - step))
        return self.copy(part, part, 2 * self.chips - 2 + step, (self.sibling, self.ctx))

    def start(self, source):
        def send(half):
            for step in range(1, self.chips):
                self.out(source, step, half).start()

        self.on_side(send)
        self.across(source).start()

    def to_pairs(self):
        def forward(half):
            for step in range(1, self.chips):
                self.out(self.rows(self.fsdp), step, half).wait_recv()
                self.to_pair(step, half).start()

        self.on_side(forward)

    def to_sibling(self):
        def forward(half):
            for step in range(1, self.chips):
                self.to_pair(step, 1 - half).wait_recv()

        self.on_side(forward)
        for step in range(1, self.chips):
            self.onward(step).start()

    def arrived(self):
        self.across(self.rows(self.fsdp)).wait_recv()
        for step in range(1, self.chips):
            self.onward(step).wait_recv()

    def sent(self):
        def wait(half):
            for step in range(1, self.chips):
                self.out(self.rows(self.fsdp), step, half).wait_send()
                self.to_pair(step, half).wait_send()

        self.on_side(wait)
        self.across(self.rows(self.fsdp)).wait_send()
        for step in range(1, self.chips):
            self.onward(step).wait_send()


def half_semaphores(many):
    return pltpu.SemaphoreType.DMA((many, 3 * (lax.axis_size("fsdp") // 2) - 2))


def group_semaphores():
    return pltpu.SemaphoreType.DMA((lax.axis_size("fsdp") - 1,))


def greet_group(barrier):
    fsdp, ctx, group = lax.axis_index("fsdp"), lax.axis_index("ctx"), lax.axis_size("fsdp")
    for step in range(1, group):
        peer = lax.rem(fsdp + step, group)
        pl.semaphore_signal(barrier, inc=1, device_id=(peer, ctx), device_id_type=MESH)
    return group - 1


class Steps:
    def __init__(self):
        self.fsdp, self.ctx = lax.axis_index("fsdp"), lax.axis_index("ctx")
        self.levels = lax.axis_size("ctx") // 2
        self.level, self.side = lax.div(self.ctx, 2), lax.rem(self.ctx, 2)
        self.peer = (self.fsdp, 2 * self.level + 1 - self.side)
        self.above = (self.fsdp, lax.rem(self.ctx + 2, 2 * self.levels))
        self.below = (self.fsdp, lax.rem(self.ctx + 2 * self.levels - 2, 2 * self.levels))
        self.has_above = self.level + 1 < self.levels
        self.has_below = self.level > 0

    def greet(self, barrier):
        pl.semaphore_signal(barrier, inc=1, device_id=self.peer, device_id_type=MESH)

        @pl.when(self.has_above)
        def _():
            pl.semaphore_signal(barrier, inc=1, device_id=self.above, device_id_type=MESH)

        @pl.when(self.has_below)
        def _():
            pl.semaphore_signal(barrier, inc=1, device_id=self.below, device_id_type=MESH)

        return 1 + jnp.minimum(self.level, 1) + jnp.minimum(self.levels - 1 - self.level, 1)


PARTS = 2


def causal(keys, wide, shape):
    key_at = lax.broadcasted_iota(jnp.int32, shape, 0)
    query_at = lax.rem(lax.broadcasted_iota(jnp.int32, shape, 1), keys)
    return key_at <= query_at


def attend_kernel(
    token_ref, upstream_ref, gain_ref, cos_ref, sin_ref, query_ref, key_ref, value_ref, out_ref, gate_ref,
    up_ref, x_ref, q_ref, normed_t_ref, gain_attn_ref, gain_ffn_ref, full_query, full_key, full_value,
    low_ref, low_t_ref, mix_ref, log_ref, all_ref, full_out_ref, my_gate_ref, my_up_ref, all_g_ref,
    normed_ref, key_rows, gain_all, own_out, own_gate, own_up, own_g,
    top_ref, total_ref, chain_sends, chain_arrivals, peer_sends, peer_arrivals,
    half_sends, half_arrivals, gain_sends, gain_arrivals,
    out_sends, out_arrivals, g_sends, g_arrivals,
    part_sends, part_arrivals, local_sems,
):
    steps = Steps()
    fsdp, ctx, group = steps.fsdp, steps.ctx, lax.axis_size("fsdp")
    units, deep, wide = q_ref.shape
    keys = all_ref.shape[2]
    per_part = units // PARTS
    rows_count, width = x_ref.shape
    own = query_ref.shape[0]
    sequences, groups = units // KVH, H // KVH
    barrier = pltpu.get_barrier_semaphore()
    greeted = steps.greet(barrier) + greet_group(barrier)
    span = KVH * HD
    pieces = [(key_ref, full_key, 0), (value_ref, full_value, 0)]
    pieces += [(query_ref, full_query, start) for start in range(0, width, span)]
    gathers = []
    for at, (source, target, start) in enumerate(pieces):
        columns = pl.ds(start, span)
        gather = HalfGather(
            target.at[:, columns], own, half_sends.at[at], half_arrivals.at[at]
        )
        gathers.append((gather, source.at[:, columns]))
    own_rows = pl.ds(fsdp * own, own)
    own_copies = [
        pltpu.make_async_copy(source, target.at[own_rows], local_sems.at[4 + at])
        for at, (source, target) in enumerate(
            ((key_ref, full_key), (value_ref, full_value), (query_ref, full_query))
        )
    ]
    for copy in own_copies:
        copy.start()
    for sequence in range(sequences):
        x_ref[sequence * keys : (sequence + 1) * keys] = token_ref[:, sequence, :]
    gain_all[fsdp] = gain_ref[...]
    pl.semaphore_wait(barrier, greeted)

    def gain_copy(step):
        peer = lax.rem(fsdp + step, group)
        return pltpu.make_async_remote_copy(
            src_ref=gain_ref,
            dst_ref=gain_all.at[fsdp],
            send_sem=gain_sends.at[step - 1],
            recv_sem=gain_arrivals.at[step - 1],
            device_id=(peer, ctx),
            device_id_type=MESH,
        )

    for step in range(1, group):
        gain_copy(step).start()
    for gather, source in gathers:
        gather.start(source)
    for sequence in range(sequences):
        own_g[sequence * keys : (sequence + 1) * keys] = upstream_ref[:, sequence, :]
    inputs = x_ref[...].astype(jnp.float32)
    scale = norm_scale(inputs)
    q_ref[:, HD:, :] = jnp.zeros((units, HD, wide), q_ref.dtype)
    for step in range(1, group):
        gain_copy(step).wait_recv()
    gains = jnp.concatenate([gain_all[shard][:, :own] for shard in range(group)], axis=1)
    gain_attn_ref[...] = gains[:1]
    gain_ffn_ref[...] = gains[1:2]
    normed_ref[...] = (inputs * scale * gains[:1]).astype(jnp.bfloat16)
    cosine, sine = cos_ref[...], sin_ref[...]

    def turn(columns):
        first, second = columns[: HD // 2], columns[HD // 2 :]
        return jnp.concatenate(
            [first * cosine - second * sine, second * cosine + first * sine], axis=0
        ).astype(jnp.bfloat16)

    def block_copy(level, part, side, semaphores, arrivals, arrives, device):
        block = 2 * (steps.level - level) + side
        held = all_ref.at[block, pl.ds(part * per_part, per_part)]
        return pltpu.make_async_remote_copy(
            src_ref=held,
            dst_ref=held,
            send_sem=semaphores.at[level, part],
            recv_sem=arrivals.at[arrives, part],
            device_id=device,
            device_id_type=MESH,
        )

    def chain(level, part):
        return block_copy(
            level, part, steps.side, chain_sends, chain_arrivals, level + 1, steps.above
        )

    def across(level, part):
        return block_copy(
            level, part, steps.side, peer_sends, peer_arrivals, level, steps.peer
        )

    def pass_on(level, part):
        @pl.when(steps.has_above)
        def _():
            chain(level, part).start()

    def project(at):
        _, weight, start = pieces[at]
        made = forward_dot(normed_ref[...], weight[:, start : start + span])
        if at == 0:
            key_rows[...] = made
            return
        for sequence in range(sequences):
            block = slice(sequence * keys, (sequence + 1) * keys)
            for pair in range(span // (2 * HD)):
                columns = slice(pair * 2 * HD, (pair + 1) * 2 * HD)
                turned = made[block, columns].T
                if at == 1:
                    turned_keys = key_rows[block, columns].T
                    for half in range(2):
                        held = slice(half * HD, (half + 1) * HD)
                        both = jnp.concatenate(
                            [turn(turned_keys[held]), turned[held].astype(jnp.bfloat16)], axis=0
                        )
                        all_ref[ctx, sequence * KVH + 2 * pair + half] = both.T
                else:
                    for half in range(2):
                        head = start // HD + 2 * pair + half
                        unit, member = sequence * KVH + head // groups, head % groups
                        part = turn(turned[half * HD : (half + 1) * HD])
                        q_ref[unit, :HD, member * keys : (member + 1) * keys] = part * jnp.bfloat16(
                            HD ** (-0.5)
                        )
        if at == 1:
            for part in range(PARTS):
                pass_on(0, part)

                @pl.when(steps.side == 0)
                def _():
                    across(0, part).start()

    columns = my_gate_ref.shape[1]
    gathered = HalfGather(full_out_ref, own, out_sends.at[0], out_arrivals.at[0])
    gathered_g = GroupGather(lambda shard: all_g_ref.at[shard], g_sends, g_arrivals)
    mine = lane_tile(fsdp, columns)
    own_parts = (
        (out_ref, own_out, full_out_ref.at[own_rows]),
        (gate_ref.at[:, mine], own_gate, my_gate_ref.at[own_rows]),
        (up_ref.at[:, mine], own_up, my_up_ref.at[own_rows]),
    )
    own_g_copy = pltpu.make_async_copy(own_g, all_g_ref.at[fsdp], local_sems.at[3])
    loads = [
        pltpu.make_async_copy(source, held, local_sems.at[at])
        for at, (source, held, _) in enumerate(own_parts)
    ]
    background = [
        pltpu.make_async_copy(held, target, local_sems.at[at])
        for at, (_, held, target) in enumerate(own_parts)
    ]
    slices = []
    for which, (source, target) in enumerate(((gate_ref, my_gate_ref), (up_ref, my_up_ref))):
        for step in range(1, group):
            peer = lax.rem(fsdp + step, group)
            slices.append(
                pltpu.make_async_remote_copy(
                    src_ref=source.at[:, lane_tile(peer, columns)],
                    dst_ref=target.at[own_rows],
                    send_sem=part_sends.at[which, step - 1],
                    recv_sem=part_arrivals.at[which, step - 1],
                    device_id=(peer, ctx),
                    device_id_type=MESH,
                )
            )

    def start_background():
        for copy in loads:
            copy.start()
        gathered.start(out_ref)
        for copy in slices:
            copy.start()
        gathered_g.start(own_g)
        own_g_copy.start()

    last = len(pieces)
    for at in range(last + 2):
        if at < last:
            gathers[at][0].to_pairs()
        if at == 0:
            start_background()
        if 1 <= at <= last:
            gathers[at - 1][0].to_sibling()
        if at == 1:
            for column in range(width // LANES):
                columns = slice(column * LANES, (column + 1) * LANES)
                normed_t_ref[columns, :] = normed_ref[:, columns].T
            for copy in own_copies:
                copy.wait()
        if at >= 2:
            gathers[at - 2][0].arrived()
            project(at - 2)

    def second_half():
        gathered.to_pairs()
        for load, copy in zip(loads, background):
            load.wait()
            copy.start()

    def add(unit, kv):
        scores = jnp.dot(kv, q_ref[unit], preferred_element_type=jnp.float32)
        top = top_ref[unit]
        new_top = jnp.maximum(top, jnp.max(scores, axis=0, keepdims=True))
        fade = jnp.exp(top - new_top)
        weights = jnp.exp(scores - new_top)
        top_ref[unit] = new_top
        total_ref[unit] = total_ref[unit] * fade + jnp.sum(weights, axis=0, keepdims=True)
        added = jnp.dot(kv.T, weights.astype(jnp.bfloat16), preferred_element_type=jnp.float32)
        mix_ref[unit] = mix_ref[unit] * fade + added[HD:]

    def over_units(body, first, count):
        def two(at, unused):
            body(first + 2 * at)
            body(first + 2 * at + 1)
            return unused

        lax.fori_loop(0, count // 2, two, 0)

    def diagonal(unit):
        kv = all_ref[ctx, unit]
        scores = jnp.dot(kv, q_ref[unit], preferred_element_type=jnp.float32)
        scores = jnp.where(causal(keys, wide, scores.shape), scores, MASKED_SCORE)
        top = jnp.max(scores, axis=0, keepdims=True)
        weights = jnp.exp(scores - top)
        top_ref[unit] = top
        total_ref[unit] = jnp.sum(weights, axis=0, keepdims=True)
        added = jnp.dot(kv.T, weights.astype(jnp.bfloat16), preferred_element_type=jnp.float32)
        mix_ref[unit] = added[HD:]

    over_units(diagonal, 0, units)

    def forward(level, part):
        chain(level - 1, part).wait_recv()
        pass_on(level, part)
        across(level, part).start()

    @pl.when(steps.level >= 1)
    def _():
        for part in range(PARTS):
            forward(1, part)

    @pl.when(steps.side == 1)
    def _():
        for part in range(PARTS):
            across(0, part).wait_recv()
            over_units(lambda unit: add(unit, all_ref[ctx - 1, unit]), part * per_part, per_part)

    def level_step(level, unused):
        first = 2 * (steps.level - level)
        for part in range(PARTS):

            @pl.when(level < steps.level)
            def _():
                forward(level + 1, part)

            across(level, part).wait_recv()
            over_units(
                lambda unit: add(unit, all_ref[pl.ds(first, 2), unit].reshape(2 * keys, deep)),
                part * per_part,
                per_part,
            )

        @pl.when(level == 1)
        def _():
            second_half()

        return unused

    @pl.when(steps.level == 0)
    def _():
        second_half()

    lax.fori_loop(1, steps.level + 1, level_step, 0)

    def close(unit):
        total = total_ref[unit]
        mix_ref[unit] = mix_ref[unit] / total
        log_ref[unit] = top_ref[unit] + jnp.log(total)

    over_units(close, 0, units)
    for sequence in range(sequences):
        for pair in range(H // 2):
            heads = []
            for head in (2 * pair, 2 * pair + 1):
                unit, member = sequence * KVH + head // groups, head % groups
                heads.append(mix_ref[unit, :, member * keys : (member + 1) * keys])
            tile = jnp.concatenate(heads, axis=0).astype(low_ref.dtype)
            block = slice(sequence * keys, (sequence + 1) * keys)
            columns = slice(pair * 2 * HD, (pair + 1) * 2 * HD)
            low_t_ref[columns, block] = tile
            low_ref[block, columns] = tile.T
    for gather, _ in gathers:
        gather.sent()
    for step in range(1, group):
        gain_copy(step).wait_send()
    gathered.to_sibling()
    gathered_g.forward()
    gathered.arrived()
    gathered.sent()
    gathered_g.sibling_here()
    for step in range(1, gathered_g.chips):
        gathered_g.crossed(step)
    gathered_g.sent()
    for copy in slices:
        copy.wait()
    own_g_copy.wait()
    for copy in background:
        copy.wait()

    def sent(level, unused):
        for part in range(PARTS):

            @pl.when(steps.has_above)
            def _():
                chain(level, part).wait_send()

            @pl.when(jnp.logical_or(level > 0, steps.side == 0))
            def _():
                across(level, part).wait_send()

        return unused

    lax.fori_loop(0, steps.level + 1, sent, 0)


ANY = pl.BlockSpec(memory_space=pl.ANY)
VMEM = pl.BlockSpec(memory_space=pltpu.VMEM)


def attend(tokens, upstream, gains, cosine, sine, w_query, w_key, w_value, w_out, w_gate, w_up):
    group, count = lax.axis_size("fsdp"), lax.axis_size("ctx")
    keys, sequences, width = tokens.shape
    own, hidden = w_query.shape[0], w_gate.shape[1] // group
    rows, units, deep = keys * sequences, sequences * KVH, 2 * HD
    wide = H // KVH * keys
    kv_width = KVH * HD
    dma = pltpu.SemaphoreType.DMA
    bf16, f32 = jnp.bfloat16, jnp.float32
    pieces = 2 + width // kv_width
    return pl.pallas_call(
        attend_kernel,
        out_shape=[
            jax.ShapeDtypeStruct((rows, width), bf16),
            jax.ShapeDtypeStruct((units, deep, wide), bf16),
            jax.ShapeDtypeStruct((width, rows), bf16),
            jax.ShapeDtypeStruct((1, width), f32),
            jax.ShapeDtypeStruct((1, width), f32),
            jax.ShapeDtypeStruct((width, width), bf16),
            jax.ShapeDtypeStruct((width, kv_width), bf16),
            jax.ShapeDtypeStruct((width, kv_width), bf16),
            jax.ShapeDtypeStruct((rows, width), bf16),
            jax.ShapeDtypeStruct((width, rows), bf16),
            jax.ShapeDtypeStruct((units, HD, wide), f32),
            jax.ShapeDtypeStruct((units, 1, wide), f32),
            jax.ShapeDtypeStruct((count, units, keys, deep), bf16),
            jax.ShapeDtypeStruct((width, width), bf16),
            jax.ShapeDtypeStruct((width, hidden), bf16),
            jax.ShapeDtypeStruct((width, hidden), bf16),
            jax.ShapeDtypeStruct((group, rows, width), bf16),
        ],
        in_specs=[VMEM] * 5 + [ANY] * 6,
        out_specs=[VMEM] * 13 + [ANY] * 4,
        scratch_shapes=[
            pltpu.VMEM((rows, width), bf16),
            pltpu.VMEM((rows, kv_width), f32),
            pltpu.VMEM((group,) + gains.shape, f32),
            pltpu.VMEM((own, width), bf16),
            pltpu.VMEM((own, hidden), bf16),
            pltpu.VMEM((own, hidden), bf16),
            pltpu.VMEM((rows, width), bf16),
            pltpu.VMEM((units, 1, wide), f32),
            pltpu.VMEM((units, 1, wide), f32),
            dma((count // 2, PARTS)),
            dma((count // 2 + 1, PARTS)),
            dma((count // 2, PARTS)),
            dma((count // 2, PARTS)),
            half_semaphores(pieces),
            half_semaphores(pieces),
            *[dma((group - 1,))] * 2,
            *[half_semaphores(1)] * 2,
            *[group_semaphores()] * 2,
            *[dma((2, group - 1))] * 2,
            dma((7,)),
        ],
        compiler_params=pltpu.CompilerParams(
            collective_id=1, has_side_effects=True, vmem_limit_bytes=60 << 20
        ),
    )(tokens, upstream, gains, cosine, sine, w_query, w_key, w_value, w_out, w_gate, w_up)


class Ring:
    def __init__(self, work, landing, total, semaphores, forward, exchange=False):
        self.fsdp, self.ctx = lax.axis_index("fsdp"), lax.axis_index("ctx")
        self.group, self.count = lax.axis_size("fsdp"), lax.axis_size("ctx")
        self.work, self.landing, self.total = work, landing, total
        self.sends, self.arrivals = semaphores[:2]
        self.part_sends, self.part_arrivals, self.own_sem = semaphores[2:] if exchange else (None,) * 3
        self.exchange = exchange
        side = 0 if forward else 1
        self.place = ring_place(self.ctx, side, self.count)
        self.after = (self.fsdp, ring_ctx(lax.rem(self.place + 1, self.count), side, self.count))
        self.ticks = 2 * self.count - 2 + int(exchange)

    def chunk(self, held, index):
        if self.exchange:
            return held.at[index]
        per = held.shape[0] // self.count
        return held.at[pl.ds(index * per, per)]

    def summing(self, step, index):
        return self.copy(self.chunk(self.work, index), self.landing.at[step], step)

    def handing(self, step, index):
        held = self.chunk(self.total, index)
        return self.copy(held, held, step)

    def copy(self, source, target, step):
        return pltpu.make_async_remote_copy(
            src_ref=source,
            dst_ref=target,
            send_sem=self.sends.at[step],
            recv_sem=self.arrivals.at[step],
            device_id=self.after,
            device_id_type=MESH,
        )

    def part(self, index, step):
        peer = lax.rem(self.fsdp + step, self.group)
        return pltpu.make_async_remote_copy(
            src_ref=self.work.at[index, peer],
            dst_ref=self.total.at[index, self.fsdp],
            send_sem=self.part_sends.at[step - 1],
            recv_sem=self.part_arrivals.at[step - 1],
            device_id=(peer, self.ctx),
            device_id_type=MESH,
        )

    def own_part(self, index):
        return pltpu.make_async_copy(
            self.work.at[index, self.fsdp], self.total.at[index, self.fsdp], self.own_sem
        )

    def start(self):
        self.summing(0, self.place).start()

    def tick(self, at):
        last = self.count - 2
        gap = int(self.exchange)
        step = at - gap * jnp.where(at > last, 1, 0) if self.exchange else at
        index = lax.rem(self.place + 3 * self.count - 1 - step, self.count)

        def add(target):
            part, landed = self.chunk(self.work, index), self.landing.at[jnp.minimum(at, last)]
            for row in range(part.shape[0]):
                target[row] = (
                    part[row].astype(jnp.float32) + landed[row].astype(jnp.float32)
                ).astype(part.dtype)

        @pl.when(at <= last)
        def _():
            self.summing(jnp.minimum(at, last), index).wait_recv()

        @pl.when(at < last)
        def _():
            add(self.chunk(self.work, index))
            self.summing(jnp.minimum(at + 1, last), index).start()

        if self.exchange:

            @pl.when(at == last)
            def _():
                add(self.chunk(self.work, index))
                for peer in range(1, self.group):
                    self.part(index, peer).start()
                self.own_part(index).start()

            @pl.when(at == last + 1)
            def _():
                done = lax.rem(self.place + 1, self.count)
                self.own_part(done).wait()
                for peer in range(1, self.group):
                    self.part(done, peer).wait_recv()
                self.handing(last + 1, done).start()

        else:

            @pl.when(at == last)
            def _():
                add(self.chunk(self.total, index))
                self.handing(last + 1, index).start()

        @pl.when(at > last + gap)
        def _():
            here = jnp.maximum(step, last + 1)
            self.handing(here, index).wait_recv()

            @pl.when(here < 2 * self.count - 3)
            def _():
                self.handing(jnp.minimum(here + 1, 2 * self.count - 3), index).start()

    def finish(self):
        def wait(step, unused):
            self.handing(step, self.place).wait_send()
            return unused

        lax.fori_loop(0, 2 * self.count - 2, wait, 0)
        if self.exchange:
            for peer in range(1, self.group):
                self.part(lax.rem(self.place + 1, self.count), peer).wait_send()


class SumRing(Ring):
    def __init__(self, *args):
        super().__init__(*args)
        self.ticks = self.count - 1

    def tick(self, at):
        last = self.count - 2
        index = lax.rem(self.place + 2 * self.count - 1 - at, self.count)
        self.summing(at, index).wait_recv()
        work, landed = self.chunk(self.work, index), self.landing.at[at]

        def add(target):
            for row in range(work.shape[0]):
                target[row] = (
                    work[row].astype(jnp.float32) + landed[row].astype(jnp.float32)
                ).astype(work.dtype)

        @pl.when(at < last)
        def _():
            add(work)
            self.summing(jnp.minimum(at + 1, last), index).start()

        @pl.when(at == last)
        def _():
            add(self.total)

    def finish(self):
        def wait(step, unused):
            self.summing(step, self.place).wait_send()
            return unused

        lax.fori_loop(0, self.ticks, wait, 0)


class SpreadRing(Ring):
    def __init__(self, total, semaphores, forward):
        super().__init__(None, None, total, semaphores, forward)
        self.ticks = self.count - 1
        self.first = lax.rem(self.place + 1, self.count)

    def start(self):
        self.handing(0, self.first).start()

    def tick(self, at):
        index = lax.rem(self.place + self.count - at, self.count)
        self.handing(at, index).wait_recv()

        @pl.when(at < self.count - 2)
        def _():
            self.handing(jnp.minimum(at + 1, self.count - 2), index).start()

    def finish(self):
        def wait(step, unused):
            self.handing(step, self.place).wait_send()
            return unused

        lax.fori_loop(0, self.ticks, wait, 0)


def ring_scratch(chunk, exchange=False):
    count = lax.axis_size("ctx")
    work = (count,) + chunk if exchange else (count * chunk[0],) + chunk[1:]
    return [pltpu.VMEM(work, jnp.bfloat16), pltpu.VMEM((count - 1,) + chunk, jnp.bfloat16)]


def ring_total(chunk, exchange=False):
    count = lax.axis_size("ctx")
    work = (count,) + chunk if exchange else (count * chunk[0],) + chunk[1:]
    return jax.ShapeDtypeStruct(work, jnp.bfloat16)


def ring_semaphores(exchange=False):
    dma, steps = pltpu.SemaphoreType.DMA, 2 * lax.axis_size("ctx") - 2
    parts = lax.axis_size("fsdp") - 1
    return [dma((steps,))] * 2 + ([dma((parts,))] * 2 + [dma] if exchange else [])


def wide_split(width):
    group, count = lax.axis_size("fsdp"), lax.axis_size("ctx")
    return 2 if FF // group // LANES * (width // group // 16) >= 4 * count else 1


def query_split(width):
    return width // LANES * 7 // 9 * LANES


def out_split(width):
    return (width // LANES + 1) // 2 * LANES


def down_split(blocks, count):
    each = -(-blocks // count)
    rings = 4 if each >= 4 else 2
    return [max(1, (each + at) // rings) for at in range(rings)]


class GroupScatter:
    def __init__(self, give_sib, got_sib, give_cross, got_cross, far, got_far, sends, arrivals):
        self.give_sib, self.got_sib = give_sib, got_sib
        self.give_cross, self.got_cross = give_cross, got_cross
        self.far, self.got_far = far, got_far
        self.sends, self.arrivals = sends, arrivals
        self.fsdp, self.ctx = lax.axis_index("fsdp"), lax.axis_index("ctx")
        self.chips = lax.axis_size("fsdp") // 2
        self.chip, self.core = lax.div(self.fsdp, 2), lax.rem(self.fsdp, 2)
        self.sibling = 2 * self.chip + 1 - self.core

    def copy(self, source, target, semaphore, device):
        return pltpu.make_async_remote_copy(
            src_ref=source,
            dst_ref=target,
            send_sem=self.sends.at[semaphore],
            recv_sem=self.arrivals.at[semaphore],
            device_id=(device, self.ctx),
            device_id_type=MESH,
        )

    def to_sibling(self):
        return self.copy(self.give_sib, self.got_sib, 0, self.sibling)

    def to_cross(self, step):
        return self.copy(
            self.give_cross(step), self.got_cross.at[step - 1], step, self.sibling
        )

    def to_far(self, step):
        chip = lax.rem(self.chip + self.chips - step, self.chips)
        return self.copy(
            self.far.at[step - 1],
            self.got_far.at[step - 1],
            self.chips - 1 + step,
            2 * chip + self.core,
        )

    def add_cross(self, step):
        self.to_cross(step).wait_recv()
        held = self.far.at[step - 1]
        held[...] = (
            held[...].astype(jnp.float32) + self.got_cross[step - 1].astype(jnp.float32)
        ).astype(held.dtype)
        self.to_far(step).start()

    def total(self, own):
        self.to_sibling().wait_recv()
        value = own + self.got_sib[...].astype(jnp.float32)
        for step in range(1, self.chips):
            self.to_far(step).wait_recv()
            value = value + self.got_far[step - 1].astype(jnp.float32)
        return value

    def sent(self):
        self.to_sibling().wait_send()
        for step in range(1, self.chips):
            self.to_cross(step).wait_send()
            self.to_far(step).wait_send()


def scatter_scratch(rows, width):
    far = lax.axis_size("fsdp") // 2 - 1
    one, many = (rows, width), (far, rows, width)
    return [pltpu.VMEM(shape, jnp.bfloat16) for shape in (one, one, many, many, many, many)]


def dot_columns(left, right):
    return lax.dot_general(
        left, right, (((1,), (1,)), ((), ())), preferred_element_type=jnp.float32
    )


def tiles(count, body):
    def step(at, unused):
        body(at)
        return unused

    lax.fori_loop(0, count, step, 0)


def lane_tile(at, size):
    return pl.ds(pl.multiple_of(at * size, LANES), size)


def width_tile(width):
    return 384 if width % 384 == 0 else width


def hidden_tile(hidden):
    return 256 if hidden % 256 == 0 else 128


def transpose_into(target, source):
    rows, columns = source.shape

    def body(at):
        part = source[:, lane_tile(at, LANES)]
        target[pl.ds(pl.multiple_of(at * LANES, LANES), LANES), :] = part.T

    tiles(columns // LANES, body)


def ffn_kernel(
    x_ref, low_ref, out_ref, gain_ref, gate_in, up_in, down_in, all_g_in,
    layer_ref, resid_grad_ref, branch_ref, g_wide_ref, gate_part_out, up_part_out, layer_part_out,
    *rest,
):
    downs = len(down_split(gate_in.shape[1] // 16, lax.axis_size("ctx")))
    taken = iter(rest)

    def take(number):
        return [next(taken) for _ in range(number)]

    down_done, (gain_grad_ref,) = take(downs), take(1)
    all_n_ref, turned_n, turned_act, act_ref, gate_grad, up_grad, resid_ref, grad_own = take(8)
    down_scratch = take(2 * downs)
    give_sib, got_sib, give_cross, got_cross, far, got_far = take(6)
    n_sends, n_arrivals, grad_sends, grad_arrivals = take(4)
    gate_ref, up_ref, down_ref, all_g_ref, gate_part_ref, up_part_ref, layer_part_ref = take(7)
    (local_sems,) = take(1)
    loads = [
        pltpu.make_async_copy(source, target, local_sems.at[at])
        for at, (source, target) in enumerate(
            ((gate_in, gate_ref), (up_in, up_ref), (all_g_in, all_g_ref), (down_in, down_ref))
        )
    ]
    for copy in loads:
        copy.start()
    stores = []

    def store(source, target):
        copy = pltpu.make_async_copy(source, target, local_sems.at[len(loads) + len(stores)])
        copy.start()
        stores.append(copy)

    rings = [
        SumRing(*down_scratch[2 * at : 2 * at + 2], down_done[at], take(2), at % 2 == 0)
        for at in range(downs)
    ]
    group = lax.axis_size("fsdp")
    rows, width = x_ref.shape
    hidden = gate_ref.shape[1]
    barrier = pltpu.get_barrier_semaphore()
    greeted = greet_group(barrier) + 2
    for ring in rings[:2]:
        pl.semaphore_signal(barrier, inc=1, device_id=ring.after, device_id_type=MESH)
    step_in, step_out = hidden_tile(hidden), width_tile(width)

    def branch(at):
        columns = lane_tile(at, step_out)
        resid_ref[:, columns] = x_ref[:, columns].astype(jnp.float32) + forward_dot(
            low_ref[...], out_ref[:, columns]
        )

    tiles(width // step_out, branch)
    gain = gain_ref[...]
    scale = norm_scale(resid_ref[...])
    gathered = GroupGather(lambda shard: all_n_ref.at[shard], n_sends, n_arrivals)
    fsdp, chips = gathered.fsdp, gathered.chips
    all_n_ref[fsdp] = (resid_ref[...] * scale * gain).astype(jnp.bfloat16)
    pl.semaphore_wait(barrier, greeted)
    gathered.start(all_n_ref.at[fsdp])
    grad_sum = GroupScatter(
        give_sib,
        got_sib,
        lambda step: give_cross.at[step - 1],
        got_cross,
        far,
        got_far,
        grad_sends,
        grad_arrivals,
    )

    def hidden_part(shard):
        def body(at):
            columns = lane_tile(at, step_in)
            normed = all_n_ref[shard]
            gate = forward_dot(normed, gate_ref[:, columns])
            upward = forward_dot(normed, up_ref[:, columns])
            grad_act = dot_columns(
                all_g_ref[shard], down_ref[pl.ds(pl.multiple_of(at * step_in, LANES), step_in), :]
            )
            sigmoid = jax.nn.sigmoid(gate)
            silu = gate * sigmoid
            act_ref[shard, :, columns] = (silu * upward).astype(jnp.bfloat16)
            gate_grad[shard, :, columns] = (
                grad_act * upward * (sigmoid * (1.0 + gate * (1.0 - sigmoid)))
            ).astype(jnp.bfloat16)
            up_grad[shard, :, columns] = (grad_act * silu).astype(jnp.bfloat16)

        tiles(hidden // step_in, body)

    def grad_part(shard, target):
        def body(at):
            columns = pl.ds(pl.multiple_of(at * step_out, LANES), step_out)
            target[:, columns] = (
                dot_columns(gate_grad[shard], gate_ref[columns, :])
                + dot_columns(up_grad[shard], up_ref[columns, :])
            ).astype(target.dtype)

        tiles(width // step_out, body)

    for copy in loads:
        copy.wait()
    hidden_part(fsdp)
    gathered.sibling_here()
    sibling = gathered.sibling
    hidden_part(sibling)
    grad_part(sibling, grad_sum.give_sib)
    grad_sum.to_sibling().start()
    gathered.forward()
    grad_part(fsdp, grad_own)
    def turn_act(shard):
        transpose_into(turned_act.at[:, lane_tile(shard, rows)], act_ref.at[shard])

    turn_act(fsdp)
    turn_act(sibling)
    far_shards = []
    for step in range(1, chips):
        ours = gathered.same_core(chips - step)
        theirs = ours + sibling - fsdp
        far_shards.append((step, ours, theirs))
        gathered.crossed(step)
        hidden_part(theirs)
        hidden_part(ours)
        turn_act(theirs)
        turn_act(ours)
    blocks = hidden // 16
    spans, first = [], 0
    for ring in rings:
        last = min(blocks, first + ring.work.shape[0])
        spans.append((first, last, ring.work))
        first = last

    def down_tile(at):
        columns = lane_tile(at, step_out)
        part = forward_dot(
            turned_act[...], all_g_ref[:, :, columns].reshape(group * rows, step_out)
        ).astype(jnp.bfloat16)
        for begin, end, work in spans:
            if end > begin:
                work[: end - begin, :, columns] = part[begin * 16 : end * 16].reshape(
                    end - begin, 16, step_out
                )

    tiles(width // step_out, down_tile)
    for begin, end, work in spans:
        for spare in range(end - begin, work.shape[0]):
            work[spare] = jnp.zeros(work.shape[1:], work.dtype)
    for ring in rings:
        ring.start()
    for step, ours, theirs in far_shards:
        grad_part(theirs, give_cross.at[step - 1])
        grad_sum.to_cross(step).start()
        grad_part(ours, far.at[step - 1])
        grad_sum.add_cross(step)
    ticked = [0]

    def ring_tick(at):
        for ring in rings:

            @pl.when(at < ring.ticks)
            def _():
                ring.tick(jnp.minimum(at, ring.ticks - 1))

    def ticking(times, body):
        begin = ticked[0]

        def step(at):
            body(at)
            ring_tick(begin + at)

        tiles(times, step)
        ticked[0] += times

    for shard in range(group):
        span = slice(shard * rows, (shard + 1) * rows)
        transpose_into(turned_n.at[:, span], all_n_ref.at[shard])
    own = width // group
    row_blocks = own // 16
    for source, target in ((gate_grad, gate_part_ref), (up_grad, up_part_ref)):

        def weight_tile(at):
            columns = lane_tile(at, step_in)
            part = forward_dot(
                turned_n[...], source[:, :, columns].reshape(group * rows, step_in)
            ).astype(jnp.bfloat16)
            for block in range(step_in // LANES):
                first = (at * (step_in // LANES) + block) * row_blocks
                for owner in range(group):
                    target[owner, pl.ds(first, row_blocks)] = part[
                        owner * own : (owner + 1) * own, block * LANES : (block + 1) * LANES
                    ].reshape(row_blocks, 16, LANES)

        ticking(hidden // step_in, weight_tile)
        filled = hidden // LANES * row_blocks
        for spare in range(filled, target.shape[1]):
            for owner in range(group):
                target[owner, spare] = jnp.zeros(target.shape[2:], target.dtype)
        store(target, gate_part_out if source is gate_grad else up_part_out)

    def layer_tile(at):
        columns = lane_tile(at, step_out)
        part = forward_dot(
            act_ref[...].reshape(group * rows, hidden), down_ref[:, columns]
        ).reshape(group, rows, step_out)
        layer_part_ref[:, :, columns] = part.astype(jnp.bfloat16)

    ticking(width // step_out, layer_tile)
    store(layer_part_ref, layer_part_out)
    layer_ref[...] = resid_ref[...] + layer_part_ref[fsdp].astype(jnp.float32)
    upstream = grad_sum.total(grad_own[...])
    resid = resid_ref[...]
    scaled = upstream * gain
    grad_resid = (
        all_g_ref[fsdp].astype(jnp.float32)
        + scale * scaled
        - resid * scale**3 * jnp.mean(scaled * resid, axis=-1, keepdims=True)
    )
    gain_grad_ref[...] = jnp.sum(upstream * resid * scale, axis=0, keepdims=True)
    resid_grad_ref[...] = grad_resid
    branch_ref[...] = grad_resid.astype(jnp.bfloat16)
    units, _, wide = g_wide_ref.shape
    sequences = units // KVH
    keys = rows // sequences
    groups = wide // keys
    g_wide_ref[:, :HD, :] = jnp.zeros((units, HD, wide), g_wide_ref.dtype)
    for pair in range(H // 2):
        columns = slice(pair * 2 * HD, (pair + 1) * 2 * HD)
        mixed = dot_columns(branch_ref[...], out_ref[columns, :]).astype(jnp.bfloat16)
        for sequence in range(sequences):
            turned = mixed[sequence * keys : (sequence + 1) * keys].T
            for half in range(2):
                head = 2 * pair + half
                unit, member = sequence * KVH + head // groups, head % groups
                g_wide_ref[unit, HD:, member * keys : (member + 1) * keys] = turned[
                    half * HD : (half + 1) * HD
                ]
    begin = ticked[0]
    tiles(max(0, rings[0].ticks - begin), lambda at: ring_tick(begin + at))
    gathered.sent()
    grad_sum.sent()
    for ring in rings:
        ring.finish()
    for copy in stores:
        copy.wait()


def spread(blocks, count):
    return -(-blocks // count) * count


def feed_forward(x, low, full_out, my_gate, my_up, my_down, all_g, gain, units, wide):
    group, count = lax.axis_size("fsdp"), lax.axis_size("ctx")
    rows, width = x.shape
    hidden = my_gate.shape[1]
    blocks = spread(hidden // LANES * (width // group // 16), wide_split(width) * count)
    chips = group // 2
    dma = pltpu.SemaphoreType.DMA((2 * chips - 1,))
    bf16 = jnp.bfloat16
    down_chunks = [(per, 16, width) for per in down_split(hidden // 16, count)]
    return pl.pallas_call(
        ffn_kernel,
        out_shape=[
            jax.ShapeDtypeStruct((rows, width), jnp.float32),
            jax.ShapeDtypeStruct((rows, width), jnp.float32),
            jax.ShapeDtypeStruct((rows, width), bf16),
            jax.ShapeDtypeStruct((units, 2 * HD, wide), bf16),
            jax.ShapeDtypeStruct((group, blocks, 16, LANES), bf16),
            jax.ShapeDtypeStruct((group, blocks, 16, LANES), bf16),
            jax.ShapeDtypeStruct((group, rows, width), bf16),
            *[jax.ShapeDtypeStruct(chunk, bf16) for chunk in down_chunks],
            jax.ShapeDtypeStruct((1, width), jnp.float32),
        ],
        in_specs=[VMEM] * 4 + [ANY] * 4,
        out_specs=[VMEM] * 4 + [ANY] * 3 + [VMEM] * (1 + len(down_chunks)),
        scratch_shapes=[
            pltpu.VMEM((group, rows, width), bf16),
            pltpu.VMEM((width, group * rows), bf16),
            pltpu.VMEM((hidden, group * rows), bf16),
            pltpu.VMEM((group, rows, hidden), bf16),
            pltpu.VMEM((group, rows, hidden), bf16),
            pltpu.VMEM((group, rows, hidden), bf16),
            pltpu.VMEM((rows, width), jnp.float32),
            pltpu.VMEM((rows, width), jnp.float32),
            *[kind for chunk in down_chunks for kind in ring_scratch(chunk)],
            *scatter_scratch(rows, width),
            *[dma] * 4,
            pltpu.VMEM(my_gate.shape, bf16),
            pltpu.VMEM(my_up.shape, bf16),
            pltpu.VMEM(my_down.shape, bf16),
            pltpu.VMEM(all_g.shape, bf16),
            pltpu.VMEM((group, blocks, 16, LANES), bf16),
            pltpu.VMEM((group, blocks, 16, LANES), bf16),
            pltpu.VMEM((group, rows, width), bf16),
            pltpu.SemaphoreType.DMA((7,)),
            *[kind for _ in down_chunks for kind in ring_semaphores()],
        ],
        compiler_params=pltpu.CompilerParams(
            collective_id=2, has_side_effects=True, vmem_limit_bytes=60 << 20
        ),
    )(x, low, full_out, gain, my_gate, my_up, my_down, all_g)


def back_kernel(
    down_blocks, q_ref, g_ref, log_ref, gain_grad_ref, gain_ref, cos_ref, sin_ref,
    pairs_ref, mix_in, gate_ref, up_ref, layer_base_in, layer_part_ref, branch_ref, low_t_ref,
    normed_t_ref, w_query_in, w_key_in, w_value_in, x_in, resid_grad_in, *rest,
):
    taken = iter(rest)

    def take(number):
        return [next(taken) for _ in range(number)]

    halves, downs = wide_split(x_in.shape[1]), len(down_blocks)
    down_refs = take(downs)
    tokens_ref, layer_ref = take(2)
    wide_totals, down_totals = take(2 * halves), take(downs)
    out_a_total, out_b_total, rest_a_total, rest_b_total = take(4)
    peer_got, chain_got, layer_sib, layer_cross, layer_far = take(5)
    kv_ref, stage_ref, final_ref, qg_ref, delta_ref, grad_q_ref = take(6)
    wide_scratch = take(4 * halves)
    out_a_work, out_a_land, out_b_work, out_b_land = take(4)
    rest_a_work, rest_a_land, rest_b_work, rest_b_land = take(4)
    low_all, normed_all, branch_all, query_all, pair_all, upstream_ref, gain_give, gain_got = take(8)
    far_ref, layer_stage = take(2)
    mix_ref, layer_base_ref, w_query_ref, w_key_ref, w_value_ref, x_ref, resid_grad_ref = take(7)
    steps = Steps()
    fsdp, ctx, group, count = steps.fsdp, steps.ctx, lax.axis_size("fsdp"), lax.axis_size("ctx")
    units, deep, wide = q_ref.shape
    keys = pairs_ref.shape[2]
    rows, width = x_ref.shape
    own = width // group
    wide_rings = [
        Ring(*wide_scratch[2 * at : 2 * at + 2], wide_totals[at], take(5), at < halves, True)
        for at in range(2 * halves)
    ]
    down_rings = [SpreadRing(total, take(2), at % 2 == 0) for at, total in enumerate(down_totals)]
    out_a = Ring(out_a_work, out_a_land, out_a_total, take(2), True)
    out_b = Ring(out_b_work, out_b_land, out_b_total, take(2), False)
    layer_sum = GroupScatter(
        None,
        layer_sib,
        lambda step: layer_part_ref.at[
            2 * lax.rem(lax.div(fsdp, 2) + group // 2 - step, group // 2) + 1 - lax.rem(fsdp, 2)
        ],
        layer_cross,
        far_ref,
        layer_far,
        *take(2),
    )
    layer_sum.give_sib = layer_part_ref.at[layer_sum.sibling]
    rest_a = Ring(rest_a_work, rest_a_land, rest_a_total, take(2), True)
    rest_b = Ring(rest_b_work, rest_b_land, rest_b_total, take(2), False)
    first_rings = []
    for at in range(halves):
        first_rings += [wide_rings[at], wide_rings[halves + at]]
        first_rings += down_rings[at * downs // halves : (at + 1) * downs // halves]
    begun_rings = len(first_rings)
    first_rings += [out_a, out_b]
    peer_sends, peer_arrivals, chain_sends, chain_arrivals = take(4)
    branch_gather = GroupGather(lambda shard: branch_all.at[shard], *take(2))
    query_gather = GroupGather(lambda shard: query_all.at[shard], *take(2))
    pair_gather = GroupGather(lambda shard: pair_all.at[shard], *take(2))
    low_sends, low_arrivals, normed_sends, normed_arrivals, gain_sends, gain_arrivals = take(6)
    local_sems, stage_sems = take(2)

    barrier = pltpu.get_barrier_semaphore()
    greeted = steps.greet(barrier) + greet_group(barrier) + 2
    for device in (out_a.after, out_b.after):
        pl.semaphore_signal(barrier, inc=1, device_id=device, device_id_type=MESH)

    loads = []

    def load(source, target):
        copy = pltpu.make_async_copy(source, target, local_sems.at[len(loads)])
        copy.start()
        loads.append(copy)

    n = wide_scratch[0].shape[2]
    for at, ring in enumerate(wide_rings):
        source = (gate_ref, up_ref)[at // halves]
        for chunk in range(count):
            load(source.at[:, pl.ds((at % halves * count + chunk) * n, n)], ring.work.at[chunk])
    for ring, source in zip(down_rings, down_refs):
        load(source, ring.chunk(ring.total, ring.first))
    ring_loads = len(loads)
    load(pairs_ref, kv_ref)
    load(mix_in, mix_ref)
    load(branch_ref, branch_all.at[fsdp])
    load(low_t_ref.at[pl.ds(fsdp * own, own)], low_all.at[:, lane_tile(fsdp, rows)])
    load(normed_t_ref.at[pl.ds(fsdp * own, own)], normed_all.at[:, lane_tile(fsdp, rows)])
    slot_loads = len(loads)
    for source, target in (
        (layer_base_in, layer_base_ref),
        (w_query_in, w_query_ref),
        (w_key_in, w_key_ref),
        (w_value_in, w_value_ref),
        (x_in, x_ref),
        (resid_grad_in, resid_grad_ref),
    ):
        load(source, target)
    for copy in loads[:ring_loads]:
        copy.wait()
    pl.semaphore_wait(barrier, greeted)
    for ring in first_rings[:begun_rings]:
        ring.start()
    branch_gather.start(branch_ref)
    layer_sum.to_sibling().start()
    for step in range(1, group // 2):
        layer_sum.to_cross(step).start()

    def slices(source, target, sends, arrivals, step):
        peer = lax.rem(fsdp + step, group)
        return pltpu.make_async_remote_copy(
            src_ref=source.at[pl.ds(peer * own, own)],
            dst_ref=target.at[:, lane_tile(fsdp, rows)],
            send_sem=sends.at[step - 1],
            recv_sem=arrivals.at[step - 1],
            device_id=(peer, ctx),
            device_id_type=MESH,
        )

    turned = [
        slices(*ends, step)
        for ends in (
            (low_t_ref, low_all, low_sends, low_arrivals),
            (normed_t_ref, normed_all, normed_sends, normed_arrivals),
        )
        for step in range(1, group)
    ]
    for copy in turned:
        copy.start()

    def prepare(unit):
        q, g = q_ref[unit], g_ref[unit]
        qg_ref[unit, :wide] = q.T
        qg_ref[unit, wide:] = g.T
        delta_ref[unit] = jnp.sum(
            g[HD:].astype(jnp.float32) * mix_ref[unit], axis=0, keepdims=True
        )
        grad_q_ref[unit] = jnp.zeros((HD, wide), jnp.float32)

    for copy in loads[ring_loads:slot_loads]:
        copy.wait()
    tiles(units, prepare)

    def tick(ring, at):
        @pl.when(jnp.logical_and(at >= 0, at < ring.ticks))
        def _():
            ring.tick(jnp.clip(at, 0, ring.ticks - 1))

    late = steps.levels // 2 + 1

    def pump(at):
        lag = [0] * begun_rings + [late, late]
        for turn, ring in enumerate(first_rings):

            @pl.when(lax.rem(at, len(first_rings)) == turn)
            def _():
                tick(ring, lax.div(at, len(first_rings)) - lag[turn])

    def back(unit, first, blocks, diagonal):
        kv = kv_ref[pl.ds(first, blocks), unit].reshape(blocks * keys, deep)
        scores = jnp.dot(kv, q_ref[unit], preferred_element_type=jnp.float32)
        probs = jnp.exp(scores - log_ref[unit])
        if diagonal:
            probs = jnp.where(causal(keys, wide, scores.shape), probs, 0.0)
        grad_probs = jnp.dot(kv, g_ref[unit], preferred_element_type=jnp.float32)
        grad_scores = (probs * (grad_probs - delta_ref[unit])).astype(jnp.bfloat16)
        both = jnp.concatenate([grad_scores, probs.astype(jnp.bfloat16)], axis=1)
        grad_kv = jnp.dot(both, qg_ref[unit], preferred_element_type=jnp.float32)
        added = jnp.dot(kv.T, grad_scores, preferred_element_type=jnp.float32)
        grad_q_ref[unit] = grad_q_ref[unit] + added[:HD]
        kv_ref[pl.ds(first, blocks), unit] = grad_kv.astype(kv_ref.dtype).reshape(
            blocks, keys, deep
        )

    def across(pair):
        return pltpu.make_async_remote_copy(
            src_ref=kv_ref.at[2 * pair + 1 - steps.side],
            dst_ref=peer_got.at[pair],
            send_sem=peer_sends.at[pair],
            recv_sem=peer_arrivals.at[pair],
            device_id=steps.peer,
            device_id_type=MESH,
        )

    def down_chain(pair):
        return pltpu.make_async_remote_copy(
            src_ref=kv_ref.at[2 * pair + steps.side],
            dst_ref=chain_got.at[pair],
            send_sem=chain_sends.at[pair],
            recv_sem=chain_arrivals.at[pair],
            device_id=steps.below,
            device_id_type=MESH,
        )

    def combine(time):
        pair = time - steps.levels + steps.level

        @pl.when(jnp.logical_and(pair >= 0, pair <= steps.level))
        def _():
            for slot, expected, arrival, source in (
                (0, jnp.logical_or(pair < steps.level, steps.side == 0), across, peer_got),
                (1, steps.has_above, down_chain, chain_got),
            ):

                @pl.when(expected)
                def _():
                    arrival(pair).wait_recv()
                    copy = pltpu.make_async_copy(
                        source.at[pair], stage_ref.at[slot], stage_sems.at[slot]
                    )
                    copy.start()
                    copy.wait()

                @pl.when(jnp.logical_not(expected))
                def _():
                    stage_ref[slot] = jnp.zeros(stage_ref.shape[1:], stage_ref.dtype)

            def add(unit):
                final_ref[unit] = (
                    kv_ref[2 * pair + steps.side, unit].astype(jnp.float32)
                    + stage_ref[0, unit].astype(jnp.float32)
                    + stage_ref[1, unit].astype(jnp.float32)
                )

            tiles(units, add)

            @pl.when(pair < steps.level)
            def _():
                kv_ref[2 * pair + steps.side] = final_ref[...].astype(kv_ref.dtype)
                down_chain(pair).start()

    row_blocks = own // 16

    def weight_grad(left, right, begin, end, target, first, loop):
        span = LANES * next(n for n in (3, 2, 1) if (end - begin) % (n * LANES) == 0)

        def body(at):
            columns = pl.ds(pl.multiple_of(begin + at * span, LANES), span)
            part = forward_dot(
                left[...], right[:, :, columns].reshape(group * rows, span)
            ).astype(jnp.bfloat16)
            for block in range(span // LANES):
                here = first + (at * (span // LANES) + block) * row_blocks
                target[pl.ds(here, row_blocks)] = part[
                    :, block * LANES : (block + 1) * LANES
                ].reshape(row_blocks, 16, LANES)

        loop((end - begin) // span, body)
        return first + (end - begin) // LANES * row_blocks

    def clear_from(target, first):
        for spare in range(first, target.shape[0]):
            target[spare] = jnp.zeros((16, LANES), jnp.bfloat16)

    def out_grad():
        for copy in turned[: group - 1]:
            copy.wait_recv()
        branch_gather.forward()
        branch_gather.sibling_here()
        for step in range(1, branch_gather.chips):
            branch_gather.crossed(step)
        split = out_split(width)
        clear_from(out_a_work, weight_grad(low_all, branch_all, 0, split, out_a_work, 0, tiles))
        clear_from(out_b_work, weight_grad(low_all, branch_all, split, width, out_b_work, 0, tiles))
        out_a.start()
        out_b.start()

    turns = units // 2
    rings = max(turns, len(first_rings))

    def slot(pair):
        def turn(at):
            @pl.when(jnp.logical_and(pair < steps.level, at < turns))
            def _():
                for unit in (2 * at, 2 * at + 1):
                    back(unit, 2 * pair, 2, False)

            @pl.when(jnp.logical_and(pair == steps.level, at < turns))
            def _():
                for unit in (2 * at, 2 * at + 1):
                    back(unit, ctx, 1, True)

            @pl.when((pair == steps.level) & (steps.side == 1) & (at < turns))
            def _():
                for unit in (2 * at, 2 * at + 1):
                    back(unit, ctx - 1, 1, False)

            pump(pair * rings + at)

        tiles(rings, turn)

        @pl.when(jnp.logical_or(pair < steps.level, (pair == steps.level) & (steps.side == 1)))
        def _():
            across(pair).start()

        combine(pair)

        @pl.when(pair == late - 1)
        def _():
            out_grad()

    tiles(steps.levels, slot)
    pumped = [steps.levels * rings]

    def pump_next(times=1):
        def body(at, unused, begin=pumped[0]):
            pump(begin + at)
            return unused

        lax.fori_loop(0, times, body, 0)
        pumped[0] += times

    def pumping(times, body):
        begin = pumped[0]

        def step(at):
            body(at)
            tiles(2, lambda more: pump(begin + 2 * at + more))

        tiles(times, step)
        pumped[0] += 2 * times

    cosine, sine = cos_ref[...], sin_ref[...]

    def unturn(columns):
        first, second = columns[: HD // 2], columns[HD // 2 :]
        return jnp.concatenate(
            [first * cosine + second * sine, second * cosine - first * sine], axis=0
        )

    sequences = units // KVH
    groups = wide // keys
    begin = pumped[0]

    def query_rows(sequence):
        span = pl.ds(pl.multiple_of(sequence * keys, LANES), keys)
        for pair in range(H // 2):
            heads = []
            for head in (2 * pair, 2 * pair + 1):
                unit, member = sequence * KVH + head // groups, head % groups
                part = grad_q_ref[unit, :, member * keys : (member + 1) * keys]
                heads.append(unturn(part * HD ** (-0.5)))
            query_all[fsdp, span, pair * 2 * HD : (pair + 1) * 2 * HD] = (
                jnp.concatenate(heads, axis=0).astype(jnp.bfloat16).T
            )
        tiles(3, lambda more: pump(begin + 3 * sequence + more))

    tiles(sequences, query_rows)
    pumped[0] += 3 * sequences
    query_gather.start(query_all.at[fsdp])
    combine(steps.levels)
    kv_width = KVH * HD
    def pair_rows(sequence):
        span = pl.ds(pl.multiple_of(sequence * keys, LANES), keys)
        for pair in range(KVH // 2):
            turned_keys, turned_values = [], []
            for unit in (sequence * KVH + 2 * pair, sequence * KVH + 2 * pair + 1):
                part = final_ref[unit].T
                turned_keys.append(unturn(part[:HD]))
                turned_values.append(part[HD:])
            for start, parts in ((0, turned_keys), (kv_width, turned_values)):
                pair_all[fsdp, span, start + pair * 2 * HD : start + (pair + 1) * 2 * HD] = (
                    jnp.concatenate(parts, axis=0).astype(jnp.bfloat16).T
                )
    tiles(sequences, pair_rows)
    pair_gather.start(pair_all.at[fsdp])
    pump_next(2)
    query_gather.forward()
    step_out = width_tile(width)

    def upstream_tile(at):
        columns = pl.ds(pl.multiple_of(at * step_out, LANES), step_out)
        upstream_ref[:, columns] = (
            dot_columns(query_all[fsdp], w_query_ref[columns, :])
            + dot_columns(pair_all[fsdp, :, :kv_width], w_key_ref[columns, :])
            + dot_columns(pair_all[fsdp, :, kv_width:], w_value_ref[columns, :])
        )

    for copy in loads[slot_loads:]:
        copy.wait()
    pumping(width // step_out, upstream_tile)
    inputs = x_ref[...].astype(jnp.float32)
    scale = norm_scale(inputs)
    upstream = upstream_ref[...]
    scaled = upstream * gain_ref[...]
    tokens_ref[...] = (
        resid_grad_ref[...]
        + scale * scaled
        - inputs * scale**3 * jnp.mean(scaled * inputs, axis=-1, keepdims=True)
    )
    gain_attn = jnp.sum(upstream * inputs * scale, axis=0, keepdims=True)
    lanes = width // LANES
    gain_give[...] = jnp.zeros(gain_give.shape, jnp.float32)
    for block in range(lanes):
        columns = slice(block * LANES, (block + 1) * LANES)
        gain_give[block : block + 1, :] = gain_attn[:, columns]
        gain_give[lanes + block : lanes + block + 1, :] = gain_grad_ref[:, columns]

    def gain_copy(step):
        peer = lax.rem(fsdp + step, group)
        return pltpu.make_async_remote_copy(
            src_ref=gain_give,
            dst_ref=gain_got.at[step - 1],
            send_sem=gain_sends.at[step - 1],
            recv_sem=gain_arrivals.at[step - 1],
            device_id=(peer, ctx),
            device_id_type=MESH,
        )

    for step in range(1, group):
        gain_copy(step).start()
    pump_next()
    for copy in turned[group - 1 :]:
        copy.wait_recv()
    query_gather.sibling_here()
    for step in range(1, query_gather.chips):
        query_gather.crossed(step)
    split = query_split(width)
    filled_a = weight_grad(normed_all, query_all, 0, split, rest_a_work, 0, pumping)
    filled_b = weight_grad(normed_all, query_all, split, width, rest_b_work, 0, pumping)
    pair_gather.forward()
    pump_next()
    pair_gather.sibling_here()
    for step in range(1, pair_gather.chips):
        pair_gather.crossed(step)
    filled_b = weight_grad(normed_all, pair_all, 0, 2 * kv_width, rest_b_work, filled_b, pumping)
    for step in range(1, layer_sum.chips):
        ours = layer_part_ref.at[2 * lax.rem(layer_sum.chip + layer_sum.chips - step, layer_sum.chips) + layer_sum.core]
        for source, target in ((ours, far_ref.at[step - 1]), (layer_cross.at[step - 1], layer_stage)):
            if source is not ours:
                layer_sum.to_cross(step).wait_recv()
            copy = pltpu.make_async_copy(source, target, stage_sems.at[0])
            copy.start()
            copy.wait()
        far_ref[step - 1] = (
            far_ref[step - 1].astype(jnp.float32) + layer_stage[...].astype(jnp.float32)
        ).astype(jnp.bfloat16)
        layer_sum.to_far(step).start()
    gains = gain_give[...]
    for step in range(1, group):
        gain_copy(step).wait_recv()
        gains = gains + gain_got[step - 1]
    gain_tiles = gains.shape[0] // 16
    rest_a_work[filled_a : filled_a + gain_tiles] = gains.astype(jnp.bfloat16).reshape(
        gain_tiles, 16, LANES
    )
    clear_from(rest_a_work, filled_a + gain_tiles)
    clear_from(rest_b_work, filled_b)
    rest_a.start()
    rest_b.start()
    begun = pumped[0]
    total_pumps = max(wide_rings[0].ticks, late + out_a.ticks) * len(first_rings)

    half = -(-(total_pumps - begun) // rest_a.ticks)

    def layer_close():
        layer_sum.to_sibling().wait_recv()
        arrived = [layer_sib]
        for step in range(1, layer_sum.chips):
            layer_sum.to_far(step).wait_recv()
            arrived.append(layer_far.at[step - 1])
        for source in arrived:
            copy = pltpu.make_async_copy(source, layer_stage, stage_sems.at[0])
            copy.start()
            copy.wait()

            def add(at):
                block = pl.ds(pl.multiple_of(at * 32, 32), 32)
                layer_base_ref[block] = layer_base_ref[block] + layer_stage[block].astype(
                    jnp.float32
                )

            tiles(rows // 32, add)

        def close(at):
            block = pl.ds(pl.multiple_of(at * 32, 32), 32)
            layer_ref[block] = layer_base_ref[block].astype(jnp.bfloat16)

        tiles(rows // 32, close)

    def last_ticks(at, unused):
        tick(rest_a, at)
        tick(rest_b, at)
        tiles(half, lambda turn: pump(jnp.minimum(begun + half * at + turn, total_pumps)))

        @pl.when(at == rest_a.ticks * 3 // 4)
        def _():
            layer_close()

        return unused

    lax.fori_loop(0, rest_a.ticks, last_ticks, 0)
    layer_sum.sent()
    for ring in first_rings + [rest_a, rest_b]:
        ring.finish()
    for copy in turned:
        copy.wait_send()
    for gather in (branch_gather, query_gather, pair_gather):
        gather.sent()
    for step in range(1, group):
        gain_copy(step).wait_send()

    def sent(pair):
        @pl.when(jnp.logical_or(pair < steps.level, steps.side == 1))
        def _():
            across(pair).wait_send()

        @pl.when(pair < steps.level)
        def _():
            down_chain(pair).wait_send()

    tiles(steps.level + 1, sent)


def layer_back(
    q_wide, g_wide, log_total, gain_grad, gain, cosine, sine, all_pairs, mix, gate_part, up_part,
    layer_base, layer_parts, branch, low_t, normed_t, w_query, w_key, w_value, x, resid_grad, downs,
):
    group, count = lax.axis_size("fsdp"), lax.axis_size("ctx")
    units, deep, wide = q_wide.shape
    keys = all_pairs.shape[2]
    rows, width = x.shape
    own, kv_width = width // group, w_key.shape[1]
    bf16, f32 = jnp.bfloat16, jnp.float32
    dma = pltpu.SemaphoreType.DMA
    halves = wide_split(width)
    wide_chunk = (group, gate_part.shape[1] // (halves * count), 16, LANES)
    gain_rows = spread(2 * (width // LANES), 16)
    split, row_blocks = query_split(width), own // 16
    out_first = out_split(width)
    chips = group // 2
    small_chunks = [
        (spread(held, count) // count, 16, LANES)
        for held in (
            out_first // LANES * row_blocks,
            (width - out_first) // LANES * row_blocks,
            split // LANES * row_blocks + gain_rows // 16,
            (width - split + 2 * kv_width) // LANES * row_blocks,
        )
    ]
    levels = count // 2
    loaded = [mix, layer_base, w_query, w_key, w_value, x, resid_grad]
    return pl.pallas_call(
        functools.partial(back_kernel, [part.shape[0] for part in downs]),
        out_shape=[
            jax.ShapeDtypeStruct((rows, width), f32),
            jax.ShapeDtypeStruct((rows, width), bf16),
            *[ring_total(wide_chunk, True)] * (2 * halves),
            *[ring_total(part.shape) for part in downs],
            *[ring_total(chunk) for chunk in small_chunks],
            *[jax.ShapeDtypeStruct((levels, units, keys, deep), bf16)] * 2,
            jax.ShapeDtypeStruct((rows, width), bf16),
            *[jax.ShapeDtypeStruct((chips - 1, rows, width), bf16)] * 2,
        ],
        in_specs=[VMEM] * 7 + [ANY] * (14 + len(downs)),
        out_specs=[VMEM] * (6 + 2 * halves + len(downs)) + [ANY] * 5,
        scratch_shapes=[
            pltpu.VMEM(all_pairs.shape, bf16),
            pltpu.VMEM((2, units, keys, deep), bf16),
            pltpu.VMEM((units, keys, deep), f32),
            pltpu.VMEM((units, 2 * wide, deep), bf16),
            pltpu.VMEM((units, 1, wide), f32),
            pltpu.VMEM((units, HD, wide), f32),
            *[kind for _ in range(2 * halves) for kind in ring_scratch(wide_chunk, True)],
            *[kind for chunk in small_chunks for kind in ring_scratch(chunk)],
            pltpu.VMEM((own, group * rows), bf16),
            pltpu.VMEM((own, group * rows), bf16),
            pltpu.VMEM((group, rows, width), bf16),
            pltpu.VMEM((group, rows, width), bf16),
            pltpu.VMEM((group, rows, 2 * kv_width), bf16),
            pltpu.VMEM((rows, width), f32),
            pltpu.VMEM((gain_rows, LANES), f32),
            pltpu.VMEM((group - 1, gain_rows, LANES), f32),
            pltpu.VMEM((chips - 1, rows, width), bf16),
            pltpu.VMEM((rows, width), bf16),
            *[pltpu.VMEM(array.shape, array.dtype) for array in loaded],
            *[kind for _ in range(2 * halves) for kind in ring_semaphores(True)],
            *[kind for _ in range(len(downs) + 2) for kind in ring_semaphores()],
            *[dma((group - 1,))] * 2,
            *[kind for _ in range(2) for kind in ring_semaphores()],
            *[dma((levels,))] * 4,
            *[group_semaphores()] * 6,
            *[dma((group - 1,))] * 6,
            dma((11 + len(downs) + 2 * halves * count,)),
            dma((2,)),
        ],
        compiler_params=pltpu.CompilerParams(
            collective_id=3, has_side_effects=True, vmem_limit_bytes=62 << 20
        ),
    )(
        q_wide, g_wide, log_total, gain_grad, gain, cosine, sine, all_pairs, mix, gate_part, up_part,
        layer_base, layer_parts, branch, low_t, normed_t, w_query, w_key, w_value, x, resid_grad,
        *downs,
    )


def finish_kernel(halves, downs, *refs):
    taken = iter(refs)

    def take(number):
        return [next(taken) for _ in range(number)]

    wides, down_refs, smalls, (rows_ref, layer_rows) = take(2 * halves), take(downs), take(4), take(2)
    outs, (tokens_ref, layer_ref) = take(7), take(2)
    wide_held, down_held, small_held = take(2 * halves), take(downs), take(4)
    made, (load_sems, store_sems) = take(7), take(2)
    sources = [*wides, *down_refs, *smalls]
    held = [*wide_held, *down_held, *small_held]
    loads = {}
    for at, (source, target) in enumerate(zip(sources, held)):
        loads[id(target)] = pltpu.make_async_copy(source, target, load_sems.at[at])
        loads[id(target)].start()
    stores = []

    def store(index, columns=None):
        source, target = made[index], outs[index]
        if columns is not None:
            source, target = source.at[:, columns], target.at[:, columns]
        copy = pltpu.make_async_copy(source, target, store_sems.at[len(stores)])
        copy.start()
        stores.append(copy)

    rows = made[4].shape[0]
    row_blocks = rows // 16
    group = wides[0].shape[1]

    def unpack(source, first, index, begin, end):
        target = made[index]
        for block in range(begin, end):
            here = first + (block - begin) * row_blocks
            target[:, block * LANES : (block + 1) * LANES] = (
                source[here : here + row_blocks].reshape(rows, LANES).astype(jnp.float32)
            )
        return first + (end - begin) * row_blocks

    for index, parts in ((4, wide_held[:halves]), (5, wide_held[halves:])):
        for part in parts:
            loads[id(part)].wait()
        target = made[index]
        columns = target.shape[1] // group
        for owner in range(group):
            tile_rows = jnp.concatenate(
                [part[:, owner].reshape((-1,) + part.shape[3:]) for part in parts], axis=0
            )
            for block in range(columns // LANES):
                begin = owner * columns + block * LANES
                target[:, begin : begin + LANES] = (
                    tile_rows[block * row_blocks : (block + 1) * row_blocks]
                    .reshape(rows, LANES)
                    .astype(jnp.float32)
                )
            store(index, pl.ds(owner * columns, columns))
    down_grad = made[6]
    blocks, begin = down_grad.shape[0] // 16, 0
    for source in down_held:
        loads[id(source)].wait()
        end = min(blocks, begin + source.shape[0])
        if end > begin:
            down_grad[begin * 16 : end * 16, :] = (
                source[: end - begin]
                .reshape((end - begin) * 16, down_grad.shape[1])
                .astype(jnp.float32)
            )
        begin = end
    store(6)
    for part in small_held:
        loads[id(part)].wait()
    out_a, out_b, rest_a, rest_b = small_held
    lanes, kv_lanes = made[0].shape[1] // LANES, made[1].shape[1] // LANES
    middle, split = out_split(made[0].shape[1]) // LANES, query_split(made[0].shape[1]) // LANES
    unpack(out_a, 0, 3, 0, middle)
    unpack(out_b, 0, 3, middle, lanes)
    store(3)
    unpack(rest_a, 0, 0, 0, split)
    at = unpack(rest_b, 0, 0, split, lanes)
    store(0)
    at = unpack(rest_b, at, 1, 0, kv_lanes)
    store(1)
    unpack(rest_b, at, 2, 0, kv_lanes)
    store(2)
    keys = tokens_ref.shape[0]
    for sequence in range(tokens_ref.shape[1]):
        block = slice(sequence * keys, (sequence + 1) * keys)
        tokens_ref[:, sequence, :] = rows_ref[block]
        layer_ref[:, sequence, :] = layer_rows[block]
    for copy in stores:
        copy.wait()


def finish(wides, downs, smalls, token_rows, layer_rows, own, kv_width, hidden, sequences):
    rows, width = token_rows.shape
    f32 = jnp.float32
    outs = [
        jax.ShapeDtypeStruct((own, columns), f32)
        for columns in (width, kv_width, kv_width, width, FF, FF)
    ] + [jax.ShapeDtypeStruct((hidden, width), f32)]
    sources = [*wides, *downs, *smalls]
    dma = pltpu.SemaphoreType.DMA
    return pl.pallas_call(
        functools.partial(finish_kernel, len(wides) // 2, len(downs)),
        out_shape=outs
        + [
            jax.ShapeDtypeStruct((rows // sequences, sequences, width), kind)
            for kind in (f32, layer_rows.dtype)
        ],
        in_specs=[ANY] * len(sources) + [VMEM] * 2,
        out_specs=[ANY] * len(outs) + [VMEM] * 2,
        scratch_shapes=[pltpu.VMEM(array.shape, array.dtype) for array in sources]
        + [pltpu.VMEM(out.shape, f32) for out in outs]
        + [dma((len(sources),)), dma((5 + 2 * wides[0].shape[1],))],
        compiler_params=pltpu.CompilerParams(vmem_limit_bytes=60 << 20),
    )(*sources, token_rows, layer_rows)


def on_device(
    tokens, w_query, w_key, w_value, w_out, w_gate, w_up, w_down, gain_attn, gain_ffn, cotangent
):
    block_len, seq_count, width = tokens.shape
    rows_count = block_len * seq_count
    kv_width = KVH * HD
    positions = lax.axis_index("ctx") * block_len + jnp.arange(block_len, dtype=jnp.int32)
    freqs = ROTARY_BASE ** (-2.0 * jnp.arange(HD // 2, dtype=jnp.float32) / HD)
    angles = freqs[:, None] * positions.astype(jnp.float32)[None, :]
    cosine, sine = jnp.cos(angles), jnp.sin(angles)
    own = gain_attn.shape[0]
    units = seq_count * KVH
    wide = H // KVH * block_len
    own_gains = jnp.pad(
        jnp.concatenate([gain_attn, gain_ffn]).reshape(2, own).astype(jnp.float32), ((0, 6), (0, spread(own, LANES) - own))
    )
    (
        x_rows, q_wide, normed_t, full_gain_attn, full_gain_ffn, full_query, full_key, full_value, attn_low, low_t, mix_unit, log_total,
        all_pairs, full_out, my_gate, my_up, all_g,
    ) = attend(
        tokens, cotangent, own_gains, cosine, sine, w_query, w_key, w_value, w_out, w_gate, w_up
    )
    layer_base, grad_resid, grad_branch, g_wide, gate_part, up_part, layer_parts, *downs = (
        feed_forward(
            x_rows, attn_low, full_out, my_gate, my_up, w_down, all_g, full_gain_ffn, units, wide
        )
    )
    downs, gain_term_ffn = downs[:-1], downs[-1]
    grad_tokens, layer_out, *sums = layer_back(
        q_wide, g_wide, log_total, gain_term_ffn, full_gain_attn, cosine, sine, all_pairs, mix_unit,
        gate_part, up_part, layer_base, layer_parts, grad_branch, low_t, normed_t, full_query,
        full_key, full_value, x_rows, grad_resid, downs,
    )
    wides, sums = sums[: 2 * wide_split(width)], sums[2 * wide_split(width) :]
    smalls = sums[len(downs) : len(downs) + 4]
    filled = query_split(width) // LANES * (own // 16)
    gain_grads = smalls[2][filled:].reshape(-1, LANES)[: 2 * (width // LANES)].reshape(2, width)
    gain_grads = lax.dynamic_slice_in_dim(gain_grads, lax.axis_index("fsdp") * own, own, 1)
    gain_grads = gain_grads.astype(jnp.float32)
    *grads, tokens_grad, layer_result = finish(
        wides, sums[: len(downs)], smalls, grad_tokens, layer_out, own, kv_width, w_down.shape[0],
        seq_count,
    )
    return (
        layer_result,
        tokens_grad,
        *grads,
        gain_grads[0],
        gain_grads[1],
    )


def solution(mesh):
    return jax.shard_map(
        on_device,
        mesh=mesh,
        in_specs=(
            P("ctx", "fsdp", None),
            P("fsdp", None),
            P("fsdp", None),
            P("fsdp", None),
            P("fsdp", None),
            P("fsdp", None),
            P("fsdp", None),
            P("fsdp", None),
            P("fsdp"),
            P("fsdp"),
            P("ctx", "fsdp", None),
        ),
        out_specs=(
            P("ctx", "fsdp", None),
            P("ctx", "fsdp", None),
            P("fsdp", None),
            P("fsdp", None),
            P("fsdp", None),
            P("fsdp", None),
            P("fsdp", None),
            P("fsdp", None),
            P("fsdp", None),
            P("fsdp"),
            P("fsdp"),
        ),
        check_vma=False,
    )
```
